32 devices in a mesh: gz: 8 (over y, x, core), ma: 4 (over z).
Axes of the slice: x: 2, y: 2, z: 4, core: 2. Of those that a mesh axis runs over, the one named last changes fastest.
Arguments:
- bricks: bfloat16 [4096, 2048], P(('gz', 'ma')), may hold values from -7 to 7
- owners: int32 [4096, 1], P(('gz', 'ma')), may hold values from 0 to 31; in each aligned block of 128 rows (0 to 127, 128 to 255, ...) at most 8 rows name the same one
- tile_ids: int32 [4096], P(('gz', 'ma')), may hold values from 0 to 511
- counts: int32 [32], P(('gz', 'ma')), may hold values from 64 to 128, as said below
Outputs:
- brick_potential: bfloat16 [4096, 2048], P(('gz', 'ma'))
The draws below stay inside these ranges and needn't reach their ends.
Inputs may be any that keep to these rules, and one draw needn't show every extreme that they name: `owners`: in the rows of one atom domain no device is named by more than 8 rows, and in every draw some device is named by exactly 8 rows of some domain. `counts`: some atom domain uses all 128 of its bricks.
All inputs are finite; a program needn't handle non-finite values.
Results may differ from the reference program's by a relative error of at most 0.0013.
Values may be sent and summed in bfloat16 or wider, within the bound.
No kernel may reach another device: no remote copies, remote signals or barrier semaphores. Data moves between devices by JAX's collectives and lax.ppermute only.
A program may use at most 192 MiB of HBM per device.

```python
import math
import jax
import jax.numpy as jnp
import numpy as np
from jax import lax

NX = 512
NY = 512
SCREEN = 16
BZ = 4
BX = 8
BY = 64
CZ = 16
BRICK_DEV = 128
NZ = 128
DOMAINS = 32
CAP = 8
CELLS = 2048
TILES_DEV = 512
N_GZ = 8
N_MA = 4


def draw_counts(key, part):
    values = jax.random.randint(key, (DOMAINS,), BRICK_DEV // 2, BRICK_DEV + 1, dtype=jnp.int32)
    chosen = jax.random.randint(jax.random.fold_in(key, 7), (), 0, DOMAINS, dtype=jnp.int32)
    positions = jnp.arange(DOMAINS, dtype=jnp.int32)
    return jnp.where(positions == chosen, BRICK_DEV, values).astype(jnp.int32)


def draw_bricks(key, part):
    rough_key = jax.random.fold_in(key, 11)
    level_key = jax.random.fold_in(key, 13)
    shape = (DOMAINS * BRICK_DEV, CELLS)
    level = jax.random.uniform(level_key, (DOMAINS * BRICK_DEV, 1), jnp.float32, 0.5, 1.5)
    rough = jnp.clip(jax.random.normal(rough_key, shape, jnp.float32), -6.0, 6.0)
    base_level = 0.012
    values = rough + base_level * level
    return values.astype(jnp.bfloat16)


def place_ends(array, stream_key, smallest, high):
    extent = array.shape
    place = [jax.random.randint(jax.random.fold_in(stream_key, axis), (), 0, extent[axis]) for axis in range(len(extent))]
    array = array.at[tuple(place)].set(smallest)
    longest = extent.index(max(extent))
    place[longest] = (place[longest] + 1) % extent[longest]
    return array.at[tuple(place)].set(high)


def assign_block(rng, own, number, rows, amount, top, reach, lean):
    order = jax.random.permutation(rng, amount)
    crowded, common = shares(amount, rows * top, reach, lean, True), shares(amount, rows * top, reach, lean, False)
    places = jnp.arange(amount)

    def named(lengths, rotation):
        used = int((lengths > 0).sum())
        fixed = max(1, used // 4)
        passed = fixed + (places - fixed + rotation * (used - fixed)) % max(1, amount - fixed)
        return jnp.zeros((amount,), jnp.int32).at[order[jnp.where(places < fixed, places, passed)]].set(jnp.asarray(lengths, jnp.int32))

    lengths = jnp.where(number % 4 == 0, named(crowded, number // 4), named(common, number - number // 4 - 1))
    mixed = jax.random.permutation(jax.random.fold_in(own, 3), amount)
    donor, sink = mixed[0:amount // 2 * 2:2], mixed[1:amount // 2 * 2:2]
    margin = jnp.minimum(lengths[donor] - 1, reach - lengths[sink]) // 2
    margin = jnp.where((donor == order[0]) | (sink == order[0]) | (lengths[sink] == 0), 0, jnp.maximum(margin, 0))
    passed = jax.random.randint(jax.random.fold_in(own, 4), (amount // 2,), 0, 1 << 20) % (margin + 1)
    lengths = lengths.at[donor].add(-passed).at[sink].add(passed)
    items = jnp.searchsorted(jnp.cumsum(lengths), jnp.arange(rows * top), side="right").astype(jnp.int32)
    grid = items.reshape(top, rows).T
    grid = grid[jax.random.permutation(jax.random.fold_in(own, 1), rows)]
    rotation = jax.random.randint(jax.random.fold_in(own, 2), (rows, 1), 0, top)
    return jnp.take_along_axis(grid, (jnp.arange(top)[None, :] + rotation) % top, axis=1)


def shares(number_of, total, reach, slope, full):
    loads = [(1 << 20) // math.isqrt(standing ** slope) + 1 for standing in range(1, number_of + 1)]
    largest = reach if full else min(reach, max(-(-total // number_of), total * loads[0] // sum(loads)))
    least = 1 if total - largest >= number_of - 1 else 0
    holding, spare = [largest] + [least] * (number_of - 1), total - largest - least * (number_of - 1)
    while spare > 0:
        free = [i for i in range(1, number_of) if holding[i] < largest] or [i for i in range(1, number_of) if holding[i] < reach]
        pool, budget = sum([loads[i] for i in free]), spare
        for i in free:
            addition = min(reach - holding[i], max(1, budget * loads[i] // pool), spare)
            holding[i] = holding[i] + addition
            spare = spare - addition
    return np.array(holding)


def setup_inputs(seed: int = 0) -> dict:
    streams_of = jax.random.split(jax.random.key(seed), 5)
    bricks = draw_bricks(jax.random.fold_in(streams_of[4], 71), 0)
    owners_keys = jax.random.split(jax.random.fold_in(streams_of[1], 1), (DOMAINS * BRICK_DEV) // BRICK_DEV)
    owners_turns = jax.random.permutation(jax.random.fold_in(streams_of[1], 3), (DOMAINS * BRICK_DEV) // BRICK_DEV)
    owners = jax.vmap(lambda own, number: assign_block(jax.random.fold_in(streams_of[1], 2), own, number, BRICK_DEV, DOMAINS, 1, CAP, 2))(owners_keys, owners_turns).reshape((DOMAINS * BRICK_DEV, 1))
    tile_ids = place_ends(jax.random.randint(streams_of[2], (DOMAINS * BRICK_DEV,), 0, TILES_DEV), jax.random.fold_in(streams_of[2], 1), 0, TILES_DEV - 1).astype(jnp.int32)
    counts = draw_counts(jax.random.fold_in(streams_of[4], 71), 0)
    return dict(bricks=bricks, owners=owners, tile_ids=tile_ids, counts=counts)


def hartley(length):
    indices = jnp.arange(length, dtype=jnp.int32)
    products = indices[:, None] * indices[None, :] % length
    angles = 2.0 * math.pi / length * products.astype(jnp.float32)
    return (jnp.cos(angles) + jnp.sin(angles)) / math.sqrt(length)

def second_difference(length, indices):
    return 2.0 - 2.0 * jnp.cos(2.0 * math.pi / length * indices.astype(jnp.float32))

def thomas(right_side, diagonal):
    start_zero = jnp.zeros(right_side.shape[1:], jnp.float32)

    def down(state_pair, plane):
        factor = 1.0 / (diagonal - state_pair[0])
        partial_value = (plane + state_pair[1]) * factor
        return ((factor, partial_value), (factor, partial_value))
    _, (factors, partials) = lax.scan(down, (start_zero, start_zero), right_side)

    def upward(beyond, factor_partial):
        solved = factor_partial[1] + factor_partial[0] * beyond
        return (solved, solved)
    _, solutions = lax.scan(upward, start_zero, (factors, partials), reverse=True)
    return solutions

def reference(bricks, owners, tile_ids, counts):
    local_x = NX // N_MA
    local_y = NY // N_MA
    row_order = jnp.arange(DOMAINS * BRICK_DEV, dtype=jnp.int32)
    is_live = row_order % BRICK_DEV < counts[row_order // BRICK_DEV]
    segment = owners[:, 0] * TILES_DEV + tile_ids
    loaded = jnp.where(is_live[:, None], bricks.astype(jnp.float32), jnp.zeros((), jnp.float32))
    placed = jax.ops.segment_sum(loaded, segment, num_segments=DOMAINS * TILES_DEV)
    charge = placed.reshape(N_GZ, N_MA, CZ // BZ, local_x // BX, NY // BY, BZ, BX, BY)
    charge = charge.transpose(0, 2, 5, 1, 3, 6, 4, 7).reshape(NZ, NX, NY)
    table_x = hartley(NX)
    table_y = hartley(NY)
    lam_x = second_difference(NX, jnp.arange(NX, dtype=jnp.int32))
    lam_y_all = second_difference(NY, jnp.arange(NY, dtype=jnp.int32))
    screening = 1.0 / (SCREEN * SCREEN)
    highest = lax.Precision.HIGHEST

    def solve_block(total, block):
        start = block * local_y
        rows_y = lax.dynamic_slice_in_dim(table_y, start, local_y, 0)
        lam_y = lax.dynamic_slice_in_dim(lam_y_all, start, local_y, 0)
        spec_y = jnp.einsum('zxy,ky->zxk', charge, rows_y, precision=highest)
        spectrum = jnp.einsum('zxk,jx->zjk', spec_y, table_x, precision=highest)
        diagonal = 2.0 + screening + lam_x[:, None] + lam_y[None, :]
        modal = thomas(spectrum, diagonal)
        back_x = jnp.einsum('zjk,jx->zxk', modal, table_x, precision=highest)
        return (total + jnp.einsum('zxk,ky->zxy', back_x, rows_y, precision=highest), None)
    potential, _ = lax.scan(solve_block, jnp.zeros((NZ, NX, NY), jnp.float32), jnp.arange(N_MA, dtype=jnp.int32))
    tiles_all = potential.reshape(N_GZ, CZ // BZ, BZ, N_MA, local_x // BX, BX, NY // BY, BY)
    tiles_all = tiles_all.transpose(0, 3, 1, 4, 6, 2, 5, 7).reshape(DOMAINS * TILES_DEV, CELLS)
    picked = tiles_all[segment]
    return jnp.where(is_live[:, None], picked, jnp.zeros((), jnp.float32)).astype(jnp.bfloat16)
```

```python
import math

import jax
import jax.numpy as jnp
import ml_dtypes
import numpy as np
from jax import lax
from jax.experimental import pallas as pl
from jax.experimental.pallas import tpu as pltpu
from jax.sharding import PartitionSpec as P

NX = 512
NY = 512
SCREEN = 16
BZ = 4
BX = 8
BY = 64
CZ = 16


def hartley(length):
    indices = jnp.arange(length, dtype=jnp.int32)
    products = indices[:, None] * indices[None, :] % length
    angles = 2.0 * math.pi / length * products.astype(jnp.float32)
    return (jnp.cos(angles) + jnp.sin(angles)) / math.sqrt(length)


def second_difference(length, indices):
    return 2.0 - 2.0 * jnp.cos(2.0 * math.pi / length * indices.astype(jnp.float32))


def thomas(right_side, diagonal):
    start_zero = jnp.zeros(right_side.shape[1:], jnp.float32)

    def down(state_pair, plane):
        factor = 1.0 / (diagonal - state_pair[0])
        partial_value = (plane + state_pair[1]) * factor
        return ((factor, partial_value), (factor, partial_value))

    _, (factors, partials) = lax.scan(down, (start_zero, start_zero), right_side)

    def upward(beyond, factor_partial):
        solved = factor_partial[1] + factor_partial[0] * beyond
        return (solved, solved)

    _, solutions = lax.scan(upward, start_zero, (factors, partials), reverse=True)
    return solutions


def regroup(values):
    return lax.all_to_all(values, "ma", split_axis=2, concat_axis=1, tiled=True)


def on_device(bricks, owners, tile_ids, counts):
    domains = lax.axis_size(("gz", "ma"))
    group_count = lax.axis_size("ma")
    slab_count = lax.axis_size("gz")
    brick_rows, brick_cells = bricks.shape
    slot_count = max(2, 2 * brick_rows // domains)
    local_x = NX // group_count
    local_y = NY // group_count
    tiles_dev = CZ // BZ * (local_x // BX) * (NY // BY)
    highest = lax.Precision.HIGHEST
    target = owners[:, 0]
    row_order = jnp.arange(brick_rows, dtype=jnp.int32)
    earlier_same = (target[:, None] == target[None, :]) & (row_order[None, :] < row_order[:, None])
    within = jnp.sum(earlier_same.astype(jnp.int32), axis=1)
    slot_of = target * slot_count + within
    is_live = row_order < counts[0]
    loaded = jnp.where(is_live[:, None], bricks, jnp.zeros_like(bricks))
    outgoing = jnp.zeros((domains * slot_count, brick_cells), jnp.bfloat16).at[slot_of].set(loaded)
    out_ids = jnp.full((domains * slot_count,), tiles_dev, jnp.int32).at[slot_of].set(tile_ids)
    incoming, in_ids = (
        lax.all_to_all(outgoing, ("gz", "ma"), split_axis=0, concat_axis=0, tiled=True),
        lax.all_to_all(out_ids, ("gz", "ma"), split_axis=0, concat_axis=0, tiled=True),
    )
    picker = (jnp.arange(tiles_dev, dtype=jnp.int32)[:, None] == in_ids[None, :]).astype(
        jnp.bfloat16
    )
    deposit = jnp.dot(picker, incoming, preferred_element_type=jnp.float32)
    charge = deposit.reshape(CZ // BZ, local_x // BX, NY // BY, BZ, BX, BY)
    charge = charge.transpose(0, 3, 1, 4, 2, 5).reshape(CZ, local_x, NY)
    table_x = hartley(NX)
    table_y = hartley(NY)
    along_y = jnp.einsum("zxy,ky->zxk", charge, table_y, precision=highest)
    gathered_x = regroup(along_y)
    spectrum = jnp.einsum("zxk,jx->zjk", gathered_x, table_x, precision=highest)
    columns = lax.axis_index("ma") * local_y + jnp.arange(local_y, dtype=jnp.int32)
    lam_y = second_difference(NY, columns)
    screening = 1.0 / (SCREEN * SCREEN)
    slab_index = lax.axis_index("gz")
    lam_x = second_difference(NX, jnp.arange(NX, dtype=jnp.int32))
    diagonal = 2.0 + screening + lam_x[:, None] + lam_y[None, :]
    interior = spectrum[1:]
    particular = thomas(interior, diagonal)
    unit_rhs = jnp.zeros_like(interior).at[0].set(1.0)
    spike = thomas(unit_rhs, diagonal)
    near_weight = spike[0]
    far_weight = spike[-1]
    head_term = spectrum[0] + particular[0]
    tail_term = particular[-1]
    reduced_first = diagonal - near_weight
    reduced_rest = diagonal - 2.0 * near_weight
    start_zero = jnp.zeros_like(diagonal)
    heads, tails = (
        lax.all_gather(head_term[None], "gz", axis=0, tiled=True),
        lax.all_gather(tail_term[None], "gz", axis=0, tiled=True),
    )
    before = jnp.concatenate([start_zero[None], tails[:-1]], axis=0)
    sources = heads + before

    def chain_down(state_pair, packed):
        source, position = packed
        base_term = jnp.where(position == 0, reduced_first, reduced_rest)
        pivot_now = 1.0 / (base_term - far_weight * far_weight * state_pair[0])
        forward_part = pivot_now * (source + far_weight * state_pair[1])
        return ((pivot_now, forward_part), (pivot_now, forward_part))

    _, (pivots, forwards) = lax.scan(
        chain_down, (start_zero, start_zero), (sources, jnp.arange(slab_count, dtype=jnp.int32))
    )

    def chain_up(beyond, packed):
        plane_value = packed[1] + far_weight * packed[0] * beyond
        return (plane_value, plane_value)

    _, separators = lax.scan(chain_up, start_zero, (pivots, forwards), reverse=True)
    padded_sep = jnp.concatenate([separators, start_zero[None]], axis=0)
    own_plane = lax.dynamic_index_in_dim(padded_sep, slab_index, 0, keepdims=False)
    next_plane = lax.dynamic_index_in_dim(padded_sep, slab_index + 1, 0, keepdims=False)
    interior_sol = particular + own_plane[None] * spike + next_plane[None] * spike[::-1]
    modal = jnp.concatenate([own_plane[None], interior_sol], axis=0)
    back_x = jnp.einsum("zjk,jx->zkx", modal, table_x, precision=highest)
    gathered_y = regroup(back_x)
    potential = jnp.einsum("zkx,ky->zxy", gathered_y, table_y, precision=highest)
    pot_tiles = potential.reshape(CZ // BZ, BZ, local_x // BX, BX, NY // BY, BY)
    pot_tiles = (
        pot_tiles.transpose(0, 2, 4, 1, 3, 5).reshape(tiles_dev, brick_cells).astype(jnp.bfloat16)
    )
    padded_tiles = jnp.concatenate([pot_tiles, jnp.zeros((1, brick_cells), jnp.bfloat16)], axis=0)
    replies = padded_tiles[in_ids]
    returned = lax.all_to_all(replies, ("gz", "ma"), split_axis=0, concat_axis=0, tiled=True)
    result = returned[slot_of]
    return jnp.where(is_live[:, None], result, jnp.zeros_like(result))


PAIR_SLOTS = 8
TILES = 512
BRICK_ROWS = 16
LANES = 128
HALF = 64
BLOCK_ROWS = 1024
HEAD_ROWS = 16
SENT_ROWS = BLOCK_ROWS + HEAD_ROWS
STEPS = 64
PLANES = 128
FULL = 32700.0
LOG_UNIT = 128.0
VMEM_BYTES = 48 * 1024 * 1024


def split_table(table):
    high = table.astype(ml_dtypes.bfloat16)
    low = (table - high.astype(np.float64)).astype(ml_dtypes.bfloat16)
    return high, low


def line_tables():
    index = np.arange(NY)
    angle = 2.0 * np.pi / NY * (index[:, None] * index[None, :] % NY)
    table = (np.cos(angle) + np.sin(angle)) / np.sqrt(NY)
    swapped = table.reshape(NY, NY // LANES, 2, HALF)[:, :, ::-1].reshape(NY, NY)
    return np.stack([*split_table(table), *split_table(swapped)])


def plane_tables():
    index = np.arange(PLANES)
    table = np.sqrt(2.0 / (PLANES + 1)) * np.sin(
        np.pi / (PLANES + 1) * ((index[:, None] + 1) * (index[None, :] + 1) % (2 * PLANES + 2))
    )
    plane_of = (index % 32) * BZ + index // 32
    down = table[:, plane_of]
    both = []
    for each in (down, down.T):
        high, low = split_table(each)
        top = np.concatenate([high, high], axis=1)
        bottom = np.concatenate([low, np.zeros_like(low)], axis=1)
        both.append(np.concatenate([top, bottom], axis=0))
    return both


def mode_tables():
    mu = 2.0 - 2.0 * np.cos(np.pi / (PLANES + 1) * (np.arange(PLANES) + 1))
    base = np.broadcast_to((mu + 1.0 / (SCREEN * SCREEN))[:, None], (PLANES, LANES))
    lam = 2.0 - 2.0 * np.cos(2.0 * np.pi / NY * np.arange(NY))
    lam = lam.reshape(NY // HALF, HALF)
    return base.astype(np.float32), np.concatenate([lam, lam], axis=1).astype(np.float32)


def low_half(shape):
    return lax.broadcasted_iota(jnp.int32, shape, len(shape) - 1) < HALF


def split(values):
    high = values.astype(jnp.bfloat16)
    return high, (values - high.astype(jnp.float32)).astype(jnp.bfloat16)


def dot(left, right):
    return jnp.dot(left, right, preferred_element_type=jnp.float32)


def line_transform(load, store, table_ref):
    rows = 256

    def body(step, _):
        start = pl.multiple_of(step * rows, rows)
        low = low_half((rows, LANES))
        evens, odds = [], []
        for pair in range(4):
            first, second = load(2 * pair, start, rows), load(2 * pair + 1, start, rows)
            crossed = pltpu.roll(jnp.where(low, second, first), HALF, 1)
            evens.append(jnp.where(low, first, crossed))
            odds.append(jnp.where(low, crossed, second))
        products = []
        for lines, at in ((evens, 0), (odds, 2)):
            high, rest = split(jnp.concatenate(lines, axis=1))
            products.append(
                dot(high, table_ref[at]) + (dot(high, table_ref[at + 1]) + dot(rest, table_ref[at]))
            )
        for pair in range(4):
            even = products[0][:, pair * LANES : (pair + 1) * LANES]
            odd = products[1][:, pair * LANES : (pair + 1) * LANES]
            store(2 * pair, start, rows, jnp.where(low, even, odd))
            store(2 * pair + 1, start, rows, pltpu.roll(jnp.where(low, odd, even), HALF, 1))
        return 0

    lax.fori_loop(0, BLOCK_ROWS // rows, body, 0)


def write_fixed(source_ref, sent_ref):
    rows = 128

    def group(g, _):
        def widest(step, most):
            block = source_ref[pl.ds(pl.multiple_of(g * BLOCK_ROWS + step * rows, rows), rows), :]
            return jnp.maximum(most, jnp.max(jnp.abs(block).reshape(rows // 8, 8, LANES), axis=0))

        most = lax.fori_loop(0, BLOCK_ROWS // rows, widest, jnp.zeros((8, LANES), jnp.float32))
        most = jnp.maximum(jnp.max(most, axis=0, keepdims=True), 1e-30)
        level = jnp.floor(jnp.log2(most) * LOG_UNIT) + 2.0
        inverse = FULL * jnp.exp2(level * (-1.0 / LOG_UNIT))

        def write(step, _):
            start = pl.multiple_of(step * rows, rows)
            block = source_ref[pl.ds(pl.multiple_of(g * BLOCK_ROWS + start, rows), rows), :]
            fixed = jnp.floor(block * inverse + 0.5).astype(jnp.int32).astype(jnp.int16)
            sent_ref[g, pl.ds(start, rows), :] = fixed
            return 0

        lax.fori_loop(0, BLOCK_ROWS // rows, write, 0)
        head = jnp.broadcast_to(level, (HEAD_ROWS, LANES))
        sent_ref[g, BLOCK_ROWS:SENT_ROWS, :] = head.astype(jnp.int32).astype(jnp.int16)
        return 0

    lax.fori_loop(0, 8, group, 0)


def unit_of(sent_ref, g):
    head = sent_ref[g, BLOCK_ROWS:SENT_ROWS, :].astype(jnp.int32).astype(jnp.float32)
    return jnp.exp2(head[0:1] * (1.0 / LOG_UNIT)) * (1.0 / FULL)


def wide(block):
    return block.astype(jnp.int32).astype(jnp.float32)


def pack_kernel(owner_ref, tile_ref, count_ref, brick_ref, out_ref, slot_ref, rows_ref, head_ref, used_ref):
    brick_rows = brick_ref.shape[0]
    for q in range(BRICK_ROWS):
        block = brick_ref[:, q * LANES : (q + 1) * LANES].astype(jnp.float32)
        rows_ref[pl.ds(q, brick_rows, stride=BRICK_ROWS), :] = block
    head_ref[...] = jnp.full(head_ref.shape, float(TILES), jnp.float32)
    out_ref[...] = jnp.zeros(out_ref.shape, jnp.bfloat16)
    for owner in range(32):
        used_ref[owner] = 0

    def place(r, _):
        owner = owner_ref[r]
        within = used_ref[owner]
        used_ref[owner] = within + 1
        slot = owner * PAIR_SLOTS + within
        slot_ref[r] = slot
        tile = tile_ref[r]
        position = (tile % 8) * HALF + tile // 8
        brick = rows_ref[pl.ds(pl.multiple_of(r * BRICK_ROWS, BRICK_ROWS), BRICK_ROWS), :]
        at = pl.multiple_of(within * BRICK_ROWS, BRICK_ROWS)
        out_ref[owner, pl.ds(at, BRICK_ROWS), :] = brick.astype(jnp.bfloat16)
        head_ref[pl.ds(slot, 1), :] = jnp.full((1, LANES), position, jnp.int32).astype(jnp.float32)
        return 0

    count = count_ref[0]
    lax.fori_loop(0, count, place, 0)

    def rest(r, _):
        slot_ref[r] = 0
        return 0

    lax.fori_loop(count, brick_rows, rest, 0)

    def heading(owner, _):
        head = head_ref[pl.ds(pl.multiple_of(owner * PAIR_SLOTS, PAIR_SLOTS), PAIR_SLOTS), :]
        high = jnp.floor(head * (1.0 / 32.0))
        both = jnp.concatenate([high, head - 32.0 * high], axis=0)
        out_ref[owner, PAIR_SLOTS * BRICK_ROWS :, :] = both.astype(jnp.bfloat16)
        return 0

    lax.fori_loop(0, 32, heading, 0)


def forward_kernel(brick_ref, table_ref, sent_ref, tiles_ref, charge_ref, lines_ref, vec_ref, sem):
    lane = lax.broadcasted_iota(jnp.int32, (PAIR_SLOTS, LANES), 1)
    found = jnp.zeros((PAIR_SLOTS, LANES), jnp.float32)
    for domain in range(32):
        head = brick_ref[domain, PAIR_SLOTS * BRICK_ROWS :, :].astype(jnp.float32)
        found = jnp.where(lane == domain, head[:8] * 32.0 + head[8:], found)
    vec_ref[...] = found.astype(jnp.int32)
    copy = pltpu.make_async_copy(vec_ref, tiles_ref, sem)
    copy.start()
    charge_ref[...] = jnp.zeros(charge_ref.shape, jnp.float32)
    copy.wait()

    def deposit(domain, _):
        for within in range(PAIR_SLOTS):
            at = pl.ds(pl.multiple_of(tiles_ref[within, domain] * BRICK_ROWS, BRICK_ROWS), BRICK_ROWS)
            brick = brick_ref[domain, within * BRICK_ROWS : (within + 1) * BRICK_ROWS, :]
            charge_ref[at, :] += brick.astype(jnp.float32)
        return 0

    lax.fori_loop(0, 32, deposit, 0)

    def load(block, start, rows):
        return charge_ref[pl.ds(pl.multiple_of(block * BLOCK_ROWS + start, rows), rows), :]

    def store(block, start, rows, values):
        lines_ref[pl.ds(pl.multiple_of(block * BLOCK_ROWS + start, rows), rows), :] = values

    line_transform(load, store, table_ref)
    write_fixed(lines_ref, sent_ref)


def roots(base_ref, lam_ref):
    excess = base_ref[...] + lam_ref[...]
    spread = jnp.sqrt(excess * (excess + 4.0))
    root = 2.0 / (2.0 + excess + spread)
    return root, spread


def down_kernel(got_ref, plane_ref, base_ref, lam_ref, walk_ref, end_ref, grid_ref, modes_ref, root_ref):
    rows = 128

    def widen(g, _):
        unit = unit_of(got_ref, g)

        def part(step, _):
            start = pl.multiple_of(step * rows, rows)
            grid_ref[pl.ds(pl.multiple_of(g * BLOCK_ROWS + start, rows), rows), :] = (
                wide(got_ref[g, pl.ds(start, rows), :]) * unit
            )
            return 0

        return lax.fori_loop(0, BLOCK_ROWS // rows, part, 0)

    lax.fori_loop(0, 8, widen, 0)

    def planes(at):
        return jnp.concatenate(
            [grid_ref[pl.ds(at + iz * 4, 32, stride=256), :] for iz in range(BZ)], axis=0
        )

    def sines(tx, _):
        for half in range(2):
            lines = jnp.concatenate([planes(tx * 16 + half * 2), planes(tx * 16 + half * 2 + 1)], axis=1)
            both = dot(plane_ref[...], jnp.concatenate(split(lines), axis=0))
            modes = both[:PLANES] + both[PLANES:]
            modes_ref[tx * 4 + half * 2] = modes[:, :LANES]
            modes_ref[tx * 4 + half * 2 + 1] = modes[:, LANES:]
        return 0

    lax.fori_loop(0, 16, sines, 0)
    root, _ = roots(base_ref, lam_ref)
    root_ref[...] = root

    part_rows = 64
    low = low_half((part_rows, LANES))
    for part in range(PLANES // part_rows):
        here = pl.ds(part * part_rows, part_rows)
        root = root_ref[here, :]
        square = root * root

        def walk(step, held):
            ahead, behind = modes_ref[step, here, :], modes_ref[STEPS - 1 - step, here, :]
            own = jnp.where(low, behind, ahead)
            other = pltpu.roll(jnp.where(low, ahead, behind), HALF, 1)
            held = square * held + (own + root * other)
            walk_ref[step, here, :] = held
            return held

        end_ref[here, :] = lax.fori_loop(0, STEPS, walk, jnp.zeros((part_rows, LANES), jnp.float32))


def up_kernel(place_ref, walk_ref, ends_ref, plane_ref, base_ref, lam_ref, sent_ref, full_ref, grid_ref, root_ref, gain_ref):
    group_count = ends_ref.shape[0]
    own = place_ref[0]
    root, spread = roots(base_ref, lam_ref)
    root_ref[...] = root
    gain_ref[...] = 1.0 / spread
    part_rows = 64
    low = low_half((part_rows, LANES))
    for part in range(PLANES // part_rows):
        here = pl.ds(part * part_rows, part_rows)
        root = root_ref[here, :]
        square = root * root
        across = square
        for _ in range(6):
            across = across * across
        entering = jnp.zeros((part_rows, LANES), jnp.float32)
        for step in range(group_count - 1, -1, -1):
            before = ends_ref[(own + 2 * group_count - 1 - step) % group_count, here, :]
            after = ends_ref[(own + 1 + step) % group_count, here, :]
            entering = entering * across + jnp.where(low, after, before)
        around = across
        for _ in range(2):
            around = around * around
        entering = entering / (1.0 - around)
        full_ref[0, here, :] = entering

        def carry(step, reach):
            full_ref[step + 1, here, :] = walk_ref[step, here, :] + reach
            return reach * square

        lax.fori_loop(0, STEPS, carry, entering * square)

    def solved(step):
        low = low_half((PLANES, LANES))
        near = jnp.where(low, full_ref[STEPS - step], full_ref[step + 1])
        far = jnp.where(low, full_ref[STEPS - 1 - step], full_ref[step])
        return gain_ref[...] * (near + root_ref[...] * pltpu.roll(far, HALF, 1))

    def sines(tx, _):
        for half in range(2):
            first = tx * 4 + half * 2
            modes = jnp.concatenate([solved(first), solved(first + 1)], axis=1)
            both = dot(plane_ref[...], jnp.concatenate(split(modes), axis=0))
            lines = both[:PLANES] + both[PLANES:]
            for one in range(2):
                for iz in range(BZ):
                    at = tx * 16 + iz * 4 + half * 2 + one
                    grid_ref[pl.ds(at, 32, stride=256), :] = lines[
                        iz * 32 : (iz + 1) * 32, one * LANES : (one + 1) * LANES
                    ]
        return 0

    lax.fori_loop(0, 16, sines, 0)
    write_fixed(grid_ref, sent_ref)


def reply_kernel(tiles_ref, got_ref, table_ref, out_ref, pot_ref):
    units = [unit_of(got_ref, g) for g in range(8)]

    def load(block, start, rows):
        return wide(got_ref[block, pl.ds(start, rows), :]) * units[block]

    def store(block, start, rows, values):
        at = pl.multiple_of(block * BLOCK_ROWS + start, rows)
        pot_ref[pl.ds(at, rows), :] = values.astype(jnp.bfloat16)

    line_transform(load, store, table_ref)
    pot_ref[TILES * BRICK_ROWS :, :] = jnp.zeros((BRICK_ROWS, LANES), jnp.bfloat16)

    def pick(domain, _):
        for within in range(PAIR_SLOTS):
            at = pl.multiple_of(tiles_ref[within, domain] * BRICK_ROWS, BRICK_ROWS)
            out_ref[domain, within * BRICK_ROWS : (within + 1) * BRICK_ROWS, :] = pot_ref[pl.ds(at, BRICK_ROWS), :]
        return 0

    lax.fori_loop(0, 32, pick, 0)


def unpack_kernel(slot_ref, count_ref, got_ref, out_ref, rows_ref):
    brick_rows = out_ref.shape[0]
    rows_ref[...] = jnp.zeros(rows_ref.shape, jnp.float32)

    def place(r, _):
        slot = slot_ref[r]
        at = pl.multiple_of((slot % PAIR_SLOTS) * BRICK_ROWS, BRICK_ROWS)
        brick = got_ref[slot // PAIR_SLOTS, pl.ds(at, BRICK_ROWS), :]
        rows_ref[pl.ds(pl.multiple_of(r * BRICK_ROWS, BRICK_ROWS), BRICK_ROWS), :] = brick.astype(jnp.float32)
        return 0

    lax.fori_loop(0, count_ref[0], place, 0)
    for q in range(BRICK_ROWS):
        block = rows_ref[pl.ds(q, brick_rows, stride=BRICK_ROWS), :]
        out_ref[:, q * LANES : (q + 1) * LANES] = block.astype(jnp.bfloat16)


def call(kernel, outs, places, scratch, operands, spaces, name):
    return pl.pallas_call(
        kernel,
        out_shape=outs,
        in_specs=[pl.BlockSpec(memory_space=space) for space in spaces],
        out_specs=[pl.BlockSpec(memory_space=space) for space in places],
        scratch_shapes=scratch,
        compiler_params=pltpu.CompilerParams(vmem_limit_bytes=VMEM_BYTES),
        name=name,
    )(*operands)


def on_device_8x4(bricks, owners, tile_ids, counts):
    V, S = pltpu.VMEM, pltpu.SMEM
    f32, bf16, i32, i16 = jnp.float32, jnp.bfloat16, jnp.int32, jnp.int16
    shape = jax.ShapeDtypeStruct
    brick_rows = bricks.shape[0]
    line_table = jnp.asarray(line_tables())
    plane_down, plane_up = (jnp.asarray(each) for each in plane_tables())
    base, lam_all = (jnp.asarray(each) for each in mode_tables())
    lam = lax.dynamic_slice_in_dim(lam_all, lax.axis_index("gz"), 1, 0)
    place = lax.axis_index("ma").astype(i32).reshape(1)
    both = ("gz", "ma")

    outgoing, slots = call(
        pack_kernel,
        [shape((32, 144, LANES), bf16), shape((brick_rows,), i32)],
        [V, S],
        [V((brick_rows * BRICK_ROWS, LANES), f32), V((32 * PAIR_SLOTS, LANES), f32), S((32,), i32)],
        (owners.reshape(brick_rows), tile_ids, counts, bricks),
        [S, S, S, V],
        "pack",
    )
    incoming = lax.all_to_all(outgoing, both, split_axis=0, concat_axis=0, tiled=True)
    sent, tiles = call(
        forward_kernel,
        [shape((8, SENT_ROWS, LANES), i16), shape((PAIR_SLOTS, LANES), i32)],
        [V, S],
        [
            V(((TILES + 1) * BRICK_ROWS, LANES), f32),
            V((TILES * BRICK_ROWS, LANES), f32),
            V((PAIR_SLOTS, LANES), i32),
            pltpu.SemaphoreType.DMA,
        ],
        (incoming, line_table),
        [V, V],
        "forward",
    )
    got = lax.all_to_all(sent, "gz", split_axis=0, concat_axis=0, tiled=True)
    cube = (STEPS, PLANES, LANES)
    walk, end = call(
        down_kernel,
        [shape(cube, f32), shape((PLANES, LANES), f32)],
        [V, V],
        [V((8 * BLOCK_ROWS, LANES), f32), V(cube, f32), V((PLANES, LANES), f32)],
        (got, plane_down, base, lam),
        [V, V, V, V],
        "down",
    )
    ends = lax.all_gather(end, "ma", axis=0, tiled=False)
    (sent,) = call(
        up_kernel,
        [shape((8, SENT_ROWS, LANES), i16)],
        [V],
        [
            V((STEPS + 1, PLANES, LANES), f32),
            V((8 * BLOCK_ROWS, LANES), f32),
            V((PLANES, LANES), f32),
            V((PLANES, LANES), f32),
        ],
        (place, walk, ends, plane_up, base, lam),
        [S, V, V, V, V, V],
        "up",
    )
    got = lax.all_to_all(sent, "gz", split_axis=0, concat_axis=0, tiled=True)
    (replies,) = call(
        reply_kernel,
        [shape((32, 128, LANES), bf16)],
        [V],
        [V(((TILES + 1) * BRICK_ROWS, LANES), bf16)],
        (tiles, got, line_table),
        [S, V, V],
        "reply",
    )
    returned = lax.all_to_all(replies, both, split_axis=0, concat_axis=0, tiled=True)
    (result,) = call(
        unpack_kernel,
        [shape((brick_rows, BRICK_ROWS * LANES), bf16)],
        [V],
        [V((brick_rows * BRICK_ROWS, LANES), f32)],
        (slots, counts, returned),
        [S, S, V],
        "unpack",
    )
    return result


def solution(mesh):
    in_specs = (P(("gz", "ma"), None), P(("gz", "ma"), None), P(("gz", "ma")), P(("gz", "ma")))
    out_specs = P(("gz", "ma"), None)
    body = on_device_8x4 if (mesh.shape["gz"], mesh.shape["ma"]) == (8, 4) else on_device
    return jax.shard_map(body, mesh=mesh, in_specs=in_specs, out_specs=out_specs, check_vma=False)
```

```python
import math

import jax
import jax.numpy as jnp
import ml_dtypes
import numpy as np
from jax import lax
from jax.experimental import pallas as pl
from jax.experimental.pallas import tpu as pltpu
from jax.sharding import PartitionSpec as P

NX = 512
NY = 512
SCREEN = 16
BZ = 4
BX = 8
BY = 64
CZ = 16


def hartley(length):
    indices = jnp.arange(length, dtype=jnp.int32)
    products = indices[:, None] * indices[None, :] % length
    angles = 2.0 * math.pi / length * products.astype(jnp.float32)
    return (jnp.cos(angles) + jnp.sin(angles)) / math.sqrt(length)


def second_difference(length, indices):
    return 2.0 - 2.0 * jnp.cos(2.0 * math.pi / length * indices.astype(jnp.float32))


def thomas(right_side, diagonal):
    start_zero = jnp.zeros(right_side.shape[1:], jnp.float32)

    def down(state_pair, plane):
        factor = 1.0 / (diagonal - state_pair[0])
        partial_value = (plane + state_pair[1]) * factor
        return ((factor, partial_value), (factor, partial_value))

    _, (factors, partials) = lax.scan(down, (start_zero, start_zero), right_side)

    def upward(beyond, factor_partial):
        solved = factor_partial[1] + factor_partial[0] * beyond
        return (solved, solved)

    _, solutions = lax.scan(upward, start_zero, (factors, partials), reverse=True)
    return solutions


def regroup(values):
    return lax.all_to_all(values, "ma", split_axis=2, concat_axis=1, tiled=True)


def on_device(bricks, owners, tile_ids, counts):
    domains = lax.axis_size(("gz", "ma"))
    group_count = lax.axis_size("ma")
    slab_count = lax.axis_size("gz")
    brick_rows, brick_cells = bricks.shape
    slot_count = max(2, 2 * brick_rows // domains)
    local_x = NX // group_count
    local_y = NY // group_count
    tiles_dev = CZ // BZ * (local_x // BX) * (NY // BY)
    highest = lax.Precision.HIGHEST
    target = owners[:, 0]
    row_order = jnp.arange(brick_rows, dtype=jnp.int32)
    earlier_same = (target[:, None] == target[None, :]) & (row_order[None, :] < row_order[:, None])
    within = jnp.sum(earlier_same.astype(jnp.int32), axis=1)
    slot_of = target * slot_count + within
    is_live = row_order < counts[0]
    loaded = jnp.where(is_live[:, None], bricks, jnp.zeros_like(bricks))
    outgoing = jnp.zeros((domains * slot_count, brick_cells), jnp.bfloat16).at[slot_of].set(loaded)
    out_ids = jnp.full((domains * slot_count,), tiles_dev, jnp.int32).at[slot_of].set(tile_ids)
    incoming, in_ids = (
        lax.all_to_all(outgoing, ("gz", "ma"), split_axis=0, concat_axis=0, tiled=True),
        lax.all_to_all(out_ids, ("gz", "ma"), split_axis=0, concat_axis=0, tiled=True),
    )
    picker = (jnp.arange(tiles_dev, dtype=jnp.int32)[:, None] == in_ids[None, :]).astype(
        jnp.bfloat16
    )
    deposit = jnp.dot(picker, incoming, preferred_element_type=jnp.float32)
    charge = deposit.reshape(CZ // BZ, local_x // BX, NY // BY, BZ, BX, BY)
    charge = charge.transpose(0, 3, 1, 4, 2, 5).reshape(CZ, local_x, NY)
    table_x = hartley(NX)
    table_y = hartley(NY)
    along_y = jnp.einsum("zxy,ky->zxk", charge, table_y, precision=highest)
    gathered_x = regroup(along_y)
    spectrum = jnp.einsum("zxk,jx->zjk", gathered_x, table_x, precision=highest)
    columns = lax.axis_index("ma") * local_y + jnp.arange(local_y, dtype=jnp.int32)
    lam_y = second_difference(NY, columns)
    screening = 1.0 / (SCREEN * SCREEN)
    slab_index = lax.axis_index("gz")
    lam_x = second_difference(NX, jnp.arange(NX, dtype=jnp.int32))
    diagonal = 2.0 + screening + lam_x[:, None] + lam_y[None, :]
    interior = spectrum[1:]
    particular = thomas(interior, diagonal)
    unit_rhs = jnp.zeros_like(interior).at[0].set(1.0)
    spike = thomas(unit_rhs, diagonal)
    near_weight = spike[0]
    far_weight = spike[-1]
    head_term = spectrum[0] + particular[0]
    tail_term = particular[-1]
    reduced_first = diagonal - near_weight
    reduced_rest = diagonal - 2.0 * near_weight
    start_zero = jnp.zeros_like(diagonal)
    heads, tails = (
        lax.all_gather(head_term[None], "gz", axis=0, tiled=True),
        lax.all_gather(tail_term[None], "gz", axis=0, tiled=True),
    )
    before = jnp.concatenate([start_zero[None], tails[:-1]], axis=0)
    sources = heads + before

    def chain_down(state_pair, packed):
        source, position = packed
        base_term = jnp.where(position == 0, reduced_first, reduced_rest)
        pivot_now = 1.0 / (base_term - far_weight * far_weight * state_pair[0])
        forward_part = pivot_now * (source + far_weight * state_pair[1])
        return ((pivot_now, forward_part), (pivot_now, forward_part))

    _, (pivots, forwards) = lax.scan(
        chain_down, (start_zero, start_zero), (sources, jnp.arange(slab_count, dtype=jnp.int32))
    )

    def chain_up(beyond, packed):
        plane_value = packed[1] + far_weight * packed[0] * beyond
        return (plane_value, plane_value)

    _, separators = lax.scan(chain_up, start_zero, (pivots, forwards), reverse=True)
    padded_sep = jnp.concatenate([separators, start_zero[None]], axis=0)
    own_plane = lax.dynamic_index_in_dim(padded_sep, slab_index, 0, keepdims=False)
    next_plane = lax.dynamic_index_in_dim(padded_sep, slab_index + 1, 0, keepdims=False)
    interior_sol = particular + own_plane[None] * spike + next_plane[None] * spike[::-1]
    modal = jnp.concatenate([own_plane[None], interior_sol], axis=0)
    back_x = jnp.einsum("zjk,jx->zkx", modal, table_x, precision=highest)
    gathered_y = regroup(back_x)
    potential = jnp.einsum("zkx,ky->zxy", gathered_y, table_y, precision=highest)
    pot_tiles = potential.reshape(CZ // BZ, BZ, local_x // BX, BX, NY // BY, BY)
    pot_tiles = (
        pot_tiles.transpose(0, 2, 4, 1, 3, 5).reshape(tiles_dev, brick_cells).astype(jnp.bfloat16)
    )
    padded_tiles = jnp.concatenate([pot_tiles, jnp.zeros((1, brick_cells), jnp.bfloat16)], axis=0)
    replies = padded_tiles[in_ids]
    returned = lax.all_to_all(replies, ("gz", "ma"), split_axis=0, concat_axis=0, tiled=True)
    result = returned[slot_of]
    return jnp.where(is_live[:, None], result, jnp.zeros_like(result))


DOMAINS = 32
SLABS = 8
PAIR_SLOTS = 8
SLOTS = DOMAINS * PAIR_SLOTS
TILES = 512
PARTS = 2
BRICK_ROWS = 16
PART_ROWS = BRICK_ROWS // PARTS
LANES = 128
HALF = 64
SPOTS = 64
BLOCK_ROWS = PART_ROWS * SPOTS
HEAD_ROWS = 16
SENT_ROWS = BLOCK_ROWS + HEAD_ROWS
STEPS = 64
PLANES = 128
FULL = 32700.0
LOG_UNIT = 128.0
VMEM_BYTES = 48 * 1024 * 1024


def split_table(table):
    high = table.astype(ml_dtypes.bfloat16)
    low = (table - high.astype(np.float64)).astype(ml_dtypes.bfloat16)
    return high, low


def line_tables():
    index = np.arange(NY)
    angle = 2.0 * np.pi / NY * (index[:, None] * index[None, :] % NY)
    table = (np.cos(angle) + np.sin(angle)) / np.sqrt(NY)
    swapped = table.reshape(NY, NY // LANES, 2, HALF)[:, :, ::-1].reshape(NY, NY)
    return np.stack([*split_table(table), *split_table(swapped)])


def plane_tables():
    index = np.arange(PLANES)
    table = np.sqrt(2.0 / (PLANES + 1)) * np.sin(
        np.pi / (PLANES + 1) * ((index[:, None] + 1) * (index[None, :] + 1) % (2 * PLANES + 2))
    )
    plane_of = index % SLABS * CZ + index // SLABS % BZ * BZ + index // 32
    down = table[:, plane_of]
    both = []
    for each in (down, down.T):
        high, low = split_table(each)
        top = np.concatenate([high, high], axis=1)
        bottom = np.concatenate([low, np.zeros_like(low)], axis=1)
        both.append(np.concatenate([top, bottom], axis=0))
    return both


def mode_tables():
    mu = 2.0 - 2.0 * np.cos(np.pi / (PLANES + 1) * (np.arange(PLANES) + 1))
    base = np.broadcast_to((mu + 1.0 / (SCREEN * SCREEN))[:, None], (PLANES, LANES))
    lam = 2.0 - 2.0 * np.cos(2.0 * np.pi / NY * np.arange(NY))
    lam = lam.reshape(NY // HALF, HALF)
    return base.astype(np.float32), np.concatenate([lam, lam], axis=1).astype(np.float32)


def low_half(shape):
    return lax.broadcasted_iota(jnp.int32, shape, len(shape) - 1) < HALF


def split(values):
    high = values.astype(jnp.bfloat16)
    return high, (values - high.astype(jnp.float32)).astype(jnp.bfloat16)


def dot(left, right):
    return jnp.dot(left, right, preferred_element_type=jnp.float32)


def line_transform(load, store, table_ref):
    low = low_half((4 * SPOTS, LANES))
    for step in range(BLOCK_ROWS // (4 * SPOTS)):
        evens, odds = [], []
        for pair in range(4):
            first, second = load(2 * pair, step), load(2 * pair + 1, step)
            crossed = pltpu.roll(jnp.where(low, second, first), HALF, 1)
            evens.append(jnp.where(low, first, crossed))
            odds.append(jnp.where(low, crossed, second))
        products = []
        for lines, at in ((evens, 0), (odds, 2)):
            high, rest = split(jnp.concatenate(lines, axis=1))
            products.append(
                dot(high, table_ref[at]) + (dot(high, table_ref[at + 1]) + dot(rest, table_ref[at]))
            )
        for pair in range(4):
            even = products[0][:, pair * LANES : (pair + 1) * LANES]
            odd = products[1][:, pair * LANES : (pair + 1) * LANES]
            store(2 * pair, step, jnp.where(low, even, odd))
            store(2 * pair + 1, step, pltpu.roll(jnp.where(low, odd, even), HALF, 1))


def level_of(most):
    return jnp.floor(jnp.log2(jnp.maximum(most, 1e-30)) * LOG_UNIT) + 2.0


def inverse_of(level):
    return FULL * jnp.exp2(level * (-1.0 / LOG_UNIT))


def fixed_of(values):
    return jnp.floor(values + 0.5).astype(jnp.int32).astype(jnp.int16)


def head_of(level):
    return jnp.broadcast_to(level, (HEAD_ROWS, LANES)).astype(jnp.int32).astype(jnp.int16)


def unit_of(sent_ref, g):
    head = sent_ref[g, BLOCK_ROWS:SENT_ROWS, :].astype(jnp.int32).astype(jnp.float32)
    return jnp.exp2(head[0:1] * (1.0 / LOG_UNIT)) * (1.0 / FULL)


def wide(block):
    return block.astype(jnp.int32).astype(jnp.float32)


def pack_kernel(owner_ref, tile_ref, count_ref, brick_ref, first_ref, second_ref, slot_ref, rows_ref, slots_ref, head_ref, used_ref):
    brick_rows = brick_ref.shape[0]
    for q in range(BRICK_ROWS):
        block = brick_ref[:, q * LANES : (q + 1) * LANES].astype(jnp.float32)
        rows_ref[pl.ds(q, brick_rows, stride=BRICK_ROWS), :] = block
    head_ref[...] = jnp.full(head_ref.shape, float(TILES), jnp.float32)
    slots_ref[...] = jnp.zeros(slots_ref.shape, jnp.float32)
    for owner in range(DOMAINS):
        used_ref[owner] = 0

    def place(r, _):
        owner = owner_ref[r]
        within = used_ref[owner]
        used_ref[owner] = within + 1
        slot = owner * PAIR_SLOTS + within
        slot_ref[r] = slot
        tile = tile_ref[r]
        line = tile // 8
        position = tile % 8 * SPOTS + line % 16 * 4 + line // 16
        for part in range(PARTS):
            brick = rows_ref[pl.ds(pl.multiple_of(r * BRICK_ROWS + part * PART_ROWS, PART_ROWS), PART_ROWS), :]
            slots_ref[part, pl.ds(pl.multiple_of(slot * PART_ROWS, PART_ROWS), PART_ROWS), :] = brick
        head_ref[pl.ds(slot, 1), :] = jnp.full((1, LANES), position, jnp.int32).astype(jnp.float32)
        return 0

    count = count_ref[0]
    lax.fori_loop(0, count, place, 0)

    def rest(r, _):
        slot_ref[r] = 0
        return 0

    lax.fori_loop(count, brick_rows, rest, 0)
    pair_rows = PAIR_SLOTS * PART_ROWS
    for owner in range(DOMAINS):
        for part, out_ref in enumerate((first_ref, second_ref)):
            block = slots_ref[part, owner * pair_rows : (owner + 1) * pair_rows, :]
            out_ref[owner, :pair_rows, :] = block.astype(jnp.bfloat16)
        head = head_ref[owner * PAIR_SLOTS : (owner + 1) * PAIR_SLOTS, :]
        high = jnp.floor(head * (1.0 / 32.0))
        both = jnp.concatenate([high, head - 32.0 * high], axis=0)
        first_ref[owner, pair_rows:, :] = both.astype(jnp.bfloat16)


def picks_kernel(brick_ref, out_ref):
    pair_rows = PAIR_SLOTS * PART_ROWS
    for domain in range(DOMAINS):
        head = brick_ref[domain, pair_rows:, :].astype(jnp.float32)
        places = (head[:PAIR_SLOTS] * 32.0 + head[PAIR_SLOTS:]).astype(jnp.int32)
        for block in range(TILES // LANES):
            lane = lax.broadcasted_iota(jnp.int32, (PAIR_SLOTS, LANES), 1) + block * LANES
            out_ref[domain * PAIR_SLOTS : (domain + 1) * PAIR_SLOTS, block * LANES : (block + 1) * LANES] = (
                jnp.where(places == lane, 1.0, 0.0)
            )


def forward_body(brick_ref, picks, table_ref, sent_ref, slots_ref, charge_ref, lines_ref):
    pair_rows = PAIR_SLOTS * PART_ROWS
    for domain in range(DOMAINS):
        slots_ref[domain * pair_rows : (domain + 1) * pair_rows, :] = brick_ref[domain, :pair_rows, :].astype(jnp.float32)
    for q in range(0, PART_ROWS, 2):
        rows = [slots_ref[pl.ds(q + one, SLOTS, stride=PART_ROWS), :] for one in range(2)]
        both = lax.dot_general(
            picks,
            jnp.concatenate(rows, axis=1).astype(jnp.bfloat16),
            (((0,), (0,)), ((), ())),
            preferred_element_type=jnp.float32,
        )
        charge_ref[q] = both[:, :LANES]
        charge_ref[q + 1] = both[:, LANES:]

    def load(block, step):
        return charge_ref[step * 4 : step * 4 + 4, block * SPOTS : (block + 1) * SPOTS, :].reshape(4 * SPOTS, LANES)

    def store(block, step, values):
        lines_ref[block, step * 4 * SPOTS : (step + 1) * 4 * SPOTS, :] = values

    line_transform(load, store, table_ref)
    for g in range(SLABS):
        block = lines_ref[g]
        most = jnp.max(jnp.abs(block).reshape(BLOCK_ROWS // 8, 8, LANES), axis=0)
        level = level_of(jnp.max(most, axis=0, keepdims=True))
        sent_ref[g, :BLOCK_ROWS, :] = fixed_of(block * inverse_of(level))
        sent_ref[g, BLOCK_ROWS:, :] = head_of(level)


def first_kernel(brick_ref, table_ref, sent_ref, picks_ref, wide_ref, *scratch):
    picks_kernel(brick_ref, wide_ref)
    picks = wide_ref[...].astype(jnp.bfloat16)
    picks_ref[...] = picks
    forward_body(brick_ref, picks, table_ref, sent_ref, *scratch)


def second_kernel(brick_ref, picks_ref, table_ref, sent_ref, *scratch):
    forward_body(brick_ref, picks_ref[...], table_ref, sent_ref, *scratch)


def roots(base_ref, lam_ref):
    excess = base_ref[...] + lam_ref[...]
    spread = jnp.sqrt(excess * (excess + 4.0))
    root = 2.0 / (2.0 + excess + spread)
    return root, spread


def grid_rows(part, iz, xq, tx):
    return pl.ds(pl.multiple_of((part * BLOCK_ROWS + (iz * 4 + xq) * SPOTS + tx * 4) * SLABS, 32), 32)


def down_kernel(first_ref, second_ref, plane_ref, base_ref, lam_ref, walk_ref, end_ref, grid_ref, modes_ref, root_ref):
    for part, got_ref in enumerate((first_ref, second_ref)):
        for g in range(SLABS):
            block = wide(got_ref[g, :BLOCK_ROWS, :]) * unit_of(got_ref, g)
            grid_ref[pl.ds(part * BLOCK_ROWS * SLABS + g, BLOCK_ROWS, stride=SLABS), :] = block

    def planes(tx, xq):
        return jnp.concatenate(
            [grid_ref[grid_rows(part, iz, xq, tx), :] for part in range(PARTS) for iz in range(2)], axis=0
        )

    def sines(tx, _):
        for half in range(2):
            lines = jnp.concatenate([planes(tx, half * 2), planes(tx, half * 2 + 1)], axis=1)
            both = dot(plane_ref[...], jnp.concatenate(split(lines), axis=0))
            modes = both[:PLANES] + both[PLANES:]
            modes_ref[tx * 4 + half * 2] = modes[:, :LANES]
            modes_ref[tx * 4 + half * 2 + 1] = modes[:, LANES:]
        return 0

    lax.fori_loop(0, 16, sines, 0, unroll=4)
    root, _ = roots(base_ref, lam_ref)
    root_ref[...] = root

    part_rows = 64
    low = low_half((part_rows, LANES))
    for part in range(PLANES // part_rows):
        here = pl.ds(part * part_rows, part_rows)
        root = root_ref[here, :]
        square = root * root

        def walk(step, held):
            ahead, behind = modes_ref[step, here, :], modes_ref[STEPS - 1 - step, here, :]
            own = jnp.where(low, behind, ahead)
            other = pltpu.roll(jnp.where(low, ahead, behind), HALF, 1)
            held = square * held + (own + root * other)
            walk_ref[step, here, :] = held
            return held

        end_ref[here, :] = lax.fori_loop(0, STEPS, walk, jnp.zeros((part_rows, LANES), jnp.float32), unroll=4)


def up_kernel(place_ref, walk_ref, ends_ref, plane_ref, base_ref, lam_ref, first_ref, second_ref, full_ref, grid_ref, root_ref, gain_ref):
    group_count = ends_ref.shape[0]
    own = place_ref[0]
    root, spread = roots(base_ref, lam_ref)
    root_ref[...] = root
    gain_ref[...] = 1.0 / spread
    part_rows = 64
    low = low_half((part_rows, LANES))
    for part in range(PLANES // part_rows):
        here = pl.ds(part * part_rows, part_rows)
        root = root_ref[here, :]
        square = root * root
        across = square
        for _ in range(6):
            across = across * across
        entering = jnp.zeros((part_rows, LANES), jnp.float32)
        for step in range(group_count - 1, -1, -1):
            before = ends_ref[(own + 2 * group_count - 1 - step) % group_count, here, :]
            after = ends_ref[(own + 1 + step) % group_count, here, :]
            entering = entering * across + jnp.where(low, after, before)
        around = across
        for _ in range(2):
            around = around * around
        entering = entering / (1.0 - around)
        full_ref[0, here, :] = entering

        def carry(step, reach):
            full_ref[step + 1, here, :] = walk_ref[step, here, :] + reach
            return reach * square

        lax.fori_loop(0, STEPS, carry, entering * square, unroll=4)

    def solved(step):
        low = low_half((PLANES, LANES))
        near = jnp.where(low, full_ref[STEPS - step], full_ref[step + 1])
        far = jnp.where(low, full_ref[STEPS - 1 - step], full_ref[step])
        return gain_ref[...] * (near + root_ref[...] * pltpu.roll(far, HALF, 1))

    def sines(tx, _):
        for half in range(2):
            first = tx * 4 + half * 2
            modes = jnp.concatenate([solved(first), solved(first + 1)], axis=1)
            both = dot(plane_ref[...], jnp.concatenate(split(modes), axis=0))
            lines = both[:PLANES] + both[PLANES:]
            for one in range(2):
                for part in range(PARTS):
                    for iz in range(2):
                        at = part * 2 + iz
                        grid_ref[grid_rows(part, iz, half * 2 + one, tx), :] = lines[
                            at * 32 : (at + 1) * 32, one * LANES : (one + 1) * LANES
                        ]
        return 0

    lax.fori_loop(0, 16, sines, 0, unroll=4)
    for part, sent_ref in enumerate((first_ref, second_ref)):
        here = pl.ds(part * BLOCK_ROWS * SLABS, BLOCK_ROWS * SLABS)
        most = jnp.max(jnp.abs(grid_ref[here, :]).reshape(BLOCK_ROWS, SLABS, LANES), axis=0)
        level = level_of(most)
        inverse = inverse_of(level)
        for g in range(SLABS):
            block = grid_ref[pl.ds(part * BLOCK_ROWS * SLABS + g, BLOCK_ROWS, stride=SLABS), :]
            sent_ref[g, :BLOCK_ROWS, :] = fixed_of(block * inverse[g : g + 1])
            sent_ref[g, BLOCK_ROWS:, :] = head_of(level[g : g + 1])


def reply_kernel(got_ref, picks_ref, table_ref, out_ref, pot_ref, slots_ref):
    units = [unit_of(got_ref, g) for g in range(SLABS)]

    def load(block, step):
        return wide(got_ref[block, step * 4 * SPOTS : (step + 1) * 4 * SPOTS, :]) * units[block]

    def store(block, step, values):
        pot_ref[step * 4 : step * 4 + 4, block * SPOTS : (block + 1) * SPOTS, :] = (
            values.astype(jnp.bfloat16).reshape(4, SPOTS, LANES)
        )

    line_transform(load, store, table_ref)
    for q in range(0, PART_ROWS, 2):
        both = dot(picks_ref[...], jnp.concatenate([pot_ref[q], pot_ref[q + 1]], axis=1))
        for one in range(2):
            slots_ref[pl.ds(q + one, SLOTS, stride=PART_ROWS), :] = both[:, one * LANES : (one + 1) * LANES]
    pair_rows = PAIR_SLOTS * PART_ROWS
    for domain in range(DOMAINS):
        out_ref[domain] = slots_ref[domain * pair_rows : (domain + 1) * pair_rows, :].astype(jnp.bfloat16)


def unpack_kernel(slot_ref, count_ref, first_ref, second_ref, out_ref, slots_ref, rows_ref):
    brick_rows = out_ref.shape[0]
    pair_rows = PAIR_SLOTS * PART_ROWS
    rows_ref[...] = jnp.zeros(rows_ref.shape, jnp.float32)
    for domain in range(DOMAINS):
        for part, got_ref in enumerate((first_ref, second_ref)):
            slots_ref[part, domain * pair_rows : (domain + 1) * pair_rows, :] = got_ref[domain].astype(jnp.float32)

    def place(r, _):
        slot = slot_ref[r]
        for part in range(PARTS):
            brick = slots_ref[part, pl.ds(pl.multiple_of(slot * PART_ROWS, PART_ROWS), PART_ROWS), :]
            rows_ref[pl.ds(pl.multiple_of(r * BRICK_ROWS + part * PART_ROWS, PART_ROWS), PART_ROWS), :] = brick
        return 0

    lax.fori_loop(0, count_ref[0], place, 0)
    for q in range(BRICK_ROWS):
        block = rows_ref[pl.ds(q, brick_rows, stride=BRICK_ROWS), :]
        out_ref[:, q * LANES : (q + 1) * LANES] = block.astype(jnp.bfloat16)


def call(kernel, outs, places, scratch, operands, spaces, name):
    return pl.pallas_call(
        kernel,
        out_shape=outs,
        in_specs=[pl.BlockSpec(memory_space=space) for space in spaces],
        out_specs=[pl.BlockSpec(memory_space=space) for space in places],
        scratch_shapes=scratch,
        compiler_params=pltpu.CompilerParams(vmem_limit_bytes=VMEM_BYTES),
        name=name,
    )(*operands)


def on_device_8x4(bricks, owners, tile_ids, counts):
    V, S = pltpu.VMEM, pltpu.SMEM
    f32, bf16, i32, i16 = jnp.float32, jnp.bfloat16, jnp.int32, jnp.int16
    shape = jax.ShapeDtypeStruct
    brick_rows = bricks.shape[0]
    line_table = jnp.asarray(line_tables())
    plane_down, plane_up = (jnp.asarray(each) for each in plane_tables())
    base, lam_all = (jnp.asarray(each) for each in mode_tables())
    lam = lax.dynamic_slice_in_dim(lam_all, lax.axis_index("gz"), 1, 0)
    place = lax.axis_index("ma").astype(i32).reshape(1)
    pair_rows = PAIR_SLOTS * PART_ROWS

    def all_ways(values):
        return lax.all_to_all(values, ("gz", "ma"), split_axis=0, concat_axis=0, tiled=True)

    def over_slabs(values):
        return lax.all_to_all(values, "gz", split_axis=0, concat_axis=0, tiled=True)

    first, second, slots = call(
        pack_kernel,
        [
            shape((DOMAINS, pair_rows + HEAD_ROWS, LANES), bf16),
            shape((DOMAINS, pair_rows, LANES), bf16),
            shape((brick_rows,), i32),
        ],
        [V, V, S],
        [
            V((brick_rows * BRICK_ROWS, LANES), f32),
            V((PARTS, SLOTS * PART_ROWS, LANES), f32),
            V((SLOTS, LANES), f32),
            S((DOMAINS,), i32),
        ],
        (owners.reshape(brick_rows), tile_ids, counts, bricks),
        [S, S, S, V],
        "pack",
    )
    first, second = all_ways(first), all_ways(second)
    sent_shape = shape((SLABS, SENT_ROWS, LANES), i16)
    forward_scratch = [
        V((SLOTS * PART_ROWS, LANES), f32),
        V((PART_ROWS, TILES, LANES), f32),
        V((SLABS, BLOCK_ROWS, LANES), f32),
    ]
    sent_first, picks = call(
        first_kernel,
        [sent_shape, shape((SLOTS, TILES), bf16)],
        [V, V],
        [V((SLOTS, TILES), f32), *forward_scratch],
        (first, line_table),
        [V, V],
        "forward_first",
    )
    got_first = over_slabs(sent_first)
    (sent_second,) = call(
        second_kernel, [sent_shape], [V], forward_scratch, (second, picks, line_table), [V, V, V], "forward_second"
    )
    got_second = over_slabs(sent_second)
    cube = (STEPS, PLANES, LANES)
    flat = V((PLANES, LANES), f32)
    grid = V((PARTS * BLOCK_ROWS * SLABS, LANES), f32)
    walk, end = call(
        down_kernel,
        [shape(cube, f32), shape((PLANES, LANES), f32)],
        [V, V],
        [grid, V(cube, f32), flat],
        (got_first, got_second, plane_down, base, lam),
        [V, V, V, V, V],
        "down",
    )
    ends = lax.all_gather(end, "ma", axis=0, tiled=False)
    sent = call(
        up_kernel,
        [sent_shape, sent_shape],
        [V, V],
        [V((STEPS + 1, PLANES, LANES), f32), grid, flat, flat],
        (place, walk, ends, plane_up, base, lam),
        [S, V, V, V, V, V],
        "up",
    )
    returned = []
    for part, name in enumerate(("reply_first", "reply_second")):
        (replies,) = call(
            reply_kernel,
            [shape((DOMAINS, pair_rows, LANES), bf16)],
            [V],
            [V((PART_ROWS, TILES, LANES), bf16), V((SLOTS * PART_ROWS, LANES), f32)],
            (over_slabs(sent[part]), picks, line_table),
            [V, V, V],
            name,
        )
        returned.append(all_ways(replies))
    (result,) = call(
        unpack_kernel,
        [shape((brick_rows, BRICK_ROWS * LANES), bf16)],
        [V],
        [V((PARTS, SLOTS * PART_ROWS, LANES), f32), V((brick_rows * BRICK_ROWS, LANES), f32)],
        (slots, counts, *returned),
        [S, S, V, V],
        "unpack",
    )
    return result


def solution(mesh):
    in_specs = (P(("gz", "ma"), None), P(("gz", "ma"), None), P(("gz", "ma")), P(("gz", "ma")))
    out_specs = P(("gz", "ma"), None)
    body = on_device_8x4 if (mesh.shape["gz"], mesh.shape["ma"]) == (8, 4) else on_device
    return jax.shard_map(body, mesh=mesh, in_specs=in_specs, out_specs=out_specs, check_vma=False)
```

```python
import math

import jax
import jax.numpy as jnp
import ml_dtypes
import numpy as np
from jax import lax
from jax.experimental import pallas as pl
from jax.experimental.pallas import tpu as pltpu
from jax.sharding import PartitionSpec as P

NX = 512
NY = 512
SCREEN = 16
BZ = 4
BX = 8
BY = 64
CZ = 16


def hartley(length):
    indices = jnp.arange(length, dtype=jnp.int32)
    products = indices[:, None] * indices[None, :] % length
    angles = 2.0 * math.pi / length * products.astype(jnp.float32)
    return (jnp.cos(angles) + jnp.sin(angles)) / math.sqrt(length)


def second_difference(length, indices):
    return 2.0 - 2.0 * jnp.cos(2.0 * math.pi / length * indices.astype(jnp.float32))


def thomas(right_side, diagonal):
    start_zero = jnp.zeros(right_side.shape[1:], jnp.float32)

    def down(state_pair, plane):
        factor = 1.0 / (diagonal - state_pair[0])
        partial_value = (plane + state_pair[1]) * factor
        return ((factor, partial_value), (factor, partial_value))

    _, (factors, partials) = lax.scan(down, (start_zero, start_zero), right_side)

    def upward(beyond, factor_partial):
        solved = factor_partial[1] + factor_partial[0] * beyond
        return (solved, solved)

    _, solutions = lax.scan(upward, start_zero, (factors, partials), reverse=True)
    return solutions


def regroup(values):
    return lax.all_to_all(values, "ma", split_axis=2, concat_axis=1, tiled=True)


def on_device(bricks, owners, tile_ids, counts):
    domains = lax.axis_size(("gz", "ma"))
    group_count = lax.axis_size("ma")
    slab_count = lax.axis_size("gz")
    brick_rows, brick_cells = bricks.shape
    slot_count = max(2, 2 * brick_rows // domains)
    local_x = NX // group_count
    local_y = NY // group_count
    tiles_dev = CZ // BZ * (local_x // BX) * (NY // BY)
    highest = lax.Precision.HIGHEST
    target = owners[:, 0]
    row_order = jnp.arange(brick_rows, dtype=jnp.int32)
    earlier_same = (target[:, None] == target[None, :]) & (row_order[None, :] < row_order[:, None])
    within = jnp.sum(earlier_same.astype(jnp.int32), axis=1)
    slot_of = target * slot_count + within
    is_live = row_order < counts[0]
    loaded = jnp.where(is_live[:, None], bricks, jnp.zeros_like(bricks))
    outgoing = jnp.zeros((domains * slot_count, brick_cells), jnp.bfloat16).at[slot_of].set(loaded)
    out_ids = jnp.full((domains * slot_count,), tiles_dev, jnp.int32).at[slot_of].set(tile_ids)
    incoming, in_ids = (
        lax.all_to_all(outgoing, ("gz", "ma"), split_axis=0, concat_axis=0, tiled=True),
        lax.all_to_all(out_ids, ("gz", "ma"), split_axis=0, concat_axis=0, tiled=True),
    )
    picker = (jnp.arange(tiles_dev, dtype=jnp.int32)[:, None] == in_ids[None, :]).astype(
        jnp.bfloat16
    )
    deposit = jnp.dot(picker, incoming, preferred_element_type=jnp.float32)
    charge = deposit.reshape(CZ // BZ, local_x // BX, NY // BY, BZ, BX, BY)
    charge = charge.transpose(0, 3, 1, 4, 2, 5).reshape(CZ, local_x, NY)
    table_x = hartley(NX)
    table_y = hartley(NY)
    along_y = jnp.einsum("zxy,ky->zxk", charge, table_y, precision=highest)
    gathered_x = regroup(along_y)
    spectrum = jnp.einsum("zxk,jx->zjk", gathered_x, table_x, precision=highest)
    columns = lax.axis_index("ma") * local_y + jnp.arange(local_y, dtype=jnp.int32)
    lam_y = second_difference(NY, columns)
    screening = 1.0 / (SCREEN * SCREEN)
    slab_index = lax.axis_index("gz")
    lam_x = second_difference(NX, jnp.arange(NX, dtype=jnp.int32))
    diagonal = 2.0 + screening + lam_x[:, None] + lam_y[None, :]
    interior = spectrum[1:]
    particular = thomas(interior, diagonal)
    unit_rhs = jnp.zeros_like(interior).at[0].set(1.0)
    spike = thomas(unit_rhs, diagonal)
    near_weight = spike[0]
    far_weight = spike[-1]
    head_term = spectrum[0] + particular[0]
    tail_term = particular[-1]
    reduced_first = diagonal - near_weight
    reduced_rest = diagonal - 2.0 * near_weight
    start_zero = jnp.zeros_like(diagonal)
    heads, tails = (
        lax.all_gather(head_term[None], "gz", axis=0, tiled=True),
        lax.all_gather(tail_term[None], "gz", axis=0, tiled=True),
    )
    before = jnp.concatenate([start_zero[None], tails[:-1]], axis=0)
    sources = heads + before

    def chain_down(state_pair, packed):
        source, position = packed
        base_term = jnp.where(position == 0, reduced_first, reduced_rest)
        pivot_now = 1.0 / (base_term - far_weight * far_weight * state_pair[0])
        forward_part = pivot_now * (source + far_weight * state_pair[1])
        return ((pivot_now, forward_part), (pivot_now, forward_part))

    _, (pivots, forwards) = lax.scan(
        chain_down, (start_zero, start_zero), (sources, jnp.arange(slab_count, dtype=jnp.int32))
    )

    def chain_up(beyond, packed):
        plane_value = packed[1] + far_weight * packed[0] * beyond
        return (plane_value, plane_value)

    _, separators = lax.scan(chain_up, start_zero, (pivots, forwards), reverse=True)
    padded_sep = jnp.concatenate([separators, start_zero[None]], axis=0)
    own_plane = lax.dynamic_index_in_dim(padded_sep, slab_index, 0, keepdims=False)
    next_plane = lax.dynamic_index_in_dim(padded_sep, slab_index + 1, 0, keepdims=False)
    interior_sol = particular + own_plane[None] * spike + next_plane[None] * spike[::-1]
    modal = jnp.concatenate([own_plane[None], interior_sol], axis=0)
    back_x = jnp.einsum("zjk,jx->zkx", modal, table_x, precision=highest)
    gathered_y = regroup(back_x)
    potential = jnp.einsum("zkx,ky->zxy", gathered_y, table_y, precision=highest)
    pot_tiles = potential.reshape(CZ // BZ, BZ, local_x // BX, BX, NY // BY, BY)
    pot_tiles = (
        pot_tiles.transpose(0, 2, 4, 1, 3, 5).reshape(tiles_dev, brick_cells).astype(jnp.bfloat16)
    )
    padded_tiles = jnp.concatenate([pot_tiles, jnp.zeros((1, brick_cells), jnp.bfloat16)], axis=0)
    replies = padded_tiles[in_ids]
    returned = lax.all_to_all(replies, ("gz", "ma"), split_axis=0, concat_axis=0, tiled=True)
    result = returned[slot_of]
    return jnp.where(is_live[:, None], result, jnp.zeros_like(result))


DOMAINS = 32
SLABS = 8
PAIR_SLOTS = 8
SLOTS = DOMAINS * PAIR_SLOTS
TILES = 512
PARTS = 1
BRICK_ROWS = 16
PART_ROWS = BRICK_ROWS // PARTS
PART_PLANES = BZ // PARTS
LANES = 128
HALF = 64
SPOTS = 64
BLOCK_ROWS = PART_ROWS * SPOTS
HEAD_ROWS = 16
SENT_ROWS = BLOCK_ROWS + HEAD_ROWS
STEPS = 64
PLANES = 128
FULL = 32700.0
LOG_UNIT = 128.0
VMEM_BYTES = 48 * 1024 * 1024


def split_table(table):
    high = table.astype(ml_dtypes.bfloat16)
    low = (table - high.astype(np.float64)).astype(ml_dtypes.bfloat16)
    return high, low


def line_tables():
    index = np.arange(NY)
    angle = 2.0 * np.pi / NY * (index[:, None] * index[None, :] % NY)
    table = (np.cos(angle) + np.sin(angle)) / np.sqrt(NY)
    swapped = table.reshape(NY, NY // LANES, 2, HALF)[:, :, ::-1].reshape(NY, NY)
    return np.stack([*split_table(table), *split_table(swapped)])


def plane_tables():
    index = np.arange(PLANES)
    table = np.sqrt(2.0 / (PLANES + 1)) * np.sin(
        np.pi / (PLANES + 1) * ((index[:, None] + 1) * (index[None, :] + 1) % (2 * PLANES + 2))
    )
    plane_of = index % SLABS * CZ + index // SLABS % BZ * BZ + index // 32
    down = table[:, plane_of]
    both = []
    for each in (down, down.T):
        high, low = split_table(each)
        top = np.concatenate([high, high], axis=1)
        bottom = np.concatenate([low, np.zeros_like(low)], axis=1)
        both.append(np.concatenate([top, bottom], axis=0))
    return both


def mode_tables():
    mu = 2.0 - 2.0 * np.cos(np.pi / (PLANES + 1) * (np.arange(PLANES) + 1))
    base = np.broadcast_to((mu + 1.0 / (SCREEN * SCREEN))[:, None], (PLANES, LANES))
    lam = 2.0 - 2.0 * np.cos(2.0 * np.pi / NY * np.arange(NY))
    lam = lam.reshape(NY // HALF, HALF)
    return base.astype(np.float32), np.concatenate([lam, lam], axis=1).astype(np.float32)


def low_half(shape):
    return lax.broadcasted_iota(jnp.int32, shape, len(shape) - 1) < HALF


def split(values):
    high = values.astype(jnp.bfloat16)
    return high, (values - high.astype(jnp.float32)).astype(jnp.bfloat16)


def dot(left, right):
    return jnp.dot(left, right, preferred_element_type=jnp.float32)


def line_transform(load, store, table_ref):
    low = low_half((4 * SPOTS, LANES))
    for step in range(BLOCK_ROWS // (4 * SPOTS)):
        evens, odds = [], []
        for pair in range(4):
            first, second = load(2 * pair, step), load(2 * pair + 1, step)
            crossed = pltpu.roll(jnp.where(low, second, first), HALF, 1)
            evens.append(jnp.where(low, first, crossed))
            odds.append(jnp.where(low, crossed, second))
        products = []
        for lines, at in ((evens, 0), (odds, 2)):
            high, rest = split(jnp.concatenate(lines, axis=1))
            products.append(
                dot(high, table_ref[at]) + (dot(high, table_ref[at + 1]) + dot(rest, table_ref[at]))
            )
        for pair in range(4):
            even = products[0][:, pair * LANES : (pair + 1) * LANES]
            odd = products[1][:, pair * LANES : (pair + 1) * LANES]
            store(2 * pair, step, jnp.where(low, even, odd))
            store(2 * pair + 1, step, pltpu.roll(jnp.where(low, odd, even), HALF, 1))


def level_of(most):
    return jnp.floor(jnp.log2(jnp.maximum(most, 1e-30)) * LOG_UNIT) + 2.0


def inverse_of(level):
    return FULL * jnp.exp2(level * (-1.0 / LOG_UNIT))


def fixed_of(values):
    return jnp.floor(values + 0.5).astype(jnp.int32).astype(jnp.int16)


def head_of(level):
    return jnp.broadcast_to(level, (HEAD_ROWS, LANES)).astype(jnp.int32).astype(jnp.int16)


def unit_of(sent_ref):
    head = sent_ref[BLOCK_ROWS:SENT_ROWS, :].astype(jnp.int32).astype(jnp.float32)
    return jnp.exp2(head[0:1] * (1.0 / LOG_UNIT)) * (1.0 / FULL)


def wide(block):
    return block.astype(jnp.int32).astype(jnp.float32)


def pack_kernel(owner_in, tile_in, count_in, brick_in, *refs):
    out_refs, slot_ref = refs[:PARTS], refs[PARTS]
    owner_ref, tile_ref, count_ref, brick_ref, rows_ref, slots_ref, head_ref, used_ref, sems = refs[PARTS + 1 :]
    copies = [
        pltpu.make_async_copy(source, place, sems.at[at])
        for at, (source, place) in enumerate(
            ((brick_in, brick_ref), (owner_in, owner_ref), (tile_in, tile_ref), (count_in, count_ref))
        )
    ]
    for each in copies:
        each.start()
    brick_rows = brick_ref.shape[0]
    head_ref[...] = jnp.full(head_ref.shape, float(TILES), jnp.float32)
    slots_ref[...] = jnp.zeros(slots_ref.shape, jnp.float32)
    for owner in range(DOMAINS):
        used_ref[owner] = 0
    for each in copies:
        each.wait()
    for q in range(BRICK_ROWS):
        block = brick_ref[:, q * LANES : (q + 1) * LANES].astype(jnp.float32)
        rows_ref[pl.ds(q, brick_rows, stride=BRICK_ROWS), :] = block

    def place(r, _):
        owner = owner_ref[r]
        within = used_ref[owner]
        used_ref[owner] = within + 1
        slot = owner * PAIR_SLOTS + within
        slot_ref[r] = slot
        tile = tile_ref[r]
        line = tile // 8
        position = tile % 8 * SPOTS + line % 16 * 4 + line // 16
        for part in range(PARTS):
            brick = rows_ref[pl.ds(pl.multiple_of(r * BRICK_ROWS + part * PART_ROWS, PART_ROWS), PART_ROWS), :]
            slots_ref[part, pl.ds(pl.multiple_of(slot * PART_ROWS, PART_ROWS), PART_ROWS), :] = brick
        head_ref[pl.ds(slot, 1), :] = jnp.full((1, LANES), position, jnp.int32).astype(jnp.float32)
        return 0

    count = count_ref[0]
    lax.fori_loop(0, count, place, 0)

    def rest(r, _):
        slot_ref[r] = 0
        return 0

    lax.fori_loop(count, brick_rows, rest, 0)
    pair_rows = PAIR_SLOTS * PART_ROWS
    for owner in range(DOMAINS):
        for part, out_ref in enumerate(out_refs):
            block = slots_ref[part, owner * pair_rows : (owner + 1) * pair_rows, :]
            out_ref[owner, :pair_rows, :] = block.astype(jnp.bfloat16)
        head = head_ref[owner * PAIR_SLOTS : (owner + 1) * PAIR_SLOTS, :]
        high = jnp.floor(head * (1.0 / 32.0))
        both = jnp.concatenate([high, head - 32.0 * high], axis=0)
        out_refs[0][owner, pair_rows:, :] = both.astype(jnp.bfloat16)


def picks_kernel(brick_ref, out_ref):
    pair_rows = PAIR_SLOTS * PART_ROWS
    for domain in range(DOMAINS):
        head = brick_ref[domain, pair_rows:, :].astype(jnp.float32)
        places = (head[:PAIR_SLOTS] * 32.0 + head[PAIR_SLOTS:]).astype(jnp.int32)
        for block in range(TILES // LANES):
            lane = lax.broadcasted_iota(jnp.int32, (PAIR_SLOTS, LANES), 1) + block * LANES
            out_ref[domain * PAIR_SLOTS : (domain + 1) * PAIR_SLOTS, block * LANES : (block + 1) * LANES] = (
                jnp.where(places == lane, 1.0, 0.0)
            )


def forward_body(own_ref, brick_ref, picks, table_ref, sent_refs, slots_ref, charge_ref, lines_ref):
    pair_rows = PAIR_SLOTS * PART_ROWS
    for domain in range(DOMAINS):
        slots_ref[domain * pair_rows : (domain + 1) * pair_rows, :] = brick_ref[domain, :pair_rows, :].astype(jnp.float32)
    for q in range(0, PART_ROWS, 2):
        rows = [slots_ref[pl.ds(q + one, SLOTS, stride=PART_ROWS), :] for one in range(2)]
        both = lax.dot_general(
            picks,
            jnp.concatenate(rows, axis=1).astype(jnp.bfloat16),
            (((0,), (0,)), ((), ())),
            preferred_element_type=jnp.float32,
        )
        charge_ref[q] = both[:, :LANES]
        charge_ref[q + 1] = both[:, LANES:]

    def load(block, step):
        return charge_ref[step * 4 : step * 4 + 4, block * SPOTS : (block + 1) * SPOTS, :].reshape(4 * SPOTS, LANES)

    def store(block, step, values):
        lines_ref[block, step * 4 * SPOTS : (step + 1) * 4 * SPOTS, :] = values

    line_transform(load, store, table_ref)
    for offset, sent_ref in enumerate(sent_refs):
        block = lines_ref[own_ref[0] ^ offset]
        most = jnp.max(jnp.abs(block).reshape(BLOCK_ROWS // 8, 8, LANES), axis=0)
        level = level_of(jnp.max(most, axis=0, keepdims=True))
        sent_ref[:BLOCK_ROWS, :] = fixed_of(block * inverse_of(level))
        sent_ref[BLOCK_ROWS:, :] = head_of(level)


def first_kernel(own_ref, brick_ref, table_ref, *refs):
    sent_refs, picks_ref, wide_ref = refs[:SLABS], refs[SLABS], refs[SLABS + 1]
    picks_kernel(brick_ref, wide_ref)
    picks = wide_ref[...].astype(jnp.bfloat16)
    picks_ref[...] = picks
    forward_body(own_ref, brick_ref, picks, table_ref, sent_refs, *refs[SLABS + 2 :])


def later_kernel(own_ref, brick_ref, picks_ref, table_ref, *refs):
    forward_body(own_ref, brick_ref, picks_ref[...], table_ref, refs[:SLABS], *refs[SLABS:])


def roots(base_ref, lam_ref):
    excess = base_ref[...] + lam_ref[...]
    spread = jnp.sqrt(excess * (excess + 4.0))
    root = 2.0 / (2.0 + excess + spread)
    return root, spread


def grid_rows(part, iz, xq, tx):
    return pl.ds(pl.multiple_of((part * BLOCK_ROWS + (iz * 4 + xq) * SPOTS + tx * 4) * SLABS, 32), 32)


def down_kernel(own_ref, *refs):
    got_refs = refs[: PARTS * SLABS]
    plane_ref, base_ref, lam_ref, walk_ref, end_ref, grid_ref, modes_ref, root_ref = refs[PARTS * SLABS :]
    for at, got_ref in enumerate(got_refs):
        part, offset = at // SLABS, at % SLABS
        block = wide(got_ref[:BLOCK_ROWS, :]) * unit_of(got_ref)
        start = part * BLOCK_ROWS * SLABS + (own_ref[0] ^ offset)
        grid_ref[pl.ds(start, BLOCK_ROWS, stride=SLABS), :] = block

    def planes(tx, xq):
        return jnp.concatenate(
            [grid_ref[grid_rows(part, iz, xq, tx), :] for part in range(PARTS) for iz in range(PART_PLANES)], axis=0
        )

    def sines(tx, _):
        for half in range(2):
            lines = jnp.concatenate([planes(tx, half * 2), planes(tx, half * 2 + 1)], axis=1)
            both = dot(plane_ref[...], jnp.concatenate(split(lines), axis=0))
            modes = both[:PLANES] + both[PLANES:]
            modes_ref[tx * 4 + half * 2] = modes[:, :LANES]
            modes_ref[tx * 4 + half * 2 + 1] = modes[:, LANES:]
        return 0

    lax.fori_loop(0, 16, sines, 0, unroll=4)
    root, _ = roots(base_ref, lam_ref)
    root_ref[...] = root

    part_rows = 64
    low = low_half((part_rows, LANES))
    for part in range(PLANES // part_rows):
        here = pl.ds(part * part_rows, part_rows)
        root = root_ref[here, :]
        square = root * root

        def walk(step, held):
            ahead, behind = modes_ref[step, here, :], modes_ref[STEPS - 1 - step, here, :]
            own = jnp.where(low, behind, ahead)
            other = pltpu.roll(jnp.where(low, ahead, behind), HALF, 1)
            held = square * held + (own + root * other)
            walk_ref[step, here, :] = held
            return held

        end_ref[here, :] = lax.fori_loop(0, STEPS, walk, jnp.zeros((part_rows, LANES), jnp.float32), unroll=4)


def up_kernel(own_ref, walk_ref, *refs):
    group_count = 4
    end_refs, (plane_ref, base_ref, lam_ref) = refs[:group_count], refs[group_count : group_count + 3]
    sent_refs = refs[group_count + 3 : group_count + 3 + PARTS * SLABS]
    full_ref, grid_ref, root_ref, gain_ref, level_ref, inverse_ref = refs[group_count + 3 + PARTS * SLABS :]
    root, spread = roots(base_ref, lam_ref)
    root_ref[...] = root
    gain_ref[...] = 1.0 / spread
    part_rows = 64
    low = low_half((part_rows, LANES))
    for part in range(PLANES // part_rows):
        here = pl.ds(part * part_rows, part_rows)
        root = root_ref[here, :]
        square = root * root
        across = square
        for _ in range(6):
            across = across * across
        entering = jnp.zeros((part_rows, LANES), jnp.float32)
        for step in range(group_count - 1, -1, -1):
            before = end_refs[(step + 1) % group_count][here, :]
            after = end_refs[group_count - 1 - step][here, :]
            entering = entering * across + jnp.where(low, after, before)
        around = across
        for _ in range(2):
            around = around * around
        entering = entering / (1.0 - around)
        full_ref[0, here, :] = entering

        def carry(step, reach):
            full_ref[step + 1, here, :] = walk_ref[step, here, :] + reach
            return reach * square

        lax.fori_loop(0, STEPS, carry, entering * square, unroll=4)

    def solved(step):
        low = low_half((PLANES, LANES))
        near = jnp.where(low, full_ref[STEPS - step], full_ref[step + 1])
        far = jnp.where(low, full_ref[STEPS - 1 - step], full_ref[step])
        return gain_ref[...] * (near + root_ref[...] * pltpu.roll(far, HALF, 1))

    def sines(tx, _):
        for half in range(2):
            first = tx * 4 + half * 2
            modes = jnp.concatenate([solved(first), solved(first + 1)], axis=1)
            both = dot(plane_ref[...], jnp.concatenate(split(modes), axis=0))
            lines = both[:PLANES] + both[PLANES:]
            for one in range(2):
                for part in range(PARTS):
                    for iz in range(PART_PLANES):
                        at = part * PART_PLANES + iz
                        grid_ref[grid_rows(part, iz, half * 2 + one, tx), :] = lines[
                            at * 32 : (at + 1) * 32, one * LANES : (one + 1) * LANES
                        ]
        return 0

    lax.fori_loop(0, 16, sines, 0, unroll=4)
    for part in range(PARTS):
        here = pl.ds(part * BLOCK_ROWS * SLABS, BLOCK_ROWS * SLABS)
        most = jnp.max(jnp.abs(grid_ref[here, :]).reshape(BLOCK_ROWS, SLABS, LANES), axis=0)
        level_ref[...] = level_of(most)
        inverse_ref[...] = inverse_of(level_of(most))
        for offset in range(SLABS):
            sent_ref = sent_refs[part * SLABS + offset]
            g = own_ref[0] ^ offset
            block = grid_ref[pl.ds(part * BLOCK_ROWS * SLABS + g, BLOCK_ROWS, stride=SLABS), :]
            sent_ref[:BLOCK_ROWS, :] = fixed_of(block * inverse_ref[pl.ds(g, 1), :])
            sent_ref[BLOCK_ROWS:, :] = head_of(level_ref[pl.ds(g, 1), :])


def reply_kernel(own_ref, *refs):
    got_refs = refs[:SLABS]
    picks_ref, table_ref, out_ref, lines_ref, pot_ref, slots_ref = refs[SLABS:]
    for offset, got_ref in enumerate(got_refs):
        lines_ref[own_ref[0] ^ offset] = wide(got_ref[:BLOCK_ROWS, :]) * unit_of(got_ref)

    def load(block, step):
        return lines_ref[block, step * 4 * SPOTS : (step + 1) * 4 * SPOTS, :]

    def store(block, step, values):
        pot_ref[step * 4 : step * 4 + 4, block * SPOTS : (block + 1) * SPOTS, :] = (
            values.astype(jnp.bfloat16).reshape(4, SPOTS, LANES)
        )

    line_transform(load, store, table_ref)
    for q in range(0, PART_ROWS, 2):
        both = dot(picks_ref[...], jnp.concatenate([pot_ref[q], pot_ref[q + 1]], axis=1))
        for one in range(2):
            slots_ref[pl.ds(q + one, SLOTS, stride=PART_ROWS), :] = both[:, one * LANES : (one + 1) * LANES]
    pair_rows = PAIR_SLOTS * PART_ROWS
    for domain in range(DOMAINS):
        out_ref[domain] = slots_ref[domain * pair_rows : (domain + 1) * pair_rows, :].astype(jnp.bfloat16)


def unpack_kernel(slot_ref, count_ref, *refs):
    got_refs, (out_ref, slots_ref, rows_ref) = refs[:PARTS], refs[PARTS:]
    brick_rows = out_ref.shape[0]
    pair_rows = PAIR_SLOTS * PART_ROWS
    rows_ref[...] = jnp.zeros(rows_ref.shape, jnp.float32)
    for domain in range(DOMAINS):
        for part, got_ref in enumerate(got_refs):
            slots_ref[part, domain * pair_rows : (domain + 1) * pair_rows, :] = got_ref[domain].astype(jnp.float32)

    def place(r, _):
        slot = slot_ref[r]
        for part in range(PARTS):
            brick = slots_ref[part, pl.ds(pl.multiple_of(slot * PART_ROWS, PART_ROWS), PART_ROWS), :]
            rows_ref[pl.ds(pl.multiple_of(r * BRICK_ROWS + part * PART_ROWS, PART_ROWS), PART_ROWS), :] = brick
        return 0

    lax.fori_loop(0, count_ref[0], place, 0)
    for q in range(BRICK_ROWS):
        block = rows_ref[pl.ds(q, brick_rows, stride=BRICK_ROWS), :]
        out_ref[:, q * LANES : (q + 1) * LANES] = block.astype(jnp.bfloat16)


def call(kernel, outs, places, scratch, operands, spaces, name):
    return pl.pallas_call(
        kernel,
        out_shape=outs,
        in_specs=[pl.BlockSpec(memory_space=space) for space in spaces],
        out_specs=[pl.BlockSpec(memory_space=space) for space in places],
        scratch_shapes=scratch,
        compiler_params=pltpu.CompilerParams(vmem_limit_bytes=VMEM_BYTES),
        name=name,
    )(*operands)


def on_device_8x4(bricks, owners, tile_ids, counts):
    V, S, A = pltpu.VMEM, pltpu.SMEM, pl.ANY
    f32, bf16, i32, i16 = jnp.float32, jnp.bfloat16, jnp.int32, jnp.int16
    shape = jax.ShapeDtypeStruct
    brick_rows = bricks.shape[0]
    line_table = jnp.asarray(line_tables())
    plane_down, plane_up = (jnp.asarray(each) for each in plane_tables())
    base, lam_all = (jnp.asarray(each) for each in mode_tables())
    lam = lax.dynamic_slice_in_dim(lam_all, lax.axis_index("gz"), 1, 0)
    own = lax.axis_index("gz").astype(i32).reshape(1)
    pair_rows = PAIR_SLOTS * PART_ROWS

    def all_ways(values):
        return lax.all_to_all(values, ("gz", "ma"), split_axis=0, concat_axis=0, tiled=True)

    def over_slabs(values):
        return [values[0]] + [
            lax.ppermute(values[offset], "gz", [(g, g ^ offset) for g in range(SLABS)])
            for offset in range(1, SLABS)
        ]

    def round_groups(values):
        return [values] + [
            lax.ppermute(values, "ma", [(m, (m + step) % 4) for m in range(4)]) for step in range(1, 4)
        ]

    *outgoing, slots = call(
        pack_kernel,
        [shape((DOMAINS, pair_rows + (HEAD_ROWS if part == 0 else 0), LANES), bf16) for part in range(PARTS)]
        + [shape((brick_rows,), i32)],
        [V] * PARTS + [S],
        [
            S((brick_rows,), i32),
            S((brick_rows,), i32),
            S((1,), i32),
            V(bricks.shape, bf16),
            V((brick_rows * BRICK_ROWS, LANES), f32),
            V((PARTS, SLOTS * PART_ROWS, LANES), f32),
            V((SLOTS, LANES), f32),
            S((DOMAINS,), i32),
            pltpu.SemaphoreType.DMA((4,)),
        ],
        (owners.reshape(brick_rows), tile_ids, counts, bricks),
        [A, A, A, A],
        "pack",
    )
    sent_shapes = [shape((SENT_ROWS, LANES), i16)] * SLABS
    forward_scratch = [
        V((SLOTS * PART_ROWS, LANES), f32),
        V((PART_ROWS, TILES, LANES), f32),
        V((SLABS, BLOCK_ROWS, LANES), f32),
    ]
    incoming = [all_ways(each) for each in outgoing]
    *sent, picks = call(
        first_kernel,
        sent_shapes + [shape((SLOTS, TILES), bf16)],
        [V] * (SLABS + 1),
        [V((SLOTS, TILES), f32), *forward_scratch],
        (own, incoming[0], line_table),
        [S, V, V],
        "forward",
    )
    got = over_slabs(sent)
    for each in incoming[1:]:
        sent = call(
            later_kernel,
            sent_shapes,
            [V] * SLABS,
            forward_scratch,
            (own, each, picks, line_table),
            [S, V, V, V],
            "forward_later",
        )
        got += over_slabs(sent)
    cube = (STEPS, PLANES, LANES)
    flat = V((PLANES, LANES), f32)
    grid = V((PARTS * BLOCK_ROWS * SLABS, LANES), f32)
    walk, end = call(
        down_kernel,
        [shape(cube, f32), shape((PLANES, LANES), f32)],
        [V, V],
        [grid, V(cube, f32), flat],
        (own, *got, plane_down, base, lam),
        [S] + [V] * (len(got) + 3),
        "down",
    )
    sent = call(
        up_kernel,
        sent_shapes * PARTS,
        [V] * (PARTS * SLABS),
        [V((STEPS + 1, PLANES, LANES), f32), grid, flat, flat, V((SLABS, LANES), f32), V((SLABS, LANES), f32)],
        (own, walk, *round_groups(end), plane_up, base, lam),
        [S] + [V] * 8,
        "up",
    )
    returned = []
    for part in range(PARTS):
        (replies,) = call(
            reply_kernel,
            [shape((DOMAINS, pair_rows, LANES), bf16)],
            [V],
            [
                V((SLABS, BLOCK_ROWS, LANES), f32),
                V((PART_ROWS, TILES, LANES), bf16),
                V((SLOTS * PART_ROWS, LANES), f32),
            ],
            (own, *over_slabs(sent[part * SLABS : (part + 1) * SLABS]), picks, line_table),
            [S] + [V] * (SLABS + 2),
            "reply",
        )
        returned.append(all_ways(replies))
    (result,) = call(
        unpack_kernel,
        [shape((brick_rows, BRICK_ROWS * LANES), bf16)],
        [V],
        [V((PARTS, SLOTS * PART_ROWS, LANES), f32), V((brick_rows * BRICK_ROWS, LANES), f32)],
        (slots, counts, *returned),
        [S, S] + [V] * PARTS,
        "unpack",
    )
    return result


def solution(mesh):
    in_specs = (P(("gz", "ma"), None), P(("gz", "ma"), None), P(("gz", "ma")), P(("gz", "ma")))
    out_specs = P(("gz", "ma"), None)
    body = on_device_8x4 if (mesh.shape["gz"], mesh.shape["ma"]) == (8, 4) else on_device
    return jax.shard_map(body, mesh=mesh, in_specs=in_specs, out_specs=out_specs, check_vma=False)
```

```python
import math

import jax
import jax.numpy as jnp
import ml_dtypes
import numpy as np
from jax import lax
from jax.experimental import pallas as pl
from jax.experimental.pallas import tpu as pltpu
from jax.sharding import PartitionSpec as P

NX = 512
NY = 512
SCREEN = 16
BZ = 4
BX = 8
BY = 64
CZ = 16


def hartley(length):
    indices = jnp.arange(length, dtype=jnp.int32)
    products = indices[:, None] * indices[None, :] % length
    angles = 2.0 * math.pi / length * products.astype(jnp.float32)
    return (jnp.cos(angles) + jnp.sin(angles)) / math.sqrt(length)


def second_difference(length, indices):
    return 2.0 - 2.0 * jnp.cos(2.0 * math.pi / length * indices.astype(jnp.float32))


def thomas(right_side, diagonal):
    start_zero = jnp.zeros(right_side.shape[1:], jnp.float32)

    def down(state_pair, plane):
        factor = 1.0 / (diagonal - state_pair[0])
        partial_value = (plane + state_pair[1]) * factor
        return ((factor, partial_value), (factor, partial_value))

    _, (factors, partials) = lax.scan(down, (start_zero, start_zero), right_side)

    def upward(beyond, factor_partial):
        solved = factor_partial[1] + factor_partial[0] * beyond
        return (solved, solved)

    _, solutions = lax.scan(upward, start_zero, (factors, partials), reverse=True)
    return solutions


def regroup(values):
    return lax.all_to_all(values, "ma", split_axis=2, concat_axis=1, tiled=True)


def on_device(bricks, owners, tile_ids, counts):
    domains = lax.axis_size(("gz", "ma"))
    group_count = lax.axis_size("ma")
    slab_count = lax.axis_size("gz")
    brick_rows, brick_cells = bricks.shape
    slot_count = max(2, 2 * brick_rows // domains)
    local_x = NX // group_count
    local_y = NY // group_count
    tiles_dev = CZ // BZ * (local_x // BX) * (NY // BY)
    highest = lax.Precision.HIGHEST
    target = owners[:, 0]
    row_order = jnp.arange(brick_rows, dtype=jnp.int32)
    earlier_same = (target[:, None] == target[None, :]) & (row_order[None, :] < row_order[:, None])
    within = jnp.sum(earlier_same.astype(jnp.int32), axis=1)
    slot_of = target * slot_count + within
    is_live = row_order < counts[0]
    loaded = jnp.where(is_live[:, None], bricks, jnp.zeros_like(bricks))
    outgoing = jnp.zeros((domains * slot_count, brick_cells), jnp.bfloat16).at[slot_of].set(loaded)
    out_ids = jnp.full((domains * slot_count,), tiles_dev, jnp.int32).at[slot_of].set(tile_ids)
    incoming, in_ids = (
        lax.all_to_all(outgoing, ("gz", "ma"), split_axis=0, concat_axis=0, tiled=True),
        lax.all_to_all(out_ids, ("gz", "ma"), split_axis=0, concat_axis=0, tiled=True),
    )
    picker = (jnp.arange(tiles_dev, dtype=jnp.int32)[:, None] == in_ids[None, :]).astype(
        jnp.bfloat16
    )
    deposit = jnp.dot(picker, incoming, preferred_element_type=jnp.float32)
    charge = deposit.reshape(CZ // BZ, local_x // BX, NY // BY, BZ, BX, BY)
    charge = charge.transpose(0, 3, 1, 4, 2, 5).reshape(CZ, local_x, NY)
    table_x = hartley(NX)
    table_y = hartley(NY)
    along_y = jnp.einsum("zxy,ky->zxk", charge, table_y, precision=highest)
    gathered_x = regroup(along_y)
    spectrum = jnp.einsum("zxk,jx->zjk", gathered_x, table_x, precision=highest)
    columns = lax.axis_index("ma") * local_y + jnp.arange(local_y, dtype=jnp.int32)
    lam_y = second_difference(NY, columns)
    screening = 1.0 / (SCREEN * SCREEN)
    slab_index = lax.axis_index("gz")
    lam_x = second_difference(NX, jnp.arange(NX, dtype=jnp.int32))
    diagonal = 2.0 + screening + lam_x[:, None] + lam_y[None, :]
    interior = spectrum[1:]
    particular = thomas(interior, diagonal)
    unit_rhs = jnp.zeros_like(interior).at[0].set(1.0)
    spike = thomas(unit_rhs, diagonal)
    near_weight = spike[0]
    far_weight = spike[-1]
    head_term = spectrum[0] + particular[0]
    tail_term = particular[-1]
    reduced_first = diagonal - near_weight
    reduced_rest = diagonal - 2.0 * near_weight
    start_zero = jnp.zeros_like(diagonal)
    heads, tails = (
        lax.all_gather(head_term[None], "gz", axis=0, tiled=True),
        lax.all_gather(tail_term[None], "gz", axis=0, tiled=True),
    )
    before = jnp.concatenate([start_zero[None], tails[:-1]], axis=0)
    sources = heads + before

    def chain_down(state_pair, packed):
        source, position = packed
        base_term = jnp.where(position == 0, reduced_first, reduced_rest)
        pivot_now = 1.0 / (base_term - far_weight * far_weight * state_pair[0])
        forward_part = pivot_now * (source + far_weight * state_pair[1])
        return ((pivot_now, forward_part), (pivot_now, forward_part))

    _, (pivots, forwards) = lax.scan(
        chain_down, (start_zero, start_zero), (sources, jnp.arange(slab_count, dtype=jnp.int32))
    )

    def chain_up(beyond, packed):
        plane_value = packed[1] + far_weight * packed[0] * beyond
        return (plane_value, plane_value)

    _, separators = lax.scan(chain_up, start_zero, (pivots, forwards), reverse=True)
    padded_sep = jnp.concatenate([separators, start_zero[None]], axis=0)
    own_plane = lax.dynamic_index_in_dim(padded_sep, slab_index, 0, keepdims=False)
    next_plane = lax.dynamic_index_in_dim(padded_sep, slab_index + 1, 0, keepdims=False)
    interior_sol = particular + own_plane[None] * spike + next_plane[None] * spike[::-1]
    modal = jnp.concatenate([own_plane[None], interior_sol], axis=0)
    back_x = jnp.einsum("zjk,jx->zkx", modal, table_x, precision=highest)
    gathered_y = regroup(back_x)
    potential = jnp.einsum("zkx,ky->zxy", gathered_y, table_y, precision=highest)
    pot_tiles = potential.reshape(CZ // BZ, BZ, local_x // BX, BX, NY // BY, BY)
    pot_tiles = (
        pot_tiles.transpose(0, 2, 4, 1, 3, 5).reshape(tiles_dev, brick_cells).astype(jnp.bfloat16)
    )
    padded_tiles = jnp.concatenate([pot_tiles, jnp.zeros((1, brick_cells), jnp.bfloat16)], axis=0)
    replies = padded_tiles[in_ids]
    returned = lax.all_to_all(replies, ("gz", "ma"), split_axis=0, concat_axis=0, tiled=True)
    result = returned[slot_of]
    return jnp.where(is_live[:, None], result, jnp.zeros_like(result))


DOMAINS = 32
SLABS = 8
PAIR_SLOTS = 8
SLOTS = DOMAINS * PAIR_SLOTS
TILES = 512
PARTS = 2
BRICK_ROWS = 16
PART_ROWS = BRICK_ROWS // PARTS
PART_PLANES = BZ // PARTS
LANES = 128
HALF = 64
SPOTS = 64
BLOCK_ROWS = PART_ROWS * SPOTS
HEAD_ROWS = 16
SENT_ROWS = BLOCK_ROWS + HEAD_ROWS
STEPS = 64
PLANES = 128
FULL = 32700.0
LOG_UNIT = 128.0
VMEM_BYTES = 48 * 1024 * 1024


def split_table(table):
    high = table.astype(ml_dtypes.bfloat16)
    low = (table - high.astype(np.float64)).astype(ml_dtypes.bfloat16)
    return high, low


def line_tables():
    index = np.arange(NY)
    angle = 2.0 * np.pi / NY * (index[:, None] * index[None, :] % NY)
    table = (np.cos(angle) + np.sin(angle)) / np.sqrt(NY)
    swapped = table.reshape(NY, NY // LANES, 2, HALF)[:, :, ::-1].reshape(NY, NY)
    return np.stack([*split_table(table), *split_table(swapped)])


def plane_tables():
    index = np.arange(PLANES)
    table = np.sqrt(2.0 / (PLANES + 1)) * np.sin(
        np.pi / (PLANES + 1) * ((index[:, None] + 1) * (index[None, :] + 1) % (2 * PLANES + 2))
    )
    plane_of = index % SLABS * CZ + index // SLABS % BZ * BZ + index // 32
    down = table[:, plane_of]
    both = []
    for each in (down, down.T):
        high, low = split_table(each)
        top = np.concatenate([high, high], axis=1)
        bottom = np.concatenate([low, np.zeros_like(low)], axis=1)
        both.append(np.concatenate([top, bottom], axis=0))
    return both


def mode_tables():
    mu = 2.0 - 2.0 * np.cos(np.pi / (PLANES + 1) * (np.arange(PLANES) + 1))
    base = np.broadcast_to((mu + 1.0 / (SCREEN * SCREEN))[:, None], (PLANES, LANES))
    lam = 2.0 - 2.0 * np.cos(2.0 * np.pi / NY * np.arange(NY))
    lam = lam.reshape(NY // HALF, HALF)
    return base.astype(np.float32), np.concatenate([lam, lam], axis=1).astype(np.float32)


def low_half(shape):
    return lax.broadcasted_iota(jnp.int32, shape, len(shape) - 1) < HALF


def split(values):
    high = values.astype(jnp.bfloat16)
    return high, (values - high.astype(jnp.float32)).astype(jnp.bfloat16)


def dot(left, right):
    return jnp.dot(left, right, preferred_element_type=jnp.float32)


def line_transform(load, store, table_ref):
    low = low_half((4 * SPOTS, LANES))
    for step in range(BLOCK_ROWS // (4 * SPOTS)):
        evens, odds = [], []
        for pair in range(4):
            first, second = load(2 * pair, step), load(2 * pair + 1, step)
            crossed = pltpu.roll(jnp.where(low, second, first), HALF, 1)
            evens.append(jnp.where(low, first, crossed))
            odds.append(jnp.where(low, crossed, second))
        products = []
        for lines, at in ((evens, 0), (odds, 2)):
            high, rest = split(jnp.concatenate(lines, axis=1))
            products.append(
                dot(high, table_ref[at]) + (dot(high, table_ref[at + 1]) + dot(rest, table_ref[at]))
            )
        for pair in range(4):
            even = products[0][:, pair * LANES : (pair + 1) * LANES]
            odd = products[1][:, pair * LANES : (pair + 1) * LANES]
            store(2 * pair, step, jnp.where(low, even, odd))
            store(2 * pair + 1, step, pltpu.roll(jnp.where(low, odd, even), HALF, 1))


def level_of(most):
    return jnp.floor(jnp.log2(jnp.maximum(most, 1e-30)) * LOG_UNIT) + 2.0


def inverse_of(level):
    return FULL * jnp.exp2(level * (-1.0 / LOG_UNIT))


def fixed_of(values):
    return jnp.floor(values + 0.5).astype(jnp.int32).astype(jnp.int16)


def head_of(level):
    return jnp.broadcast_to(level, (HEAD_ROWS, LANES)).astype(jnp.int32).astype(jnp.int16)


def unit_of(sent_ref):
    head = sent_ref[BLOCK_ROWS:SENT_ROWS, :].astype(jnp.int32).astype(jnp.float32)
    return jnp.exp2(head[0:1] * (1.0 / LOG_UNIT)) * (1.0 / FULL)


def wide(block):
    return block.astype(jnp.int32).astype(jnp.float32)


def pack_kernel(owner_in, tile_in, count_in, brick_in, *refs):
    out_refs, slot_ref = refs[:PARTS], refs[PARTS]
    owner_ref, tile_ref, count_ref, brick_ref, rows_ref, slots_ref, head_ref, used_ref, sems = refs[PARTS + 1 :]
    copies = [
        pltpu.make_async_copy(source, place, sems.at[at])
        for at, (source, place) in enumerate(
            ((brick_in, brick_ref), (owner_in, owner_ref), (tile_in, tile_ref), (count_in, count_ref))
        )
    ]
    for each in copies:
        each.start()
    brick_rows = brick_ref.shape[0]
    head_ref[...] = jnp.full(head_ref.shape, float(TILES), jnp.float32)
    slots_ref[...] = jnp.zeros(slots_ref.shape, jnp.float32)
    for owner in range(DOMAINS):
        used_ref[owner] = 0
    for each in copies:
        each.wait()
    for q in range(BRICK_ROWS):
        block = brick_ref[:, q * LANES : (q + 1) * LANES].astype(jnp.float32)
        rows_ref[pl.ds(q, brick_rows, stride=BRICK_ROWS), :] = block

    def place(r, _):
        owner = owner_ref[r]
        within = used_ref[owner]
        used_ref[owner] = within + 1
        slot = owner * PAIR_SLOTS + within
        slot_ref[r] = slot
        tile = tile_ref[r]
        line = tile // 8
        position = tile % 8 * SPOTS + line % 16 * 4 + line // 16
        for part in range(PARTS):
            brick = rows_ref[pl.ds(pl.multiple_of(r * BRICK_ROWS + part * PART_ROWS, PART_ROWS), PART_ROWS), :]
            slots_ref[part, pl.ds(pl.multiple_of(slot * PART_ROWS, PART_ROWS), PART_ROWS), :] = brick
        head_ref[pl.ds(slot, 1), :] = jnp.full((1, LANES), position, jnp.int32).astype(jnp.float32)
        return 0

    count = count_ref[0]
    lax.fori_loop(0, count, place, 0)

    def rest(r, _):
        slot_ref[r] = 0
        return 0

    lax.fori_loop(count, brick_rows, rest, 0)
    pair_rows = PAIR_SLOTS * PART_ROWS
    for owner in range(DOMAINS):
        for part, out_ref in enumerate(out_refs):
            block = slots_ref[part, owner * pair_rows : (owner + 1) * pair_rows, :]
            out_ref[owner, :pair_rows, :] = block.astype(jnp.bfloat16)
        head = head_ref[owner * PAIR_SLOTS : (owner + 1) * PAIR_SLOTS, :]
        high = jnp.floor(head * (1.0 / 32.0))
        both = jnp.concatenate([high, head - 32.0 * high], axis=0)
        out_refs[0][owner, pair_rows:, :] = both.astype(jnp.bfloat16)


def picks_kernel(brick_ref, out_ref):
    pair_rows = PAIR_SLOTS * PART_ROWS
    for domain in range(DOMAINS):
        head = brick_ref[domain, pair_rows:, :].astype(jnp.float32)
        places = (head[:PAIR_SLOTS] * 32.0 + head[PAIR_SLOTS:]).astype(jnp.int32)
        for block in range(TILES // LANES):
            lane = lax.broadcasted_iota(jnp.int32, (PAIR_SLOTS, LANES), 1) + block * LANES
            out_ref[domain * PAIR_SLOTS : (domain + 1) * PAIR_SLOTS, block * LANES : (block + 1) * LANES] = (
                jnp.where(places == lane, 1.0, 0.0)
            )


def forward_body(own_ref, brick_ref, picks, table_ref, sent_refs, slots_ref, charge_ref, lines_ref):
    pair_rows = PAIR_SLOTS * PART_ROWS
    for domain in range(DOMAINS):
        slots_ref[domain * pair_rows : (domain + 1) * pair_rows, :] = brick_ref[domain, :pair_rows, :].astype(jnp.float32)
    for q in range(0, PART_ROWS, 2):
        rows = [slots_ref[pl.ds(q + one, SLOTS, stride=PART_ROWS), :] for one in range(2)]
        both = lax.dot_general(
            picks,
            jnp.concatenate(rows, axis=1).astype(jnp.bfloat16),
            (((0,), (0,)), ((), ())),
            preferred_element_type=jnp.float32,
        )
        charge_ref[q] = both[:, :LANES]
        charge_ref[q + 1] = both[:, LANES:]

    def load(block, step):
        return charge_ref[step * 4 : step * 4 + 4, block * SPOTS : (block + 1) * SPOTS, :].reshape(4 * SPOTS, LANES)

    def store(block, step, values):
        lines_ref[block, step * 4 * SPOTS : (step + 1) * 4 * SPOTS, :] = values

    line_transform(load, store, table_ref)
    for offset, sent_ref in enumerate(sent_refs):
        block = lines_ref[own_ref[0] ^ offset]
        most = jnp.max(jnp.abs(block).reshape(BLOCK_ROWS // 8, 8, LANES), axis=0)
        level = level_of(jnp.max(most, axis=0, keepdims=True))
        sent_ref[:BLOCK_ROWS, :] = fixed_of(block * inverse_of(level))
        sent_ref[BLOCK_ROWS:, :] = head_of(level)


def first_kernel(own_ref, brick_ref, table_ref, *refs):
    sent_refs, picks_ref, wide_ref = refs[:SLABS], refs[SLABS], refs[SLABS + 1]
    picks_kernel(brick_ref, wide_ref)
    picks = wide_ref[...].astype(jnp.bfloat16)
    picks_ref[...] = picks
    forward_body(own_ref, brick_ref, picks, table_ref, sent_refs, *refs[SLABS + 2 :])


def later_kernel(own_ref, brick_ref, picks_ref, table_ref, *refs):
    forward_body(own_ref, brick_ref, picks_ref[...], table_ref, refs[:SLABS], *refs[SLABS:])


def roots(base_ref, lam_ref):
    excess = base_ref[...] + lam_ref[...]
    spread = jnp.sqrt(excess * (excess + 4.0))
    root = 2.0 / (2.0 + excess + spread)
    return root, spread


def grid_rows(part, iz, xq, tx):
    return pl.ds(pl.multiple_of((part * BLOCK_ROWS + (iz * 4 + xq) * SPOTS + tx * 4) * SLABS, 32), 32)


def down_kernel(own_ref, *refs):
    got_refs = refs[: PARTS * SLABS]
    plane_ref, base_ref, lam_ref, walk_ref, end_ref, grid_ref, modes_ref, root_ref = refs[PARTS * SLABS :]
    for at, got_ref in enumerate(got_refs):
        part, offset = at // SLABS, at % SLABS
        block = wide(got_ref[:BLOCK_ROWS, :]) * unit_of(got_ref)
        start = part * BLOCK_ROWS * SLABS + (own_ref[0] ^ offset)
        grid_ref[pl.ds(start, BLOCK_ROWS, stride=SLABS), :] = block

    def planes(tx, xq):
        return jnp.concatenate(
            [grid_ref[grid_rows(part, iz, xq, tx), :] for part in range(PARTS) for iz in range(PART_PLANES)], axis=0
        )

    def sines(tx, _):
        for half in range(2):
            lines = jnp.concatenate([planes(tx, half * 2), planes(tx, half * 2 + 1)], axis=1)
            both = dot(plane_ref[...], jnp.concatenate(split(lines), axis=0))
            modes = both[:PLANES] + both[PLANES:]
            modes_ref[tx * 4 + half * 2] = modes[:, :LANES]
            modes_ref[tx * 4 + half * 2 + 1] = modes[:, LANES:]
        return 0

    lax.fori_loop(0, 16, sines, 0, unroll=4)
    root, _ = roots(base_ref, lam_ref)
    root_ref[...] = root

    part_rows = 64
    low = low_half((part_rows, LANES))
    for part in range(PLANES // part_rows):
        here = pl.ds(part * part_rows, part_rows)
        root = root_ref[here, :]
        square = root * root

        def walk(step, held):
            ahead, behind = modes_ref[step, here, :], modes_ref[STEPS - 1 - step, here, :]
            own = jnp.where(low, behind, ahead)
            other = pltpu.roll(jnp.where(low, ahead, behind), HALF, 1)
            held = square * held + (own + root * other)
            walk_ref[step, here, :] = held
            return held

        end_ref[here, :] = lax.fori_loop(0, STEPS, walk, jnp.zeros((part_rows, LANES), jnp.float32), unroll=4)


def up_kernel(own_ref, walk_ref, *refs):
    group_count = 4
    end_refs, (plane_ref, base_ref, lam_ref) = refs[:group_count], refs[group_count : group_count + 3]
    sent_refs = refs[group_count + 3 : group_count + 3 + PARTS * SLABS]
    full_ref, grid_ref, root_ref, gain_ref, level_ref, inverse_ref = refs[group_count + 3 + PARTS * SLABS :]
    root, spread = roots(base_ref, lam_ref)
    root_ref[...] = root
    gain_ref[...] = 1.0 / spread
    part_rows = 64
    low = low_half((part_rows, LANES))
    for part in range(PLANES // part_rows):
        here = pl.ds(part * part_rows, part_rows)
        root = root_ref[here, :]
        square = root * root
        across = square
        for _ in range(6):
            across = across * across
        entering = jnp.zeros((part_rows, LANES), jnp.float32)
        for step in range(group_count - 1, -1, -1):
            before = end_refs[(step + 1) % group_count][here, :]
            after = end_refs[group_count - 1 - step][here, :]
            entering = entering * across + jnp.where(low, after, before)
        around = across
        for _ in range(2):
            around = around * around
        entering = entering / (1.0 - around)
        full_ref[0, here, :] = entering

        def carry(step, reach):
            full_ref[step + 1, here, :] = walk_ref[step, here, :] + reach
            return reach * square

        lax.fori_loop(0, STEPS, carry, entering * square, unroll=4)

    def solved(step):
        low = low_half((PLANES, LANES))
        near = jnp.where(low, full_ref[STEPS - step], full_ref[step + 1])
        far = jnp.where(low, full_ref[STEPS - 1 - step], full_ref[step])
        return gain_ref[...] * (near + root_ref[...] * pltpu.roll(far, HALF, 1))

    def sines(tx, _):
        for half in range(2):
            first = tx * 4 + half * 2
            modes = jnp.concatenate([solved(first), solved(first + 1)], axis=1)
            both = dot(plane_ref[...], jnp.concatenate(split(modes), axis=0))
            lines = both[:PLANES] + both[PLANES:]
            for one in range(2):
                for part in range(PARTS):
                    for iz in range(PART_PLANES):
                        at = part * PART_PLANES + iz
                        grid_ref[grid_rows(part, iz, half * 2 + one, tx), :] = lines[
                            at * 32 : (at + 1) * 32, one * LANES : (one + 1) * LANES
                        ]
        return 0

    lax.fori_loop(0, 16, sines, 0, unroll=4)
    for part in range(PARTS):
        here = pl.ds(part * BLOCK_ROWS * SLABS, BLOCK_ROWS * SLABS)
        most = jnp.max(jnp.abs(grid_ref[here, :]).reshape(BLOCK_ROWS, SLABS, LANES), axis=0)
        level_ref[...] = level_of(most)
        inverse_ref[...] = inverse_of(level_of(most))
        for offset in range(SLABS):
            sent_ref = sent_refs[part * SLABS + offset]
            g = own_ref[0] ^ offset
            block = grid_ref[pl.ds(part * BLOCK_ROWS * SLABS + g, BLOCK_ROWS, stride=SLABS), :]
            sent_ref[:BLOCK_ROWS, :] = fixed_of(block * inverse_ref[pl.ds(g, 1), :])
            sent_ref[BLOCK_ROWS:, :] = head_of(level_ref[pl.ds(g, 1), :])


def reply_kernel(own_ref, *refs):
    got_refs = refs[:SLABS]
    picks_ref, table_ref, out_ref, lines_ref, pot_ref, slots_ref = refs[SLABS:]
    for offset, got_ref in enumerate(got_refs):
        lines_ref[own_ref[0] ^ offset] = wide(got_ref[:BLOCK_ROWS, :]) * unit_of(got_ref)

    def load(block, step):
        return lines_ref[block, step * 4 * SPOTS : (step + 1) * 4 * SPOTS, :]

    def store(block, step, values):
        pot_ref[step * 4 : step * 4 + 4, block * SPOTS : (block + 1) * SPOTS, :] = (
            values.astype(jnp.bfloat16).reshape(4, SPOTS, LANES)
        )

    line_transform(load, store, table_ref)
    for q in range(0, PART_ROWS, 2):
        both = dot(picks_ref[...], jnp.concatenate([pot_ref[q], pot_ref[q + 1]], axis=1))
        for one in range(2):
            slots_ref[pl.ds(q + one, SLOTS, stride=PART_ROWS), :] = both[:, one * LANES : (one + 1) * LANES]
    pair_rows = PAIR_SLOTS * PART_ROWS
    for domain in range(DOMAINS):
        out_ref[domain] = slots_ref[domain * pair_rows : (domain + 1) * pair_rows, :].astype(jnp.bfloat16)


def unpack_kernel(slot_ref, count_ref, *refs):
    got_refs, (out_ref, slots_ref, rows_ref) = refs[:PARTS], refs[PARTS:]
    brick_rows = out_ref.shape[0]
    pair_rows = PAIR_SLOTS * PART_ROWS
    rows_ref[...] = jnp.zeros(rows_ref.shape, jnp.float32)
    for domain in range(DOMAINS):
        for part, got_ref in enumerate(got_refs):
            slots_ref[part, domain * pair_rows : (domain + 1) * pair_rows, :] = got_ref[domain].astype(jnp.float32)

    def place(r, _):
        slot = slot_ref[r]
        for part in range(PARTS):
            brick = slots_ref[part, pl.ds(pl.multiple_of(slot * PART_ROWS, PART_ROWS), PART_ROWS), :]
            rows_ref[pl.ds(pl.multiple_of(r * BRICK_ROWS + part * PART_ROWS, PART_ROWS), PART_ROWS), :] = brick
        return 0

    lax.fori_loop(0, count_ref[0], place, 0)
    for q in range(BRICK_ROWS):
        block = rows_ref[pl.ds(q, brick_rows, stride=BRICK_ROWS), :]
        out_ref[:, q * LANES : (q + 1) * LANES] = block.astype(jnp.bfloat16)


def call(kernel, outs, places, scratch, operands, spaces, name):
    return pl.pallas_call(
        kernel,
        out_shape=outs,
        in_specs=[pl.BlockSpec(memory_space=space) for space in spaces],
        out_specs=[pl.BlockSpec(memory_space=space) for space in places],
        scratch_shapes=scratch,
        compiler_params=pltpu.CompilerParams(vmem_limit_bytes=VMEM_BYTES),
        name=name,
    )(*operands)


def on_device_8x4(bricks, owners, tile_ids, counts):
    V, S, A = pltpu.VMEM, pltpu.SMEM, pl.ANY
    f32, bf16, i32, i16 = jnp.float32, jnp.bfloat16, jnp.int32, jnp.int16
    shape = jax.ShapeDtypeStruct
    brick_rows = bricks.shape[0]
    line_table = jnp.asarray(line_tables())
    plane_down, plane_up = (jnp.asarray(each) for each in plane_tables())
    base, lam_all = (jnp.asarray(each) for each in mode_tables())
    lam = lax.dynamic_slice_in_dim(lam_all, lax.axis_index("gz"), 1, 0)
    own = lax.axis_index("gz").astype(i32).reshape(1)
    pair_rows = PAIR_SLOTS * PART_ROWS

    def all_ways(values):
        return lax.all_to_all(values, ("gz", "ma"), split_axis=0, concat_axis=0, tiled=True)

    def over_slabs(values):
        return [values[0]] + [
            lax.ppermute(values[offset], "gz", [(g, g ^ offset) for g in range(SLABS)])
            for offset in range(1, SLABS)
        ]

    def round_groups(values):
        return [values] + [
            lax.ppermute(values, "ma", [(m, (m + step) % 4) for m in range(4)]) for step in range(1, 4)
        ]

    *outgoing, slots = call(
        pack_kernel,
        [shape((DOMAINS, pair_rows + (HEAD_ROWS if part == 0 else 0), LANES), bf16) for part in range(PARTS)]
        + [shape((brick_rows,), i32)],
        [V] * PARTS + [S],
        [
            S((brick_rows,), i32),
            S((brick_rows,), i32),
            S((1,), i32),
            V(bricks.shape, bf16),
            V((brick_rows * BRICK_ROWS, LANES), f32),
            V((PARTS, SLOTS * PART_ROWS, LANES), f32),
            V((SLOTS, LANES), f32),
            S((DOMAINS,), i32),
            pltpu.SemaphoreType.DMA((4,)),
        ],
        (owners.reshape(brick_rows), tile_ids, counts, bricks),
        [A, A, A, A],
        "pack",
    )
    sent_shapes = [shape((SENT_ROWS, LANES), i16)] * SLABS
    forward_scratch = [
        V((SLOTS * PART_ROWS, LANES), f32),
        V((PART_ROWS, TILES, LANES), f32),
        V((SLABS, BLOCK_ROWS, LANES), f32),
    ]
    incoming = [all_ways(each) for each in outgoing]
    *sent, picks = call(
        first_kernel,
        sent_shapes + [shape((SLOTS, TILES), bf16)],
        [V] * (SLABS + 1),
        [V((SLOTS, TILES), f32), *forward_scratch],
        (own, incoming[0], line_table),
        [S, V, V],
        "forward",
    )
    got = over_slabs(sent)
    for each in incoming[1:]:
        sent = call(
            later_kernel,
            sent_shapes,
            [V] * SLABS,
            forward_scratch,
            (own, each, picks, line_table),
            [S, V, V, V],
            "forward_later",
        )
        got += over_slabs(sent)
    cube = (STEPS, PLANES, LANES)
    flat = V((PLANES, LANES), f32)
    grid = V((PARTS * BLOCK_ROWS * SLABS, LANES), f32)
    walk, end = call(
        down_kernel,
        [shape(cube, f32), shape((PLANES, LANES), f32)],
        [V, V],
        [grid, V(cube, f32), flat],
        (own, *got, plane_down, base, lam),
        [S] + [V] * (len(got) + 3),
        "down",
    )
    sent = call(
        up_kernel,
        sent_shapes * PARTS,
        [V] * (PARTS * SLABS),
        [V((STEPS + 1, PLANES, LANES), f32), grid, flat, flat, V((SLABS, LANES), f32), V((SLABS, LANES), f32)],
        (own, walk, *round_groups(end), plane_up, base, lam),
        [S] + [V] * 8,
        "up",
    )
    returned = []
    for part in range(PARTS):
        (replies,) = call(
            reply_kernel,
            [shape((DOMAINS, pair_rows, LANES), bf16)],
            [V],
            [
                V((SLABS, BLOCK_ROWS, LANES), f32),
                V((PART_ROWS, TILES, LANES), bf16),
                V((SLOTS * PART_ROWS, LANES), f32),
            ],
            (own, *over_slabs(sent[part * SLABS : (part + 1) * SLABS]), picks, line_table),
            [S] + [V] * (SLABS + 2),
            "reply",
        )
        returned.append(all_ways(replies))
    (result,) = call(
        unpack_kernel,
        [shape((brick_rows, BRICK_ROWS * LANES), bf16)],
        [V],
        [V((PARTS, SLOTS * PART_ROWS, LANES), f32), V((brick_rows * BRICK_ROWS, LANES), f32)],
        (slots, counts, *returned),
        [S, S] + [V] * PARTS,
        "unpack",
    )
    return result


def solution(mesh):
    in_specs = (P(("gz", "ma"), None), P(("gz", "ma"), None), P(("gz", "ma")), P(("gz", "ma")))
    out_specs = P(("gz", "ma"), None)
    body = on_device_8x4 if (mesh.shape["gz"], mesh.shape["ma"]) == (8, 4) else on_device
    return jax.shard_map(body, mesh=mesh, in_specs=in_specs, out_specs=out_specs, check_vma=False)
```

```python
import functools
import math

import jax
import jax.numpy as jnp
import ml_dtypes
import numpy as np
from jax import lax
from jax.experimental import pallas as pl
from jax.experimental.pallas import tpu as pltpu
from jax.sharding import PartitionSpec as P

NX = 512
NY = 512
SCREEN = 16
BZ = 4
BX = 8
BY = 64
CZ = 16


def hartley(length):
    indices = jnp.arange(length, dtype=jnp.int32)
    products = indices[:, None] * indices[None, :] % length
    angles = 2.0 * math.pi / length * products.astype(jnp.float32)
    return (jnp.cos(angles) + jnp.sin(angles)) / math.sqrt(length)


def second_difference(length, indices):
    return 2.0 - 2.0 * jnp.cos(2.0 * math.pi / length * indices.astype(jnp.float32))


def thomas(right_side, diagonal):
    start_zero = jnp.zeros(right_side.shape[1:], jnp.float32)

    def down(state_pair, plane):
        factor = 1.0 / (diagonal - state_pair[0])
        partial_value = (plane + state_pair[1]) * factor
        return ((factor, partial_value), (factor, partial_value))

    _, (factors, partials) = lax.scan(down, (start_zero, start_zero), right_side)

    def upward(beyond, factor_partial):
        solved = factor_partial[1] + factor_partial[0] * beyond
        return (solved, solved)

    _, solutions = lax.scan(upward, start_zero, (factors, partials), reverse=True)
    return solutions


def regroup(values):
    return lax.all_to_all(values, "ma", split_axis=2, concat_axis=1, tiled=True)


def on_device(bricks, owners, tile_ids, counts):
    domains = lax.axis_size(("gz", "ma"))
    group_count = lax.axis_size("ma")
    slab_count = lax.axis_size("gz")
    brick_rows, brick_cells = bricks.shape
    slot_count = max(2, 2 * brick_rows // domains)
    local_x = NX // group_count
    local_y = NY // group_count
    tiles_dev = CZ // BZ * (local_x // BX) * (NY // BY)
    highest = lax.Precision.HIGHEST
    target = owners[:, 0]
    row_order = jnp.arange(brick_rows, dtype=jnp.int32)
    earlier_same = (target[:, None] == target[None, :]) & (row_order[None, :] < row_order[:, None])
    within = jnp.sum(earlier_same.astype(jnp.int32), axis=1)
    slot_of = target * slot_count + within
    is_live = row_order < counts[0]
    loaded = jnp.where(is_live[:, None], bricks, jnp.zeros_like(bricks))
    outgoing = jnp.zeros((domains * slot_count, brick_cells), jnp.bfloat16).at[slot_of].set(loaded)
    out_ids = jnp.full((domains * slot_count,), tiles_dev, jnp.int32).at[slot_of].set(tile_ids)
    incoming, in_ids = (
        lax.all_to_all(outgoing, ("gz", "ma"), split_axis=0, concat_axis=0, tiled=True),
        lax.all_to_all(out_ids, ("gz", "ma"), split_axis=0, concat_axis=0, tiled=True),
    )
    picker = (jnp.arange(tiles_dev, dtype=jnp.int32)[:, None] == in_ids[None, :]).astype(
        jnp.bfloat16
    )
    deposit = jnp.dot(picker, incoming, preferred_element_type=jnp.float32)
    charge = deposit.reshape(CZ // BZ, local_x // BX, NY // BY, BZ, BX, BY)
    charge = charge.transpose(0, 3, 1, 4, 2, 5).reshape(CZ, local_x, NY)
    table_x = hartley(NX)
    table_y = hartley(NY)
    along_y = jnp.einsum("zxy,ky->zxk", charge, table_y, precision=highest)
    gathered_x = regroup(along_y)
    spectrum = jnp.einsum("zxk,jx->zjk", gathered_x, table_x, precision=highest)
    columns = lax.axis_index("ma") * local_y + jnp.arange(local_y, dtype=jnp.int32)
    lam_y = second_difference(NY, columns)
    screening = 1.0 / (SCREEN * SCREEN)
    slab_index = lax.axis_index("gz")
    lam_x = second_difference(NX, jnp.arange(NX, dtype=jnp.int32))
    diagonal = 2.0 + screening + lam_x[:, None] + lam_y[None, :]
    interior = spectrum[1:]
    particular = thomas(interior, diagonal)
    unit_rhs = jnp.zeros_like(interior).at[0].set(1.0)
    spike = thomas(unit_rhs, diagonal)
    near_weight = spike[0]
    far_weight = spike[-1]
    head_term = spectrum[0] + particular[0]
    tail_term = particular[-1]
    reduced_first = diagonal - near_weight
    reduced_rest = diagonal - 2.0 * near_weight
    start_zero = jnp.zeros_like(diagonal)
    heads, tails = (
        lax.all_gather(head_term[None], "gz", axis=0, tiled=True),
        lax.all_gather(tail_term[None], "gz", axis=0, tiled=True),
    )
    before = jnp.concatenate([start_zero[None], tails[:-1]], axis=0)
    sources = heads + before

    def chain_down(state_pair, packed):
        source, position = packed
        base_term = jnp.where(position == 0, reduced_first, reduced_rest)
        pivot_now = 1.0 / (base_term - far_weight * far_weight * state_pair[0])
        forward_part = pivot_now * (source + far_weight * state_pair[1])
        return ((pivot_now, forward_part), (pivot_now, forward_part))

    _, (pivots, forwards) = lax.scan(
        chain_down, (start_zero, start_zero), (sources, jnp.arange(slab_count, dtype=jnp.int32))
    )

    def chain_up(beyond, packed):
        plane_value = packed[1] + far_weight * packed[0] * beyond
        return (plane_value, plane_value)

    _, separators = lax.scan(chain_up, start_zero, (pivots, forwards), reverse=True)
    padded_sep = jnp.concatenate([separators, start_zero[None]], axis=0)
    own_plane = lax.dynamic_index_in_dim(padded_sep, slab_index, 0, keepdims=False)
    next_plane = lax.dynamic_index_in_dim(padded_sep, slab_index + 1, 0, keepdims=False)
    interior_sol = particular + own_plane[None] * spike + next_plane[None] * spike[::-1]
    modal = jnp.concatenate([own_plane[None], interior_sol], axis=0)
    back_x = jnp.einsum("zjk,jx->zkx", modal, table_x, precision=highest)
    gathered_y = regroup(back_x)
    potential = jnp.einsum("zkx,ky->zxy", gathered_y, table_y, precision=highest)
    pot_tiles = potential.reshape(CZ // BZ, BZ, local_x // BX, BX, NY // BY, BY)
    pot_tiles = (
        pot_tiles.transpose(0, 2, 4, 1, 3, 5).reshape(tiles_dev, brick_cells).astype(jnp.bfloat16)
    )
    padded_tiles = jnp.concatenate([pot_tiles, jnp.zeros((1, brick_cells), jnp.bfloat16)], axis=0)
    replies = padded_tiles[in_ids]
    returned = lax.all_to_all(replies, ("gz", "ma"), split_axis=0, concat_axis=0, tiled=True)
    result = returned[slot_of]
    return jnp.where(is_live[:, None], result, jnp.zeros_like(result))


PARTS_IN = 1
PARTS_BACK = 1
DOMAINS = 32
GROUPS = 4
SLABS = 8
PAIR_SLOTS = 8
SLOTS = DOMAINS * PAIR_SLOTS
TILES = 512
BRICK_ROWS = 16
LANES = 128
HALF = 64
SPOTS = 64
HEAD_ROWS = 16
STEPS = 64
PLANES = 128
FULL = 32700.0
LOG_UNIT = 128.0
VMEM_BYTES = 24 * 1024 * 1024


def split_table(table):
    high = table.astype(ml_dtypes.bfloat16)
    low = (table - high.astype(np.float64)).astype(ml_dtypes.bfloat16)
    return high, low


def line_tables():
    index = np.arange(NY)
    angle = 2.0 * np.pi / NY * (index[:, None] * index[None, :] % NY)
    table = (np.cos(angle) + np.sin(angle)) / np.sqrt(NY)
    swapped = table.reshape(NY, NY // LANES, 2, HALF)[:, :, ::-1].reshape(NY, NY)
    return np.stack([*split_table(table), *split_table(swapped)])


def plane_tables():
    index = np.arange(PLANES)
    table = np.sqrt(2.0 / (PLANES + 1)) * np.sin(
        np.pi / (PLANES + 1) * ((index[:, None] + 1) * (index[None, :] + 1) % (2 * PLANES + 2))
    )
    plane_of = index % SLABS * CZ + index // SLABS % BZ * BZ + index // 32
    down = table[:, plane_of]
    both = []
    for each in (down, down.T):
        high, low = split_table(each)
        top = np.concatenate([high, high], axis=1)
        bottom = np.concatenate([low, np.zeros_like(low)], axis=1)
        both.append(np.concatenate([top, bottom], axis=0))
    return both


def mode_tables():
    mu = 2.0 - 2.0 * np.cos(np.pi / (PLANES + 1) * (np.arange(PLANES) + 1))
    base = np.broadcast_to((mu + 1.0 / (SCREEN * SCREEN))[:, None], (PLANES, LANES))
    lam = 2.0 - 2.0 * np.cos(2.0 * np.pi / NY * np.arange(NY))
    lam = lam.reshape(NY // HALF, HALF)
    return base.astype(np.float32), np.concatenate([lam, lam], axis=1).astype(np.float32)


def low_half(shape):
    return lax.broadcasted_iota(jnp.int32, shape, len(shape) - 1) < HALF


def split(values):
    high = values.astype(jnp.bfloat16)
    return high, (values - high.astype(jnp.float32)).astype(jnp.bfloat16)


def dot(left, right):
    return jnp.dot(left, right, preferred_element_type=jnp.float32)


def start_copies(pairs, sems):
    copies = [pltpu.make_async_copy(source, place, sems.at[at]) for at, (source, place) in enumerate(pairs)]
    for each in copies:
        each.start()
    return copies


def line_transform(rows, load, store, table_ref, left_ref):
    low = low_half((4 * SPOTS, LANES))
    for step in range(rows // (4 * SPOTS)):
        evens, odds = [], []
        for pair in range(4):
            first, second = load(2 * pair, step), load(2 * pair + 1, step)
            crossed = pltpu.roll(jnp.where(low, second, first), HALF, 1)
            evens.append(jnp.where(low, first, crossed))
            odds.append(jnp.where(low, crossed, second))
        here = slice(step * 4 * SPOTS, (step + 1) * 4 * SPOTS)
        for at, lines in enumerate((evens, odds)):
            high, rest = split(jnp.concatenate(lines, axis=1))
            left_ref[at, here, :NY] = high
            left_ref[at, here, NY:] = rest
    block = 512
    low = low_half((block, LANES))
    for part in range(rows // block):
        here = slice(part * block, (part + 1) * block)
        for columns in range(0, NY, 2 * LANES):
            there = slice(columns, columns + 2 * LANES)
            products = []
            for at in range(2):
                left = jnp.concatenate([left_ref[at, here, :], left_ref[at, here, :NY]], axis=1)
                main = table_ref[2 * at, :, there]
                right = jnp.concatenate([main, main, table_ref[2 * at + 1, :, there]], axis=0)
                products.append(dot(left, right))
            for pair in range(2):
                even, odd = (each[:, pair * LANES : (pair + 1) * LANES] for each in products)
                g = columns // HALF + 2 * pair
                store(g, part, jnp.where(low, even, odd))
                store(g + 1, part, pltpu.roll(jnp.where(low, odd, even), HALF, 1))


def level_of(most):
    return jnp.floor(jnp.log2(jnp.maximum(most, 1e-30)) * LOG_UNIT) + 2.0


def inverse_of(level):
    return FULL * jnp.exp2(level * (-1.0 / LOG_UNIT))


def fixed_of(values):
    return jnp.floor(values + 0.5).astype(jnp.int32).astype(jnp.int16)


def head_of(level):
    return jnp.broadcast_to(level, (HEAD_ROWS, LANES)).astype(jnp.int32).astype(jnp.int16)


def unit_of(sent_ref):
    head = sent_ref[sent_ref.shape[0] - HEAD_ROWS :, :].astype(jnp.int32).astype(jnp.float32)
    return jnp.exp2(head[0:1] * (1.0 / LOG_UNIT)) * (1.0 / FULL)


def wide(sent_ref):
    block = sent_ref[: sent_ref.shape[0] - HEAD_ROWS, :]
    return block.astype(jnp.int32).astype(jnp.float32) * unit_of(sent_ref)


def pack_kernel(parts, owner_in, tile_in, count_in, brick_in, *refs):
    outs, slot_ref = refs[:parts], refs[parts]
    (owner_ref, tile_ref, count_ref, brick_ref, rows_ref, slots_ref, head_ref, used_ref, sems, out_sems, *ready) = refs[
        parts + 1 :
    ]
    part_rows = BRICK_ROWS // parts
    pair_rows = PAIR_SLOTS * part_rows
    copies = start_copies(
        ((brick_in, brick_ref), (owner_in, owner_ref), (tile_in, tile_ref), (count_in, count_ref)), sems
    )
    brick_rows = brick_ref.shape[0]
    head_ref[...] = jnp.full(head_ref.shape, float(TILES), jnp.float32)
    slots_ref[...] = jnp.zeros(slots_ref.shape, jnp.float32)
    for owner in range(DOMAINS):
        used_ref[owner] = 0
    for each in copies:
        each.wait()
    for q in range(BRICK_ROWS):
        block = brick_ref[:, q * LANES : (q + 1) * LANES].astype(jnp.float32)
        rows_ref[pl.ds(q, brick_rows, stride=BRICK_ROWS), :] = block

    def place(r, _):
        owner = owner_ref[r]
        within = used_ref[owner]
        used_ref[owner] = within + 1
        slot = owner * PAIR_SLOTS + within
        slot_ref[r] = slot
        tile = tile_ref[r]
        line = tile // 8
        position = tile % 8 * SPOTS + line % 16 * 4 + line // 16
        for part in range(parts):
            brick = rows_ref[pl.ds(pl.multiple_of(r * BRICK_ROWS + part * part_rows, part_rows), part_rows), :]
            slots_ref[part, pl.ds(pl.multiple_of(slot * part_rows, part_rows), part_rows), :] = brick
        head_ref[pl.ds(slot, 1), :] = jnp.full((1, LANES), position, jnp.int32).astype(jnp.float32)
        return 0

    count = count_ref[0]
    lax.fori_loop(0, count, place, 0)

    def rest(r, _):
        slot_ref[r] = 0
        return 0

    lax.fori_loop(count, brick_rows, rest, 0)
    copies = []
    for part in range(parts):
        for owner in range(DOMAINS):
            block = slots_ref[part, owner * pair_rows : (owner + 1) * pair_rows, :]
            ready[part][owner, :pair_rows, :] = block.astype(jnp.bfloat16)
            if part == 0:
                head = head_ref[owner * PAIR_SLOTS : (owner + 1) * PAIR_SLOTS, :]
                high = jnp.floor(head * (1.0 / 32.0))
                both = jnp.concatenate([high, head - 32.0 * high], axis=0)
                ready[part][owner, pair_rows:, :] = both.astype(jnp.bfloat16)
            if owner % 8 == 7:
                some = pl.ds(owner - 7, 8)
                copy = pltpu.make_async_copy(
                    ready[part].at[some], outs[part].at[some], out_sems.at[part * 4 + owner // 8]
                )
                copy.start()
                copies.append(copy)
    for each in copies:
        each.wait()


def write_picks(brick_ref, pair_rows, picks_ref, across_ref):
    for block in range(TILES // LANES):
        there = slice(block * LANES, (block + 1) * LANES)
        for part in range(SLOTS // LANES):
            pieces = []
            for domain in range(part * 16, part * 16 + 16):
                head = brick_ref[domain, pair_rows:, :].astype(jnp.float32)
                places = (head[:PAIR_SLOTS] * 32.0 + head[PAIR_SLOTS:]).astype(jnp.int32)
                lane = lax.broadcasted_iota(jnp.int32, (PAIR_SLOTS, LANES), 1) + block * LANES
                pieces.append(jnp.where(places == lane, 1.0, 0.0))
            square = jnp.concatenate(pieces, axis=0)
            here = slice(part * LANES, (part + 1) * LANES)
            picks_ref[here, there] = square.astype(jnp.bfloat16)
            across_ref[there, here] = square.T.astype(jnp.bfloat16)


def forward_body(parts, own_ref, brick_ref, across_ref, table_ref, sent_refs, slots_ref, wide_ref, charge_ref, lines_ref, left_ref):
    part_rows = BRICK_ROWS // parts
    pair_rows = PAIR_SLOTS * part_rows
    for domain in range(DOMAINS):
        slots_ref[domain * pair_rows : (domain + 1) * pair_rows, :] = brick_ref[domain, :pair_rows, :].astype(jnp.float32)
    for q in range(part_rows):
        wide_ref[:, q * LANES : (q + 1) * LANES] = slots_ref[pl.ds(q, SLOTS, stride=part_rows), :].astype(jnp.bfloat16)
    for q in range(0, part_rows, 4):
        there = slice(q * LANES, (q + 4) * LANES)
        charge_ref[:, there] = dot(across_ref[...], wide_ref[:, there])

    def load(block, step):
        return jnp.concatenate(
            [
                charge_ref[block * SPOTS : (block + 1) * SPOTS, q * LANES : (q + 1) * LANES]
                for q in range(step * 4, step * 4 + 4)
            ],
            axis=0,
        )

    def store(block, part, values):
        lines_ref[block, part * 512 : (part + 1) * 512, :] = values

    rows = part_rows * SPOTS
    line_transform(rows, load, store, table_ref, left_ref)
    for offset, sent_ref in enumerate(sent_refs):
        block = lines_ref[own_ref[0] ^ offset]
        most = jnp.max(jnp.abs(block).reshape(rows // 8, 8, LANES), axis=0)
        level = level_of(jnp.max(most, axis=0, keepdims=True))
        sent_ref[:rows, :] = fixed_of(block * inverse_of(level))
        sent_ref[rows:, :] = head_of(level)


def first_kernel(parts, own_ref, brick_ref, table_ref, *refs):
    sent_refs, picks_ref, across_ref = refs[:SLABS], refs[SLABS], refs[SLABS + 1]
    write_picks(brick_ref, PAIR_SLOTS * BRICK_ROWS // parts, picks_ref, across_ref)
    forward_body(parts, own_ref, brick_ref, across_ref, table_ref, sent_refs, *refs[SLABS + 2 :])


def later_kernel(parts, own_ref, brick_ref, across_ref, table_ref, *refs):
    forward_body(parts, own_ref, brick_ref, across_ref, table_ref, refs[:SLABS], *refs[SLABS:])


def roots(own_ref, base_ref, lam_ref):
    excess = base_ref[...] + lam_ref[pl.ds(own_ref[0], 1), :]
    spread = jnp.sqrt(excess * (excess + 4.0))
    root = 2.0 / (2.0 + excess + spread)
    return root, spread


def grid_rows(parts, plane, xq, tx):
    planes = BZ // parts
    row = (plane // planes) * planes * 4 * SPOTS + (plane % planes * 4 + xq) * SPOTS + tx * 4
    return pl.ds(pl.multiple_of(row * SLABS, 32), 32)


def down_kernel(parts, own_ref, *refs):
    got_refs = refs[: parts * SLABS]
    (plane_in, base_in, lam_in, walk_ref, end_ref, grid_ref, modes_ref, root_ref, plane_ref, base_ref, lam_ref, sems) = refs[
        parts * SLABS :
    ]
    copies = start_copies(((plane_in, plane_ref), (base_in, base_ref), (lam_in, lam_ref)), sems)
    for at, got_ref in enumerate(got_refs):
        part, offset = at // SLABS, at % SLABS
        block = wide(got_ref)
        rows = block.shape[0]
        grid_ref[pl.ds(part * rows * SLABS + (own_ref[0] ^ offset), rows, stride=SLABS), :] = block
    for each in copies:
        each.wait()

    def planes(tx, xq):
        return jnp.concatenate([grid_ref[grid_rows(parts, plane, xq, tx), :] for plane in range(BZ)], axis=0)

    def sines(tx, _):
        for half in range(2):
            lines = jnp.concatenate([planes(tx, half * 2), planes(tx, half * 2 + 1)], axis=1)
            both = dot(plane_ref[...], jnp.concatenate(split(lines), axis=0))
            modes = both[:PLANES] + both[PLANES:]
            modes_ref[tx * 4 + half * 2] = modes[:, :LANES]
            modes_ref[tx * 4 + half * 2 + 1] = modes[:, LANES:]
        return 0

    lax.fori_loop(0, 16, sines, 0, unroll=8)
    root, _ = roots(own_ref, base_ref, lam_ref)
    root_ref[...] = root

    part_rows = 64
    low = low_half((part_rows, LANES))
    for part in range(PLANES // part_rows):
        here = pl.ds(part * part_rows, part_rows)
        root = root_ref[here, :]
        square = root * root

        def walk(step, held):
            ahead, behind = modes_ref[step, here, :], modes_ref[STEPS - 1 - step, here, :]
            own = jnp.where(low, behind, ahead)
            other = pltpu.roll(jnp.where(low, ahead, behind), HALF, 1)
            held = square * held + (own + root * other)
            walk_ref[step, here, :] = held
            return held

        end_ref[here, :] = lax.fori_loop(0, STEPS, walk, jnp.zeros((part_rows, LANES), jnp.float32), unroll=8)


def up_kernel(parts, own_ref, walk_ref, *refs):
    end_refs, (plane_in, base_in, lam_in) = refs[:GROUPS], refs[GROUPS : GROUPS + 3]
    sent_refs = refs[GROUPS + 3 : GROUPS + 3 + parts * SLABS]
    (full_ref, grid_ref, root_ref, gain_ref, level_ref, inverse_ref, plane_ref, base_ref, lam_ref, sems) = refs[
        GROUPS + 3 + parts * SLABS :
    ]
    copies = start_copies(((base_in, base_ref), (lam_in, lam_ref), (plane_in, plane_ref)), sems)
    for each in copies[:2]:
        each.wait()
    root, spread = roots(own_ref, base_ref, lam_ref)
    root_ref[...] = root
    gain_ref[...] = 1.0 / spread
    part_rows = 64
    low = low_half((part_rows, LANES))
    for part in range(PLANES // part_rows):
        here = pl.ds(part * part_rows, part_rows)
        root = root_ref[here, :]
        square = root * root
        across = square
        for _ in range(6):
            across = across * across
        entering = jnp.zeros((part_rows, LANES), jnp.float32)
        for step in range(GROUPS - 1, -1, -1):
            before = end_refs[(step + 1) % GROUPS][here, :]
            after = end_refs[GROUPS - 1 - step][here, :]
            entering = entering * across + jnp.where(low, after, before)
        around = across
        for _ in range(2):
            around = around * around
        entering = entering / (1.0 - around)
        full_ref[0, here, :] = entering

        def carry(step, reach):
            full_ref[step + 1, here, :] = walk_ref[step, here, :] + reach
            return reach * square

        lax.fori_loop(0, STEPS, carry, entering * square, unroll=8)
    copies[2].wait()

    def solved(step):
        low = low_half((PLANES, LANES))
        near = jnp.where(low, full_ref[STEPS - step], full_ref[step + 1])
        far = jnp.where(low, full_ref[STEPS - 1 - step], full_ref[step])
        return gain_ref[...] * (near + root_ref[...] * pltpu.roll(far, HALF, 1))

    def sines(tx, _):
        for half in range(2):
            first = tx * 4 + half * 2
            modes = jnp.concatenate([solved(first), solved(first + 1)], axis=1)
            both = dot(plane_ref[...], jnp.concatenate(split(modes), axis=0))
            lines = both[:PLANES] + both[PLANES:]
            for one in range(2):
                for plane in range(BZ):
                    grid_ref[grid_rows(parts, plane, half * 2 + one, tx), :] = lines[
                        plane * 32 : (plane + 1) * 32, one * LANES : (one + 1) * LANES
                    ]
        return 0

    lax.fori_loop(0, 16, sines, 0, unroll=8)
    rows = BRICK_ROWS // parts * SPOTS
    for part in range(parts):
        here = pl.ds(part * rows * SLABS, rows * SLABS)
        most = jnp.max(jnp.abs(grid_ref[here, :]).reshape(rows, SLABS, LANES), axis=0)
        level_ref[...] = level_of(most)
        inverse_ref[...] = inverse_of(level_of(most))
        for offset in range(SLABS):
            sent_ref = sent_refs[part * SLABS + offset]
            g = own_ref[0] ^ offset
            block = grid_ref[pl.ds(part * rows * SLABS + g, rows, stride=SLABS), :]
            sent_ref[:rows, :] = fixed_of(block * inverse_ref[pl.ds(g, 1), :])
            sent_ref[rows:, :] = head_of(level_ref[pl.ds(g, 1), :])


def reply_kernel(parts, own_ref, *refs):
    got_refs = refs[:SLABS]
    picks_ref, table_ref, out_ref, lines_ref, pot_ref, slots_ref, left_ref = refs[SLABS:]
    part_rows = BRICK_ROWS // parts
    for offset, got_ref in enumerate(got_refs):
        lines_ref[own_ref[0] ^ offset] = wide(got_ref)

    def load(block, step):
        return lines_ref[block, step * 4 * SPOTS : (step + 1) * 4 * SPOTS, :]

    def store(block, part, values):
        for one in range(8):
            q = part * 8 + one
            pot_ref[block * SPOTS : (block + 1) * SPOTS, q * LANES : (q + 1) * LANES] = values[
                one * SPOTS : (one + 1) * SPOTS
            ].astype(jnp.bfloat16)

    line_transform(part_rows * SPOTS, load, store, table_ref, left_ref)
    for q in range(0, part_rows, 4):
        both = dot(picks_ref[...], pot_ref[:, q * LANES : (q + 4) * LANES])
        for one in range(4):
            slots_ref[pl.ds(q + one, SLOTS, stride=part_rows), :] = both[:, one * LANES : (one + 1) * LANES]
    pair_rows = PAIR_SLOTS * part_rows
    for domain in range(DOMAINS):
        out_ref[domain] = slots_ref[domain * pair_rows : (domain + 1) * pair_rows, :].astype(jnp.bfloat16)


def unpack_kernel(parts, slot_ref, count_ref, *refs):
    got_refs, (out_ref, slots_ref, rows_ref) = refs[:parts], refs[parts:]
    part_rows = BRICK_ROWS // parts
    brick_rows = out_ref.shape[0]
    pair_rows = PAIR_SLOTS * part_rows
    rows_ref[...] = jnp.zeros(rows_ref.shape, jnp.float32)
    for domain in range(DOMAINS):
        for part, got_ref in enumerate(got_refs):
            slots_ref[part, domain * pair_rows : (domain + 1) * pair_rows, :] = got_ref[domain].astype(jnp.float32)

    def place(r, _):
        slot = slot_ref[r]
        for part in range(parts):
            brick = slots_ref[part, pl.ds(pl.multiple_of(slot * part_rows, part_rows), part_rows), :]
            rows_ref[pl.ds(pl.multiple_of(r * BRICK_ROWS + part * part_rows, part_rows), part_rows), :] = brick
        return 0

    lax.fori_loop(0, count_ref[0], place, 0)
    for q in range(BRICK_ROWS):
        block = rows_ref[pl.ds(q, brick_rows, stride=BRICK_ROWS), :]
        out_ref[:, q * LANES : (q + 1) * LANES] = block.astype(jnp.bfloat16)


def call(kernel, outs, places, scratch, operands, spaces, name):
    return pl.pallas_call(
        kernel,
        out_shape=outs,
        in_specs=[pl.BlockSpec(memory_space=space) for space in spaces],
        out_specs=[pl.BlockSpec(memory_space=space) for space in places],
        scratch_shapes=scratch,
        compiler_params=pltpu.CompilerParams(vmem_limit_bytes=VMEM_BYTES),
        name=name,
    )(*operands)


def on_device_8x4(bricks, owners, tile_ids, counts):
    V, S, H = pltpu.VMEM, pltpu.SMEM, pltpu.HBM
    f32, bf16, i32, i16 = jnp.float32, jnp.bfloat16, jnp.int32, jnp.int16
    shape, bind, dma = jax.ShapeDtypeStruct, functools.partial, pltpu.SemaphoreType.DMA
    brick_rows = bricks.shape[0]
    line_table = jnp.asarray(line_tables())
    plane_down, plane_up = (jnp.asarray(each) for each in plane_tables())
    base, lam = (jnp.asarray(each) for each in mode_tables())
    own = lax.axis_index("gz").astype(i32).reshape(1)
    rows_in, rows_back = BRICK_ROWS // PARTS_IN, BRICK_ROWS // PARTS_BACK

    def all_ways(values):
        return lax.all_to_all(values, ("gz", "ma"), split_axis=0, concat_axis=0, tiled=True)

    def over_slabs(values):
        return [values[0]] + [
            lax.ppermute(values[offset], "gz", [(g, g ^ offset) for g in range(SLABS)])
            for offset in range(1, SLABS)
        ]

    def round_groups(values):
        return [values] + [
            lax.ppermute(values, "ma", [(m, (m + step) % GROUPS) for m in range(GROUPS)])
            for step in range(1, GROUPS)
        ]

    packed = [
        ((DOMAINS, PAIR_SLOTS * rows_in + (HEAD_ROWS if part == 0 else 0), LANES), bf16) for part in range(PARTS_IN)
    ]
    *outgoing, slots = call(
        bind(pack_kernel, PARTS_IN),
        [shape(*each) for each in packed] + [shape((brick_rows,), i32)],
        [H] * PARTS_IN + [S],
        [
            S((brick_rows,), i32),
            S((brick_rows,), i32),
            S((1,), i32),
            V(bricks.shape, bf16),
            V((brick_rows * BRICK_ROWS, LANES), f32),
            V((PARTS_IN, SLOTS * rows_in, LANES), f32),
            V((SLOTS, LANES), f32),
            S((DOMAINS,), i32),
            dma((4,)),
            dma((4 * PARTS_IN,)),
        ]
        + [V(*each) for each in packed],
        (owners.reshape(brick_rows), tile_ids, counts, bricks),
        [H, H, H, H],
        "pack",
    )
    incoming = [all_ways(each) for each in outgoing]
    sent_shapes = [shape((rows_in * SPOTS + HEAD_ROWS, LANES), i16)] * SLABS
    forward_scratch = [
        V((SLOTS * rows_in, LANES), f32),
        V((SLOTS, rows_in * LANES), bf16),
        V((TILES, rows_in * LANES), f32),
        V((SLABS, rows_in * SPOTS, LANES), f32),
        V((2, rows_in * SPOTS, 2 * NY), bf16),
    ]
    *sent, picks, across = call(
        bind(first_kernel, PARTS_IN),
        sent_shapes + [shape((SLOTS, TILES), bf16), shape((TILES, SLOTS), bf16)],
        [V] * (SLABS + 2),
        forward_scratch,
        (own, incoming[0], line_table),
        [S, V, V],
        "forward",
    )
    got = over_slabs(sent)
    for each in incoming[1:]:
        sent = call(
            bind(later_kernel, PARTS_IN),
            sent_shapes,
            [V] * SLABS,
            forward_scratch,
            (own, each, across, line_table),
            [S, V, V, V],
            "forward_later",
        )
        got += over_slabs(sent)
    cube = (STEPS, PLANES, LANES)
    flat = V((PLANES, LANES), f32)
    grid = V((BRICK_ROWS * SPOTS * SLABS, LANES), f32)
    tables = [V(plane_down.shape, bf16), V(base.shape, f32), V(lam.shape, f32), dma((3,))]
    walk, end = call(
        bind(down_kernel, PARTS_IN),
        [shape(cube, f32), shape((PLANES, LANES), f32)],
        [V, V],
        [grid, V(cube, f32), flat, *tables],
        (own, *got, plane_down, base, lam),
        [S] + [V] * len(got) + [H] * 3,
        "down",
    )
    sent_shapes = [shape((rows_back * SPOTS + HEAD_ROWS, LANES), i16)] * SLABS
    sent = call(
        bind(up_kernel, PARTS_BACK),
        sent_shapes * PARTS_BACK,
        [V] * (PARTS_BACK * SLABS),
        [V((STEPS + 1, PLANES, LANES), f32), grid, flat, flat, V((SLABS, LANES), f32), V((SLABS, LANES), f32), *tables],
        (own, walk, *round_groups(end), plane_up, base, lam),
        [S] + [V] * (1 + GROUPS) + [H] * 3,
        "up",
    )
    returned = []
    for part in range(PARTS_BACK):
        (replies,) = call(
            bind(reply_kernel, PARTS_BACK),
            [shape((DOMAINS, PAIR_SLOTS * rows_back, LANES), bf16)],
            [V],
            [
                V((SLABS, rows_back * SPOTS, LANES), f32),
                V((TILES, rows_back * LANES), bf16),
                V((SLOTS * rows_back, LANES), f32),
                V((2, rows_back * SPOTS, 2 * NY), bf16),
            ],
            (own, *over_slabs(sent[part * SLABS : (part + 1) * SLABS]), picks, line_table),
            [S] + [V] * (SLABS + 2),
            "reply",
        )
        returned.append(all_ways(replies))
    (result,) = call(
        bind(unpack_kernel, PARTS_BACK),
        [shape((brick_rows, BRICK_ROWS * LANES), bf16)],
        [V],
        [V((PARTS_BACK, SLOTS * rows_back, LANES), f32), V((brick_rows * BRICK_ROWS, LANES), f32)],
        (slots, counts, *returned),
        [S, S] + [V] * PARTS_BACK,
        "unpack",
    )
    return result


def solution(mesh):
    in_specs = (P(("gz", "ma"), None), P(("gz", "ma"), None), P(("gz", "ma")), P(("gz", "ma")))
    out_specs = P(("gz", "ma"), None)
    body = on_device_8x4 if (mesh.shape["gz"], mesh.shape["ma"]) == (SLABS, GROUPS) else on_device
    return jax.shard_map(body, mesh=mesh, in_specs=in_specs, out_specs=out_specs, check_vma=False)
```

```python
import functools
import math

import jax
import jax.numpy as jnp
import ml_dtypes
import numpy as np
from jax import lax
from jax.experimental import pallas as pl
from jax.experimental.pallas import tpu as pltpu
from jax.sharding import PartitionSpec as P

NX = 512
NY = 512
SCREEN = 16
BZ = 4
BX = 8
BY = 64
CZ = 16


def hartley(length):
    indices = jnp.arange(length, dtype=jnp.int32)
    products = indices[:, None] * indices[None, :] % length
    angles = 2.0 * math.pi / length * products.astype(jnp.float32)
    return (jnp.cos(angles) + jnp.sin(angles)) / math.sqrt(length)


def second_difference(length, indices):
    return 2.0 - 2.0 * jnp.cos(2.0 * math.pi / length * indices.astype(jnp.float32))


def thomas(right_side, diagonal):
    start_zero = jnp.zeros(right_side.shape[1:], jnp.float32)

    def down(state_pair, plane):
        factor = 1.0 / (diagonal - state_pair[0])
        partial_value = (plane + state_pair[1]) * factor
        return ((factor, partial_value), (factor, partial_value))

    _, (factors, partials) = lax.scan(down, (start_zero, start_zero), right_side)

    def upward(beyond, factor_partial):
        solved = factor_partial[1] + factor_partial[0] * beyond
        return (solved, solved)

    _, solutions = lax.scan(upward, start_zero, (factors, partials), reverse=True)
    return solutions


def regroup(values):
    return lax.all_to_all(values, "ma", split_axis=2, concat_axis=1, tiled=True)


def on_device(bricks, owners, tile_ids, counts):
    domains = lax.axis_size(("gz", "ma"))
    group_count = lax.axis_size("ma")
    slab_count = lax.axis_size("gz")
    brick_rows, brick_cells = bricks.shape
    slot_count = max(2, 2 * brick_rows // domains)
    local_x = NX // group_count
    local_y = NY // group_count
    tiles_dev = CZ // BZ * (local_x // BX) * (NY // BY)
    highest = lax.Precision.HIGHEST
    target = owners[:, 0]
    row_order = jnp.arange(brick_rows, dtype=jnp.int32)
    earlier_same = (target[:, None] == target[None, :]) & (row_order[None, :] < row_order[:, None])
    within = jnp.sum(earlier_same.astype(jnp.int32), axis=1)
    slot_of = target * slot_count + within
    is_live = row_order < counts[0]
    loaded = jnp.where(is_live[:, None], bricks, jnp.zeros_like(bricks))
    outgoing = jnp.zeros((domains * slot_count, brick_cells), jnp.bfloat16).at[slot_of].set(loaded)
    out_ids = jnp.full((domains * slot_count,), tiles_dev, jnp.int32).at[slot_of].set(tile_ids)
    incoming, in_ids = (
        lax.all_to_all(outgoing, ("gz", "ma"), split_axis=0, concat_axis=0, tiled=True),
        lax.all_to_all(out_ids, ("gz", "ma"), split_axis=0, concat_axis=0, tiled=True),
    )
    picker = (jnp.arange(tiles_dev, dtype=jnp.int32)[:, None] == in_ids[None, :]).astype(
        jnp.bfloat16
    )
    deposit = jnp.dot(picker, incoming, preferred_element_type=jnp.float32)
    charge = deposit.reshape(CZ // BZ, local_x // BX, NY // BY, BZ, BX, BY)
    charge = charge.transpose(0, 3, 1, 4, 2, 5).reshape(CZ, local_x, NY)
    table_x = hartley(NX)
    table_y = hartley(NY)
    along_y = jnp.einsum("zxy,ky->zxk", charge, table_y, precision=highest)
    gathered_x = regroup(along_y)
    spectrum = jnp.einsum("zxk,jx->zjk", gathered_x, table_x, precision=highest)
    columns = lax.axis_index("ma") * local_y + jnp.arange(local_y, dtype=jnp.int32)
    lam_y = second_difference(NY, columns)
    screening = 1.0 / (SCREEN * SCREEN)
    slab_index = lax.axis_index("gz")
    lam_x = second_difference(NX, jnp.arange(NX, dtype=jnp.int32))
    diagonal = 2.0 + screening + lam_x[:, None] + lam_y[None, :]
    interior = spectrum[1:]
    particular = thomas(interior, diagonal)
    unit_rhs = jnp.zeros_like(interior).at[0].set(1.0)
    spike = thomas(unit_rhs, diagonal)
    near_weight = spike[0]
    far_weight = spike[-1]
    head_term = spectrum[0] + particular[0]
    tail_term = particular[-1]
    reduced_first = diagonal - near_weight
    reduced_rest = diagonal - 2.0 * near_weight
    start_zero = jnp.zeros_like(diagonal)
    heads, tails = (
        lax.all_gather(head_term[None], "gz", axis=0, tiled=True),
        lax.all_gather(tail_term[None], "gz", axis=0, tiled=True),
    )
    before = jnp.concatenate([start_zero[None], tails[:-1]], axis=0)
    sources = heads + before

    def chain_down(state_pair, packed):
        source, position = packed
        base_term = jnp.where(position == 0, reduced_first, reduced_rest)
        pivot_now = 1.0 / (base_term - far_weight * far_weight * state_pair[0])
        forward_part = pivot_now * (source + far_weight * state_pair[1])
        return ((pivot_now, forward_part), (pivot_now, forward_part))

    _, (pivots, forwards) = lax.scan(
        chain_down, (start_zero, start_zero), (sources, jnp.arange(slab_count, dtype=jnp.int32))
    )

    def chain_up(beyond, packed):
        plane_value = packed[1] + far_weight * packed[0] * beyond
        return (plane_value, plane_value)

    _, separators = lax.scan(chain_up, start_zero, (pivots, forwards), reverse=True)
    padded_sep = jnp.concatenate([separators, start_zero[None]], axis=0)
    own_plane = lax.dynamic_index_in_dim(padded_sep, slab_index, 0, keepdims=False)
    next_plane = lax.dynamic_index_in_dim(padded_sep, slab_index + 1, 0, keepdims=False)
    interior_sol = particular + own_plane[None] * spike + next_plane[None] * spike[::-1]
    modal = jnp.concatenate([own_plane[None], interior_sol], axis=0)
    back_x = jnp.einsum("zjk,jx->zkx", modal, table_x, precision=highest)
    gathered_y = regroup(back_x)
    potential = jnp.einsum("zkx,ky->zxy", gathered_y, table_y, precision=highest)
    pot_tiles = potential.reshape(CZ // BZ, BZ, local_x // BX, BX, NY // BY, BY)
    pot_tiles = (
        pot_tiles.transpose(0, 2, 4, 1, 3, 5).reshape(tiles_dev, brick_cells).astype(jnp.bfloat16)
    )
    padded_tiles = jnp.concatenate([pot_tiles, jnp.zeros((1, brick_cells), jnp.bfloat16)], axis=0)
    replies = padded_tiles[in_ids]
    returned = lax.all_to_all(replies, ("gz", "ma"), split_axis=0, concat_axis=0, tiled=True)
    result = returned[slot_of]
    return jnp.where(is_live[:, None], result, jnp.zeros_like(result))


PARTS_IN = 1
PARTS_BACK = 1
DOMAINS = 32
GROUPS = 4
SLABS = 8
PAIR_SLOTS = 8
SLOTS = DOMAINS * PAIR_SLOTS
TILES = 512
BRICK_ROWS = 16
LANES = 128
HALF = 64
SPOTS = 64
HEAD_ROWS = 16
PLACE_ROWS = 8
ORDER = (4, 2, 6, 5, 3, 7, 1)
STEPS = 64
PLANES = 128
FULL = 32700.0
LOG_UNIT = 128.0
VMEM_BYTES = 24 * 1024 * 1024
ALL_VMEM_BYTES = 60 * 1024 * 1024


def split_table(table):
    high = table.astype(ml_dtypes.bfloat16)
    low = (table - high.astype(np.float64)).astype(ml_dtypes.bfloat16)
    return high, low


def line_tables():
    index = np.arange(NY)
    angle = 2.0 * np.pi / NY * (index[:, None] * index[None, :] % NY)
    table = (np.cos(angle) + np.sin(angle)) / np.sqrt(NY)
    swapped = table.reshape(NY, NY // LANES, 2, HALF)[:, :, ::-1].reshape(NY, NY)
    return np.stack([*split_table(table), *split_table(swapped)])


def plane_tables():
    index = np.arange(PLANES)
    table = np.sqrt(2.0 / (PLANES + 1)) * np.sin(
        np.pi / (PLANES + 1) * ((index[:, None] + 1) * (index[None, :] + 1) % (2 * PLANES + 2))
    )
    plane_of = index % SLABS * CZ + index // SLABS % BZ * BZ + index // 32
    down = table[:, plane_of]
    both = []
    for each in (down, down.T):
        high, low = split_table(each)
        top = np.concatenate([high, high], axis=1)
        bottom = np.concatenate([low, np.zeros_like(low)], axis=1)
        both.append(np.concatenate([top, bottom], axis=0))
    return both


def mode_tables():
    mu = 2.0 - 2.0 * np.cos(np.pi / (PLANES + 1) * (np.arange(PLANES) + 1))
    base = np.broadcast_to((mu + 1.0 / (SCREEN * SCREEN))[:, None], (PLANES, LANES))
    lam = 2.0 - 2.0 * np.cos(2.0 * np.pi / NY * np.arange(NY))
    lam = lam.reshape(NY // HALF, HALF)
    return base.astype(np.float32), np.concatenate([lam, lam], axis=1).astype(np.float32)


def low_half(shape):
    return lax.broadcasted_iota(jnp.int32, shape, len(shape) - 1) < HALF


def split(values):
    high = values.astype(jnp.bfloat16)
    return high, (values - high.astype(jnp.float32)).astype(jnp.bfloat16)


def dot(left, right):
    return jnp.dot(left, right, preferred_element_type=jnp.float32)


def start_copies(pairs, sems):
    copies = [pltpu.make_async_copy(source, place, sems.at[at]) for at, (source, place) in enumerate(pairs)]
    for each in copies:
        each.start()
    return copies


def line_transform(rows, load, store, table_ref, left_ref):
    low = low_half((4 * SPOTS, LANES))
    for step in range(rows // (4 * SPOTS)):
        evens, odds = [], []
        for pair in range(4):
            first, second = load(2 * pair, step), load(2 * pair + 1, step)
            crossed = pltpu.roll(jnp.where(low, second, first), HALF, 1)
            evens.append(jnp.where(low, first, crossed))
            odds.append(jnp.where(low, crossed, second))
        here = slice(step * 4 * SPOTS, (step + 1) * 4 * SPOTS)
        for at, lines in enumerate((evens, odds)):
            high, rest = split(jnp.concatenate(lines, axis=1))
            left_ref[at, here, :NY] = high
            left_ref[at, here, NY:] = rest
    block = 512
    low = low_half((block, LANES))
    for part in range(rows // block):
        here = slice(part * block, (part + 1) * block)
        for columns in range(0, NY, 2 * LANES):
            there = slice(columns, columns + 2 * LANES)
            products = []
            for at in range(2):
                left = jnp.concatenate([left_ref[at, here, :], left_ref[at, here, :NY]], axis=1)
                main = table_ref[2 * at, :, there]
                right = jnp.concatenate([main, main, table_ref[2 * at + 1, :, there]], axis=0)
                products.append(dot(left, right))
            for pair in range(2):
                even, odd = (each[:, pair * LANES : (pair + 1) * LANES] for each in products)
                g = columns // HALF + 2 * pair
                store(g, part, jnp.where(low, even, odd))
                store(g + 1, part, pltpu.roll(jnp.where(low, odd, even), HALF, 1))


def level_of(most):
    return jnp.floor(jnp.log2(jnp.maximum(most, 1e-30)) * LOG_UNIT) + 2.0


def inverse_of(level):
    return FULL * jnp.exp2(level * (-1.0 / LOG_UNIT))


def fixed_of(values):
    return jnp.floor(values + 0.5).astype(jnp.int32).astype(jnp.int16)


def head_of(level):
    return jnp.broadcast_to(level, (HEAD_ROWS, LANES)).astype(jnp.int32).astype(jnp.int16)


def unit_of(sent_ref):
    head = sent_ref[sent_ref.shape[0] - HEAD_ROWS :, :].astype(jnp.int32).astype(jnp.float32)
    return jnp.exp2(head[0:1] * (1.0 / LOG_UNIT)) * (1.0 / FULL)


def wide(sent_ref):
    block = sent_ref[: sent_ref.shape[0] - HEAD_ROWS, :]
    return block.astype(jnp.int32).astype(jnp.float32) * unit_of(sent_ref)


def pack_kernel(parts, owner_in, tile_in, count_in, brick_in, *refs):
    outs, slot_ref = refs[:parts], refs[parts]
    (owner_ref, tile_ref, count_ref, brick_ref, rows_ref, slots_ref, head_ref, used_ref, sems, out_sems, *ready) = refs[
        parts + 1 :
    ]
    part_rows = BRICK_ROWS // parts
    pair_rows = PAIR_SLOTS * part_rows
    copies = start_copies(
        ((brick_in, brick_ref), (owner_in, owner_ref), (tile_in, tile_ref), (count_in, count_ref)), sems
    )
    brick_rows = brick_ref.shape[0]
    head_ref[...] = jnp.full(head_ref.shape, float(TILES), jnp.float32)
    slots_ref[...] = jnp.zeros(slots_ref.shape, jnp.float32)
    for owner in range(DOMAINS):
        used_ref[owner] = 0
    for each in copies:
        each.wait()
    for q in range(BRICK_ROWS):
        block = brick_ref[:, q * LANES : (q + 1) * LANES].astype(jnp.float32)
        rows_ref[pl.ds(q, brick_rows, stride=BRICK_ROWS), :] = block

    count = count_ref[0]

    def place(r, _):
        owner = owner_ref[r]
        within = used_ref[owner]
        used_ref[owner] = within + 1
        own_slot = owner * PAIR_SLOTS + within
        slot_ref[r] = own_slot
        slot = jnp.where(r < count, own_slot, SLOTS)
        tile = tile_ref[r]
        line = tile // 8
        position = tile % 8 * SPOTS + line % 16 * 4 + line // 16
        for part in range(parts):
            brick = rows_ref[pl.ds(pl.multiple_of(r * BRICK_ROWS + part * part_rows, part_rows), part_rows), :]
            slots_ref[part, pl.ds(pl.multiple_of(slot * part_rows, part_rows), part_rows), :] = brick
        head_ref[pl.ds(slot, 1), :] = jnp.full((1, LANES), position, jnp.int32).astype(jnp.float32)
        return 0

    lax.fori_loop(0, brick_rows, place, 0, unroll=4)
    copies = []
    for part in range(parts):
        for owner in range(DOMAINS):
            block = slots_ref[part, owner * pair_rows : (owner + 1) * pair_rows, :]
            ready[part][owner, :pair_rows, :] = block.astype(jnp.bfloat16)
            if part == 0:
                head = head_ref[owner * PAIR_SLOTS : (owner + 1) * PAIR_SLOTS, :]
                high = jnp.floor(head * (1.0 / 32.0))
                both = jnp.where(low_half(head.shape), high, head - 32.0 * high)
                ready[part][owner, pair_rows:, :] = both.astype(jnp.bfloat16)
            if owner % 8 == 7:
                some = pl.ds(owner - 7, 8)
                copy = pltpu.make_async_copy(
                    ready[part].at[some], outs[part].at[some], out_sems.at[part * 4 + owner // 8]
                )
                copy.start()
                copies.append(copy)
    for each in copies:
        each.wait()


def write_picks(brick_ref, pair_rows, picks_ref, across_ref):
    for block in range(TILES // LANES):
        there = slice(block * LANES, (block + 1) * LANES)
        for part in range(SLOTS // LANES):
            pieces = []
            for domain in range(part * 16, part * 16 + 16):
                head = brick_ref[domain, pair_rows:, :].astype(jnp.float32)
                turned = pltpu.roll(head, HALF, 1)
                low = low_half(head.shape)
                places = (jnp.where(low, head, turned) * 32.0 + jnp.where(low, turned, head)).astype(jnp.int32)
                lane = lax.broadcasted_iota(jnp.int32, (PAIR_SLOTS, LANES), 1) + block * LANES
                pieces.append(jnp.where(places == lane, 1.0, 0.0))
            square = jnp.concatenate(pieces, axis=0)
            here = slice(part * LANES, (part + 1) * LANES)
            picks_ref[here, there] = square.astype(jnp.bfloat16)
            across_ref[there, here] = square.T.astype(jnp.bfloat16)


def forward_body(parts, own_ref, brick_ref, across_ref, table_ref, sent_refs, slots_ref, wide_ref, charge_ref, lines_ref, left_ref):
    part_rows = BRICK_ROWS // parts
    pair_rows = PAIR_SLOTS * part_rows
    for domain in range(DOMAINS):
        slots_ref[domain * pair_rows : (domain + 1) * pair_rows, :] = brick_ref[domain, :pair_rows, :].astype(jnp.float32)
    for q in range(part_rows):
        wide_ref[:, q * LANES : (q + 1) * LANES] = slots_ref[pl.ds(q, SLOTS, stride=part_rows), :].astype(jnp.bfloat16)
    for q in range(0, part_rows, 4):
        there = slice(q * LANES, (q + 4) * LANES)
        charge_ref[:, there] = dot(across_ref[...], wide_ref[:, there])

    def load(block, step):
        return jnp.concatenate(
            [
                charge_ref[block * SPOTS : (block + 1) * SPOTS, q * LANES : (q + 1) * LANES]
                for q in range(step * 4, step * 4 + 4)
            ],
            axis=0,
        )

    def store(block, part, values):
        lines_ref[block, part * 512 : (part + 1) * 512, :] = values

    rows = part_rows * SPOTS
    line_transform(rows, load, store, table_ref, left_ref)
    for offset, sent_ref in enumerate(sent_refs):
        block = lines_ref[own_ref[0] ^ offset]
        most = jnp.max(jnp.abs(block).reshape(rows // 8, 8, LANES), axis=0)
        level = level_of(jnp.max(most, axis=0, keepdims=True))
        sent_ref[:rows, :] = fixed_of(block * inverse_of(level))
        sent_ref[rows:, :] = head_of(level)


def first_kernel(parts, own_ref, brick_ref, table_ref, *refs):
    sent_refs, picks_ref, across_ref = refs[:SLABS], refs[SLABS], refs[SLABS + 1]
    write_picks(brick_ref, PAIR_SLOTS * BRICK_ROWS // parts, picks_ref, across_ref)
    forward_body(parts, own_ref, brick_ref, across_ref, table_ref, sent_refs, *refs[SLABS + 2 :])


def later_kernel(parts, own_ref, brick_ref, across_ref, table_ref, *refs):
    forward_body(parts, own_ref, brick_ref, across_ref, table_ref, refs[:SLABS], *refs[SLABS:])


def roots(own_ref, base_ref, lam_ref):
    excess = base_ref[...] + lam_ref[pl.ds(own_ref[0], 1), :]
    spread = jnp.sqrt(excess * (excess + 4.0))
    root = 2.0 / (2.0 + excess + spread)
    return root, spread


def grid_rows(parts, plane, xq, tx):
    planes = BZ // parts
    row = (plane // planes) * planes * 4 * SPOTS + (plane % planes * 4 + xq) * SPOTS + tx * 4
    return pl.ds(pl.multiple_of(row * SLABS, 32), 32)


def down_kernel(parts, own_ref, *refs):
    got_refs = refs[: parts * SLABS]
    (plane_in, base_in, lam_in, walk_ref, end_ref, grid_ref, modes_ref, root_ref, plane_ref, base_ref, lam_ref, sems) = refs[
        parts * SLABS :
    ]
    copies = start_copies(((plane_in, plane_ref), (base_in, base_ref), (lam_in, lam_ref)), sems)
    for at, got_ref in enumerate(got_refs):
        part, offset = at // SLABS, at % SLABS
        block = wide(got_ref)
        rows = block.shape[0]
        grid_ref[pl.ds(part * rows * SLABS + (own_ref[0] ^ offset), rows, stride=SLABS), :] = block
    for each in copies:
        each.wait()

    def planes(tx, xq):
        return jnp.concatenate([grid_ref[grid_rows(parts, plane, xq, tx), :] for plane in range(BZ)], axis=0)

    def sines(tx, _):
        for half in range(2):
            lines = jnp.concatenate([planes(tx, half * 2), planes(tx, half * 2 + 1)], axis=1)
            both = dot(plane_ref[...], jnp.concatenate(split(lines), axis=0))
            modes = both[:PLANES] + both[PLANES:]
            modes_ref[tx * 4 + half * 2] = modes[:, :LANES]
            modes_ref[tx * 4 + half * 2 + 1] = modes[:, LANES:]
        return 0

    lax.fori_loop(0, 16, sines, 0, unroll=8)
    root, _ = roots(own_ref, base_ref, lam_ref)
    root_ref[...] = root

    part_rows = 64
    low = low_half((part_rows, LANES))
    for part in range(PLANES // part_rows):
        here = pl.ds(part * part_rows, part_rows)
        root = root_ref[here, :]
        square = root * root

        def walk(step, held):
            ahead, behind = modes_ref[step, here, :], modes_ref[STEPS - 1 - step, here, :]
            own = jnp.where(low, behind, ahead)
            other = pltpu.roll(jnp.where(low, ahead, behind), HALF, 1)
            held = square * held + (own + root * other)
            walk_ref[step, here, :] = held
            return held

        end_ref[here, :] = lax.fori_loop(0, STEPS, walk, jnp.zeros((part_rows, LANES), jnp.float32), unroll=8)


def up_kernel(parts, own_ref, walk_ref, *refs):
    end_refs, (plane_in, base_in, lam_in) = refs[:GROUPS], refs[GROUPS : GROUPS + 3]
    sent_refs = refs[GROUPS + 3 : GROUPS + 3 + parts * SLABS]
    (full_ref, grid_ref, root_ref, gain_ref, level_ref, inverse_ref, plane_ref, base_ref, lam_ref, sems) = refs[
        GROUPS + 3 + parts * SLABS :
    ]
    copies = start_copies(((base_in, base_ref), (lam_in, lam_ref), (plane_in, plane_ref)), sems)
    for each in copies[:2]:
        each.wait()
    root, spread = roots(own_ref, base_ref, lam_ref)
    root_ref[...] = root
    gain_ref[...] = 1.0 / spread
    part_rows = 64
    low = low_half((part_rows, LANES))
    for part in range(PLANES // part_rows):
        here = pl.ds(part * part_rows, part_rows)
        root = root_ref[here, :]
        square = root * root
        across = square
        for _ in range(6):
            across = across * across
        entering = jnp.zeros((part_rows, LANES), jnp.float32)
        for step in range(GROUPS - 1, -1, -1):
            before = end_refs[(step + 1) % GROUPS][here, :]
            after = end_refs[GROUPS - 1 - step][here, :]
            entering = entering * across + jnp.where(low, after, before)
        around = across
        for _ in range(2):
            around = around * around
        entering = entering / (1.0 - around)
        full_ref[0, here, :] = entering

        def carry(step, reach):
            full_ref[step + 1, here, :] = walk_ref[step, here, :] + reach
            return reach * square

        lax.fori_loop(0, STEPS, carry, entering * square, unroll=8)
    copies[2].wait()

    def solved(step):
        low = low_half((PLANES, LANES))
        near = jnp.where(low, full_ref[STEPS - step], full_ref[step + 1])
        far = jnp.where(low, full_ref[STEPS - 1 - step], full_ref[step])
        return gain_ref[...] * (near + root_ref[...] * pltpu.roll(far, HALF, 1))

    def sines(tx, _):
        for half in range(2):
            first = tx * 4 + half * 2
            modes = jnp.concatenate([solved(first), solved(first + 1)], axis=1)
            both = dot(plane_ref[...], jnp.concatenate(split(modes), axis=0))
            lines = both[:PLANES] + both[PLANES:]
            for one in range(2):
                for plane in range(BZ):
                    grid_ref[grid_rows(parts, plane, half * 2 + one, tx), :] = lines[
                        plane * 32 : (plane + 1) * 32, one * LANES : (one + 1) * LANES
                    ]
        return 0

    lax.fori_loop(0, 16, sines, 0, unroll=8)
    rows = BRICK_ROWS // parts * SPOTS
    for part in range(parts):
        here = pl.ds(part * rows * SLABS, rows * SLABS)
        most = jnp.max(jnp.abs(grid_ref[here, :]).reshape(rows, SLABS, LANES), axis=0)
        level_ref[...] = level_of(most)
        inverse_ref[...] = inverse_of(level_of(most))
        for offset in range(SLABS):
            sent_ref = sent_refs[part * SLABS + offset]
            g = own_ref[0] ^ offset
            block = grid_ref[pl.ds(part * rows * SLABS + g, rows, stride=SLABS), :]
            sent_ref[:rows, :] = fixed_of(block * inverse_ref[pl.ds(g, 1), :])
            sent_ref[rows:, :] = head_of(level_ref[pl.ds(g, 1), :])


def reply_kernel(parts, own_ref, *refs):
    got_refs = refs[:SLABS]
    picks_ref, table_ref, out_ref, lines_ref, pot_ref, slots_ref, left_ref = refs[SLABS:]
    part_rows = BRICK_ROWS // parts
    for offset, got_ref in enumerate(got_refs):
        lines_ref[own_ref[0] ^ offset] = wide(got_ref)

    def load(block, step):
        return lines_ref[block, step * 4 * SPOTS : (step + 1) * 4 * SPOTS, :]

    def store(block, part, values):
        for one in range(8):
            q = part * 8 + one
            pot_ref[block * SPOTS : (block + 1) * SPOTS, q * LANES : (q + 1) * LANES] = values[
                one * SPOTS : (one + 1) * SPOTS
            ].astype(jnp.bfloat16)

    line_transform(part_rows * SPOTS, load, store, table_ref, left_ref)
    for q in range(0, part_rows, 4):
        both = dot(picks_ref[...], pot_ref[:, q * LANES : (q + 4) * LANES])
        for one in range(4):
            slots_ref[pl.ds(q + one, SLOTS, stride=part_rows), :] = both[:, one * LANES : (one + 1) * LANES]
    pair_rows = PAIR_SLOTS * part_rows
    for domain in range(DOMAINS):
        out_ref[domain] = slots_ref[domain * pair_rows : (domain + 1) * pair_rows, :].astype(jnp.bfloat16)


def unpack_kernel(parts, slot_ref, count_ref, *refs):
    got_refs, (out_ref, slots_ref, rows_ref) = refs[:parts], refs[parts:]
    part_rows = BRICK_ROWS // parts
    brick_rows = out_ref.shape[0]
    pair_rows = PAIR_SLOTS * part_rows
    for domain in range(DOMAINS):
        for part, got_ref in enumerate(got_refs):
            slots_ref[part, domain * pair_rows : (domain + 1) * pair_rows, :] = got_ref[domain].astype(jnp.float32)

    count = count_ref[0]

    def place(r, _):
        slot = slot_ref[r]
        for part in range(parts):
            brick = slots_ref[part, pl.ds(pl.multiple_of(slot * part_rows, part_rows), part_rows), :]
            brick = jnp.where(r < count, brick, 0.0)
            rows_ref[pl.ds(pl.multiple_of(r * BRICK_ROWS + part * part_rows, part_rows), part_rows), :] = brick
        return 0

    lax.fori_loop(0, brick_rows, place, 0, unroll=8)
    for q in range(BRICK_ROWS):
        block = rows_ref[pl.ds(q, brick_rows, stride=BRICK_ROWS), :]
        out_ref[:, q * LANES : (q + 1) * LANES] = block.astype(jnp.bfloat16)


def call(kernel, outs, places, scratch, operands, spaces, name, vmem=VMEM_BYTES):
    return pl.pallas_call(
        kernel,
        out_shape=outs,
        in_specs=[pl.BlockSpec(memory_space=space) for space in spaces],
        out_specs=[pl.BlockSpec(memory_space=space) for space in places],
        scratch_shapes=scratch,
        compiler_params=pltpu.CompilerParams(vmem_limit_bytes=vmem),
        name=name,
    )(*operands)


def on_device_8x4(bricks, owners, tile_ids, counts):
    V, S, H = pltpu.VMEM, pltpu.SMEM, pltpu.HBM
    f32, bf16, i32, i16 = jnp.float32, jnp.bfloat16, jnp.int32, jnp.int16
    shape, bind, dma = jax.ShapeDtypeStruct, functools.partial, pltpu.SemaphoreType.DMA
    brick_rows = bricks.shape[0]
    line_table = jnp.asarray(line_tables())
    plane_down, plane_up = (jnp.asarray(each) for each in plane_tables())
    base, lam = (jnp.asarray(each) for each in mode_tables())
    own = lax.axis_index("gz").astype(i32).reshape(1)
    rows_in, rows_back = BRICK_ROWS // PARTS_IN, BRICK_ROWS // PARTS_BACK

    def all_ways(values):
        return lax.all_to_all(values, ("gz", "ma"), split_axis=0, concat_axis=0, tiled=True)

    def over_slabs(values):
        got = {
            offset: lax.ppermute(values[offset], "gz", [(g, g ^ offset) for g in range(SLABS)]) for offset in ORDER
        }
        return [values[0]] + [got[offset] for offset in range(1, SLABS)]

    def round_groups(values):
        return [values] + [
            lax.ppermute(values, "ma", [(m, (m + step) % GROUPS) for m in range(GROUPS)])
            for step in range(1, GROUPS)
        ]

    packed = [
        ((DOMAINS, PAIR_SLOTS * rows_in + (PLACE_ROWS if part == 0 else 0), LANES), bf16) for part in range(PARTS_IN)
    ]
    *outgoing, slots = call(
        bind(pack_kernel, PARTS_IN),
        [shape(*each) for each in packed] + [shape((brick_rows,), i32)],
        [H] * PARTS_IN + [S],
        [
            S((brick_rows,), i32),
            S((brick_rows,), i32),
            S((1,), i32),
            V(bricks.shape, bf16),
            V((brick_rows * BRICK_ROWS, LANES), f32),
            V((PARTS_IN, (SLOTS + 1) * rows_in, LANES), f32),
            V((SLOTS + PAIR_SLOTS, LANES), f32),
            S((DOMAINS,), i32),
            dma((4,)),
            dma((4 * PARTS_IN,)),
        ]
        + [V(*each) for each in packed],
        (owners.reshape(brick_rows), tile_ids, counts, bricks),
        [H, H, H, H],
        "pack",
        ALL_VMEM_BYTES,
    )
    incoming = [all_ways(each) for each in outgoing]
    sent_shapes = [shape((rows_in * SPOTS + HEAD_ROWS, LANES), i16)] * SLABS
    forward_scratch = [
        V((SLOTS * rows_in, LANES), f32),
        V((SLOTS, rows_in * LANES), bf16),
        V((TILES, rows_in * LANES), f32),
        V((SLABS, rows_in * SPOTS, LANES), f32),
        V((2, rows_in * SPOTS, 2 * NY), bf16),
    ]
    *sent, picks, across = call(
        bind(first_kernel, PARTS_IN),
        sent_shapes + [shape((SLOTS, TILES), bf16), shape((TILES, SLOTS), bf16)],
        [V] * (SLABS + 2),
        forward_scratch,
        (own, incoming[0], line_table),
        [S, V, V],
        "forward",
    )
    got = over_slabs(sent)
    for each in incoming[1:]:
        sent = call(
            bind(later_kernel, PARTS_IN),
            sent_shapes,
            [V] * SLABS,
            forward_scratch,
            (own, each, across, line_table),
            [S, V, V, V],
            "forward_later",
        )
        got += over_slabs(sent)
    cube = (STEPS, PLANES, LANES)
    flat = V((PLANES, LANES), f32)
    grid = V((BRICK_ROWS * SPOTS * SLABS, LANES), f32)
    tables = [V(plane_down.shape, bf16), V(base.shape, f32), V(lam.shape, f32), dma((3,))]
    walk, end = call(
        bind(down_kernel, PARTS_IN),
        [shape(cube, f32), shape((PLANES, LANES), f32)],
        [V, V],
        [grid, V(cube, f32), flat, *tables],
        (own, *got, plane_down, base, lam),
        [S] + [V] * len(got) + [H] * 3,
        "down",
    )
    sent_shapes = [shape((rows_back * SPOTS + HEAD_ROWS, LANES), i16)] * SLABS
    sent = call(
        bind(up_kernel, PARTS_BACK),
        sent_shapes * PARTS_BACK,
        [V] * (PARTS_BACK * SLABS),
        [V((STEPS + 1, PLANES, LANES), f32), grid, flat, flat, V((SLABS, LANES), f32), V((SLABS, LANES), f32), *tables],
        (own, walk, *round_groups(end), plane_up, base, lam),
        [S] + [V] * (1 + GROUPS) + [H] * 3,
        "up",
    )
    returned = []
    for part in range(PARTS_BACK):
        (replies,) = call(
            bind(reply_kernel, PARTS_BACK),
            [shape((DOMAINS, PAIR_SLOTS * rows_back, LANES), bf16)],
            [V],
            [
                V((SLABS, rows_back * SPOTS, LANES), f32),
                V((TILES, rows_back * LANES), bf16),
                V((SLOTS * rows_back, LANES), f32),
                V((2, rows_back * SPOTS, 2 * NY), bf16),
            ],
            (own, *over_slabs(sent[part * SLABS : (part + 1) * SLABS]), picks, line_table),
            [S] + [V] * (SLABS + 2),
            "reply",
        )
        returned.append(all_ways(replies))
    (result,) = call(
        bind(unpack_kernel, PARTS_BACK),
        [shape((brick_rows, BRICK_ROWS * LANES), bf16)],
        [V],
        [V((PARTS_BACK, SLOTS * rows_back, LANES), f32), V((brick_rows * BRICK_ROWS, LANES), f32)],
        (slots, counts, *returned),
        [S, S] + [V] * PARTS_BACK,
        "unpack",
    )
    return result


def solution(mesh):
    in_specs = (P(("gz", "ma"), None), P(("gz", "ma"), None), P(("gz", "ma")), P(("gz", "ma")))
    out_specs = P(("gz", "ma"), None)
    body = on_device_8x4 if (mesh.shape["gz"], mesh.shape["ma"]) == (SLABS, GROUPS) else on_device
    return jax.shard_map(body, mesh=mesh, in_specs=in_specs, out_specs=out_specs, check_vma=False)
```

```python
import functools
import math

import jax
import jax.numpy as jnp
import ml_dtypes
import numpy as np
from jax import lax
from jax.experimental import pallas as pl
from jax.experimental.pallas import tpu as pltpu
from jax.sharding import PartitionSpec as P

NX = 512
NY = 512
SCREEN = 16
BZ = 4
BX = 8
BY = 64
CZ = 16


def hartley(length):
    indices = jnp.arange(length, dtype=jnp.int32)
    products = indices[:, None] * indices[None, :] % length
    angles = 2.0 * math.pi / length * products.astype(jnp.float32)
    return (jnp.cos(angles) + jnp.sin(angles)) / math.sqrt(length)


def second_difference(length, indices):
    return 2.0 - 2.0 * jnp.cos(2.0 * math.pi / length * indices.astype(jnp.float32))


def thomas(right_side, diagonal):
    start_zero = jnp.zeros(right_side.shape[1:], jnp.float32)

    def down(state_pair, plane):
        factor = 1.0 / (diagonal - state_pair[0])
        partial_value = (plane + state_pair[1]) * factor
        return ((factor, partial_value), (factor, partial_value))

    _, (factors, partials) = lax.scan(down, (start_zero, start_zero), right_side)

    def upward(beyond, factor_partial):
        solved = factor_partial[1] + factor_partial[0] * beyond
        return (solved, solved)

    _, solutions = lax.scan(upward, start_zero, (factors, partials), reverse=True)
    return solutions


def regroup(values):
    return lax.all_to_all(values, "ma", split_axis=2, concat_axis=1, tiled=True)


def on_device(bricks, owners, tile_ids, counts):
    domains = lax.axis_size(("gz", "ma"))
    group_count = lax.axis_size("ma")
    slab_count = lax.axis_size("gz")
    brick_rows, brick_cells = bricks.shape
    slot_count = max(2, 2 * brick_rows // domains)
    local_x = NX // group_count
    local_y = NY // group_count
    tiles_dev = CZ // BZ * (local_x // BX) * (NY // BY)
    highest = lax.Precision.HIGHEST
    target = owners[:, 0]
    row_order = jnp.arange(brick_rows, dtype=jnp.int32)
    earlier_same = (target[:, None] == target[None, :]) & (row_order[None, :] < row_order[:, None])
    within = jnp.sum(earlier_same.astype(jnp.int32), axis=1)
    slot_of = target * slot_count + within
    is_live = row_order < counts[0]
    loaded = jnp.where(is_live[:, None], bricks, jnp.zeros_like(bricks))
    outgoing = jnp.zeros((domains * slot_count, brick_cells), jnp.bfloat16).at[slot_of].set(loaded)
    out_ids = jnp.full((domains * slot_count,), tiles_dev, jnp.int32).at[slot_of].set(tile_ids)
    incoming, in_ids = (
        lax.all_to_all(outgoing, ("gz", "ma"), split_axis=0, concat_axis=0, tiled=True),
        lax.all_to_all(out_ids, ("gz", "ma"), split_axis=0, concat_axis=0, tiled=True),
    )
    picker = (jnp.arange(tiles_dev, dtype=jnp.int32)[:, None] == in_ids[None, :]).astype(
        jnp.bfloat16
    )
    deposit = jnp.dot(picker, incoming, preferred_element_type=jnp.float32)
    charge = deposit.reshape(CZ // BZ, local_x // BX, NY // BY, BZ, BX, BY)
    charge = charge.transpose(0, 3, 1, 4, 2, 5).reshape(CZ, local_x, NY)
    table_x = hartley(NX)
    table_y = hartley(NY)
    along_y = jnp.einsum("zxy,ky->zxk", charge, table_y, precision=highest)
    gathered_x = regroup(along_y)
    spectrum = jnp.einsum("zxk,jx->zjk", gathered_x, table_x, precision=highest)
    columns = lax.axis_index("ma") * local_y + jnp.arange(local_y, dtype=jnp.int32)
    lam_y = second_difference(NY, columns)
    screening = 1.0 / (SCREEN * SCREEN)
    slab_index = lax.axis_index("gz")
    lam_x = second_difference(NX, jnp.arange(NX, dtype=jnp.int32))
    diagonal = 2.0 + screening + lam_x[:, None] + lam_y[None, :]
    interior = spectrum[1:]
    particular = thomas(interior, diagonal)
    unit_rhs = jnp.zeros_like(interior).at[0].set(1.0)
    spike = thomas(unit_rhs, diagonal)
    near_weight = spike[0]
    far_weight = spike[-1]
    head_term = spectrum[0] + particular[0]
    tail_term = particular[-1]
    reduced_first = diagonal - near_weight
    reduced_rest = diagonal - 2.0 * near_weight
    start_zero = jnp.zeros_like(diagonal)
    heads, tails = (
        lax.all_gather(head_term[None], "gz", axis=0, tiled=True),
        lax.all_gather(tail_term[None], "gz", axis=0, tiled=True),
    )
    before = jnp.concatenate([start_zero[None], tails[:-1]], axis=0)
    sources = heads + before

    def chain_down(state_pair, packed):
        source, position = packed
        base_term = jnp.where(position == 0, reduced_first, reduced_rest)
        pivot_now = 1.0 / (base_term - far_weight * far_weight * state_pair[0])
        forward_part = pivot_now * (source + far_weight * state_pair[1])
        return ((pivot_now, forward_part), (pivot_now, forward_part))

    _, (pivots, forwards) = lax.scan(
        chain_down, (start_zero, start_zero), (sources, jnp.arange(slab_count, dtype=jnp.int32))
    )

    def chain_up(beyond, packed):
        plane_value = packed[1] + far_weight * packed[0] * beyond
        return (plane_value, plane_value)

    _, separators = lax.scan(chain_up, start_zero, (pivots, forwards), reverse=True)
    padded_sep = jnp.concatenate([separators, start_zero[None]], axis=0)
    own_plane = lax.dynamic_index_in_dim(padded_sep, slab_index, 0, keepdims=False)
    next_plane = lax.dynamic_index_in_dim(padded_sep, slab_index + 1, 0, keepdims=False)
    interior_sol = particular + own_plane[None] * spike + next_plane[None] * spike[::-1]
    modal = jnp.concatenate([own_plane[None], interior_sol], axis=0)
    back_x = jnp.einsum("zjk,jx->zkx", modal, table_x, precision=highest)
    gathered_y = regroup(back_x)
    potential = jnp.einsum("zkx,ky->zxy", gathered_y, table_y, precision=highest)
    pot_tiles = potential.reshape(CZ // BZ, BZ, local_x // BX, BX, NY // BY, BY)
    pot_tiles = (
        pot_tiles.transpose(0, 2, 4, 1, 3, 5).reshape(tiles_dev, brick_cells).astype(jnp.bfloat16)
    )
    padded_tiles = jnp.concatenate([pot_tiles, jnp.zeros((1, brick_cells), jnp.bfloat16)], axis=0)
    replies = padded_tiles[in_ids]
    returned = lax.all_to_all(replies, ("gz", "ma"), split_axis=0, concat_axis=0, tiled=True)
    result = returned[slot_of]
    return jnp.where(is_live[:, None], result, jnp.zeros_like(result))


PARTS_IN = 1
PARTS_BACK = 1
DOMAINS = 32
GROUPS = 4
SLABS = 8
PAIR_SLOTS = 8
SLOTS = DOMAINS * PAIR_SLOTS
TILES = 512
BRICK_ROWS = 16
LANES = 128
HALF = 64
SPOTS = 64
HEAD_ROWS = 16
PLACE_ROWS = 8
OFFSETS = (0, 4, 2, 6, 5, 3, 7, 1)
STEPS = 64
PLANES = 128
FULL = 32700.0
LOG_UNIT = 128.0
VMEM_BYTES = 24 * 1024 * 1024
ALL_VMEM_BYTES = 60 * 1024 * 1024


def split_table(table):
    high = table.astype(ml_dtypes.bfloat16)
    low = (table - high.astype(np.float64)).astype(ml_dtypes.bfloat16)
    return high, low


def line_tables():
    index = np.arange(NY)
    angle = 2.0 * np.pi / NY * (index[:, None] * index[None, :] % NY)
    table = (np.cos(angle) + np.sin(angle)) / np.sqrt(NY)
    swapped = table.reshape(NY, NY // LANES, 2, HALF)[:, :, ::-1].reshape(NY, NY)
    return np.stack([*split_table(table), *split_table(swapped)])


def plane_tables():
    index = np.arange(PLANES)
    table = np.sqrt(2.0 / (PLANES + 1)) * np.sin(
        np.pi / (PLANES + 1) * ((index[:, None] + 1) * (index[None, :] + 1) % (2 * PLANES + 2))
    )
    plane_of = index % SLABS * CZ + index // SLABS % BZ * BZ + index // 32
    down = table[:, plane_of]
    both = []
    for each in (down, down.T):
        high, low = split_table(each)
        top = np.concatenate([high, high], axis=1)
        bottom = np.concatenate([low, np.zeros_like(low)], axis=1)
        both.append(np.concatenate([top, bottom], axis=0))
    return both


def mode_tables():
    mu = 2.0 - 2.0 * np.cos(np.pi / (PLANES + 1) * (np.arange(PLANES) + 1))
    base = np.broadcast_to((mu + 1.0 / (SCREEN * SCREEN))[:, None], (PLANES, LANES))
    lam = 2.0 - 2.0 * np.cos(2.0 * np.pi / NY * np.arange(NY))
    lam = lam.reshape(NY // HALF, HALF)
    return base.astype(np.float32), np.concatenate([lam, lam], axis=1).astype(np.float32)


def low_half(shape):
    return lax.broadcasted_iota(jnp.int32, shape, len(shape) - 1) < HALF


def split(values):
    high = values.astype(jnp.bfloat16)
    return high, (values - high.astype(jnp.float32)).astype(jnp.bfloat16)


def dot(left, right):
    return jnp.dot(left, right, preferred_element_type=jnp.float32)


def start_copies(pairs, sems):
    copies = [pltpu.make_async_copy(source, place, sems.at[at]) for at, (source, place) in enumerate(pairs)]
    for each in copies:
        each.start()
    return copies


def line_transform(rows, load, store, table_ref, left_ref):
    low = low_half((4 * SPOTS, LANES))
    for step in range(rows // (4 * SPOTS)):
        evens, odds = [], []
        for pair in range(4):
            first, second = load(2 * pair, step), load(2 * pair + 1, step)
            crossed = pltpu.roll(jnp.where(low, second, first), HALF, 1)
            evens.append(jnp.where(low, first, crossed))
            odds.append(jnp.where(low, crossed, second))
        here = slice(step * 4 * SPOTS, (step + 1) * 4 * SPOTS)
        for at, lines in enumerate((evens, odds)):
            high, rest = split(jnp.concatenate(lines, axis=1))
            left_ref[at, here, :NY] = high
            left_ref[at, here, NY:] = rest
    block = 512
    low = low_half((block, LANES))
    for part in range(rows // block):
        here = slice(part * block, (part + 1) * block)
        for columns in range(0, NY, 2 * LANES):
            there = slice(columns, columns + 2 * LANES)
            products = []
            for at in range(2):
                left = jnp.concatenate([left_ref[at, here, :], left_ref[at, here, :NY]], axis=1)
                main = table_ref[2 * at, :, there]
                right = jnp.concatenate([main, main, table_ref[2 * at + 1, :, there]], axis=0)
                products.append(dot(left, right))
            for pair in range(2):
                even, odd = (each[:, pair * LANES : (pair + 1) * LANES] for each in products)
                g = columns // HALF + 2 * pair
                store(g, part, jnp.where(low, even, odd))
                store(g + 1, part, pltpu.roll(jnp.where(low, odd, even), HALF, 1))


def level_of(most):
    return jnp.floor(jnp.log2(jnp.maximum(most, 1e-30)) * LOG_UNIT) + 2.0


def inverse_of(level):
    return FULL * jnp.exp2(level * (-1.0 / LOG_UNIT))


def fixed_of(values):
    return jnp.floor(values + 0.5).astype(jnp.int32).astype(jnp.int16)


def head_of(level):
    return jnp.broadcast_to(level, (HEAD_ROWS, LANES)).astype(jnp.int32).astype(jnp.int16)


def unit_of(sent_ref):
    head = sent_ref[sent_ref.shape[0] - HEAD_ROWS :, :].astype(jnp.int32).astype(jnp.float32)
    return jnp.exp2(head[0:1] * (1.0 / LOG_UNIT)) * (1.0 / FULL)


def wide(sent_ref):
    block = sent_ref[: sent_ref.shape[0] - HEAD_ROWS, :]
    return block.astype(jnp.int32).astype(jnp.float32) * unit_of(sent_ref)


def pack_kernel(parts, owner_in, tile_in, count_in, brick_in, *refs):
    outs, slot_ref = refs[:parts], refs[parts]
    (owner_ref, tile_ref, count_ref, brick_ref, rows_ref, head_ref, used_ref, sems, out_sems, *ready) = refs[
        parts + 1 :
    ]
    part_rows = BRICK_ROWS // parts
    pair_rows = PAIR_SLOTS * part_rows
    copies = start_copies(
        ((brick_in, brick_ref), (owner_in, owner_ref), (tile_in, tile_ref), (count_in, count_ref)), sems
    )
    brick_rows = brick_ref.shape[0]
    head_ref[...] = jnp.full(head_ref.shape, float(TILES), jnp.float32)
    for owner in range(DOMAINS):
        used_ref[owner] = 0
    for each in ready:
        each[...] = jnp.zeros(each.shape, jnp.bfloat16)
    for each in copies:
        each.wait()
    for q in range(BRICK_ROWS):
        block = brick_ref[:, q * LANES : (q + 1) * LANES].astype(jnp.float32)
        rows_ref[pl.ds(q, brick_rows, stride=BRICK_ROWS), :] = block

    count = count_ref[0]

    def place(r, _):
        owner = owner_ref[r]
        within = used_ref[owner]
        used_ref[owner] = within + 1
        own_slot = owner * PAIR_SLOTS + within
        slot_ref[r] = own_slot
        owner = jnp.where(r < count, owner, DOMAINS)
        tile = tile_ref[r]
        line = tile // 8
        position = tile % 8 * SPOTS + line % 16 * 4 + line // 16
        for part in range(parts):
            brick = rows_ref[pl.ds(pl.multiple_of(r * BRICK_ROWS + part * part_rows, part_rows), part_rows), :]
            at = pl.multiple_of(within * part_rows, part_rows)
            ready[part][owner, pl.ds(at, part_rows), :] = brick.astype(jnp.bfloat16)
        head_ref[pl.ds(owner * PAIR_SLOTS + within, 1), :] = jnp.full((1, LANES), position, jnp.int32).astype(jnp.float32)
        return 0

    lax.fori_loop(0, brick_rows, place, 0, unroll=4)
    copies = []
    for part in range(parts):
        for owner in range(DOMAINS):
            if part == 0:
                head = head_ref[owner * PAIR_SLOTS : (owner + 1) * PAIR_SLOTS, :]
                high = jnp.floor(head * (1.0 / 32.0))
                both = jnp.where(low_half(head.shape), high, head - 32.0 * high)
                ready[part][owner, pair_rows:, :] = both.astype(jnp.bfloat16)
            if owner % 8 == 7:
                some = pl.ds(owner - 7, 8)
                copy = pltpu.make_async_copy(
                    ready[part].at[some], outs[part].at[some], out_sems.at[part * 4 + owner // 8]
                )
                copy.start()
                copies.append(copy)
    for each in copies:
        each.wait()


def write_picks(brick_ref, pair_rows, picks_ref, across_ref):
    for block in range(TILES // LANES):
        there = slice(block * LANES, (block + 1) * LANES)
        for part in range(SLOTS // LANES):
            pieces = []
            for domain in range(part * 16, part * 16 + 16):
                head = brick_ref[domain, pair_rows:, :].astype(jnp.float32)
                turned = pltpu.roll(head, HALF, 1)
                low = low_half(head.shape)
                places = (jnp.where(low, head, turned) * 32.0 + jnp.where(low, turned, head)).astype(jnp.int32)
                lane = lax.broadcasted_iota(jnp.int32, (PAIR_SLOTS, LANES), 1) + block * LANES
                pieces.append(jnp.where(places == lane, 1.0, 0.0))
            square = jnp.concatenate(pieces, axis=0)
            here = slice(part * LANES, (part + 1) * LANES)
            picks_ref[here, there] = square.astype(jnp.bfloat16)
            across_ref[there, here] = square.T.astype(jnp.bfloat16)


def forward_body(parts, own_ref, brick_ref, across_ref, table_ref, sent_refs, slots_ref, wide_ref, charge_ref, lines_ref, left_ref, most_ref):
    part_rows = BRICK_ROWS // parts
    pair_rows = PAIR_SLOTS * part_rows
    for domain in range(DOMAINS):
        slots_ref[domain * pair_rows : (domain + 1) * pair_rows, :] = brick_ref[domain, :pair_rows, :].astype(jnp.float32)
    for q in range(part_rows):
        wide_ref[:, q * LANES : (q + 1) * LANES] = slots_ref[pl.ds(q, SLOTS, stride=part_rows), :].astype(jnp.bfloat16)
    for q in range(0, part_rows, 4):
        there = slice(q * LANES, (q + 4) * LANES)
        charge_ref[:, there] = dot(across_ref[...], wide_ref[:, there])

    def load(block, step):
        return jnp.concatenate(
            [
                charge_ref[block * SPOTS : (block + 1) * SPOTS, q * LANES : (q + 1) * LANES]
                for q in range(step * 4, step * 4 + 4)
            ],
            axis=0,
        )

    def store(block, part, values):
        lines_ref[block, part * 512 : (part + 1) * 512, :] = values
        most = jnp.max(jnp.abs(values).reshape(64, 8, LANES), axis=0)
        most_ref[block] = most if part == 0 else jnp.maximum(most_ref[block], most)

    rows = part_rows * SPOTS
    line_transform(rows, load, store, table_ref, left_ref)
    for offset, sent_ref in zip(OFFSETS, sent_refs):
        block = lines_ref[own_ref[0] ^ offset]
        most = jnp.max(most_ref[own_ref[0] ^ offset], axis=0, keepdims=True)
        level = level_of(most)
        sent_ref[:rows, :] = fixed_of(block * inverse_of(level))
        sent_ref[rows:, :] = head_of(level)


def first_kernel(parts, own_ref, brick_ref, table_ref, *refs):
    sent_refs, picks_ref, across_ref = refs[:SLABS], refs[SLABS], refs[SLABS + 1]
    write_picks(brick_ref, PAIR_SLOTS * BRICK_ROWS // parts, picks_ref, across_ref)
    forward_body(parts, own_ref, brick_ref, across_ref, table_ref, sent_refs, *refs[SLABS + 2 :])


def later_kernel(parts, own_ref, brick_ref, across_ref, table_ref, *refs):
    forward_body(parts, own_ref, brick_ref, across_ref, table_ref, refs[:SLABS], *refs[SLABS:])


def roots(own_ref, base_ref, lam_ref):
    excess = base_ref[...] + lam_ref[pl.ds(own_ref[0], 1), :]
    spread = jnp.sqrt(excess * (excess + 4.0))
    root = 2.0 / (2.0 + excess + spread)
    return root, spread


def grid_rows(parts, plane, xq, tx):
    planes = BZ // parts
    row = (plane // planes) * planes * 4 * SPOTS + (plane % planes * 4 + xq) * SPOTS + tx * 4
    return pl.ds(pl.multiple_of(row * SLABS, 32), 32)


def down_kernel(parts, own_ref, *refs):
    got_refs = refs[: parts * SLABS]
    (plane_in, base_in, lam_in, walk_ref, end_ref, grid_ref, modes_ref, root_ref, last_ref, plane_ref, base_ref, lam_ref, sems) = refs[
        parts * SLABS :
    ]
    copies = start_copies(((plane_in, plane_ref), (base_in, base_ref), (lam_in, lam_ref)), sems)
    for at, got_ref in enumerate(got_refs):
        part, offset = at // SLABS, OFFSETS[at % SLABS]
        block = wide(got_ref)
        rows = block.shape[0]
        grid_ref[pl.ds(part * rows * SLABS + (own_ref[0] ^ offset), rows, stride=SLABS), :] = block
    for each in copies:
        each.wait()

    def planes(tx, xq):
        return jnp.concatenate([grid_ref[grid_rows(parts, plane, xq, tx), :] for plane in range(BZ)], axis=0)

    def sines(tx, _):
        for half in range(2):
            lines = jnp.concatenate([planes(tx, half * 2), planes(tx, half * 2 + 1)], axis=1)
            both = dot(plane_ref[...], jnp.concatenate(split(lines), axis=0))
            modes = both[:PLANES] + both[PLANES:]
            modes_ref[tx * 4 + half * 2] = modes[:, :LANES]
            modes_ref[tx * 4 + half * 2 + 1] = modes[:, LANES:]
        return 0

    lax.fori_loop(0, 16, sines, 0, unroll=8)
    root, _ = roots(own_ref, base_ref, lam_ref)
    root_ref[...] = root

    part_rows = 64
    low = low_half((part_rows, LANES))
    for part in range(PLANES // part_rows):
        here = pl.ds(part * part_rows, part_rows)
        root = root_ref[here, :]
        square = root * root

        def walk(step, held):
            ahead, behind = modes_ref[step, here, :], modes_ref[STEPS - 1 - step, here, :]
            own = jnp.where(low, behind, ahead)
            other = pltpu.roll(jnp.where(low, ahead, behind), HALF, 1)
            held = square * held + (own + root * other)
            walk_ref[step, here, :] = held
            return held

        last_ref[here, :] = lax.fori_loop(0, STEPS, walk, jnp.zeros((part_rows, LANES), jnp.float32), unroll=8)
    last = last_ref[...]
    level = level_of(jnp.max(jnp.abs(last), axis=0, keepdims=True))
    end_ref[:PLANES, :] = fixed_of(last * inverse_of(level))
    end_ref[PLANES:, :] = head_of(level)


def up_kernel(parts, own_ref, walk_ref, *refs):
    end_refs, (plane_in, base_in, lam_in) = refs[:GROUPS], refs[GROUPS : GROUPS + 3]
    sent_refs = refs[GROUPS + 3 : GROUPS + 3 + parts * SLABS]
    (full_ref, grid_ref, root_ref, gain_ref, level_ref, inverse_ref, ends_ref, plane_ref, base_ref, lam_ref, sems) = refs[
        GROUPS + 3 + parts * SLABS :
    ]
    copies = start_copies(((base_in, base_ref), (lam_in, lam_ref), (plane_in, plane_ref)), sems)
    for at, end_ref in enumerate(end_refs):
        ends_ref[at] = wide(end_ref)
    for each in copies[:2]:
        each.wait()
    root, spread = roots(own_ref, base_ref, lam_ref)
    root_ref[...] = root
    gain_ref[...] = 1.0 / spread
    part_rows = 64
    low = low_half((part_rows, LANES))
    for part in range(PLANES // part_rows):
        here = pl.ds(part * part_rows, part_rows)
        root = root_ref[here, :]
        square = root * root
        across = square
        for _ in range(6):
            across = across * across
        entering = jnp.zeros((part_rows, LANES), jnp.float32)
        for step in range(GROUPS - 1, -1, -1):
            before = ends_ref[(step + 1) % GROUPS, here, :]
            after = ends_ref[GROUPS - 1 - step, here, :]
            entering = entering * across + jnp.where(low, after, before)
        around = across
        for _ in range(2):
            around = around * around
        entering = entering / (1.0 - around)
        full_ref[0, here, :] = entering

        def carry(step, reach):
            full_ref[step + 1, here, :] = walk_ref[step, here, :] + reach
            return reach * square

        lax.fori_loop(0, STEPS, carry, entering * square, unroll=8)
    copies[2].wait()

    def solved(step):
        low = low_half((PLANES, LANES))
        near = jnp.where(low, full_ref[STEPS - step], full_ref[step + 1])
        far = jnp.where(low, full_ref[STEPS - 1 - step], full_ref[step])
        return gain_ref[...] * (near + root_ref[...] * pltpu.roll(far, HALF, 1))

    def sines(tx, _):
        for half in range(2):
            first = tx * 4 + half * 2
            modes = jnp.concatenate([solved(first), solved(first + 1)], axis=1)
            both = dot(plane_ref[...], jnp.concatenate(split(modes), axis=0))
            lines = both[:PLANES] + both[PLANES:]
            for one in range(2):
                for plane in range(BZ):
                    grid_ref[grid_rows(parts, plane, half * 2 + one, tx), :] = lines[
                        plane * 32 : (plane + 1) * 32, one * LANES : (one + 1) * LANES
                    ]
        return 0

    lax.fori_loop(0, 16, sines, 0, unroll=8)
    rows = BRICK_ROWS // parts * SPOTS
    for part in range(parts):
        here = pl.ds(part * rows * SLABS, rows * SLABS)
        most = jnp.max(jnp.abs(grid_ref[here, :]).reshape(rows, SLABS, LANES), axis=0)
        level_ref[...] = level_of(most)
        inverse_ref[...] = inverse_of(level_of(most))
        for offset, sent_ref in zip(OFFSETS, sent_refs[part * SLABS : (part + 1) * SLABS]):
            g = own_ref[0] ^ offset
            block = grid_ref[pl.ds(part * rows * SLABS + g, rows, stride=SLABS), :]
            sent_ref[:rows, :] = fixed_of(block * inverse_ref[pl.ds(g, 1), :])
            sent_ref[rows:, :] = head_of(level_ref[pl.ds(g, 1), :])


def reply_kernel(parts, own_ref, *refs):
    got_refs = refs[:SLABS]
    picks_ref, table_ref, out_ref, lines_ref, pot_ref, slots_ref, left_ref = refs[SLABS:]
    part_rows = BRICK_ROWS // parts
    for offset, got_ref in zip(OFFSETS, got_refs):
        lines_ref[own_ref[0] ^ offset] = wide(got_ref)

    def load(block, step):
        return lines_ref[block, step * 4 * SPOTS : (step + 1) * 4 * SPOTS, :]

    def store(block, part, values):
        for one in range(8):
            q = part * 8 + one
            pot_ref[block * SPOTS : (block + 1) * SPOTS, q * LANES : (q + 1) * LANES] = values[
                one * SPOTS : (one + 1) * SPOTS
            ].astype(jnp.bfloat16)

    line_transform(part_rows * SPOTS, load, store, table_ref, left_ref)
    for q in range(0, part_rows, 4):
        both = dot(picks_ref[...], pot_ref[:, q * LANES : (q + 4) * LANES])
        for one in range(4):
            slots_ref[pl.ds(q + one, SLOTS, stride=part_rows), :] = both[:, one * LANES : (one + 1) * LANES]
    pair_rows = PAIR_SLOTS * part_rows
    for domain in range(DOMAINS):
        out_ref[domain] = slots_ref[domain * pair_rows : (domain + 1) * pair_rows, :].astype(jnp.bfloat16)


def unpack_kernel(parts, slot_ref, count_ref, *refs):
    got_refs, (out_ref, rows_ref) = refs[:parts], refs[parts:]
    part_rows = BRICK_ROWS // parts
    brick_rows = out_ref.shape[0]
    count = count_ref[0]

    def place(r, _):
        slot = slot_ref[r]
        for part in range(parts):
            at = pl.multiple_of(slot % PAIR_SLOTS * part_rows, part_rows)
            brick = got_refs[part][slot // PAIR_SLOTS, pl.ds(at, part_rows), :].astype(jnp.float32)
            brick = jnp.where(r < count, brick, 0.0)
            rows_ref[pl.ds(pl.multiple_of(r * BRICK_ROWS + part * part_rows, part_rows), part_rows), :] = brick
        return 0

    lax.fori_loop(0, brick_rows, place, 0, unroll=8)
    for q in range(BRICK_ROWS):
        block = rows_ref[pl.ds(q, brick_rows, stride=BRICK_ROWS), :]
        out_ref[:, q * LANES : (q + 1) * LANES] = block.astype(jnp.bfloat16)


def call(kernel, outs, places, scratch, operands, spaces, name, vmem=VMEM_BYTES):
    return pl.pallas_call(
        kernel,
        out_shape=outs,
        in_specs=[pl.BlockSpec(memory_space=space) for space in spaces],
        out_specs=[pl.BlockSpec(memory_space=space) for space in places],
        scratch_shapes=scratch,
        compiler_params=pltpu.CompilerParams(vmem_limit_bytes=vmem),
        name=name,
    )(*operands)


def on_device_8x4(bricks, owners, tile_ids, counts):
    V, S, H = pltpu.VMEM, pltpu.SMEM, pltpu.HBM
    f32, bf16, i32, i16 = jnp.float32, jnp.bfloat16, jnp.int32, jnp.int16
    shape, bind, dma = jax.ShapeDtypeStruct, functools.partial, pltpu.SemaphoreType.DMA
    brick_rows = bricks.shape[0]
    line_table = jnp.asarray(line_tables())
    plane_down, plane_up = (jnp.asarray(each) for each in plane_tables())
    base, lam = (jnp.asarray(each) for each in mode_tables())
    own = lax.axis_index("gz").astype(i32).reshape(1)
    rows_in, rows_back = BRICK_ROWS // PARTS_IN, BRICK_ROWS // PARTS_BACK

    def all_ways(values):
        return lax.all_to_all(values, ("gz", "ma"), split_axis=0, concat_axis=0, tiled=True)

    def over_slabs(values):
        return [values[0]] + [
            lax.ppermute(each, "gz", [(g, g ^ offset) for g in range(SLABS)])
            for each, offset in zip(values[1:], OFFSETS[1:])
        ]

    def round_groups(values):
        return [values] + [
            lax.ppermute(values, "ma", [(m, (m + step) % GROUPS) for m in range(GROUPS)])
            for step in range(1, GROUPS)
        ]

    packed = [
        ((DOMAINS, PAIR_SLOTS * rows_in + (PLACE_ROWS if part == 0 else 0), LANES), bf16) for part in range(PARTS_IN)
    ]
    *outgoing, slots = call(
        bind(pack_kernel, PARTS_IN),
        [shape(*each) for each in packed] + [shape((brick_rows,), i32)],
        [H] * PARTS_IN + [S],
        [
            S((brick_rows,), i32),
            S((brick_rows,), i32),
            S((1,), i32),
            V(bricks.shape, bf16),
            V((brick_rows * BRICK_ROWS, LANES), f32),
            V((SLOTS + PAIR_SLOTS, LANES), f32),
            S((DOMAINS,), i32),
            dma((4,)),
            dma((4 * PARTS_IN,)),
        ]
        + [V((DOMAINS + 1, *each[0][1:]), bf16) for each in packed],
        (owners.reshape(brick_rows), tile_ids, counts, bricks),
        [H, H, H, H],
        "pack",
        ALL_VMEM_BYTES,
    )
    incoming = [all_ways(each) for each in outgoing]
    sent_shapes = [shape((rows_in * SPOTS + HEAD_ROWS, LANES), i16)] * SLABS
    forward_scratch = [
        V((SLOTS * rows_in, LANES), f32),
        V((SLOTS, rows_in * LANES), bf16),
        V((TILES, rows_in * LANES), f32),
        V((SLABS, rows_in * SPOTS, LANES), f32),
        V((2, rows_in * SPOTS, 2 * NY), bf16),
        V((SLABS, 8, LANES), f32),
    ]
    *sent, picks, across = call(
        bind(first_kernel, PARTS_IN),
        sent_shapes + [shape((SLOTS, TILES), bf16), shape((TILES, SLOTS), bf16)],
        [V] * (SLABS + 2),
        forward_scratch,
        (own, incoming[0], line_table),
        [S, V, V],
        "forward",
    )
    got = over_slabs(sent)
    for each in incoming[1:]:
        sent = call(
            bind(later_kernel, PARTS_IN),
            sent_shapes,
            [V] * SLABS,
            forward_scratch,
            (own, each, across, line_table),
            [S, V, V, V],
            "forward_later",
        )
        got += over_slabs(sent)
    cube = (STEPS, PLANES, LANES)
    flat = V((PLANES, LANES), f32)
    grid = V((BRICK_ROWS * SPOTS * SLABS, LANES), f32)
    tables = [V(plane_down.shape, bf16), V(base.shape, f32), V(lam.shape, f32), dma((3,))]
    walk, end = call(
        bind(down_kernel, PARTS_IN),
        [shape(cube, f32), shape((PLANES + HEAD_ROWS, LANES), i16)],
        [V, V],
        [grid, V(cube, f32), flat, flat, *tables],
        (own, *got, plane_down, base, lam),
        [S] + [V] * len(got) + [H] * 3,
        "down",
    )
    sent_shapes = [shape((rows_back * SPOTS + HEAD_ROWS, LANES), i16)] * SLABS
    sent = call(
        bind(up_kernel, PARTS_BACK),
        sent_shapes * PARTS_BACK,
        [V] * (PARTS_BACK * SLABS),
        [
            V((STEPS + 1, PLANES, LANES), f32),
            grid,
            flat,
            flat,
            V((SLABS, LANES), f32),
            V((SLABS, LANES), f32),
            V((GROUPS, PLANES, LANES), f32),
            *tables,
        ],
        (own, walk, *round_groups(end), plane_up, base, lam),
        [S] + [V] * (1 + GROUPS) + [H] * 3,
        "up",
    )
    returned = []
    for part in range(PARTS_BACK):
        (replies,) = call(
            bind(reply_kernel, PARTS_BACK),
            [shape((DOMAINS, PAIR_SLOTS * rows_back, LANES), bf16)],
            [V],
            [
                V((SLABS, rows_back * SPOTS, LANES), f32),
                V((TILES, rows_back * LANES), bf16),
                V((SLOTS * rows_back, LANES), f32),
                V((2, rows_back * SPOTS, 2 * NY), bf16),
            ],
            (own, *over_slabs(sent[part * SLABS : (part + 1) * SLABS]), picks, line_table),
            [S] + [V] * (SLABS + 2),
            "reply",
        )
        returned.append(all_ways(replies))
    (result,) = call(
        bind(unpack_kernel, PARTS_BACK),
        [shape((brick_rows, BRICK_ROWS * LANES), bf16)],
        [V],
        [V((brick_rows * BRICK_ROWS, LANES), f32)],
        (slots, counts, *returned),
        [S, S] + [V] * PARTS_BACK,
        "unpack",
    )
    return result


def solution(mesh):
    in_specs = (P(("gz", "ma"), None), P(("gz", "ma"), None), P(("gz", "ma")), P(("gz", "ma")))
    out_specs = P(("gz", "ma"), None)
    body = on_device_8x4 if (mesh.shape["gz"], mesh.shape["ma"]) == (SLABS, GROUPS) else on_device
    return jax.shard_map(body, mesh=mesh, in_specs=in_specs, out_specs=out_specs, check_vma=False)
```

```python
import math

import jax
import jax.numpy as jnp
import ml_dtypes
import numpy as np
from jax import lax
from jax.experimental import pallas as pl
from jax.experimental.pallas import tpu as pltpu
from jax.sharding import PartitionSpec as P

NX = 512
NY = 512
SCREEN = 16
BZ = 4
BX = 8
BY = 64
CZ = 16


def hartley(length):
    indices = jnp.arange(length, dtype=jnp.int32)
    products = indices[:, None] * indices[None, :] % length
    angles = 2.0 * math.pi / length * products.astype(jnp.float32)
    return (jnp.cos(angles) + jnp.sin(angles)) / math.sqrt(length)


def second_difference(length, indices):
    return 2.0 - 2.0 * jnp.cos(2.0 * math.pi / length * indices.astype(jnp.float32))


def thomas(right_side, diagonal):
    start_zero = jnp.zeros(right_side.shape[1:], jnp.float32)

    def down(state_pair, plane):
        factor = 1.0 / (diagonal - state_pair[0])
        partial_value = (plane + state_pair[1]) * factor
        return ((factor, partial_value), (factor, partial_value))

    _, (factors, partials) = lax.scan(down, (start_zero, start_zero), right_side)

    def upward(beyond, factor_partial):
        solved = factor_partial[1] + factor_partial[0] * beyond
        return (solved, solved)

    _, solutions = lax.scan(upward, start_zero, (factors, partials), reverse=True)
    return solutions


def regroup(values):
    return lax.all_to_all(values, "ma", split_axis=2, concat_axis=1, tiled=True)


def on_device(bricks, owners, tile_ids, counts):
    domains = lax.axis_size(("gz", "ma"))
    group_count = lax.axis_size("ma")
    slab_count = lax.axis_size("gz")
    brick_rows, brick_cells = bricks.shape
    slot_count = max(2, 2 * brick_rows // domains)
    local_x = NX // group_count
    local_y = NY // group_count
    tiles_dev = CZ // BZ * (local_x // BX) * (NY // BY)
    highest = lax.Precision.HIGHEST
    target = owners[:, 0]
    row_order = jnp.arange(brick_rows, dtype=jnp.int32)
    earlier_same = (target[:, None] == target[None, :]) & (row_order[None, :] < row_order[:, None])
    within = jnp.sum(earlier_same.astype(jnp.int32), axis=1)
    slot_of = target * slot_count + within
    is_live = row_order < counts[0]
    loaded = jnp.where(is_live[:, None], bricks, jnp.zeros_like(bricks))
    outgoing = jnp.zeros((domains * slot_count, brick_cells), jnp.bfloat16).at[slot_of].set(loaded)
    out_ids = jnp.full((domains * slot_count,), tiles_dev, jnp.int32).at[slot_of].set(tile_ids)
    incoming, in_ids = (
        lax.all_to_all(outgoing, ("gz", "ma"), split_axis=0, concat_axis=0, tiled=True),
        lax.all_to_all(out_ids, ("gz", "ma"), split_axis=0, concat_axis=0, tiled=True),
    )
    picker = (jnp.arange(tiles_dev, dtype=jnp.int32)[:, None] == in_ids[None, :]).astype(
        jnp.bfloat16
    )
    deposit = jnp.dot(picker, incoming, preferred_element_type=jnp.float32)
    charge = deposit.reshape(CZ // BZ, local_x // BX, NY // BY, BZ, BX, BY)
    charge = charge.transpose(0, 3, 1, 4, 2, 5).reshape(CZ, local_x, NY)
    table_x = hartley(NX)
    table_y = hartley(NY)
    along_y = jnp.einsum("zxy,ky->zxk", charge, table_y, precision=highest)
    gathered_x = regroup(along_y)
    spectrum = jnp.einsum("zxk,jx->zjk", gathered_x, table_x, precision=highest)
    columns = lax.axis_index("ma") * local_y + jnp.arange(local_y, dtype=jnp.int32)
    lam_y = second_difference(NY, columns)
    screening = 1.0 / (SCREEN * SCREEN)
    slab_index = lax.axis_index("gz")
    lam_x = second_difference(NX, jnp.arange(NX, dtype=jnp.int32))
    diagonal = 2.0 + screening + lam_x[:, None] + lam_y[None, :]
    interior = spectrum[1:]
    particular = thomas(interior, diagonal)
    unit_rhs = jnp.zeros_like(interior).at[0].set(1.0)
    spike = thomas(unit_rhs, diagonal)
    near_weight = spike[0]
    far_weight = spike[-1]
    head_term = spectrum[0] + particular[0]
    tail_term = particular[-1]
    reduced_first = diagonal - near_weight
    reduced_rest = diagonal - 2.0 * near_weight
    start_zero = jnp.zeros_like(diagonal)
    heads, tails = (
        lax.all_gather(head_term[None], "gz", axis=0, tiled=True),
        lax.all_gather(tail_term[None], "gz", axis=0, tiled=True),
    )
    before = jnp.concatenate([start_zero[None], tails[:-1]], axis=0)
    sources = heads + before

    def chain_down(state_pair, packed):
        source, position = packed
        base_term = jnp.where(position == 0, reduced_first, reduced_rest)
        pivot_now = 1.0 / (base_term - far_weight * far_weight * state_pair[0])
        forward_part = pivot_now * (source + far_weight * state_pair[1])
        return ((pivot_now, forward_part), (pivot_now, forward_part))

    _, (pivots, forwards) = lax.scan(
        chain_down, (start_zero, start_zero), (sources, jnp.arange(slab_count, dtype=jnp.int32))
    )

    def chain_up(beyond, packed):
        plane_value = packed[1] + far_weight * packed[0] * beyond
        return (plane_value, plane_value)

    _, separators = lax.scan(chain_up, start_zero, (pivots, forwards), reverse=True)
    padded_sep = jnp.concatenate([separators, start_zero[None]], axis=0)
    own_plane = lax.dynamic_index_in_dim(padded_sep, slab_index, 0, keepdims=False)
    next_plane = lax.dynamic_index_in_dim(padded_sep, slab_index + 1, 0, keepdims=False)
    interior_sol = particular + own_plane[None] * spike + next_plane[None] * spike[::-1]
    modal = jnp.concatenate([own_plane[None], interior_sol], axis=0)
    back_x = jnp.einsum("zjk,jx->zkx", modal, table_x, precision=highest)
    gathered_y = regroup(back_x)
    potential = jnp.einsum("zkx,ky->zxy", gathered_y, table_y, precision=highest)
    pot_tiles = potential.reshape(CZ // BZ, BZ, local_x // BX, BX, NY // BY, BY)
    pot_tiles = (
        pot_tiles.transpose(0, 2, 4, 1, 3, 5).reshape(tiles_dev, brick_cells).astype(jnp.bfloat16)
    )
    padded_tiles = jnp.concatenate([pot_tiles, jnp.zeros((1, brick_cells), jnp.bfloat16)], axis=0)
    replies = padded_tiles[in_ids]
    returned = lax.all_to_all(replies, ("gz", "ma"), split_axis=0, concat_axis=0, tiled=True)
    result = returned[slot_of]
    return jnp.where(is_live[:, None], result, jnp.zeros_like(result))


DOMAINS = 32
GROUPS = 4
SLABS = 8
SEND_FIRST = (4, 2, 5, 3)
SEND_LATER = (0, 1, 6, 7)
TAKE_FIRST = (0, 4, 2, 5, 3, 1)
TAKE_LATER = (6, 7)
PAIR_SLOTS = 8
SLOTS = DOMAINS * PAIR_SLOTS
TILES = 512
BRICK_ROWS = 16
PAIR_ROWS = PAIR_SLOTS * BRICK_ROWS
LANES = 128
HALF = 64
SPOTS = 64
ROWS = BRICK_ROWS * SPOTS
DOT_ROWS = 512
HEAD_ROWS = 16
PLACE_ROWS = 8
STEPS = 64
PLANES = 128
FULL = 32700.0
LOG_UNIT = 128.0
VMEM_BYTES = 24 * 1024 * 1024
ALL_VMEM_BYTES = 60 * 1024 * 1024


def split_table(table):
    high = table.astype(ml_dtypes.bfloat16)
    low = (table - high.astype(np.float64)).astype(ml_dtypes.bfloat16)
    return high, low


def line_tables():
    index = np.arange(NY)
    angle = 2.0 * np.pi / NY * (index[:, None] * index[None, :] % NY)
    table = (np.cos(angle) + np.sin(angle)) / np.sqrt(NY)
    swapped = table.reshape(NY, NY // LANES, 2, HALF)[:, :, ::-1].reshape(NY, NY)
    tables = np.stack([*split_table(table), *split_table(swapped)])
    return np.ascontiguousarray(tables.reshape(4, NY, NY // LANES, LANES).transpose(0, 2, 1, 3))


def plane_tables(offsets, turned):
    index = np.arange(PLANES)
    table = np.sqrt(2.0 / (PLANES + 1)) * np.sin(
        np.pi / (PLANES + 1) * ((index[:, None] + 1) * (index[None, :] + 1) % (2 * PLANES + 2))
    )
    each = []
    for own in range(SLABS):
        slabs = np.array([own ^ offset for offset in offsets])
        plane, tz = np.arange(BZ)[:, None, None], np.arange(BZ)[None, :, None]
        part = table[:, (slabs * CZ + tz * BZ + plane).reshape(-1)]
        high, low = split_table(part.T if turned else part)
        top = np.concatenate([high, high], axis=1)
        bottom = np.concatenate([low, np.zeros_like(low)], axis=1)
        each.append(np.concatenate([top, bottom], axis=0))
    return np.stack(each)


def mode_tables():
    mu = 2.0 - 2.0 * np.cos(np.pi / (PLANES + 1) * (np.arange(PLANES) + 1))
    base = np.broadcast_to((mu + 1.0 / (SCREEN * SCREEN))[:, None], (PLANES, LANES))
    lam = 2.0 - 2.0 * np.cos(2.0 * np.pi / NY * np.arange(NY))
    lam = lam.reshape(NY // HALF, HALF)
    return base.astype(np.float32), np.concatenate([lam, lam], axis=1).astype(np.float32)


def low_half(shape):
    return lax.broadcasted_iota(jnp.int32, shape, len(shape) - 1) < HALF


def split(values):
    high = values.astype(jnp.bfloat16)
    return high, (values - high.astype(jnp.float32)).astype(jnp.bfloat16)


def dot(left, right):
    return jnp.dot(left, right, preferred_element_type=jnp.float32)


def start_copies(pairs, sems):
    copies = [pltpu.make_async_copy(source, place, sems.at[at]) for at, (source, place) in enumerate(pairs)]
    for each in copies:
        each.start()
    return copies


def even_odd(first, second, low):
    crossed = pltpu.roll(jnp.where(low, second, first), HALF, 1)
    return jnp.where(low, first, crossed), jnp.where(low, crossed, second)


def first_second(even, odd, low):
    return jnp.where(low, even, odd), pltpu.roll(jnp.where(low, odd, even), HALF, 1)


def write_left(load, pairs, left_ref):
    low = low_half((4 * SPOTS, LANES))
    width = left_ref.shape[2] // 2
    for step in range(ROWS // (4 * SPOTS)):
        here = slice(step * 4 * SPOTS, (step + 1) * 4 * SPOTS)
        for pair in range(pairs):
            for at, lines in enumerate(even_odd(load(2 * pair, step), load(2 * pair + 1, step), low)):
                high, rest = split(lines)
                left_ref[at, here, pair * LANES : (pair + 1) * LANES] = high
                left_ref[at, here, width + pair * LANES : width + (pair + 1) * LANES] = rest


def table_part(table_ref, kind, columns, rows):
    def block(column, row):
        if row is None:
            return table_ref[kind, column]
        return table_ref[kind, column, pl.ds(pl.multiple_of(row * LANES, LANES), LANES), :]

    return jnp.concatenate(
        [jnp.concatenate([block(column, row) for column in columns], axis=1) for row in rows], axis=0
    )


def line_product(at, here, left_ref, table_ref, columns, rows):
    width = left_ref.shape[2] // 2
    left = jnp.concatenate([left_ref[at, here, :], left_ref[at, here, :width]], axis=1)
    main = table_part(table_ref, 2 * at, columns, rows)
    rest = table_part(table_ref, 2 * at + 1, columns, rows)
    return dot(left, jnp.concatenate([main, main, rest], axis=0))


def level_of(most):
    return jnp.floor(jnp.log2(jnp.maximum(most, 1e-30)) * LOG_UNIT) + 2.0


def inverse_of(level):
    return FULL * jnp.exp2(level * (-1.0 / LOG_UNIT))


def fixed_of(values):
    return jnp.floor(values + 0.5).astype(jnp.int32).astype(jnp.int16)


def head_of(level):
    return jnp.broadcast_to(level, (HEAD_ROWS, LANES)).astype(jnp.int32).astype(jnp.int16)


def unit_of(sent_ref):
    head = sent_ref[sent_ref.shape[0] - HEAD_ROWS :, :].astype(jnp.int32).astype(jnp.float32)
    return jnp.exp2(head[0:1] * (1.0 / LOG_UNIT)) * (1.0 / FULL)


def wide(sent_ref):
    block = sent_ref[: sent_ref.shape[0] - HEAD_ROWS, :]
    return block.astype(jnp.int32).astype(jnp.float32) * unit_of(sent_ref)


def pack_kernel(
    owner_in, tile_in, count_in, brick_in, out_ref, slot_ref,
    owner_ref, tile_ref, count_ref, brick_ref, rows_ref, head_ref, ready_ref, used_ref, sems, out_sems,
):
    copies = start_copies(
        ((brick_in, brick_ref), (owner_in, owner_ref), (tile_in, tile_ref), (count_in, count_ref)), sems
    )
    brick_rows = brick_ref.shape[0]
    head_ref[...] = jnp.full(head_ref.shape, float(TILES), jnp.float32)
    ready_ref[...] = jnp.zeros(ready_ref.shape, jnp.bfloat16)
    for owner in range(DOMAINS):
        used_ref[owner] = 0
    for each in copies:
        each.wait()
    for q in range(BRICK_ROWS):
        block = brick_ref[:, q * LANES : (q + 1) * LANES].astype(jnp.float32)
        rows_ref[pl.ds(q, brick_rows, stride=BRICK_ROWS), :] = block
    count = count_ref[0]

    def place(r, _):
        owner = owner_ref[r]
        within = used_ref[owner]
        used_ref[owner] = within + 1
        slot_ref[r] = owner * PAIR_SLOTS + within
        owner = jnp.where(r < count, owner, DOMAINS)
        tile = tile_ref[r]
        position = (tile & 7) * SPOTS + ((tile >> 3) & 15) * 4 + (tile >> 7)
        brick = rows_ref[pl.ds(pl.multiple_of(r * BRICK_ROWS, BRICK_ROWS), BRICK_ROWS), :]
        at = pl.multiple_of(within * BRICK_ROWS, BRICK_ROWS)
        ready_ref[owner, pl.ds(at, BRICK_ROWS), :] = brick.astype(jnp.bfloat16)
        spot = jnp.full((1, LANES), position, jnp.int32).astype(jnp.float32)
        head_ref[pl.ds(owner * PAIR_SLOTS + within, 1), :] = spot
        return 0

    lax.fori_loop(0, brick_rows, place, 0, unroll=8)
    copies = []
    for owner in range(DOMAINS):
        head = head_ref[owner * PAIR_SLOTS : (owner + 1) * PAIR_SLOTS, :]
        high = jnp.floor(head * (1.0 / 32.0))
        both = jnp.where(low_half(head.shape), high, head - 32.0 * high)
        ready_ref[owner, PAIR_ROWS:, :] = both.astype(jnp.bfloat16)
        if owner % 8 == 7:
            some = pl.ds(owner - 7, 8)
            copies.append(pltpu.make_async_copy(ready_ref.at[some], out_ref.at[some], out_sems.at[owner // 8]))
            copies[-1].start()
    for each in copies:
        each.wait()


def write_picks(brick_ref, picks_ref, across_ref):
    for block in range(TILES // LANES):
        there = slice(block * LANES, (block + 1) * LANES)
        for part in range(SLOTS // LANES):
            pieces = []
            for domain in range(part * 16, part * 16 + 16):
                head = brick_ref[domain, PAIR_ROWS:, :].astype(jnp.float32)
                turned = pltpu.roll(head, HALF, 1)
                low = low_half(head.shape)
                places = (jnp.where(low, head, turned) * 32.0 + jnp.where(low, turned, head)).astype(jnp.int32)
                lane = lax.broadcasted_iota(jnp.int32, (PAIR_SLOTS, LANES), 1) + block * LANES
                pieces.append(jnp.where(places == lane, 1.0, 0.0))
            square = jnp.concatenate(pieces, axis=0)
            here = slice(part * LANES, (part + 1) * LANES)
            picks_ref[here, there] = square.astype(jnp.bfloat16)
            across_ref[there, here] = square.T.astype(jnp.bfloat16)


def send_lines(own_ref, offsets, left_ref, table_ref, sent_refs, lines_ref, most_ref):
    own = own_ref[0]
    pairs = list(dict.fromkeys(offset // 2 for offset in offsets))
    columns = [(own >> 1) ^ pair for pair in pairs]
    low = low_half((DOT_ROWS, LANES))
    for part in range(ROWS // DOT_ROWS):
        here = slice(part * DOT_ROWS, (part + 1) * DOT_ROWS)
        even, odd = (line_product(at, here, left_ref, table_ref, columns, (None,)) for at in range(2))
        for pair in range(2):
            there = slice(pair * LANES, (pair + 1) * LANES)
            for one, values in enumerate(first_second(even[:, there], odd[:, there], low)):
                line = 2 * pair + one
                lines_ref[line, here, :] = values
                most = jnp.max(jnp.abs(values).reshape(DOT_ROWS // 8, 8, LANES), axis=0)
                most_ref[line] = most if part == 0 else jnp.maximum(most_ref[line], most)
    for offset, sent_ref in zip(offsets, sent_refs):
        line = 2 * pairs.index(offset // 2) + ((own ^ offset) & 1)
        level = level_of(jnp.max(most_ref[line], axis=0, keepdims=True))
        sent_ref[:ROWS, :] = fixed_of(lines_ref[line] * inverse_of(level))
        sent_ref[ROWS:, :] = head_of(level)


def forward_first_kernel(own_ref, brick_ref, table_ref, *refs):
    sent_refs = refs[: len(SEND_FIRST)]
    picks_ref, left_ref, across_ref, slots_ref, wide_ref, charge_ref, lines_ref, most_ref = refs[len(SEND_FIRST) :]
    write_picks(brick_ref, picks_ref, across_ref)
    for domain in range(DOMAINS):
        here = slice(domain * PAIR_ROWS, (domain + 1) * PAIR_ROWS)
        slots_ref[here, :] = brick_ref[domain, :PAIR_ROWS, :].astype(jnp.float32)
    for q in range(BRICK_ROWS):
        wide_ref[:, q * LANES : (q + 1) * LANES] = slots_ref[pl.ds(q, SLOTS, stride=BRICK_ROWS), :].astype(jnp.bfloat16)
    for q in range(0, BRICK_ROWS, 4):
        there = slice(q * LANES, (q + 4) * LANES)
        charge_ref[:, there] = dot(across_ref[...], wide_ref[:, there])

    def load(block, step):
        here = slice(block * SPOTS, (block + 1) * SPOTS)
        return jnp.concatenate(
            [charge_ref[here, q * LANES : (q + 1) * LANES] for q in range(step * 4, step * 4 + 4)], axis=0
        )

    write_left(load, 4, left_ref)
    send_lines(own_ref, SEND_FIRST, left_ref, table_ref, sent_refs, lines_ref, most_ref)


def forward_later_kernel(own_ref, left_ref, table_ref, *refs):
    count = len(SEND_LATER)
    send_lines(own_ref, SEND_LATER, left_ref, table_ref, refs[:count], *refs[count:])


def roots(own_ref, base_ref, lam_ref):
    excess = base_ref[...] + lam_ref[pl.ds(own_ref[0], 1), :]
    spread = jnp.sqrt(excess * (excess + 4.0))
    root = 2.0 / (2.0 + excess + spread)
    return root, spread


def grid_rows(slabs, plane, xq, tx):
    start = ((plane * 4 + xq) * SPOTS + tx * 4) * slabs
    return pl.ds(pl.multiple_of(start, 4 * slabs), 4 * slabs)


def add_sines(got_refs, plane_ref, grid_ref, finish):
    slabs = len(got_refs)
    for at, got_ref in enumerate(got_refs):
        grid_ref[pl.ds(at, ROWS, stride=slabs), :] = wide(got_ref)

    def planes(tx, xq):
        return jnp.concatenate([grid_ref[grid_rows(slabs, plane, xq, tx), :] for plane in range(BZ)], axis=0)

    def sines(tx, _):
        for half in range(2):
            lines = jnp.concatenate([planes(tx, half * 2), planes(tx, half * 2 + 1)], axis=1)
            both = dot(plane_ref[...], jnp.concatenate(split(lines), axis=0))
            modes = both[:PLANES] + both[PLANES:]
            finish(tx * 4 + half * 2, modes[:, :LANES])
            finish(tx * 4 + half * 2 + 1, modes[:, LANES:])
        return 0

    lax.fori_loop(0, 16, sines, 0, unroll=8)


def down_first_kernel(own_ref, *refs):
    count = len(TAKE_FIRST)
    plane_in, modes_ref, grid_ref, plane_ref, sems = refs[count:]
    [copy] = start_copies(((plane_in.at[own_ref[0]], plane_ref),), sems)
    copy.wait()

    def finish(line, values):
        modes_ref[line] = values

    add_sines(refs[:count], plane_ref, grid_ref, finish)


def down_later_kernel(own_ref, *refs):
    count = len(TAKE_LATER)
    (
        sums_ref, plane_in, base_in, lam_in, walk_ref, end_ref,
        grid_ref, modes_ref, root_ref, last_ref, plane_ref, base_ref, lam_ref, sems,
    ) = refs[count:]
    copies = start_copies(((plane_in.at[own_ref[0]], plane_ref), (base_in, base_ref), (lam_in, lam_ref)), sems)
    for each in copies:
        each.wait()

    def finish(line, values):
        modes_ref[line] = sums_ref[line] + values

    add_sines(refs[:count], plane_ref, grid_ref, finish)
    root_ref[...] = roots(own_ref, base_ref, lam_ref)[0]
    part_rows = 64
    low = low_half((part_rows, LANES))
    for part in range(PLANES // part_rows):
        here = pl.ds(part * part_rows, part_rows)
        root = root_ref[here, :]
        square = root * root

        def walk(step, held):
            ahead, behind = modes_ref[step, here, :], modes_ref[STEPS - 1 - step, here, :]
            own = jnp.where(low, behind, ahead)
            other = pltpu.roll(jnp.where(low, ahead, behind), HALF, 1)
            held = square * held + (own + root * other)
            walk_ref[step, here, :] = held
            return held

        last_ref[here, :] = lax.fori_loop(0, STEPS, walk, jnp.zeros((part_rows, LANES), jnp.float32), unroll=8)
    last = last_ref[...]
    level = level_of(jnp.max(jnp.abs(last), axis=0, keepdims=True))
    end_ref[:PLANES, :] = fixed_of(last * inverse_of(level))
    end_ref[PLANES:, :] = head_of(level)


def send_planes(full_ref, sent_refs, plane_ref, root_ref, gain_ref, grid_ref, level_ref):
    slabs = len(sent_refs)
    rows = 4 * BZ * slabs

    def solved(step):
        low = low_half((PLANES, LANES))
        near = jnp.where(low, full_ref[STEPS - step], full_ref[step + 1])
        far = jnp.where(low, full_ref[STEPS - 1 - step], full_ref[step])
        return gain_ref[...] * (near + root_ref[...] * pltpu.roll(far, HALF, 1))

    def sines(tx, most):
        for half in range(2):
            first = tx * 4 + half * 2
            modes = jnp.concatenate([solved(first), solved(first + 1)], axis=1)
            both = dot(plane_ref[...], jnp.concatenate(split(modes), axis=0))
            lines = both[:rows] + both[rows:]
            for one in range(2):
                part = lines[:, one * LANES : (one + 1) * LANES]
                most = jnp.maximum(most, jnp.max(jnp.abs(part).reshape(rows // 8, 8, LANES), axis=0))
                for plane in range(BZ):
                    grid_ref[grid_rows(slabs, plane, half * 2 + one, tx), :] = part[
                        plane * 4 * slabs : (plane + 1) * 4 * slabs
                    ]
        return most

    most = lax.fori_loop(0, 16, sines, jnp.zeros((8, LANES), jnp.float32), unroll=8)
    level_ref[...] = level_of(jnp.maximum(most, pltpu.roll(most, slabs, 0)))
    for at, sent_ref in enumerate(sent_refs):
        level = level_ref[at : at + 1, :]
        sent_ref[:ROWS, :] = fixed_of(grid_ref[pl.ds(at, ROWS, stride=slabs), :] * inverse_of(level))
        sent_ref[ROWS:, :] = head_of(level)


def up_first_kernel(own_ref, walk_ref, *refs):
    end_refs, (plane_in, base_in, lam_in) = refs[:GROUPS], refs[GROUPS : GROUPS + 3]
    count = GROUPS + 3 + len(SEND_FIRST)
    sent_refs = refs[GROUPS + 3 : count]
    full_ref, root_ref, gain_ref, grid_ref, level_ref, ends_ref, plane_ref, base_ref, lam_ref, sems = refs[count:]
    copies = start_copies(((base_in, base_ref), (lam_in, lam_ref), (plane_in.at[own_ref[0]], plane_ref)), sems)
    for at, end_ref in enumerate(end_refs):
        ends_ref[at] = wide(end_ref)
    for each in copies:
        each.wait()
    root, spread = roots(own_ref, base_ref, lam_ref)
    root_ref[...] = root
    gain_ref[...] = 1.0 / spread
    part_rows = 64
    low = low_half((part_rows, LANES))
    for part in range(PLANES // part_rows):
        here = pl.ds(part * part_rows, part_rows)
        root = root_ref[here, :]
        square = root * root
        across = square
        for _ in range(6):
            across = across * across
        entering = jnp.zeros((part_rows, LANES), jnp.float32)
        for step in range(GROUPS - 1, -1, -1):
            before = ends_ref[(step + 1) % GROUPS, here, :]
            after = ends_ref[GROUPS - 1 - step, here, :]
            entering = entering * across + jnp.where(low, after, before)
        around = across
        for _ in range(2):
            around = around * around
        entering = entering / (1.0 - around)
        full_ref[0, here, :] = entering

        def carry(step, reach):
            full_ref[step + 1, here, :] = walk_ref[step, here, :] + reach
            return reach * square

        lax.fori_loop(0, STEPS, carry, entering * square, unroll=8)
    send_planes(full_ref, sent_refs, plane_ref, root_ref, gain_ref, grid_ref, level_ref)


def up_later_kernel(own_ref, full_ref, root_ref, gain_ref, plane_in, *refs):
    count = len(SEND_LATER)
    grid_ref, level_ref, plane_ref, sems = refs[count:]
    [copy] = start_copies(((plane_in.at[own_ref[0]], plane_ref),), sems)
    copy.wait()
    send_planes(full_ref, refs[:count], plane_ref, root_ref, gain_ref, grid_ref, level_ref)


def take_lines(own_ref, offsets, got_refs, left_ref, lines_ref):
    own = own_ref[0]
    pairs = list(dict.fromkeys(offset // 2 for offset in offsets))
    for offset, got_ref in zip(offsets, got_refs):
        lines_ref[2 * pairs.index(offset // 2) + ((own ^ offset) & 1)] = wide(got_ref)

    def load(block, step):
        return lines_ref[block, step * 4 * SPOTS : (step + 1) * 4 * SPOTS, :]

    write_left(load, len(pairs), left_ref)
    return [(own >> 1) ^ pair for pair in pairs]


def reply_first_kernel(own_ref, *refs):
    count = len(TAKE_FIRST)
    table_ref, sums_ref, lines_ref, left_ref = refs[count:]
    rows = take_lines(own_ref, TAKE_FIRST, refs[:count], left_ref, lines_ref)
    for part in range(ROWS // DOT_ROWS):
        here = slice(part * DOT_ROWS, (part + 1) * DOT_ROWS)
        for column in (0, 2):
            for at in range(2):
                sums_ref[at, here, column * LANES : (column + 2) * LANES] = line_product(
                    at, here, left_ref, table_ref, (column, column + 1), rows
                )


def reply_later_kernel(own_ref, *refs):
    count = len(TAKE_LATER)
    sums_ref, picks_ref, table_ref, out_ref, lines_ref, left_ref, pot_ref, slots_ref = refs[count:]
    rows = take_lines(own_ref, TAKE_LATER, refs[:count], left_ref, lines_ref)
    low = low_half((DOT_ROWS, LANES))
    for part in range(ROWS // DOT_ROWS):
        here = slice(part * DOT_ROWS, (part + 1) * DOT_ROWS)
        for column in (0, 2):
            even, odd = (
                line_product(at, here, left_ref, table_ref, (column, column + 1), rows)
                + sums_ref[at, here, column * LANES : (column + 2) * LANES]
                for at in range(2)
            )
            for pair in range(2):
                there = slice(pair * LANES, (pair + 1) * LANES)
                for one, values in enumerate(first_second(even[:, there], odd[:, there], low)):
                    ty = 2 * (column + pair) + one
                    for q in range(DOT_ROWS // SPOTS):
                        at = part * (DOT_ROWS // SPOTS) + q
                        pot_ref[ty * SPOTS : (ty + 1) * SPOTS, at * LANES : (at + 1) * LANES] = values[
                            q * SPOTS : (q + 1) * SPOTS
                        ].astype(jnp.bfloat16)
    for q in range(0, BRICK_ROWS, 4):
        both = dot(picks_ref[...], pot_ref[:, q * LANES : (q + 4) * LANES])
        for one in range(4):
            slots_ref[pl.ds(q + one, SLOTS, stride=BRICK_ROWS), :] = both[:, one * LANES : (one + 1) * LANES]
    out_ref[...] = slots_ref[...].astype(jnp.bfloat16)


def unpack_kernel(slot_ref, count_ref, got_ref, out_ref, slots_ref, rows_ref):
    brick_rows = out_ref.shape[0]
    slots_ref[...] = got_ref[...].astype(jnp.float32)
    count = count_ref[0]

    def place(r, _):
        at = pl.multiple_of(slot_ref[r] * BRICK_ROWS, BRICK_ROWS)
        brick = jnp.where(r < count, slots_ref[pl.ds(at, BRICK_ROWS), :], 0.0)
        rows_ref[pl.ds(pl.multiple_of(r * BRICK_ROWS, BRICK_ROWS), BRICK_ROWS), :] = brick
        return 0

    lax.fori_loop(0, brick_rows, place, 0, unroll=8)
    for q in range(BRICK_ROWS):
        block = rows_ref[pl.ds(q, brick_rows, stride=BRICK_ROWS), :]
        out_ref[:, q * LANES : (q + 1) * LANES] = block.astype(jnp.bfloat16)


def call(kernel, name, operands, spaces, outs, places, scratch, vmem=VMEM_BYTES):
    return pl.pallas_call(
        kernel,
        out_shape=outs,
        in_specs=[pl.BlockSpec(memory_space=space) for space in spaces],
        out_specs=[pl.BlockSpec(memory_space=space) for space in places],
        scratch_shapes=scratch,
        compiler_params=pltpu.CompilerParams(vmem_limit_bytes=vmem),
        name=name,
    )(*operands)


def on_device_8x4(bricks, owners, tile_ids, counts):
    V, S, H = pltpu.VMEM, pltpu.SMEM, pltpu.HBM
    f32, bf16, i32, i16 = jnp.float32, jnp.bfloat16, jnp.int32, jnp.int16
    shape, dma = jax.ShapeDtypeStruct, pltpu.SemaphoreType.DMA
    brick_rows = bricks.shape[0]
    line_table = jnp.asarray(line_tables())
    planes_in = [jnp.asarray(plane_tables(offsets, False)) for offsets in (TAKE_FIRST, TAKE_LATER)]
    planes_out = [jnp.asarray(plane_tables(offsets, True)) for offsets in (SEND_FIRST, SEND_LATER)]
    base, lam = (jnp.asarray(each) for each in mode_tables())
    own = lax.axis_index("gz").astype(i32).reshape(1)
    sent_shape = shape((ROWS + HEAD_ROWS, LANES), i16)
    end_shape = shape((PLANES + HEAD_ROWS, LANES), i16)
    cube, flat, sums_shape = (STEPS, PLANES, LANES), (PLANES, LANES), (2, ROWS, NY)
    line, place_shape = (ROWS, LANES), (DOMAINS, PAIR_ROWS + PLACE_ROWS, LANES)

    def all_ways(values):
        return lax.all_to_all(values, ("gz", "ma"), split_axis=0, concat_axis=0, tiled=True)

    def over_slabs(offset, values):
        return lax.ppermute(values, "gz", [(g, g ^ offset) for g in range(SLABS)]) if offset else values

    def round_groups(values, step):
        return lax.ppermute(values, "ma", [(m, (m + step) % GROUPS) for m in range(GROUPS)]) if step else values

    def exchanged(first, later):
        sent = dict(zip(SEND_FIRST + SEND_LATER, [*first, *later]))
        got = {offset: over_slabs(offset, sent[offset]) for offset in TAKE_FIRST + TAKE_LATER}
        return [got[offset] for offset in TAKE_FIRST], [got[offset] for offset in TAKE_LATER]

    outgoing, slots = call(
        pack_kernel,
        "pack",
        (owners.reshape(brick_rows), tile_ids, counts, bricks),
        [H] * 4,
        [shape(place_shape, bf16), shape((brick_rows,), i32)],
        [H, S],
        [
            S((brick_rows,), i32),
            S((brick_rows,), i32),
            S((1,), i32),
            V(bricks.shape, bf16),
            V((brick_rows * BRICK_ROWS, LANES), f32),
            V((SLOTS + PAIR_SLOTS, LANES), f32),
            V((DOMAINS + 1, *place_shape[1:]), bf16),
            S((DOMAINS,), i32),
            dma((4,)),
            dma((4,)),
        ],
        ALL_VMEM_BYTES,
    )
    *first, picks, left = call(
        forward_first_kernel,
        "forward_first",
        (own, all_ways(outgoing), line_table),
        [S, V, V],
        [sent_shape] * len(SEND_FIRST) + [shape((SLOTS, TILES), bf16), shape((2, ROWS, 2 * NY), bf16)],
        [V] * (len(SEND_FIRST) + 2),
        [
            V((TILES, SLOTS), bf16),
            V((SLOTS * BRICK_ROWS, LANES), f32),
            V((SLOTS, BRICK_ROWS * LANES), bf16),
            V((TILES, BRICK_ROWS * LANES), f32),
            V((4, *line), f32),
            V((4, 8, LANES), f32),
        ],
    )
    later = call(
        forward_later_kernel,
        "forward_later",
        (own, left, line_table),
        [S, V, V],
        [sent_shape] * len(SEND_LATER),
        [V] * len(SEND_LATER),
        [V((4, *line), f32), V((4, 8, LANES), f32)],
    )
    first, later = exchanged(first, later)
    (sums,) = call(
        down_first_kernel,
        "down_first",
        (own, *first, planes_in[0]),
        [S] + [V] * len(first) + [H],
        [shape(cube, f32)],
        [V],
        [V((len(first) * ROWS, LANES), f32), V(planes_in[0].shape[1:], bf16), dma((1,))],
    )
    tables = [V(base.shape, f32), V(lam.shape, f32), dma((3,))]
    walk, end = call(
        down_later_kernel,
        "down_later",
        (own, *later, sums, planes_in[1], base, lam),
        [S] + [V] * (len(later) + 1) + [H] * 3,
        [shape(cube, f32), end_shape],
        [V, V],
        [
            V((len(later) * ROWS, LANES), f32),
            V(cube, f32),
            V(flat, f32),
            V(flat, f32),
            V(planes_in[1].shape[1:], bf16),
            *tables,
        ],
    )
    ends = [round_groups(end, step) for step in range(GROUPS)]
    *first, full, root, gain = call(
        up_first_kernel,
        "up_first",
        (own, walk, *ends, planes_out[0], base, lam),
        [S] + [V] * (1 + GROUPS) + [H] * 3,
        [sent_shape] * len(SEND_FIRST) + [shape((STEPS + 1, *flat), f32), shape(flat, f32), shape(flat, f32)],
        [V] * (len(SEND_FIRST) + 3),
        [
            V((len(SEND_FIRST) * ROWS, LANES), f32),
            V((8, LANES), f32),
            V((GROUPS, *flat), f32),
            V(planes_out[0].shape[1:], bf16),
            *tables,
        ],
    )
    later = call(
        up_later_kernel,
        "up_later",
        (own, full, root, gain, planes_out[1]),
        [S] + [V] * 3 + [H],
        [sent_shape] * len(SEND_LATER),
        [V] * len(SEND_LATER),
        [V((len(SEND_LATER) * ROWS, LANES), f32), V((8, LANES), f32), V(planes_out[1].shape[1:], bf16), dma((1,))],
    )
    first, later = exchanged(first, later)
    (sums,) = call(
        reply_first_kernel,
        "reply_first",
        (own, *first, line_table),
        [S] + [V] * (len(first) + 1),
        [shape(sums_shape, f32)],
        [V],
        [V((len(first), *line), f32), V((2, ROWS, len(first) * LANES), bf16)],
    )
    (replies,) = call(
        reply_later_kernel,
        "reply_later",
        (own, *later, sums, picks, line_table),
        [S] + [V] * (len(later) + 3),
        [shape((SLOTS * BRICK_ROWS, LANES), bf16)],
        [V],
        [
            V((len(later), *line), f32),
            V((2, ROWS, len(later) * LANES), bf16),
            V((TILES, BRICK_ROWS * LANES), bf16),
            V((SLOTS * BRICK_ROWS, LANES), f32),
        ],
    )
    returned = all_ways(replies.reshape(DOMAINS, PAIR_ROWS, LANES)).reshape(SLOTS * BRICK_ROWS, LANES)
    (result,) = call(
        unpack_kernel,
        "unpack",
        (slots, counts, returned),
        [S, S, V],
        [shape((brick_rows, BRICK_ROWS * LANES), bf16)],
        [V],
        [V((SLOTS * BRICK_ROWS, LANES), f32), V((brick_rows * BRICK_ROWS, LANES), f32)],
    )
    return result


def solution(mesh):
    in_specs = (P(("gz", "ma"), None), P(("gz", "ma"), None), P(("gz", "ma")), P(("gz", "ma")))
    out_specs = P(("gz", "ma"), None)
    body = on_device_8x4 if (mesh.shape["gz"], mesh.shape["ma"]) == (SLABS, GROUPS) else on_device
    return jax.shard_map(body, mesh=mesh, in_specs=in_specs, out_specs=out_specs, check_vma=False)
```

```python
import math

import jax
import jax.numpy as jnp
import ml_dtypes
import numpy as np
from jax import lax
from jax.experimental import pallas as pl
from jax.experimental.pallas import tpu as pltpu
from jax.sharding import PartitionSpec as P

NX = 512
NY = 512
SCREEN = 16
BZ = 4
BX = 8
BY = 64
CZ = 16


def hartley(length):
    indices = jnp.arange(length, dtype=jnp.int32)
    products = indices[:, None] * indices[None, :] % length
    angles = 2.0 * math.pi / length * products.astype(jnp.float32)
    return (jnp.cos(angles) + jnp.sin(angles)) / math.sqrt(length)


def second_difference(length, indices):
    return 2.0 - 2.0 * jnp.cos(2.0 * math.pi / length * indices.astype(jnp.float32))


def thomas(right_side, diagonal):
    start_zero = jnp.zeros(right_side.shape[1:], jnp.float32)

    def down(state_pair, plane):
        factor = 1.0 / (diagonal - state_pair[0])
        partial_value = (plane + state_pair[1]) * factor
        return ((factor, partial_value), (factor, partial_value))

    _, (factors, partials) = lax.scan(down, (start_zero, start_zero), right_side)

    def upward(beyond, factor_partial):
        solved = factor_partial[1] + factor_partial[0] * beyond
        return (solved, solved)

    _, solutions = lax.scan(upward, start_zero, (factors, partials), reverse=True)
    return solutions


def regroup(values):
    return lax.all_to_all(values, "ma", split_axis=2, concat_axis=1, tiled=True)


def on_device(bricks, owners, tile_ids, counts):
    domains = lax.axis_size(("gz", "ma"))
    group_count = lax.axis_size("ma")
    slab_count = lax.axis_size("gz")
    brick_rows, brick_cells = bricks.shape
    slot_count = max(2, 2 * brick_rows // domains)
    local_x = NX // group_count
    local_y = NY // group_count
    tiles_dev = CZ // BZ * (local_x // BX) * (NY // BY)
    highest = lax.Precision.HIGHEST
    target = owners[:, 0]
    row_order = jnp.arange(brick_rows, dtype=jnp.int32)
    earlier_same = (target[:, None] == target[None, :]) & (row_order[None, :] < row_order[:, None])
    within = jnp.sum(earlier_same.astype(jnp.int32), axis=1)
    slot_of = target * slot_count + within
    is_live = row_order < counts[0]
    loaded = jnp.where(is_live[:, None], bricks, jnp.zeros_like(bricks))
    outgoing = jnp.zeros((domains * slot_count, brick_cells), jnp.bfloat16).at[slot_of].set(loaded)
    out_ids = jnp.full((domains * slot_count,), tiles_dev, jnp.int32).at[slot_of].set(tile_ids)
    incoming, in_ids = (
        lax.all_to_all(outgoing, ("gz", "ma"), split_axis=0, concat_axis=0, tiled=True),
        lax.all_to_all(out_ids, ("gz", "ma"), split_axis=0, concat_axis=0, tiled=True),
    )
    picker = (jnp.arange(tiles_dev, dtype=jnp.int32)[:, None] == in_ids[None, :]).astype(
        jnp.bfloat16
    )
    deposit = jnp.dot(picker, incoming, preferred_element_type=jnp.float32)
    charge = deposit.reshape(CZ // BZ, local_x // BX, NY // BY, BZ, BX, BY)
    charge = charge.transpose(0, 3, 1, 4, 2, 5).reshape(CZ, local_x, NY)
    table_x = hartley(NX)
    table_y = hartley(NY)
    along_y = jnp.einsum("zxy,ky->zxk", charge, table_y, precision=highest)
    gathered_x = regroup(along_y)
    spectrum = jnp.einsum("zxk,jx->zjk", gathered_x, table_x, precision=highest)
    columns = lax.axis_index("ma") * local_y + jnp.arange(local_y, dtype=jnp.int32)
    lam_y = second_difference(NY, columns)
    screening = 1.0 / (SCREEN * SCREEN)
    slab_index = lax.axis_index("gz")
    lam_x = second_difference(NX, jnp.arange(NX, dtype=jnp.int32))
    diagonal = 2.0 + screening + lam_x[:, None] + lam_y[None, :]
    interior = spectrum[1:]
    particular = thomas(interior, diagonal)
    unit_rhs = jnp.zeros_like(interior).at[0].set(1.0)
    spike = thomas(unit_rhs, diagonal)
    near_weight = spike[0]
    far_weight = spike[-1]
    head_term = spectrum[0] + particular[0]
    tail_term = particular[-1]
    reduced_first = diagonal - near_weight
    reduced_rest = diagonal - 2.0 * near_weight
    start_zero = jnp.zeros_like(diagonal)
    heads, tails = (
        lax.all_gather(head_term[None], "gz", axis=0, tiled=True),
        lax.all_gather(tail_term[None], "gz", axis=0, tiled=True),
    )
    before = jnp.concatenate([start_zero[None], tails[:-1]], axis=0)
    sources = heads + before

    def chain_down(state_pair, packed):
        source, position = packed
        base_term = jnp.where(position == 0, reduced_first, reduced_rest)
        pivot_now = 1.0 / (base_term - far_weight * far_weight * state_pair[0])
        forward_part = pivot_now * (source + far_weight * state_pair[1])
        return ((pivot_now, forward_part), (pivot_now, forward_part))

    _, (pivots, forwards) = lax.scan(
        chain_down, (start_zero, start_zero), (sources, jnp.arange(slab_count, dtype=jnp.int32))
    )

    def chain_up(beyond, packed):
        plane_value = packed[1] + far_weight * packed[0] * beyond
        return (plane_value, plane_value)

    _, separators = lax.scan(chain_up, start_zero, (pivots, forwards), reverse=True)
    padded_sep = jnp.concatenate([separators, start_zero[None]], axis=0)
    own_plane = lax.dynamic_index_in_dim(padded_sep, slab_index, 0, keepdims=False)
    next_plane = lax.dynamic_index_in_dim(padded_sep, slab_index + 1, 0, keepdims=False)
    interior_sol = particular + own_plane[None] * spike + next_plane[None] * spike[::-1]
    modal = jnp.concatenate([own_plane[None], interior_sol], axis=0)
    back_x = jnp.einsum("zjk,jx->zkx", modal, table_x, precision=highest)
    gathered_y = regroup(back_x)
    potential = jnp.einsum("zkx,ky->zxy", gathered_y, table_y, precision=highest)
    pot_tiles = potential.reshape(CZ // BZ, BZ, local_x // BX, BX, NY // BY, BY)
    pot_tiles = (
        pot_tiles.transpose(0, 2, 4, 1, 3, 5).reshape(tiles_dev, brick_cells).astype(jnp.bfloat16)
    )
    padded_tiles = jnp.concatenate([pot_tiles, jnp.zeros((1, brick_cells), jnp.bfloat16)], axis=0)
    replies = padded_tiles[in_ids]
    returned = lax.all_to_all(replies, ("gz", "ma"), split_axis=0, concat_axis=0, tiled=True)
    result = returned[slot_of]
    return jnp.where(is_live[:, None], result, jnp.zeros_like(result))


DOMAINS = 32
GROUPS = 4
SLABS = 8
SEND = (4, 2, 5, 3, 0, 1, 6, 7)
TAKE_FIRST = (0, 4, 2, 5, 3, 1)
TAKE_LATER = (6, 7)
PAIR_SLOTS = 8
SLOTS = DOMAINS * PAIR_SLOTS
TILES = 512
BRICK_ROWS = 16
CELLS = 2048
LANES = 128
HALF = 64
SPOTS = 64
ROWS = BRICK_ROWS * SPOTS
DOT_ROWS = 512
HEAD_ROWS = 16
STEPS = 64
PLANES = 128
FULL = 32700.0
LOG_UNIT = 128.0
VMEM_BYTES = 24 * 1024 * 1024
ALL_VMEM_BYTES = 60 * 1024 * 1024


def split_table(table):
    high = table.astype(ml_dtypes.bfloat16)
    low = (table - high.astype(np.float64)).astype(ml_dtypes.bfloat16)
    return high, low


def line_tables():
    index = np.arange(NY)
    angle = 2.0 * np.pi / NY * (index[:, None] * index[None, :] % NY)
    table = (np.cos(angle) + np.sin(angle)) / np.sqrt(NY)
    swapped = table.reshape(NY, NY // LANES, 2, HALF)[:, :, ::-1].reshape(NY, NY)
    tables = np.stack([*split_table(table), *split_table(swapped)])
    return np.ascontiguousarray(tables.reshape(4, NY, NY // LANES, LANES).transpose(0, 2, 1, 3))


def plane_tables(offsets, turned):
    index = np.arange(PLANES)
    table = np.sqrt(2.0 / (PLANES + 1)) * np.sin(
        np.pi / (PLANES + 1) * ((index[:, None] + 1) * (index[None, :] + 1) % (2 * PLANES + 2))
    )
    each = []
    for own in range(SLABS):
        slabs = np.array([own ^ offset for offset in offsets])
        plane, tz = np.arange(BZ)[:, None, None], np.arange(BZ)[None, :, None]
        part = table[:, (slabs * CZ + tz * BZ + plane).reshape(-1)]
        high, low = split_table(part.T if turned else part)
        top = np.concatenate([high, high], axis=1)
        bottom = np.concatenate([low, np.zeros_like(low)], axis=1)
        each.append(np.concatenate([top, bottom], axis=0))
    return np.stack(each)


def mode_tables():
    mu = 2.0 - 2.0 * np.cos(np.pi / (PLANES + 1) * (np.arange(PLANES) + 1))
    base = np.broadcast_to((mu + 1.0 / (SCREEN * SCREEN))[:, None], (PLANES, LANES))
    lam = 2.0 - 2.0 * np.cos(2.0 * np.pi / NY * np.arange(NY))
    lam = lam.reshape(NY // HALF, HALF)
    return base.astype(np.float32), np.concatenate([lam, lam], axis=1).astype(np.float32)


def low_half(shape):
    return lax.broadcasted_iota(jnp.int32, shape, len(shape) - 1) < HALF


def split(values):
    high = values.astype(jnp.bfloat16)
    return high, (values - high.astype(jnp.float32)).astype(jnp.bfloat16)


def dot(left, right):
    return jnp.dot(left, right, preferred_element_type=jnp.float32)


def start_copies(pairs, sems):
    copies = [pltpu.make_async_copy(source, place, sems.at[at]) for at, (source, place) in enumerate(pairs)]
    for each in copies:
        each.start()
    return copies


def even_odd(first, second, low):
    crossed = pltpu.roll(jnp.where(low, second, first), HALF, 1)
    return jnp.where(low, first, crossed), jnp.where(low, crossed, second)


def first_second(even, odd, low):
    return jnp.where(low, even, odd), pltpu.roll(jnp.where(low, odd, even), HALF, 1)


def write_left(load, pairs, left_ref):
    low = low_half((4 * SPOTS, LANES))
    width = left_ref.shape[2] // 2
    for step in range(ROWS // (4 * SPOTS)):
        here = slice(step * 4 * SPOTS, (step + 1) * 4 * SPOTS)
        for pair in range(pairs):
            for at, lines in enumerate(even_odd(load(2 * pair, step), load(2 * pair + 1, step), low)):
                high, rest = split(lines)
                left_ref[at, here, pair * LANES : (pair + 1) * LANES] = high
                left_ref[at, here, width + pair * LANES : width + (pair + 1) * LANES] = rest


def table_part(table_ref, kind, columns, rows):
    def block(column, row):
        if row is None:
            return table_ref[kind, column]
        return table_ref[kind, column, pl.ds(pl.multiple_of(row * LANES, LANES), LANES), :]

    return jnp.concatenate(
        [jnp.concatenate([block(column, row) for column in columns], axis=1) for row in rows], axis=0
    )


def line_product(at, here, left_ref, table_ref, columns, rows):
    width = left_ref.shape[2] // 2
    left = jnp.concatenate([left_ref[at, here, :], left_ref[at, here, :width]], axis=1)
    main = table_part(table_ref, 2 * at, columns, rows)
    rest = table_part(table_ref, 2 * at + 1, columns, rows)
    return dot(left, jnp.concatenate([main, main, rest], axis=0))


def level_of(most):
    return jnp.floor(jnp.log2(jnp.maximum(most, 1e-30)) * LOG_UNIT) + 2.0


def inverse_of(level):
    return FULL * jnp.exp2(level * (-1.0 / LOG_UNIT))


def fixed_of(values):
    return jnp.floor(values + 0.5).astype(jnp.int32).astype(jnp.int16)


def head_of(level):
    return jnp.broadcast_to(level, (HEAD_ROWS, LANES)).astype(jnp.int32).astype(jnp.int16)


def unit_of(sent_ref):
    head = sent_ref[sent_ref.shape[0] - HEAD_ROWS :, :].astype(jnp.int32).astype(jnp.float32)
    return jnp.exp2(head[0:1] * (1.0 / LOG_UNIT)) * (1.0 / FULL)


def wide(sent_ref):
    block = sent_ref[: sent_ref.shape[0] - HEAD_ROWS, :]
    return block.astype(jnp.int32).astype(jnp.float32) * unit_of(sent_ref)


def pack_kernel(
    owner_in, tile_in, count_in, brick_in, out_ref, back_ref,
    owner_ref, tile_ref, count_ref, brick_ref, pick_ref, head_ref, ready_ref, used_ref, sems, out_sems,
):
    copies = start_copies(
        ((owner_in, owner_ref), (tile_in, tile_ref), (count_in, count_ref), (brick_in, brick_ref)), sems
    )
    brick_rows = brick_ref.shape[0]
    head_ref[...] = jnp.full(head_ref.shape, float(TILES), jnp.float32)
    pick_ref[...] = jnp.zeros(pick_ref.shape, jnp.float32)
    for owner in range(DOMAINS):
        used_ref[owner] = 0
    for each in copies[:3]:
        each.wait()
    count = count_ref[0]
    lane = lax.broadcasted_iota(jnp.int32, (1, brick_rows), 1)

    def place(r, _):
        owner = owner_ref[r]
        within = used_ref[owner]
        used_ref[owner] = within + 1
        slot = jnp.where(r < count, owner * PAIR_SLOTS + within, SLOTS)
        tile = tile_ref[r]
        position = (tile & 7) * SPOTS + ((tile >> 3) & 15) * 4 + (tile >> 7)
        pick_ref[pl.ds(slot, 1), :] = jnp.where(lane == r, 1.0, 0.0)
        head_ref[pl.ds(slot, 1), :] = jnp.full((1, LANES), position, jnp.int32).astype(jnp.float32)
        return 0

    lax.fori_loop(0, brick_rows, place, 0, unroll=8)
    copies[3].wait()
    copies = []
    rows = 64
    for part in range(SLOTS // rows):
        here = slice(part * rows, (part + 1) * rows)
        ready_ref[here, :CELLS] = dot(pick_ref[here, :].astype(jnp.bfloat16), brick_ref[...]).astype(jnp.bfloat16)
        head = head_ref[here, :]
        high = jnp.floor(head * (1.0 / 32.0))
        ready_ref[here, CELLS:] = jnp.where(low_half(head.shape), high, head - 32.0 * high).astype(jnp.bfloat16)
        some = pl.ds(part * rows, rows)
        copies.append(pltpu.make_async_copy(ready_ref.at[some], out_ref.at[some], out_sems.at[part]))
        copies[-1].start()
    for part in range(SLOTS // LANES):
        here = slice(part * LANES, (part + 1) * LANES)
        back_ref[:, here] = pick_ref[here, :].T.astype(jnp.bfloat16)
    for each in copies:
        each.wait()


def write_picks(brick_ref, picks_ref, across_ref):
    for part in range(SLOTS // LANES):
        here = slice(part * LANES, (part + 1) * LANES)
        head = brick_ref[here, CELLS:].astype(jnp.float32)
        turned = pltpu.roll(head, HALF, 1)
        low = low_half(head.shape)
        places = (jnp.where(low, head, turned) * 32.0 + jnp.where(low, turned, head)).astype(jnp.int32)
        for block in range(TILES // LANES):
            there = slice(block * LANES, (block + 1) * LANES)
            lane = lax.broadcasted_iota(jnp.int32, (LANES, LANES), 1) + block * LANES
            square = jnp.where(places == lane, 1.0, 0.0)
            picks_ref[here, there] = square.astype(jnp.bfloat16)
            across_ref[there, here] = square.T.astype(jnp.bfloat16)


def send_lines(own_ref, offsets, left_ref, table_ref, sent_refs, lines_ref, most_ref):
    own = own_ref[0]
    pairs = list(dict.fromkeys(offset // 2 for offset in offsets))
    columns = [(own >> 1) ^ pair for pair in pairs]
    low = low_half((DOT_ROWS, LANES))
    for part in range(ROWS // DOT_ROWS):
        here = slice(part * DOT_ROWS, (part + 1) * DOT_ROWS)
        for two in range(0, len(pairs), 2):
            even, odd = (
                line_product(at, here, left_ref, table_ref, columns[two : two + 2], (None,)) for at in range(2)
            )
            for pair in range(2):
                there = slice(pair * LANES, (pair + 1) * LANES)
                for one, values in enumerate(first_second(even[:, there], odd[:, there], low)):
                    line = 2 * (two + pair) + one
                    lines_ref[line, here, :] = values
                    most = jnp.max(jnp.abs(values).reshape(DOT_ROWS // 8, 8, LANES), axis=0)
                    most_ref[line] = most if part == 0 else jnp.maximum(most_ref[line], most)
    for offset, sent_ref in zip(offsets, sent_refs):
        line = 2 * pairs.index(offset // 2) + ((own ^ offset) & 1)
        level = level_of(jnp.max(most_ref[line], axis=0, keepdims=True))
        sent_ref[:ROWS, :] = fixed_of(lines_ref[line] * inverse_of(level))
        sent_ref[ROWS:, :] = head_of(level)


def forward_kernel(own_ref, brick_ref, table_ref, *refs):
    sent_refs = refs[: len(SEND)]
    picks_ref, across_ref, charge_ref, left_ref, lines_ref, most_ref = refs[len(SEND) :]
    write_picks(brick_ref, picks_ref, across_ref)
    for q in range(0, BRICK_ROWS, 4):
        there = slice(q * LANES, (q + 4) * LANES)
        charge_ref[:, there] = dot(across_ref[...], brick_ref[:, there])

    def load(block, step):
        here = slice(block * SPOTS, (block + 1) * SPOTS)
        return jnp.concatenate(
            [charge_ref[here, q * LANES : (q + 1) * LANES] for q in range(step * 4, step * 4 + 4)], axis=0
        )

    write_left(load, 4, left_ref)
    send_lines(own_ref, SEND, left_ref, table_ref, sent_refs, lines_ref, most_ref)


def roots(own_ref, base_ref, lam_ref):
    excess = base_ref[...] + lam_ref[pl.ds(own_ref[0], 1), :]
    spread = jnp.sqrt(excess * (excess + 4.0))
    root = 2.0 / (2.0 + excess + spread)
    return root, spread


def grid_rows(slabs, plane, xq, tx):
    start = ((plane * 4 + xq) * SPOTS + tx * 4) * slabs
    return pl.ds(pl.multiple_of(start, 4 * slabs), 4 * slabs)


def add_sines(got_refs, plane_ref, grid_ref, finish):
    slabs = len(got_refs)
    for at, got_ref in enumerate(got_refs):
        grid_ref[pl.ds(at, ROWS, stride=slabs), :] = wide(got_ref)

    def planes(tx, xq):
        return jnp.concatenate([grid_ref[grid_rows(slabs, plane, xq, tx), :] for plane in range(BZ)], axis=0)

    def sines(tx, _):
        for half in range(2):
            lines = jnp.concatenate([planes(tx, half * 2), planes(tx, half * 2 + 1)], axis=1)
            both = dot(plane_ref[...], jnp.concatenate(split(lines), axis=0))
            modes = both[:PLANES] + both[PLANES:]
            finish(tx * 4 + half * 2, modes[:, :LANES])
            finish(tx * 4 + half * 2 + 1, modes[:, LANES:])
        return 0

    lax.fori_loop(0, 16, sines, 0, unroll=8)


def down_first_kernel(own_ref, *refs):
    count = len(TAKE_FIRST)
    plane_in, modes_ref, grid_ref, plane_ref, sems = refs[count:]
    [copy] = start_copies(((plane_in.at[own_ref[0]], plane_ref),), sems)
    copy.wait()

    def finish(line, values):
        modes_ref[line] = values

    add_sines(refs[:count], plane_ref, grid_ref, finish)


def down_later_kernel(own_ref, *refs):
    count = len(TAKE_LATER)
    (
        sums_ref, plane_in, base_in, lam_in, walk_ref, end_ref,
        grid_ref, modes_ref, root_ref, last_ref, plane_ref, base_ref, lam_ref, sems,
    ) = refs[count:]
    copies = start_copies(((plane_in.at[own_ref[0]], plane_ref), (base_in, base_ref), (lam_in, lam_ref)), sems)
    for each in copies:
        each.wait()

    def finish(line, values):
        modes_ref[line] = sums_ref[line] + values

    add_sines(refs[:count], plane_ref, grid_ref, finish)
    root_ref[...] = roots(own_ref, base_ref, lam_ref)[0]
    part_rows = 64
    low = low_half((part_rows, LANES))
    for part in range(PLANES // part_rows):
        here = pl.ds(part * part_rows, part_rows)
        root = root_ref[here, :]
        square = root * root

        def walk(step, held):
            ahead, behind = modes_ref[step, here, :], modes_ref[STEPS - 1 - step, here, :]
            own = jnp.where(low, behind, ahead)
            other = pltpu.roll(jnp.where(low, ahead, behind), HALF, 1)
            held = square * held + (own + root * other)
            walk_ref[step, here, :] = held
            return held

        last_ref[here, :] = lax.fori_loop(0, STEPS, walk, jnp.zeros((part_rows, LANES), jnp.float32), unroll=8)
    last = last_ref[...]
    level = level_of(jnp.max(jnp.abs(last), axis=0, keepdims=True))
    end_ref[:PLANES, :] = fixed_of(last * inverse_of(level))
    end_ref[PLANES:, :] = head_of(level)


def send_planes(full_ref, sent_refs, plane_ref, root_ref, gain_ref, grid_ref, level_ref):
    slabs = len(sent_refs)
    rows = 4 * BZ * slabs

    def solved(step):
        low = low_half((PLANES, LANES))
        near = jnp.where(low, full_ref[STEPS - step], full_ref[step + 1])
        far = jnp.where(low, full_ref[STEPS - 1 - step], full_ref[step])
        return gain_ref[...] * (near + root_ref[...] * pltpu.roll(far, HALF, 1))

    def sines(tx, most):
        for half in range(2):
            first = tx * 4 + half * 2
            modes = jnp.concatenate([solved(first), solved(first + 1)], axis=1)
            both = dot(plane_ref[...], jnp.concatenate(split(modes), axis=0))
            lines = both[:rows] + both[rows:]
            for one in range(2):
                part = lines[:, one * LANES : (one + 1) * LANES]
                most = jnp.maximum(most, jnp.max(jnp.abs(part).reshape(rows // 8, 8, LANES), axis=0))
                for plane in range(BZ):
                    grid_ref[grid_rows(slabs, plane, half * 2 + one, tx), :] = part[
                        plane * 4 * slabs : (plane + 1) * 4 * slabs
                    ]
        return most

    most = lax.fori_loop(0, 16, sines, jnp.zeros((8, LANES), jnp.float32), unroll=8)
    level_ref[...] = level_of(most)
    for at, sent_ref in enumerate(sent_refs):
        level = level_ref[at : at + 1, :]
        sent_ref[:ROWS, :] = fixed_of(grid_ref[pl.ds(at, ROWS, stride=slabs), :] * inverse_of(level))
        sent_ref[ROWS:, :] = head_of(level)


def up_kernel(own_ref, walk_ref, *refs):
    end_refs, (plane_in, base_in, lam_in) = refs[:GROUPS], refs[GROUPS : GROUPS + 3]
    count = GROUPS + 3 + len(SEND)
    sent_refs = refs[GROUPS + 3 : count]
    full_ref, root_ref, gain_ref, grid_ref, level_ref, ends_ref, plane_ref, base_ref, lam_ref, sems = refs[count:]
    copies = start_copies(((base_in, base_ref), (lam_in, lam_ref), (plane_in.at[own_ref[0]], plane_ref)), sems)
    for at, end_ref in enumerate(end_refs):
        ends_ref[at] = wide(end_ref)
    for each in copies:
        each.wait()
    root, spread = roots(own_ref, base_ref, lam_ref)
    root_ref[...] = root
    gain_ref[...] = 1.0 / spread
    part_rows = 64
    low = low_half((part_rows, LANES))
    for part in range(PLANES // part_rows):
        here = pl.ds(part * part_rows, part_rows)
        root = root_ref[here, :]
        square = root * root
        across = square
        for _ in range(6):
            across = across * across
        entering = jnp.zeros((part_rows, LANES), jnp.float32)
        for step in range(GROUPS - 1, -1, -1):
            before = ends_ref[(step + 1) % GROUPS, here, :]
            after = ends_ref[GROUPS - 1 - step, here, :]
            entering = entering * across + jnp.where(low, after, before)
        around = across
        for _ in range(2):
            around = around * around
        entering = entering / (1.0 - around)
        full_ref[0, here, :] = entering

        def carry(step, reach):
            full_ref[step + 1, here, :] = walk_ref[step, here, :] + reach
            return reach * square

        lax.fori_loop(0, STEPS, carry, entering * square, unroll=8)
    send_planes(full_ref, sent_refs, plane_ref, root_ref, gain_ref, grid_ref, level_ref)


def take_lines(own_ref, offsets, got_refs, left_ref, lines_ref):
    own = own_ref[0]
    pairs = list(dict.fromkeys(offset // 2 for offset in offsets))
    for offset, got_ref in zip(offsets, got_refs):
        lines_ref[2 * pairs.index(offset // 2) + ((own ^ offset) & 1)] = wide(got_ref)

    def load(block, step):
        return lines_ref[block, step * 4 * SPOTS : (step + 1) * 4 * SPOTS, :]

    write_left(load, len(pairs), left_ref)
    return [(own >> 1) ^ pair for pair in pairs]


def reply_first_kernel(own_ref, *refs):
    count = len(TAKE_FIRST)
    table_ref, sums_ref, lines_ref, left_ref = refs[count:]
    rows = take_lines(own_ref, TAKE_FIRST, refs[:count], left_ref, lines_ref)
    for part in range(ROWS // DOT_ROWS):
        here = slice(part * DOT_ROWS, (part + 1) * DOT_ROWS)
        for column in (0, 2):
            for at in range(2):
                sums_ref[at, here, column * LANES : (column + 2) * LANES] = line_product(
                    at, here, left_ref, table_ref, (column, column + 1), rows
                )


def reply_later_kernel(own_ref, *refs):
    count = len(TAKE_LATER)
    sums_ref, picks_ref, table_ref, out_ref, lines_ref, left_ref, pot_ref = refs[count:]
    rows = take_lines(own_ref, TAKE_LATER, refs[:count], left_ref, lines_ref)
    low = low_half((DOT_ROWS, LANES))
    for part in range(ROWS // DOT_ROWS):
        here = slice(part * DOT_ROWS, (part + 1) * DOT_ROWS)
        for column in (0, 2):
            even, odd = (
                line_product(at, here, left_ref, table_ref, (column, column + 1), rows)
                + sums_ref[at, here, column * LANES : (column + 2) * LANES]
                for at in range(2)
            )
            for pair in range(2):
                there = slice(pair * LANES, (pair + 1) * LANES)
                for one, values in enumerate(first_second(even[:, there], odd[:, there], low)):
                    ty = 2 * (column + pair) + one
                    for q in range(DOT_ROWS // SPOTS):
                        at = part * (DOT_ROWS // SPOTS) + q
                        pot_ref[ty * SPOTS : (ty + 1) * SPOTS, at * LANES : (at + 1) * LANES] = values[
                            q * SPOTS : (q + 1) * SPOTS
                        ].astype(jnp.bfloat16)
    for q in range(0, BRICK_ROWS, 4):
        there = slice(q * LANES, (q + 4) * LANES)
        out_ref[:, there] = dot(picks_ref[...], pot_ref[:, there]).astype(jnp.bfloat16)


def unpack_kernel(back_ref, got_ref, out_ref):
    for q in range(0, BRICK_ROWS, 4):
        there = slice(q * LANES, (q + 4) * LANES)
        out_ref[:, there] = dot(back_ref[...], got_ref[:, there]).astype(jnp.bfloat16)


def call(kernel, name, operands, spaces, outs, places, scratch, vmem=VMEM_BYTES):
    return pl.pallas_call(
        kernel,
        out_shape=outs,
        in_specs=[pl.BlockSpec(memory_space=space) for space in spaces],
        out_specs=[pl.BlockSpec(memory_space=space) for space in places],
        scratch_shapes=scratch,
        compiler_params=pltpu.CompilerParams(vmem_limit_bytes=vmem),
        name=name,
    )(*operands)


def on_device_8x4(bricks, owners, tile_ids, counts):
    V, S, H = pltpu.VMEM, pltpu.SMEM, pltpu.HBM
    f32, bf16, i32, i16 = jnp.float32, jnp.bfloat16, jnp.int32, jnp.int16
    shape, dma = jax.ShapeDtypeStruct, pltpu.SemaphoreType.DMA
    brick_rows = bricks.shape[0]
    line_table = jnp.asarray(line_tables())
    planes_in = [jnp.asarray(plane_tables(offsets, False)) for offsets in (TAKE_FIRST, TAKE_LATER)]
    planes_out = jnp.asarray(plane_tables(SEND, True))
    base, lam = (jnp.asarray(each) for each in mode_tables())
    own = lax.axis_index("gz").astype(i32).reshape(1)
    sent_shape = shape((ROWS + HEAD_ROWS, LANES), i16)
    end_shape = shape((PLANES + HEAD_ROWS, LANES), i16)
    cube, flat, sums_shape = (STEPS, PLANES, LANES), (PLANES, LANES), (2, ROWS, NY)
    line, rows_shape = (ROWS, LANES), (SLOTS, CELLS + LANES)

    def all_ways(values):
        return lax.all_to_all(values, ("gz", "ma"), split_axis=0, concat_axis=0, tiled=True)

    def over_slabs(offset, values):
        return lax.ppermute(values, "gz", [(g, g ^ offset) for g in range(SLABS)]) if offset else values

    def round_groups(values, step):
        return lax.ppermute(values, "ma", [(m, (m + step) % GROUPS) for m in range(GROUPS)]) if step else values

    def exchanged(sent):
        sent = dict(zip(SEND, sent))
        got = {offset: over_slabs(offset, sent[offset]) for offset in TAKE_FIRST + TAKE_LATER}
        return [got[offset] for offset in TAKE_FIRST], [got[offset] for offset in TAKE_LATER]

    outgoing, back = call(
        pack_kernel,
        "pack",
        (owners.reshape(brick_rows), tile_ids, counts, bricks),
        [H] * 4,
        [shape(rows_shape, bf16), shape((brick_rows, SLOTS), bf16)],
        [H, V],
        [
            S((brick_rows,), i32),
            S((brick_rows,), i32),
            S((1,), i32),
            V(bricks.shape, bf16),
            V((SLOTS + PAIR_SLOTS, brick_rows), f32),
            V((SLOTS + PAIR_SLOTS, LANES), f32),
            V(rows_shape, bf16),
            S((DOMAINS,), i32),
            dma((4,)),
            dma((4,)),
        ],
        ALL_VMEM_BYTES,
    )
    *sent, picks = call(
        forward_kernel,
        "forward",
        (own, all_ways(outgoing), line_table),
        [S, V, V],
        [sent_shape] * len(SEND) + [shape((SLOTS, TILES), bf16)],
        [V] * (len(SEND) + 1),
        [
            V((TILES, SLOTS), bf16),
            V((TILES, CELLS), f32),
            V((2, ROWS, 2 * NY), bf16),
            V((len(SEND), *line), f32),
            V((len(SEND), 8, LANES), f32),
        ],
    )
    first, later = exchanged(sent)
    (sums,) = call(
        down_first_kernel,
        "down_first",
        (own, *first, planes_in[0]),
        [S] + [V] * len(first) + [H],
        [shape(cube, f32)],
        [V],
        [V((len(first) * ROWS, LANES), f32), V(planes_in[0].shape[1:], bf16), dma((1,))],
    )
    tables = [V(base.shape, f32), V(lam.shape, f32), dma((3,))]
    walk, end = call(
        down_later_kernel,
        "down_later",
        (own, *later, sums, planes_in[1], base, lam),
        [S] + [V] * (len(later) + 1) + [H] * 3,
        [shape(cube, f32), end_shape],
        [V, V],
        [
            V((len(later) * ROWS, LANES), f32),
            V(cube, f32),
            V(flat, f32),
            V(flat, f32),
            V(planes_in[1].shape[1:], bf16),
            *tables,
        ],
    )
    ends = [round_groups(end, step) for step in range(GROUPS)]
    sent = call(
        up_kernel,
        "up",
        (own, walk, *ends, planes_out, base, lam),
        [S] + [V] * (1 + GROUPS) + [H] * 3,
        [sent_shape] * len(SEND),
        [V] * len(SEND),
        [
            V((STEPS + 1, *flat), f32),
            V(flat, f32),
            V(flat, f32),
            V((len(SEND) * ROWS, LANES), f32),
            V((8, LANES), f32),
            V((GROUPS, *flat), f32),
            V(planes_out.shape[1:], bf16),
            *tables,
        ],
    )
    first, later = exchanged(sent)
    (sums,) = call(
        reply_first_kernel,
        "reply_first",
        (own, *first, line_table),
        [S] + [V] * (len(first) + 1),
        [shape(sums_shape, f32)],
        [V],
        [V((len(first), *line), f32), V((2, ROWS, len(first) * LANES), bf16)],
    )
    (replies,) = call(
        reply_later_kernel,
        "reply_later",
        (own, *later, sums, picks, line_table),
        [S] + [V] * (len(later) + 3),
        [shape((SLOTS, CELLS), bf16)],
        [V],
        [
            V((len(later), *line), f32),
            V((2, ROWS, len(later) * LANES), bf16),
            V((TILES, CELLS), bf16),
        ],
    )
    (result,) = call(
        unpack_kernel,
        "unpack",
        (back, all_ways(replies)),
        [V, V],
        [shape((brick_rows, CELLS), bf16)],
        [V],
        [],
    )
    return result


def solution(mesh):
    in_specs = (P(("gz", "ma"), None), P(("gz", "ma"), None), P(("gz", "ma")), P(("gz", "ma")))
    out_specs = P(("gz", "ma"), None)
    body = on_device_8x4 if (mesh.shape["gz"], mesh.shape["ma"]) == (SLABS, GROUPS) else on_device
    return jax.shard_map(body, mesh=mesh, in_specs=in_specs, out_specs=out_specs, check_vma=False)
```

```python
import math

import jax
import jax.numpy as jnp
import ml_dtypes
import numpy as np
from jax import lax
from jax.experimental import pallas as pl
from jax.experimental.pallas import tpu as pltpu
from jax.sharding import PartitionSpec as P

NX = 512
NY = 512
SCREEN = 16
BZ = 4
BX = 8
BY = 64
CZ = 16


def hartley(length):
    indices = jnp.arange(length, dtype=jnp.int32)
    products = indices[:, None] * indices[None, :] % length
    angles = 2.0 * math.pi / length * products.astype(jnp.float32)
    return (jnp.cos(angles) + jnp.sin(angles)) / math.sqrt(length)


def second_difference(length, indices):
    return 2.0 - 2.0 * jnp.cos(2.0 * math.pi / length * indices.astype(jnp.float32))


def thomas(right_side, diagonal):
    start_zero = jnp.zeros(right_side.shape[1:], jnp.float32)

    def down(state_pair, plane):
        factor = 1.0 / (diagonal - state_pair[0])
        partial_value = (plane + state_pair[1]) * factor
        return ((factor, partial_value), (factor, partial_value))

    _, (factors, partials) = lax.scan(down, (start_zero, start_zero), right_side)

    def upward(beyond, factor_partial):
        solved = factor_partial[1] + factor_partial[0] * beyond
        return (solved, solved)

    _, solutions = lax.scan(upward, start_zero, (factors, partials), reverse=True)
    return solutions


def regroup(values):
    return lax.all_to_all(values, "ma", split_axis=2, concat_axis=1, tiled=True)


def on_device(bricks, owners, tile_ids, counts):
    domains = lax.axis_size(("gz", "ma"))
    group_count = lax.axis_size("ma")
    slab_count = lax.axis_size("gz")
    brick_rows, brick_cells = bricks.shape
    slot_count = max(2, 2 * brick_rows // domains)
    local_x = NX // group_count
    local_y = NY // group_count
    tiles_dev = CZ // BZ * (local_x // BX) * (NY // BY)
    highest = lax.Precision.HIGHEST
    target = owners[:, 0]
    row_order = jnp.arange(brick_rows, dtype=jnp.int32)
    earlier_same = (target[:, None] == target[None, :]) & (row_order[None, :] < row_order[:, None])
    within = jnp.sum(earlier_same.astype(jnp.int32), axis=1)
    slot_of = target * slot_count + within
    is_live = row_order < counts[0]
    loaded = jnp.where(is_live[:, None], bricks, jnp.zeros_like(bricks))
    outgoing = jnp.zeros((domains * slot_count, brick_cells), jnp.bfloat16).at[slot_of].set(loaded)
    out_ids = jnp.full((domains * slot_count,), tiles_dev, jnp.int32).at[slot_of].set(tile_ids)
    incoming, in_ids = (
        lax.all_to_all(outgoing, ("gz", "ma"), split_axis=0, concat_axis=0, tiled=True),
        lax.all_to_all(out_ids, ("gz", "ma"), split_axis=0, concat_axis=0, tiled=True),
    )
    picker = (jnp.arange(tiles_dev, dtype=jnp.int32)[:, None] == in_ids[None, :]).astype(
        jnp.bfloat16
    )
    deposit = jnp.dot(picker, incoming, preferred_element_type=jnp.float32)
    charge = deposit.reshape(CZ // BZ, local_x // BX, NY // BY, BZ, BX, BY)
    charge = charge.transpose(0, 3, 1, 4, 2, 5).reshape(CZ, local_x, NY)
    table_x = hartley(NX)
    table_y = hartley(NY)
    along_y = jnp.einsum("zxy,ky->zxk", charge, table_y, precision=highest)
    gathered_x = regroup(along_y)
    spectrum = jnp.einsum("zxk,jx->zjk", gathered_x, table_x, precision=highest)
    columns = lax.axis_index("ma") * local_y + jnp.arange(local_y, dtype=jnp.int32)
    lam_y = second_difference(NY, columns)
    screening = 1.0 / (SCREEN * SCREEN)
    slab_index = lax.axis_index("gz")
    lam_x = second_difference(NX, jnp.arange(NX, dtype=jnp.int32))
    diagonal = 2.0 + screening + lam_x[:, None] + lam_y[None, :]
    interior = spectrum[1:]
    particular = thomas(interior, diagonal)
    unit_rhs = jnp.zeros_like(interior).at[0].set(1.0)
    spike = thomas(unit_rhs, diagonal)
    near_weight = spike[0]
    far_weight = spike[-1]
    head_term = spectrum[0] + particular[0]
    tail_term = particular[-1]
    reduced_first = diagonal - near_weight
    reduced_rest = diagonal - 2.0 * near_weight
    start_zero = jnp.zeros_like(diagonal)
    heads, tails = (
        lax.all_gather(head_term[None], "gz", axis=0, tiled=True),
        lax.all_gather(tail_term[None], "gz", axis=0, tiled=True),
    )
    before = jnp.concatenate([start_zero[None], tails[:-1]], axis=0)
    sources = heads + before

    def chain_down(state_pair, packed):
        source, position = packed
        base_term = jnp.where(position == 0, reduced_first, reduced_rest)
        pivot_now = 1.0 / (base_term - far_weight * far_weight * state_pair[0])
        forward_part = pivot_now * (source + far_weight * state_pair[1])
        return ((pivot_now, forward_part), (pivot_now, forward_part))

    _, (pivots, forwards) = lax.scan(
        chain_down, (start_zero, start_zero), (sources, jnp.arange(slab_count, dtype=jnp.int32))
    )

    def chain_up(beyond, packed):
        plane_value = packed[1] + far_weight * packed[0] * beyond
        return (plane_value, plane_value)

    _, separators = lax.scan(chain_up, start_zero, (pivots, forwards), reverse=True)
    padded_sep = jnp.concatenate([separators, start_zero[None]], axis=0)
    own_plane = lax.dynamic_index_in_dim(padded_sep, slab_index, 0, keepdims=False)
    next_plane = lax.dynamic_index_in_dim(padded_sep, slab_index + 1, 0, keepdims=False)
    interior_sol = particular + own_plane[None] * spike + next_plane[None] * spike[::-1]
    modal = jnp.concatenate([own_plane[None], interior_sol], axis=0)
    back_x = jnp.einsum("zjk,jx->zkx", modal, table_x, precision=highest)
    gathered_y = regroup(back_x)
    potential = jnp.einsum("zkx,ky->zxy", gathered_y, table_y, precision=highest)
    pot_tiles = potential.reshape(CZ // BZ, BZ, local_x // BX, BX, NY // BY, BY)
    pot_tiles = (
        pot_tiles.transpose(0, 2, 4, 1, 3, 5).reshape(tiles_dev, brick_cells).astype(jnp.bfloat16)
    )
    padded_tiles = jnp.concatenate([pot_tiles, jnp.zeros((1, brick_cells), jnp.bfloat16)], axis=0)
    replies = padded_tiles[in_ids]
    returned = lax.all_to_all(replies, ("gz", "ma"), split_axis=0, concat_axis=0, tiled=True)
    result = returned[slot_of]
    return jnp.where(is_live[:, None], result, jnp.zeros_like(result))


DOMAINS = 32
GROUPS = 4
SLABS = 8
SEND = (4, 2, 5, 3, 0, 1, 6, 7)
TAKE_FIRST = (0, 4, 2, 5, 3, 1)
TAKE_LATER = (6, 7)
PAIR_SLOTS = 8
SLOTS = DOMAINS * PAIR_SLOTS
TILES = 512
BRICK_ROWS = 16
CELLS = 2048
LANES = 128
HALF = 64
SPOTS = 64
ROWS = BRICK_ROWS * SPOTS
DOT_ROWS = 512
PAIRS = 4
CLASSES = (0, 4, 1, 7, 2, 6, 3, 5)
HEAD_ROWS = 16
STEPS = 64
PLANES = 128
FULL = 32700.0
LOG_UNIT = 128.0
VMEM_BYTES = 24 * 1024 * 1024
ALL_VMEM_BYTES = 60 * 1024 * 1024


def split_table(table):
    high = table.astype(ml_dtypes.bfloat16)
    low = (table - high.astype(np.float64)).astype(ml_dtypes.bfloat16)
    return high, low


def line_tables():
    iy, k2 = np.arange(HALF)[:, None], np.arange(HALF)[None, :]
    tables = []
    for pair in range(PAIRS):
        table = np.zeros((LANES, LANES))
        for one in range(2):
            angle = 2.0 * np.pi / NY * (iy * (CLASSES[2 * pair + one] + 8 * k2) % NY)
            cosine, sine = np.cos(angle) / np.sqrt(NY), np.sin(angle) / np.sqrt(NY)
            there = slice(one * HALF, (one + 1) * HALF)
            if pair == 0:
                table[there, there] = cosine + sine
            else:
                table[:HALF, there] = cosine + sine
                table[HALF:, there] = (cosine - sine) * (1 - 2 * one)
        tables.append(table)

    def stacked(table):
        high, low = split_table(table)
        return np.concatenate(
            [np.concatenate([high, low], axis=1), np.concatenate([high, np.zeros_like(low)], axis=1)], axis=0
        )

    return np.stack([stacked(table) for table in tables]), np.stack([stacked(table.T) for table in tables])


def class_weights():
    pair, ty = np.arange(PAIRS)[:, None], np.arange(4)[None, :]
    cosine, sine = np.cos(np.pi / 4.0 * pair * ty), np.sin(np.pi / 4.0 * pair * ty)
    sine[0] = (-1.0) ** np.arange(4)
    sign = (-1.0) ** pair * np.ones((1, 4))
    return np.concatenate([cosine, sine, sign], axis=1).astype(np.float32)


def plane_tables(offsets, turned):
    index = np.arange(PLANES)
    table = np.sqrt(2.0 / (PLANES + 1)) * np.sin(
        np.pi / (PLANES + 1) * ((index[:, None] + 1) * (index[None, :] + 1) % (2 * PLANES + 2))
    )
    each = []
    for own in range(SLABS):
        slabs = np.array([own ^ offset for offset in offsets])
        plane, tz = np.arange(BZ)[:, None, None], np.arange(BZ)[None, :, None]
        part = table[:, (slabs * CZ + tz * BZ + plane).reshape(-1)]
        high, low = split_table(part.T if turned else part)
        top = np.concatenate([high, high], axis=1)
        bottom = np.concatenate([low, np.zeros_like(low)], axis=1)
        each.append(np.concatenate([top, bottom], axis=0))
    return np.stack(each)


def mode_tables():
    mu = 2.0 - 2.0 * np.cos(np.pi / (PLANES + 1) * (np.arange(PLANES) + 1))
    base = np.broadcast_to((mu + 1.0 / (SCREEN * SCREEN))[:, None], (PLANES, LANES))
    lam = 2.0 - 2.0 * np.cos(2.0 * np.pi / NY * np.arange(NY))
    lam = np.stack([lam[number::8] for number in CLASSES])
    return base.astype(np.float32), np.concatenate([lam, lam], axis=1).astype(np.float32)


def low_half(shape):
    return lax.broadcasted_iota(jnp.int32, shape, len(shape) - 1) < HALF


def split(values):
    high = values.astype(jnp.bfloat16)
    return high, (values - high.astype(jnp.float32)).astype(jnp.bfloat16)


def dot(left, right):
    return jnp.dot(left, right, preferred_element_type=jnp.float32)


def start_copies(pairs, sems):
    copies = [pltpu.make_async_copy(source, place, sems.at[at]) for at, (source, place) in enumerate(pairs)]
    for each in copies:
        each.start()
    return copies


def even_odd(first, second, low):
    crossed = pltpu.roll(jnp.where(low, second, first), HALF, 1)
    return jnp.where(low, first, crossed), jnp.where(low, crossed, second)


def write_left(at, here, lines, left_ref):
    for line, values in enumerate(lines):
        high, rest = split(values)
        there = slice(line * ROWS + here.start, line * ROWS + here.stop)
        left_ref[at, there, :LANES] = high
        left_ref[at, there, LANES:] = rest


def line_product(at, here, left_ref, table):
    products = []
    for line in range(2):
        there = slice(line * ROWS + here.start, line * ROWS + here.stop)
        both = dot(left_ref[at, there, :], table)
        products.append(both[:, :LANES] + both[:, LANES:])
    return even_odd(*products, low_half(products[0].shape))


def class_sums(points):
    half = [points[ty] + points[ty + 4] for ty in range(4)]
    rest = [points[ty] - points[ty + 4] for ty in range(4)]
    even, odd = half[0] + half[2], half[1] + half[3]
    turn = math.sqrt(0.5)
    across, along = turn * (rest[1] - rest[3]), turn * (rest[1] + rest[3])
    return (
        (even + odd, even - odd),
        (rest[0] + across, rest[2] + along),
        (half[0] - half[2], half[1] - half[3]),
        (rest[0] - across, along - rest[2]),
    )


def level_of(most):
    return jnp.floor(jnp.log2(jnp.maximum(most, 1e-30)) * LOG_UNIT) + 2.0


def inverse_of(level):
    return FULL * jnp.exp2(level * (-1.0 / LOG_UNIT))


def fixed_of(values):
    return jnp.floor(values + 0.5).astype(jnp.int32).astype(jnp.int16)


def head_of(level):
    return jnp.broadcast_to(level, (HEAD_ROWS, LANES)).astype(jnp.int32).astype(jnp.int16)


def unit_of(sent_ref):
    head = sent_ref[sent_ref.shape[0] - HEAD_ROWS :, :].astype(jnp.int32).astype(jnp.float32)
    return jnp.exp2(head[0:1] * (1.0 / LOG_UNIT)) * (1.0 / FULL)


def wide(sent_ref):
    block = sent_ref[: sent_ref.shape[0] - HEAD_ROWS, :]
    return block.astype(jnp.int32).astype(jnp.float32) * unit_of(sent_ref)


def pack_kernel(
    owner_in, tile_in, count_in, brick_in, out_ref, back_ref,
    owner_ref, tile_ref, count_ref, brick_ref, pick_ref, head_ref, ready_ref, used_ref, sems, out_sems,
):
    copies = start_copies(
        ((owner_in, owner_ref), (tile_in, tile_ref), (count_in, count_ref), (brick_in, brick_ref)), sems
    )
    brick_rows = brick_ref.shape[0]
    head_ref[...] = jnp.full(head_ref.shape, float(TILES), jnp.float32)
    pick_ref[...] = jnp.zeros(pick_ref.shape, jnp.float32)
    for owner in range(DOMAINS):
        used_ref[owner] = 0
    for each in copies[:3]:
        each.wait()
    count = count_ref[0]
    lane = lax.broadcasted_iota(jnp.int32, (1, brick_rows), 1)

    def place(r, _):
        owner = owner_ref[r]
        within = used_ref[owner]
        used_ref[owner] = within + 1
        slot = jnp.where(r < count, owner * PAIR_SLOTS + within, SLOTS)
        tile = tile_ref[r]
        position = (tile & 7) * SPOTS + ((tile >> 3) & 15) * 4 + (tile >> 7)
        pick_ref[pl.ds(slot, 1), :] = jnp.where(lane == r, 1.0, 0.0)
        head_ref[pl.ds(slot, 1), :] = jnp.full((1, LANES), position, jnp.int32).astype(jnp.float32)
        return 0

    lax.fori_loop(0, brick_rows, place, 0, unroll=8)
    copies[3].wait()
    copies = []
    rows = 64
    for part in range(SLOTS // rows):
        here = slice(part * rows, (part + 1) * rows)
        ready_ref[here, :CELLS] = dot(pick_ref[here, :].astype(jnp.bfloat16), brick_ref[...]).astype(jnp.bfloat16)
        head = head_ref[here, :]
        high = jnp.floor(head * (1.0 / 32.0))
        ready_ref[here, CELLS:] = jnp.where(low_half(head.shape), high, head - 32.0 * high).astype(jnp.bfloat16)
        some = pl.ds(part * rows, rows)
        copies.append(pltpu.make_async_copy(ready_ref.at[some], out_ref.at[some], out_sems.at[part]))
        copies[-1].start()
    for part in range(SLOTS // LANES):
        here = slice(part * LANES, (part + 1) * LANES)
        back_ref[:, here] = pick_ref[here, :].T.astype(jnp.bfloat16)
    for each in copies:
        each.wait()


def write_picks(brick_ref, picks_ref, across_ref):
    for part in range(SLOTS // LANES):
        here = slice(part * LANES, (part + 1) * LANES)
        head = brick_ref[here, CELLS:].astype(jnp.float32)
        turned = pltpu.roll(head, HALF, 1)
        low = low_half(head.shape)
        places = (jnp.where(low, head, turned) * 32.0 + jnp.where(low, turned, head)).astype(jnp.int32)
        for block in range(TILES // LANES):
            there = slice(block * LANES, (block + 1) * LANES)
            lane = lax.broadcasted_iota(jnp.int32, (LANES, LANES), 1) + block * LANES
            square = jnp.where(places == lane, 1.0, 0.0)
            picks_ref[here, there] = square.astype(jnp.bfloat16)
            across_ref[there, here] = square.T.astype(jnp.bfloat16)


def forward_kernel(own_ref, brick_ref, table_ref, *refs):
    sent_refs = refs[: len(SEND)]
    picks_ref, across_ref, left_ref, lines_ref, most_ref = refs[len(SEND) :]
    write_picks(brick_ref, picks_ref, across_ref)
    low = low_half((SPOTS, LANES))
    for q in range(0, BRICK_ROWS, 4):
        charge = dot(across_ref[...], brick_ref[:, q * LANES : (q + 4) * LANES])
        for one in range(4):
            there = slice(one * LANES, (one + 1) * LANES)
            here = slice((q + one) * SPOTS, (q + one + 1) * SPOTS)
            points = [charge[ty * SPOTS : (ty + 1) * SPOTS, there] for ty in range(8)]
            for pair, (cosines, sines) in enumerate(class_sums(points)):
                write_left(pair, here, even_odd(cosines, sines, low), left_ref)
    for pair in range(PAIRS):
        for part in range(ROWS // DOT_ROWS):
            here = slice(part * DOT_ROWS, (part + 1) * DOT_ROWS)
            for one, values in enumerate(line_product(pair, here, left_ref, table_ref[pair])):
                lines_ref[2 * pair + one, here, :] = values
                most = jnp.max(jnp.abs(values).reshape(DOT_ROWS // 8, 8, LANES), axis=0)
                most_ref[2 * pair + one] = most if part == 0 else jnp.maximum(most_ref[2 * pair + one], most)
    for offset, sent_ref in zip(SEND, sent_refs):
        g = own_ref[0] ^ offset
        level = level_of(jnp.max(most_ref[g], axis=0, keepdims=True))
        sent_ref[:ROWS, :] = fixed_of(lines_ref[g] * inverse_of(level))
        sent_ref[ROWS:, :] = head_of(level)


def roots(own_ref, base_ref, lam_ref):
    excess = base_ref[...] + lam_ref[pl.ds(own_ref[0], 1), :]
    spread = jnp.sqrt(excess * (excess + 4.0))
    root = 2.0 / (2.0 + excess + spread)
    return root, spread


def grid_rows(slabs, plane, xq, tx):
    start = ((plane * 4 + xq) * SPOTS + tx * 4) * slabs
    return pl.ds(pl.multiple_of(start, 4 * slabs), 4 * slabs)


def add_sines(got_refs, plane_ref, grid_ref, finish):
    slabs = len(got_refs)
    for at, got_ref in enumerate(got_refs):
        grid_ref[pl.ds(at, ROWS, stride=slabs), :] = wide(got_ref)

    def planes(tx, xq):
        return jnp.concatenate([grid_ref[grid_rows(slabs, plane, xq, tx), :] for plane in range(BZ)], axis=0)

    def sines(tx, _):
        for half in range(2):
            lines = jnp.concatenate([planes(tx, half * 2), planes(tx, half * 2 + 1)], axis=1)
            both = dot(plane_ref[...], jnp.concatenate(split(lines), axis=0))
            modes = both[:PLANES] + both[PLANES:]
            finish(tx * 4 + half * 2, modes[:, :LANES])
            finish(tx * 4 + half * 2 + 1, modes[:, LANES:])
        return 0

    lax.fori_loop(0, 16, sines, 0, unroll=8)


def down_first_kernel(own_ref, *refs):
    count = len(TAKE_FIRST)
    plane_in, modes_ref, grid_ref, plane_ref, sems = refs[count:]
    [copy] = start_copies(((plane_in.at[own_ref[0]], plane_ref),), sems)
    copy.wait()

    def finish(line, values):
        modes_ref[line] = values

    add_sines(refs[:count], plane_ref, grid_ref, finish)


def down_later_kernel(own_ref, *refs):
    count = len(TAKE_LATER)
    (
        sums_ref, plane_in, base_in, lam_in, walk_ref, end_ref,
        grid_ref, modes_ref, root_ref, last_ref, plane_ref, base_ref, lam_ref, sems,
    ) = refs[count:]
    copies = start_copies(((plane_in.at[own_ref[0]], plane_ref), (base_in, base_ref), (lam_in, lam_ref)), sems)
    for each in copies:
        each.wait()

    def finish(line, values):
        modes_ref[line] = sums_ref[line] + values

    add_sines(refs[:count], plane_ref, grid_ref, finish)
    root_ref[...] = roots(own_ref, base_ref, lam_ref)[0]
    part_rows = 64
    low = low_half((part_rows, LANES))
    for part in range(PLANES // part_rows):
        here = pl.ds(part * part_rows, part_rows)
        root = root_ref[here, :]
        square = root * root

        def walk(step, held):
            ahead, behind = modes_ref[step, here, :], modes_ref[STEPS - 1 - step, here, :]
            own = jnp.where(low, behind, ahead)
            other = pltpu.roll(jnp.where(low, ahead, behind), HALF, 1)
            held = square * held + (own + root * other)
            walk_ref[step, here, :] = held
            return held

        last_ref[here, :] = lax.fori_loop(0, STEPS, walk, jnp.zeros((part_rows, LANES), jnp.float32), unroll=8)
    last = last_ref[...]
    level = level_of(jnp.max(jnp.abs(last), axis=0, keepdims=True))
    end_ref[:PLANES, :] = fixed_of(last * inverse_of(level))
    end_ref[PLANES:, :] = head_of(level)


def send_planes(full_ref, sent_refs, plane_ref, root_ref, gain_ref, grid_ref, level_ref):
    slabs = len(sent_refs)
    rows = 4 * BZ * slabs

    def solved(step):
        low = low_half((PLANES, LANES))
        near = jnp.where(low, full_ref[STEPS - step], full_ref[step + 1])
        far = jnp.where(low, full_ref[STEPS - 1 - step], full_ref[step])
        return gain_ref[...] * (near + root_ref[...] * pltpu.roll(far, HALF, 1))

    def sines(tx, most):
        for half in range(2):
            first = tx * 4 + half * 2
            modes = jnp.concatenate([solved(first), solved(first + 1)], axis=1)
            both = dot(plane_ref[...], jnp.concatenate(split(modes), axis=0))
            lines = both[:rows] + both[rows:]
            for one in range(2):
                part = lines[:, one * LANES : (one + 1) * LANES]
                most = jnp.maximum(most, jnp.max(jnp.abs(part).reshape(rows // 8, 8, LANES), axis=0))
                for plane in range(BZ):
                    grid_ref[grid_rows(slabs, plane, half * 2 + one, tx), :] = part[
                        plane * 4 * slabs : (plane + 1) * 4 * slabs
                    ]
        return most

    most = lax.fori_loop(0, 16, sines, jnp.zeros((8, LANES), jnp.float32), unroll=8)
    level_ref[...] = level_of(most)
    for at, sent_ref in enumerate(sent_refs):
        level = level_ref[at : at + 1, :]
        sent_ref[:ROWS, :] = fixed_of(grid_ref[pl.ds(at, ROWS, stride=slabs), :] * inverse_of(level))
        sent_ref[ROWS:, :] = head_of(level)


def up_kernel(own_ref, walk_ref, *refs):
    end_refs, (plane_in, base_in, lam_in) = refs[:GROUPS], refs[GROUPS : GROUPS + 3]
    count = GROUPS + 3 + len(SEND)
    sent_refs = refs[GROUPS + 3 : count]
    full_ref, root_ref, gain_ref, grid_ref, level_ref, ends_ref, plane_ref, base_ref, lam_ref, sems = refs[count:]
    copies = start_copies(((base_in, base_ref), (lam_in, lam_ref), (plane_in.at[own_ref[0]], plane_ref)), sems)
    for at, end_ref in enumerate(end_refs):
        ends_ref[at] = wide(end_ref)
    for each in copies:
        each.wait()
    root, spread = roots(own_ref, base_ref, lam_ref)
    root_ref[...] = root
    gain_ref[...] = 1.0 / spread
    part_rows = 64
    low = low_half((part_rows, LANES))
    for part in range(PLANES // part_rows):
        here = pl.ds(part * part_rows, part_rows)
        root = root_ref[here, :]
        square = root * root
        across = square
        for _ in range(6):
            across = across * across
        entering = jnp.zeros((part_rows, LANES), jnp.float32)
        for step in range(GROUPS - 1, -1, -1):
            before = ends_ref[(step + 1) % GROUPS, here, :]
            after = ends_ref[GROUPS - 1 - step, here, :]
            entering = entering * across + jnp.where(low, after, before)
        around = across
        for _ in range(2):
            around = around * around
        entering = entering / (1.0 - around)
        full_ref[0, here, :] = entering

        def carry(step, reach):
            full_ref[step + 1, here, :] = walk_ref[step, here, :] + reach
            return reach * square

        lax.fori_loop(0, STEPS, carry, entering * square, unroll=8)
    send_planes(full_ref, sent_refs, plane_ref, root_ref, gain_ref, grid_ref, level_ref)


def take_lines(own_ref, offsets, got_refs, table_ref, left_ref, lines_ref, part_rows):
    own = own_ref[0]
    pairs = list(dict.fromkeys(offset // 2 for offset in offsets))
    for offset, got_ref in zip(offsets, got_refs):
        lines_ref[2 * pairs.index(offset // 2) + ((own ^ offset) & 1)] = wide(got_ref)
    low = low_half((part_rows, LANES))
    for at in range(len(pairs)):
        for start in range(0, ROWS, part_rows):
            here = slice(start, start + part_rows)
            write_left(at, here, even_odd(lines_ref[2 * at, here, :], lines_ref[2 * at + 1, here, :], low), left_ref)
    return [(own >> 1) ^ pair for pair in pairs]


def point_parts(pair, cosines, sines, weight_ref):
    for ty in range(4):
        part = weight_ref[pair, ty] * cosines + weight_ref[pair, 4 + ty] * sines
        yield ty, part
        yield ty + 4, weight_ref[pair, 8] * part


def reply_first_kernel(own_ref, weight_ref, *refs):
    count = len(TAKE_FIRST)
    table_ref, sums_ref, lines_ref, left_ref = refs[count:]
    pairs = take_lines(own_ref, TAKE_FIRST, refs[:count], table_ref, left_ref, lines_ref, DOT_ROWS)
    for at, pair in enumerate(pairs):
        for part in range(ROWS // DOT_ROWS):
            here = slice(part * DOT_ROWS, (part + 1) * DOT_ROWS)
            cosines, sines = line_product(at, here, left_ref, table_ref[pair])
            for ty, values in point_parts(pair, cosines, sines, weight_ref):
                sums_ref[ty, here, :] = values if at == 0 else sums_ref[ty, here, :] + values


def reply_later_kernel(own_ref, weight_ref, *refs):
    count = len(TAKE_LATER)
    sums_ref, picks_ref, table_ref, out_ref, lines_ref, left_ref, pot_ref = refs[count:]
    [pair] = take_lines(own_ref, TAKE_LATER, refs[:count], table_ref, left_ref, lines_ref, DOT_ROWS)
    for part in range(ROWS // DOT_ROWS):
        here = slice(part * DOT_ROWS, (part + 1) * DOT_ROWS)
        cosines, sines = line_product(0, here, left_ref, table_ref[pair])
        for ty, values in point_parts(pair, cosines, sines, weight_ref):
            values = (sums_ref[ty, here, :] + values).astype(jnp.bfloat16)
            for one in range(DOT_ROWS // SPOTS):
                q = part * (DOT_ROWS // SPOTS) + one
                pot_ref[ty * SPOTS : (ty + 1) * SPOTS, q * LANES : (q + 1) * LANES] = values[
                    one * SPOTS : (one + 1) * SPOTS
                ]
    for q in range(0, BRICK_ROWS, 4):
        there = slice(q * LANES, (q + 4) * LANES)
        out_ref[:, there] = dot(picks_ref[...], pot_ref[:, there]).astype(jnp.bfloat16)


def unpack_kernel(back_ref, got_ref, out_ref):
    for q in range(0, BRICK_ROWS, 4):
        there = slice(q * LANES, (q + 4) * LANES)
        out_ref[:, there] = dot(back_ref[...], got_ref[:, there]).astype(jnp.bfloat16)


def call(kernel, name, operands, spaces, outs, places, scratch, vmem=VMEM_BYTES):
    return pl.pallas_call(
        kernel,
        out_shape=outs,
        in_specs=[pl.BlockSpec(memory_space=space) for space in spaces],
        out_specs=[pl.BlockSpec(memory_space=space) for space in places],
        scratch_shapes=scratch,
        compiler_params=pltpu.CompilerParams(vmem_limit_bytes=vmem),
        name=name,
    )(*operands)


def on_device_8x4(bricks, owners, tile_ids, counts):
    V, S, H = pltpu.VMEM, pltpu.SMEM, pltpu.HBM
    f32, bf16, i32, i16 = jnp.float32, jnp.bfloat16, jnp.int32, jnp.int16
    shape, dma = jax.ShapeDtypeStruct, pltpu.SemaphoreType.DMA
    brick_rows = bricks.shape[0]
    lines_in, lines_out = (jnp.asarray(each) for each in line_tables())
    weights = jnp.asarray(class_weights())
    planes_in = [jnp.asarray(plane_tables(offsets, False)) for offsets in (TAKE_FIRST, TAKE_LATER)]
    planes_out = jnp.asarray(plane_tables(SEND, True))
    base, lam = (jnp.asarray(each) for each in mode_tables())
    own = lax.axis_index("gz").astype(i32).reshape(1)
    sent_shape = shape((ROWS + HEAD_ROWS, LANES), i16)
    end_shape = shape((PLANES + HEAD_ROWS, LANES), i16)
    cube, flat, sums_shape = (STEPS, PLANES, LANES), (PLANES, LANES), (8, ROWS, LANES)
    line, rows_shape = (ROWS, LANES), (SLOTS, CELLS + LANES)

    def all_ways(values):
        return lax.all_to_all(values, ("gz", "ma"), split_axis=0, concat_axis=0, tiled=True)

    def over_slabs(offset, values):
        return lax.ppermute(values, "gz", [(g, g ^ offset) for g in range(SLABS)]) if offset else values

    def round_groups(values, step):
        return lax.ppermute(values, "ma", [(m, (m + step) % GROUPS) for m in range(GROUPS)]) if step else values

    def exchanged(sent):
        sent = dict(zip(SEND, sent))
        got = {offset: over_slabs(offset, sent[offset]) for offset in TAKE_FIRST + TAKE_LATER}
        return [got[offset] for offset in TAKE_FIRST], [got[offset] for offset in TAKE_LATER]

    outgoing, back = call(
        pack_kernel,
        "pack",
        (owners.reshape(brick_rows), tile_ids, counts, bricks),
        [H] * 4,
        [shape(rows_shape, bf16), shape((brick_rows, SLOTS), bf16)],
        [H, V],
        [
            S((brick_rows,), i32),
            S((brick_rows,), i32),
            S((1,), i32),
            V(bricks.shape, bf16),
            V((SLOTS + PAIR_SLOTS, brick_rows), f32),
            V((SLOTS + PAIR_SLOTS, LANES), f32),
            V(rows_shape, bf16),
            S((DOMAINS,), i32),
            dma((4,)),
            dma((4,)),
        ],
        ALL_VMEM_BYTES,
    )
    *sent, picks = call(
        forward_kernel,
        "forward",
        (own, all_ways(outgoing), lines_in),
        [S, V, V],
        [sent_shape] * len(SEND) + [shape((SLOTS, TILES), bf16)],
        [V] * (len(SEND) + 1),
        [
            V((TILES, SLOTS), bf16),
            V((PAIRS, 2 * ROWS, 2 * LANES), bf16),
            V((len(SEND), *line), f32),
            V((len(SEND), 8, LANES), f32),
        ],
    )
    first, later = exchanged(sent)
    (sums,) = call(
        down_first_kernel,
        "down_first",
        (own, *first, planes_in[0]),
        [S] + [V] * len(first) + [H],
        [shape(cube, f32)],
        [V],
        [V((len(first) * ROWS, LANES), f32), V(planes_in[0].shape[1:], bf16), dma((1,))],
    )
    tables = [V(base.shape, f32), V(lam.shape, f32), dma((3,))]
    walk, end = call(
        down_later_kernel,
        "down_later",
        (own, *later, sums, planes_in[1], base, lam),
        [S] + [V] * (len(later) + 1) + [H] * 3,
        [shape(cube, f32), end_shape],
        [V, V],
        [
            V((len(later) * ROWS, LANES), f32),
            V(cube, f32),
            V(flat, f32),
            V(flat, f32),
            V(planes_in[1].shape[1:], bf16),
            *tables,
        ],
    )
    ends = [round_groups(end, step) for step in range(GROUPS)]
    sent = call(
        up_kernel,
        "up",
        (own, walk, *ends, planes_out, base, lam),
        [S] + [V] * (1 + GROUPS) + [H] * 3,
        [sent_shape] * len(SEND),
        [V] * len(SEND),
        [
            V((STEPS + 1, *flat), f32),
            V(flat, f32),
            V(flat, f32),
            V((len(SEND) * ROWS, LANES), f32),
            V((8, LANES), f32),
            V((GROUPS, *flat), f32),
            V(planes_out.shape[1:], bf16),
            *tables,
        ],
    )
    first, later = exchanged(sent)
    (sums,) = call(
        reply_first_kernel,
        "reply_first",
        (own, weights, *first, lines_out),
        [S, S] + [V] * (len(first) + 1),
        [shape(sums_shape, f32)],
        [V],
        [V((len(first), *line), f32), V((len(first) // 2, 2 * ROWS, 2 * LANES), bf16)],
    )
    (replies,) = call(
        reply_later_kernel,
        "reply_later",
        (own, weights, *later, sums, picks, lines_out),
        [S, S] + [V] * (len(later) + 3),
        [shape((SLOTS, CELLS), bf16)],
        [V],
        [
            V((len(later), *line), f32),
            V((len(later) // 2, 2 * ROWS, 2 * LANES), bf16),
            V((TILES, CELLS), bf16),
        ],
    )
    (result,) = call(
        unpack_kernel,
        "unpack",
        (back, all_ways(replies)),
        [V, V],
        [shape((brick_rows, CELLS), bf16)],
        [V],
        [],
    )
    return result


def solution(mesh):
    in_specs = (P(("gz", "ma"), None), P(("gz", "ma"), None), P(("gz", "ma")), P(("gz", "ma")))
    out_specs = P(("gz", "ma"), None)
    body = on_device_8x4 if (mesh.shape["gz"], mesh.shape["ma"]) == (SLABS, GROUPS) else on_device
    return jax.shard_map(body, mesh=mesh, in_specs=in_specs, out_specs=out_specs, check_vma=False)
```

```python
import math

import jax
import jax.numpy as jnp
import ml_dtypes
import numpy as np
from jax import lax
from jax.experimental import pallas as pl
from jax.experimental.pallas import tpu as pltpu
from jax.sharding import PartitionSpec as P

NX = 512
NY = 512
SCREEN = 16
BZ = 4
BX = 8
BY = 64
CZ = 16


def hartley(length):
    indices = jnp.arange(length, dtype=jnp.int32)
    products = indices[:, None] * indices[None, :] % length
    angles = 2.0 * math.pi / length * products.astype(jnp.float32)
    return (jnp.cos(angles) + jnp.sin(angles)) / math.sqrt(length)


def second_difference(length, indices):
    return 2.0 - 2.0 * jnp.cos(2.0 * math.pi / length * indices.astype(jnp.float32))


def thomas(right_side, diagonal):
    start_zero = jnp.zeros(right_side.shape[1:], jnp.float32)

    def down(state_pair, plane):
        factor = 1.0 / (diagonal - state_pair[0])
        partial_value = (plane + state_pair[1]) * factor
        return ((factor, partial_value), (factor, partial_value))

    _, (factors, partials) = lax.scan(down, (start_zero, start_zero), right_side)

    def upward(beyond, factor_partial):
        solved = factor_partial[1] + factor_partial[0] * beyond
        return (solved, solved)

    _, solutions = lax.scan(upward, start_zero, (factors, partials), reverse=True)
    return solutions


def regroup(values):
    return lax.all_to_all(values, "ma", split_axis=2, concat_axis=1, tiled=True)


def on_device(bricks, owners, tile_ids, counts):
    domains = lax.axis_size(("gz", "ma"))
    group_count = lax.axis_size("ma")
    slab_count = lax.axis_size("gz")
    brick_rows, brick_cells = bricks.shape
    slot_count = max(2, 2 * brick_rows // domains)
    local_x = NX // group_count
    local_y = NY // group_count
    tiles_dev = CZ // BZ * (local_x // BX) * (NY // BY)
    highest = lax.Precision.HIGHEST
    target = owners[:, 0]
    row_order = jnp.arange(brick_rows, dtype=jnp.int32)
    earlier_same = (target[:, None] == target[None, :]) & (row_order[None, :] < row_order[:, None])
    within = jnp.sum(earlier_same.astype(jnp.int32), axis=1)
    slot_of = target * slot_count + within
    is_live = row_order < counts[0]
    loaded = jnp.where(is_live[:, None], bricks, jnp.zeros_like(bricks))
    outgoing = jnp.zeros((domains * slot_count, brick_cells), jnp.bfloat16).at[slot_of].set(loaded)
    out_ids = jnp.full((domains * slot_count,), tiles_dev, jnp.int32).at[slot_of].set(tile_ids)
    incoming, in_ids = (
        lax.all_to_all(outgoing, ("gz", "ma"), split_axis=0, concat_axis=0, tiled=True),
        lax.all_to_all(out_ids, ("gz", "ma"), split_axis=0, concat_axis=0, tiled=True),
    )
    picker = (jnp.arange(tiles_dev, dtype=jnp.int32)[:, None] == in_ids[None, :]).astype(
        jnp.bfloat16
    )
    deposit = jnp.dot(picker, incoming, preferred_element_type=jnp.float32)
    charge = deposit.reshape(CZ // BZ, local_x // BX, NY // BY, BZ, BX, BY)
    charge = charge.transpose(0, 3, 1, 4, 2, 5).reshape(CZ, local_x, NY)
    table_x = hartley(NX)
    table_y = hartley(NY)
    along_y = jnp.einsum("zxy,ky->zxk", charge, table_y, precision=highest)
    gathered_x = regroup(along_y)
    spectrum = jnp.einsum("zxk,jx->zjk", gathered_x, table_x, precision=highest)
    columns = lax.axis_index("ma") * local_y + jnp.arange(local_y, dtype=jnp.int32)
    lam_y = second_difference(NY, columns)
    screening = 1.0 / (SCREEN * SCREEN)
    slab_index = lax.axis_index("gz")
    lam_x = second_difference(NX, jnp.arange(NX, dtype=jnp.int32))
    diagonal = 2.0 + screening + lam_x[:, None] + lam_y[None, :]
    interior = spectrum[1:]
    particular = thomas(interior, diagonal)
    unit_rhs = jnp.zeros_like(interior).at[0].set(1.0)
    spike = thomas(unit_rhs, diagonal)
    near_weight = spike[0]
    far_weight = spike[-1]
    head_term = spectrum[0] + particular[0]
    tail_term = particular[-1]
    reduced_first = diagonal - near_weight
    reduced_rest = diagonal - 2.0 * near_weight
    start_zero = jnp.zeros_like(diagonal)
    heads, tails = (
        lax.all_gather(head_term[None], "gz", axis=0, tiled=True),
        lax.all_gather(tail_term[None], "gz", axis=0, tiled=True),
    )
    before = jnp.concatenate([start_zero[None], tails[:-1]], axis=0)
    sources = heads + before

    def chain_down(state_pair, packed):
        source, position = packed
        base_term = jnp.where(position == 0, reduced_first, reduced_rest)
        pivot_now = 1.0 / (base_term - far_weight * far_weight * state_pair[0])
        forward_part = pivot_now * (source + far_weight * state_pair[1])
        return ((pivot_now, forward_part), (pivot_now, forward_part))

    _, (pivots, forwards) = lax.scan(
        chain_down, (start_zero, start_zero), (sources, jnp.arange(slab_count, dtype=jnp.int32))
    )

    def chain_up(beyond, packed):
        plane_value = packed[1] + far_weight * packed[0] * beyond
        return (plane_value, plane_value)

    _, separators = lax.scan(chain_up, start_zero, (pivots, forwards), reverse=True)
    padded_sep = jnp.concatenate([separators, start_zero[None]], axis=0)
    own_plane = lax.dynamic_index_in_dim(padded_sep, slab_index, 0, keepdims=False)
    next_plane = lax.dynamic_index_in_dim(padded_sep, slab_index + 1, 0, keepdims=False)
    interior_sol = particular + own_plane[None] * spike + next_plane[None] * spike[::-1]
    modal = jnp.concatenate([own_plane[None], interior_sol], axis=0)
    back_x = jnp.einsum("zjk,jx->zkx", modal, table_x, precision=highest)
    gathered_y = regroup(back_x)
    potential = jnp.einsum("zkx,ky->zxy", gathered_y, table_y, precision=highest)
    pot_tiles = potential.reshape(CZ // BZ, BZ, local_x // BX, BX, NY // BY, BY)
    pot_tiles = (
        pot_tiles.transpose(0, 2, 4, 1, 3, 5).reshape(tiles_dev, brick_cells).astype(jnp.bfloat16)
    )
    padded_tiles = jnp.concatenate([pot_tiles, jnp.zeros((1, brick_cells), jnp.bfloat16)], axis=0)
    replies = padded_tiles[in_ids]
    returned = lax.all_to_all(replies, ("gz", "ma"), split_axis=0, concat_axis=0, tiled=True)
    result = returned[slot_of]
    return jnp.where(is_live[:, None], result, jnp.zeros_like(result))


DOMAINS = 32
GROUPS = 4
SLABS = 8
SEND = (4, 2, 5, 3, 0, 1, 6, 7)
TAKE_FIRST = (0, 4, 2, 5, 3, 1)
TAKE_LATER = (6, 7)
PAIR_SLOTS = 8
SLOTS = DOMAINS * PAIR_SLOTS
TILES = 512
BRICK_ROWS = 16
CELLS = 2048
LANES = 128
HALF = 64
SPOTS = 64
ROWS = BRICK_ROWS * SPOTS
DOT_ROWS = 512
PAIRS = 4
CLASSES = (0, 4, 1, 7, 2, 6, 3, 5)
HEAD_ROWS = 16
STEPS = 64
PLANES = 128
FULL = 32700.0
LOG_UNIT = 128.0
VMEM_BYTES = 24 * 1024 * 1024
ALL_VMEM_BYTES = 60 * 1024 * 1024


def split_table(table):
    high = table.astype(ml_dtypes.bfloat16)
    low = (table - high.astype(np.float64)).astype(ml_dtypes.bfloat16)
    return high, low


def line_tables():
    iy, k2 = np.arange(HALF)[:, None], np.arange(HALF)[None, :]
    tables = []
    for pair in range(PAIRS):
        table = np.zeros((LANES, LANES))
        for one in range(2):
            angle = 2.0 * np.pi / NY * (iy * (CLASSES[2 * pair + one] + 8 * k2) % NY)
            cosine, sine = np.cos(angle) / np.sqrt(NY), np.sin(angle) / np.sqrt(NY)
            there = slice(one * HALF, (one + 1) * HALF)
            if pair == 0:
                table[there, there] = cosine + sine
            else:
                table[:HALF, there] = cosine + sine
                table[HALF:, there] = (cosine - sine) * (1 - 2 * one)
        tables.append(table)

    def stacked(table):
        high, low = split_table(table)
        return np.concatenate(
            [np.concatenate([high, low], axis=1), np.concatenate([high, np.zeros_like(low)], axis=1)], axis=0
        )

    return np.stack([stacked(table) for table in tables] + [stacked(table.T) for table in tables])


def class_weights():
    pair, ty = np.arange(PAIRS)[:, None], np.arange(4)[None, :]
    cosine, sine = np.cos(np.pi / 4.0 * pair * ty), np.sin(np.pi / 4.0 * pair * ty)
    sine[0] = (-1.0) ** np.arange(4)
    sign = (-1.0) ** pair * np.ones((1, 4))
    return np.concatenate([cosine, sine, sign], axis=1).astype(np.float32)


def plane_tables(offsets, turned):
    index = np.arange(PLANES)
    table = np.sqrt(2.0 / (PLANES + 1)) * np.sin(
        np.pi / (PLANES + 1) * ((index[:, None] + 1) * (index[None, :] + 1) % (2 * PLANES + 2))
    )
    each = []
    for own in range(SLABS):
        slabs = np.array([own ^ offset for offset in offsets])
        plane, tz = np.arange(BZ)[:, None, None], np.arange(BZ)[None, :, None]
        part = table[:, (slabs * CZ + tz * BZ + plane).reshape(-1)]
        high, low = split_table(part.T if turned else part)
        if 3 * high.shape[1] <= 2 * LANES:
            each.append(np.concatenate([high, high, low], axis=1))
            continue
        top = np.concatenate([high, high], axis=1)
        bottom = np.concatenate([low, np.zeros_like(low)], axis=1)
        each.append(np.concatenate([top, bottom], axis=0))
    return np.stack(each)


def mode_tables():
    mu = 2.0 - 2.0 * np.cos(np.pi / (PLANES + 1) * (np.arange(PLANES) + 1))
    base = np.broadcast_to((mu + 1.0 / (SCREEN * SCREEN))[:, None], (PLANES, LANES))
    lam = 2.0 - 2.0 * np.cos(2.0 * np.pi / NY * np.arange(NY))
    lam = np.stack([lam[number::8] for number in CLASSES])
    return base.astype(np.float32), np.concatenate([lam, lam], axis=1).astype(np.float32)


def low_half(shape):
    return lax.broadcasted_iota(jnp.int32, shape, len(shape) - 1) < HALF


def split(values):
    high = values.astype(jnp.bfloat16)
    return high, (values - high.astype(jnp.float32)).astype(jnp.bfloat16)


def dot(left, right):
    return jnp.dot(left, right, preferred_element_type=jnp.float32)


def start_copies(pairs, sems):
    copies = [pltpu.make_async_copy(source, place, sems.at[at]) for at, (source, place) in enumerate(pairs)]
    for each in copies:
        each.start()
    return copies


def even_odd(first, second, low):
    crossed = pltpu.roll(jnp.where(low, second, first), HALF, 1)
    return jnp.where(low, first, crossed), jnp.where(low, crossed, second)


def write_left(at, here, lines, left_ref):
    for line, values in enumerate(lines):
        high, rest = split(values)
        there = slice(line * ROWS + here.start, line * ROWS + here.stop)
        left_ref[at, there, :LANES] = high
        left_ref[at, there, LANES:] = rest


def line_product(at, here, left_ref, table):
    products = []
    for line in range(2):
        there = slice(line * ROWS + here.start, line * ROWS + here.stop)
        both = dot(left_ref[at, there, :], table)
        products.append(both[:, :LANES] + both[:, LANES:])
    return even_odd(*products, low_half(products[0].shape))


def class_sums(points):
    half = [points[ty] + points[ty + 4] for ty in range(4)]
    rest = [points[ty] - points[ty + 4] for ty in range(4)]
    even, odd = half[0] + half[2], half[1] + half[3]
    turn = math.sqrt(0.5)
    across, along = turn * (rest[1] - rest[3]), turn * (rest[1] + rest[3])
    return (
        (even + odd, even - odd),
        (rest[0] + across, rest[2] + along),
        (half[0] - half[2], half[1] - half[3]),
        (rest[0] - across, along - rest[2]),
    )


def level_of(most):
    return jnp.floor(jnp.log2(jnp.maximum(most, 1e-30)) * LOG_UNIT) + 2.0


def inverse_of(level):
    return FULL * jnp.exp2(level * (-1.0 / LOG_UNIT))


def fixed_of(values):
    return jnp.floor(values + 0.5).astype(jnp.int32).astype(jnp.int16)


def head_of(level):
    return jnp.broadcast_to(level, (HEAD_ROWS, LANES)).astype(jnp.int32).astype(jnp.int16)


def unit_of(sent_ref):
    head = sent_ref[sent_ref.shape[0] - HEAD_ROWS :, :].astype(jnp.int32).astype(jnp.float32)
    return jnp.exp2(head[0:1] * (1.0 / LOG_UNIT)) * (1.0 / FULL)


def wide(sent_ref):
    block = sent_ref[: sent_ref.shape[0] - HEAD_ROWS, :]
    return block.astype(jnp.int32).astype(jnp.float32) * unit_of(sent_ref)


def pack_kernel(
    owner_in, tile_in, count_in, brick_in, out_ref, back_ref,
    owner_ref, tile_ref, count_ref, brick_ref, pick_ref, head_ref, ready_ref, used_ref, sems, out_sems,
):
    copies = start_copies(
        ((owner_in, owner_ref), (tile_in, tile_ref), (count_in, count_ref), (brick_in, brick_ref)), sems
    )
    brick_rows = brick_ref.shape[0]
    head_ref[...] = jnp.full(head_ref.shape, float(TILES), jnp.float32)
    pick_ref[...] = jnp.zeros(pick_ref.shape, jnp.float32)
    for owner in range(DOMAINS):
        used_ref[owner] = 0
    for each in copies[:3]:
        each.wait()
    count = count_ref[0]
    lane = lax.broadcasted_iota(jnp.int32, (1, brick_rows), 1)

    def place(r, _):
        owner = owner_ref[r]
        within = used_ref[owner]
        used_ref[owner] = within + 1
        slot = jnp.where(r < count, owner * PAIR_SLOTS + within, SLOTS)
        tile = tile_ref[r]
        position = (tile & 7) * SPOTS + ((tile >> 3) & 15) * 4 + (tile >> 7)
        pick_ref[pl.ds(slot, 1), :] = jnp.where(lane == r, 1.0, 0.0)
        head_ref[pl.ds(slot, 1), :] = jnp.full((1, LANES), position, jnp.int32).astype(jnp.float32)
        return 0

    lax.fori_loop(0, brick_rows, place, 0, unroll=8)
    copies[3].wait()
    copies = []
    rows = 64
    for part in range(SLOTS // rows):
        here = slice(part * rows, (part + 1) * rows)
        ready_ref[here, :CELLS] = dot(pick_ref[here, :].astype(jnp.bfloat16), brick_ref[...]).astype(jnp.bfloat16)
        head = head_ref[here, :]
        high = jnp.floor(head * (1.0 / 32.0))
        ready_ref[here, CELLS:] = jnp.where(low_half(head.shape), high, head - 32.0 * high).astype(jnp.bfloat16)
        some = pl.ds(part * rows, rows)
        copies.append(pltpu.make_async_copy(ready_ref.at[some], out_ref.at[some], out_sems.at[part]))
        copies[-1].start()
    for part in range(SLOTS // LANES):
        here = slice(part * LANES, (part + 1) * LANES)
        back_ref[:, here] = pick_ref[here, :].T.astype(jnp.bfloat16)
    for each in copies:
        each.wait()


def write_picks(brick_ref, picks_ref, across_ref):
    for part in range(SLOTS // LANES):
        here = slice(part * LANES, (part + 1) * LANES)
        head = brick_ref[here, CELLS:].astype(jnp.float32)
        turned = pltpu.roll(head, HALF, 1)
        low = low_half(head.shape)
        places = (jnp.where(low, head, turned) * 32.0 + jnp.where(low, turned, head)).astype(jnp.int32)
        for block in range(TILES // LANES):
            there = slice(block * LANES, (block + 1) * LANES)
            lane = lax.broadcasted_iota(jnp.int32, (LANES, LANES), 1) + block * LANES
            square = jnp.where(places == lane, 1.0, 0.0)
            picks_ref[here, there] = square.astype(jnp.bfloat16)
            across_ref[there, here] = square.T.astype(jnp.bfloat16)


def forward_kernel(own_ref, brick_ref, table_ref, *refs):
    sent_refs = refs[: len(SEND)]
    picks_ref, across_ref, left_ref, lines_ref, most_ref = refs[len(SEND) :]
    write_picks(brick_ref, picks_ref, across_ref)
    low = low_half((SPOTS, LANES))
    for q in range(0, BRICK_ROWS, 4):
        charge = dot(across_ref[...], brick_ref[:, q * LANES : (q + 4) * LANES])
        for one in range(4):
            there = slice(one * LANES, (one + 1) * LANES)
            here = slice((q + one) * SPOTS, (q + one + 1) * SPOTS)
            points = [charge[ty * SPOTS : (ty + 1) * SPOTS, there] for ty in range(8)]
            for pair, (cosines, sines) in enumerate(class_sums(points)):
                write_left(pair, here, even_odd(cosines, sines, low), left_ref)
    for pair in range(PAIRS):
        for part in range(ROWS // DOT_ROWS):
            here = slice(part * DOT_ROWS, (part + 1) * DOT_ROWS)
            for one, values in enumerate(line_product(pair, here, left_ref, table_ref[pair])):
                lines_ref[2 * pair + one, here, :] = values
                most = jnp.max(jnp.abs(values).reshape(DOT_ROWS // 8, 8, LANES), axis=0)
                most_ref[2 * pair + one] = most if part == 0 else jnp.maximum(most_ref[2 * pair + one], most)
    for offset, sent_ref in zip(SEND, sent_refs):
        g = own_ref[0] ^ offset
        level = level_of(jnp.max(most_ref[g], axis=0, keepdims=True))
        sent_ref[:ROWS, :] = fixed_of(lines_ref[g] * inverse_of(level))
        sent_ref[ROWS:, :] = head_of(level)


def grid_rows(slabs, plane, xq, tx):
    start = ((plane * 4 + xq) * SPOTS + tx * 4) * slabs
    return pl.ds(pl.multiple_of(start, 4 * slabs), 4 * slabs)


def plane_product(plane_ref, lines):
    high, rest = split(lines)
    rows = plane_ref.shape[0]
    if plane_ref.shape[1] == 3 * high.shape[0]:
        return dot(plane_ref[...], jnp.concatenate([high, rest, high], axis=0))
    both = dot(plane_ref[...], jnp.concatenate([high, rest], axis=0))
    return both[: rows // 2] + both[rows // 2 :]


def add_sines(got_refs, plane_ref, grid_ref, finish):
    slabs = len(got_refs)
    for at, got_ref in enumerate(got_refs):
        grid_ref[pl.ds(at, ROWS, stride=slabs), :] = wide(got_ref)

    def planes(tx, xq):
        return jnp.concatenate([grid_ref[grid_rows(slabs, plane, xq, tx), :] for plane in range(BZ)], axis=0)

    def sines(tx, _):
        for half in range(2):
            lines = jnp.concatenate([planes(tx, half * 2), planes(tx, half * 2 + 1)], axis=1)
            modes = plane_product(plane_ref, lines)
            finish(tx * 4 + half * 2, modes[:, :LANES])
            finish(tx * 4 + half * 2 + 1, modes[:, LANES:])
        return 0

    lax.fori_loop(0, 16, sines, 0, unroll=8)


def down_first_kernel(own_ref, *refs):
    count = len(TAKE_FIRST)
    (
        plane_in, base_in, lam_in, modes_ref, root_ref, gain_ref, power_ref,
        grid_ref, plane_ref, base_ref, lam_ref, sems,
    ) = refs[count:]
    copies = start_copies(((plane_in.at[own_ref[0]], plane_ref), (base_in, base_ref), (lam_in, lam_ref)), sems)
    for each in copies:
        each.wait()
    excess = base_ref[...] + lam_ref[pl.ds(own_ref[0], 1), :]
    spread = jnp.sqrt(excess * (excess + 4.0))
    root_ref[...] = 2.0 / (2.0 + excess + spread)
    gain_ref[...] = 1.0 / spread
    for part in range(2):
        here = pl.ds(part * PLANES // 2, PLANES // 2)
        square = root_ref[here, :] * root_ref[here, :]

        def raised(step, power):
            power_ref[step, here, :] = power
            return power * square

        lax.fori_loop(0, STEPS, raised, jnp.ones(square.shape, jnp.float32), unroll=8)

    def finish(line, values):
        modes_ref[line] = values

    add_sines(refs[:count], plane_ref, grid_ref, finish)


def down_later_kernel(own_ref, *refs):
    count = len(TAKE_LATER)
    (
        sums_ref, root_ref, plane_in, walk_ref, end_ref, grid_ref, modes_ref, last_ref, plane_ref, sems,
    ) = refs[count:]
    [copy] = start_copies(((plane_in.at[own_ref[0]], plane_ref),), sems)
    copy.wait()

    def finish(line, values):
        modes_ref[line] = sums_ref[line] + values

    add_sines(refs[:count], plane_ref, grid_ref, finish)
    part_rows = 64
    low = low_half((part_rows, LANES))
    for part in range(PLANES // part_rows):
        here = pl.ds(part * part_rows, part_rows)
        root = root_ref[here, :]
        square = root * root

        def walk(step, held):
            ahead, behind = modes_ref[step, here, :], modes_ref[STEPS - 1 - step, here, :]
            own = jnp.where(low, behind, ahead)
            other = pltpu.roll(jnp.where(low, ahead, behind), HALF, 1)
            held = square * held + (own + root * other)
            walk_ref[step, here, :] = held
            return held

        last_ref[here, :] = lax.fori_loop(0, STEPS, walk, jnp.zeros((part_rows, LANES), jnp.float32), unroll=8)
    last = last_ref[...]
    level = level_of(jnp.max(jnp.abs(last), axis=0, keepdims=True))
    end_ref[:PLANES, :] = fixed_of(last * inverse_of(level))
    end_ref[PLANES:, :] = head_of(level)


def local_kernel(walk_ref, root_ref, gain_ref, local_ref):
    part_rows = 64
    low = low_half((part_rows, LANES))
    for part in range(PLANES // part_rows):
        here = pl.ds(part * part_rows, part_rows)
        root, gain = root_ref[here, :], gain_ref[here, :]
        zero = jnp.zeros(root.shape, jnp.float32)

        def line(step, ahead_before, behind_after):
            near = jnp.where(low, walk_ref[STEPS - 1 - step, here, :], walk_ref[step, here, :])
            far = pltpu.roll(jnp.where(low, behind_after, ahead_before), HALF, 1)
            local_ref[step, here, :] = gain * (near + root * far)

        def inner(step, _):
            line(step, walk_ref[step - 1, here, :], walk_ref[STEPS - 2 - step, here, :])
            return 0

        line(0, zero, walk_ref[STEPS - 2, here, :])
        lax.fori_loop(1, STEPS - 1, inner, 0, unroll=6)
        line(STEPS - 1, walk_ref[STEPS - 2, here, :], zero)


def up_kernel(own_ref, local_ref, power_ref, root_ref, gain_ref, *refs):
    end_refs, plane_in = refs[:GROUPS], refs[GROUPS]
    count = GROUPS + 1 + len(SEND)
    sent_refs = refs[GROUPS + 1 : count]
    rise_ref, fall_ref, grid_ref, level_ref, plane_ref, sems = refs[count:]
    [copy] = start_copies(((plane_in.at[own_ref[0]], plane_ref),), sems)
    low = low_half((PLANES, LANES))
    root = root_ref[...]
    square = root * root
    across = square
    for _ in range(6):
        across = across * across
    around = across
    for _ in range(2):
        around = around * around
    ends = [wide(end_ref) for end_ref in end_refs]
    entering = jnp.zeros((PLANES, LANES), jnp.float32)
    for step in range(GROUPS - 1, -1, -1):
        entering = entering * across + jnp.where(low, ends[GROUPS - 1 - step], ends[(step + 1) % GROUPS])
    entering = gain_ref[...] * entering / (1.0 - around)
    straight, turned = square * entering, root * pltpu.roll(entering, HALF, 1)
    rise_ref[...] = jnp.where(low, turned, straight)
    fall_ref[...] = jnp.where(low, straight, turned)
    copy.wait()
    slabs = len(sent_refs)

    def solved(step):
        reach = rise_ref[...] * power_ref[step] + fall_ref[...] * power_ref[STEPS - 1 - step]
        return local_ref[step] + reach

    def sines(tx, most):
        for half in range(2):
            first = tx * 4 + half * 2
            lines = plane_product(plane_ref, jnp.concatenate([solved(first), solved(first + 1)], axis=1))
            for one in range(2):
                part = lines[:, one * LANES : (one + 1) * LANES]
                most = jnp.maximum(most, jnp.max(jnp.abs(part).reshape(4 * BZ, slabs, LANES), axis=0))
                for plane in range(BZ):
                    grid_ref[grid_rows(slabs, plane, half * 2 + one, tx), :] = part[
                        plane * 4 * slabs : (plane + 1) * 4 * slabs
                    ]
        return most

    most = lax.fori_loop(0, 16, sines, jnp.zeros((slabs, LANES), jnp.float32), unroll=8)
    level_ref[...] = level_of(most)
    for at, sent_ref in enumerate(sent_refs):
        level = level_ref[at : at + 1, :]
        sent_ref[:ROWS, :] = fixed_of(grid_ref[pl.ds(at, ROWS, stride=slabs), :] * inverse_of(level))
        sent_ref[ROWS:, :] = head_of(level)


def take_lines(own_ref, offsets, got_refs, left_ref, lines_ref):
    own = own_ref[0]
    pairs = list(dict.fromkeys(offset // 2 for offset in offsets))
    for offset, got_ref in zip(offsets, got_refs):
        lines_ref[2 * pairs.index(offset // 2) + ((own ^ offset) & 1)] = wide(got_ref)
    low = low_half((DOT_ROWS, LANES))
    for at in range(len(pairs)):
        for start in range(0, ROWS, DOT_ROWS):
            here = slice(start, start + DOT_ROWS)
            write_left(at, here, even_odd(lines_ref[2 * at, here, :], lines_ref[2 * at + 1, here, :], low), left_ref)
    return [(own >> 1) ^ pair for pair in pairs]


def point_parts(pair, cosines, sines, weight_ref):
    for ty in range(4):
        part = weight_ref[pair, ty] * cosines + weight_ref[pair, 4 + ty] * sines
        yield ty, part
        yield ty + 4, weight_ref[pair, 8] * part


def reply_first_kernel(own_ref, weight_ref, *refs):
    count = len(TAKE_FIRST)
    table_ref, sums_ref, lines_ref, left_ref = refs[count:]
    pairs = take_lines(own_ref, TAKE_FIRST, refs[:count], left_ref, lines_ref)
    for at, pair in enumerate(pairs):
        for part in range(ROWS // DOT_ROWS):
            here = slice(part * DOT_ROWS, (part + 1) * DOT_ROWS)
            cosines, sines = line_product(at, here, left_ref, table_ref[PAIRS + pair])
            for ty, values in point_parts(pair, cosines, sines, weight_ref):
                sums_ref[ty, here, :] = values if at == 0 else sums_ref[ty, here, :] + values


def reply_later_kernel(own_ref, weight_ref, *refs):
    count = len(TAKE_LATER)
    sums_ref, picks_ref, table_ref, out_ref, lines_ref, left_ref, pot_ref = refs[count:]
    [pair] = take_lines(own_ref, TAKE_LATER, refs[:count], left_ref, lines_ref)
    for part in range(ROWS // DOT_ROWS):
        here = slice(part * DOT_ROWS, (part + 1) * DOT_ROWS)
        cosines, sines = line_product(0, here, left_ref, table_ref[PAIRS + pair])
        for ty, values in point_parts(pair, cosines, sines, weight_ref):
            values = (sums_ref[ty, here, :] + values).astype(jnp.bfloat16)
            for one in range(DOT_ROWS // SPOTS):
                q = part * (DOT_ROWS // SPOTS) + one
                pot_ref[ty * SPOTS : (ty + 1) * SPOTS, q * LANES : (q + 1) * LANES] = values[
                    one * SPOTS : (one + 1) * SPOTS
                ]
    for q in range(0, BRICK_ROWS, 4):
        there = slice(q * LANES, (q + 4) * LANES)
        out_ref[:, there] = dot(picks_ref[...], pot_ref[:, there]).astype(jnp.bfloat16)


def unpack_kernel(back_ref, got_ref, out_ref):
    for q in range(0, BRICK_ROWS, 4):
        there = slice(q * LANES, (q + 4) * LANES)
        out_ref[:, there] = dot(back_ref[...], got_ref[:, there]).astype(jnp.bfloat16)


def call(kernel, name, operands, spaces, outs, places, scratch, vmem=VMEM_BYTES):
    return pl.pallas_call(
        kernel,
        out_shape=outs,
        in_specs=[pl.BlockSpec(memory_space=space) for space in spaces],
        out_specs=[pl.BlockSpec(memory_space=space) for space in places],
        scratch_shapes=scratch,
        compiler_params=pltpu.CompilerParams(vmem_limit_bytes=vmem),
        name=name,
    )(*operands)


def on_device_8x4(bricks, owners, tile_ids, counts):
    V, S, H = pltpu.VMEM, pltpu.SMEM, pltpu.HBM
    f32, bf16, i32, i16 = jnp.float32, jnp.bfloat16, jnp.int32, jnp.int16
    shape, dma = jax.ShapeDtypeStruct, pltpu.SemaphoreType.DMA
    brick_rows = bricks.shape[0]
    lines = jnp.asarray(line_tables())
    weights = jnp.asarray(class_weights())
    planes_in = [jnp.asarray(plane_tables(offsets, False)) for offsets in (TAKE_FIRST, TAKE_LATER)]
    planes_out = jnp.asarray(plane_tables(SEND, True))
    base, lam = (jnp.asarray(each) for each in mode_tables())
    own = lax.axis_index("gz").astype(i32).reshape(1)
    sent_shape = shape((ROWS + HEAD_ROWS, LANES), i16)
    end_shape = shape((PLANES + HEAD_ROWS, LANES), i16)
    cube, flat, sums_shape = (STEPS, PLANES, LANES), (PLANES, LANES), (8, ROWS, LANES)
    line, rows_shape = (ROWS, LANES), (SLOTS, CELLS + LANES)

    def all_ways(values):
        return lax.all_to_all(values, ("gz", "ma"), split_axis=0, concat_axis=0, tiled=True)

    def over_slabs(offset, values):
        return lax.ppermute(values, "gz", [(g, g ^ offset) for g in range(SLABS)]) if offset else values

    def round_groups(values, step):
        return lax.ppermute(values, "ma", [(m, (m + step) % GROUPS) for m in range(GROUPS)]) if step else values

    def exchanged(sent):
        sent = dict(zip(SEND, sent))
        got = {offset: over_slabs(offset, sent[offset]) for offset in TAKE_FIRST + TAKE_LATER}
        return [got[offset] for offset in TAKE_FIRST], [got[offset] for offset in TAKE_LATER]

    outgoing, back = call(
        pack_kernel,
        "pack",
        (owners.reshape(brick_rows), tile_ids, counts, bricks),
        [H] * 4,
        [shape(rows_shape, bf16), shape((brick_rows, SLOTS), bf16)],
        [H, V],
        [
            S((brick_rows,), i32),
            S((brick_rows,), i32),
            S((1,), i32),
            V(bricks.shape, bf16),
            V((SLOTS + PAIR_SLOTS, brick_rows), f32),
            V((SLOTS + PAIR_SLOTS, LANES), f32),
            V(rows_shape, bf16),
            S((DOMAINS,), i32),
            dma((4,)),
            dma((4,)),
        ],
        ALL_VMEM_BYTES,
    )
    *sent, picks = call(
        forward_kernel,
        "forward",
        (own, all_ways(outgoing), lines),
        [S, V, V],
        [sent_shape] * len(SEND) + [shape((SLOTS, TILES), bf16)],
        [V] * (len(SEND) + 1),
        [
            V((TILES, SLOTS), bf16),
            V((PAIRS, 2 * ROWS, 2 * LANES), bf16),
            V((len(SEND), *line), f32),
            V((len(SEND), 8, LANES), f32),
        ],
    )
    first, later = exchanged(sent)
    sums, root, gain, power = call(
        down_first_kernel,
        "down_first",
        (own, *first, planes_in[0], base, lam),
        [S] + [V] * len(first) + [H] * 3,
        [shape(cube, f32), shape(flat, f32), shape(flat, f32), shape(cube, f32)],
        [V] * 4,
        [
            V((len(first) * ROWS, LANES), f32),
            V(planes_in[0].shape[1:], bf16),
            V(base.shape, f32),
            V(lam.shape, f32),
            dma((3,)),
        ],
    )
    walk, end = call(
        down_later_kernel,
        "down_later",
        (own, *later, sums, root, planes_in[1]),
        [S] + [V] * (len(later) + 2) + [H],
        [shape(cube, f32), end_shape],
        [V, V],
        [
            V((len(later) * ROWS, LANES), f32),
            V(cube, f32),
            V(flat, f32),
            V(planes_in[1].shape[1:], bf16),
            dma((1,)),
        ],
    )
    ends = [round_groups(end, step) for step in range(GROUPS)]
    (local,) = call(local_kernel, "local", (walk, root, gain), [V] * 3, [shape(cube, f32)], [V], [])
    sent = call(
        up_kernel,
        "up",
        (own, local, power, root, gain, *ends, planes_out),
        [S] + [V] * (4 + GROUPS) + [H],
        [sent_shape] * len(SEND),
        [V] * len(SEND),
        [
            V(flat, f32),
            V(flat, f32),
            V((len(SEND) * ROWS, LANES), f32),
            V((len(SEND), LANES), f32),
            V(planes_out.shape[1:], bf16),
            dma((1,)),
        ],
    )
    first, later = exchanged(sent)
    (sums,) = call(
        reply_first_kernel,
        "reply_first",
        (own, weights, *first, lines),
        [S, S] + [V] * (len(first) + 1),
        [shape(sums_shape, f32)],
        [V],
        [V((len(first), *line), f32), V((len(first) // 2, 2 * ROWS, 2 * LANES), bf16)],
    )
    (replies,) = call(
        reply_later_kernel,
        "reply_later",
        (own, weights, *later, sums, picks, lines),
        [S, S] + [V] * (len(later) + 3),
        [shape((SLOTS, CELLS), bf16)],
        [V],
        [
            V((len(later), *line), f32),
            V((len(later) // 2, 2 * ROWS, 2 * LANES), bf16),
            V((TILES, CELLS), bf16),
        ],
    )
    (result,) = call(
        unpack_kernel,
        "unpack",
        (back, all_ways(replies)),
        [V, V],
        [shape((brick_rows, CELLS), bf16)],
        [V],
        [],
    )
    return result


def solution(mesh):
    in_specs = (P(("gz", "ma"), None), P(("gz", "ma"), None), P(("gz", "ma")), P(("gz", "ma")))
    out_specs = P(("gz", "ma"), None)
    body = on_device_8x4 if (mesh.shape["gz"], mesh.shape["ma"]) == (SLABS, GROUPS) else on_device
    return jax.shard_map(body, mesh=mesh, in_specs=in_specs, out_specs=out_specs, check_vma=False)
```

```python
import math

import jax
import jax.numpy as jnp
import ml_dtypes
import numpy as np
from jax import lax
from jax.experimental import pallas as pl
from jax.experimental.pallas import tpu as pltpu
from jax.sharding import PartitionSpec as P

NX = 512
NY = 512
SCREEN = 16
BZ = 4
BX = 8
BY = 64
CZ = 16


def hartley(length):
    indices = jnp.arange(length, dtype=jnp.int32)
    products = indices[:, None] * indices[None, :] % length
    angles = 2.0 * math.pi / length * products.astype(jnp.float32)
    return (jnp.cos(angles) + jnp.sin(angles)) / math.sqrt(length)


def second_difference(length, indices):
    return 2.0 - 2.0 * jnp.cos(2.0 * math.pi / length * indices.astype(jnp.float32))


def thomas(right_side, diagonal):
    start_zero = jnp.zeros(right_side.shape[1:], jnp.float32)

    def down(state_pair, plane):
        factor = 1.0 / (diagonal - state_pair[0])
        partial_value = (plane + state_pair[1]) * factor
        return ((factor, partial_value), (factor, partial_value))

    _, (factors, partials) = lax.scan(down, (start_zero, start_zero), right_side)

    def upward(beyond, factor_partial):
        solved = factor_partial[1] + factor_partial[0] * beyond
        return (solved, solved)

    _, solutions = lax.scan(upward, start_zero, (factors, partials), reverse=True)
    return solutions


def regroup(values):
    return lax.all_to_all(values, "ma", split_axis=2, concat_axis=1, tiled=True)


def on_device(bricks, owners, tile_ids, counts):
    domains = lax.axis_size(("gz", "ma"))
    group_count = lax.axis_size("ma")
    slab_count = lax.axis_size("gz")
    brick_rows, brick_cells = bricks.shape
    slot_count = max(2, 2 * brick_rows // domains)
    local_x = NX // group_count
    local_y = NY // group_count
    tiles_dev = CZ // BZ * (local_x // BX) * (NY // BY)
    highest = lax.Precision.HIGHEST
    target = owners[:, 0]
    row_order = jnp.arange(brick_rows, dtype=jnp.int32)
    earlier_same = (target[:, None] == target[None, :]) & (row_order[None, :] < row_order[:, None])
    within = jnp.sum(earlier_same.astype(jnp.int32), axis=1)
    slot_of = target * slot_count + within
    is_live = row_order < counts[0]
    loaded = jnp.where(is_live[:, None], bricks, jnp.zeros_like(bricks))
    outgoing = jnp.zeros((domains * slot_count, brick_cells), jnp.bfloat16).at[slot_of].set(loaded)
    out_ids = jnp.full((domains * slot_count,), tiles_dev, jnp.int32).at[slot_of].set(tile_ids)
    incoming, in_ids = (
        lax.all_to_all(outgoing, ("gz", "ma"), split_axis=0, concat_axis=0, tiled=True),
        lax.all_to_all(out_ids, ("gz", "ma"), split_axis=0, concat_axis=0, tiled=True),
    )
    picker = (jnp.arange(tiles_dev, dtype=jnp.int32)[:, None] == in_ids[None, :]).astype(
        jnp.bfloat16
    )
    deposit = jnp.dot(picker, incoming, preferred_element_type=jnp.float32)
    charge = deposit.reshape(CZ // BZ, local_x // BX, NY // BY, BZ, BX, BY)
    charge = charge.transpose(0, 3, 1, 4, 2, 5).reshape(CZ, local_x, NY)
    table_x = hartley(NX)
    table_y = hartley(NY)
    along_y = jnp.einsum("zxy,ky->zxk", charge, table_y, precision=highest)
    gathered_x = regroup(along_y)
    spectrum = jnp.einsum("zxk,jx->zjk", gathered_x, table_x, precision=highest)
    columns = lax.axis_index("ma") * local_y + jnp.arange(local_y, dtype=jnp.int32)
    lam_y = second_difference(NY, columns)
    screening = 1.0 / (SCREEN * SCREEN)
    slab_index = lax.axis_index("gz")
    lam_x = second_difference(NX, jnp.arange(NX, dtype=jnp.int32))
    diagonal = 2.0 + screening + lam_x[:, None] + lam_y[None, :]
    interior = spectrum[1:]
    particular = thomas(interior, diagonal)
    unit_rhs = jnp.zeros_like(interior).at[0].set(1.0)
    spike = thomas(unit_rhs, diagonal)
    near_weight = spike[0]
    far_weight = spike[-1]
    head_term = spectrum[0] + particular[0]
    tail_term = particular[-1]
    reduced_first = diagonal - near_weight
    reduced_rest = diagonal - 2.0 * near_weight
    start_zero = jnp.zeros_like(diagonal)
    heads, tails = (
        lax.all_gather(head_term[None], "gz", axis=0, tiled=True),
        lax.all_gather(tail_term[None], "gz", axis=0, tiled=True),
    )
    before = jnp.concatenate([start_zero[None], tails[:-1]], axis=0)
    sources = heads + before

    def chain_down(state_pair, packed):
        source, position = packed
        base_term = jnp.where(position == 0, reduced_first, reduced_rest)
        pivot_now = 1.0 / (base_term - far_weight * far_weight * state_pair[0])
        forward_part = pivot_now * (source + far_weight * state_pair[1])
        return ((pivot_now, forward_part), (pivot_now, forward_part))

    _, (pivots, forwards) = lax.scan(
        chain_down, (start_zero, start_zero), (sources, jnp.arange(slab_count, dtype=jnp.int32))
    )

    def chain_up(beyond, packed):
        plane_value = packed[1] + far_weight * packed[0] * beyond
        return (plane_value, plane_value)

    _, separators = lax.scan(chain_up, start_zero, (pivots, forwards), reverse=True)
    padded_sep = jnp.concatenate([separators, start_zero[None]], axis=0)
    own_plane = lax.dynamic_index_in_dim(padded_sep, slab_index, 0, keepdims=False)
    next_plane = lax.dynamic_index_in_dim(padded_sep, slab_index + 1, 0, keepdims=False)
    interior_sol = particular + own_plane[None] * spike + next_plane[None] * spike[::-1]
    modal = jnp.concatenate([own_plane[None], interior_sol], axis=0)
    back_x = jnp.einsum("zjk,jx->zkx", modal, table_x, precision=highest)
    gathered_y = regroup(back_x)
    potential = jnp.einsum("zkx,ky->zxy", gathered_y, table_y, precision=highest)
    pot_tiles = potential.reshape(CZ // BZ, BZ, local_x // BX, BX, NY // BY, BY)
    pot_tiles = (
        pot_tiles.transpose(0, 2, 4, 1, 3, 5).reshape(tiles_dev, brick_cells).astype(jnp.bfloat16)
    )
    padded_tiles = jnp.concatenate([pot_tiles, jnp.zeros((1, brick_cells), jnp.bfloat16)], axis=0)
    replies = padded_tiles[in_ids]
    returned = lax.all_to_all(replies, ("gz", "ma"), split_axis=0, concat_axis=0, tiled=True)
    result = returned[slot_of]
    return jnp.where(is_live[:, None], result, jnp.zeros_like(result))


DOMAINS = 32
GROUPS = 4
SLABS = 8
SEND = (4, 2, 5, 3, 0, 1, 6, 7)
TAKE_FIRST = (0, 4, 2, 5, 3, 1)
TAKE_LATER = (6, 7)
PAIR_SLOTS = 8
SLOTS = DOMAINS * PAIR_SLOTS
TILES = 512
BRICK_ROWS = 16
CELLS = 2048
LANES = 128
HALF = 64
SPOTS = 64
ROWS = BRICK_ROWS * SPOTS
DOT_ROWS = 512
PAIRS = 4
CLASSES = (0, 4, 1, 7, 2, 6, 3, 5)
HEAD_ROWS = 16
STEPS = 64
PLANES = 128
FULL = 32700.0
LOG_UNIT = 128.0
VMEM_BYTES = 24 * 1024 * 1024
ALL_VMEM_BYTES = 60 * 1024 * 1024


def split_table(table):
    high = table.astype(ml_dtypes.bfloat16)
    low = (table - high.astype(np.float64)).astype(ml_dtypes.bfloat16)
    return high, low


def line_tables():
    iy, k2 = np.arange(HALF)[:, None], np.arange(HALF)[None, :]
    tables = []
    for pair in range(PAIRS):
        table = np.zeros((LANES, LANES))
        for one in range(2):
            angle = 2.0 * np.pi / NY * (iy * (CLASSES[2 * pair + one] + 8 * k2) % NY)
            cosine, sine = np.cos(angle) / np.sqrt(NY), np.sin(angle) / np.sqrt(NY)
            there = slice(one * HALF, (one + 1) * HALF)
            if pair == 0:
                table[there, there] = cosine + sine
            else:
                table[:HALF, there] = cosine + sine
                table[HALF:, there] = (cosine - sine) * (1 - 2 * one)
        tables.append(table)

    def stacked(table):
        high, low = split_table(table)
        return np.concatenate(
            [np.concatenate([high, low], axis=1), np.concatenate([high, np.zeros_like(low)], axis=1)], axis=0
        )

    return np.stack([stacked(table) for table in tables] + [stacked(table.T) for table in tables])


def class_weights():
    pair, ty = np.arange(PAIRS)[:, None], np.arange(4)[None, :]
    cosine, sine = np.cos(np.pi / 4.0 * pair * ty), np.sin(np.pi / 4.0 * pair * ty)
    sine[0] = (-1.0) ** np.arange(4)
    sign = (-1.0) ** pair * np.ones((1, 4))
    return np.concatenate([cosine, sine, sign], axis=1).astype(np.float32)


def plane_tables(offsets, turned):
    index = np.arange(PLANES)
    table = np.sqrt(2.0 / (PLANES + 1)) * np.sin(
        np.pi / (PLANES + 1) * ((index[:, None] + 1) * (index[None, :] + 1) % (2 * PLANES + 2))
    )
    each = []
    for own in range(SLABS):
        slabs = np.array([own ^ offset for offset in offsets])
        plane, tz = np.arange(BZ)[:, None, None], np.arange(BZ)[None, :, None]
        part = table[:, (slabs * CZ + tz * BZ + plane).reshape(-1)]
        high, low = split_table(part.T if turned else part)
        if 3 * high.shape[1] <= 2 * LANES:
            each.append(np.concatenate([high, high, low], axis=1))
            continue
        top = np.concatenate([high, high], axis=1)
        bottom = np.concatenate([low, np.zeros_like(low)], axis=1)
        each.append(np.concatenate([top, bottom], axis=0))
    return np.stack(each)


def mode_tables():
    mu = 2.0 - 2.0 * np.cos(np.pi / (PLANES + 1) * (np.arange(PLANES) + 1))
    base = np.broadcast_to((mu + 1.0 / (SCREEN * SCREEN))[:, None], (PLANES, LANES))
    lam = 2.0 - 2.0 * np.cos(2.0 * np.pi / NY * np.arange(NY))
    lam = np.stack([lam[number::8] for number in CLASSES])
    return base.astype(np.float32), np.concatenate([lam, lam], axis=1).astype(np.float32)


def low_half(shape):
    return lax.broadcasted_iota(jnp.int32, shape, len(shape) - 1) < HALF


def split(values):
    high = values.astype(jnp.bfloat16)
    return high, (values - high.astype(jnp.float32)).astype(jnp.bfloat16)


def dot(left, right):
    return jnp.dot(left, right, preferred_element_type=jnp.float32)


def start_copies(pairs, sems):
    copies = [pltpu.make_async_copy(source, place, sems.at[at]) for at, (source, place) in enumerate(pairs)]
    for each in copies:
        each.start()
    return copies


def even_odd(first, second, low):
    crossed = pltpu.roll(jnp.where(low, second, first), HALF, 1)
    return jnp.where(low, first, crossed), jnp.where(low, crossed, second)


def write_left(at, here, lines, left_ref):
    for line, values in enumerate(lines):
        high, rest = split(values)
        there = slice(line * ROWS + here.start, line * ROWS + here.stop)
        left_ref[at, there, :LANES] = high
        left_ref[at, there, LANES:] = rest


def line_product(at, here, left_ref, table):
    products = []
    for line in range(2):
        there = slice(line * ROWS + here.start, line * ROWS + here.stop)
        both = dot(left_ref[at, there, :], table)
        products.append(both[:, :LANES] + both[:, LANES:])
    return even_odd(*products, low_half(products[0].shape))


def class_sums(points):
    half = [points[ty] + points[ty + 4] for ty in range(4)]
    rest = [points[ty] - points[ty + 4] for ty in range(4)]
    even, odd = half[0] + half[2], half[1] + half[3]
    turn = math.sqrt(0.5)
    across, along = turn * (rest[1] - rest[3]), turn * (rest[1] + rest[3])
    return (
        (even + odd, even - odd),
        (rest[0] + across, rest[2] + along),
        (half[0] - half[2], half[1] - half[3]),
        (rest[0] - across, along - rest[2]),
    )


def level_of(most):
    return jnp.floor(jnp.log2(jnp.maximum(most, 1e-30)) * LOG_UNIT) + 2.0


def inverse_of(level):
    return FULL * jnp.exp2(level * (-1.0 / LOG_UNIT))


def fixed_of(values):
    return jnp.floor(values + 0.5).astype(jnp.int32).astype(jnp.int16)


def head_of(level):
    return jnp.broadcast_to(level, (HEAD_ROWS, LANES)).astype(jnp.int32).astype(jnp.int16)


def unit_of(sent_ref):
    head = sent_ref[sent_ref.shape[0] - HEAD_ROWS :, :].astype(jnp.int32).astype(jnp.float32)
    return jnp.exp2(head[0:1] * (1.0 / LOG_UNIT)) * (1.0 / FULL)


def wide(sent_ref):
    block = sent_ref[: sent_ref.shape[0] - HEAD_ROWS, :]
    return block.astype(jnp.int32).astype(jnp.float32) * unit_of(sent_ref)


def pack_kernel(
    owner_in, tile_in, count_in, brick_in, out_ref, back_ref,
    owner_ref, tile_ref, count_ref, brick_ref, pick_ref, head_ref, ready_ref, used_ref, sems, out_sems,
):
    copies = start_copies(
        ((owner_in, owner_ref), (tile_in, tile_ref), (count_in, count_ref), (brick_in, brick_ref)), sems
    )
    brick_rows = brick_ref.shape[0]
    head_ref[...] = jnp.full(head_ref.shape, float(TILES), jnp.float32)
    pick_ref[...] = jnp.zeros(pick_ref.shape, jnp.float32)
    for owner in range(DOMAINS):
        used_ref[owner] = 0
    for each in copies[:3]:
        each.wait()
    count = count_ref[0]
    lane = lax.broadcasted_iota(jnp.int32, (1, brick_rows), 1)

    def place(r, _):
        owner = owner_ref[r]
        within = used_ref[owner]
        used_ref[owner] = within + 1
        slot = jnp.where(r < count, owner * PAIR_SLOTS + within, SLOTS)
        tile = tile_ref[r]
        position = (tile & 7) * SPOTS + ((tile >> 3) & 15) * 4 + (tile >> 7)
        pick_ref[pl.ds(slot, 1), :] = jnp.where(lane == r, 1.0, 0.0)
        head_ref[pl.ds(slot, 1), :] = jnp.full((1, LANES), position, jnp.int32).astype(jnp.float32)
        return 0

    lax.fori_loop(0, brick_rows, place, 0, unroll=8)
    copies[3].wait()
    copies = []
    rows = 64
    for part in range(SLOTS // rows):
        here = slice(part * rows, (part + 1) * rows)
        ready_ref[here, :CELLS] = dot(pick_ref[here, :].astype(jnp.bfloat16), brick_ref[...]).astype(jnp.bfloat16)
        head = head_ref[here, :]
        high = jnp.floor(head * (1.0 / 32.0))
        ready_ref[here, CELLS:] = jnp.where(low_half(head.shape), high, head - 32.0 * high).astype(jnp.bfloat16)
        some = pl.ds(part * rows, rows)
        copies.append(pltpu.make_async_copy(ready_ref.at[some], out_ref.at[some], out_sems.at[part]))
        copies[-1].start()
    for part in range(SLOTS // LANES):
        here = slice(part * LANES, (part + 1) * LANES)
        back_ref[:, here] = pick_ref[here, :].T.astype(jnp.bfloat16)
    for each in copies:
        each.wait()


def write_picks(brick_ref, picks_ref, across_ref):
    for part in range(SLOTS // LANES):
        here = slice(part * LANES, (part + 1) * LANES)
        head = brick_ref[here, CELLS:].astype(jnp.float32)
        turned = pltpu.roll(head, HALF, 1)
        low = low_half(head.shape)
        places = (jnp.where(low, head, turned) * 32.0 + jnp.where(low, turned, head)).astype(jnp.int32)
        for block in range(TILES // LANES):
            there = slice(block * LANES, (block + 1) * LANES)
            lane = lax.broadcasted_iota(jnp.int32, (LANES, LANES), 1) + block * LANES
            square = jnp.where(places == lane, 1.0, 0.0)
            picks_ref[here, there] = square.astype(jnp.bfloat16)
            across_ref[there, here] = square.T.astype(jnp.bfloat16)


def forward_kernel(own_ref, brick_ref, table_in, *refs):
    sent_refs = refs[: len(SEND)]
    picks_ref, across_ref, left_ref, lines_ref, most_ref, table_ref, sems = refs[len(SEND) :]
    [copy] = start_copies(((table_in.at[pl.ds(0, PAIRS)], table_ref),), sems)
    write_picks(brick_ref, picks_ref, across_ref)
    low = low_half((SPOTS, LANES))
    for q in range(0, BRICK_ROWS, 4):
        charge = dot(across_ref[...], brick_ref[:, q * LANES : (q + 4) * LANES])
        for one in range(4):
            there = slice(one * LANES, (one + 1) * LANES)
            here = slice((q + one) * SPOTS, (q + one + 1) * SPOTS)
            points = [charge[ty * SPOTS : (ty + 1) * SPOTS, there] for ty in range(8)]
            for pair, (cosines, sines) in enumerate(class_sums(points)):
                write_left(pair, here, even_odd(cosines, sines, low), left_ref)
    copy.wait()
    for pair in range(PAIRS):
        for part in range(ROWS // DOT_ROWS):
            here = slice(part * DOT_ROWS, (part + 1) * DOT_ROWS)
            for one, values in enumerate(line_product(pair, here, left_ref, table_ref[pair])):
                lines_ref[2 * pair + one, here, :] = values
                most = jnp.max(jnp.abs(values).reshape(DOT_ROWS // 8, 8, LANES), axis=0)
                most_ref[2 * pair + one] = most if part == 0 else jnp.maximum(most_ref[2 * pair + one], most)
    for offset, sent_ref in zip(SEND, sent_refs):
        g = own_ref[0] ^ offset
        level = level_of(jnp.max(most_ref[g], axis=0, keepdims=True))
        sent_ref[:ROWS, :] = fixed_of(lines_ref[g] * inverse_of(level))
        sent_ref[ROWS:, :] = head_of(level)


def grid_rows(slabs, plane, xq, tx):
    start = ((plane * 4 + xq) * SPOTS + tx * 4) * slabs
    return pl.ds(pl.multiple_of(start, 4 * slabs), 4 * slabs)


def plane_product(plane_ref, lines):
    high, rest = split(lines)
    rows = plane_ref.shape[0]
    if plane_ref.shape[1] == 3 * high.shape[0]:
        return dot(plane_ref[...], jnp.concatenate([high, rest, high], axis=0))
    both = dot(plane_ref[...], jnp.concatenate([high, rest], axis=0))
    return both[: rows // 2] + both[rows // 2 :]


def add_sines(got_refs, plane_ref, grid_ref, finish):
    slabs = len(got_refs)
    for at, got_ref in enumerate(got_refs):
        grid_ref[pl.ds(at, ROWS, stride=slabs), :] = wide(got_ref)

    def planes(tx, xq):
        return jnp.concatenate([grid_ref[grid_rows(slabs, plane, xq, tx), :] for plane in range(BZ)], axis=0)

    def sines(tx, _):
        for half in range(2):
            lines = jnp.concatenate([planes(tx, half * 2), planes(tx, half * 2 + 1)], axis=1)
            modes = plane_product(plane_ref, lines)
            finish(tx * 4 + half * 2, modes[:, :LANES])
            finish(tx * 4 + half * 2 + 1, modes[:, LANES:])
        return 0

    lax.fori_loop(0, 16, sines, 0, unroll=8)


def down_first_kernel(own_ref, *refs):
    count = len(TAKE_FIRST)
    (
        plane_in, base_in, lam_in, modes_ref, root_ref, gain_ref, power_ref,
        grid_ref, plane_ref, base_ref, lam_ref, sems,
    ) = refs[count:]
    copies = start_copies(((plane_in.at[own_ref[0]], plane_ref), (base_in, base_ref), (lam_in, lam_ref)), sems)
    for each in copies:
        each.wait()
    excess = base_ref[...] + lam_ref[pl.ds(own_ref[0], 1), :]
    spread = jnp.sqrt(excess * (excess + 4.0))
    root_ref[...] = 2.0 / (2.0 + excess + spread)
    gain_ref[...] = 1.0 / spread
    for part in range(2):
        here = pl.ds(part * PLANES // 2, PLANES // 2)
        square = root_ref[here, :] * root_ref[here, :]

        def raised(step, power):
            power_ref[step, here, :] = power
            return power * square

        lax.fori_loop(0, STEPS, raised, jnp.ones(square.shape, jnp.float32), unroll=8)

    def finish(line, values):
        modes_ref[line] = values

    add_sines(refs[:count], plane_ref, grid_ref, finish)


def down_later_kernel(own_ref, *refs):
    count = len(TAKE_LATER)
    (
        sums_ref, root_ref, plane_in, walk_ref, end_ref, grid_ref, modes_ref, last_ref, plane_ref, sems,
    ) = refs[count:]
    [copy] = start_copies(((plane_in.at[own_ref[0]], plane_ref),), sems)
    copy.wait()

    def finish(line, values):
        modes_ref[line] = sums_ref[line] + values

    add_sines(refs[:count], plane_ref, grid_ref, finish)
    part_rows = 64
    low = low_half((part_rows, LANES))
    for part in range(PLANES // part_rows):
        here = pl.ds(part * part_rows, part_rows)
        root = root_ref[here, :]
        square = root * root

        def walk(step, held):
            ahead, behind = modes_ref[step, here, :], modes_ref[STEPS - 1 - step, here, :]
            own = jnp.where(low, behind, ahead)
            other = pltpu.roll(jnp.where(low, ahead, behind), HALF, 1)
            held = square * held + (own + root * other)
            walk_ref[step, here, :] = held
            return held

        last_ref[here, :] = lax.fori_loop(0, STEPS, walk, jnp.zeros((part_rows, LANES), jnp.float32), unroll=8)
    last = last_ref[...]
    level = level_of(jnp.max(jnp.abs(last), axis=0, keepdims=True))
    end_ref[:PLANES, :] = fixed_of(last * inverse_of(level))
    end_ref[PLANES:, :] = head_of(level)


def local_kernel(walk_ref, root_ref, gain_ref, local_ref):
    part_rows = 64
    low = low_half((part_rows, LANES))
    for part in range(PLANES // part_rows):
        here = pl.ds(part * part_rows, part_rows)
        root, gain = root_ref[here, :], gain_ref[here, :]
        zero = jnp.zeros(root.shape, jnp.float32)

        def line(step, ahead_before, behind_after):
            near = jnp.where(low, walk_ref[STEPS - 1 - step, here, :], walk_ref[step, here, :])
            far = pltpu.roll(jnp.where(low, behind_after, ahead_before), HALF, 1)
            local_ref[step, here, :] = gain * (near + root * far)

        def inner(step, _):
            line(step, walk_ref[step - 1, here, :], walk_ref[STEPS - 2 - step, here, :])
            return 0

        line(0, zero, walk_ref[STEPS - 2, here, :])
        lax.fori_loop(1, STEPS - 1, inner, 0, unroll=6)
        line(STEPS - 1, walk_ref[STEPS - 2, here, :], zero)


def up_kernel(own_ref, local_ref, power_ref, root_ref, gain_ref, *refs):
    end_refs, plane_in = refs[:GROUPS], refs[GROUPS]
    count = GROUPS + 1 + len(SEND)
    sent_refs = refs[GROUPS + 1 : count]
    rise_ref, fall_ref, grid_ref, level_ref, plane_ref, sems = refs[count:]
    [copy] = start_copies(((plane_in.at[own_ref[0]], plane_ref),), sems)
    low = low_half((PLANES, LANES))
    root = root_ref[...]
    square = root * root
    across = square
    for _ in range(6):
        across = across * across
    around = across
    for _ in range(2):
        around = around * around
    ends = [wide(end_ref) for end_ref in end_refs]
    entering = jnp.zeros((PLANES, LANES), jnp.float32)
    for step in range(GROUPS - 1, -1, -1):
        entering = entering * across + jnp.where(low, ends[GROUPS - 1 - step], ends[(step + 1) % GROUPS])
    entering = gain_ref[...] * entering / (1.0 - around)
    straight, turned = square * entering, root * pltpu.roll(entering, HALF, 1)
    rise_ref[...] = jnp.where(low, turned, straight)
    fall_ref[...] = jnp.where(low, straight, turned)
    copy.wait()
    slabs = len(sent_refs)

    def solved(step):
        reach = rise_ref[...] * power_ref[step] + fall_ref[...] * power_ref[STEPS - 1 - step]
        return local_ref[step] + reach

    def sines(tx, most):
        for half in range(2):
            first = tx * 4 + half * 2
            lines = plane_product(plane_ref, jnp.concatenate([solved(first), solved(first + 1)], axis=1))
            for one in range(2):
                part = lines[:, one * LANES : (one + 1) * LANES]
                most = jnp.maximum(most, jnp.max(jnp.abs(part).reshape(4 * BZ, slabs, LANES), axis=0))
                for plane in range(BZ):
                    grid_ref[grid_rows(slabs, plane, half * 2 + one, tx), :] = part[
                        plane * 4 * slabs : (plane + 1) * 4 * slabs
                    ]
        return most

    most = lax.fori_loop(0, 16, sines, jnp.zeros((slabs, LANES), jnp.float32), unroll=8)
    level_ref[...] = level_of(most)
    for at, sent_ref in enumerate(sent_refs):
        level = level_ref[at : at + 1, :]
        sent_ref[:ROWS, :] = fixed_of(grid_ref[pl.ds(at, ROWS, stride=slabs), :] * inverse_of(level))
        sent_ref[ROWS:, :] = head_of(level)


def take_lines(own_ref, offsets, got_refs, left_ref, lines_ref):
    own = own_ref[0]
    pairs = list(dict.fromkeys(offset // 2 for offset in offsets))
    for offset, got_ref in zip(offsets, got_refs):
        lines_ref[2 * pairs.index(offset // 2) + ((own ^ offset) & 1)] = wide(got_ref)
    low = low_half((DOT_ROWS, LANES))
    for at in range(len(pairs)):
        for start in range(0, ROWS, DOT_ROWS):
            here = slice(start, start + DOT_ROWS)
            write_left(at, here, even_odd(lines_ref[2 * at, here, :], lines_ref[2 * at + 1, here, :], low), left_ref)
    return [(own >> 1) ^ pair for pair in pairs]


def point_parts(pair, cosines, sines, weight_ref):
    for ty in range(4):
        part = weight_ref[pair, ty] * cosines + weight_ref[pair, 4 + ty] * sines
        yield ty, part
        yield ty + 4, weight_ref[pair, 8] * part


def reply_first_kernel(own_ref, weight_ref, *refs):
    count = len(TAKE_FIRST)
    table_in, sums_ref, lines_ref, left_ref, table_ref, sems = refs[count:]
    [copy] = start_copies(((table_in.at[pl.ds(PAIRS, PAIRS)], table_ref),), sems)
    pairs = take_lines(own_ref, TAKE_FIRST, refs[:count], left_ref, lines_ref)
    copy.wait()
    for at, pair in enumerate(pairs):
        for part in range(ROWS // DOT_ROWS):
            here = slice(part * DOT_ROWS, (part + 1) * DOT_ROWS)
            cosines, sines = line_product(at, here, left_ref, table_ref[pair])
            for ty, values in point_parts(pair, cosines, sines, weight_ref):
                sums_ref[ty, here, :] = values if at == 0 else sums_ref[ty, here, :] + values


def reply_later_kernel(own_ref, weight_ref, *refs):
    count = len(TAKE_LATER)
    sums_ref, picks_ref, table_in, out_ref, lines_ref, left_ref, pot_ref, table_ref, sems = refs[count:]
    own_pair = (own_ref[0] >> 1) ^ (TAKE_LATER[0] // 2)
    [copy] = start_copies(((table_in.at[PAIRS + own_pair], table_ref),), sems)
    [pair] = take_lines(own_ref, TAKE_LATER, refs[:count], left_ref, lines_ref)
    copy.wait()
    for part in range(ROWS // DOT_ROWS):
        here = slice(part * DOT_ROWS, (part + 1) * DOT_ROWS)
        cosines, sines = line_product(0, here, left_ref, table_ref[...])
        for ty, values in point_parts(pair, cosines, sines, weight_ref):
            values = (sums_ref[ty, here, :] + values).astype(jnp.bfloat16)
            for one in range(DOT_ROWS // SPOTS):
                q = part * (DOT_ROWS // SPOTS) + one
                pot_ref[ty * SPOTS : (ty + 1) * SPOTS, q * LANES : (q + 1) * LANES] = values[
                    one * SPOTS : (one + 1) * SPOTS
                ]
    for q in range(0, BRICK_ROWS, 4):
        there = slice(q * LANES, (q + 4) * LANES)
        out_ref[:, there] = dot(picks_ref[...], pot_ref[:, there]).astype(jnp.bfloat16)


def unpack_kernel(back_ref, got_ref, out_ref):
    for q in range(0, BRICK_ROWS, 4):
        there = slice(q * LANES, (q + 4) * LANES)
        out_ref[:, there] = dot(back_ref[...], got_ref[:, there]).astype(jnp.bfloat16)


def call(kernel, name, operands, spaces, outs, places, scratch, vmem=VMEM_BYTES):
    return pl.pallas_call(
        kernel,
        out_shape=outs,
        in_specs=[pl.BlockSpec(memory_space=space) for space in spaces],
        out_specs=[pl.BlockSpec(memory_space=space) for space in places],
        scratch_shapes=scratch,
        compiler_params=pltpu.CompilerParams(vmem_limit_bytes=vmem),
        name=name,
    )(*operands)


def on_device_8x4(bricks, owners, tile_ids, counts):
    V, S, H = pltpu.VMEM, pltpu.SMEM, pltpu.HBM
    f32, bf16, i32, i16 = jnp.float32, jnp.bfloat16, jnp.int32, jnp.int16
    shape, dma = jax.ShapeDtypeStruct, pltpu.SemaphoreType.DMA
    brick_rows = bricks.shape[0]

    def held(table):
        return pltpu.with_memory_space_constraint(jnp.asarray(table), pltpu.HBM)

    lines = held(line_tables())
    weights = jnp.asarray(class_weights())
    planes_in = [held(plane_tables(offsets, False)) for offsets in (TAKE_FIRST, TAKE_LATER)]
    planes_out = held(plane_tables(SEND, True))
    base, lam = (held(each) for each in mode_tables())
    own = lax.axis_index("gz").astype(i32).reshape(1)
    sent_shape = shape((ROWS + HEAD_ROWS, LANES), i16)
    end_shape = shape((PLANES + HEAD_ROWS, LANES), i16)
    cube, flat, sums_shape = (STEPS, PLANES, LANES), (PLANES, LANES), (8, ROWS, LANES)
    line, rows_shape = (ROWS, LANES), (SLOTS, CELLS + LANES)

    def all_ways(values):
        return lax.all_to_all(values, ("gz", "ma"), split_axis=0, concat_axis=0, tiled=True)

    def over_slabs(offset, values):
        return lax.ppermute(values, "gz", [(g, g ^ offset) for g in range(SLABS)]) if offset else values

    def round_groups(values, step):
        return lax.ppermute(values, "ma", [(m, (m + step) % GROUPS) for m in range(GROUPS)]) if step else values

    def exchanged(sent):
        sent = dict(zip(SEND, sent))
        got = {offset: over_slabs(offset, sent[offset]) for offset in TAKE_FIRST + TAKE_LATER}
        return [got[offset] for offset in TAKE_FIRST], [got[offset] for offset in TAKE_LATER]

    outgoing, back = call(
        pack_kernel,
        "pack",
        (owners.reshape(brick_rows), tile_ids, counts, bricks),
        [H] * 4,
        [shape(rows_shape, bf16), shape((brick_rows, SLOTS), bf16)],
        [H, V],
        [
            S((brick_rows,), i32),
            S((brick_rows,), i32),
            S((1,), i32),
            V(bricks.shape, bf16),
            V((SLOTS + PAIR_SLOTS, brick_rows), f32),
            V((SLOTS + PAIR_SLOTS, LANES), f32),
            V(rows_shape, bf16),
            S((DOMAINS,), i32),
            dma((4,)),
            dma((4,)),
        ],
        ALL_VMEM_BYTES,
    )
    *sent, picks = call(
        forward_kernel,
        "forward",
        (own, all_ways(outgoing), lines),
        [S, V, H],
        [sent_shape] * len(SEND) + [shape((SLOTS, TILES), bf16)],
        [V] * (len(SEND) + 1),
        [
            V((TILES, SLOTS), bf16),
            V((PAIRS, 2 * ROWS, 2 * LANES), bf16),
            V((len(SEND), *line), f32),
            V((len(SEND), 8, LANES), f32),
            V((PAIRS, *lines.shape[1:]), bf16),
            dma((1,)),
        ],
    )
    first, later = exchanged(sent)
    sums, root, gain, power = call(
        down_first_kernel,
        "down_first",
        (own, *first, planes_in[0], base, lam),
        [S] + [V] * len(first) + [H] * 3,
        [shape(cube, f32), shape(flat, f32), shape(flat, f32), shape(cube, f32)],
        [V] * 4,
        [
            V((len(first) * ROWS, LANES), f32),
            V(planes_in[0].shape[1:], bf16),
            V(base.shape, f32),
            V(lam.shape, f32),
            dma((3,)),
        ],
    )
    walk, end = call(
        down_later_kernel,
        "down_later",
        (own, *later, sums, root, planes_in[1]),
        [S] + [V] * (len(later) + 2) + [H],
        [shape(cube, f32), end_shape],
        [V, V],
        [
            V((len(later) * ROWS, LANES), f32),
            V(cube, f32),
            V(flat, f32),
            V(planes_in[1].shape[1:], bf16),
            dma((1,)),
        ],
    )
    ends = [round_groups(end, step) for step in range(GROUPS)]
    (local,) = call(local_kernel, "local", (walk, root, gain), [V] * 3, [shape(cube, f32)], [V], [])
    sent = call(
        up_kernel,
        "up",
        (own, local, power, root, gain, *ends, planes_out),
        [S] + [V] * (4 + GROUPS) + [H],
        [sent_shape] * len(SEND),
        [V] * len(SEND),
        [
            V(flat, f32),
            V(flat, f32),
            V((len(SEND) * ROWS, LANES), f32),
            V((len(SEND), LANES), f32),
            V(planes_out.shape[1:], bf16),
            dma((1,)),
        ],
    )
    first, later = exchanged(sent)
    (sums,) = call(
        reply_first_kernel,
        "reply_first",
        (own, weights, *first, lines),
        [S, S] + [V] * len(first) + [H],
        [shape(sums_shape, f32)],
        [V],
        [V((len(first), *line), f32), V((len(first) // 2, 2 * ROWS, 2 * LANES), bf16), V((PAIRS, *lines.shape[1:]), bf16), dma((1,))],
    )
    (replies,) = call(
        reply_later_kernel,
        "reply_later",
        (own, weights, *later, sums, picks, lines),
        [S, S] + [V] * (len(later) + 2) + [H],
        [shape((SLOTS, CELLS), bf16)],
        [V],
        [
            V((len(later), *line), f32),
            V((len(later) // 2, 2 * ROWS, 2 * LANES), bf16),
            V((TILES, CELLS), bf16),
            V(lines.shape[1:], bf16),
            dma((1,)),
        ],
    )
    (result,) = call(
        unpack_kernel,
        "unpack",
        (back, all_ways(replies)),
        [V, V],
        [shape((brick_rows, CELLS), bf16)],
        [V],
        [],
    )
    return result


def solution(mesh):
    in_specs = (P(("gz", "ma"), None), P(("gz", "ma"), None), P(("gz", "ma")), P(("gz", "ma")))
    out_specs = P(("gz", "ma"), None)
    body = on_device_8x4 if (mesh.shape["gz"], mesh.shape["ma"]) == (SLABS, GROUPS) else on_device
    return jax.shard_map(body, mesh=mesh, in_specs=in_specs, out_specs=out_specs, check_vma=False)
```

```python
import math

import jax
import jax.numpy as jnp
import ml_dtypes
import numpy as np
from jax import lax
from jax.experimental import pallas as pl
from jax.experimental.pallas import tpu as pltpu
from jax.sharding import PartitionSpec as P

NX = 512
NY = 512
SCREEN = 16
BZ = 4
BX = 8
BY = 64
CZ = 16


def hartley(length):
    indices = jnp.arange(length, dtype=jnp.int32)
    products = indices[:, None] * indices[None, :] % length
    angles = 2.0 * math.pi / length * products.astype(jnp.float32)
    return (jnp.cos(angles) + jnp.sin(angles)) / math.sqrt(length)


def second_difference(length, indices):
    return 2.0 - 2.0 * jnp.cos(2.0 * math.pi / length * indices.astype(jnp.float32))


def thomas(right_side, diagonal):
    start_zero = jnp.zeros(right_side.shape[1:], jnp.float32)

    def down(state_pair, plane):
        factor = 1.0 / (diagonal - state_pair[0])
        partial_value = (plane + state_pair[1]) * factor
        return ((factor, partial_value), (factor, partial_value))

    _, (factors, partials) = lax.scan(down, (start_zero, start_zero), right_side)

    def upward(beyond, factor_partial):
        solved = factor_partial[1] + factor_partial[0] * beyond
        return (solved, solved)

    _, solutions = lax.scan(upward, start_zero, (factors, partials), reverse=True)
    return solutions


def regroup(values):
    return lax.all_to_all(values, "ma", split_axis=2, concat_axis=1, tiled=True)


def on_device(bricks, owners, tile_ids, counts):
    domains = lax.axis_size(("gz", "ma"))
    group_count = lax.axis_size("ma")
    slab_count = lax.axis_size("gz")
    brick_rows, brick_cells = bricks.shape
    slot_count = max(2, 2 * brick_rows // domains)
    local_x = NX // group_count
    local_y = NY // group_count
    tiles_dev = CZ // BZ * (local_x // BX) * (NY // BY)
    highest = lax.Precision.HIGHEST
    target = owners[:, 0]
    row_order = jnp.arange(brick_rows, dtype=jnp.int32)
    earlier_same = (target[:, None] == target[None, :]) & (row_order[None, :] < row_order[:, None])
    within = jnp.sum(earlier_same.astype(jnp.int32), axis=1)
    slot_of = target * slot_count + within
    is_live = row_order < counts[0]
    loaded = jnp.where(is_live[:, None], bricks, jnp.zeros_like(bricks))
    outgoing = jnp.zeros((domains * slot_count, brick_cells), jnp.bfloat16).at[slot_of].set(loaded)
    out_ids = jnp.full((domains * slot_count,), tiles_dev, jnp.int32).at[slot_of].set(tile_ids)
    incoming, in_ids = (
        lax.all_to_all(outgoing, ("gz", "ma"), split_axis=0, concat_axis=0, tiled=True),
        lax.all_to_all(out_ids, ("gz", "ma"), split_axis=0, concat_axis=0, tiled=True),
    )
    picker = (jnp.arange(tiles_dev, dtype=jnp.int32)[:, None] == in_ids[None, :]).astype(
        jnp.bfloat16
    )
    deposit = jnp.dot(picker, incoming, preferred_element_type=jnp.float32)
    charge = deposit.reshape(CZ // BZ, local_x // BX, NY // BY, BZ, BX, BY)
    charge = charge.transpose(0, 3, 1, 4, 2, 5).reshape(CZ, local_x, NY)
    table_x = hartley(NX)
    table_y = hartley(NY)
    along_y = jnp.einsum("zxy,ky->zxk", charge, table_y, precision=highest)
    gathered_x = regroup(along_y)
    spectrum = jnp.einsum("zxk,jx->zjk", gathered_x, table_x, precision=highest)
    columns = lax.axis_index("ma") * local_y + jnp.arange(local_y, dtype=jnp.int32)
    lam_y = second_difference(NY, columns)
    screening = 1.0 / (SCREEN * SCREEN)
    slab_index = lax.axis_index("gz")
    lam_x = second_difference(NX, jnp.arange(NX, dtype=jnp.int32))
    diagonal = 2.0 + screening + lam_x[:, None] + lam_y[None, :]
    interior = spectrum[1:]
    particular = thomas(interior, diagonal)
    unit_rhs = jnp.zeros_like(interior).at[0].set(1.0)
    spike = thomas(unit_rhs, diagonal)
    near_weight = spike[0]
    far_weight = spike[-1]
    head_term = spectrum[0] + particular[0]
    tail_term = particular[-1]
    reduced_first = diagonal - near_weight
    reduced_rest = diagonal - 2.0 * near_weight
    start_zero = jnp.zeros_like(diagonal)
    heads, tails = (
        lax.all_gather(head_term[None], "gz", axis=0, tiled=True),
        lax.all_gather(tail_term[None], "gz", axis=0, tiled=True),
    )
    before = jnp.concatenate([start_zero[None], tails[:-1]], axis=0)
    sources = heads + before

    def chain_down(state_pair, packed):
        source, position = packed
        base_term = jnp.where(position == 0, reduced_first, reduced_rest)
        pivot_now = 1.0 / (base_term - far_weight * far_weight * state_pair[0])
        forward_part = pivot_now * (source + far_weight * state_pair[1])
        return ((pivot_now, forward_part), (pivot_now, forward_part))

    _, (pivots, forwards) = lax.scan(
        chain_down, (start_zero, start_zero), (sources, jnp.arange(slab_count, dtype=jnp.int32))
    )

    def chain_up(beyond, packed):
        plane_value = packed[1] + far_weight * packed[0] * beyond
        return (plane_value, plane_value)

    _, separators = lax.scan(chain_up, start_zero, (pivots, forwards), reverse=True)
    padded_sep = jnp.concatenate([separators, start_zero[None]], axis=0)
    own_plane = lax.dynamic_index_in_dim(padded_sep, slab_index, 0, keepdims=False)
    next_plane = lax.dynamic_index_in_dim(padded_sep, slab_index + 1, 0, keepdims=False)
    interior_sol = particular + own_plane[None] * spike + next_plane[None] * spike[::-1]
    modal = jnp.concatenate([own_plane[None], interior_sol], axis=0)
    back_x = jnp.einsum("zjk,jx->zkx", modal, table_x, precision=highest)
    gathered_y = regroup(back_x)
    potential = jnp.einsum("zkx,ky->zxy", gathered_y, table_y, precision=highest)
    pot_tiles = potential.reshape(CZ // BZ, BZ, local_x // BX, BX, NY // BY, BY)
    pot_tiles = (
        pot_tiles.transpose(0, 2, 4, 1, 3, 5).reshape(tiles_dev, brick_cells).astype(jnp.bfloat16)
    )
    padded_tiles = jnp.concatenate([pot_tiles, jnp.zeros((1, brick_cells), jnp.bfloat16)], axis=0)
    replies = padded_tiles[in_ids]
    returned = lax.all_to_all(replies, ("gz", "ma"), split_axis=0, concat_axis=0, tiled=True)
    result = returned[slot_of]
    return jnp.where(is_live[:, None], result, jnp.zeros_like(result))


DOMAINS = 32
GROUPS = 4
SLABS = 8
SEND = (4, 2, 5, 3, 0, 1, 6, 7)
TAKE_FIRST = (0, 4, 2, 5, 3, 1)
TAKE_LATER = (6, 7)
PAIR_SLOTS = 8
SLOTS = DOMAINS * PAIR_SLOTS
TILES = 512
BRICK_ROWS = 16
CELLS = 2048
LANES = 128
HALF = 64
SPOTS = 64
ROWS = BRICK_ROWS * SPOTS
DOT_ROWS = 512
PAIRS = 4
CLASSES = (0, 4, 1, 7, 2, 6, 3, 5)
HEAD_ROWS = 16
STEPS = 64
PLANES = 128
FULL = 32700.0
LOG_UNIT = 128.0
VMEM_BYTES = 24 * 1024 * 1024
ALL_VMEM_BYTES = 60 * 1024 * 1024


def split_table(table):
    high = table.astype(ml_dtypes.bfloat16)
    low = (table - high.astype(np.float64)).astype(ml_dtypes.bfloat16)
    return high, low


def line_tables():
    iy, k2 = np.arange(HALF)[:, None], np.arange(HALF)[None, :]
    tables = []
    for pair in range(PAIRS):
        table = np.zeros((LANES, LANES))
        for one in range(2):
            angle = 2.0 * np.pi / NY * (iy * (CLASSES[2 * pair + one] + 8 * k2) % NY)
            cosine, sine = np.cos(angle) / np.sqrt(NY), np.sin(angle) / np.sqrt(NY)
            there = slice(one * HALF, (one + 1) * HALF)
            if pair == 0:
                table[there, there] = cosine + sine
            else:
                table[:HALF, there] = cosine + sine
                table[HALF:, there] = (cosine - sine) * (1 - 2 * one)
        tables.append(table)

    def stacked(table):
        high, low = split_table(table)
        return np.concatenate(
            [np.concatenate([high, low], axis=1), np.concatenate([high, np.zeros_like(low)], axis=1)], axis=0
        )

    return np.stack([stacked(table) for table in tables]), np.stack([stacked(table.T) for table in tables])


def class_weights():
    pair, ty = np.arange(PAIRS)[:, None], np.arange(4)[None, :]
    cosine, sine = np.cos(np.pi / 4.0 * pair * ty), np.sin(np.pi / 4.0 * pair * ty)
    sine[0] = (-1.0) ** np.arange(4)
    sign = (-1.0) ** pair * np.ones((1, 4))
    return np.concatenate([cosine, sine, sign], axis=1).astype(np.float32)


def plane_tables(offsets, turned):
    index = np.arange(PLANES)
    table = np.sqrt(2.0 / (PLANES + 1)) * np.sin(
        np.pi / (PLANES + 1) * ((index[:, None] + 1) * (index[None, :] + 1) % (2 * PLANES + 2))
    )
    each = []
    for own in range(SLABS):
        slabs = np.array([own ^ offset for offset in offsets])
        plane, tz = np.arange(BZ)[:, None, None], np.arange(BZ)[None, :, None]
        part = table[:, (slabs * CZ + tz * BZ + plane).reshape(-1)]
        high, low = split_table(part.T if turned else part)
        if 3 * high.shape[1] <= 2 * LANES:
            each.append(np.concatenate([high, high, low], axis=1))
            continue
        top = np.concatenate([high, high], axis=1)
        bottom = np.concatenate([low, np.zeros_like(low)], axis=1)
        each.append(np.concatenate([top, bottom], axis=0))
    return np.stack(each)


def mode_tables():
    mu = 2.0 - 2.0 * np.cos(np.pi / (PLANES + 1) * (np.arange(PLANES) + 1))
    base = np.broadcast_to((mu + 1.0 / (SCREEN * SCREEN))[:, None], (PLANES, LANES))
    lam = 2.0 - 2.0 * np.cos(2.0 * np.pi / NY * np.arange(NY))
    lam = np.stack([lam[number::8] for number in CLASSES])
    return base.astype(np.float32), np.concatenate([lam, lam], axis=1).astype(np.float32)


def low_half(shape):
    return lax.broadcasted_iota(jnp.int32, shape, len(shape) - 1) < HALF


def split(values):
    high = values.astype(jnp.bfloat16)
    return high, (values - high.astype(jnp.float32)).astype(jnp.bfloat16)


def dot(left, right):
    return jnp.dot(left, right, preferred_element_type=jnp.float32)


def start_copies(pairs, sems):
    copies = [pltpu.make_async_copy(source, place, sems.at[at]) for at, (source, place) in enumerate(pairs)]
    for each in copies:
        each.start()
    return copies


def even_odd(first, second, low):
    crossed = pltpu.roll(jnp.where(low, second, first), HALF, 1)
    return jnp.where(low, first, crossed), jnp.where(low, crossed, second)


def write_left(at, here, lines, left_ref):
    for line, values in enumerate(lines):
        high, rest = split(values)
        there = slice(line * ROWS + here.start, line * ROWS + here.stop)
        left_ref[at, there, :LANES] = high
        left_ref[at, there, LANES:] = rest


def line_product(at, here, left_ref, table):
    products = []
    for line in range(2):
        there = slice(line * ROWS + here.start, line * ROWS + here.stop)
        both = dot(left_ref[at, there, :], table)
        products.append(both[:, :LANES] + both[:, LANES:])
    return even_odd(*products, low_half(products[0].shape))


def class_sums(points):
    half = [points[ty] + points[ty + 4] for ty in range(4)]
    rest = [points[ty] - points[ty + 4] for ty in range(4)]
    even, odd = half[0] + half[2], half[1] + half[3]
    turn = math.sqrt(0.5)
    across, along = turn * (rest[1] - rest[3]), turn * (rest[1] + rest[3])
    return (
        (even + odd, even - odd),
        (rest[0] + across, rest[2] + along),
        (half[0] - half[2], half[1] - half[3]),
        (rest[0] - across, along - rest[2]),
    )


def level_of(most):
    return jnp.floor(jnp.log2(jnp.maximum(most, 1e-30)) * LOG_UNIT) + 2.0


def inverse_of(level):
    return FULL * jnp.exp2(level * (-1.0 / LOG_UNIT))


def fixed_of(values):
    return jnp.floor(values + 0.5).astype(jnp.int32).astype(jnp.int16)


def head_of(level):
    return jnp.broadcast_to(level, (HEAD_ROWS, LANES)).astype(jnp.int32).astype(jnp.int16)


def unit_of(sent_ref):
    head = sent_ref[sent_ref.shape[0] - HEAD_ROWS :, :].astype(jnp.int32).astype(jnp.float32)
    return jnp.exp2(head[0:1] * (1.0 / LOG_UNIT)) * (1.0 / FULL)


def wide(sent_ref):
    block = sent_ref[: sent_ref.shape[0] - HEAD_ROWS, :]
    return block.astype(jnp.int32).astype(jnp.float32) * unit_of(sent_ref)


def pack_kernel(
    owner_in, tile_in, count_in, brick_in, out_ref, back_ref,
    owner_ref, tile_ref, count_ref, brick_ref, pick_ref, head_ref, ready_ref, used_ref, sems, out_sems,
):
    copies = start_copies(
        ((owner_in, owner_ref), (tile_in, tile_ref), (count_in, count_ref), (brick_in, brick_ref)), sems
    )
    brick_rows = brick_ref.shape[0]
    head_ref[...] = jnp.full(head_ref.shape, float(TILES), jnp.float32)
    pick_ref[...] = jnp.zeros(pick_ref.shape, jnp.float32)
    for owner in range(DOMAINS):
        used_ref[owner] = 0
    for each in copies[:3]:
        each.wait()
    count = count_ref[0]
    lane = lax.broadcasted_iota(jnp.int32, (1, brick_rows), 1)

    def place(r, _):
        owner = owner_ref[r]
        within = used_ref[owner]
        used_ref[owner] = within + 1
        slot = jnp.where(r < count, owner * PAIR_SLOTS + within, SLOTS)
        tile = tile_ref[r]
        position = (tile & 7) * SPOTS + ((tile >> 3) & 15) * 4 + (tile >> 7)
        pick_ref[pl.ds(slot, 1), :] = jnp.where(lane == r, 1.0, 0.0)
        head_ref[pl.ds(slot, 1), :] = jnp.full((1, LANES), position, jnp.int32).astype(jnp.float32)
        return 0

    lax.fori_loop(0, brick_rows, place, 0, unroll=8)
    copies[3].wait()
    copies = []
    rows = 64
    for part in range(SLOTS // rows):
        here = slice(part * rows, (part + 1) * rows)
        ready_ref[here, :CELLS] = dot(pick_ref[here, :].astype(jnp.bfloat16), brick_ref[...]).astype(jnp.bfloat16)
        head = head_ref[here, :]
        high = jnp.floor(head * (1.0 / 32.0))
        ready_ref[here, CELLS:] = jnp.where(low_half(head.shape), high, head - 32.0 * high).astype(jnp.bfloat16)
        some = pl.ds(part * rows, rows)
        copies.append(pltpu.make_async_copy(ready_ref.at[some], out_ref.at[some], out_sems.at[part]))
        copies[-1].start()
    for part in range(SLOTS // LANES):
        here = slice(part * LANES, (part + 1) * LANES)
        back_ref[:, here] = pick_ref[here, :].T.astype(jnp.bfloat16)
    for each in copies:
        each.wait()


def write_picks(brick_ref, picks_ref, across_ref):
    for part in range(SLOTS // LANES):
        here = slice(part * LANES, (part + 1) * LANES)
        head = brick_ref[here, CELLS:].astype(jnp.float32)
        turned = pltpu.roll(head, HALF, 1)
        low = low_half(head.shape)
        places = (jnp.where(low, head, turned) * 32.0 + jnp.where(low, turned, head)).astype(jnp.int32)
        for block in range(TILES // LANES):
            there = slice(block * LANES, (block + 1) * LANES)
            lane = lax.broadcasted_iota(jnp.int32, (LANES, LANES), 1) + block * LANES
            square = jnp.where(places == lane, 1.0, 0.0)
            picks_ref[here, there] = square.astype(jnp.bfloat16)
            across_ref[there, here] = square.T.astype(jnp.bfloat16)


def forward_kernel(own_ref, brick_ref, table_in, *refs):
    sent_refs = refs[: len(SEND)]
    picks_ref, across_ref, left_ref, lines_ref, most_ref, table_ref, sems = refs[len(SEND) :]
    [copy] = start_copies(((table_in, table_ref),), sems)
    write_picks(brick_ref, picks_ref, across_ref)
    low = low_half((SPOTS, LANES))
    for q in range(0, BRICK_ROWS, 4):
        charge = dot(across_ref[...], brick_ref[:, q * LANES : (q + 4) * LANES])
        for one in range(4):
            there = slice(one * LANES, (one + 1) * LANES)
            here = slice((q + one) * SPOTS, (q + one + 1) * SPOTS)
            points = [charge[ty * SPOTS : (ty + 1) * SPOTS, there] for ty in range(8)]
            for pair, (cosines, sines) in enumerate(class_sums(points)):
                write_left(pair, here, even_odd(cosines, sines, low), left_ref)
    copy.wait()
    for pair in range(PAIRS):
        for part in range(ROWS // DOT_ROWS):
            here = slice(part * DOT_ROWS, (part + 1) * DOT_ROWS)
            for one, values in enumerate(line_product(pair, here, left_ref, table_ref[pair])):
                lines_ref[2 * pair + one, here, :] = values
                most = jnp.max(jnp.abs(values).reshape(DOT_ROWS // 8, 8, LANES), axis=0)
                most_ref[2 * pair + one] = most if part == 0 else jnp.maximum(most_ref[2 * pair + one], most)
    for offset, sent_ref in zip(SEND, sent_refs):
        g = own_ref[0] ^ offset
        level = level_of(jnp.max(most_ref[g], axis=0, keepdims=True))
        sent_ref[:ROWS, :] = fixed_of(lines_ref[g] * inverse_of(level))
        sent_ref[ROWS:, :] = head_of(level)


def grid_rows(slabs, plane, xq, tx):
    start = ((plane * 4 + xq) * SPOTS + tx * 4) * slabs
    return pl.ds(pl.multiple_of(start, 4 * slabs), 4 * slabs)


def plane_product(plane_ref, lines):
    high, rest = split(lines)
    rows = plane_ref.shape[0]
    if plane_ref.shape[1] == 3 * high.shape[0]:
        return dot(plane_ref[...], jnp.concatenate([high, rest, high], axis=0))
    both = dot(plane_ref[...], jnp.concatenate([high, rest], axis=0))
    return both[: rows // 2] + both[rows // 2 :]


def add_sines(got_refs, plane_ref, grid_ref, finish):
    slabs = len(got_refs)
    for at, got_ref in enumerate(got_refs):
        grid_ref[pl.ds(at, ROWS, stride=slabs), :] = wide(got_ref)

    def planes(tx, xq):
        return jnp.concatenate([grid_ref[grid_rows(slabs, plane, xq, tx), :] for plane in range(BZ)], axis=0)

    def sines(tx, _):
        modes = plane_product(plane_ref, jnp.concatenate([planes(tx, xq) for xq in range(4)], axis=1))
        for xq in range(4):
            finish(tx * 4 + xq, modes[:, xq * LANES : (xq + 1) * LANES])
        return 0

    lax.fori_loop(0, 16, sines, 0, unroll=8)


def down_first_kernel(own_ref, *refs):
    count = len(TAKE_FIRST)
    planes_ref, base_ref, lam_ref, modes_ref, root_ref, gain_ref, power_ref, grid_ref = refs[count:]
    excess = base_ref[...] + lam_ref[pl.ds(own_ref[0], 1), :]
    spread = jnp.sqrt(excess * (excess + 4.0))
    root_ref[...] = 2.0 / (2.0 + excess + spread)
    gain_ref[...] = 1.0 / spread
    for part in range(2):
        here = pl.ds(part * PLANES // 2, PLANES // 2)
        square = root_ref[here, :] * root_ref[here, :]

        def raised(step, power):
            power_ref[step, here, :] = power
            return power * square

        lax.fori_loop(0, STEPS, raised, jnp.ones(square.shape, jnp.float32), unroll=8)

    def finish(line, values):
        modes_ref[line] = values

    add_sines(refs[:count], planes_ref.at[own_ref[0]], grid_ref, finish)


def down_later_kernel(own_ref, *refs):
    count = len(TAKE_LATER)
    sums_ref, root_ref, planes_ref, walk_ref, end_ref, grid_ref, modes_ref, last_ref = refs[count:]

    def finish(line, values):
        modes_ref[line] = sums_ref[line] + values

    add_sines(refs[:count], planes_ref.at[own_ref[0]], grid_ref, finish)
    part_rows = 64
    low = low_half((part_rows, LANES))
    for part in range(PLANES // part_rows):
        here = pl.ds(part * part_rows, part_rows)
        root = root_ref[here, :]
        square = root * root

        def walk(step, held):
            ahead, behind = modes_ref[step, here, :], modes_ref[STEPS - 1 - step, here, :]
            own = jnp.where(low, behind, ahead)
            other = pltpu.roll(jnp.where(low, ahead, behind), HALF, 1)
            held = square * held + (own + root * other)
            walk_ref[step, here, :] = held
            return held

        last_ref[here, :] = lax.fori_loop(0, STEPS, walk, jnp.zeros((part_rows, LANES), jnp.float32), unroll=8)
    last = last_ref[...]
    level = level_of(jnp.max(jnp.abs(last), axis=0, keepdims=True))
    end_ref[:PLANES, :] = fixed_of(last * inverse_of(level))
    end_ref[PLANES:, :] = head_of(level)


def local_kernel(walk_ref, root_ref, gain_ref, local_ref):
    part_rows = 64
    low = low_half((part_rows, LANES))
    for part in range(PLANES // part_rows):
        here = pl.ds(part * part_rows, part_rows)
        root, gain = root_ref[here, :], gain_ref[here, :]
        zero = jnp.zeros(root.shape, jnp.float32)

        def line(step, ahead_before, behind_after):
            near = jnp.where(low, walk_ref[STEPS - 1 - step, here, :], walk_ref[step, here, :])
            far = pltpu.roll(jnp.where(low, behind_after, ahead_before), HALF, 1)
            local_ref[step, here, :] = gain * (near + root * far)

        def inner(step, _):
            line(step, walk_ref[step - 1, here, :], walk_ref[STEPS - 2 - step, here, :])
            return 0

        line(0, zero, walk_ref[STEPS - 2, here, :])
        lax.fori_loop(1, STEPS - 1, inner, 0, unroll=6)
        line(STEPS - 1, walk_ref[STEPS - 2, here, :], zero)


def up_kernel(own_ref, local_ref, power_ref, root_ref, gain_ref, *refs):
    end_refs, plane_ref = refs[:GROUPS], refs[GROUPS].at[own_ref[0]]
    count = GROUPS + 1 + len(SEND)
    sent_refs = refs[GROUPS + 1 : count]
    rise_ref, fall_ref, grid_ref, level_ref = refs[count:]
    low = low_half((PLANES, LANES))
    root = root_ref[...]
    square = root * root
    across = square
    for _ in range(6):
        across = across * across
    around = across
    for _ in range(2):
        around = around * around
    ends = [wide(end_ref) for end_ref in end_refs]
    entering = jnp.zeros((PLANES, LANES), jnp.float32)
    for step in range(GROUPS - 1, -1, -1):
        entering = entering * across + jnp.where(low, ends[GROUPS - 1 - step], ends[(step + 1) % GROUPS])
    entering = gain_ref[...] * entering / (1.0 - around)
    straight, turned = square * entering, root * pltpu.roll(entering, HALF, 1)
    rise_ref[...] = jnp.where(low, turned, straight)
    fall_ref[...] = jnp.where(low, straight, turned)
    slabs = len(sent_refs)

    def solved(step):
        reach = rise_ref[...] * power_ref[step] + fall_ref[...] * power_ref[STEPS - 1 - step]
        return local_ref[step] + reach

    def sines(tx, most):
        lines = plane_product(plane_ref, jnp.concatenate([solved(tx * 4 + xq) for xq in range(4)], axis=1))
        for xq in range(4):
            part = lines[:, xq * LANES : (xq + 1) * LANES]
            most = jnp.maximum(most, jnp.max(jnp.abs(part).reshape(4 * BZ, slabs, LANES), axis=0))
            for plane in range(BZ):
                grid_ref[grid_rows(slabs, plane, xq, tx), :] = part[plane * 4 * slabs : (plane + 1) * 4 * slabs]
        return most

    most = lax.fori_loop(0, 16, sines, jnp.zeros((slabs, LANES), jnp.float32), unroll=8)
    level_ref[...] = level_of(most)
    for at, sent_ref in enumerate(sent_refs):
        level = level_ref[at : at + 1, :]
        sent_ref[:ROWS, :] = fixed_of(grid_ref[pl.ds(at, ROWS, stride=slabs), :] * inverse_of(level))
        sent_ref[ROWS:, :] = head_of(level)


def take_lines(own_ref, offsets, got_refs, left_ref, lines_ref):
    own = own_ref[0]
    pairs = list(dict.fromkeys(offset // 2 for offset in offsets))
    for offset, got_ref in zip(offsets, got_refs):
        lines_ref[2 * pairs.index(offset // 2) + ((own ^ offset) & 1)] = wide(got_ref)
    low = low_half((DOT_ROWS, LANES))
    for at in range(len(pairs)):
        for start in range(0, ROWS, DOT_ROWS):
            here = slice(start, start + DOT_ROWS)
            write_left(at, here, even_odd(lines_ref[2 * at, here, :], lines_ref[2 * at + 1, here, :], low), left_ref)
    return [(own >> 1) ^ pair for pair in pairs]


def point_parts(pair, cosines, sines, weight_ref):
    for ty in range(4):
        part = weight_ref[pair, ty] * cosines + weight_ref[pair, 4 + ty] * sines
        yield ty, part
        yield ty + 4, weight_ref[pair, 8] * part


def reply_first_kernel(own_ref, weight_ref, *refs):
    count = len(TAKE_FIRST)
    table_ref, sums_ref, lines_ref, left_ref = refs[count:]
    pairs = take_lines(own_ref, TAKE_FIRST, refs[:count], left_ref, lines_ref)
    for at, pair in enumerate(pairs):
        for part in range(ROWS // DOT_ROWS):
            here = slice(part * DOT_ROWS, (part + 1) * DOT_ROWS)
            cosines, sines = line_product(at, here, left_ref, table_ref[pair])
            for ty, values in point_parts(pair, cosines, sines, weight_ref):
                sums_ref[ty, here, :] = values if at == 0 else sums_ref[ty, here, :] + values


def reply_later_kernel(own_ref, weight_ref, *refs):
    count = len(TAKE_LATER)
    sums_ref, picks_ref, table_ref, out_ref, lines_ref, left_ref, pot_ref = refs[count:]
    [pair] = take_lines(own_ref, TAKE_LATER, refs[:count], left_ref, lines_ref)
    for part in range(ROWS // DOT_ROWS):
        here = slice(part * DOT_ROWS, (part + 1) * DOT_ROWS)
        cosines, sines = line_product(0, here, left_ref, table_ref[pair])
        for ty, values in point_parts(pair, cosines, sines, weight_ref):
            values = (sums_ref[ty, here, :] + values).astype(jnp.bfloat16)
            for one in range(DOT_ROWS // SPOTS):
                q = part * (DOT_ROWS // SPOTS) + one
                pot_ref[ty * SPOTS : (ty + 1) * SPOTS, q * LANES : (q + 1) * LANES] = values[
                    one * SPOTS : (one + 1) * SPOTS
                ]
    for q in range(0, BRICK_ROWS, 4):
        there = slice(q * LANES, (q + 4) * LANES)
        out_ref[:, there] = dot(picks_ref[...], pot_ref[:, there]).astype(jnp.bfloat16)


def unpack_kernel(back_ref, got_ref, out_ref):
    for q in range(0, BRICK_ROWS, 4):
        there = slice(q * LANES, (q + 4) * LANES)
        out_ref[:, there] = dot(back_ref[...], got_ref[:, there]).astype(jnp.bfloat16)


def call(kernel, name, operands, spaces, outs, places, scratch, vmem=VMEM_BYTES):
    return pl.pallas_call(
        kernel,
        out_shape=outs,
        in_specs=[pl.BlockSpec(memory_space=space) for space in spaces],
        out_specs=[pl.BlockSpec(memory_space=space) for space in places],
        scratch_shapes=scratch,
        compiler_params=pltpu.CompilerParams(vmem_limit_bytes=vmem),
        name=name,
    )(*operands)


def on_device_8x4(bricks, owners, tile_ids, counts):
    V, S, H = pltpu.VMEM, pltpu.SMEM, pltpu.HBM
    f32, bf16, i32, i16 = jnp.float32, jnp.bfloat16, jnp.int32, jnp.int16
    shape, dma = jax.ShapeDtypeStruct, pltpu.SemaphoreType.DMA
    brick_rows = bricks.shape[0]
    lines_in, lines_out = (jnp.asarray(each) for each in line_tables())
    weights = jnp.asarray(class_weights())
    lines_in = pltpu.with_memory_space_constraint(lines_in, H)
    planes_in = [jnp.asarray(plane_tables(offsets, False)) for offsets in (TAKE_FIRST, TAKE_LATER)]
    planes_out = jnp.asarray(plane_tables(SEND, True))
    base, lam = (jnp.asarray(each) for each in mode_tables())
    own = lax.axis_index("gz").astype(i32).reshape(1)
    sent_shape = shape((ROWS + HEAD_ROWS, LANES), i16)
    end_shape = shape((PLANES + HEAD_ROWS, LANES), i16)
    cube, flat, sums_shape = (STEPS, PLANES, LANES), (PLANES, LANES), (8, ROWS, LANES)
    line, rows_shape = (ROWS, LANES), (SLOTS, CELLS + LANES)

    def all_ways(values):
        return lax.all_to_all(values, ("gz", "ma"), split_axis=0, concat_axis=0, tiled=True)

    def over_slabs(offset, values):
        return lax.ppermute(values, "gz", [(g, g ^ offset) for g in range(SLABS)]) if offset else values

    def round_groups(values, step):
        return lax.ppermute(values, "ma", [(m, (m + step) % GROUPS) for m in range(GROUPS)]) if step else values

    def exchanged(sent):
        sent = dict(zip(SEND, sent))
        got = {offset: over_slabs(offset, sent[offset]) for offset in TAKE_FIRST + TAKE_LATER}
        return [got[offset] for offset in TAKE_FIRST], [got[offset] for offset in TAKE_LATER]

    outgoing, back = call(
        pack_kernel,
        "pack",
        (owners.reshape(brick_rows), tile_ids, counts, bricks),
        [H] * 4,
        [shape(rows_shape, bf16), shape((brick_rows, SLOTS), bf16)],
        [H, V],
        [
            S((brick_rows,), i32),
            S((brick_rows,), i32),
            S((1,), i32),
            V(bricks.shape, bf16),
            V((SLOTS + PAIR_SLOTS, brick_rows), f32),
            V((SLOTS + PAIR_SLOTS, LANES), f32),
            V(rows_shape, bf16),
            S((DOMAINS,), i32),
            dma((4,)),
            dma((4,)),
        ],
        ALL_VMEM_BYTES,
    )
    *sent, picks = call(
        forward_kernel,
        "forward",
        (own, all_ways(outgoing), lines_in),
        [S, V, H],
        [sent_shape] * len(SEND) + [shape((SLOTS, TILES), bf16)],
        [V] * (len(SEND) + 1),
        [
            V((TILES, SLOTS), bf16),
            V((PAIRS, 2 * ROWS, 2 * LANES), bf16),
            V((len(SEND), *line), f32),
            V((len(SEND), 8, LANES), f32),
            V(lines_in.shape, bf16),
            dma((1,)),
        ],
    )
    first, later = exchanged(sent)
    sums, root, gain, power = call(
        down_first_kernel,
        "down_first",
        (own, *first, planes_in[0], base, lam),
        [S] + [V] * (len(first) + 3),
        [shape(cube, f32), shape(flat, f32), shape(flat, f32), shape(cube, f32)],
        [V] * 4,
        [
            V((len(first) * ROWS, LANES), f32),
        ],
    )
    walk, end = call(
        down_later_kernel,
        "down_later",
        (own, *later, sums, root, planes_in[1]),
        [S] + [V] * (len(later) + 3),
        [shape(cube, f32), end_shape],
        [V, V],
        [
            V((len(later) * ROWS, LANES), f32),
            V(cube, f32),
            V(flat, f32),
        ],
    )
    ends = [round_groups(end, step) for step in range(GROUPS)]
    (local,) = call(local_kernel, "local", (walk, root, gain), [V] * 3, [shape(cube, f32)], [V], [])
    sent = call(
        up_kernel,
        "up",
        (own, local, power, root, gain, *ends, planes_out),
        [S] + [V] * (5 + GROUPS),
        [sent_shape] * len(SEND),
        [V] * len(SEND),
        [
            V(flat, f32),
            V(flat, f32),
            V((len(SEND) * ROWS, LANES), f32),
            V((len(SEND), LANES), f32),
        ],
    )
    first, later = exchanged(sent)
    (sums,) = call(
        reply_first_kernel,
        "reply_first",
        (own, weights, *first, lines_out),
        [S, S] + [V] * (len(first) + 1),
        [shape(sums_shape, f32)],
        [V],
        [V((len(first), *line), f32), V((len(first) // 2, 2 * ROWS, 2 * LANES), bf16)],
    )
    (replies,) = call(
        reply_later_kernel,
        "reply_later",
        (own, weights, *later, sums, picks, lines_out),
        [S, S] + [V] * (len(later) + 3),
        [shape((SLOTS, CELLS), bf16)],
        [V],
        [
            V((len(later), *line), f32),
            V((len(later) // 2, 2 * ROWS, 2 * LANES), bf16),
            V((TILES, CELLS), bf16),
        ],
    )
    (result,) = call(
        unpack_kernel,
        "unpack",
        (back, all_ways(replies)),
        [V, V],
        [shape((brick_rows, CELLS), bf16)],
        [V],
        [],
    )
    return result


def solution(mesh):
    in_specs = (P(("gz", "ma"), None), P(("gz", "ma"), None), P(("gz", "ma")), P(("gz", "ma")))
    out_specs = P(("gz", "ma"), None)
    body = on_device_8x4 if (mesh.shape["gz"], mesh.shape["ma"]) == (SLABS, GROUPS) else on_device
    return jax.shard_map(body, mesh=mesh, in_specs=in_specs, out_specs=out_specs, check_vma=False)
```

```python
import math

import jax
import jax.numpy as jnp
import ml_dtypes
import numpy as np
from jax import lax
from jax.experimental import pallas as pl
from jax.experimental.pallas import tpu as pltpu
from jax.sharding import PartitionSpec as P

NX = 512
NY = 512
SCREEN = 16
BZ = 4
BX = 8
BY = 64
CZ = 16


def hartley(length):
    indices = jnp.arange(length, dtype=jnp.int32)
    products = indices[:, None] * indices[None, :] % length
    angles = 2.0 * math.pi / length * products.astype(jnp.float32)
    return (jnp.cos(angles) + jnp.sin(angles)) / math.sqrt(length)


def second_difference(length, indices):
    return 2.0 - 2.0 * jnp.cos(2.0 * math.pi / length * indices.astype(jnp.float32))


def thomas(right_side, diagonal):
    start_zero = jnp.zeros(right_side.shape[1:], jnp.float32)

    def down(state_pair, plane):
        factor = 1.0 / (diagonal - state_pair[0])
        partial_value = (plane + state_pair[1]) * factor
        return ((factor, partial_value), (factor, partial_value))

    _, (factors, partials) = lax.scan(down, (start_zero, start_zero), right_side)

    def upward(beyond, factor_partial):
        solved = factor_partial[1] + factor_partial[0] * beyond
        return (solved, solved)

    _, solutions = lax.scan(upward, start_zero, (factors, partials), reverse=True)
    return solutions


def regroup(values):
    return lax.all_to_all(values, "ma", split_axis=2, concat_axis=1, tiled=True)


def on_device(bricks, owners, tile_ids, counts):
    domains = lax.axis_size(("gz", "ma"))
    group_count = lax.axis_size("ma")
    slab_count = lax.axis_size("gz")
    brick_rows, brick_cells = bricks.shape
    slot_count = max(2, 2 * brick_rows // domains)
    local_x = NX // group_count
    local_y = NY // group_count
    tiles_dev = CZ // BZ * (local_x // BX) * (NY // BY)
    highest = lax.Precision.HIGHEST
    target = owners[:, 0]
    row_order = jnp.arange(brick_rows, dtype=jnp.int32)
    earlier_same = (target[:, None] == target[None, :]) & (row_order[None, :] < row_order[:, None])
    within = jnp.sum(earlier_same.astype(jnp.int32), axis=1)
    slot_of = target * slot_count + within
    is_live = row_order < counts[0]
    loaded = jnp.where(is_live[:, None], bricks, jnp.zeros_like(bricks))
    outgoing = jnp.zeros((domains * slot_count, brick_cells), jnp.bfloat16).at[slot_of].set(loaded)
    out_ids = jnp.full((domains * slot_count,), tiles_dev, jnp.int32).at[slot_of].set(tile_ids)
    incoming, in_ids = (
        lax.all_to_all(outgoing, ("gz", "ma"), split_axis=0, concat_axis=0, tiled=True),
        lax.all_to_all(out_ids, ("gz", "ma"), split_axis=0, concat_axis=0, tiled=True),
    )
    picker = (jnp.arange(tiles_dev, dtype=jnp.int32)[:, None] == in_ids[None, :]).astype(
        jnp.bfloat16
    )
    deposit = jnp.dot(picker, incoming, preferred_element_type=jnp.float32)
    charge = deposit.reshape(CZ // BZ, local_x // BX, NY // BY, BZ, BX, BY)
    charge = charge.transpose(0, 3, 1, 4, 2, 5).reshape(CZ, local_x, NY)
    table_x = hartley(NX)
    table_y = hartley(NY)
    along_y = jnp.einsum("zxy,ky->zxk", charge, table_y, precision=highest)
    gathered_x = regroup(along_y)
    spectrum = jnp.einsum("zxk,jx->zjk", gathered_x, table_x, precision=highest)
    columns = lax.axis_index("ma") * local_y + jnp.arange(local_y, dtype=jnp.int32)
    lam_y = second_difference(NY, columns)
    screening = 1.0 / (SCREEN * SCREEN)
    slab_index = lax.axis_index("gz")
    lam_x = second_difference(NX, jnp.arange(NX, dtype=jnp.int32))
    diagonal = 2.0 + screening + lam_x[:, None] + lam_y[None, :]
    interior = spectrum[1:]
    particular = thomas(interior, diagonal)
    unit_rhs = jnp.zeros_like(interior).at[0].set(1.0)
    spike = thomas(unit_rhs, diagonal)
    near_weight = spike[0]
    far_weight = spike[-1]
    head_term = spectrum[0] + particular[0]
    tail_term = particular[-1]
    reduced_first = diagonal - near_weight
    reduced_rest = diagonal - 2.0 * near_weight
    start_zero = jnp.zeros_like(diagonal)
    heads, tails = (
        lax.all_gather(head_term[None], "gz", axis=0, tiled=True),
        lax.all_gather(tail_term[None], "gz", axis=0, tiled=True),
    )
    before = jnp.concatenate([start_zero[None], tails[:-1]], axis=0)
    sources = heads + before

    def chain_down(state_pair, packed):
        source, position = packed
        base_term = jnp.where(position == 0, reduced_first, reduced_rest)
        pivot_now = 1.0 / (base_term - far_weight * far_weight * state_pair[0])
        forward_part = pivot_now * (source + far_weight * state_pair[1])
        return ((pivot_now, forward_part), (pivot_now, forward_part))

    _, (pivots, forwards) = lax.scan(
        chain_down, (start_zero, start_zero), (sources, jnp.arange(slab_count, dtype=jnp.int32))
    )

    def chain_up(beyond, packed):
        plane_value = packed[1] + far_weight * packed[0] * beyond
        return (plane_value, plane_value)

    _, separators = lax.scan(chain_up, start_zero, (pivots, forwards), reverse=True)
    padded_sep = jnp.concatenate([separators, start_zero[None]], axis=0)
    own_plane = lax.dynamic_index_in_dim(padded_sep, slab_index, 0, keepdims=False)
    next_plane = lax.dynamic_index_in_dim(padded_sep, slab_index + 1, 0, keepdims=False)
    interior_sol = particular + own_plane[None] * spike + next_plane[None] * spike[::-1]
    modal = jnp.concatenate([own_plane[None], interior_sol], axis=0)
    back_x = jnp.einsum("zjk,jx->zkx", modal, table_x, precision=highest)
    gathered_y = regroup(back_x)
    potential = jnp.einsum("zkx,ky->zxy", gathered_y, table_y, precision=highest)
    pot_tiles = potential.reshape(CZ // BZ, BZ, local_x // BX, BX, NY // BY, BY)
    pot_tiles = (
        pot_tiles.transpose(0, 2, 4, 1, 3, 5).reshape(tiles_dev, brick_cells).astype(jnp.bfloat16)
    )
    padded_tiles = jnp.concatenate([pot_tiles, jnp.zeros((1, brick_cells), jnp.bfloat16)], axis=0)
    replies = padded_tiles[in_ids]
    returned = lax.all_to_all(replies, ("gz", "ma"), split_axis=0, concat_axis=0, tiled=True)
    result = returned[slot_of]
    return jnp.where(is_live[:, None], result, jnp.zeros_like(result))


DOMAINS = 32
GROUPS = 4
SLABS = 8
SEND = (4, 2, 5, 3, 0, 1, 6, 7)
ARRIVAL = (0, 4, 2, 5, 3, 1, 6, 7)
PARTS = 2
PART_PLANES = 2
TAKE_FIRST = (0, 4, 2, 5, 3, 1)
TAKE_LATER = (6, 7)
PAIR_SLOTS = 8
SLOTS = DOMAINS * PAIR_SLOTS
TILES = 512
BRICK_ROWS = 16
CELLS = 2048
LANES = 128
HALF = 64
SPOTS = 64
ROWS = BRICK_ROWS * SPOTS
PART_ROWS = ROWS // PARTS
PART_CELLS = CELLS // PARTS
DOT_ROWS = 512
PAIRS = 4
CLASSES = (0, 4, 1, 7, 2, 6, 3, 5)
HEAD_ROWS = 16
STEPS = 64
PLANES = 128
FULL = 32700.0
LOG_UNIT = 128.0
VMEM_BYTES = 24 * 1024 * 1024
ALL_VMEM_BYTES = 60 * 1024 * 1024


def split_table(table):
    high = table.astype(ml_dtypes.bfloat16)
    low = (table - high.astype(np.float64)).astype(ml_dtypes.bfloat16)
    return high, low


def line_tables():
    iy, k2 = np.arange(HALF)[:, None], np.arange(HALF)[None, :]
    tables = []
    for pair in range(PAIRS):
        table = np.zeros((LANES, LANES))
        for one in range(2):
            angle = 2.0 * np.pi / NY * (iy * (CLASSES[2 * pair + one] + 8 * k2) % NY)
            cosine, sine = np.cos(angle) / np.sqrt(NY), np.sin(angle) / np.sqrt(NY)
            there = slice(one * HALF, (one + 1) * HALF)
            if pair == 0:
                table[there, there] = cosine + sine
            else:
                table[:HALF, there] = cosine + sine
                table[HALF:, there] = (cosine - sine) * (1 - 2 * one)
        tables.append(table)

    def stacked(table):
        high, low = split_table(table)
        return np.concatenate(
            [np.concatenate([high, low], axis=1), np.concatenate([high, np.zeros_like(low)], axis=1)], axis=0
        )

    return np.stack([stacked(table) for table in tables]), np.stack([stacked(table.T) for table in tables])


def class_weights():
    pair, ty = np.arange(PAIRS)[:, None], np.arange(4)[None, :]
    cosine, sine = np.cos(np.pi / 4.0 * pair * ty), np.sin(np.pi / 4.0 * pair * ty)
    sine[0] = (-1.0) ** np.arange(4)
    sign = (-1.0) ** pair * np.ones((1, 4))
    return np.concatenate([cosine, sine, sign], axis=1).astype(np.float32)


def plane_tables(offsets, planes, turned):
    index = np.arange(PLANES)
    table = np.sqrt(2.0 / (PLANES + 1)) * np.sin(
        np.pi / (PLANES + 1) * ((index[:, None] + 1) * (index[None, :] + 1) % (2 * PLANES + 2))
    )
    each = []
    for own in range(SLABS):
        slabs = np.array([own ^ offset for offset in offsets])
        plane, tz = np.array(planes)[:, None, None], np.arange(BZ)[None, :, None]
        part = table[:, (slabs * CZ + tz * BZ + plane).reshape(-1)]
        high, low = split_table(part.T if turned else part)
        if 3 * high.shape[1] <= 2 * LANES:
            each.append(np.concatenate([high, high, low], axis=1))
            continue
        top = np.concatenate([high, high], axis=1)
        bottom = np.concatenate([low, np.zeros_like(low)], axis=1)
        each.append(np.concatenate([top, bottom], axis=0))
    return np.stack(each)


def mode_tables():
    mu = 2.0 - 2.0 * np.cos(np.pi / (PLANES + 1) * (np.arange(PLANES) + 1))
    base = np.broadcast_to((mu + 1.0 / (SCREEN * SCREEN))[:, None], (PLANES, LANES))
    lam = 2.0 - 2.0 * np.cos(2.0 * np.pi / NY * np.arange(NY))
    lam = np.stack([lam[number::8] for number in CLASSES])
    return base.astype(np.float32), np.concatenate([lam, lam], axis=1).astype(np.float32)


def low_half(shape):
    return lax.broadcasted_iota(jnp.int32, shape, len(shape) - 1) < HALF


def split(values):
    high = values.astype(jnp.bfloat16)
    return high, (values - high.astype(jnp.float32)).astype(jnp.bfloat16)


def dot(left, right):
    return jnp.dot(left, right, preferred_element_type=jnp.float32)


def start_copies(pairs, sems):
    copies = [pltpu.make_async_copy(source, place, sems.at[at]) for at, (source, place) in enumerate(pairs)]
    for each in copies:
        each.start()
    return copies


def even_odd(first, second, low):
    crossed = pltpu.roll(jnp.where(low, second, first), HALF, 1)
    return jnp.where(low, first, crossed), jnp.where(low, crossed, second)


def write_left(at, here, lines, left_ref):
    rows = left_ref.shape[1] // 2
    for line, values in enumerate(lines):
        high, rest = split(values)
        there = slice(line * rows + here.start, line * rows + here.stop)
        left_ref[at, there, :LANES] = high
        left_ref[at, there, LANES:] = rest


def line_product(at, here, left_ref, table):
    products = []
    rows = left_ref.shape[1] // 2
    for line in range(2):
        there = slice(line * rows + here.start, line * rows + here.stop)
        both = dot(left_ref[at, there, :], table)
        products.append(both[:, :LANES] + both[:, LANES:])
    return even_odd(*products, low_half(products[0].shape))


def class_sums(points):
    half = [points[ty] + points[ty + 4] for ty in range(4)]
    rest = [points[ty] - points[ty + 4] for ty in range(4)]
    even, odd = half[0] + half[2], half[1] + half[3]
    turn = math.sqrt(0.5)
    across, along = turn * (rest[1] - rest[3]), turn * (rest[1] + rest[3])
    return (
        (even + odd, even - odd),
        (rest[0] + across, rest[2] + along),
        (half[0] - half[2], half[1] - half[3]),
        (rest[0] - across, along - rest[2]),
    )


def level_of(most):
    return jnp.floor(jnp.log2(jnp.maximum(most, 1e-30)) * LOG_UNIT) + 2.0


def inverse_of(level):
    return FULL * jnp.exp2(level * (-1.0 / LOG_UNIT))


def fixed_of(values):
    return jnp.floor(values + 0.5).astype(jnp.int32).astype(jnp.int16)


def head_of(level):
    return jnp.broadcast_to(level, (HEAD_ROWS, LANES)).astype(jnp.int32).astype(jnp.int16)


def unit_of(sent_ref):
    head = sent_ref[sent_ref.shape[0] - HEAD_ROWS :, :].astype(jnp.int32).astype(jnp.float32)
    return jnp.exp2(head[0:1] * (1.0 / LOG_UNIT)) * (1.0 / FULL)


def wide(sent_ref):
    block = sent_ref[: sent_ref.shape[0] - HEAD_ROWS, :]
    return block.astype(jnp.int32).astype(jnp.float32) * unit_of(sent_ref)


def pack_kernel(
    owner_in, tile_in, count_in, brick_in, first_ref, second_ref, back_ref,
    owner_ref, tile_ref, count_ref, brick_ref, pick_ref, head_ref, ready_ref, later_ref, used_ref, sems, out_sems,
):
    copies = start_copies(
        ((owner_in, owner_ref), (tile_in, tile_ref), (count_in, count_ref), (brick_in, brick_ref)), sems
    )
    brick_rows = brick_ref.shape[0]
    head_ref[...] = jnp.full(head_ref.shape, float(TILES), jnp.float32)
    pick_ref[...] = jnp.zeros(pick_ref.shape, jnp.float32)
    for owner in range(DOMAINS):
        used_ref[owner] = 0
    for each in copies[:3]:
        each.wait()
    count = count_ref[0]
    lane = lax.broadcasted_iota(jnp.int32, (1, brick_rows), 1)

    def place(r, _):
        owner = owner_ref[r]
        within = used_ref[owner]
        used_ref[owner] = within + 1
        slot = jnp.where(r < count, owner * PAIR_SLOTS + within, SLOTS)
        tile = tile_ref[r]
        position = (tile & 7) * SPOTS + ((tile >> 3) & 15) * 4 + (tile >> 7)
        pick_ref[pl.ds(slot, 1), :] = jnp.where(lane == r, 1.0, 0.0)
        head_ref[pl.ds(slot, 1), :] = jnp.full((1, LANES), position, jnp.int32).astype(jnp.float32)
        return 0

    lax.fori_loop(0, brick_rows, place, 0, unroll=8)
    copies[3].wait()
    copies = []
    rows = 64
    for at, (out_ref, held_ref) in enumerate(((first_ref, ready_ref), (second_ref, later_ref))):
        for part in range(SLOTS // rows):
            here = slice(part * rows, (part + 1) * rows)
            picks = pick_ref[here, :].astype(jnp.bfloat16)
            cells = slice(at * PART_CELLS, (at + 1) * PART_CELLS)
            held_ref[here, :PART_CELLS] = dot(picks, brick_ref[:, cells]).astype(jnp.bfloat16)
            if at == 0:
                head = head_ref[here, :]
                high = jnp.floor(head * (1.0 / 32.0))
                places = jnp.where(low_half(head.shape), high, head - 32.0 * high)
                held_ref[here, PART_CELLS:] = places.astype(jnp.bfloat16)
            some = pl.ds(part * rows, rows)
            copies.append(pltpu.make_async_copy(held_ref.at[some], out_ref.at[some], out_sems.at[4 * at + part]))
            copies[-1].start()
    for part in range(SLOTS // LANES):
        here = slice(part * LANES, (part + 1) * LANES)
        back_ref[:, here] = pick_ref[here, :].T.astype(jnp.bfloat16)
    for each in copies:
        each.wait()


def write_picks(brick_ref, picks_ref, across_ref):
    for part in range(SLOTS // LANES):
        here = slice(part * LANES, (part + 1) * LANES)
        head = brick_ref[here, PART_CELLS:].astype(jnp.float32)
        turned = pltpu.roll(head, HALF, 1)
        low = low_half(head.shape)
        places = (jnp.where(low, head, turned) * 32.0 + jnp.where(low, turned, head)).astype(jnp.int32)
        for block in range(TILES // LANES):
            there = slice(block * LANES, (block + 1) * LANES)
            lane = lax.broadcasted_iota(jnp.int32, (LANES, LANES), 1) + block * LANES
            square = jnp.where(places == lane, 1.0, 0.0)
            picks_ref[here, there] = square.astype(jnp.bfloat16)
            across_ref[there, here] = square.T.astype(jnp.bfloat16)


def forward_lines(own_ref, brick_ref, across_ref, table_in, sent_refs, left_ref, lines_ref, table_ref, sems):
    [copy] = start_copies(((table_in, table_ref),), sems)
    low = low_half((SPOTS, LANES))
    for q in range(0, BRICK_ROWS // PARTS, 4):
        charge = dot(across_ref[...], brick_ref[:, q * LANES : (q + 4) * LANES])
        for one in range(4):
            there = slice(one * LANES, (one + 1) * LANES)
            here = slice((q + one) * SPOTS, (q + one + 1) * SPOTS)
            points = [charge[ty * SPOTS : (ty + 1) * SPOTS, there] for ty in range(8)]
            for pair, (cosines, sines) in enumerate(class_sums(points)):
                write_left(pair, here, even_odd(cosines, sines, low), left_ref)
    copy.wait()
    for pair in range(PAIRS):
        for one, values in enumerate(line_product(pair, slice(0, PART_ROWS), left_ref, table_ref[pair])):
            most = jnp.max(jnp.abs(values).reshape(PART_ROWS // 8, 8, LANES), axis=0)
            level = level_of(jnp.max(most, axis=0, keepdims=True))
            lines_ref[2 * pair + one, :PART_ROWS, :] = fixed_of(values * inverse_of(level))
            lines_ref[2 * pair + one, PART_ROWS:, :] = head_of(level)
    for offset, sent_ref in zip(SEND, sent_refs):
        sent_ref[...] = lines_ref[own_ref[0] ^ offset]


def forward_first_kernel(own_ref, brick_ref, table_in, *refs):
    sent_refs, (picks_ref, across_ref) = refs[: len(SEND)], refs[len(SEND) : len(SEND) + 2]
    write_picks(brick_ref, picks_ref, across_ref)
    forward_lines(own_ref, brick_ref, across_ref, table_in, sent_refs, *refs[len(SEND) + 2 :])


def forward_later_kernel(own_ref, brick_ref, across_ref, table_in, *refs):
    forward_lines(own_ref, brick_ref, across_ref, table_in, refs[: len(SEND)], *refs[len(SEND) :])


def grid_rows(slabs, plane, xq, tx):
    start = ((plane * 4 + xq) * SPOTS + tx * 4) * slabs
    return pl.ds(pl.multiple_of(start, 4 * slabs), 4 * slabs)


def plane_product(plane_ref, lines):
    high, rest = split(lines)
    rows = plane_ref.shape[0]
    if plane_ref.shape[1] == 3 * high.shape[0]:
        return dot(plane_ref[...], jnp.concatenate([high, rest, high], axis=0))
    both = dot(plane_ref[...], jnp.concatenate([high, rest], axis=0))
    return both[: rows // 2] + both[rows // 2 :]


def add_sines(got_refs, plane_ref, grid_ref, finish):
    slabs = len(got_refs)
    for at, got_ref in enumerate(got_refs):
        grid_ref[pl.ds(at, PART_ROWS, stride=slabs), :] = wide(got_ref)

    def planes(tx, xq):
        return jnp.concatenate(
            [grid_ref[grid_rows(slabs, plane, xq, tx), :] for plane in range(PART_PLANES)], axis=0
        )

    def sines(tx, _):
        modes = plane_product(plane_ref, jnp.concatenate([planes(tx, xq) for xq in range(4)], axis=1))
        for xq in range(4):
            finish(tx * 4 + xq, modes[:, xq * LANES : (xq + 1) * LANES])
        return 0

    lax.fori_loop(0, 16, sines, 0, unroll=8)


def down_first_kernel(own_ref, *refs):
    count = len(ARRIVAL)
    planes_ref, base_ref, lam_ref, modes_ref, root_ref, gain_ref, power_ref, grid_ref = refs[count:]
    excess = base_ref[...] + lam_ref[pl.ds(own_ref[0], 1), :]
    spread = jnp.sqrt(excess * (excess + 4.0))
    root_ref[...] = 2.0 / (2.0 + excess + spread)
    gain_ref[...] = 1.0 / spread
    for part in range(2):
        here = pl.ds(part * PLANES // 2, PLANES // 2)
        square = root_ref[here, :] * root_ref[here, :]

        def raised(step, power):
            power_ref[step, here, :] = power
            return power * square

        lax.fori_loop(0, STEPS, raised, jnp.ones(square.shape, jnp.float32), unroll=8)

    def finish(line, values):
        modes_ref[line] = values

    add_sines(refs[:count], planes_ref.at[own_ref[0]], grid_ref, finish)


def down_later_kernel(own_ref, *refs):
    count = len(ARRIVAL)
    sums_ref, root_ref, planes_ref, walk_ref, end_ref, grid_ref, modes_ref, last_ref = refs[count:]

    def finish(line, values):
        modes_ref[line] = sums_ref[line] + values

    add_sines(refs[:count], planes_ref.at[own_ref[0]], grid_ref, finish)
    part_rows = 64
    low = low_half((part_rows, LANES))
    for part in range(PLANES // part_rows):
        here = pl.ds(part * part_rows, part_rows)
        root = root_ref[here, :]
        square = root * root

        def walk(step, held):
            ahead, behind = modes_ref[step, here, :], modes_ref[STEPS - 1 - step, here, :]
            own = jnp.where(low, behind, ahead)
            other = pltpu.roll(jnp.where(low, ahead, behind), HALF, 1)
            held = square * held + (own + root * other)
            walk_ref[step, here, :] = held
            return held

        last_ref[here, :] = lax.fori_loop(0, STEPS, walk, jnp.zeros((part_rows, LANES), jnp.float32), unroll=8)
    last = last_ref[...]
    level = level_of(jnp.max(jnp.abs(last), axis=0, keepdims=True))
    end_ref[:PLANES, :] = fixed_of(last * inverse_of(level))
    end_ref[PLANES:, :] = head_of(level)


def local_kernel(walk_ref, root_ref, gain_ref, local_ref):
    part_rows = 64
    low = low_half((part_rows, LANES))
    for part in range(PLANES // part_rows):
        here = pl.ds(part * part_rows, part_rows)
        root, gain = root_ref[here, :], gain_ref[here, :]
        zero = jnp.zeros(root.shape, jnp.float32)

        def line(step, ahead_before, behind_after):
            near = jnp.where(low, walk_ref[STEPS - 1 - step, here, :], walk_ref[step, here, :])
            far = pltpu.roll(jnp.where(low, behind_after, ahead_before), HALF, 1)
            local_ref[step, here, :] = gain * (near + root * far)

        def inner(step, _):
            line(step, walk_ref[step - 1, here, :], walk_ref[STEPS - 2 - step, here, :])
            return 0

        line(0, zero, walk_ref[STEPS - 2, here, :])
        lax.fori_loop(1, STEPS - 1, inner, 0, unroll=6)
        line(STEPS - 1, walk_ref[STEPS - 2, here, :], zero)


def up_kernel(own_ref, local_ref, power_ref, root_ref, gain_ref, *refs):
    end_refs, plane_ref = refs[:GROUPS], refs[GROUPS].at[own_ref[0]]
    count = GROUPS + 1 + len(SEND)
    sent_refs = refs[GROUPS + 1 : count]
    rise_ref, fall_ref, grid_ref, level_ref = refs[count:]
    low = low_half((PLANES, LANES))
    root = root_ref[...]
    square = root * root
    across = square
    for _ in range(6):
        across = across * across
    around = across
    for _ in range(2):
        around = around * around
    ends = [wide(end_ref) for end_ref in end_refs]
    entering = jnp.zeros((PLANES, LANES), jnp.float32)
    for step in range(GROUPS - 1, -1, -1):
        entering = entering * across + jnp.where(low, ends[GROUPS - 1 - step], ends[(step + 1) % GROUPS])
    entering = gain_ref[...] * entering / (1.0 - around)
    straight, turned = square * entering, root * pltpu.roll(entering, HALF, 1)
    rise_ref[...] = jnp.where(low, turned, straight)
    fall_ref[...] = jnp.where(low, straight, turned)
    slabs = len(sent_refs)

    def solved(step):
        reach = rise_ref[...] * power_ref[step] + fall_ref[...] * power_ref[STEPS - 1 - step]
        return local_ref[step] + reach

    def sines(tx, most):
        lines = plane_product(plane_ref, jnp.concatenate([solved(tx * 4 + xq) for xq in range(4)], axis=1))
        for xq in range(4):
            part = lines[:, xq * LANES : (xq + 1) * LANES]
            most = jnp.maximum(most, jnp.max(jnp.abs(part).reshape(4 * BZ, slabs, LANES), axis=0))
            for plane in range(BZ):
                grid_ref[grid_rows(slabs, plane, xq, tx), :] = part[plane * 4 * slabs : (plane + 1) * 4 * slabs]
        return most

    most = lax.fori_loop(0, 16, sines, jnp.zeros((slabs, LANES), jnp.float32), unroll=8)
    level_ref[...] = level_of(most)
    for at, sent_ref in enumerate(sent_refs):
        level = level_ref[at : at + 1, :]
        sent_ref[:ROWS, :] = fixed_of(grid_ref[pl.ds(at, ROWS, stride=slabs), :] * inverse_of(level))
        sent_ref[ROWS:, :] = head_of(level)


def take_lines(own_ref, offsets, got_refs, left_ref, lines_ref):
    own = own_ref[0]
    pairs = list(dict.fromkeys(offset // 2 for offset in offsets))
    for offset, got_ref in zip(offsets, got_refs):
        lines_ref[2 * pairs.index(offset // 2) + ((own ^ offset) & 1)] = wide(got_ref)
    low = low_half((DOT_ROWS, LANES))
    for at in range(len(pairs)):
        for start in range(0, ROWS, DOT_ROWS):
            here = slice(start, start + DOT_ROWS)
            write_left(at, here, even_odd(lines_ref[2 * at, here, :], lines_ref[2 * at + 1, here, :], low), left_ref)
    return [(own >> 1) ^ pair for pair in pairs]


def point_parts(pair, cosines, sines, weight_ref):
    for ty in range(4):
        part = weight_ref[pair, ty] * cosines + weight_ref[pair, 4 + ty] * sines
        yield ty, part
        yield ty + 4, weight_ref[pair, 8] * part


def reply_first_kernel(own_ref, weight_ref, *refs):
    count = len(TAKE_FIRST)
    table_ref, sums_ref, lines_ref, left_ref = refs[count:]
    pairs = take_lines(own_ref, TAKE_FIRST, refs[:count], left_ref, lines_ref)
    for at, pair in enumerate(pairs):
        for part in range(ROWS // DOT_ROWS):
            here = slice(part * DOT_ROWS, (part + 1) * DOT_ROWS)
            cosines, sines = line_product(at, here, left_ref, table_ref[pair])
            for ty, values in point_parts(pair, cosines, sines, weight_ref):
                sums_ref[ty, here, :] = values if at == 0 else sums_ref[ty, here, :] + values


def reply_later_kernel(own_ref, weight_ref, *refs):
    count = len(TAKE_LATER)
    sums_ref, picks_ref, table_ref, out_ref, lines_ref, left_ref, pot_ref = refs[count:]
    [pair] = take_lines(own_ref, TAKE_LATER, refs[:count], left_ref, lines_ref)
    for part in range(ROWS // DOT_ROWS):
        here = slice(part * DOT_ROWS, (part + 1) * DOT_ROWS)
        cosines, sines = line_product(0, here, left_ref, table_ref[pair])
        for ty, values in point_parts(pair, cosines, sines, weight_ref):
            values = (sums_ref[ty, here, :] + values).astype(jnp.bfloat16)
            for one in range(DOT_ROWS // SPOTS):
                q = part * (DOT_ROWS // SPOTS) + one
                pot_ref[ty * SPOTS : (ty + 1) * SPOTS, q * LANES : (q + 1) * LANES] = values[
                    one * SPOTS : (one + 1) * SPOTS
                ]
    for q in range(0, BRICK_ROWS, 4):
        there = slice(q * LANES, (q + 4) * LANES)
        out_ref[:, there] = dot(picks_ref[...], pot_ref[:, there]).astype(jnp.bfloat16)


def unpack_kernel(back_ref, got_ref, out_ref):
    for q in range(0, BRICK_ROWS, 4):
        there = slice(q * LANES, (q + 4) * LANES)
        out_ref[:, there] = dot(back_ref[...], got_ref[:, there]).astype(jnp.bfloat16)


def call(kernel, name, operands, spaces, outs, places, scratch, vmem=VMEM_BYTES):
    return pl.pallas_call(
        kernel,
        out_shape=outs,
        in_specs=[pl.BlockSpec(memory_space=space) for space in spaces],
        out_specs=[pl.BlockSpec(memory_space=space) for space in places],
        scratch_shapes=scratch,
        compiler_params=pltpu.CompilerParams(vmem_limit_bytes=vmem),
        name=name,
    )(*operands)


def on_device_8x4(bricks, owners, tile_ids, counts):
    V, S, H = pltpu.VMEM, pltpu.SMEM, pltpu.HBM
    f32, bf16, i32, i16 = jnp.float32, jnp.bfloat16, jnp.int32, jnp.int16
    shape, dma = jax.ShapeDtypeStruct, pltpu.SemaphoreType.DMA
    brick_rows = bricks.shape[0]
    lines_in, lines_out = (jnp.asarray(each) for each in line_tables())
    weights = jnp.asarray(class_weights())
    lines_in = pltpu.with_memory_space_constraint(lines_in, H)
    planes_in = [jnp.asarray(plane_tables(ARRIVAL, planes, False)) for planes in ((0, 1), (2, 3))]
    planes_out = jnp.asarray(plane_tables(SEND, range(BZ), True))
    base, lam = (jnp.asarray(each) for each in mode_tables())
    own = lax.axis_index("gz").astype(i32).reshape(1)
    sent_shape = shape((ROWS + HEAD_ROWS, LANES), i16)
    end_shape = shape((PLANES + HEAD_ROWS, LANES), i16)
    cube, flat, sums_shape = (STEPS, PLANES, LANES), (PLANES, LANES), (8, ROWS, LANES)
    line, packed = (ROWS, LANES), [(SLOTS, PART_CELLS + LANES), (SLOTS, PART_CELLS)]
    part_shape = shape((PART_ROWS + HEAD_ROWS, LANES), i16)

    def all_ways(values):
        return lax.all_to_all(values, ("gz", "ma"), split_axis=0, concat_axis=0, tiled=True)

    def over_slabs(offset, values):
        return lax.ppermute(values, "gz", [(g, g ^ offset) for g in range(SLABS)]) if offset else values

    def round_groups(values, step):
        return lax.ppermute(values, "ma", [(m, (m + step) % GROUPS) for m in range(GROUPS)]) if step else values

    def exchanged(sent):
        sent = dict(zip(SEND, sent))
        return [over_slabs(offset, sent[offset]) for offset in ARRIVAL]

    *outgoing, back = call(
        pack_kernel,
        "pack",
        (owners.reshape(brick_rows), tile_ids, counts, bricks),
        [H] * 4,
        [shape(each, bf16) for each in packed] + [shape((brick_rows, SLOTS), bf16)],
        [H, H, V],
        [
            S((brick_rows,), i32),
            S((brick_rows,), i32),
            S((1,), i32),
            V(bricks.shape, bf16),
            V((SLOTS + PAIR_SLOTS, brick_rows), f32),
            V((SLOTS + PAIR_SLOTS, LANES), f32),
            *[V(each, bf16) for each in packed],
            S((DOMAINS,), i32),
            dma((4,)),
            dma((8,)),
        ],
        ALL_VMEM_BYTES,
    )
    incoming = [all_ways(each) for each in outgoing]
    forward_scratch = [
        V((PAIRS, 2 * PART_ROWS, 2 * LANES), bf16),
        V((len(SEND), *part_shape.shape), i16),
        V(lines_in.shape, bf16),
        dma((1,)),
    ]
    *sent, picks, across = call(
        forward_first_kernel,
        "forward_first",
        (own, incoming[0], lines_in),
        [S, V, H],
        [part_shape] * len(SEND) + [shape((SLOTS, TILES), bf16), shape((TILES, SLOTS), bf16)],
        [V] * (len(SEND) + 2),
        forward_scratch,
    )
    first = exchanged(sent)
    second, first[1], first[2] = lax.optimization_barrier((incoming[1], first[1], first[2]))
    sent = call(
        forward_later_kernel,
        "forward_later",
        (own, second, across, lines_in),
        [S, V, V, H],
        [part_shape] * len(SEND),
        [V] * len(SEND),
        forward_scratch,
    )
    later = exchanged(sent)
    sums, root, gain, power = call(
        down_first_kernel,
        "down_first",
        (own, *first, planes_in[0], base, lam),
        [S] + [V] * (len(first) + 3),
        [shape(cube, f32), shape(flat, f32), shape(flat, f32), shape(cube, f32)],
        [V] * 4,
        [
            V((len(first) * PART_ROWS, LANES), f32),
        ],
    )
    walk, end = call(
        down_later_kernel,
        "down_later",
        (own, *later, sums, root, planes_in[1]),
        [S] + [V] * (len(later) + 3),
        [shape(cube, f32), end_shape],
        [V, V],
        [
            V((len(later) * PART_ROWS, LANES), f32),
            V(cube, f32),
            V(flat, f32),
        ],
    )
    ends = [round_groups(end, step) for step in range(GROUPS)]
    (local,) = call(local_kernel, "local", (walk, root, gain), [V] * 3, [shape(cube, f32)], [V], [])
    sent = call(
        up_kernel,
        "up",
        (own, local, power, root, gain, *ends, planes_out),
        [S] + [V] * (5 + GROUPS),
        [sent_shape] * len(SEND),
        [V] * len(SEND),
        [
            V(flat, f32),
            V(flat, f32),
            V((len(SEND) * ROWS, LANES), f32),
            V((len(SEND), LANES), f32),
        ],
    )
    got = exchanged(sent)
    first, later = got[: len(TAKE_FIRST)], got[len(TAKE_FIRST) :]
    (sums,) = call(
        reply_first_kernel,
        "reply_first",
        (own, weights, *first, lines_out),
        [S, S] + [V] * (len(first) + 1),
        [shape(sums_shape, f32)],
        [V],
        [V((len(first), *line), f32), V((len(first) // 2, 2 * ROWS, 2 * LANES), bf16)],
    )
    (replies,) = call(
        reply_later_kernel,
        "reply_later",
        (own, weights, *later, sums, picks, lines_out),
        [S, S] + [V] * (len(later) + 3),
        [shape((SLOTS, CELLS), bf16)],
        [V],
        [
            V((len(later), *line), f32),
            V((len(later) // 2, 2 * ROWS, 2 * LANES), bf16),
            V((TILES, CELLS), bf16),
        ],
    )
    (result,) = call(
        unpack_kernel,
        "unpack",
        (back, all_ways(replies)),
        [V, V],
        [shape((brick_rows, CELLS), bf16)],
        [V],
        [],
    )
    return result


def solution(mesh):
    in_specs = (P(("gz", "ma"), None), P(("gz", "ma"), None), P(("gz", "ma")), P(("gz", "ma")))
    out_specs = P(("gz", "ma"), None)
    body = on_device_8x4 if (mesh.shape["gz"], mesh.shape["ma"]) == (SLABS, GROUPS) else on_device
    return jax.shard_map(body, mesh=mesh, in_specs=in_specs, out_specs=out_specs, check_vma=False)
```

```python
import math

import jax
import jax.numpy as jnp
import ml_dtypes
import numpy as np
from jax import lax
from jax.experimental import pallas as pl
from jax.experimental.pallas import tpu as pltpu
from jax.sharding import PartitionSpec as P

NX = 512
NY = 512
SCREEN = 16
BZ = 4
BX = 8
BY = 64
CZ = 16


def hartley(length):
    indices = jnp.arange(length, dtype=jnp.int32)
    products = indices[:, None] * indices[None, :] % length
    angles = 2.0 * math.pi / length * products.astype(jnp.float32)
    return (jnp.cos(angles) + jnp.sin(angles)) / math.sqrt(length)


def second_difference(length, indices):
    return 2.0 - 2.0 * jnp.cos(2.0 * math.pi / length * indices.astype(jnp.float32))


def thomas(right_side, diagonal):
    start_zero = jnp.zeros(right_side.shape[1:], jnp.float32)

    def down(state_pair, plane):
        factor = 1.0 / (diagonal - state_pair[0])
        partial_value = (plane + state_pair[1]) * factor
        return ((factor, partial_value), (factor, partial_value))

    _, (factors, partials) = lax.scan(down, (start_zero, start_zero), right_side)

    def upward(beyond, factor_partial):
        solved = factor_partial[1] + factor_partial[0] * beyond
        return (solved, solved)

    _, solutions = lax.scan(upward, start_zero, (factors, partials), reverse=True)
    return solutions


def regroup(values):
    return lax.all_to_all(values, "ma", split_axis=2, concat_axis=1, tiled=True)


def on_device(bricks, owners, tile_ids, counts):
    domains = lax.axis_size(("gz", "ma"))
    group_count = lax.axis_size("ma")
    slab_count = lax.axis_size("gz")
    brick_rows, brick_cells = bricks.shape
    slot_count = max(2, 2 * brick_rows // domains)
    local_x = NX // group_count
    local_y = NY // group_count
    tiles_dev = CZ // BZ * (local_x // BX) * (NY // BY)
    highest = lax.Precision.HIGHEST
    target = owners[:, 0]
    row_order = jnp.arange(brick_rows, dtype=jnp.int32)
    earlier_same = (target[:, None] == target[None, :]) & (row_order[None, :] < row_order[:, None])
    within = jnp.sum(earlier_same.astype(jnp.int32), axis=1)
    slot_of = target * slot_count + within
    is_live = row_order < counts[0]
    loaded = jnp.where(is_live[:, None], bricks, jnp.zeros_like(bricks))
    outgoing = jnp.zeros((domains * slot_count, brick_cells), jnp.bfloat16).at[slot_of].set(loaded)
    out_ids = jnp.full((domains * slot_count,), tiles_dev, jnp.int32).at[slot_of].set(tile_ids)
    incoming, in_ids = (
        lax.all_to_all(outgoing, ("gz", "ma"), split_axis=0, concat_axis=0, tiled=True),
        lax.all_to_all(out_ids, ("gz", "ma"), split_axis=0, concat_axis=0, tiled=True),
    )
    picker = (jnp.arange(tiles_dev, dtype=jnp.int32)[:, None] == in_ids[None, :]).astype(
        jnp.bfloat16
    )
    deposit = jnp.dot(picker, incoming, preferred_element_type=jnp.float32)
    charge = deposit.reshape(CZ // BZ, local_x // BX, NY // BY, BZ, BX, BY)
    charge = charge.transpose(0, 3, 1, 4, 2, 5).reshape(CZ, local_x, NY)
    table_x = hartley(NX)
    table_y = hartley(NY)
    along_y = jnp.einsum("zxy,ky->zxk", charge, table_y, precision=highest)
    gathered_x = regroup(along_y)
    spectrum = jnp.einsum("zxk,jx->zjk", gathered_x, table_x, precision=highest)
    columns = lax.axis_index("ma") * local_y + jnp.arange(local_y, dtype=jnp.int32)
    lam_y = second_difference(NY, columns)
    screening = 1.0 / (SCREEN * SCREEN)
    slab_index = lax.axis_index("gz")
    lam_x = second_difference(NX, jnp.arange(NX, dtype=jnp.int32))
    diagonal = 2.0 + screening + lam_x[:, None] + lam_y[None, :]
    interior = spectrum[1:]
    particular = thomas(interior, diagonal)
    unit_rhs = jnp.zeros_like(interior).at[0].set(1.0)
    spike = thomas(unit_rhs, diagonal)
    near_weight = spike[0]
    far_weight = spike[-1]
    head_term = spectrum[0] + particular[0]
    tail_term = particular[-1]
    reduced_first = diagonal - near_weight
    reduced_rest = diagonal - 2.0 * near_weight
    start_zero = jnp.zeros_like(diagonal)
    heads, tails = (
        lax.all_gather(head_term[None], "gz", axis=0, tiled=True),
        lax.all_gather(tail_term[None], "gz", axis=0, tiled=True),
    )
    before = jnp.concatenate([start_zero[None], tails[:-1]], axis=0)
    sources = heads + before

    def chain_down(state_pair, packed):
        source, position = packed
        base_term = jnp.where(position == 0, reduced_first, reduced_rest)
        pivot_now = 1.0 / (base_term - far_weight * far_weight * state_pair[0])
        forward_part = pivot_now * (source + far_weight * state_pair[1])
        return ((pivot_now, forward_part), (pivot_now, forward_part))

    _, (pivots, forwards) = lax.scan(
        chain_down, (start_zero, start_zero), (sources, jnp.arange(slab_count, dtype=jnp.int32))
    )

    def chain_up(beyond, packed):
        plane_value = packed[1] + far_weight * packed[0] * beyond
        return (plane_value, plane_value)

    _, separators = lax.scan(chain_up, start_zero, (pivots, forwards), reverse=True)
    padded_sep = jnp.concatenate([separators, start_zero[None]], axis=0)
    own_plane = lax.dynamic_index_in_dim(padded_sep, slab_index, 0, keepdims=False)
    next_plane = lax.dynamic_index_in_dim(padded_sep, slab_index + 1, 0, keepdims=False)
    interior_sol = particular + own_plane[None] * spike + next_plane[None] * spike[::-1]
    modal = jnp.concatenate([own_plane[None], interior_sol], axis=0)
    back_x = jnp.einsum("zjk,jx->zkx", modal, table_x, precision=highest)
    gathered_y = regroup(back_x)
    potential = jnp.einsum("zkx,ky->zxy", gathered_y, table_y, precision=highest)
    pot_tiles = potential.reshape(CZ // BZ, BZ, local_x // BX, BX, NY // BY, BY)
    pot_tiles = (
        pot_tiles.transpose(0, 2, 4, 1, 3, 5).reshape(tiles_dev, brick_cells).astype(jnp.bfloat16)
    )
    padded_tiles = jnp.concatenate([pot_tiles, jnp.zeros((1, brick_cells), jnp.bfloat16)], axis=0)
    replies = padded_tiles[in_ids]
    returned = lax.all_to_all(replies, ("gz", "ma"), split_axis=0, concat_axis=0, tiled=True)
    result = returned[slot_of]
    return jnp.where(is_live[:, None], result, jnp.zeros_like(result))


DOMAINS = 32
GROUPS = 4
SLABS = 8
SEND = (4, 2, 5, 3, 0, 1, 6, 7)
ARRIVAL_FIRST = (0, 1, 4, 2, 5, 3, 6, 7)
ARRIVAL = (0, 4, 2, 5, 3, 1, 6, 7)
PARTS = 2
PART_PLANES = 2
TAKE_FIRST = (0, 4, 2, 5, 3, 1)
TAKE_LATER = (6, 7)
PAIR_SLOTS = 8
SLOTS = DOMAINS * PAIR_SLOTS
TILES = 512
BRICK_ROWS = 16
CELLS = 2048
LANES = 128
HALF = 64
SPOTS = 64
ROWS = BRICK_ROWS * SPOTS
PART_ROWS = ROWS // PARTS
PART_CELLS = CELLS // PARTS
DOT_ROWS = 512
PAIRS = 4
CLASSES = (0, 4, 1, 7, 2, 6, 3, 5)
HEAD_ROWS = 16
STEPS = 64
PLANES = 128
FULL = 32700.0
LOG_UNIT = 128.0
VMEM_BYTES = 24 * 1024 * 1024
ALL_VMEM_BYTES = 60 * 1024 * 1024


def split_table(table):
    high = table.astype(ml_dtypes.bfloat16)
    low = (table - high.astype(np.float64)).astype(ml_dtypes.bfloat16)
    return high, low


def line_tables():
    iy, k2 = np.arange(HALF)[:, None], np.arange(HALF)[None, :]
    tables = []
    for pair in range(PAIRS):
        table = np.zeros((LANES, LANES))
        for one in range(2):
            angle = 2.0 * np.pi / NY * (iy * (CLASSES[2 * pair + one] + 8 * k2) % NY)
            cosine, sine = np.cos(angle) / np.sqrt(NY), np.sin(angle) / np.sqrt(NY)
            there = slice(one * HALF, (one + 1) * HALF)
            if pair == 0:
                table[there, there] = cosine + sine
            else:
                table[:HALF, there] = cosine + sine
                table[HALF:, there] = (cosine - sine) * (1 - 2 * one)
        tables.append(table)

    def stacked(table):
        high, low = split_table(table)
        return np.concatenate(
            [np.concatenate([high, low], axis=1), np.concatenate([high, np.zeros_like(low)], axis=1)], axis=0
        )

    return np.stack([stacked(table) for table in tables]), np.stack([stacked(table.T) for table in tables])


def class_weights():
    pair, ty = np.arange(PAIRS)[:, None], np.arange(4)[None, :]
    cosine, sine = np.cos(np.pi / 4.0 * pair * ty), np.sin(np.pi / 4.0 * pair * ty)
    sine[0] = (-1.0) ** np.arange(4)
    sign = (-1.0) ** pair * np.ones((1, 4))
    return np.concatenate([cosine, sine, sign], axis=1).astype(np.float32)


def plane_tables(offsets, planes, turned):
    index = np.arange(PLANES)
    table = np.sqrt(2.0 / (PLANES + 1)) * np.sin(
        np.pi / (PLANES + 1) * ((index[:, None] + 1) * (index[None, :] + 1) % (2 * PLANES + 2))
    )
    each = []
    for own in range(SLABS):
        slabs = np.array([own ^ offset for offset in offsets])
        plane, tz = np.array(planes)[:, None, None], np.arange(BZ)[None, :, None]
        part = table[:, (slabs * CZ + tz * BZ + plane).reshape(-1)]
        high, low = split_table(part.T if turned else part)
        if 3 * high.shape[1] <= 2 * LANES:
            each.append(np.concatenate([high, high, low], axis=1))
            continue
        top = np.concatenate([high, high], axis=1)
        bottom = np.concatenate([low, np.zeros_like(low)], axis=1)
        each.append(np.concatenate([top, bottom], axis=0))
    return np.stack(each)


def mode_tables():
    mu = 2.0 - 2.0 * np.cos(np.pi / (PLANES + 1) * (np.arange(PLANES) + 1))
    base = np.broadcast_to((mu + 1.0 / (SCREEN * SCREEN))[:, None], (PLANES, LANES))
    lam = 2.0 - 2.0 * np.cos(2.0 * np.pi / NY * np.arange(NY))
    lam = np.stack([lam[number::8] for number in CLASSES])
    return base.astype(np.float32), np.concatenate([lam, lam], axis=1).astype(np.float32)


def low_half(shape):
    return lax.broadcasted_iota(jnp.int32, shape, len(shape) - 1) < HALF


def split(values):
    high = values.astype(jnp.bfloat16)
    return high, (values - high.astype(jnp.float32)).astype(jnp.bfloat16)


def dot(left, right):
    return jnp.dot(left, right, preferred_element_type=jnp.float32)


def start_copies(pairs, sems):
    copies = [pltpu.make_async_copy(source, place, sems.at[at]) for at, (source, place) in enumerate(pairs)]
    for each in copies:
        each.start()
    return copies


def even_odd(first, second, low):
    crossed = pltpu.roll(jnp.where(low, second, first), HALF, 1)
    return jnp.where(low, first, crossed), jnp.where(low, crossed, second)


def write_left(at, here, lines, left_ref):
    rows = left_ref.shape[1] // 2
    for line, values in enumerate(lines):
        high, rest = split(values)
        there = slice(line * rows + here.start, line * rows + here.stop)
        left_ref[at, there, :LANES] = high
        left_ref[at, there, LANES:] = rest


def line_product(at, here, left_ref, table):
    products = []
    rows = left_ref.shape[1] // 2
    for line in range(2):
        there = slice(line * rows + here.start, line * rows + here.stop)
        both = dot(left_ref[at, there, :], table)
        products.append(both[:, :LANES] + both[:, LANES:])
    return even_odd(*products, low_half(products[0].shape))


def class_sums(points):
    half = [points[ty] + points[ty + 4] for ty in range(4)]
    rest = [points[ty] - points[ty + 4] for ty in range(4)]
    even, odd = half[0] + half[2], half[1] + half[3]
    turn = math.sqrt(0.5)
    across, along = turn * (rest[1] - rest[3]), turn * (rest[1] + rest[3])
    return (
        (even + odd, even - odd),
        (rest[0] + across, rest[2] + along),
        (half[0] - half[2], half[1] - half[3]),
        (rest[0] - across, along - rest[2]),
    )


def level_of(most):
    return jnp.floor(jnp.log2(jnp.maximum(most, 1e-30)) * LOG_UNIT) + 2.0


def inverse_of(level):
    return FULL * jnp.exp2(level * (-1.0 / LOG_UNIT))


def fixed_of(values):
    return jnp.floor(values + 0.5).astype(jnp.int32).astype(jnp.int16)


def head_of(level):
    return jnp.broadcast_to(level, (HEAD_ROWS, LANES)).astype(jnp.int32).astype(jnp.int16)


def unit_of(sent_ref):
    head = sent_ref[sent_ref.shape[0] - HEAD_ROWS :, :].astype(jnp.int32).astype(jnp.float32)
    return jnp.exp2(head[0:1] * (1.0 / LOG_UNIT)) * (1.0 / FULL)


def wide(sent_ref):
    block = sent_ref[: sent_ref.shape[0] - HEAD_ROWS, :]
    return block.astype(jnp.int32).astype(jnp.float32) * unit_of(sent_ref)


def pack_kernel(
    owner_in, tile_in, count_in, brick_in, first_ref, second_ref, back_ref,
    owner_ref, tile_ref, count_ref, brick_ref, pick_ref, head_ref, ready_ref, later_ref, used_ref, sems, out_sems,
):
    copies = start_copies(
        ((owner_in, owner_ref), (tile_in, tile_ref), (count_in, count_ref), (brick_in, brick_ref)), sems
    )
    brick_rows = brick_ref.shape[0]
    head_ref[...] = jnp.full(head_ref.shape, float(TILES), jnp.float32)
    pick_ref[...] = jnp.zeros(pick_ref.shape, jnp.float32)
    for owner in range(DOMAINS):
        used_ref[owner] = 0
    for each in copies[:3]:
        each.wait()
    count = count_ref[0]
    lane = lax.broadcasted_iota(jnp.int32, (1, brick_rows), 1)

    def place(r, _):
        owner = owner_ref[r]
        within = used_ref[owner]
        used_ref[owner] = within + 1
        slot = jnp.where(r < count, owner * PAIR_SLOTS + within, SLOTS)
        tile = tile_ref[r]
        position = (tile & 7) * SPOTS + ((tile >> 3) & 15) * 4 + (tile >> 7)
        pick_ref[pl.ds(slot, 1), :] = jnp.where(lane == r, 1.0, 0.0)
        head_ref[pl.ds(slot, 1), :] = jnp.full((1, LANES), position, jnp.int32).astype(jnp.float32)
        return 0

    lax.fori_loop(0, brick_rows, place, 0, unroll=8)
    copies[3].wait()
    copies = []
    rows = 64
    for at, (out_ref, held_ref) in enumerate(((first_ref, ready_ref), (second_ref, later_ref))):
        for part in range(SLOTS // rows):
            here = slice(part * rows, (part + 1) * rows)
            picks = pick_ref[here, :].astype(jnp.bfloat16)
            cells = slice(at * PART_CELLS, (at + 1) * PART_CELLS)
            held_ref[here, :PART_CELLS] = dot(picks, brick_ref[:, cells]).astype(jnp.bfloat16)
            if at == 0:
                head = head_ref[here, :]
                high = jnp.floor(head * (1.0 / 32.0))
                places = jnp.where(low_half(head.shape), high, head - 32.0 * high)
                held_ref[here, PART_CELLS:] = places.astype(jnp.bfloat16)
            some = pl.ds(part * rows, rows)
            copies.append(pltpu.make_async_copy(held_ref.at[some], out_ref.at[some], out_sems.at[4 * at + part]))
            copies[-1].start()
    for part in range(SLOTS // LANES):
        here = slice(part * LANES, (part + 1) * LANES)
        back_ref[:, here] = pick_ref[here, :].T.astype(jnp.bfloat16)
    for each in copies:
        each.wait()


def write_picks(brick_ref, picks_ref, across_ref):
    for part in range(SLOTS // LANES):
        here = slice(part * LANES, (part + 1) * LANES)
        head = brick_ref[here, PART_CELLS:].astype(jnp.float32)
        turned = pltpu.roll(head, HALF, 1)
        low = low_half(head.shape)
        places = (jnp.where(low, head, turned) * 32.0 + jnp.where(low, turned, head)).astype(jnp.int32)
        for block in range(TILES // LANES):
            there = slice(block * LANES, (block + 1) * LANES)
            lane = lax.broadcasted_iota(jnp.int32, (LANES, LANES), 1) + block * LANES
            square = jnp.where(places == lane, 1.0, 0.0)
            picks_ref[here, there] = square.astype(jnp.bfloat16)
            across_ref[there, here] = square.T.astype(jnp.bfloat16)


def forward_lines(own_ref, brick_ref, across_ref, table_in, sent_refs, left_ref, lines_ref, table_ref, sems):
    [copy] = start_copies(((table_in, table_ref),), sems)
    low = low_half((SPOTS, LANES))
    for q in range(0, BRICK_ROWS // PARTS, 4):
        charge = dot(across_ref[...], brick_ref[:, q * LANES : (q + 4) * LANES])
        for one in range(4):
            there = slice(one * LANES, (one + 1) * LANES)
            here = slice((q + one) * SPOTS, (q + one + 1) * SPOTS)
            points = [charge[ty * SPOTS : (ty + 1) * SPOTS, there] for ty in range(8)]
            for pair, (cosines, sines) in enumerate(class_sums(points)):
                write_left(pair, here, even_odd(cosines, sines, low), left_ref)
    copy.wait()
    for pair in range(PAIRS):
        for one, values in enumerate(line_product(pair, slice(0, PART_ROWS), left_ref, table_ref[pair])):
            most = jnp.max(jnp.abs(values).reshape(PART_ROWS // 8, 8, LANES), axis=0)
            level = level_of(jnp.max(most, axis=0, keepdims=True))
            lines_ref[2 * pair + one, :PART_ROWS, :] = fixed_of(values * inverse_of(level))
            lines_ref[2 * pair + one, PART_ROWS:, :] = head_of(level)
    for offset, sent_ref in zip(SEND, sent_refs):
        sent_ref[...] = lines_ref[own_ref[0] ^ offset]


def forward_first_kernel(own_ref, brick_ref, table_in, *refs):
    sent_refs, (picks_ref, across_ref) = refs[: len(SEND)], refs[len(SEND) : len(SEND) + 2]
    write_picks(brick_ref, picks_ref, across_ref)
    forward_lines(own_ref, brick_ref, across_ref, table_in, sent_refs, *refs[len(SEND) + 2 :])


def forward_later_kernel(own_ref, brick_ref, across_ref, table_in, *refs):
    forward_lines(own_ref, brick_ref, across_ref, table_in, refs[: len(SEND)], *refs[len(SEND) :])


def grid_rows(slabs, plane, xq, tx):
    start = ((plane * 4 + xq) * SPOTS + tx * 4) * slabs
    return pl.ds(pl.multiple_of(start, 4 * slabs), 4 * slabs)


def plane_product(plane_ref, lines):
    high, rest = split(lines)
    rows = plane_ref.shape[0]
    if plane_ref.shape[1] == 3 * high.shape[0]:
        return dot(plane_ref[...], jnp.concatenate([high, rest, high], axis=0))
    both = dot(plane_ref[...], jnp.concatenate([high, rest], axis=0))
    return both[: rows // 2] + both[rows // 2 :]


def add_sines(got_refs, plane_ref, grid_ref, finish):
    slabs = len(got_refs)
    for at, got_ref in enumerate(got_refs):
        grid_ref[pl.ds(at, PART_ROWS, stride=slabs), :] = wide(got_ref)

    def planes(tx, xq):
        return jnp.concatenate(
            [grid_ref[grid_rows(slabs, plane, xq, tx), :] for plane in range(PART_PLANES)], axis=0
        )

    def sines(tx, _):
        modes = plane_product(plane_ref, jnp.concatenate([planes(tx, xq) for xq in range(4)], axis=1))
        for xq in range(4):
            finish(tx * 4 + xq, modes[:, xq * LANES : (xq + 1) * LANES])
        return 0

    lax.fori_loop(0, 16, sines, 0, unroll=8)


def down_first_kernel(own_ref, *refs):
    count = len(ARRIVAL)
    planes_ref, base_ref, lam_ref, modes_ref, root_ref, gain_ref, power_ref, grid_ref = refs[count:]
    excess = base_ref[...] + lam_ref[pl.ds(own_ref[0], 1), :]
    spread = jnp.sqrt(excess * (excess + 4.0))
    root_ref[...] = 2.0 / (2.0 + excess + spread)
    gain_ref[...] = 1.0 / spread
    for part in range(2):
        here = pl.ds(part * PLANES // 2, PLANES // 2)
        square = root_ref[here, :] * root_ref[here, :]

        def raised(step, power):
            power_ref[step, here, :] = power
            return power * square

        lax.fori_loop(0, STEPS, raised, jnp.ones(square.shape, jnp.float32), unroll=8)

    def finish(line, values):
        modes_ref[line] = values

    add_sines(refs[:count], planes_ref.at[own_ref[0]], grid_ref, finish)


def down_later_kernel(own_ref, *refs):
    count = len(ARRIVAL)
    sums_ref, root_ref, planes_ref, walk_ref, end_ref, grid_ref, modes_ref, last_ref = refs[count:]

    def finish(line, values):
        modes_ref[line] = sums_ref[line] + values

    add_sines(refs[:count], planes_ref.at[own_ref[0]], grid_ref, finish)
    part_rows = 64
    low = low_half((part_rows, LANES))
    for part in range(PLANES // part_rows):
        here = pl.ds(part * part_rows, part_rows)
        root = root_ref[here, :]
        square = root * root

        def walk(step, held):
            ahead, behind = modes_ref[step, here, :], modes_ref[STEPS - 1 - step, here, :]
            own = jnp.where(low, behind, ahead)
            other = pltpu.roll(jnp.where(low, ahead, behind), HALF, 1)
            held = square * held + (own + root * other)
            walk_ref[step, here, :] = held
            return held

        last_ref[here, :] = lax.fori_loop(0, STEPS, walk, jnp.zeros((part_rows, LANES), jnp.float32), unroll=8)
    last = last_ref[...]
    level = level_of(jnp.max(jnp.abs(last), axis=0, keepdims=True))
    end_ref[:PLANES, :] = fixed_of(last * inverse_of(level))
    end_ref[PLANES:, :] = head_of(level)


def local_kernel(walk_ref, root_ref, gain_ref, local_ref):
    part_rows = 64
    low = low_half((part_rows, LANES))
    for part in range(PLANES // part_rows):
        here = pl.ds(part * part_rows, part_rows)
        root, gain = root_ref[here, :], gain_ref[here, :]
        zero = jnp.zeros(root.shape, jnp.float32)

        def line(step, ahead_before, behind_after):
            near = jnp.where(low, walk_ref[STEPS - 1 - step, here, :], walk_ref[step, here, :])
            far = pltpu.roll(jnp.where(low, behind_after, ahead_before), HALF, 1)
            local_ref[step, here, :] = gain * (near + root * far)

        def inner(step, _):
            line(step, walk_ref[step - 1, here, :], walk_ref[STEPS - 2 - step, here, :])
            return 0

        line(0, zero, walk_ref[STEPS - 2, here, :])
        lax.fori_loop(1, STEPS - 1, inner, 0, unroll=6)
        line(STEPS - 1, walk_ref[STEPS - 2, here, :], zero)


def up_kernel(own_ref, local_ref, power_ref, root_ref, gain_ref, *refs):
    end_refs, plane_ref = refs[:GROUPS], refs[GROUPS].at[own_ref[0]]
    count = GROUPS + 1 + len(SEND)
    sent_refs = refs[GROUPS + 1 : count]
    rise_ref, fall_ref, grid_ref, level_ref = refs[count:]
    low = low_half((PLANES, LANES))
    root = root_ref[...]
    square = root * root
    across = square
    for _ in range(6):
        across = across * across
    around = across
    for _ in range(2):
        around = around * around
    ends = [wide(end_ref) for end_ref in end_refs]
    entering = jnp.zeros((PLANES, LANES), jnp.float32)
    for step in range(GROUPS - 1, -1, -1):
        entering = entering * across + jnp.where(low, ends[GROUPS - 1 - step], ends[(step + 1) % GROUPS])
    entering = gain_ref[...] * entering / (1.0 - around)
    straight, turned = square * entering, root * pltpu.roll(entering, HALF, 1)
    rise_ref[...] = jnp.where(low, turned, straight)
    fall_ref[...] = jnp.where(low, straight, turned)
    slabs = len(sent_refs)

    def solved(step):
        reach = rise_ref[...] * power_ref[step] + fall_ref[...] * power_ref[STEPS - 1 - step]
        return local_ref[step] + reach

    def sines(tx, most):
        lines = plane_product(plane_ref, jnp.concatenate([solved(tx * 4 + xq) for xq in range(4)], axis=1))
        for xq in range(4):
            part = lines[:, xq * LANES : (xq + 1) * LANES]
            most = jnp.maximum(most, jnp.max(jnp.abs(part).reshape(4 * BZ, slabs, LANES), axis=0))
            for plane in range(BZ):
                grid_ref[grid_rows(slabs, plane, xq, tx), :] = part[plane * 4 * slabs : (plane + 1) * 4 * slabs]
        return most

    most = lax.fori_loop(0, 16, sines, jnp.zeros((slabs, LANES), jnp.float32), unroll=8)
    level_ref[...] = level_of(most)
    for at, sent_ref in enumerate(sent_refs):
        level = level_ref[at : at + 1, :]
        sent_ref[:ROWS, :] = fixed_of(grid_ref[pl.ds(at, ROWS, stride=slabs), :] * inverse_of(level))
        sent_ref[ROWS:, :] = head_of(level)


def take_lines(own_ref, offsets, got_refs, left_ref, lines_ref):
    own = own_ref[0]
    pairs = list(dict.fromkeys(offset // 2 for offset in offsets))
    for offset, got_ref in zip(offsets, got_refs):
        lines_ref[2 * pairs.index(offset // 2) + ((own ^ offset) & 1)] = wide(got_ref)
    low = low_half((DOT_ROWS, LANES))
    for at in range(len(pairs)):
        for start in range(0, ROWS, DOT_ROWS):
            here = slice(start, start + DOT_ROWS)
            write_left(at, here, even_odd(lines_ref[2 * at, here, :], lines_ref[2 * at + 1, here, :], low), left_ref)
    return [(own >> 1) ^ pair for pair in pairs]


def point_parts(pair, cosines, sines, weight_ref):
    for ty in range(4):
        part = weight_ref[pair, ty] * cosines + weight_ref[pair, 4 + ty] * sines
        yield ty, part
        yield ty + 4, weight_ref[pair, 8] * part


def reply_first_kernel(own_ref, weight_ref, *refs):
    count = len(TAKE_FIRST)
    table_ref, sums_ref, lines_ref, left_ref = refs[count:]
    pairs = take_lines(own_ref, TAKE_FIRST, refs[:count], left_ref, lines_ref)
    for at, pair in enumerate(pairs):
        for part in range(ROWS // DOT_ROWS):
            here = slice(part * DOT_ROWS, (part + 1) * DOT_ROWS)
            cosines, sines = line_product(at, here, left_ref, table_ref[pair])
            for ty, values in point_parts(pair, cosines, sines, weight_ref):
                sums_ref[ty, here, :] = values if at == 0 else sums_ref[ty, here, :] + values


def reply_later_kernel(own_ref, weight_ref, *refs):
    count = len(TAKE_LATER)
    sums_ref, picks_ref, table_ref, out_ref, lines_ref, left_ref, pot_ref = refs[count:]
    [pair] = take_lines(own_ref, TAKE_LATER, refs[:count], left_ref, lines_ref)
    for part in range(ROWS // DOT_ROWS):
        here = slice(part * DOT_ROWS, (part + 1) * DOT_ROWS)
        cosines, sines = line_product(0, here, left_ref, table_ref[pair])
        for ty, values in point_parts(pair, cosines, sines, weight_ref):
            values = (sums_ref[ty, here, :] + values).astype(jnp.bfloat16)
            for one in range(DOT_ROWS // SPOTS):
                q = part * (DOT_ROWS // SPOTS) + one
                pot_ref[ty * SPOTS : (ty + 1) * SPOTS, q * LANES : (q + 1) * LANES] = values[
                    one * SPOTS : (one + 1) * SPOTS
                ]
    for q in range(0, BRICK_ROWS, 4):
        there = slice(q * LANES, (q + 4) * LANES)
        out_ref[:, there] = dot(picks_ref[...], pot_ref[:, there]).astype(jnp.bfloat16)


def unpack_kernel(back_ref, got_ref, out_ref):
    for q in range(0, BRICK_ROWS, 4):
        there = slice(q * LANES, (q + 4) * LANES)
        out_ref[:, there] = dot(back_ref[...], got_ref[:, there]).astype(jnp.bfloat16)


def call(kernel, name, operands, spaces, outs, places, scratch, vmem=VMEM_BYTES):
    return pl.pallas_call(
        kernel,
        out_shape=outs,
        in_specs=[pl.BlockSpec(memory_space=space) for space in spaces],
        out_specs=[pl.BlockSpec(memory_space=space) for space in places],
        scratch_shapes=scratch,
        compiler_params=pltpu.CompilerParams(vmem_limit_bytes=vmem),
        name=name,
    )(*operands)


def on_device_8x4(bricks, owners, tile_ids, counts):
    V, S, H = pltpu.VMEM, pltpu.SMEM, pltpu.HBM
    f32, bf16, i32, i16 = jnp.float32, jnp.bfloat16, jnp.int32, jnp.int16
    shape, dma = jax.ShapeDtypeStruct, pltpu.SemaphoreType.DMA
    brick_rows = bricks.shape[0]
    lines_in, lines_out = (jnp.asarray(each) for each in line_tables())
    weights = jnp.asarray(class_weights())
    lines_in = pltpu.with_memory_space_constraint(lines_in, H)
    planes_in = [
        jnp.asarray(plane_tables(offsets, planes, False))
        for offsets, planes in ((ARRIVAL_FIRST, (0, 1)), (ARRIVAL, (2, 3)))
    ]
    planes_out = jnp.asarray(plane_tables(SEND, range(BZ), True))
    base, lam = (jnp.asarray(each) for each in mode_tables())
    own = lax.axis_index("gz").astype(i32).reshape(1)
    sent_shape = shape((ROWS + HEAD_ROWS, LANES), i16)
    end_shape = shape((PLANES + HEAD_ROWS, LANES), i16)
    cube, flat, sums_shape = (STEPS, PLANES, LANES), (PLANES, LANES), (8, ROWS, LANES)
    line, packed = (ROWS, LANES), [(SLOTS, PART_CELLS + LANES), (SLOTS, PART_CELLS)]
    part_shape = shape((PART_ROWS + HEAD_ROWS, LANES), i16)

    def all_ways(values):
        return lax.all_to_all(values, ("gz", "ma"), split_axis=0, concat_axis=0, tiled=True)

    def over_slabs(offset, values):
        return lax.ppermute(values, "gz", [(g, g ^ offset) for g in range(SLABS)]) if offset else values

    def round_groups(values, step):
        return lax.ppermute(values, "ma", [(m, (m + step) % GROUPS) for m in range(GROUPS)]) if step else values

    def exchanged(sent, arrival=ARRIVAL):
        sent = dict(zip(SEND, sent))
        return [over_slabs(offset, sent[offset]) for offset in arrival]

    *outgoing, back = call(
        pack_kernel,
        "pack",
        (owners.reshape(brick_rows), tile_ids, counts, bricks),
        [H] * 4,
        [shape(each, bf16) for each in packed] + [shape((brick_rows, SLOTS), bf16)],
        [H, H, V],
        [
            S((brick_rows,), i32),
            S((brick_rows,), i32),
            S((1,), i32),
            V(bricks.shape, bf16),
            V((SLOTS + PAIR_SLOTS, brick_rows), f32),
            V((SLOTS + PAIR_SLOTS, LANES), f32),
            *[V(each, bf16) for each in packed],
            S((DOMAINS,), i32),
            dma((4,)),
            dma((8,)),
        ],
        ALL_VMEM_BYTES,
    )
    incoming = [all_ways(each) for each in outgoing]
    forward_scratch = [
        V((PAIRS, 2 * PART_ROWS, 2 * LANES), bf16),
        V((len(SEND), *part_shape.shape), i16),
        V(lines_in.shape, bf16),
        dma((1,)),
    ]
    *sent, picks, across = call(
        forward_first_kernel,
        "forward_first",
        (own, incoming[0], lines_in),
        [S, V, H],
        [part_shape] * len(SEND) + [shape((SLOTS, TILES), bf16), shape((TILES, SLOTS), bf16)],
        [V] * (len(SEND) + 2),
        forward_scratch,
    )
    first = exchanged(sent, ARRIVAL_FIRST)
    second, first[1], first[2] = lax.optimization_barrier((incoming[1], first[1], first[2]))
    sent = call(
        forward_later_kernel,
        "forward_later",
        (own, second, across, lines_in),
        [S, V, V, H],
        [part_shape] * len(SEND),
        [V] * len(SEND),
        forward_scratch,
    )
    later = exchanged(sent)
    sums, root, gain, power = call(
        down_first_kernel,
        "down_first",
        (own, *first, planes_in[0], base, lam),
        [S] + [V] * (len(first) + 3),
        [shape(cube, f32), shape(flat, f32), shape(flat, f32), shape(cube, f32)],
        [V] * 4,
        [
            V((len(first) * PART_ROWS, LANES), f32),
        ],
    )
    walk, end = call(
        down_later_kernel,
        "down_later",
        (own, *later, sums, root, planes_in[1]),
        [S] + [V] * (len(later) + 3),
        [shape(cube, f32), end_shape],
        [V, V],
        [
            V((len(later) * PART_ROWS, LANES), f32),
            V(cube, f32),
            V(flat, f32),
        ],
    )
    ends = [round_groups(end, step) for step in range(GROUPS)]
    (local,) = call(local_kernel, "local", (walk, root, gain), [V] * 3, [shape(cube, f32)], [V], [])
    sent = call(
        up_kernel,
        "up",
        (own, local, power, root, gain, *ends, planes_out),
        [S] + [V] * (5 + GROUPS),
        [sent_shape] * len(SEND),
        [V] * len(SEND),
        [
            V(flat, f32),
            V(flat, f32),
            V((len(SEND) * ROWS, LANES), f32),
            V((len(SEND), LANES), f32),
        ],
    )
    got = exchanged(sent)
    first, later = got[: len(TAKE_FIRST)], got[len(TAKE_FIRST) :]
    (sums,) = call(
        reply_first_kernel,
        "reply_first",
        (own, weights, *first, lines_out),
        [S, S] + [V] * (len(first) + 1),
        [shape(sums_shape, f32)],
        [V],
        [V((len(first), *line), f32), V((len(first) // 2, 2 * ROWS, 2 * LANES), bf16)],
    )
    (replies,) = call(
        reply_later_kernel,
        "reply_later",
        (own, weights, *later, sums, picks, lines_out),
        [S, S] + [V] * (len(later) + 3),
        [shape((SLOTS, CELLS), bf16)],
        [V],
        [
            V((len(later), *line), f32),
            V((len(later) // 2, 2 * ROWS, 2 * LANES), bf16),
            V((TILES, CELLS), bf16),
        ],
    )
    (result,) = call(
        unpack_kernel,
        "unpack",
        (back, all_ways(replies)),
        [V, V],
        [shape((brick_rows, CELLS), bf16)],
        [V],
        [],
    )
    return result


def solution(mesh):
    in_specs = (P(("gz", "ma"), None), P(("gz", "ma"), None), P(("gz", "ma")), P(("gz", "ma")))
    out_specs = P(("gz", "ma"), None)
    body = on_device_8x4 if (mesh.shape["gz"], mesh.shape["ma"]) == (SLABS, GROUPS) else on_device
    return jax.shard_map(body, mesh=mesh, in_specs=in_specs, out_specs=out_specs, check_vma=False)
```

```python
import math

import jax
import jax.numpy as jnp
import ml_dtypes
import numpy as np
from jax import lax
from jax.experimental import pallas as pl
from jax.experimental.pallas import tpu as pltpu
from jax.sharding import PartitionSpec as P

NX = 512
NY = 512
SCREEN = 16
BZ = 4
BX = 8
BY = 64
CZ = 16


def hartley(length):
    indices = jnp.arange(length, dtype=jnp.int32)
    products = indices[:, None] * indices[None, :] % length
    angles = 2.0 * math.pi / length * products.astype(jnp.float32)
    return (jnp.cos(angles) + jnp.sin(angles)) / math.sqrt(length)


def second_difference(length, indices):
    return 2.0 - 2.0 * jnp.cos(2.0 * math.pi / length * indices.astype(jnp.float32))


def thomas(right_side, diagonal):
    start_zero = jnp.zeros(right_side.shape[1:], jnp.float32)

    def down(state_pair, plane):
        factor = 1.0 / (diagonal - state_pair[0])
        partial_value = (plane + state_pair[1]) * factor
        return ((factor, partial_value), (factor, partial_value))

    _, (factors, partials) = lax.scan(down, (start_zero, start_zero), right_side)

    def upward(beyond, factor_partial):
        solved = factor_partial[1] + factor_partial[0] * beyond
        return (solved, solved)

    _, solutions = lax.scan(upward, start_zero, (factors, partials), reverse=True)
    return solutions


def regroup(values):
    return lax.all_to_all(values, "ma", split_axis=2, concat_axis=1, tiled=True)


def on_device(bricks, owners, tile_ids, counts):
    domains = lax.axis_size(("gz", "ma"))
    group_count = lax.axis_size("ma")
    slab_count = lax.axis_size("gz")
    brick_rows, brick_cells = bricks.shape
    slot_count = max(2, 2 * brick_rows // domains)
    local_x = NX // group_count
    local_y = NY // group_count
    tiles_dev = CZ // BZ * (local_x // BX) * (NY // BY)
    highest = lax.Precision.HIGHEST
    target = owners[:, 0]
    row_order = jnp.arange(brick_rows, dtype=jnp.int32)
    earlier_same = (target[:, None] == target[None, :]) & (row_order[None, :] < row_order[:, None])
    within = jnp.sum(earlier_same.astype(jnp.int32), axis=1)
    slot_of = target * slot_count + within
    is_live = row_order < counts[0]
    loaded = jnp.where(is_live[:, None], bricks, jnp.zeros_like(bricks))
    outgoing = jnp.zeros((domains * slot_count, brick_cells), jnp.bfloat16).at[slot_of].set(loaded)
    out_ids = jnp.full((domains * slot_count,), tiles_dev, jnp.int32).at[slot_of].set(tile_ids)
    incoming, in_ids = (
        lax.all_to_all(outgoing, ("gz", "ma"), split_axis=0, concat_axis=0, tiled=True),
        lax.all_to_all(out_ids, ("gz", "ma"), split_axis=0, concat_axis=0, tiled=True),
    )
    picker = (jnp.arange(tiles_dev, dtype=jnp.int32)[:, None] == in_ids[None, :]).astype(
        jnp.bfloat16
    )
    deposit = jnp.dot(picker, incoming, preferred_element_type=jnp.float32)
    charge = deposit.reshape(CZ // BZ, local_x // BX, NY // BY, BZ, BX, BY)
    charge = charge.transpose(0, 3, 1, 4, 2, 5).reshape(CZ, local_x, NY)
    table_x = hartley(NX)
    table_y = hartley(NY)
    along_y = jnp.einsum("zxy,ky->zxk", charge, table_y, precision=highest)
    gathered_x = regroup(along_y)
    spectrum = jnp.einsum("zxk,jx->zjk", gathered_x, table_x, precision=highest)
    columns = lax.axis_index("ma") * local_y + jnp.arange(local_y, dtype=jnp.int32)
    lam_y = second_difference(NY, columns)
    screening = 1.0 / (SCREEN * SCREEN)
    slab_index = lax.axis_index("gz")
    lam_x = second_difference(NX, jnp.arange(NX, dtype=jnp.int32))
    diagonal = 2.0 + screening + lam_x[:, None] + lam_y[None, :]
    interior = spectrum[1:]
    particular = thomas(interior, diagonal)
    unit_rhs = jnp.zeros_like(interior).at[0].set(1.0)
    spike = thomas(unit_rhs, diagonal)
    near_weight = spike[0]
    far_weight = spike[-1]
    head_term = spectrum[0] + particular[0]
    tail_term = particular[-1]
    reduced_first = diagonal - near_weight
    reduced_rest = diagonal - 2.0 * near_weight
    start_zero = jnp.zeros_like(diagonal)
    heads, tails = (
        lax.all_gather(head_term[None], "gz", axis=0, tiled=True),
        lax.all_gather(tail_term[None], "gz", axis=0, tiled=True),
    )
    before = jnp.concatenate([start_zero[None], tails[:-1]], axis=0)
    sources = heads + before

    def chain_down(state_pair, packed):
        source, position = packed
        base_term = jnp.where(position == 0, reduced_first, reduced_rest)
        pivot_now = 1.0 / (base_term - far_weight * far_weight * state_pair[0])
        forward_part = pivot_now * (source + far_weight * state_pair[1])
        return ((pivot_now, forward_part), (pivot_now, forward_part))

    _, (pivots, forwards) = lax.scan(
        chain_down, (start_zero, start_zero), (sources, jnp.arange(slab_count, dtype=jnp.int32))
    )

    def chain_up(beyond, packed):
        plane_value = packed[1] + far_weight * packed[0] * beyond
        return (plane_value, plane_value)

    _, separators = lax.scan(chain_up, start_zero, (pivots, forwards), reverse=True)
    padded_sep = jnp.concatenate([separators, start_zero[None]], axis=0)
    own_plane = lax.dynamic_index_in_dim(padded_sep, slab_index, 0, keepdims=False)
    next_plane = lax.dynamic_index_in_dim(padded_sep, slab_index + 1, 0, keepdims=False)
    interior_sol = particular + own_plane[None] * spike + next_plane[None] * spike[::-1]
    modal = jnp.concatenate([own_plane[None], interior_sol], axis=0)
    back_x = jnp.einsum("zjk,jx->zkx", modal, table_x, precision=highest)
    gathered_y = regroup(back_x)
    potential = jnp.einsum("zkx,ky->zxy", gathered_y, table_y, precision=highest)
    pot_tiles = potential.reshape(CZ // BZ, BZ, local_x // BX, BX, NY // BY, BY)
    pot_tiles = (
        pot_tiles.transpose(0, 2, 4, 1, 3, 5).reshape(tiles_dev, brick_cells).astype(jnp.bfloat16)
    )
    padded_tiles = jnp.concatenate([pot_tiles, jnp.zeros((1, brick_cells), jnp.bfloat16)], axis=0)
    replies = padded_tiles[in_ids]
    returned = lax.all_to_all(replies, ("gz", "ma"), split_axis=0, concat_axis=0, tiled=True)
    result = returned[slot_of]
    return jnp.where(is_live[:, None], result, jnp.zeros_like(result))


DOMAINS = 32
GROUPS = 4
SLABS = 8
SEND = (4, 2, 5, 3, 0, 1, 6, 7)
ARRIVAL = (0, 4, 2, 5, 3, 1, 6, 7)
PARTS = 2
PART_PLANES = 2
TAKE_FIRST = (0, 4, 2, 5, 3, 1)
TAKE_LATER = (6, 7)
PAIR_SLOTS = 8
SLOTS = DOMAINS * PAIR_SLOTS
TILES = 512
BRICK_ROWS = 16
CELLS = 2048
LANES = 128
HALF = 64
SPOTS = 64
ROWS = BRICK_ROWS * SPOTS
PART_ROWS = ROWS // PARTS
PART_CELLS = CELLS // PARTS
DOT_ROWS = 512
PAIRS = 4
CLASSES = (0, 4, 1, 7, 2, 6, 3, 5)
HEAD_ROWS = 16
STEPS = 64
PLANES = 128
FULL = 32700.0
LOG_UNIT = 128.0
VMEM_BYTES = 24 * 1024 * 1024
ALL_VMEM_BYTES = 60 * 1024 * 1024


def split_table(table):
    high = table.astype(ml_dtypes.bfloat16)
    low = (table - high.astype(np.float64)).astype(ml_dtypes.bfloat16)
    return high, low


def line_tables():
    iy, k2 = np.arange(HALF)[:, None], np.arange(HALF)[None, :]
    tables = []
    for pair in range(PAIRS):
        table = np.zeros((LANES, LANES))
        for one in range(2):
            angle = 2.0 * np.pi / NY * (iy * (CLASSES[2 * pair + one] + 8 * k2) % NY)
            cosine, sine = np.cos(angle) / np.sqrt(NY), np.sin(angle) / np.sqrt(NY)
            there = slice(one * HALF, (one + 1) * HALF)
            if pair == 0:
                table[there, there] = cosine + sine
            else:
                table[:HALF, there] = cosine + sine
                table[HALF:, there] = (cosine - sine) * (1 - 2 * one)
        tables.append(table)

    def stacked(table):
        high, low = split_table(table)
        return np.concatenate(
            [np.concatenate([high, low], axis=1), np.concatenate([high, np.zeros_like(low)], axis=1)], axis=0
        )

    return np.stack([stacked(table) for table in tables]), np.stack([stacked(table.T) for table in tables])


def class_weights():
    pair, ty = np.arange(PAIRS)[:, None], np.arange(4)[None, :]
    cosine, sine = np.cos(np.pi / 4.0 * pair * ty), np.sin(np.pi / 4.0 * pair * ty)
    sine[0] = (-1.0) ** np.arange(4)
    sign = (-1.0) ** pair * np.ones((1, 4))
    return np.concatenate([cosine, sine, sign], axis=1).astype(np.float32)


def plane_tables(offsets, planes, turned):
    index = np.arange(PLANES)
    table = np.sqrt(2.0 / (PLANES + 1)) * np.sin(
        np.pi / (PLANES + 1) * ((index[:, None] + 1) * (index[None, :] + 1) % (2 * PLANES + 2))
    )
    each = []
    for own in range(SLABS):
        slabs = np.array([own ^ offset for offset in offsets])
        plane, tz = np.array(planes)[:, None, None], np.arange(BZ)[None, :, None]
        part = table[:, (slabs * CZ + tz * BZ + plane).reshape(-1)]
        high, low = split_table(part.T if turned else part)
        if 3 * high.shape[1] <= 2 * LANES:
            each.append(np.concatenate([high, high, low], axis=1))
            continue
        top = np.concatenate([high, high], axis=1)
        bottom = np.concatenate([low, np.zeros_like(low)], axis=1)
        each.append(np.concatenate([top, bottom], axis=0))
    return np.stack(each)


def mode_tables():
    mu = 2.0 - 2.0 * np.cos(np.pi / (PLANES + 1) * (np.arange(PLANES) + 1))
    base = np.broadcast_to((mu + 1.0 / (SCREEN * SCREEN))[:, None], (PLANES, LANES))
    lam = 2.0 - 2.0 * np.cos(2.0 * np.pi / NY * np.arange(NY))
    lam = np.stack([lam[number::8] for number in CLASSES])
    return base.astype(np.float32), np.concatenate([lam, lam], axis=1).astype(np.float32)


def low_half(shape):
    return lax.broadcasted_iota(jnp.int32, shape, len(shape) - 1) < HALF


def split(values):
    high = values.astype(jnp.bfloat16)
    return high, (values - high.astype(jnp.float32)).astype(jnp.bfloat16)


def dot(left, right):
    return jnp.dot(left, right, preferred_element_type=jnp.float32)


def start_copies(pairs, sems):
    copies = [pltpu.make_async_copy(source, place, sems.at[at]) for at, (source, place) in enumerate(pairs)]
    for each in copies:
        each.start()
    return copies


def even_odd(first, second, low):
    crossed = pltpu.roll(jnp.where(low, second, first), HALF, 1)
    return jnp.where(low, first, crossed), jnp.where(low, crossed, second)


def write_left(at, here, lines, left_ref):
    rows = left_ref.shape[1] // 2
    for line, values in enumerate(lines):
        high, rest = split(values)
        there = slice(line * rows + here.start, line * rows + here.stop)
        left_ref[at, there, :LANES] = high
        left_ref[at, there, LANES:] = rest


def line_product(at, here, left_ref, table):
    products = []
    rows = left_ref.shape[1] // 2
    for line in range(2):
        there = slice(line * rows + here.start, line * rows + here.stop)
        both = dot(left_ref[at, there, :], table)
        products.append(both[:, :LANES] + both[:, LANES:])
    return even_odd(*products, low_half(products[0].shape))


def class_sums(points):
    half = [points[ty] + points[ty + 4] for ty in range(4)]
    rest = [points[ty] - points[ty + 4] for ty in range(4)]
    even, odd = half[0] + half[2], half[1] + half[3]
    turn = math.sqrt(0.5)
    across, along = turn * (rest[1] - rest[3]), turn * (rest[1] + rest[3])
    return (
        (even + odd, even - odd),
        (rest[0] + across, rest[2] + along),
        (half[0] - half[2], half[1] - half[3]),
        (rest[0] - across, along - rest[2]),
    )


def level_of(most):
    return jnp.floor(jnp.log2(jnp.maximum(most, 1e-30)) * LOG_UNIT) + 2.0


def inverse_of(level):
    return FULL * jnp.exp2(level * (-1.0 / LOG_UNIT))


def fixed_of(values):
    return jnp.floor(values + 0.5).astype(jnp.int32).astype(jnp.int16)


def head_of(level):
    return jnp.broadcast_to(level, (HEAD_ROWS, LANES)).astype(jnp.int32).astype(jnp.int16)


def unit_of(sent_ref):
    head = sent_ref[sent_ref.shape[0] - HEAD_ROWS :, :].astype(jnp.int32).astype(jnp.float32)
    return jnp.exp2(head[0:1] * (1.0 / LOG_UNIT)) * (1.0 / FULL)


def wide(sent_ref):
    block = sent_ref[: sent_ref.shape[0] - HEAD_ROWS, :]
    return block.astype(jnp.int32).astype(jnp.float32) * unit_of(sent_ref)


def pack_kernel(
    owner_in, tile_in, count_in, brick_in, first_ref, second_ref, back_ref,
    owner_ref, tile_ref, count_ref, brick_ref, pick_ref, head_ref, ready_ref, later_ref, used_ref, sems, out_sems,
):
    copies = start_copies(
        ((owner_in, owner_ref), (tile_in, tile_ref), (count_in, count_ref), (brick_in, brick_ref)), sems
    )
    brick_rows = brick_ref.shape[0]
    head_ref[...] = jnp.full(head_ref.shape, float(TILES), jnp.float32)
    pick_ref[...] = jnp.zeros(pick_ref.shape, jnp.float32)
    for owner in range(DOMAINS):
        used_ref[owner] = 0
    for each in copies[:3]:
        each.wait()
    count = count_ref[0]
    lane = lax.broadcasted_iota(jnp.int32, (1, brick_rows), 1)

    def place(r, _):
        owner = owner_ref[r]
        within = used_ref[owner]
        used_ref[owner] = within + 1
        slot = jnp.where(r < count, owner * PAIR_SLOTS + within, SLOTS)
        tile = tile_ref[r]
        position = (tile & 7) * SPOTS + ((tile >> 3) & 15) * 4 + (tile >> 7)
        pick_ref[pl.ds(slot, 1), :] = jnp.where(lane == r, 1.0, 0.0)
        head_ref[pl.ds(slot, 1), :] = jnp.full((1, LANES), position, jnp.int32).astype(jnp.float32)
        return 0

    lax.fori_loop(0, brick_rows, place, 0, unroll=8)
    copies[3].wait()
    copies = []
    rows = 64
    for at, (out_ref, held_ref) in enumerate(((first_ref, ready_ref), (second_ref, later_ref))):
        for part in range(SLOTS // rows):
            here = slice(part * rows, (part + 1) * rows)
            picks = pick_ref[here, :].astype(jnp.bfloat16)
            cells = slice(at * PART_CELLS, (at + 1) * PART_CELLS)
            held_ref[here, :PART_CELLS] = dot(picks, brick_ref[:, cells]).astype(jnp.bfloat16)
            if at == 0:
                head = head_ref[here, :]
                high = jnp.floor(head * (1.0 / 32.0))
                places = jnp.where(low_half(head.shape), high, head - 32.0 * high)
                held_ref[here, PART_CELLS:] = places.astype(jnp.bfloat16)
            some = pl.ds(part * rows, rows)
            copies.append(pltpu.make_async_copy(held_ref.at[some], out_ref.at[some], out_sems.at[4 * at + part]))
            copies[-1].start()
    for part in range(SLOTS // LANES):
        here = slice(part * LANES, (part + 1) * LANES)
        back_ref[:, here] = pick_ref[here, :].T.astype(jnp.bfloat16)
    for each in copies:
        each.wait()


def write_picks(brick_ref, picks_ref, across_ref):
    for part in range(SLOTS // LANES):
        here = slice(part * LANES, (part + 1) * LANES)
        head = brick_ref[here, PART_CELLS:].astype(jnp.float32)
        turned = pltpu.roll(head, HALF, 1)
        low = low_half(head.shape)
        places = (jnp.where(low, head, turned) * 32.0 + jnp.where(low, turned, head)).astype(jnp.int32)
        for block in range(TILES // LANES):
            there = slice(block * LANES, (block + 1) * LANES)
            lane = lax.broadcasted_iota(jnp.int32, (LANES, LANES), 1) + block * LANES
            square = jnp.where(places == lane, 1.0, 0.0)
            picks_ref[here, there] = square.astype(jnp.bfloat16)
            across_ref[there, here] = square.T.astype(jnp.bfloat16)


def forward_lines(own_ref, brick_ref, across_ref, table_in, sent_refs, left_ref, lines_ref, table_ref, sems):
    [copy] = start_copies(((table_in, table_ref),), sems)
    low = low_half((SPOTS, LANES))
    for q in range(0, BRICK_ROWS // PARTS, 4):
        charge = dot(across_ref[...], brick_ref[:, q * LANES : (q + 4) * LANES])
        for one in range(4):
            there = slice(one * LANES, (one + 1) * LANES)
            here = slice((q + one) * SPOTS, (q + one + 1) * SPOTS)
            points = [charge[ty * SPOTS : (ty + 1) * SPOTS, there] for ty in range(8)]
            for pair, (cosines, sines) in enumerate(class_sums(points)):
                write_left(pair, here, even_odd(cosines, sines, low), left_ref)
    copy.wait()
    for pair in range(PAIRS):
        for one, values in enumerate(line_product(pair, slice(0, PART_ROWS), left_ref, table_ref[pair])):
            most = jnp.max(jnp.abs(values).reshape(PART_ROWS // 8, 8, LANES), axis=0)
            level = level_of(jnp.max(most, axis=0, keepdims=True))
            lines_ref[2 * pair + one, :PART_ROWS, :] = fixed_of(values * inverse_of(level))
            lines_ref[2 * pair + one, PART_ROWS:, :] = head_of(level)
    for offset, sent_ref in zip(SEND, sent_refs):
        sent_ref[...] = lines_ref[own_ref[0] ^ offset]


def forward_first_kernel(own_ref, brick_ref, table_in, *refs):
    sent_refs, (picks_ref, across_ref) = refs[: len(SEND)], refs[len(SEND) : len(SEND) + 2]
    write_picks(brick_ref, picks_ref, across_ref)
    forward_lines(own_ref, brick_ref, across_ref, table_in, sent_refs, *refs[len(SEND) + 2 :])


def forward_later_kernel(own_ref, brick_ref, across_ref, table_in, *refs):
    forward_lines(own_ref, brick_ref, across_ref, table_in, refs[: len(SEND)], *refs[len(SEND) :])


def grid_rows(slabs, plane, xq, tx):
    start = ((plane * 4 + xq) * SPOTS + tx * 4) * slabs
    return pl.ds(pl.multiple_of(start, 4 * slabs), 4 * slabs)


def plane_product(plane_ref, lines):
    high, rest = split(lines)
    rows = plane_ref.shape[0]
    if plane_ref.shape[1] == 3 * high.shape[0]:
        return dot(plane_ref[...], jnp.concatenate([high, rest, high], axis=0))
    both = dot(plane_ref[...], jnp.concatenate([high, rest], axis=0))
    return both[: rows // 2] + both[rows // 2 :]


def add_sines(got_refs, plane_ref, grid_ref, finish):
    slabs = len(got_refs)
    for at, got_ref in enumerate(got_refs):
        grid_ref[pl.ds(at, PART_ROWS, stride=slabs), :] = wide(got_ref)

    def planes(tx, xq):
        return jnp.concatenate(
            [grid_ref[grid_rows(slabs, plane, xq, tx), :] for plane in range(PART_PLANES)], axis=0
        )

    def sines(tx, _):
        modes = plane_product(plane_ref, jnp.concatenate([planes(tx, xq) for xq in range(4)], axis=1))
        for xq in range(4):
            finish(tx * 4 + xq, modes[:, xq * LANES : (xq + 1) * LANES])
        return 0

    lax.fori_loop(0, 16, sines, 0, unroll=8)


def down_first_kernel(own_ref, *refs):
    count = len(ARRIVAL)
    planes_ref, base_ref, lam_ref, modes_ref, root_ref, gain_ref, power_ref, grid_ref = refs[count:]
    excess = base_ref[...] + lam_ref[pl.ds(own_ref[0], 1), :]
    spread = jnp.sqrt(excess * (excess + 4.0))
    root_ref[...] = 2.0 / (2.0 + excess + spread)
    gain_ref[...] = 1.0 / spread
    for part in range(2):
        here = pl.ds(part * PLANES // 2, PLANES // 2)
        square = root_ref[here, :] * root_ref[here, :]

        def raised(step, power):
            power_ref[step, here, :] = power
            return power * square

        lax.fori_loop(0, STEPS, raised, jnp.ones(square.shape, jnp.float32), unroll=8)

    def finish(line, values):
        modes_ref[line] = values

    add_sines(refs[:count], planes_ref.at[own_ref[0]], grid_ref, finish)


def down_later_kernel(own_ref, *refs):
    count = len(ARRIVAL)
    sums_ref, root_ref, planes_ref, walk_ref, end_ref, grid_ref, modes_ref, last_ref = refs[count:]

    def finish(line, values):
        modes_ref[line] = sums_ref[line] + values

    add_sines(refs[:count], planes_ref.at[own_ref[0]], grid_ref, finish)
    part_rows = 64
    low = low_half((part_rows, LANES))
    for part in range(PLANES // part_rows):
        here = pl.ds(part * part_rows, part_rows)
        root = root_ref[here, :]
        square = root * root

        def walk(step, held):
            ahead, behind = modes_ref[step, here, :], modes_ref[STEPS - 1 - step, here, :]
            own = jnp.where(low, behind, ahead)
            other = pltpu.roll(jnp.where(low, ahead, behind), HALF, 1)
            held = square * held + (own + root * other)
            walk_ref[step, here, :] = held
            return held

        last_ref[here, :] = lax.fori_loop(0, STEPS, walk, jnp.zeros((part_rows, LANES), jnp.float32), unroll=8)
    last = last_ref[...]
    level = level_of(jnp.max(jnp.abs(last), axis=0, keepdims=True))
    end_ref[:PLANES, :] = fixed_of(last * inverse_of(level))
    end_ref[PLANES:, :] = head_of(level)


def local_kernel(walk_ref, root_ref, gain_ref, local_ref):
    part_rows = 64
    low = low_half((part_rows, LANES))
    for part in range(PLANES // part_rows):
        here = pl.ds(part * part_rows, part_rows)
        root, gain = root_ref[here, :], gain_ref[here, :]
        zero = jnp.zeros(root.shape, jnp.float32)

        def line(step, ahead_before, behind_after):
            near = jnp.where(low, walk_ref[STEPS - 1 - step, here, :], walk_ref[step, here, :])
            far = pltpu.roll(jnp.where(low, behind_after, ahead_before), HALF, 1)
            local_ref[step, here, :] = gain * (near + root * far)

        def inner(step, _):
            line(step, walk_ref[step - 1, here, :], walk_ref[STEPS - 2 - step, here, :])
            return 0

        line(0, zero, walk_ref[STEPS - 2, here, :])
        lax.fori_loop(1, STEPS - 1, inner, 0, unroll=6)
        line(STEPS - 1, walk_ref[STEPS - 2, here, :], zero)


def up_kernel(own_ref, local_ref, power_ref, root_ref, gain_ref, *refs):
    end_refs, plane_ref = refs[:GROUPS], refs[GROUPS].at[own_ref[0]]
    count = GROUPS + 1 + PARTS * len(SEND)
    sent_refs = refs[GROUPS + 1 : count]
    rise_ref, fall_ref, grid_ref, level_ref = refs[count:]
    low = low_half((PLANES, LANES))
    root = root_ref[...]
    square = root * root
    across = square
    for _ in range(6):
        across = across * across
    around = across
    for _ in range(2):
        around = around * around
    ends = [wide(end_ref) for end_ref in end_refs]
    entering = jnp.zeros((PLANES, LANES), jnp.float32)
    for step in range(GROUPS - 1, -1, -1):
        entering = entering * across + jnp.where(low, ends[GROUPS - 1 - step], ends[(step + 1) % GROUPS])
    entering = gain_ref[...] * entering / (1.0 - around)
    straight, turned = square * entering, root * pltpu.roll(entering, HALF, 1)
    rise_ref[...] = jnp.where(low, turned, straight)
    fall_ref[...] = jnp.where(low, straight, turned)
    slabs = len(SEND)

    def solved(step):
        reach = rise_ref[...] * power_ref[step] + fall_ref[...] * power_ref[STEPS - 1 - step]
        return local_ref[step] + reach

    def sines(tx, most):
        lines = plane_product(plane_ref, jnp.concatenate([solved(tx * 4 + xq) for xq in range(4)], axis=1))
        for xq in range(4):
            part = lines[:, xq * LANES : (xq + 1) * LANES]
            most = jnp.maximum(most, jnp.max(jnp.abs(part).reshape(PARTS, 4 * PART_PLANES, slabs, LANES), axis=1))
            for plane in range(BZ):
                grid_ref[grid_rows(slabs, plane, xq, tx), :] = part[plane * 4 * slabs : (plane + 1) * 4 * slabs]
        return most

    most = lax.fori_loop(0, 16, sines, jnp.zeros((PARTS, slabs, LANES), jnp.float32), unroll=8)
    level_ref[...] = level_of(most)
    for at, sent_ref in enumerate(sent_refs):
        part, slab = at // slabs, at % slabs
        level = level_ref[part, slab : slab + 1, :]
        here = pl.ds(part * PART_ROWS * slabs + slab, PART_ROWS, stride=slabs)
        sent_ref[:PART_ROWS, :] = fixed_of(grid_ref[here, :] * inverse_of(level))
        sent_ref[PART_ROWS:, :] = head_of(level)


def take_lines(own_ref, offsets, got_refs, left_ref, lines_ref):
    own = own_ref[0]
    pairs = list(dict.fromkeys(offset // 2 for offset in offsets))
    for offset, got_ref in zip(offsets, got_refs):
        lines_ref[2 * pairs.index(offset // 2) + ((own ^ offset) & 1)] = wide(got_ref)
    low = low_half((PART_ROWS, LANES))
    for at in range(len(pairs)):
        write_left(at, slice(0, PART_ROWS), even_odd(lines_ref[2 * at], lines_ref[2 * at + 1], low), left_ref)
    return [(own >> 1) ^ pair for pair in pairs]


def point_parts(pair, cosines, sines, weight_ref):
    for ty in range(4):
        part = weight_ref[pair, ty] * cosines + weight_ref[pair, 4 + ty] * sines
        yield ty, part
        yield ty + 4, weight_ref[pair, 8] * part


def reply_first_kernel(own_ref, weight_ref, *refs):
    count = len(TAKE_FIRST)
    table_ref, sums_ref, lines_ref, left_ref = refs[count:]
    pairs = take_lines(own_ref, TAKE_FIRST, refs[:count], left_ref, lines_ref)
    for at, pair in enumerate(pairs):
        cosines, sines = line_product(at, slice(0, PART_ROWS), left_ref, table_ref[pair])
        for ty, values in point_parts(pair, cosines, sines, weight_ref):
            sums_ref[ty] = values if at == 0 else sums_ref[ty] + values


def reply_later_kernel(own_ref, weight_ref, *refs):
    count = len(TAKE_LATER)
    sums_ref, picks_ref, table_ref, out_ref, lines_ref, left_ref, pot_ref = refs[count:]
    [pair] = take_lines(own_ref, TAKE_LATER, refs[:count], left_ref, lines_ref)
    cosines, sines = line_product(0, slice(0, PART_ROWS), left_ref, table_ref[pair])
    for ty, values in point_parts(pair, cosines, sines, weight_ref):
        values = (sums_ref[ty] + values).astype(jnp.bfloat16)
        for q in range(PART_ROWS // SPOTS):
            pot_ref[ty * SPOTS : (ty + 1) * SPOTS, q * LANES : (q + 1) * LANES] = values[q * SPOTS : (q + 1) * SPOTS]
    for q in range(0, PART_ROWS // SPOTS, 4):
        there = slice(q * LANES, (q + 4) * LANES)
        out_ref[:, there] = dot(picks_ref[...], pot_ref[:, there]).astype(jnp.bfloat16)


def unpack_kernel(back_ref, *refs):
    got_refs, out_ref = refs[:PARTS], refs[PARTS]
    for part, got_ref in enumerate(got_refs):
        for q in range(0, PART_CELLS, 4 * LANES):
            taken = dot(back_ref[...], got_ref[:, q : q + 4 * LANES])
            out_ref[:, part * PART_CELLS + q : part * PART_CELLS + q + 4 * LANES] = taken.astype(jnp.bfloat16)


def call(kernel, name, operands, spaces, outs, places, scratch, vmem=VMEM_BYTES):
    return pl.pallas_call(
        kernel,
        out_shape=outs,
        in_specs=[pl.BlockSpec(memory_space=space) for space in spaces],
        out_specs=[pl.BlockSpec(memory_space=space) for space in places],
        scratch_shapes=scratch,
        compiler_params=pltpu.CompilerParams(vmem_limit_bytes=vmem),
        name=name,
    )(*operands)


def on_device_8x4(bricks, owners, tile_ids, counts):
    V, S, H = pltpu.VMEM, pltpu.SMEM, pltpu.HBM
    f32, bf16, i32, i16 = jnp.float32, jnp.bfloat16, jnp.int32, jnp.int16
    shape, dma = jax.ShapeDtypeStruct, pltpu.SemaphoreType.DMA
    brick_rows = bricks.shape[0]
    lines_in, lines_out = (jnp.asarray(each) for each in line_tables())
    weights = jnp.asarray(class_weights())
    lines_in = pltpu.with_memory_space_constraint(lines_in, H)
    planes_in = [jnp.asarray(plane_tables(ARRIVAL, planes, False)) for planes in ((0, 1), (2, 3))]
    planes_out = jnp.asarray(plane_tables(SEND, range(BZ), True))
    base, lam = (jnp.asarray(each) for each in mode_tables())
    own = lax.axis_index("gz").astype(i32).reshape(1)
    end_shape = shape((PLANES + HEAD_ROWS, LANES), i16)
    cube, flat, sums_shape = (STEPS, PLANES, LANES), (PLANES, LANES), (8, PART_ROWS, LANES)
    line, packed = (PART_ROWS, LANES), [(SLOTS, PART_CELLS + LANES), (SLOTS, PART_CELLS)]
    part_shape = shape((PART_ROWS + HEAD_ROWS, LANES), i16)

    def all_ways(values):
        return lax.all_to_all(values, ("gz", "ma"), split_axis=0, concat_axis=0, tiled=True)

    def over_slabs(offset, values):
        return lax.ppermute(values, "gz", [(g, g ^ offset) for g in range(SLABS)]) if offset else values

    def round_groups(values, step):
        return lax.ppermute(values, "ma", [(m, (m + step) % GROUPS) for m in range(GROUPS)]) if step else values

    def exchanged(sent):
        sent = dict(zip(SEND, sent))
        return [over_slabs(offset, sent[offset]) for offset in ARRIVAL]

    *outgoing, back = call(
        pack_kernel,
        "pack",
        (owners.reshape(brick_rows), tile_ids, counts, bricks),
        [H] * 4,
        [shape(each, bf16) for each in packed] + [shape((brick_rows, SLOTS), bf16)],
        [H, H, V],
        [
            S((brick_rows,), i32),
            S((brick_rows,), i32),
            S((1,), i32),
            V(bricks.shape, bf16),
            V((SLOTS + PAIR_SLOTS, brick_rows), f32),
            V((SLOTS + PAIR_SLOTS, LANES), f32),
            *[V(each, bf16) for each in packed],
            S((DOMAINS,), i32),
            dma((4,)),
            dma((8,)),
        ],
        ALL_VMEM_BYTES,
    )
    incoming = [all_ways(each) for each in outgoing]
    forward_scratch = [
        V((PAIRS, 2 * PART_ROWS, 2 * LANES), bf16),
        V((len(SEND), *part_shape.shape), i16),
        V(lines_in.shape, bf16),
        dma((1,)),
    ]
    *sent, picks, across = call(
        forward_first_kernel,
        "forward_first",
        (own, incoming[0], lines_in),
        [S, V, H],
        [part_shape] * len(SEND) + [shape((SLOTS, TILES), bf16), shape((TILES, SLOTS), bf16)],
        [V] * (len(SEND) + 2),
        forward_scratch,
    )
    first = exchanged(sent)
    second, first[1], first[2] = lax.optimization_barrier((incoming[1], first[1], first[2]))
    sent = call(
        forward_later_kernel,
        "forward_later",
        (own, second, across, lines_in),
        [S, V, V, H],
        [part_shape] * len(SEND),
        [V] * len(SEND),
        forward_scratch,
    )
    later = exchanged(sent)
    sums, root, gain, power = call(
        down_first_kernel,
        "down_first",
        (own, *first, planes_in[0], base, lam),
        [S] + [V] * (len(first) + 3),
        [shape(cube, f32), shape(flat, f32), shape(flat, f32), shape(cube, f32)],
        [V] * 4,
        [
            V((len(first) * PART_ROWS, LANES), f32),
        ],
    )
    walk, end = call(
        down_later_kernel,
        "down_later",
        (own, *later, sums, root, planes_in[1]),
        [S] + [V] * (len(later) + 3),
        [shape(cube, f32), end_shape],
        [V, V],
        [
            V((len(later) * PART_ROWS, LANES), f32),
            V(cube, f32),
            V(flat, f32),
        ],
    )
    ends = [round_groups(end, step) for step in range(GROUPS)]
    (local,) = call(local_kernel, "local", (walk, root, gain), [V] * 3, [shape(cube, f32)], [V], [])
    sent = call(
        up_kernel,
        "up",
        (own, local, power, root, gain, *ends, planes_out),
        [S] + [V] * (5 + GROUPS),
        [part_shape] * (PARTS * len(SEND)),
        [V] * (PARTS * len(SEND)),
        [
            V(flat, f32),
            V(flat, f32),
            V((len(SEND) * ROWS, LANES), f32),
            V((PARTS, len(SEND), LANES), f32),
        ],
    )
    got = [exchanged(sent[: len(SEND)]), exchanged(sent[len(SEND) :])]
    near = ARRIVAL.index(1)
    got[0][-1], got[1][near] = lax.optimization_barrier((got[0][-1], got[1][near]))
    returned = []
    for part in got:
        first, later = part[: len(TAKE_FIRST)], part[len(TAKE_FIRST) :]
        (sums,) = call(
            reply_first_kernel,
            "reply_first",
            (own, weights, *first, lines_out),
            [S, S] + [V] * (len(first) + 1),
            [shape(sums_shape, f32)],
            [V],
            [V((len(first), *line), f32), V((len(first) // 2, 2 * PART_ROWS, 2 * LANES), bf16)],
        )
        (replies,) = call(
            reply_later_kernel,
            "reply_later",
            (own, weights, *later, sums, picks, lines_out),
            [S, S] + [V] * (len(later) + 3),
            [shape((SLOTS, PART_CELLS), bf16)],
            [V],
            [
                V((len(later), *line), f32),
                V((len(later) // 2, 2 * PART_ROWS, 2 * LANES), bf16),
                V((TILES, PART_CELLS), bf16),
            ],
        )
        returned.append(all_ways(replies))
    (result,) = call(
        unpack_kernel,
        "unpack",
        (back, *returned),
        [V] * (1 + PARTS),
        [shape((brick_rows, CELLS), bf16)],
        [V],
        [],
    )
    return result


def solution(mesh):
    in_specs = (P(("gz", "ma"), None), P(("gz", "ma"), None), P(("gz", "ma")), P(("gz", "ma")))
    out_specs = P(("gz", "ma"), None)
    body = on_device_8x4 if (mesh.shape["gz"], mesh.shape["ma"]) == (SLABS, GROUPS) else on_device
    return jax.shard_map(body, mesh=mesh, in_specs=in_specs, out_specs=out_specs, check_vma=False)
```

```python
import math

import jax
import jax.numpy as jnp
import ml_dtypes
import numpy as np
from jax import lax
from jax.experimental import pallas as pl
from jax.experimental.pallas import tpu as pltpu
from jax.sharding import PartitionSpec as P

NX = 512
NY = 512
SCREEN = 16
BZ = 4
BX = 8
BY = 64
CZ = 16


def hartley(length):
    indices = jnp.arange(length, dtype=jnp.int32)
    products = indices[:, None] * indices[None, :] % length
    angles = 2.0 * math.pi / length * products.astype(jnp.float32)
    return (jnp.cos(angles) + jnp.sin(angles)) / math.sqrt(length)


def second_difference(length, indices):
    return 2.0 - 2.0 * jnp.cos(2.0 * math.pi / length * indices.astype(jnp.float32))


def thomas(right_side, diagonal):
    start_zero = jnp.zeros(right_side.shape[1:], jnp.float32)

    def down(state_pair, plane):
        factor = 1.0 / (diagonal - state_pair[0])
        partial_value = (plane + state_pair[1]) * factor
        return ((factor, partial_value), (factor, partial_value))

    _, (factors, partials) = lax.scan(down, (start_zero, start_zero), right_side)

    def upward(beyond, factor_partial):
        solved = factor_partial[1] + factor_partial[0] * beyond
        return (solved, solved)

    _, solutions = lax.scan(upward, start_zero, (factors, partials), reverse=True)
    return solutions


def regroup(values):
    return lax.all_to_all(values, "ma", split_axis=2, concat_axis=1, tiled=True)


def on_device(bricks, owners, tile_ids, counts):
    domains = lax.axis_size(("gz", "ma"))
    group_count = lax.axis_size("ma")
    slab_count = lax.axis_size("gz")
    brick_rows, brick_cells = bricks.shape
    slot_count = max(2, 2 * brick_rows // domains)
    local_x = NX // group_count
    local_y = NY // group_count
    tiles_dev = CZ // BZ * (local_x // BX) * (NY // BY)
    highest = lax.Precision.HIGHEST
    target = owners[:, 0]
    row_order = jnp.arange(brick_rows, dtype=jnp.int32)
    earlier_same = (target[:, None] == target[None, :]) & (row_order[None, :] < row_order[:, None])
    within = jnp.sum(earlier_same.astype(jnp.int32), axis=1)
    slot_of = target * slot_count + within
    is_live = row_order < counts[0]
    loaded = jnp.where(is_live[:, None], bricks, jnp.zeros_like(bricks))
    outgoing = jnp.zeros((domains * slot_count, brick_cells), jnp.bfloat16).at[slot_of].set(loaded)
    out_ids = jnp.full((domains * slot_count,), tiles_dev, jnp.int32).at[slot_of].set(tile_ids)
    incoming, in_ids = (
        lax.all_to_all(outgoing, ("gz", "ma"), split_axis=0, concat_axis=0, tiled=True),
        lax.all_to_all(out_ids, ("gz", "ma"), split_axis=0, concat_axis=0, tiled=True),
    )
    picker = (jnp.arange(tiles_dev, dtype=jnp.int32)[:, None] == in_ids[None, :]).astype(
        jnp.bfloat16
    )
    deposit = jnp.dot(picker, incoming, preferred_element_type=jnp.float32)
    charge = deposit.reshape(CZ // BZ, local_x // BX, NY // BY, BZ, BX, BY)
    charge = charge.transpose(0, 3, 1, 4, 2, 5).reshape(CZ, local_x, NY)
    table_x = hartley(NX)
    table_y = hartley(NY)
    along_y = jnp.einsum("zxy,ky->zxk", charge, table_y, precision=highest)
    gathered_x = regroup(along_y)
    spectrum = jnp.einsum("zxk,jx->zjk", gathered_x, table_x, precision=highest)
    columns = lax.axis_index("ma") * local_y + jnp.arange(local_y, dtype=jnp.int32)
    lam_y = second_difference(NY, columns)
    screening = 1.0 / (SCREEN * SCREEN)
    slab_index = lax.axis_index("gz")
    lam_x = second_difference(NX, jnp.arange(NX, dtype=jnp.int32))
    diagonal = 2.0 + screening + lam_x[:, None] + lam_y[None, :]
    interior = spectrum[1:]
    particular = thomas(interior, diagonal)
    unit_rhs = jnp.zeros_like(interior).at[0].set(1.0)
    spike = thomas(unit_rhs, diagonal)
    near_weight = spike[0]
    far_weight = spike[-1]
    head_term = spectrum[0] + particular[0]
    tail_term = particular[-1]
    reduced_first = diagonal - near_weight
    reduced_rest = diagonal - 2.0 * near_weight
    start_zero = jnp.zeros_like(diagonal)
    heads, tails = (
        lax.all_gather(head_term[None], "gz", axis=0, tiled=True),
        lax.all_gather(tail_term[None], "gz", axis=0, tiled=True),
    )
    before = jnp.concatenate([start_zero[None], tails[:-1]], axis=0)
    sources = heads + before

    def chain_down(state_pair, packed):
        source, position = packed
        base_term = jnp.where(position == 0, reduced_first, reduced_rest)
        pivot_now = 1.0 / (base_term - far_weight * far_weight * state_pair[0])
        forward_part = pivot_now * (source + far_weight * state_pair[1])
        return ((pivot_now, forward_part), (pivot_now, forward_part))

    _, (pivots, forwards) = lax.scan(
        chain_down, (start_zero, start_zero), (sources, jnp.arange(slab_count, dtype=jnp.int32))
    )

    def chain_up(beyond, packed):
        plane_value = packed[1] + far_weight * packed[0] * beyond
        return (plane_value, plane_value)

    _, separators = lax.scan(chain_up, start_zero, (pivots, forwards), reverse=True)
    padded_sep = jnp.concatenate([separators, start_zero[None]], axis=0)
    own_plane = lax.dynamic_index_in_dim(padded_sep, slab_index, 0, keepdims=False)
    next_plane = lax.dynamic_index_in_dim(padded_sep, slab_index + 1, 0, keepdims=False)
    interior_sol = particular + own_plane[None] * spike + next_plane[None] * spike[::-1]
    modal = jnp.concatenate([own_plane[None], interior_sol], axis=0)
    back_x = jnp.einsum("zjk,jx->zkx", modal, table_x, precision=highest)
    gathered_y = regroup(back_x)
    potential = jnp.einsum("zkx,ky->zxy", gathered_y, table_y, precision=highest)
    pot_tiles = potential.reshape(CZ // BZ, BZ, local_x // BX, BX, NY // BY, BY)
    pot_tiles = (
        pot_tiles.transpose(0, 2, 4, 1, 3, 5).reshape(tiles_dev, brick_cells).astype(jnp.bfloat16)
    )
    padded_tiles = jnp.concatenate([pot_tiles, jnp.zeros((1, brick_cells), jnp.bfloat16)], axis=0)
    replies = padded_tiles[in_ids]
    returned = lax.all_to_all(replies, ("gz", "ma"), split_axis=0, concat_axis=0, tiled=True)
    result = returned[slot_of]
    return jnp.where(is_live[:, None], result, jnp.zeros_like(result))


DOMAINS = 32
GROUPS = 4
SLABS = 8
SEND = (4, 2, 5, 3, 0, 1, 6, 7)
ARRIVAL = (0, 4, 2, 5, 3, 1, 6, 7)
PARTS = 2
PART_PLANES = 2
TAKE_FIRST = (0, 4, 2, 5, 3, 1)
TAKE_LATER = (6, 7)
PAIR_SLOTS = 8
SLOTS = DOMAINS * PAIR_SLOTS
TILES = 512
BRICK_ROWS = 16
CELLS = 2048
LANES = 128
HALF = 64
SPOTS = 64
ROWS = BRICK_ROWS * SPOTS
PART_ROWS = ROWS // PARTS
PART_CELLS = CELLS // PARTS
DOT_ROWS = 512
PAIRS = 4
CLASSES = (0, 4, 1, 7, 2, 6, 3, 5)
HEAD_ROWS = 8
STEPS = 64
PLANES = 128
FULL = 32700.0
LOG_UNIT = 128.0
VMEM_BYTES = 24 * 1024 * 1024
ALL_VMEM_BYTES = 60 * 1024 * 1024


def split_table(table):
    high = table.astype(ml_dtypes.bfloat16)
    low = (table - high.astype(np.float64)).astype(ml_dtypes.bfloat16)
    return high, low


def line_tables():
    iy, k2 = np.arange(HALF)[:, None], np.arange(HALF)[None, :]
    tables = []
    for pair in range(PAIRS):
        table = np.zeros((LANES, LANES))
        for one in range(2):
            angle = 2.0 * np.pi / NY * (iy * (CLASSES[2 * pair + one] + 8 * k2) % NY)
            cosine, sine = np.cos(angle) / np.sqrt(NY), np.sin(angle) / np.sqrt(NY)
            there = slice(one * HALF, (one + 1) * HALF)
            if pair == 0:
                table[there, there] = cosine + sine
            else:
                table[:HALF, there] = cosine + sine
                table[HALF:, there] = (cosine - sine) * (1 - 2 * one)
        tables.append(table)

    def stacked(table):
        high, low = split_table(table)
        return np.concatenate(
            [np.concatenate([high, low], axis=1), np.concatenate([high, np.zeros_like(low)], axis=1)], axis=0
        )

    return np.stack([stacked(table) for table in tables]), np.stack([stacked(table.T) for table in tables])


def class_weights():
    pair, ty = np.arange(PAIRS)[:, None], np.arange(4)[None, :]
    cosine, sine = np.cos(np.pi / 4.0 * pair * ty), np.sin(np.pi / 4.0 * pair * ty)
    sine[0] = (-1.0) ** np.arange(4)
    sign = (-1.0) ** pair * np.ones((1, 4))
    return np.concatenate([cosine, sine, sign], axis=1).astype(np.float32)


def plane_tables(offsets, planes, turned):
    index = np.arange(PLANES)
    table = np.sqrt(2.0 / (PLANES + 1)) * np.sin(
        np.pi / (PLANES + 1) * ((index[:, None] + 1) * (index[None, :] + 1) % (2 * PLANES + 2))
    )
    each = []
    for own in range(SLABS):
        slabs = np.array([own ^ offset for offset in offsets])
        plane, tz = np.array(planes)[:, None, None], np.arange(BZ)[None, :, None]
        part = table[:, (slabs * CZ + tz * BZ + plane).reshape(-1)]
        high, low = split_table(part.T if turned else part)
        if 3 * high.shape[1] <= 2 * LANES:
            each.append(np.concatenate([high, high, low], axis=1))
            continue
        top = np.concatenate([high, high], axis=1)
        bottom = np.concatenate([low, np.zeros_like(low)], axis=1)
        each.append(np.concatenate([top, bottom], axis=0))
    return np.stack(each)


def mode_tables():
    mu = 2.0 - 2.0 * np.cos(np.pi / (PLANES + 1) * (np.arange(PLANES) + 1))
    base = np.broadcast_to((mu + 1.0 / (SCREEN * SCREEN))[:, None], (PLANES, LANES))
    lam = 2.0 - 2.0 * np.cos(2.0 * np.pi / NY * np.arange(NY))
    lam = np.stack([lam[number::8] for number in CLASSES])
    return base.astype(np.float32), np.concatenate([lam, lam], axis=1).astype(np.float32)


def low_half(shape):
    return lax.broadcasted_iota(jnp.int32, shape, len(shape) - 1) < HALF


def split(values):
    high = values.astype(jnp.bfloat16)
    return high, (values - high.astype(jnp.float32)).astype(jnp.bfloat16)


def dot(left, right):
    return jnp.dot(left, right, preferred_element_type=jnp.float32)


def start_copies(pairs, sems):
    copies = [pltpu.make_async_copy(source, place, sems.at[at]) for at, (source, place) in enumerate(pairs)]
    for each in copies:
        each.start()
    return copies


def even_odd(first, second, low):
    crossed = pltpu.roll(jnp.where(low, second, first), HALF, 1)
    return jnp.where(low, first, crossed), jnp.where(low, crossed, second)


def write_left(at, here, lines, left_ref):
    rows = left_ref.shape[1] // 2
    for line, values in enumerate(lines):
        high, rest = split(values)
        there = slice(line * rows + here.start, line * rows + here.stop)
        left_ref[at, there, :LANES] = high
        left_ref[at, there, LANES:] = rest


def line_product(at, here, left_ref, table):
    products = []
    rows = left_ref.shape[1] // 2
    for line in range(2):
        there = slice(line * rows + here.start, line * rows + here.stop)
        both = dot(left_ref[at, there, :], table)
        products.append(both[:, :LANES] + both[:, LANES:])
    return even_odd(*products, low_half(products[0].shape))


def class_sums(points):
    half = [points[ty] + points[ty + 4] for ty in range(4)]
    rest = [points[ty] - points[ty + 4] for ty in range(4)]
    even, odd = half[0] + half[2], half[1] + half[3]
    turn = math.sqrt(0.5)
    across, along = turn * (rest[1] - rest[3]), turn * (rest[1] + rest[3])
    return (
        (even + odd, even - odd),
        (rest[0] + across, rest[2] + along),
        (half[0] - half[2], half[1] - half[3]),
        (rest[0] - across, along - rest[2]),
    )


def level_of(most):
    return jnp.floor(jnp.log2(jnp.maximum(most, 1e-30)) * LOG_UNIT) + 2.0


def inverse_of(level):
    return FULL * jnp.exp2(level * (-1.0 / LOG_UNIT))


def fixed_of(values):
    return jnp.floor(values + 0.5).astype(jnp.int32).astype(jnp.int16)


def head_of(level):
    return jnp.broadcast_to(level, (HEAD_ROWS, LANES)).astype(jnp.int32).astype(jnp.int16)


def unit_of(sent_ref):
    head = sent_ref[sent_ref.shape[0] - HEAD_ROWS :, :].astype(jnp.int32).astype(jnp.float32)
    return jnp.exp2(head[0:1] * (1.0 / LOG_UNIT)) * (1.0 / FULL)


def wide(sent_ref):
    block = sent_ref[: sent_ref.shape[0] - HEAD_ROWS, :]
    return block.astype(jnp.int32).astype(jnp.float32) * unit_of(sent_ref)


def pack_kernel(
    owner_in, tile_in, count_in, brick_in, out_ref, one_hot_ref,
    owner_ref, tile_ref, count_ref, brick_ref, pick_ref, head_ref, ready_ref, used_ref, sems, out_sems,
):
    cells = brick_in.at[:, pl.ds(0, PART_CELLS)]
    copies = start_copies(((owner_in, owner_ref), (tile_in, tile_ref), (count_in, count_ref), (cells, brick_ref)), sems)
    brick_rows = brick_ref.shape[0]
    head_ref[...] = jnp.full(head_ref.shape, float(TILES), jnp.float32)
    pick_ref[...] = jnp.zeros(pick_ref.shape, jnp.float32)
    for owner in range(DOMAINS):
        used_ref[owner] = 0
    for each in copies[:3]:
        each.wait()
    count = count_ref[0]
    lane = lax.broadcasted_iota(jnp.int32, (1, brick_rows), 1)

    def place(r, _):
        owner = owner_ref[r]
        within = used_ref[owner]
        used_ref[owner] = within + 1
        slot = jnp.where(r < count, owner * PAIR_SLOTS + within, SLOTS)
        tile = tile_ref[r]
        position = (tile & 7) * SPOTS + ((tile >> 3) & 15) * 4 + (tile >> 7)
        pick_ref[pl.ds(slot, 1), :] = jnp.where(lane == r, 1.0, 0.0)
        head_ref[pl.ds(slot, 1), :] = jnp.full((1, LANES), position, jnp.int32).astype(jnp.float32)
        return 0

    lax.fori_loop(0, brick_rows, place, 0, unroll=8)
    copies[3].wait()
    copies = []
    rows = 64
    for part in range(SLOTS // rows):
        here = slice(part * rows, (part + 1) * rows)
        picks = pick_ref[here, :].astype(jnp.bfloat16)
        one_hot_ref[here, :] = picks
        ready_ref[here, :PART_CELLS] = dot(picks, brick_ref[...]).astype(jnp.bfloat16)
        head = head_ref[here, :]
        high = jnp.floor(head * (1.0 / 32.0))
        places = jnp.where(low_half(head.shape), high, head - 32.0 * high)
        ready_ref[here, PART_CELLS:] = places.astype(jnp.bfloat16)
        some = pl.ds(part * rows, rows)
        copies.append(pltpu.make_async_copy(ready_ref.at[some], out_ref.at[some], out_sems.at[part]))
        copies[-1].start()
    for each in copies:
        each.wait()


def pack_later_kernel(brick_in, one_hot_ref, out_ref, back_ref, brick_ref, sems):
    [copy] = start_copies(((brick_in.at[:, pl.ds(PART_CELLS, PART_CELLS)], brick_ref),), sems)
    for part in range(SLOTS // LANES):
        here = slice(part * LANES, (part + 1) * LANES)
        back_ref[:, here] = one_hot_ref[here, :].astype(jnp.float32).T.astype(jnp.bfloat16)
    copy.wait()
    out_ref[...] = dot(one_hot_ref[...], brick_ref[...]).astype(jnp.bfloat16)


def write_picks(brick_ref, picks_ref, across_ref):
    for part in range(SLOTS // LANES):
        here = slice(part * LANES, (part + 1) * LANES)
        head = brick_ref[here, PART_CELLS:].astype(jnp.float32)
        turned = pltpu.roll(head, HALF, 1)
        low = low_half(head.shape)
        places = (jnp.where(low, head, turned) * 32.0 + jnp.where(low, turned, head)).astype(jnp.int32)
        for block in range(TILES // LANES):
            there = slice(block * LANES, (block + 1) * LANES)
            lane = lax.broadcasted_iota(jnp.int32, (LANES, LANES), 1) + block * LANES
            square = jnp.where(places == lane, 1.0, 0.0)
            picks_ref[here, there] = square.astype(jnp.bfloat16)
            across_ref[there, here] = square.T.astype(jnp.bfloat16)


def forward_lines(own_ref, brick_ref, across_ref, table_in, sent_refs, left_ref, lines_ref, table_ref, sems):
    [copy] = start_copies(((table_in, table_ref),), sems)
    low = low_half((SPOTS, LANES))
    for q in range(0, BRICK_ROWS // PARTS, 4):
        charge = dot(across_ref[...], brick_ref[:, q * LANES : (q + 4) * LANES])
        for one in range(4):
            there = slice(one * LANES, (one + 1) * LANES)
            here = slice((q + one) * SPOTS, (q + one + 1) * SPOTS)
            points = [charge[ty * SPOTS : (ty + 1) * SPOTS, there] for ty in range(8)]
            for pair, (cosines, sines) in enumerate(class_sums(points)):
                write_left(pair, here, even_odd(cosines, sines, low), left_ref)
    copy.wait()
    for pair in range(PAIRS):
        for one, values in enumerate(line_product(pair, slice(0, PART_ROWS), left_ref, table_ref[pair])):
            most = jnp.max(jnp.abs(values).reshape(PART_ROWS // 8, 8, LANES), axis=0)
            level = level_of(jnp.max(most, axis=0, keepdims=True))
            lines_ref[2 * pair + one, :PART_ROWS, :] = fixed_of(values * inverse_of(level))
            lines_ref[2 * pair + one, PART_ROWS:, :] = head_of(level)
    for offset, sent_ref in zip(SEND, sent_refs):
        sent_ref[...] = lines_ref[own_ref[0] ^ offset]


def forward_first_kernel(own_ref, brick_ref, table_in, *refs):
    sent_refs, (picks_ref, across_ref) = refs[: len(SEND)], refs[len(SEND) : len(SEND) + 2]
    write_picks(brick_ref, picks_ref, across_ref)
    forward_lines(own_ref, brick_ref, across_ref, table_in, sent_refs, *refs[len(SEND) + 2 :])


def forward_later_kernel(own_ref, brick_ref, across_ref, table_in, *refs):
    forward_lines(own_ref, brick_ref, across_ref, table_in, refs[: len(SEND)], *refs[len(SEND) :])


def grid_rows(slabs, plane, xq, tx):
    start = ((plane * 4 + xq) * SPOTS + tx * 4) * slabs
    return pl.ds(pl.multiple_of(start, 4 * slabs), 4 * slabs)


def plane_product(plane_ref, lines):
    high, rest = split(lines)
    rows = plane_ref.shape[0]
    if plane_ref.shape[1] == 3 * high.shape[0]:
        return dot(plane_ref[...], jnp.concatenate([high, rest, high], axis=0))
    both = dot(plane_ref[...], jnp.concatenate([high, rest], axis=0))
    return both[: rows // 2] + both[rows // 2 :]


def add_sines(got_refs, plane_ref, grid_ref, finish):
    slabs = len(got_refs)
    for at, got_ref in enumerate(got_refs):
        grid_ref[pl.ds(at, PART_ROWS, stride=slabs), :] = wide(got_ref)

    def planes(tx, xq):
        return jnp.concatenate(
            [grid_ref[grid_rows(slabs, plane, xq, tx), :] for plane in range(PART_PLANES)], axis=0
        )

    def sines(tx, _):
        modes = plane_product(plane_ref, jnp.concatenate([planes(tx, xq) for xq in range(4)], axis=1))
        for xq in range(4):
            finish(tx * 4 + xq, modes[:, xq * LANES : (xq + 1) * LANES])
        return 0

    lax.fori_loop(0, 16, sines, 0, unroll=8)


def down_first_kernel(own_ref, *refs):
    count = len(ARRIVAL)
    planes_ref, base_ref, lam_ref, modes_ref, root_ref, gain_ref, power_ref, grid_ref = refs[count:]
    excess = base_ref[...] + lam_ref[pl.ds(own_ref[0], 1), :]
    spread = jnp.sqrt(excess * (excess + 4.0))
    root_ref[...] = 2.0 / (2.0 + excess + spread)
    gain_ref[...] = 1.0 / spread
    for part in range(2):
        here = pl.ds(part * PLANES // 2, PLANES // 2)
        square = root_ref[here, :] * root_ref[here, :]

        def raised(step, power):
            power_ref[step, here, :] = power
            return power * square

        lax.fori_loop(0, STEPS, raised, jnp.ones(square.shape, jnp.float32), unroll=8)

    def finish(line, values):
        modes_ref[line] = values

    add_sines(refs[:count], planes_ref.at[own_ref[0]], grid_ref, finish)


def down_later_kernel(own_ref, *refs):
    count = len(ARRIVAL)
    sums_ref, root_ref, planes_ref, walk_ref, end_ref, grid_ref, modes_ref, last_ref = refs[count:]

    def finish(line, values):
        modes_ref[line] = sums_ref[line] + values

    add_sines(refs[:count], planes_ref.at[own_ref[0]], grid_ref, finish)
    part_rows = 64
    low = low_half((part_rows, LANES))
    for part in range(PLANES // part_rows):
        here = pl.ds(part * part_rows, part_rows)
        root = root_ref[here, :]
        square = root * root

        def walk(step, held):
            ahead, behind = modes_ref[step, here, :], modes_ref[STEPS - 1 - step, here, :]
            own = jnp.where(low, behind, ahead)
            other = pltpu.roll(jnp.where(low, ahead, behind), HALF, 1)
            held = square * held + (own + root * other)
            walk_ref[step, here, :] = held
            return held

        last_ref[here, :] = lax.fori_loop(0, STEPS, walk, jnp.zeros((part_rows, LANES), jnp.float32), unroll=8)
    last = last_ref[...]
    level = level_of(jnp.max(jnp.abs(last), axis=0, keepdims=True))
    end_ref[:PLANES, :] = fixed_of(last * inverse_of(level))
    end_ref[PLANES:, :] = head_of(level)


def local_kernel(walk_ref, root_ref, gain_ref, local_ref):
    part_rows = 64
    low = low_half((part_rows, LANES))
    for part in range(PLANES // part_rows):
        here = pl.ds(part * part_rows, part_rows)
        root, gain = root_ref[here, :], gain_ref[here, :]
        zero = jnp.zeros(root.shape, jnp.float32)

        def line(step, ahead_before, behind_after):
            near = jnp.where(low, walk_ref[STEPS - 1 - step, here, :], walk_ref[step, here, :])
            far = pltpu.roll(jnp.where(low, behind_after, ahead_before), HALF, 1)
            local_ref[step, here, :] = gain * (near + root * far)

        def inner(step, _):
            line(step, walk_ref[step - 1, here, :], walk_ref[STEPS - 2 - step, here, :])
            return 0

        line(0, zero, walk_ref[STEPS - 2, here, :])
        lax.fori_loop(1, STEPS - 1, inner, 0, unroll=6)
        line(STEPS - 1, walk_ref[STEPS - 2, here, :], zero)


def up_kernel(own_ref, local_ref, power_ref, root_ref, gain_ref, *refs):
    end_refs, plane_ref = refs[:GROUPS], refs[GROUPS].at[own_ref[0]]
    count = GROUPS + 1 + len(SEND)
    sent_refs = refs[GROUPS + 1 : count]
    rise_ref, fall_ref, grid_ref, level_ref = refs[count:]
    low = low_half((PLANES, LANES))
    root = root_ref[...]
    square = root * root
    across = square
    for _ in range(6):
        across = across * across
    around = across
    for _ in range(2):
        around = around * around
    ends = [wide(end_ref) for end_ref in end_refs]
    entering = jnp.zeros((PLANES, LANES), jnp.float32)
    for step in range(GROUPS - 1, -1, -1):
        entering = entering * across + jnp.where(low, ends[GROUPS - 1 - step], ends[(step + 1) % GROUPS])
    entering = gain_ref[...] * entering / (1.0 - around)
    straight, turned = square * entering, root * pltpu.roll(entering, HALF, 1)
    rise_ref[...] = jnp.where(low, turned, straight)
    fall_ref[...] = jnp.where(low, straight, turned)
    slabs = len(sent_refs)

    def solved(step):
        reach = rise_ref[...] * power_ref[step] + fall_ref[...] * power_ref[STEPS - 1 - step]
        return local_ref[step] + reach

    def sines(tx, most):
        lines = plane_product(plane_ref, jnp.concatenate([solved(tx * 4 + xq) for xq in range(4)], axis=1))
        for xq in range(4):
            part = lines[:, xq * LANES : (xq + 1) * LANES]
            most = jnp.maximum(most, jnp.max(jnp.abs(part).reshape(4 * BZ, slabs, LANES), axis=0))
            for plane in range(BZ):
                grid_ref[grid_rows(slabs, plane, xq, tx), :] = part[plane * 4 * slabs : (plane + 1) * 4 * slabs]
        return most

    most = lax.fori_loop(0, 16, sines, jnp.zeros((slabs, LANES), jnp.float32), unroll=8)
    level_ref[...] = level_of(most)
    for at, sent_ref in enumerate(sent_refs):
        level = level_ref[at : at + 1, :]
        sent_ref[:ROWS, :] = fixed_of(grid_ref[pl.ds(at, ROWS, stride=slabs), :] * inverse_of(level))
        sent_ref[ROWS:, :] = head_of(level)


def take_lines(own_ref, offsets, got_refs, left_ref, lines_ref):
    own = own_ref[0]
    pairs = list(dict.fromkeys(offset // 2 for offset in offsets))
    for offset, got_ref in zip(offsets, got_refs):
        lines_ref[2 * pairs.index(offset // 2) + ((own ^ offset) & 1)] = wide(got_ref)
    low = low_half((DOT_ROWS, LANES))
    for at in range(len(pairs)):
        for start in range(0, ROWS, DOT_ROWS):
            here = slice(start, start + DOT_ROWS)
            write_left(at, here, even_odd(lines_ref[2 * at, here, :], lines_ref[2 * at + 1, here, :], low), left_ref)
    return [(own >> 1) ^ pair for pair in pairs]


def point_parts(pair, cosines, sines, weight_ref):
    for ty in range(4):
        part = weight_ref[pair, ty] * cosines + weight_ref[pair, 4 + ty] * sines
        yield ty, part
        yield ty + 4, weight_ref[pair, 8] * part


def reply_first_kernel(own_ref, weight_ref, *refs):
    count = len(TAKE_FIRST)
    table_ref, sums_ref, lines_ref, left_ref = refs[count:]
    pairs = take_lines(own_ref, TAKE_FIRST, refs[:count], left_ref, lines_ref)
    for at, pair in enumerate(pairs):
        for part in range(ROWS // DOT_ROWS):
            here = slice(part * DOT_ROWS, (part + 1) * DOT_ROWS)
            cosines, sines = line_product(at, here, left_ref, table_ref[pair])
            for ty, values in point_parts(pair, cosines, sines, weight_ref):
                sums_ref[ty, here, :] = values if at == 0 else sums_ref[ty, here, :] + values


def reply_later_kernel(own_ref, weight_ref, *refs):
    count = len(TAKE_LATER)
    sums_ref, picks_ref, table_ref, out_ref, lines_ref, left_ref, pot_ref = refs[count:]
    [pair] = take_lines(own_ref, TAKE_LATER, refs[:count], left_ref, lines_ref)
    for part in range(ROWS // DOT_ROWS):
        here = slice(part * DOT_ROWS, (part + 1) * DOT_ROWS)
        cosines, sines = line_product(0, here, left_ref, table_ref[pair])
        for ty, values in point_parts(pair, cosines, sines, weight_ref):
            values = (sums_ref[ty, here, :] + values).astype(jnp.bfloat16)
            for one in range(DOT_ROWS // SPOTS):
                q = part * (DOT_ROWS // SPOTS) + one
                pot_ref[ty * SPOTS : (ty + 1) * SPOTS, q * LANES : (q + 1) * LANES] = values[
                    one * SPOTS : (one + 1) * SPOTS
                ]
    for q in range(0, BRICK_ROWS, 4):
        there = slice(q * LANES, (q + 4) * LANES)
        out_ref[:, there] = dot(picks_ref[...], pot_ref[:, there]).astype(jnp.bfloat16)


def unpack_kernel(back_ref, got_ref, out_ref):
    for q in range(0, BRICK_ROWS, 4):
        there = slice(q * LANES, (q + 4) * LANES)
        out_ref[:, there] = dot(back_ref[...], got_ref[:, there]).astype(jnp.bfloat16)


def call(kernel, name, operands, spaces, outs, places, scratch, vmem=VMEM_BYTES):
    return pl.pallas_call(
        kernel,
        out_shape=outs,
        in_specs=[pl.BlockSpec(memory_space=space) for space in spaces],
        out_specs=[pl.BlockSpec(memory_space=space) for space in places],
        scratch_shapes=scratch,
        compiler_params=pltpu.CompilerParams(vmem_limit_bytes=vmem),
        name=name,
    )(*operands)


def on_device_8x4(bricks, owners, tile_ids, counts):
    V, S, H = pltpu.VMEM, pltpu.SMEM, pltpu.HBM
    f32, bf16, i32, i16 = jnp.float32, jnp.bfloat16, jnp.int32, jnp.int16
    shape, dma = jax.ShapeDtypeStruct, pltpu.SemaphoreType.DMA
    brick_rows = bricks.shape[0]
    lines_in, lines_out = (jnp.asarray(each) for each in line_tables())
    weights = jnp.asarray(class_weights())
    lines_in = pltpu.with_memory_space_constraint(lines_in, H)
    planes_in = [jnp.asarray(plane_tables(ARRIVAL, planes, False)) for planes in ((0, 1), (2, 3))]
    planes_out = jnp.asarray(plane_tables(SEND, range(BZ), True))
    base, lam = (jnp.asarray(each) for each in mode_tables())
    own = lax.axis_index("gz").astype(i32).reshape(1)
    sent_shape = shape((ROWS + HEAD_ROWS, LANES), i16)
    end_shape = shape((PLANES + HEAD_ROWS, LANES), i16)
    cube, flat, sums_shape = (STEPS, PLANES, LANES), (PLANES, LANES), (8, ROWS, LANES)
    line, packed = (ROWS, LANES), [(SLOTS, PART_CELLS + LANES), (SLOTS, PART_CELLS)]
    part_shape = shape((PART_ROWS + HEAD_ROWS, LANES), i16)

    def all_ways(values):
        return lax.all_to_all(values, ("gz", "ma"), split_axis=0, concat_axis=0, tiled=True)

    def over_slabs(offset, values):
        return lax.ppermute(values, "gz", [(g, g ^ offset) for g in range(SLABS)]) if offset else values

    def round_groups(values, step):
        return lax.ppermute(values, "ma", [(m, (m + step) % GROUPS) for m in range(GROUPS)]) if step else values

    def exchanged(sent):
        sent = dict(zip(SEND, sent))
        return [over_slabs(offset, sent[offset]) for offset in ARRIVAL]

    outgoing, one_hot = call(
        pack_kernel,
        "pack",
        (owners.reshape(brick_rows), tile_ids, counts, bricks),
        [H] * 4,
        [shape(packed[0], bf16), shape((SLOTS, brick_rows), bf16)],
        [H, V],
        [
            S((brick_rows,), i32),
            S((brick_rows,), i32),
            S((1,), i32),
            V((brick_rows, PART_CELLS), bf16),
            V((SLOTS + PAIR_SLOTS, brick_rows), f32),
            V((SLOTS + PAIR_SLOTS, LANES), f32),
            V(packed[0], bf16),
            S((DOMAINS,), i32),
            dma((4,)),
            dma((4,)),
        ],
        ALL_VMEM_BYTES,
    )
    outgoing_later, back = call(
        pack_later_kernel,
        "pack_later",
        (bricks, one_hot),
        [H, V],
        [shape(packed[1], bf16), shape((brick_rows, SLOTS), bf16)],
        [V, V],
        [V((brick_rows, PART_CELLS), bf16), dma((1,))],
    )
    incoming = [all_ways(outgoing), all_ways(outgoing_later)]
    forward_scratch = [
        V((PAIRS, 2 * PART_ROWS, 2 * LANES), bf16),
        V((len(SEND), *part_shape.shape), i16),
        V(lines_in.shape, bf16),
        dma((1,)),
    ]
    *sent, picks, across = call(
        forward_first_kernel,
        "forward_first",
        (own, incoming[0], lines_in),
        [S, V, H],
        [part_shape] * len(SEND) + [shape((SLOTS, TILES), bf16), shape((TILES, SLOTS), bf16)],
        [V] * (len(SEND) + 2),
        forward_scratch,
    )
    first = exchanged(sent)
    second, first[1], first[2] = lax.optimization_barrier((incoming[1], first[1], first[2]))
    sent = call(
        forward_later_kernel,
        "forward_later",
        (own, second, across, lines_in),
        [S, V, V, H],
        [part_shape] * len(SEND),
        [V] * len(SEND),
        forward_scratch,
    )
    later = exchanged(sent)
    sums, root, gain, power = call(
        down_first_kernel,
        "down_first",
        (own, *first, planes_in[0], base, lam),
        [S] + [V] * (len(first) + 3),
        [shape(cube, f32), shape(flat, f32), shape(flat, f32), shape(cube, f32)],
        [V] * 4,
        [
            V((len(first) * PART_ROWS, LANES), f32),
        ],
    )
    walk, end = call(
        down_later_kernel,
        "down_later",
        (own, *later, sums, root, planes_in[1]),
        [S] + [V] * (len(later) + 3),
        [shape(cube, f32), end_shape],
        [V, V],
        [
            V((len(later) * PART_ROWS, LANES), f32),
            V(cube, f32),
            V(flat, f32),
        ],
    )
    ends = [round_groups(end, step) for step in range(GROUPS)]
    (local,) = call(local_kernel, "local", (walk, root, gain), [V] * 3, [shape(cube, f32)], [V], [])
    sent = call(
        up_kernel,
        "up",
        (own, local, power, root, gain, *ends, planes_out),
        [S] + [V] * (5 + GROUPS),
        [sent_shape] * len(SEND),
        [V] * len(SEND),
        [
            V(flat, f32),
            V(flat, f32),
            V((len(SEND) * ROWS, LANES), f32),
            V((len(SEND), LANES), f32),
        ],
    )
    got = exchanged(sent)
    first, later = got[: len(TAKE_FIRST)], got[len(TAKE_FIRST) :]
    (sums,) = call(
        reply_first_kernel,
        "reply_first",
        (own, weights, *first, lines_out),
        [S, S] + [V] * (len(first) + 1),
        [shape(sums_shape, f32)],
        [V],
        [V((len(first), *line), f32), V((len(first) // 2, 2 * ROWS, 2 * LANES), bf16)],
    )
    (replies,) = call(
        reply_later_kernel,
        "reply_later",
        (own, weights, *later, sums, picks, lines_out),
        [S, S] + [V] * (len(later) + 3),
        [shape((SLOTS, CELLS), bf16)],
        [V],
        [
            V((len(later), *line), f32),
            V((len(later) // 2, 2 * ROWS, 2 * LANES), bf16),
            V((TILES, CELLS), bf16),
        ],
    )
    (result,) = call(
        unpack_kernel,
        "unpack",
        (back, all_ways(replies)),
        [V, V],
        [shape((brick_rows, CELLS), bf16)],
        [V],
        [],
    )
    return result


def solution(mesh):
    in_specs = (P(("gz", "ma"), None), P(("gz", "ma"), None), P(("gz", "ma")), P(("gz", "ma")))
    out_specs = P(("gz", "ma"), None)
    body = on_device_8x4 if (mesh.shape["gz"], mesh.shape["ma"]) == (SLABS, GROUPS) else on_device
    return jax.shard_map(body, mesh=mesh, in_specs=in_specs, out_specs=out_specs, check_vma=False)
```

```python
import math

import jax
import jax.numpy as jnp
import ml_dtypes
import numpy as np
from jax import lax
from jax.experimental import pallas as pl
from jax.experimental.pallas import tpu as pltpu
from jax.sharding import PartitionSpec as P

NX = 512
NY = 512
SCREEN = 16
BZ = 4
BX = 8
BY = 64
CZ = 16


def hartley(length):
    indices = jnp.arange(length, dtype=jnp.int32)
    products = indices[:, None] * indices[None, :] % length
    angles = 2.0 * math.pi / length * products.astype(jnp.float32)
    return (jnp.cos(angles) + jnp.sin(angles)) / math.sqrt(length)


def second_difference(length, indices):
    return 2.0 - 2.0 * jnp.cos(2.0 * math.pi / length * indices.astype(jnp.float32))


def thomas(right_side, diagonal):
    start_zero = jnp.zeros(right_side.shape[1:], jnp.float32)

    def down(state_pair, plane):
        factor = 1.0 / (diagonal - state_pair[0])
        partial_value = (plane + state_pair[1]) * factor
        return ((factor, partial_value), (factor, partial_value))

    _, (factors, partials) = lax.scan(down, (start_zero, start_zero), right_side)

    def upward(beyond, factor_partial):
        solved = factor_partial[1] + factor_partial[0] * beyond
        return (solved, solved)

    _, solutions = lax.scan(upward, start_zero, (factors, partials), reverse=True)
    return solutions


def regroup(values):
    return lax.all_to_all(values, "ma", split_axis=2, concat_axis=1, tiled=True)


def on_device(bricks, owners, tile_ids, counts):
    domains = lax.axis_size(("gz", "ma"))
    group_count = lax.axis_size("ma")
    slab_count = lax.axis_size("gz")
    brick_rows, brick_cells = bricks.shape
    slot_count = max(2, 2 * brick_rows // domains)
    local_x = NX // group_count
    local_y = NY // group_count
    tiles_dev = CZ // BZ * (local_x // BX) * (NY // BY)
    highest = lax.Precision.HIGHEST
    target = owners[:, 0]
    row_order = jnp.arange(brick_rows, dtype=jnp.int32)
    earlier_same = (target[:, None] == target[None, :]) & (row_order[None, :] < row_order[:, None])
    within = jnp.sum(earlier_same.astype(jnp.int32), axis=1)
    slot_of = target * slot_count + within
    is_live = row_order < counts[0]
    loaded = jnp.where(is_live[:, None], bricks, jnp.zeros_like(bricks))
    outgoing = jnp.zeros((domains * slot_count, brick_cells), jnp.bfloat16).at[slot_of].set(loaded)
    out_ids = jnp.full((domains * slot_count,), tiles_dev, jnp.int32).at[slot_of].set(tile_ids)
    incoming, in_ids = (
        lax.all_to_all(outgoing, ("gz", "ma"), split_axis=0, concat_axis=0, tiled=True),
        lax.all_to_all(out_ids, ("gz", "ma"), split_axis=0, concat_axis=0, tiled=True),
    )
    picker = (jnp.arange(tiles_dev, dtype=jnp.int32)[:, None] == in_ids[None, :]).astype(
        jnp.bfloat16
    )
    deposit = jnp.dot(picker, incoming, preferred_element_type=jnp.float32)
    charge = deposit.reshape(CZ // BZ, local_x // BX, NY // BY, BZ, BX, BY)
    charge = charge.transpose(0, 3, 1, 4, 2, 5).reshape(CZ, local_x, NY)
    table_x = hartley(NX)
    table_y = hartley(NY)
    along_y = jnp.einsum("zxy,ky->zxk", charge, table_y, precision=highest)
    gathered_x = regroup(along_y)
    spectrum = jnp.einsum("zxk,jx->zjk", gathered_x, table_x, precision=highest)
    columns = lax.axis_index("ma") * local_y + jnp.arange(local_y, dtype=jnp.int32)
    lam_y = second_difference(NY, columns)
    screening = 1.0 / (SCREEN * SCREEN)
    slab_index = lax.axis_index("gz")
    lam_x = second_difference(NX, jnp.arange(NX, dtype=jnp.int32))
    diagonal = 2.0 + screening + lam_x[:, None] + lam_y[None, :]
    interior = spectrum[1:]
    particular = thomas(interior, diagonal)
    unit_rhs = jnp.zeros_like(interior).at[0].set(1.0)
    spike = thomas(unit_rhs, diagonal)
    near_weight = spike[0]
    far_weight = spike[-1]
    head_term = spectrum[0] + particular[0]
    tail_term = particular[-1]
    reduced_first = diagonal - near_weight
    reduced_rest = diagonal - 2.0 * near_weight
    start_zero = jnp.zeros_like(diagonal)
    heads, tails = (
        lax.all_gather(head_term[None], "gz", axis=0, tiled=True),
        lax.all_gather(tail_term[None], "gz", axis=0, tiled=True),
    )
    before = jnp.concatenate([start_zero[None], tails[:-1]], axis=0)
    sources = heads + before

    def chain_down(state_pair, packed):
        source, position = packed
        base_term = jnp.where(position == 0, reduced_first, reduced_rest)
        pivot_now = 1.0 / (base_term - far_weight * far_weight * state_pair[0])
        forward_part = pivot_now * (source + far_weight * state_pair[1])
        return ((pivot_now, forward_part), (pivot_now, forward_part))

    _, (pivots, forwards) = lax.scan(
        chain_down, (start_zero, start_zero), (sources, jnp.arange(slab_count, dtype=jnp.int32))
    )

    def chain_up(beyond, packed):
        plane_value = packed[1] + far_weight * packed[0] * beyond
        return (plane_value, plane_value)

    _, separators = lax.scan(chain_up, start_zero, (pivots, forwards), reverse=True)
    padded_sep = jnp.concatenate([separators, start_zero[None]], axis=0)
    own_plane = lax.dynamic_index_in_dim(padded_sep, slab_index, 0, keepdims=False)
    next_plane = lax.dynamic_index_in_dim(padded_sep, slab_index + 1, 0, keepdims=False)
    interior_sol = particular + own_plane[None] * spike + next_plane[None] * spike[::-1]
    modal = jnp.concatenate([own_plane[None], interior_sol], axis=0)
    back_x = jnp.einsum("zjk,jx->zkx", modal, table_x, precision=highest)
    gathered_y = regroup(back_x)
    potential = jnp.einsum("zkx,ky->zxy", gathered_y, table_y, precision=highest)
    pot_tiles = potential.reshape(CZ // BZ, BZ, local_x // BX, BX, NY // BY, BY)
    pot_tiles = (
        pot_tiles.transpose(0, 2, 4, 1, 3, 5).reshape(tiles_dev, brick_cells).astype(jnp.bfloat16)
    )
    padded_tiles = jnp.concatenate([pot_tiles, jnp.zeros((1, brick_cells), jnp.bfloat16)], axis=0)
    replies = padded_tiles[in_ids]
    returned = lax.all_to_all(replies, ("gz", "ma"), split_axis=0, concat_axis=0, tiled=True)
    result = returned[slot_of]
    return jnp.where(is_live[:, None], result, jnp.zeros_like(result))


DOMAINS = 32
GROUPS = 4
SLABS = 8
SEND = (4, 2, 5, 3, 0, 1, 6, 7)
ARRIVAL = (0, 4, 2, 5, 3, 1, 6, 7)
PARTS = 2
PART_PLANES = 2
TAKE_FIRST = (0, 4, 2, 5, 3, 1)
TAKE_LATER = (6, 7)
PAIR_SLOTS = 8
SLOTS = DOMAINS * PAIR_SLOTS
TILES = 512
BRICK_ROWS = 16
CELLS = 2048
LANES = 128
HALF = 64
SPOTS = 64
ROWS = BRICK_ROWS * SPOTS
PART_ROWS = ROWS // PARTS
PART_CELLS = CELLS // PARTS
DOT_ROWS = 512
PAIRS = 4
CLASSES = (0, 4, 1, 7, 2, 6, 3, 5)
HEAD_ROWS = 8
STEPS = 64
PLANES = 128
FULL = 32700.0
LOG_UNIT = 128.0
VMEM_BYTES = 24 * 1024 * 1024
ALL_VMEM_BYTES = 60 * 1024 * 1024


def split_table(table):
    high = table.astype(ml_dtypes.bfloat16)
    low = (table - high.astype(np.float64)).astype(ml_dtypes.bfloat16)
    return high, low


def line_tables():
    iy, k2 = np.arange(HALF)[:, None], np.arange(HALF)[None, :]
    tables = []
    for pair in range(PAIRS):
        table = np.zeros((LANES, LANES))
        for one in range(2):
            angle = 2.0 * np.pi / NY * (iy * (CLASSES[2 * pair + one] + 8 * k2) % NY)
            cosine, sine = np.cos(angle) / np.sqrt(NY), np.sin(angle) / np.sqrt(NY)
            there = slice(one * HALF, (one + 1) * HALF)
            if pair == 0:
                table[there, there] = cosine + sine
            else:
                table[:HALF, there] = cosine + sine
                table[HALF:, there] = (cosine - sine) * (1 - 2 * one)
        tables.append(table)

    def stacked(table):
        high, low = split_table(table)
        return np.concatenate(
            [np.concatenate([high, low], axis=1), np.concatenate([high, np.zeros_like(low)], axis=1)], axis=0
        )

    return np.stack([stacked(table) for table in tables]), np.stack([stacked(table.T) for table in tables])


def class_weights():
    pair, ty = np.arange(PAIRS)[:, None], np.arange(4)[None, :]
    cosine, sine = np.cos(np.pi / 4.0 * pair * ty), np.sin(np.pi / 4.0 * pair * ty)
    sine[0] = (-1.0) ** np.arange(4)
    sign = (-1.0) ** pair * np.ones((1, 4))
    return np.concatenate([cosine, sine, sign], axis=1).astype(np.float32)


def plane_tables(offsets, planes, turned):
    index = np.arange(PLANES)
    table = np.sqrt(2.0 / (PLANES + 1)) * np.sin(
        np.pi / (PLANES + 1) * ((index[:, None] + 1) * (index[None, :] + 1) % (2 * PLANES + 2))
    )
    each = []
    for own in range(SLABS):
        slabs = np.array([own ^ offset for offset in offsets])
        plane, tz = np.array(planes)[:, None, None], np.arange(BZ)[None, :, None]
        part = table[:, (slabs * CZ + tz * BZ + plane).reshape(-1)]
        high, low = split_table(part.T if turned else part)
        if 3 * high.shape[1] <= 2 * LANES:
            each.append(np.concatenate([high, high, low], axis=1))
            continue
        top = np.concatenate([high, high], axis=1)
        bottom = np.concatenate([low, np.zeros_like(low)], axis=1)
        each.append(np.concatenate([top, bottom], axis=0))
    return np.stack(each)


def mode_tables():
    mu = 2.0 - 2.0 * np.cos(np.pi / (PLANES + 1) * (np.arange(PLANES) + 1))
    base = np.broadcast_to((mu + 1.0 / (SCREEN * SCREEN))[:, None], (PLANES, LANES))
    lam = 2.0 - 2.0 * np.cos(2.0 * np.pi / NY * np.arange(NY))
    lam = np.stack([lam[number::8] for number in CLASSES])
    return base.astype(np.float32), np.concatenate([lam, lam], axis=1).astype(np.float32)


def low_half(shape):
    return lax.broadcasted_iota(jnp.int32, shape, len(shape) - 1) < HALF


def split(values):
    high = values.astype(jnp.bfloat16)
    return high, (values - high.astype(jnp.float32)).astype(jnp.bfloat16)


def dot(left, right):
    return jnp.dot(left, right, preferred_element_type=jnp.float32)


def start_copies(pairs, sems):
    copies = [pltpu.make_async_copy(source, place, sems.at[at]) for at, (source, place) in enumerate(pairs)]
    for each in copies:
        each.start()
    return copies


def even_odd(first, second, low):
    crossed = pltpu.roll(jnp.where(low, second, first), HALF, 1)
    return jnp.where(low, first, crossed), jnp.where(low, crossed, second)


def write_left(at, here, lines, left_ref):
    rows = left_ref.shape[1] // 2
    for line, values in enumerate(lines):
        high, rest = split(values)
        there = slice(line * rows + here.start, line * rows + here.stop)
        left_ref[at, there, :LANES] = high
        left_ref[at, there, LANES:] = rest


def line_product(at, here, left_ref, table):
    products = []
    rows = left_ref.shape[1] // 2
    for line in range(2):
        there = slice(line * rows + here.start, line * rows + here.stop)
        both = dot(left_ref[at, there, :], table)
        products.append(both[:, :LANES] + both[:, LANES:])
    return even_odd(*products, low_half(products[0].shape))


def class_sums(points):
    half = [points[ty] + points[ty + 4] for ty in range(4)]
    rest = [points[ty] - points[ty + 4] for ty in range(4)]
    even, odd = half[0] + half[2], half[1] + half[3]
    turn = math.sqrt(0.5)
    across, along = turn * (rest[1] - rest[3]), turn * (rest[1] + rest[3])
    return (
        (even + odd, even - odd),
        (rest[0] + across, rest[2] + along),
        (half[0] - half[2], half[1] - half[3]),
        (rest[0] - across, along - rest[2]),
    )


def level_of(most):
    return jnp.floor(jnp.log2(jnp.maximum(most, 1e-30)) * LOG_UNIT) + 2.0


def inverse_of(level):
    return FULL * jnp.exp2(level * (-1.0 / LOG_UNIT))


def fixed_of(values):
    return jnp.floor(values + 0.5).astype(jnp.int32).astype(jnp.int16)


def head_of(level):
    return jnp.broadcast_to(level, (HEAD_ROWS, LANES)).astype(jnp.int32).astype(jnp.int16)


def unit_of(sent_ref):
    head = sent_ref[sent_ref.shape[0] - HEAD_ROWS :, :].astype(jnp.int32).astype(jnp.float32)
    return jnp.exp2(head[0:1] * (1.0 / LOG_UNIT)) * (1.0 / FULL)


def wide(sent_ref):
    block = sent_ref[: sent_ref.shape[0] - HEAD_ROWS, :]
    return block.astype(jnp.int32).astype(jnp.float32) * unit_of(sent_ref)


def pack_kernel(
    owner_in, tile_in, count_in, brick_in, out_ref, one_hot_ref, code_ref,
    owner_ref, tile_ref, count_ref, brick_ref, pick_ref, ready_ref, used_ref, sems, out_sems,
):
    cells = brick_in.at[:, pl.ds(0, PART_CELLS)]
    copies = start_copies(((owner_in, owner_ref), (tile_in, tile_ref), (count_in, count_ref), (cells, brick_ref)), sems)
    brick_rows = brick_ref.shape[0]
    pick_ref[...] = jnp.zeros(pick_ref.shape, jnp.float32)
    for owner in range(DOMAINS):
        used_ref[owner] = 0
    for each in copies[:3]:
        each.wait()
    count = count_ref[0]
    lane = lax.broadcasted_iota(jnp.int32, (1, brick_rows), 1)

    def place(r, _):
        owner = owner_ref[r]
        within = used_ref[owner]
        used_ref[owner] = within + 1
        slot = jnp.where(r < count, owner * PAIR_SLOTS + within, SLOTS)
        tile = tile_ref[r]
        position = (tile & 7) * SPOTS + ((tile >> 3) & 15) * 4 + (tile >> 7)
        code_ref[r] = jnp.where(r < count, owner * TILES + position, -1)
        pick_ref[pl.ds(slot, 1), :] = jnp.where(lane == r, 1.0, 0.0)
        return 0

    lax.fori_loop(0, brick_rows, place, 0, unroll=8)
    copies[3].wait()
    copies = []
    rows = 64
    for part in range(SLOTS // rows):
        here = slice(part * rows, (part + 1) * rows)
        picks = pick_ref[here, :].astype(jnp.bfloat16)
        one_hot_ref[here, :] = picks
        ready_ref[here, :] = dot(picks, brick_ref[...]).astype(jnp.bfloat16)
        some = pl.ds(part * rows, rows)
        copies.append(pltpu.make_async_copy(ready_ref.at[some], out_ref.at[some], out_sems.at[part]))
        copies[-1].start()
    for each in copies:
        each.wait()


def pack_later_kernel(brick_in, one_hot_ref, out_ref, back_ref, brick_ref, sems):
    [copy] = start_copies(((brick_in.at[:, pl.ds(PART_CELLS, PART_CELLS)], brick_ref),), sems)
    for part in range(SLOTS // LANES):
        here = slice(part * LANES, (part + 1) * LANES)
        back_ref[:, here] = one_hot_ref[here, :].astype(jnp.float32).T.astype(jnp.bfloat16)
    copy.wait()
    out_ref[...] = dot(one_hot_ref[...], brick_ref[...]).astype(jnp.bfloat16)


def picks_kernel(place_ref, code_ref, picks_ref, across_ref, spot_ref):
    code = code_ref[...]
    mine = jnp.where((code >> 9) == place_ref[0], 1.0, 0.0)
    rows = code.shape[1]
    before = lax.broadcasted_iota(jnp.int32, (rows, rows), 0) < lax.broadcasted_iota(jnp.int32, (rows, rows), 1)
    rank = dot(mine.astype(jnp.bfloat16), jnp.where(before, 1.0, 0.0).astype(jnp.bfloat16))
    spot = mine * ((code & (TILES - 1)) + 1).astype(jnp.float32)
    for within in range(PAIR_SLOTS):
        found = jnp.sum(jnp.where(rank == float(within), spot, 0.0), axis=1, keepdims=True)
        spot_ref[pl.ds(within, DOMAINS, stride=PAIR_SLOTS), :] = jnp.broadcast_to(found, (DOMAINS, LANES))
    for part in range(SLOTS // LANES):
        here = slice(part * LANES, (part + 1) * LANES)
        places = spot_ref[here, :].astype(jnp.int32) - 1
        for block in range(TILES // LANES):
            there = slice(block * LANES, (block + 1) * LANES)
            lane = lax.broadcasted_iota(jnp.int32, (LANES, LANES), 1) + block * LANES
            square = jnp.where(places == lane, 1.0, 0.0)
            picks_ref[here, there] = square.astype(jnp.bfloat16)
            across_ref[there, here] = square.T.astype(jnp.bfloat16)


def write_left(at, here, lines, left_ref):
    rows = left_ref.shape[1] // 2
    for line, values in enumerate(lines):
        high, rest = split(values)
        there = slice(line * rows + here.start, line * rows + here.stop)
        left_ref[at, there, :LANES] = high
        left_ref[at, there, LANES:] = rest


def line_product(at, here, left_ref, table):
    products = []
    rows = left_ref.shape[1] // 2
    for line in range(2):
        there = slice(line * rows + here.start, line * rows + here.stop)
        both = dot(left_ref[at, there, :], table)
        products.append(both[:, :LANES] + both[:, LANES:])
    return even_odd(*products, low_half(products[0].shape))


def class_sums(points):
    half = [points[ty] + points[ty + 4] for ty in range(4)]
    rest = [points[ty] - points[ty + 4] for ty in range(4)]
    even, odd = half[0] + half[2], half[1] + half[3]
    turn = math.sqrt(0.5)
    across, along = turn * (rest[1] - rest[3]), turn * (rest[1] + rest[3])
    return (
        (even + odd, even - odd),
        (rest[0] + across, rest[2] + along),
        (half[0] - half[2], half[1] - half[3]),
        (rest[0] - across, along - rest[2]),
    )


def level_of(most):
    return jnp.floor(jnp.log2(jnp.maximum(most, 1e-30)) * LOG_UNIT) + 2.0


def inverse_of(level):
    return FULL * jnp.exp2(level * (-1.0 / LOG_UNIT))


def fixed_of(values):
    return jnp.floor(values + 0.5).astype(jnp.int32).astype(jnp.int16)


def head_of(level):
    return jnp.broadcast_to(level, (HEAD_ROWS, LANES)).astype(jnp.int32).astype(jnp.int16)


def unit_of(sent_ref):
    head = sent_ref[sent_ref.shape[0] - HEAD_ROWS :, :].astype(jnp.int32).astype(jnp.float32)
    return jnp.exp2(head[0:1] * (1.0 / LOG_UNIT)) * (1.0 / FULL)


def wide(sent_ref):
    block = sent_ref[: sent_ref.shape[0] - HEAD_ROWS, :]
    return block.astype(jnp.int32).astype(jnp.float32) * unit_of(sent_ref)


def pack_kernel(
    owner_in, tile_in, count_in, brick_in, out_ref, one_hot_ref, code_ref,
    owner_ref, tile_ref, count_ref, brick_ref, pick_ref, ready_ref, used_ref, sems, out_sems,
):
    cells = brick_in.at[:, pl.ds(0, PART_CELLS)]
    copies = start_copies(((owner_in, owner_ref), (tile_in, tile_ref), (count_in, count_ref), (cells, brick_ref)), sems)
    brick_rows = brick_ref.shape[0]
    pick_ref[...] = jnp.zeros(pick_ref.shape, jnp.float32)
    for owner in range(DOMAINS):
        used_ref[owner] = 0
    for each in copies[:3]:
        each.wait()
    count = count_ref[0]
    lane = lax.broadcasted_iota(jnp.int32, (1, brick_rows), 1)

    def place(r, _):
        owner = owner_ref[r]
        within = used_ref[owner]
        used_ref[owner] = within + 1
        slot = jnp.where(r < count, owner * PAIR_SLOTS + within, SLOTS)
        tile = tile_ref[r]
        position = (tile & 7) * SPOTS + ((tile >> 3) & 15) * 4 + (tile >> 7)
        code_ref[r] = jnp.where(r < count, owner * TILES + position, -1)
        pick_ref[pl.ds(slot, 1), :] = jnp.where(lane == r, 1.0, 0.0)
        return 0

    lax.fori_loop(0, brick_rows, place, 0, unroll=8)
    copies[3].wait()
    copies = []
    rows = 64
    for part in range(SLOTS // rows):
        here = slice(part * rows, (part + 1) * rows)
        picks = pick_ref[here, :].astype(jnp.bfloat16)
        one_hot_ref[here, :] = picks
        ready_ref[here, :] = dot(picks, brick_ref[...]).astype(jnp.bfloat16)
        some = pl.ds(part * rows, rows)
        copies.append(pltpu.make_async_copy(ready_ref.at[some], out_ref.at[some], out_sems.at[part]))
        copies[-1].start()
    for each in copies:
        each.wait()


def pack_later_kernel(brick_in, one_hot_ref, out_ref, back_ref, brick_ref, sems):
    [copy] = start_copies(((brick_in.at[:, pl.ds(PART_CELLS, PART_CELLS)], brick_ref),), sems)
    for part in range(SLOTS // LANES):
        here = slice(part * LANES, (part + 1) * LANES)
        back_ref[:, here] = one_hot_ref[here, :].astype(jnp.float32).T.astype(jnp.bfloat16)
    copy.wait()
    out_ref[...] = dot(one_hot_ref[...], brick_ref[...]).astype(jnp.bfloat16)


def write_picks(brick_ref, picks_ref, across_ref):
    for part in range(SLOTS // LANES):
        here = slice(part * LANES, (part + 1) * LANES)
        head = brick_ref[here, PART_CELLS:].astype(jnp.float32)
        turned = pltpu.roll(head, HALF, 1)
        low = low_half(head.shape)
        places = (jnp.where(low, head, turned) * 32.0 + jnp.where(low, turned, head)).astype(jnp.int32)
        for block in range(TILES // LANES):
            there = slice(block * LANES, (block + 1) * LANES)
            lane = lax.broadcasted_iota(jnp.int32, (LANES, LANES), 1) + block * LANES
            square = jnp.where(places == lane, 1.0, 0.0)
            picks_ref[here, there] = square.astype(jnp.bfloat16)
            across_ref[there, here] = square.T.astype(jnp.bfloat16)


def forward_kernel(own_ref, brick_ref, across_ref, table_in, *refs):
    sent_refs, (left_ref, lines_ref, table_ref, sems) = refs[: len(SEND)], refs[len(SEND) :]
    [copy] = start_copies(((table_in, table_ref),), sems)
    low = low_half((SPOTS, LANES))
    for q in range(0, BRICK_ROWS // PARTS, 4):
        charge = dot(across_ref[...], brick_ref[:, q * LANES : (q + 4) * LANES])
        for one in range(4):
            there = slice(one * LANES, (one + 1) * LANES)
            here = slice((q + one) * SPOTS, (q + one + 1) * SPOTS)
            points = [charge[ty * SPOTS : (ty + 1) * SPOTS, there] for ty in range(8)]
            for pair, (cosines, sines) in enumerate(class_sums(points)):
                write_left(pair, here, even_odd(cosines, sines, low), left_ref)
    copy.wait()
    for pair in range(PAIRS):
        for one, values in enumerate(line_product(pair, slice(0, PART_ROWS), left_ref, table_ref[pair])):
            most = jnp.max(jnp.abs(values).reshape(PART_ROWS // 8, 8, LANES), axis=0)
            level = level_of(jnp.max(most, axis=0, keepdims=True))
            lines_ref[2 * pair + one, :PART_ROWS, :] = fixed_of(values * inverse_of(level))
            lines_ref[2 * pair + one, PART_ROWS:, :] = head_of(level)
    for offset, sent_ref in zip(SEND, sent_refs):
        sent_ref[...] = lines_ref[own_ref[0] ^ offset]


def grid_rows(slabs, plane, xq, tx):
    start = ((plane * 4 + xq) * SPOTS + tx * 4) * slabs
    return pl.ds(pl.multiple_of(start, 4 * slabs), 4 * slabs)


def plane_product(plane_ref, lines):
    high, rest = split(lines)
    rows = plane_ref.shape[0]
    if plane_ref.shape[1] == 3 * high.shape[0]:
        return dot(plane_ref[...], jnp.concatenate([high, rest, high], axis=0))
    both = dot(plane_ref[...], jnp.concatenate([high, rest], axis=0))
    return both[: rows // 2] + both[rows // 2 :]


def add_sines(got_refs, plane_ref, grid_ref, finish):
    slabs = len(got_refs)
    for at, got_ref in enumerate(got_refs):
        grid_ref[pl.ds(at, PART_ROWS, stride=slabs), :] = wide(got_ref)

    def planes(tx, xq):
        return jnp.concatenate(
            [grid_ref[grid_rows(slabs, plane, xq, tx), :] for plane in range(PART_PLANES)], axis=0
        )

    def sines(tx, _):
        modes = plane_product(plane_ref, jnp.concatenate([planes(tx, xq) for xq in range(4)], axis=1))
        for xq in range(4):
            finish(tx * 4 + xq, modes[:, xq * LANES : (xq + 1) * LANES])
        return 0

    lax.fori_loop(0, 16, sines, 0, unroll=8)


def down_first_kernel(own_ref, *refs):
    count = len(ARRIVAL)
    planes_ref, base_ref, lam_ref, modes_ref, root_ref, gain_ref, power_ref, grid_ref = refs[count:]
    excess = base_ref[...] + lam_ref[pl.ds(own_ref[0], 1), :]
    spread = jnp.sqrt(excess * (excess + 4.0))
    root_ref[...] = 2.0 / (2.0 + excess + spread)
    gain_ref[...] = 1.0 / spread
    for part in range(2):
        here = pl.ds(part * PLANES // 2, PLANES // 2)
        square = root_ref[here, :] * root_ref[here, :]

        def raised(step, power):
            power_ref[step, here, :] = power
            return power * square

        lax.fori_loop(0, STEPS, raised, jnp.ones(square.shape, jnp.float32), unroll=8)

    def finish(line, values):
        modes_ref[line] = values

    add_sines(refs[:count], planes_ref.at[own_ref[0]], grid_ref, finish)


def down_later_kernel(own_ref, *refs):
    count = len(ARRIVAL)
    sums_ref, root_ref, planes_ref, walk_ref, end_ref, grid_ref, modes_ref, last_ref = refs[count:]

    def finish(line, values):
        modes_ref[line] = sums_ref[line] + values

    add_sines(refs[:count], planes_ref.at[own_ref[0]], grid_ref, finish)
    part_rows = 64
    low = low_half((part_rows, LANES))
    for part in range(PLANES // part_rows):
        here = pl.ds(part * part_rows, part_rows)
        root = root_ref[here, :]
        square = root * root

        def walk(step, held):
            ahead, behind = modes_ref[step, here, :], modes_ref[STEPS - 1 - step, here, :]
            own = jnp.where(low, behind, ahead)
            other = pltpu.roll(jnp.where(low, ahead, behind), HALF, 1)
            held = square * held + (own + root * other)
            walk_ref[step, here, :] = held
            return held

        last_ref[here, :] = lax.fori_loop(0, STEPS, walk, jnp.zeros((part_rows, LANES), jnp.float32), unroll=8)
    last = last_ref[...]
    level = level_of(jnp.max(jnp.abs(last), axis=0, keepdims=True))
    end_ref[:PLANES, :] = fixed_of(last * inverse_of(level))
    end_ref[PLANES:, :] = head_of(level)


def local_kernel(walk_ref, root_ref, gain_ref, local_ref):
    part_rows = 64
    low = low_half((part_rows, LANES))
    for part in range(PLANES // part_rows):
        here = pl.ds(part * part_rows, part_rows)
        root, gain = root_ref[here, :], gain_ref[here, :]
        zero = jnp.zeros(root.shape, jnp.float32)

        def line(step, ahead_before, behind_after):
            near = jnp.where(low, walk_ref[STEPS - 1 - step, here, :], walk_ref[step, here, :])
            far = pltpu.roll(jnp.where(low, behind_after, ahead_before), HALF, 1)
            local_ref[step, here, :] = gain * (near + root * far)

        def inner(step, _):
            line(step, walk_ref[step - 1, here, :], walk_ref[STEPS - 2 - step, here, :])
            return 0

        line(0, zero, walk_ref[STEPS - 2, here, :])
        lax.fori_loop(1, STEPS - 1, inner, 0, unroll=6)
        line(STEPS - 1, walk_ref[STEPS - 2, here, :], zero)


def up_kernel(own_ref, local_ref, power_ref, root_ref, gain_ref, *refs):
    end_refs, plane_ref = refs[:GROUPS], refs[GROUPS].at[own_ref[0]]
    count = GROUPS + 1 + len(SEND)
    sent_refs = refs[GROUPS + 1 : count]
    rise_ref, fall_ref, grid_ref, level_ref = refs[count:]
    low = low_half((PLANES, LANES))
    root = root_ref[...]
    square = root * root
    across = square
    for _ in range(6):
        across = across * across
    around = across
    for _ in range(2):
        around = around * around
    ends = [wide(end_ref) for end_ref in end_refs]
    entering = jnp.zeros((PLANES, LANES), jnp.float32)
    for step in range(GROUPS - 1, -1, -1):
        entering = entering * across + jnp.where(low, ends[GROUPS - 1 - step], ends[(step + 1) % GROUPS])
    entering = gain_ref[...] * entering / (1.0 - around)
    straight, turned = square * entering, root * pltpu.roll(entering, HALF, 1)
    rise_ref[...] = jnp.where(low, turned, straight)
    fall_ref[...] = jnp.where(low, straight, turned)
    slabs = len(sent_refs)

    def solved(step):
        reach = rise_ref[...] * power_ref[step] + fall_ref[...] * power_ref[STEPS - 1 - step]
        return local_ref[step] + reach

    def sines(tx, most):
        lines = plane_product(plane_ref, jnp.concatenate([solved(tx * 4 + xq) for xq in range(4)], axis=1))
        for xq in range(4):
            part = lines[:, xq * LANES : (xq + 1) * LANES]
            most = jnp.maximum(most, jnp.max(jnp.abs(part).reshape(4 * BZ, slabs, LANES), axis=0))
            for plane in range(BZ):
                grid_ref[grid_rows(slabs, plane, xq, tx), :] = part[plane * 4 * slabs : (plane + 1) * 4 * slabs]
        return most

    most = lax.fori_loop(0, 16, sines, jnp.zeros((slabs, LANES), jnp.float32), unroll=8)
    level_ref[...] = level_of(most)
    for at, sent_ref in enumerate(sent_refs):
        level = level_ref[at : at + 1, :]
        sent_ref[:ROWS, :] = fixed_of(grid_ref[pl.ds(at, ROWS, stride=slabs), :] * inverse_of(level))
        sent_ref[ROWS:, :] = head_of(level)


def take_lines(own_ref, offsets, got_refs, left_ref, lines_ref):
    own = own_ref[0]
    pairs = list(dict.fromkeys(offset // 2 for offset in offsets))
    for offset, got_ref in zip(offsets, got_refs):
        lines_ref[2 * pairs.index(offset // 2) + ((own ^ offset) & 1)] = wide(got_ref)
    low = low_half((DOT_ROWS, LANES))
    for at in range(len(pairs)):
        for start in range(0, ROWS, DOT_ROWS):
            here = slice(start, start + DOT_ROWS)
            write_left(at, here, even_odd(lines_ref[2 * at, here, :], lines_ref[2 * at + 1, here, :], low), left_ref)
    return [(own >> 1) ^ pair for pair in pairs]


def point_parts(pair, cosines, sines, weight_ref):
    for ty in range(4):
        part = weight_ref[pair, ty] * cosines + weight_ref[pair, 4 + ty] * sines
        yield ty, part
        yield ty + 4, weight_ref[pair, 8] * part


def reply_first_kernel(own_ref, weight_ref, *refs):
    count = len(TAKE_FIRST)
    table_ref, sums_ref, lines_ref, left_ref = refs[count:]
    pairs = take_lines(own_ref, TAKE_FIRST, refs[:count], left_ref, lines_ref)
    for at, pair in enumerate(pairs):
        for part in range(ROWS // DOT_ROWS):
            here = slice(part * DOT_ROWS, (part + 1) * DOT_ROWS)
            cosines, sines = line_product(at, here, left_ref, table_ref[pair])
            for ty, values in point_parts(pair, cosines, sines, weight_ref):
                sums_ref[ty, here, :] = values if at == 0 else sums_ref[ty, here, :] + values


def reply_later_kernel(own_ref, weight_ref, *refs):
    count = len(TAKE_LATER)
    sums_ref, picks_ref, table_ref, out_ref, lines_ref, left_ref, pot_ref = refs[count:]
    [pair] = take_lines(own_ref, TAKE_LATER, refs[:count], left_ref, lines_ref)
    for part in range(ROWS // DOT_ROWS):
        here = slice(part * DOT_ROWS, (part + 1) * DOT_ROWS)
        cosines, sines = line_product(0, here, left_ref, table_ref[pair])
        for ty, values in point_parts(pair, cosines, sines, weight_ref):
            values = (sums_ref[ty, here, :] + values).astype(jnp.bfloat16)
            for one in range(DOT_ROWS // SPOTS):
                q = part * (DOT_ROWS // SPOTS) + one
                pot_ref[ty * SPOTS : (ty + 1) * SPOTS, q * LANES : (q + 1) * LANES] = values[
                    one * SPOTS : (one + 1) * SPOTS
                ]
    for q in range(0, BRICK_ROWS, 4):
        there = slice(q * LANES, (q + 4) * LANES)
        out_ref[:, there] = dot(picks_ref[...], pot_ref[:, there]).astype(jnp.bfloat16)


def unpack_kernel(back_ref, got_ref, out_ref):
    for q in range(0, BRICK_ROWS, 4):
        there = slice(q * LANES, (q + 4) * LANES)
        out_ref[:, there] = dot(back_ref[...], got_ref[:, there]).astype(jnp.bfloat16)


def call(kernel, name, operands, spaces, outs, places, scratch, vmem=VMEM_BYTES):
    return pl.pallas_call(
        kernel,
        out_shape=outs,
        in_specs=[pl.BlockSpec(memory_space=space) for space in spaces],
        out_specs=[pl.BlockSpec(memory_space=space) for space in places],
        scratch_shapes=scratch,
        compiler_params=pltpu.CompilerParams(vmem_limit_bytes=vmem),
        name=name,
    )(*operands)


def on_device_8x4(bricks, owners, tile_ids, counts):
    V, S, H = pltpu.VMEM, pltpu.SMEM, pltpu.HBM
    f32, bf16, i32, i16 = jnp.float32, jnp.bfloat16, jnp.int32, jnp.int16
    shape, dma = jax.ShapeDtypeStruct, pltpu.SemaphoreType.DMA
    brick_rows = bricks.shape[0]
    lines_in, lines_out = (jnp.asarray(each) for each in line_tables())
    weights = jnp.asarray(class_weights())
    lines_in = pltpu.with_memory_space_constraint(lines_in, H)
    planes_in = [jnp.asarray(plane_tables(ARRIVAL, planes, False)) for planes in ((0, 1), (2, 3))]
    planes_out = jnp.asarray(plane_tables(SEND, range(BZ), True))
    base, lam = (jnp.asarray(each) for each in mode_tables())
    own = lax.axis_index("gz").astype(i32).reshape(1)
    sent_shape = shape((ROWS + HEAD_ROWS, LANES), i16)
    end_shape = shape((PLANES + HEAD_ROWS, LANES), i16)
    cube, flat, sums_shape = (STEPS, PLANES, LANES), (PLANES, LANES), (8, ROWS, LANES)
    line, packed = (ROWS, LANES), (SLOTS, PART_CELLS)
    part_shape = shape((PART_ROWS + HEAD_ROWS, LANES), i16)

    def all_ways(values):
        return lax.all_to_all(values, ("gz", "ma"), split_axis=0, concat_axis=0, tiled=True)

    def over_slabs(offset, values):
        return lax.ppermute(values, "gz", [(g, g ^ offset) for g in range(SLABS)]) if offset else values

    def round_groups(values, step):
        return lax.ppermute(values, "ma", [(m, (m + step) % GROUPS) for m in range(GROUPS)]) if step else values

    def exchanged(sent):
        sent = dict(zip(SEND, sent))
        return [over_slabs(offset, sent[offset]) for offset in ARRIVAL]

    outgoing, one_hot, codes = call(
        pack_kernel,
        "pack",
        (owners.reshape(brick_rows), tile_ids, counts, bricks),
        [H] * 4,
        [shape(packed, bf16), shape((SLOTS, brick_rows), bf16), shape((brick_rows,), i32)],
        [H, V, S],
        [
            S((brick_rows,), i32),
            S((brick_rows,), i32),
            S((1,), i32),
            V((brick_rows, PART_CELLS), bf16),
            V((SLOTS + PAIR_SLOTS, brick_rows), f32),
            V(packed, bf16),
            S((DOMAINS,), i32),
            dma((4,)),
            dma((4,)),
        ],
        ALL_VMEM_BYTES,
    )
    outgoing_later, back = call(
        pack_later_kernel,
        "pack_later",
        (bricks, one_hot),
        [H, V],
        [shape(packed, bf16), shape((brick_rows, SLOTS), bf16)],
        [V, V],
        [V((brick_rows, PART_CELLS), bf16), dma((1,))],
    )
    place = lax.axis_index(("gz", "ma")).astype(i32).reshape(1)
    picks, across = call(
        picks_kernel,
        "picks",
        (place, lax.all_gather(codes, ("gz", "ma"))),
        [S, V],
        [shape((SLOTS, TILES), bf16), shape((TILES, SLOTS), bf16)],
        [V, V],
        [V((SLOTS, LANES), f32)],
    )

    def forward(values):
        return call(
            forward_kernel,
            "forward",
            (own, values, across, lines_in),
            [S, V, V, H],
            [part_shape] * len(SEND),
            [V] * len(SEND),
            [
                V((PAIRS, 2 * PART_ROWS, 2 * LANES), bf16),
                V((len(SEND), *part_shape.shape), i16),
                V(lines_in.shape, bf16),
                dma((1,)),
            ],
        )

    first = exchanged(forward(all_ways(outgoing)))
    second, first[1], first[2] = lax.optimization_barrier((all_ways(outgoing_later), first[1], first[2]))
    later = exchanged(forward(second))
    sums, root, gain, power = call(
        down_first_kernel,
        "down_first",
        (own, *first, planes_in[0], base, lam),
        [S] + [V] * (len(first) + 3),
        [shape(cube, f32), shape(flat, f32), shape(flat, f32), shape(cube, f32)],
        [V] * 4,
        [
            V((len(first) * PART_ROWS, LANES), f32),
        ],
    )
    walk, end = call(
        down_later_kernel,
        "down_later",
        (own, *later, sums, root, planes_in[1]),
        [S] + [V] * (len(later) + 3),
        [shape(cube, f32), end_shape],
        [V, V],
        [
            V((len(later) * PART_ROWS, LANES), f32),
            V(cube, f32),
            V(flat, f32),
        ],
    )
    ends = [round_groups(end, step) for step in range(GROUPS)]
    (local,) = call(local_kernel, "local", (walk, root, gain), [V] * 3, [shape(cube, f32)], [V], [])
    sent = call(
        up_kernel,
        "up",
        (own, local, power, root, gain, *ends, planes_out),
        [S] + [V] * (5 + GROUPS),
        [sent_shape] * len(SEND),
        [V] * len(SEND),
        [
            V(flat, f32),
            V(flat, f32),
            V((len(SEND) * ROWS, LANES), f32),
            V((len(SEND), LANES), f32),
        ],
    )
    got = exchanged(sent)
    first, later = got[: len(TAKE_FIRST)], got[len(TAKE_FIRST) :]
    (sums,) = call(
        reply_first_kernel,
        "reply_first",
        (own, weights, *first, lines_out),
        [S, S] + [V] * (len(first) + 1),
        [shape(sums_shape, f32)],
        [V],
        [V((len(first), *line), f32), V((len(first) // 2, 2 * ROWS, 2 * LANES), bf16)],
    )
    (replies,) = call(
        reply_later_kernel,
        "reply_later",
        (own, weights, *later, sums, picks, lines_out),
        [S, S] + [V] * (len(later) + 3),
        [shape((SLOTS, CELLS), bf16)],
        [V],
        [
            V((len(later), *line), f32),
            V((len(later) // 2, 2 * ROWS, 2 * LANES), bf16),
            V((TILES, CELLS), bf16),
        ],
    )
    (result,) = call(
        unpack_kernel,
        "unpack",
        (back, all_ways(replies)),
        [V, V],
        [shape((brick_rows, CELLS), bf16)],
        [V],
        [],
    )
    return result


def solution(mesh):
    in_specs = (P(("gz", "ma"), None), P(("gz", "ma"), None), P(("gz", "ma")), P(("gz", "ma")))
    out_specs = P(("gz", "ma"), None)
    body = on_device_8x4 if (mesh.shape["gz"], mesh.shape["ma"]) == (SLABS, GROUPS) else on_device
    return jax.shard_map(body, mesh=mesh, in_specs=in_specs, out_specs=out_specs, check_vma=False)
```

```python
import math

import jax
import jax.numpy as jnp
import ml_dtypes
import numpy as np
from jax import lax
from jax.experimental import pallas as pl
from jax.experimental.pallas import tpu as pltpu
from jax.sharding import PartitionSpec as P

NX = 512
NY = 512
SCREEN = 16
BZ = 4
BX = 8
BY = 64
CZ = 16


def hartley(length):
    indices = jnp.arange(length, dtype=jnp.int32)
    products = indices[:, None] * indices[None, :] % length
    angles = 2.0 * math.pi / length * products.astype(jnp.float32)
    return (jnp.cos(angles) + jnp.sin(angles)) / math.sqrt(length)


def second_difference(length, indices):
    return 2.0 - 2.0 * jnp.cos(2.0 * math.pi / length * indices.astype(jnp.float32))


def thomas(right_side, diagonal):
    start_zero = jnp.zeros(right_side.shape[1:], jnp.float32)

    def down(state_pair, plane):
        factor = 1.0 / (diagonal - state_pair[0])
        partial_value = (plane + state_pair[1]) * factor
        return ((factor, partial_value), (factor, partial_value))

    _, (factors, partials) = lax.scan(down, (start_zero, start_zero), right_side)

    def upward(beyond, factor_partial):
        solved = factor_partial[1] + factor_partial[0] * beyond
        return (solved, solved)

    _, solutions = lax.scan(upward, start_zero, (factors, partials), reverse=True)
    return solutions


def regroup(values):
    return lax.all_to_all(values, "ma", split_axis=2, concat_axis=1, tiled=True)


def on_device(bricks, owners, tile_ids, counts):
    domains = lax.axis_size(("gz", "ma"))
    group_count = lax.axis_size("ma")
    slab_count = lax.axis_size("gz")
    brick_rows, brick_cells = bricks.shape
    slot_count = max(2, 2 * brick_rows // domains)
    local_x = NX // group_count
    local_y = NY // group_count
    tiles_dev = CZ // BZ * (local_x // BX) * (NY // BY)
    highest = lax.Precision.HIGHEST
    target = owners[:, 0]
    row_order = jnp.arange(brick_rows, dtype=jnp.int32)
    earlier_same = (target[:, None] == target[None, :]) & (row_order[None, :] < row_order[:, None])
    within = jnp.sum(earlier_same.astype(jnp.int32), axis=1)
    slot_of = target * slot_count + within
    is_live = row_order < counts[0]
    loaded = jnp.where(is_live[:, None], bricks, jnp.zeros_like(bricks))
    outgoing = jnp.zeros((domains * slot_count, brick_cells), jnp.bfloat16).at[slot_of].set(loaded)
    out_ids = jnp.full((domains * slot_count,), tiles_dev, jnp.int32).at[slot_of].set(tile_ids)
    incoming, in_ids = (
        lax.all_to_all(outgoing, ("gz", "ma"), split_axis=0, concat_axis=0, tiled=True),
        lax.all_to_all(out_ids, ("gz", "ma"), split_axis=0, concat_axis=0, tiled=True),
    )
    picker = (jnp.arange(tiles_dev, dtype=jnp.int32)[:, None] == in_ids[None, :]).astype(
        jnp.bfloat16
    )
    deposit = jnp.dot(picker, incoming, preferred_element_type=jnp.float32)
    charge = deposit.reshape(CZ // BZ, local_x // BX, NY // BY, BZ, BX, BY)
    charge = charge.transpose(0, 3, 1, 4, 2, 5).reshape(CZ, local_x, NY)
    table_x = hartley(NX)
    table_y = hartley(NY)
    along_y = jnp.einsum("zxy,ky->zxk", charge, table_y, precision=highest)
    gathered_x = regroup(along_y)
    spectrum = jnp.einsum("zxk,jx->zjk", gathered_x, table_x, precision=highest)
    columns = lax.axis_index("ma") * local_y + jnp.arange(local_y, dtype=jnp.int32)
    lam_y = second_difference(NY, columns)
    screening = 1.0 / (SCREEN * SCREEN)
    slab_index = lax.axis_index("gz")
    lam_x = second_difference(NX, jnp.arange(NX, dtype=jnp.int32))
    diagonal = 2.0 + screening + lam_x[:, None] + lam_y[None, :]
    interior = spectrum[1:]
    particular = thomas(interior, diagonal)
    unit_rhs = jnp.zeros_like(interior).at[0].set(1.0)
    spike = thomas(unit_rhs, diagonal)
    near_weight = spike[0]
    far_weight = spike[-1]
    head_term = spectrum[0] + particular[0]
    tail_term = particular[-1]
    reduced_first = diagonal - near_weight
    reduced_rest = diagonal - 2.0 * near_weight
    start_zero = jnp.zeros_like(diagonal)
    heads, tails = (
        lax.all_gather(head_term[None], "gz", axis=0, tiled=True),
        lax.all_gather(tail_term[None], "gz", axis=0, tiled=True),
    )
    before = jnp.concatenate([start_zero[None], tails[:-1]], axis=0)
    sources = heads + before

    def chain_down(state_pair, packed):
        source, position = packed
        base_term = jnp.where(position == 0, reduced_first, reduced_rest)
        pivot_now = 1.0 / (base_term - far_weight * far_weight * state_pair[0])
        forward_part = pivot_now * (source + far_weight * state_pair[1])
        return ((pivot_now, forward_part), (pivot_now, forward_part))

    _, (pivots, forwards) = lax.scan(
        chain_down, (start_zero, start_zero), (sources, jnp.arange(slab_count, dtype=jnp.int32))
    )

    def chain_up(beyond, packed):
        plane_value = packed[1] + far_weight * packed[0] * beyond
        return (plane_value, plane_value)

    _, separators = lax.scan(chain_up, start_zero, (pivots, forwards), reverse=True)
    padded_sep = jnp.concatenate([separators, start_zero[None]], axis=0)
    own_plane = lax.dynamic_index_in_dim(padded_sep, slab_index, 0, keepdims=False)
    next_plane = lax.dynamic_index_in_dim(padded_sep, slab_index + 1, 0, keepdims=False)
    interior_sol = particular + own_plane[None] * spike + next_plane[None] * spike[::-1]
    modal = jnp.concatenate([own_plane[None], interior_sol], axis=0)
    back_x = jnp.einsum("zjk,jx->zkx", modal, table_x, precision=highest)
    gathered_y = regroup(back_x)
    potential = jnp.einsum("zkx,ky->zxy", gathered_y, table_y, precision=highest)
    pot_tiles = potential.reshape(CZ // BZ, BZ, local_x // BX, BX, NY // BY, BY)
    pot_tiles = (
        pot_tiles.transpose(0, 2, 4, 1, 3, 5).reshape(tiles_dev, brick_cells).astype(jnp.bfloat16)
    )
    padded_tiles = jnp.concatenate([pot_tiles, jnp.zeros((1, brick_cells), jnp.bfloat16)], axis=0)
    replies = padded_tiles[in_ids]
    returned = lax.all_to_all(replies, ("gz", "ma"), split_axis=0, concat_axis=0, tiled=True)
    result = returned[slot_of]
    return jnp.where(is_live[:, None], result, jnp.zeros_like(result))


DOMAINS = 32
GROUPS = 4
SLABS = 8
SEND = (4, 2, 5, 3, 0, 1, 6, 7)
ARRIVAL = (0, 4, 2, 5, 3, 1, 6, 7)
PARTS = 2
PART_PLANES = 2
TAKE_FIRST = (0, 4, 2, 5, 3, 1)
TAKE_LATER = (6, 7)
PAIR_SLOTS = 8
SLOTS = DOMAINS * PAIR_SLOTS
TILES = 512
BRICK_ROWS = 16
CELLS = 2048
LANES = 128
HALF = 64
SPOTS = 64
ROWS = BRICK_ROWS * SPOTS
PART_ROWS = ROWS // PARTS
PART_CELLS = CELLS // PARTS
DOT_ROWS = 512
PAIRS = 4
CLASSES = (0, 4, 1, 7, 2, 6, 3, 5)
HEAD_ROWS = 8
STEPS = 64
PLANES = 128
FULL = 32700.0
LOG_UNIT = 128.0
VMEM_BYTES = 24 * 1024 * 1024
ALL_VMEM_BYTES = 60 * 1024 * 1024


def split_table(table):
    high = table.astype(ml_dtypes.bfloat16)
    low = (table - high.astype(np.float64)).astype(ml_dtypes.bfloat16)
    return high, low


def line_tables():
    iy, k2 = np.arange(HALF)[:, None], np.arange(HALF)[None, :]
    tables = []
    for pair in range(PAIRS):
        table = np.zeros((LANES, LANES))
        for one in range(2):
            angle = 2.0 * np.pi / NY * (iy * (CLASSES[2 * pair + one] + 8 * k2) % NY)
            cosine, sine = np.cos(angle) / np.sqrt(NY), np.sin(angle) / np.sqrt(NY)
            there = slice(one * HALF, (one + 1) * HALF)
            if pair == 0:
                table[there, there] = cosine + sine
            else:
                table[:HALF, there] = cosine + sine
                table[HALF:, there] = (cosine - sine) * (1 - 2 * one)
        tables.append(table)

    def stacked(table):
        high, low = split_table(table)
        return np.concatenate(
            [np.concatenate([high, low], axis=1), np.concatenate([high, np.zeros_like(low)], axis=1)], axis=0
        )

    return np.stack([stacked(table) for table in tables]), np.stack([stacked(table.T) for table in tables])


def class_weights():
    pair, ty = np.arange(PAIRS)[:, None], np.arange(4)[None, :]
    cosine, sine = np.cos(np.pi / 4.0 * pair * ty), np.sin(np.pi / 4.0 * pair * ty)
    sine[0] = (-1.0) ** np.arange(4)
    sign = (-1.0) ** pair * np.ones((1, 4))
    return np.concatenate([cosine, sine, sign], axis=1).astype(np.float32)


def plane_tables(offsets, planes, turned):
    index = np.arange(PLANES)
    table = np.sqrt(2.0 / (PLANES + 1)) * np.sin(
        np.pi / (PLANES + 1) * ((index[:, None] + 1) * (index[None, :] + 1) % (2 * PLANES + 2))
    )
    each = []
    for own in range(SLABS):
        slabs = np.array([own ^ offset for offset in offsets])
        plane, tz = np.array(planes)[:, None, None], np.arange(BZ)[None, :, None]
        part = table[:, (slabs * CZ + tz * BZ + plane).reshape(-1)]
        high, low = split_table(part.T if turned else part)
        if 3 * high.shape[1] <= 2 * LANES:
            each.append(np.concatenate([high, high, low], axis=1))
            continue
        top = np.concatenate([high, high], axis=1)
        bottom = np.concatenate([low, np.zeros_like(low)], axis=1)
        each.append(np.concatenate([top, bottom], axis=0))
    return np.stack(each)


def mode_tables():
    mu = 2.0 - 2.0 * np.cos(np.pi / (PLANES + 1) * (np.arange(PLANES) + 1))
    base = np.broadcast_to((mu + 1.0 / (SCREEN * SCREEN))[:, None], (PLANES, LANES))
    lam = 2.0 - 2.0 * np.cos(2.0 * np.pi / NY * np.arange(NY))
    lam = np.stack([lam[number::8] for number in CLASSES])
    return base.astype(np.float32), np.concatenate([lam, lam], axis=1).astype(np.float32)


def low_half(shape):
    return lax.broadcasted_iota(jnp.int32, shape, len(shape) - 1) < HALF


def split(values):
    high = values.astype(jnp.bfloat16)
    return high, (values - high.astype(jnp.float32)).astype(jnp.bfloat16)


def dot(left, right):
    return jnp.dot(left, right, preferred_element_type=jnp.float32)


def start_copies(pairs, sems):
    copies = [pltpu.make_async_copy(source, place, sems.at[at]) for at, (source, place) in enumerate(pairs)]
    for each in copies:
        each.start()
    return copies


def even_odd(first, second, low):
    crossed = pltpu.roll(jnp.where(low, second, first), HALF, 1)
    return jnp.where(low, first, crossed), jnp.where(low, crossed, second)


def write_left(at, here, lines, left_ref):
    rows = left_ref.shape[1] // 2
    for line, values in enumerate(lines):
        high, rest = split(values)
        there = slice(line * rows + here.start, line * rows + here.stop)
        left_ref[at, there, :LANES] = high
        left_ref[at, there, LANES:] = rest


def line_product(at, here, left_ref, table):
    products = []
    rows = left_ref.shape[1] // 2
    for line in range(2):
        there = slice(line * rows + here.start, line * rows + here.stop)
        both = dot(left_ref[at, there, :], table)
        products.append(both[:, :LANES] + both[:, LANES:])
    return even_odd(*products, low_half(products[0].shape))


def class_sums(points):
    half = [points[ty] + points[ty + 4] for ty in range(4)]
    rest = [points[ty] - points[ty + 4] for ty in range(4)]
    even, odd = half[0] + half[2], half[1] + half[3]
    turn = math.sqrt(0.5)
    across, along = turn * (rest[1] - rest[3]), turn * (rest[1] + rest[3])
    return (
        (even + odd, even - odd),
        (rest[0] + across, rest[2] + along),
        (half[0] - half[2], half[1] - half[3]),
        (rest[0] - across, along - rest[2]),
    )


def level_of(most):
    return jnp.floor(jnp.log2(jnp.maximum(most, 1e-30)) * LOG_UNIT) + 2.0


def inverse_of(level):
    return FULL * jnp.exp2(level * (-1.0 / LOG_UNIT))


def fixed_of(values):
    return jnp.floor(values + 0.5).astype(jnp.int32).astype(jnp.int16)


def head_of(level):
    return jnp.broadcast_to(level, (HEAD_ROWS, LANES)).astype(jnp.int32).astype(jnp.int16)


def unit_of(sent_ref):
    head = sent_ref[sent_ref.shape[0] - HEAD_ROWS :, :].astype(jnp.int32).astype(jnp.float32)
    return jnp.exp2(head[0:1] * (1.0 / LOG_UNIT)) * (1.0 / FULL)


def wide(sent_ref):
    block = sent_ref[: sent_ref.shape[0] - HEAD_ROWS, :]
    return block.astype(jnp.int32).astype(jnp.float32) * unit_of(sent_ref)


def turned_up(row):
    return jnp.broadcast_to(row, (row.shape[1], row.shape[1])).T


def pack_kernel(
    owner_in, tile_in, count_in, brick_in, out_ref, one_hot_ref,
    owner_ref, tile_ref, count_ref, brick_ref, ready_ref, sems, out_sems,
):
    cells = brick_in.at[:, pl.ds(0, PART_CELLS)]
    copies = start_copies(((owner_in, owner_ref), (tile_in, tile_ref), (count_in, count_ref), (cells, brick_ref)), sems)
    for each in copies[:3]:
        each.wait()
    owner, tile = owner_ref[...], tile_ref[...]
    brick_rows = owner.shape[1]
    square = (brick_rows, brick_rows)
    position = (tile & 7) * SPOTS + ((tile >> 3) & 15) * 4 + (tile >> 7)
    spot = (position + 1).astype(jnp.float32)
    high = jnp.floor(spot * (1.0 / 32.0))
    heads = jnp.where(low_half(square), turned_up(high), turned_up(spot - 32.0 * high)).astype(jnp.bfloat16)
    named = owner.astype(jnp.float32)
    earlier = lax.broadcasted_iota(jnp.int32, square, 0) < lax.broadcasted_iota(jnp.int32, square, 1)
    same = jnp.where((turned_up(named) == named) & earlier, 1.0, 0.0)
    within = jnp.sum(same, axis=0, keepdims=True).astype(jnp.int32)
    live = lax.broadcasted_iota(jnp.int32, owner.shape, 1) < count_ref[0]
    slot = jnp.where(live, owner * PAIR_SLOTS + within, SLOTS)
    copies[3].wait()
    copies = []
    rows = 64
    for part in range(SLOTS // rows):
        here = slice(part * rows, (part + 1) * rows)
        index = lax.broadcasted_iota(jnp.int32, (rows, brick_rows), 0) + part * rows
        picks = jnp.where(index == slot, 1.0, 0.0).astype(jnp.bfloat16)
        one_hot_ref[here, :] = picks
        ready_ref[here, :PART_CELLS] = dot(picks, brick_ref[...]).astype(jnp.bfloat16)
        ready_ref[here, PART_CELLS:] = dot(picks, heads).astype(jnp.bfloat16)
        some = pl.ds(part * rows, rows)
        copies.append(pltpu.make_async_copy(ready_ref.at[some], out_ref.at[some], out_sems.at[part]))
        copies[-1].start()
    for each in copies:
        each.wait()


def pack_later_kernel(brick_in, one_hot_ref, out_ref, back_ref, brick_ref, sems):
    [copy] = start_copies(((brick_in.at[:, pl.ds(PART_CELLS, PART_CELLS)], brick_ref),), sems)
    for part in range(SLOTS // LANES):
        here = slice(part * LANES, (part + 1) * LANES)
        back_ref[:, here] = one_hot_ref[here, :].astype(jnp.float32).T.astype(jnp.bfloat16)
    copy.wait()
    out_ref[...] = dot(one_hot_ref[...], brick_ref[...]).astype(jnp.bfloat16)


def write_picks(brick_ref, picks_ref, across_ref):
    for part in range(SLOTS // LANES):
        here = slice(part * LANES, (part + 1) * LANES)
        head = brick_ref[here, PART_CELLS:].astype(jnp.float32)
        turned = pltpu.roll(head, HALF, 1)
        low = low_half(head.shape)
        places = (jnp.where(low, head, turned) * 32.0 + jnp.where(low, turned, head)).astype(jnp.int32) - 1
        for block in range(TILES // LANES):
            there = slice(block * LANES, (block + 1) * LANES)
            lane = lax.broadcasted_iota(jnp.int32, (LANES, LANES), 1) + block * LANES
            square = jnp.where(places == lane, 1.0, 0.0)
            picks_ref[here, there] = square.astype(jnp.bfloat16)
            across_ref[there, here] = square.T.astype(jnp.bfloat16)


def forward_lines(own_ref, brick_ref, across_ref, table_in, sent_refs, left_ref, lines_ref, table_ref, sems):
    [copy] = start_copies(((table_in, table_ref),), sems)
    low = low_half((SPOTS, LANES))
    for q in range(0, BRICK_ROWS // PARTS, 4):
        charge = dot(across_ref[...], brick_ref[:, q * LANES : (q + 4) * LANES])
        for one in range(4):
            there = slice(one * LANES, (one + 1) * LANES)
            here = slice((q + one) * SPOTS, (q + one + 1) * SPOTS)
            points = [charge[ty * SPOTS : (ty + 1) * SPOTS, there] for ty in range(8)]
            for pair, (cosines, sines) in enumerate(class_sums(points)):
                write_left(pair, here, even_odd(cosines, sines, low), left_ref)
    copy.wait()
    for pair in range(PAIRS):
        for one, values in enumerate(line_product(pair, slice(0, PART_ROWS), left_ref, table_ref[pair])):
            most = jnp.max(jnp.abs(values).reshape(PART_ROWS // 8, 8, LANES), axis=0)
            level = level_of(jnp.max(most, axis=0, keepdims=True))
            lines_ref[2 * pair + one, :PART_ROWS, :] = fixed_of(values * inverse_of(level))
            lines_ref[2 * pair + one, PART_ROWS:, :] = head_of(level)
    for offset, sent_ref in zip(SEND, sent_refs):
        sent_ref[...] = lines_ref[own_ref[0] ^ offset]


def forward_first_kernel(own_ref, brick_ref, table_in, *refs):
    sent_refs, (picks_ref, across_ref) = refs[: len(SEND)], refs[len(SEND) : len(SEND) + 2]
    write_picks(brick_ref, picks_ref, across_ref)
    forward_lines(own_ref, brick_ref, across_ref, table_in, sent_refs, *refs[len(SEND) + 2 :])


def forward_later_kernel(own_ref, brick_ref, across_ref, table_in, *refs):
    forward_lines(own_ref, brick_ref, across_ref, table_in, refs[: len(SEND)], *refs[len(SEND) :])


def grid_rows(slabs, plane, xq, tx):
    start = ((plane * 4 + xq) * SPOTS + tx * 4) * slabs
    return pl.ds(pl.multiple_of(start, 4 * slabs), 4 * slabs)


def plane_product(plane_ref, lines):
    high, rest = split(lines)
    rows = plane_ref.shape[0]
    if plane_ref.shape[1] == 3 * high.shape[0]:
        return dot(plane_ref[...], jnp.concatenate([high, rest, high], axis=0))
    both = dot(plane_ref[...], jnp.concatenate([high, rest], axis=0))
    return both[: rows // 2] + both[rows // 2 :]


def add_sines(got_refs, plane_ref, grid_ref, finish):
    slabs = len(got_refs)
    for at, got_ref in enumerate(got_refs):
        grid_ref[pl.ds(at, PART_ROWS, stride=slabs), :] = wide(got_ref)

    def planes(tx, xq):
        return jnp.concatenate(
            [grid_ref[grid_rows(slabs, plane, xq, tx), :] for plane in range(PART_PLANES)], axis=0
        )

    def sines(tx, _):
        modes = plane_product(plane_ref, jnp.concatenate([planes(tx, xq) for xq in range(4)], axis=1))
        for xq in range(4):
            finish(tx * 4 + xq, modes[:, xq * LANES : (xq + 1) * LANES])
        return 0

    lax.fori_loop(0, 16, sines, 0, unroll=8)


def down_first_kernel(own_ref, *refs):
    count = len(ARRIVAL)
    planes_ref, base_ref, lam_ref, modes_ref, root_ref, gain_ref, power_ref, grid_ref = refs[count:]
    excess = base_ref[...] + lam_ref[pl.ds(own_ref[0], 1), :]
    spread = jnp.sqrt(excess * (excess + 4.0))
    root_ref[...] = 2.0 / (2.0 + excess + spread)
    gain_ref[...] = 1.0 / spread
    for part in range(2):
        here = pl.ds(part * PLANES // 2, PLANES // 2)
        square = root_ref[here, :] * root_ref[here, :]

        def raised(step, power):
            power_ref[step, here, :] = power
            return power * square

        lax.fori_loop(0, STEPS, raised, jnp.ones(square.shape, jnp.float32), unroll=8)

    def finish(line, values):
        modes_ref[line] = values

    add_sines(refs[:count], planes_ref.at[own_ref[0]], grid_ref, finish)


def down_later_kernel(own_ref, *refs):
    count = len(ARRIVAL)
    sums_ref, root_ref, planes_ref, walk_ref, end_ref, grid_ref, modes_ref, last_ref = refs[count:]

    def finish(line, values):
        modes_ref[line] = sums_ref[line] + values

    add_sines(refs[:count], planes_ref.at[own_ref[0]], grid_ref, finish)
    part_rows = 64
    low = low_half((part_rows, LANES))
    for part in range(PLANES // part_rows):
        here = pl.ds(part * part_rows, part_rows)
        root = root_ref[here, :]
        square = root * root

        def walk(step, held):
            ahead, behind = modes_ref[step, here, :], modes_ref[STEPS - 1 - step, here, :]
            own = jnp.where(low, behind, ahead)
            other = pltpu.roll(jnp.where(low, ahead, behind), HALF, 1)
            held = square * held + (own + root * other)
            walk_ref[step, here, :] = held
            return held

        last_ref[here, :] = lax.fori_loop(0, STEPS, walk, jnp.zeros((part_rows, LANES), jnp.float32), unroll=8)
    last = last_ref[...]
    level = level_of(jnp.max(jnp.abs(last), axis=0, keepdims=True))
    end_ref[:PLANES, :] = fixed_of(last * inverse_of(level))
    end_ref[PLANES:, :] = head_of(level)


def local_kernel(walk_ref, root_ref, gain_ref, local_ref):
    part_rows = 64
    low = low_half((part_rows, LANES))
    for part in range(PLANES // part_rows):
        here = pl.ds(part * part_rows, part_rows)
        root, gain = root_ref[here, :], gain_ref[here, :]
        zero = jnp.zeros(root.shape, jnp.float32)

        def line(step, ahead_before, behind_after):
            near = jnp.where(low, walk_ref[STEPS - 1 - step, here, :], walk_ref[step, here, :])
            far = pltpu.roll(jnp.where(low, behind_after, ahead_before), HALF, 1)
            local_ref[step, here, :] = gain * (near + root * far)

        def inner(step, _):
            line(step, walk_ref[step - 1, here, :], walk_ref[STEPS - 2 - step, here, :])
            return 0

        line(0, zero, walk_ref[STEPS - 2, here, :])
        lax.fori_loop(1, STEPS - 1, inner, 0, unroll=6)
        line(STEPS - 1, walk_ref[STEPS - 2, here, :], zero)


def up_kernel(own_ref, local_ref, power_ref, root_ref, gain_ref, *refs):
    end_refs, plane_ref = refs[:GROUPS], refs[GROUPS].at[own_ref[0]]
    count = GROUPS + 1 + len(SEND)
    sent_refs = refs[GROUPS + 1 : count]
    rise_ref, fall_ref, grid_ref, level_ref = refs[count:]
    low = low_half((PLANES, LANES))
    root = root_ref[...]
    square = root * root
    across = square
    for _ in range(6):
        across = across * across
    around = across
    for _ in range(2):
        around = around * around
    ends = [wide(end_ref) for end_ref in end_refs]
    entering = jnp.zeros((PLANES, LANES), jnp.float32)
    for step in range(GROUPS - 1, -1, -1):
        entering = entering * across + jnp.where(low, ends[GROUPS - 1 - step], ends[(step + 1) % GROUPS])
    entering = gain_ref[...] * entering / (1.0 - around)
    straight, turned = square * entering, root * pltpu.roll(entering, HALF, 1)
    rise_ref[...] = jnp.where(low, turned, straight)
    fall_ref[...] = jnp.where(low, straight, turned)
    slabs = len(sent_refs)

    def solved(step):
        reach = rise_ref[...] * power_ref[step] + fall_ref[...] * power_ref[STEPS - 1 - step]
        return local_ref[step] + reach

    def sines(tx, most):
        lines = plane_product(plane_ref, jnp.concatenate([solved(tx * 4 + xq) for xq in range(4)], axis=1))
        for xq in range(4):
            part = lines[:, xq * LANES : (xq + 1) * LANES]
            most = jnp.maximum(most, jnp.max(jnp.abs(part).reshape(4 * BZ, slabs, LANES), axis=0))
            for plane in range(BZ):
                grid_ref[grid_rows(slabs, plane, xq, tx), :] = part[plane * 4 * slabs : (plane + 1) * 4 * slabs]
        return most

    most = lax.fori_loop(0, 16, sines, jnp.zeros((slabs, LANES), jnp.float32), unroll=8)
    level_ref[...] = level_of(most)
    for at, sent_ref in enumerate(sent_refs):
        level = level_ref[at : at + 1, :]
        sent_ref[:ROWS, :] = fixed_of(grid_ref[pl.ds(at, ROWS, stride=slabs), :] * inverse_of(level))
        sent_ref[ROWS:, :] = head_of(level)


def take_lines(own_ref, offsets, got_refs, left_ref, lines_ref):
    own = own_ref[0]
    pairs = list(dict.fromkeys(offset // 2 for offset in offsets))
    for offset, got_ref in zip(offsets, got_refs):
        lines_ref[2 * pairs.index(offset // 2) + ((own ^ offset) & 1)] = wide(got_ref)
    low = low_half((DOT_ROWS, LANES))
    for at in range(len(pairs)):
        for start in range(0, ROWS, DOT_ROWS):
            here = slice(start, start + DOT_ROWS)
            write_left(at, here, even_odd(lines_ref[2 * at, here, :], lines_ref[2 * at + 1, here, :], low), left_ref)
    return [(own >> 1) ^ pair for pair in pairs]


def point_parts(pair, cosines, sines, weight_ref):
    for ty in range(4):
        part = weight_ref[pair, ty] * cosines + weight_ref[pair, 4 + ty] * sines
        yield ty, part
        yield ty + 4, weight_ref[pair, 8] * part


def reply_first_kernel(own_ref, weight_ref, *refs):
    count = len(TAKE_FIRST)
    table_ref, sums_ref, lines_ref, left_ref = refs[count:]
    pairs = take_lines(own_ref, TAKE_FIRST, refs[:count], left_ref, lines_ref)
    for at, pair in enumerate(pairs):
        for part in range(ROWS // DOT_ROWS):
            here = slice(part * DOT_ROWS, (part + 1) * DOT_ROWS)
            cosines, sines = line_product(at, here, left_ref, table_ref[pair])
            for ty, values in point_parts(pair, cosines, sines, weight_ref):
                sums_ref[ty, here, :] = values if at == 0 else sums_ref[ty, here, :] + values


def reply_later_kernel(own_ref, weight_ref, *refs):
    count = len(TAKE_LATER)
    sums_ref, picks_ref, table_ref, out_ref, lines_ref, left_ref, pot_ref = refs[count:]
    [pair] = take_lines(own_ref, TAKE_LATER, refs[:count], left_ref, lines_ref)
    for part in range(ROWS // DOT_ROWS):
        here = slice(part * DOT_ROWS, (part + 1) * DOT_ROWS)
        cosines, sines = line_product(0, here, left_ref, table_ref[pair])
        for ty, values in point_parts(pair, cosines, sines, weight_ref):
            values = (sums_ref[ty, here, :] + values).astype(jnp.bfloat16)
            for one in range(DOT_ROWS // SPOTS):
                q = part * (DOT_ROWS // SPOTS) + one
                pot_ref[ty * SPOTS : (ty + 1) * SPOTS, q * LANES : (q + 1) * LANES] = values[
                    one * SPOTS : (one + 1) * SPOTS
                ]
    for q in range(0, BRICK_ROWS, 4):
        there = slice(q * LANES, (q + 4) * LANES)
        out_ref[:, there] = dot(picks_ref[...], pot_ref[:, there]).astype(jnp.bfloat16)


def unpack_kernel(back_ref, got_ref, out_ref):
    for q in range(0, BRICK_ROWS, 4):
        there = slice(q * LANES, (q + 4) * LANES)
        out_ref[:, there] = dot(back_ref[...], got_ref[:, there]).astype(jnp.bfloat16)


def call(kernel, name, operands, spaces, outs, places, scratch, vmem=VMEM_BYTES):
    return pl.pallas_call(
        kernel,
        out_shape=outs,
        in_specs=[pl.BlockSpec(memory_space=space) for space in spaces],
        out_specs=[pl.BlockSpec(memory_space=space) for space in places],
        scratch_shapes=scratch,
        compiler_params=pltpu.CompilerParams(vmem_limit_bytes=vmem),
        name=name,
    )(*operands)


def on_device_8x4(bricks, owners, tile_ids, counts):
    V, S, H = pltpu.VMEM, pltpu.SMEM, pltpu.HBM
    f32, bf16, i32, i16 = jnp.float32, jnp.bfloat16, jnp.int32, jnp.int16
    shape, dma = jax.ShapeDtypeStruct, pltpu.SemaphoreType.DMA
    brick_rows = bricks.shape[0]
    lines_in, lines_out = (jnp.asarray(each) for each in line_tables())
    weights = jnp.asarray(class_weights())
    lines_in = pltpu.with_memory_space_constraint(lines_in, H)
    planes_in = [jnp.asarray(plane_tables(ARRIVAL, planes, False)) for planes in ((0, 1), (2, 3))]
    planes_out = jnp.asarray(plane_tables(SEND, range(BZ), True))
    base, lam = (jnp.asarray(each) for each in mode_tables())
    own = lax.axis_index("gz").astype(i32).reshape(1)
    sent_shape = shape((ROWS + HEAD_ROWS, LANES), i16)
    end_shape = shape((PLANES + HEAD_ROWS, LANES), i16)
    cube, flat, sums_shape = (STEPS, PLANES, LANES), (PLANES, LANES), (8, ROWS, LANES)
    line, packed = (ROWS, LANES), [(SLOTS, PART_CELLS + LANES), (SLOTS, PART_CELLS)]
    part_shape = shape((PART_ROWS + HEAD_ROWS, LANES), i16)

    def all_ways(values):
        return lax.all_to_all(values, ("gz", "ma"), split_axis=0, concat_axis=0, tiled=True)

    def over_slabs(offset, values):
        return lax.ppermute(values, "gz", [(g, g ^ offset) for g in range(SLABS)]) if offset else values

    def round_groups(values, step):
        return lax.ppermute(values, "ma", [(m, (m + step) % GROUPS) for m in range(GROUPS)]) if step else values

    def exchanged(sent):
        sent = dict(zip(SEND, sent))
        return [over_slabs(offset, sent[offset]) for offset in ARRIVAL]

    outgoing, one_hot = call(
        pack_kernel,
        "pack",
        (owners.reshape(1, brick_rows), tile_ids.reshape(1, brick_rows), counts, bricks),
        [H] * 4,
        [shape(packed[0], bf16), shape((SLOTS, brick_rows), bf16)],
        [H, V],
        [
            V((1, brick_rows), i32),
            V((1, brick_rows), i32),
            S((1,), i32),
            V((brick_rows, PART_CELLS), bf16),
            V(packed[0], bf16),
            dma((4,)),
            dma((4,)),
        ],
        ALL_VMEM_BYTES,
    )
    outgoing_later, back = call(
        pack_later_kernel,
        "pack_later",
        (bricks, one_hot),
        [H, V],
        [shape(packed[1], bf16), shape((brick_rows, SLOTS), bf16)],
        [V, V],
        [V((brick_rows, PART_CELLS), bf16), dma((1,))],
    )
    incoming = [all_ways(outgoing), all_ways(outgoing_later)]
    forward_scratch = [
        V((PAIRS, 2 * PART_ROWS, 2 * LANES), bf16),
        V((len(SEND), *part_shape.shape), i16),
        V(lines_in.shape, bf16),
        dma((1,)),
    ]
    *sent, picks, across = call(
        forward_first_kernel,
        "forward_first",
        (own, incoming[0], lines_in),
        [S, V, H],
        [part_shape] * len(SEND) + [shape((SLOTS, TILES), bf16), shape((TILES, SLOTS), bf16)],
        [V] * (len(SEND) + 2),
        forward_scratch,
    )
    first = exchanged(sent)
    second, first[1], first[2] = lax.optimization_barrier((incoming[1], first[1], first[2]))
    sent = call(
        forward_later_kernel,
        "forward_later",
        (own, second, across, lines_in),
        [S, V, V, H],
        [part_shape] * len(SEND),
        [V] * len(SEND),
        forward_scratch,
    )
    later = exchanged(sent)
    sums, root, gain, power = call(
        down_first_kernel,
        "down_first",
        (own, *first, planes_in[0], base, lam),
        [S] + [V] * (len(first) + 3),
        [shape(cube, f32), shape(flat, f32), shape(flat, f32), shape(cube, f32)],
        [V] * 4,
        [
            V((len(first) * PART_ROWS, LANES), f32),
        ],
    )
    walk, end = call(
        down_later_kernel,
        "down_later",
        (own, *later, sums, root, planes_in[1]),
        [S] + [V] * (len(later) + 3),
        [shape(cube, f32), end_shape],
        [V, V],
        [
            V((len(later) * PART_ROWS, LANES), f32),
            V(cube, f32),
            V(flat, f32),
        ],
    )
    ends = [round_groups(end, step) for step in range(GROUPS)]
    (local,) = call(local_kernel, "local", (walk, root, gain), [V] * 3, [shape(cube, f32)], [V], [])
    sent = call(
        up_kernel,
        "up",
        (own, local, power, root, gain, *ends, planes_out),
        [S] + [V] * (5 + GROUPS),
        [sent_shape] * len(SEND),
        [V] * len(SEND),
        [
            V(flat, f32),
            V(flat, f32),
            V((len(SEND) * ROWS, LANES), f32),
            V((len(SEND), LANES), f32),
        ],
    )
    got = exchanged(sent)
    first, later = got[: len(TAKE_FIRST)], got[len(TAKE_FIRST) :]
    (sums,) = call(
        reply_first_kernel,
        "reply_first",
        (own, weights, *first, lines_out),
        [S, S] + [V] * (len(first) + 1),
        [shape(sums_shape, f32)],
        [V],
        [V((len(first), *line), f32), V((len(first) // 2, 2 * ROWS, 2 * LANES), bf16)],
    )
    (replies,) = call(
        reply_later_kernel,
        "reply_later",
        (own, weights, *later, sums, picks, lines_out),
        [S, S] + [V] * (len(later) + 3),
        [shape((SLOTS, CELLS), bf16)],
        [V],
        [
            V((len(later), *line), f32),
            V((len(later) // 2, 2 * ROWS, 2 * LANES), bf16),
            V((TILES, CELLS), bf16),
        ],
    )
    (result,) = call(
        unpack_kernel,
        "unpack",
        (back, all_ways(replies)),
        [V, V],
        [shape((brick_rows, CELLS), bf16)],
        [V],
        [],
    )
    return result


def solution(mesh):
    in_specs = (P(("gz", "ma"), None), P(("gz", "ma"), None), P(("gz", "ma")), P(("gz", "ma")))
    out_specs = P(("gz", "ma"), None)
    body = on_device_8x4 if (mesh.shape["gz"], mesh.shape["ma"]) == (SLABS, GROUPS) else on_device
    return jax.shard_map(body, mesh=mesh, in_specs=in_specs, out_specs=out_specs, check_vma=False)
```

```python
import math

import jax
import jax.numpy as jnp
import ml_dtypes
import numpy as np
from jax import lax
from jax.experimental import pallas as pl
from jax.experimental.pallas import tpu as pltpu
from jax.sharding import PartitionSpec as P

NX = 512
NY = 512
SCREEN = 16
BZ = 4
BX = 8
BY = 64
CZ = 16


def hartley(length):
    indices = jnp.arange(length, dtype=jnp.int32)
    products = indices[:, None] * indices[None, :] % length
    angles = 2.0 * math.pi / length * products.astype(jnp.float32)
    return (jnp.cos(angles) + jnp.sin(angles)) / math.sqrt(length)


def second_difference(length, indices):
    return 2.0 - 2.0 * jnp.cos(2.0 * math.pi / length * indices.astype(jnp.float32))


def thomas(right_side, diagonal):
    start_zero = jnp.zeros(right_side.shape[1:], jnp.float32)

    def down(state_pair, plane):
        factor = 1.0 / (diagonal - state_pair[0])
        partial_value = (plane + state_pair[1]) * factor
        return ((factor, partial_value), (factor, partial_value))

    _, (factors, partials) = lax.scan(down, (start_zero, start_zero), right_side)

    def upward(beyond, factor_partial):
        solved = factor_partial[1] + factor_partial[0] * beyond
        return (solved, solved)

    _, solutions = lax.scan(upward, start_zero, (factors, partials), reverse=True)
    return solutions


def regroup(values):
    return lax.all_to_all(values, "ma", split_axis=2, concat_axis=1, tiled=True)


def on_device(bricks, owners, tile_ids, counts):
    domains = lax.axis_size(("gz", "ma"))
    group_count = lax.axis_size("ma")
    slab_count = lax.axis_size("gz")
    brick_rows, brick_cells = bricks.shape
    slot_count = max(2, 2 * brick_rows // domains)
    local_x = NX // group_count
    local_y = NY // group_count
    tiles_dev = CZ // BZ * (local_x // BX) * (NY // BY)
    highest = lax.Precision.HIGHEST
    target = owners[:, 0]
    row_order = jnp.arange(brick_rows, dtype=jnp.int32)
    earlier_same = (target[:, None] == target[None, :]) & (row_order[None, :] < row_order[:, None])
    within = jnp.sum(earlier_same.astype(jnp.int32), axis=1)
    slot_of = target * slot_count + within
    is_live = row_order < counts[0]
    loaded = jnp.where(is_live[:, None], bricks, jnp.zeros_like(bricks))
    outgoing = jnp.zeros((domains * slot_count, brick_cells), jnp.bfloat16).at[slot_of].set(loaded)
    out_ids = jnp.full((domains * slot_count,), tiles_dev, jnp.int32).at[slot_of].set(tile_ids)
    incoming, in_ids = (
        lax.all_to_all(outgoing, ("gz", "ma"), split_axis=0, concat_axis=0, tiled=True),
        lax.all_to_all(out_ids, ("gz", "ma"), split_axis=0, concat_axis=0, tiled=True),
    )
    picker = (jnp.arange(tiles_dev, dtype=jnp.int32)[:, None] == in_ids[None, :]).astype(
        jnp.bfloat16
    )
    deposit = jnp.dot(picker, incoming, preferred_element_type=jnp.float32)
    charge = deposit.reshape(CZ // BZ, local_x // BX, NY // BY, BZ, BX, BY)
    charge = charge.transpose(0, 3, 1, 4, 2, 5).reshape(CZ, local_x, NY)
    table_x = hartley(NX)
    table_y = hartley(NY)
    along_y = jnp.einsum("zxy,ky->zxk", charge, table_y, precision=highest)
    gathered_x = regroup(along_y)
    spectrum = jnp.einsum("zxk,jx->zjk", gathered_x, table_x, precision=highest)
    columns = lax.axis_index("ma") * local_y + jnp.arange(local_y, dtype=jnp.int32)
    lam_y = second_difference(NY, columns)
    screening = 1.0 / (SCREEN * SCREEN)
    slab_index = lax.axis_index("gz")
    lam_x = second_difference(NX, jnp.arange(NX, dtype=jnp.int32))
    diagonal = 2.0 + screening + lam_x[:, None] + lam_y[None, :]
    interior = spectrum[1:]
    particular = thomas(interior, diagonal)
    unit_rhs = jnp.zeros_like(interior).at[0].set(1.0)
    spike = thomas(unit_rhs, diagonal)
    near_weight = spike[0]
    far_weight = spike[-1]
    head_term = spectrum[0] + particular[0]
    tail_term = particular[-1]
    reduced_first = diagonal - near_weight
    reduced_rest = diagonal - 2.0 * near_weight
    start_zero = jnp.zeros_like(diagonal)
    heads, tails = (
        lax.all_gather(head_term[None], "gz", axis=0, tiled=True),
        lax.all_gather(tail_term[None], "gz", axis=0, tiled=True),
    )
    before = jnp.concatenate([start_zero[None], tails[:-1]], axis=0)
    sources = heads + before

    def chain_down(state_pair, packed):
        source, position = packed
        base_term = jnp.where(position == 0, reduced_first, reduced_rest)
        pivot_now = 1.0 / (base_term - far_weight * far_weight * state_pair[0])
        forward_part = pivot_now * (source + far_weight * state_pair[1])
        return ((pivot_now, forward_part), (pivot_now, forward_part))

    _, (pivots, forwards) = lax.scan(
        chain_down, (start_zero, start_zero), (sources, jnp.arange(slab_count, dtype=jnp.int32))
    )

    def chain_up(beyond, packed):
        plane_value = packed[1] + far_weight * packed[0] * beyond
        return (plane_value, plane_value)

    _, separators = lax.scan(chain_up, start_zero, (pivots, forwards), reverse=True)
    padded_sep = jnp.concatenate([separators, start_zero[None]], axis=0)
    own_plane = lax.dynamic_index_in_dim(padded_sep, slab_index, 0, keepdims=False)
    next_plane = lax.dynamic_index_in_dim(padded_sep, slab_index + 1, 0, keepdims=False)
    interior_sol = particular + own_plane[None] * spike + next_plane[None] * spike[::-1]
    modal = jnp.concatenate([own_plane[None], interior_sol], axis=0)
    back_x = jnp.einsum("zjk,jx->zkx", modal, table_x, precision=highest)
    gathered_y = regroup(back_x)
    potential = jnp.einsum("zkx,ky->zxy", gathered_y, table_y, precision=highest)
    pot_tiles = potential.reshape(CZ // BZ, BZ, local_x // BX, BX, NY // BY, BY)
    pot_tiles = (
        pot_tiles.transpose(0, 2, 4, 1, 3, 5).reshape(tiles_dev, brick_cells).astype(jnp.bfloat16)
    )
    padded_tiles = jnp.concatenate([pot_tiles, jnp.zeros((1, brick_cells), jnp.bfloat16)], axis=0)
    replies = padded_tiles[in_ids]
    returned = lax.all_to_all(replies, ("gz", "ma"), split_axis=0, concat_axis=0, tiled=True)
    result = returned[slot_of]
    return jnp.where(is_live[:, None], result, jnp.zeros_like(result))


DOMAINS = 32
GROUPS = 4
SLABS = 8
SEND = (4, 2, 5, 3, 0, 1, 6, 7)
ARRIVAL = (0, 4, 2, 5, 3, 1, 6, 7)
PARTS = 2
PART_PLANES = 2
TAKE_FIRST = (0, 4, 2, 5, 3, 1)
TAKE_LATER = (6, 7)
PAIR_SLOTS = 8
SLOTS = DOMAINS * PAIR_SLOTS
TILES = 512
BRICK_ROWS = 16
CELLS = 2048
LANES = 128
HALF = 64
SPOTS = 64
ROWS = BRICK_ROWS * SPOTS
PART_ROWS = ROWS // PARTS
PART_CELLS = CELLS // PARTS
DOT_ROWS = 512
PAIRS = 4
CLASSES = (0, 4, 1, 7, 2, 6, 3, 5)
HEAD_ROWS = 8
STEPS = 64
PLANES = 128
FULL = 32700.0
LOG_UNIT = 128.0
VMEM_BYTES = 24 * 1024 * 1024
ALL_VMEM_BYTES = 60 * 1024 * 1024


def split_table(table):
    high = table.astype(ml_dtypes.bfloat16)
    low = (table - high.astype(np.float64)).astype(ml_dtypes.bfloat16)
    return high, low


def line_tables():
    iy, k2 = np.arange(HALF)[:, None], np.arange(HALF)[None, :]
    tables = []
    for pair in range(PAIRS):
        table = np.zeros((LANES, LANES))
        for one in range(2):
            angle = 2.0 * np.pi / NY * (iy * (CLASSES[2 * pair + one] + 8 * k2) % NY)
            cosine, sine = np.cos(angle) / np.sqrt(NY), np.sin(angle) / np.sqrt(NY)
            there = slice(one * HALF, (one + 1) * HALF)
            if pair == 0:
                table[there, there] = cosine + sine
            else:
                table[:HALF, there] = cosine + sine
                table[HALF:, there] = (cosine - sine) * (1 - 2 * one)
        tables.append(table)

    def stacked(table):
        high, low = split_table(table)
        return np.concatenate(
            [np.concatenate([high, low], axis=1), np.concatenate([high, np.zeros_like(low)], axis=1)], axis=0
        )

    return np.stack([stacked(table) for table in tables]), np.stack([stacked(table.T) for table in tables])


def class_weights():
    pair, ty = np.arange(PAIRS)[:, None], np.arange(4)[None, :]
    cosine, sine = np.cos(np.pi / 4.0 * pair * ty), np.sin(np.pi / 4.0 * pair * ty)
    sine[0] = (-1.0) ** np.arange(4)
    sign = (-1.0) ** pair * np.ones((1, 4))
    return np.concatenate([cosine, sine, sign], axis=1).astype(np.float32)


def plane_tables(offsets, planes, turned):
    index = np.arange(PLANES)
    table = np.sqrt(2.0 / (PLANES + 1)) * np.sin(
        np.pi / (PLANES + 1) * ((index[:, None] + 1) * (index[None, :] + 1) % (2 * PLANES + 2))
    )
    each = []
    for own in range(SLABS):
        slabs = np.array([own ^ offset for offset in offsets])
        plane, tz = np.array(planes)[:, None, None], np.arange(BZ)[None, :, None]
        part = table[:, (slabs * CZ + tz * BZ + plane).reshape(-1)]
        high, low = split_table(part.T if turned else part)
        if 3 * high.shape[1] <= 2 * LANES:
            each.append(np.concatenate([high, high, low], axis=1))
            continue
        top = np.concatenate([high, high], axis=1)
        bottom = np.concatenate([low, np.zeros_like(low)], axis=1)
        each.append(np.concatenate([top, bottom], axis=0))
    return np.stack(each)


def mode_tables():
    mu = 2.0 - 2.0 * np.cos(np.pi / (PLANES + 1) * (np.arange(PLANES) + 1))
    base = np.broadcast_to((mu + 1.0 / (SCREEN * SCREEN))[:, None], (PLANES, LANES))
    lam = 2.0 - 2.0 * np.cos(2.0 * np.pi / NY * np.arange(NY))
    lam = np.stack([lam[number::8] for number in CLASSES])
    return base.astype(np.float32), np.concatenate([lam, lam], axis=1).astype(np.float32)


def low_half(shape):
    return lax.broadcasted_iota(jnp.int32, shape, len(shape) - 1) < HALF


def split(values):
    high = values.astype(jnp.bfloat16)
    return high, (values - high.astype(jnp.float32)).astype(jnp.bfloat16)


def dot(left, right):
    return jnp.dot(left, right, preferred_element_type=jnp.float32)


def start_copies(pairs, sems):
    copies = [pltpu.make_async_copy(source, place, sems.at[at]) for at, (source, place) in enumerate(pairs)]
    for each in copies:
        each.start()
    return copies


def even_odd(first, second, low):
    crossed = pltpu.roll(jnp.where(low, second, first), HALF, 1)
    return jnp.where(low, first, crossed), jnp.where(low, crossed, second)


def write_left(at, here, lines, left_ref):
    rows = left_ref.shape[1] // 2
    for line, values in enumerate(lines):
        high, rest = split(values)
        there = slice(line * rows + here.start, line * rows + here.stop)
        left_ref[at, there, :LANES] = high
        left_ref[at, there, LANES:] = rest


def line_product(at, here, left_ref, table):
    products = []
    rows = left_ref.shape[1] // 2
    for line in range(2):
        there = slice(line * rows + here.start, line * rows + here.stop)
        both = dot(left_ref[at, there, :], table)
        products.append(both[:, :LANES] + both[:, LANES:])
    return even_odd(*products, low_half(products[0].shape))


def class_sums(points):
    half = [points[ty] + points[ty + 4] for ty in range(4)]
    rest = [points[ty] - points[ty + 4] for ty in range(4)]
    even, odd = half[0] + half[2], half[1] + half[3]
    turn = math.sqrt(0.5)
    across, along = turn * (rest[1] - rest[3]), turn * (rest[1] + rest[3])
    return (
        (even + odd, even - odd),
        (rest[0] + across, rest[2] + along),
        (half[0] - half[2], half[1] - half[3]),
        (rest[0] - across, along - rest[2]),
    )


def level_of(most):
    return jnp.floor(jnp.log2(jnp.maximum(most, 1e-30)) * LOG_UNIT) + 2.0


def inverse_of(level):
    return FULL * jnp.exp2(level * (-1.0 / LOG_UNIT))


def fixed_of(values):
    return jnp.floor(values + 0.5).astype(jnp.int32).astype(jnp.int16)


def head_of(level):
    return jnp.broadcast_to(level, (HEAD_ROWS, LANES)).astype(jnp.int32).astype(jnp.int16)


def unit_of(sent_ref):
    head = sent_ref[sent_ref.shape[0] - HEAD_ROWS :, :].astype(jnp.int32).astype(jnp.float32)
    return jnp.exp2(head[0:1] * (1.0 / LOG_UNIT)) * (1.0 / FULL)


def wide(sent_ref):
    block = sent_ref[: sent_ref.shape[0] - HEAD_ROWS, :]
    return block.astype(jnp.int32).astype(jnp.float32) * unit_of(sent_ref)


def turned_up(row):
    return jnp.broadcast_to(row, (row.shape[1], row.shape[1])).T


def pack_kernel(
    owner_in, tile_in, count_in, brick_in, out_ref, one_hot_ref,
    owner_ref, tile_ref, count_ref, brick_ref, ready_ref, sems, out_sems,
):
    cells = brick_in.at[:, pl.ds(0, PART_CELLS)]
    copies = start_copies(((owner_in, owner_ref), (tile_in, tile_ref), (count_in, count_ref), (cells, brick_ref)), sems)
    for each in copies[:3]:
        each.wait()
    owner, tile = owner_ref[...], tile_ref[...]
    brick_rows = owner.shape[1]
    square = (brick_rows, brick_rows)
    position = (tile & 7) * SPOTS + ((tile >> 3) & 15) * 4 + (tile >> 7)
    spot = (position + 1).astype(jnp.float32)
    high = jnp.floor(spot * (1.0 / 32.0))
    heads = jnp.where(low_half(square), turned_up(high), turned_up(spot - 32.0 * high)).astype(jnp.bfloat16)
    named = owner.astype(jnp.float32)
    earlier = lax.broadcasted_iota(jnp.int32, square, 0) < lax.broadcasted_iota(jnp.int32, square, 1)
    same = jnp.where((turned_up(named) == named) & earlier, 1.0, 0.0)
    within = jnp.sum(same, axis=0, keepdims=True).astype(jnp.int32)
    live = lax.broadcasted_iota(jnp.int32, owner.shape, 1) < count_ref[0]
    slot = jnp.where(live, owner * PAIR_SLOTS + within, SLOTS)
    copies[3].wait()
    copies = []
    rows = 64
    for part in range(SLOTS // rows):
        here = slice(part * rows, (part + 1) * rows)
        index = lax.broadcasted_iota(jnp.int32, (rows, brick_rows), 0) + part * rows
        picks = jnp.where(index == slot, 1.0, 0.0).astype(jnp.bfloat16)
        one_hot_ref[here, :] = picks
        ready_ref[here, :PART_CELLS] = dot(picks, brick_ref[...]).astype(jnp.bfloat16)
        ready_ref[here, PART_CELLS:] = dot(picks, heads).astype(jnp.bfloat16)
        some = pl.ds(part * rows, rows)
        copies.append(pltpu.make_async_copy(ready_ref.at[some], out_ref.at[some], out_sems.at[part]))
        copies[-1].start()
    for each in copies:
        each.wait()


def pack_later_kernel(brick_in, one_hot_ref, out_ref, back_ref, brick_ref, sems):
    [copy] = start_copies(((brick_in.at[:, pl.ds(PART_CELLS, PART_CELLS)], brick_ref),), sems)
    for part in range(SLOTS // LANES):
        here = slice(part * LANES, (part + 1) * LANES)
        back_ref[:, here] = one_hot_ref[here, :].astype(jnp.float32).T.astype(jnp.bfloat16)
    copy.wait()
    out_ref[...] = dot(one_hot_ref[...], brick_ref[...]).astype(jnp.bfloat16)


def write_picks(brick_ref, picks_ref, across_ref):
    for part in range(SLOTS // LANES):
        here = slice(part * LANES, (part + 1) * LANES)
        head = brick_ref[here, PART_CELLS:].astype(jnp.float32)
        turned = pltpu.roll(head, HALF, 1)
        low = low_half(head.shape)
        places = (jnp.where(low, head, turned) * 32.0 + jnp.where(low, turned, head)).astype(jnp.int32) - 1
        for block in range(TILES // LANES):
            there = slice(block * LANES, (block + 1) * LANES)
            lane = lax.broadcasted_iota(jnp.int32, (LANES, LANES), 1) + block * LANES
            square = jnp.where(places == lane, 1.0, 0.0)
            picks_ref[here, there] = square.astype(jnp.bfloat16)
            across_ref[there, here] = square.T.astype(jnp.bfloat16)


def forward_lines(own_ref, brick_ref, across_ref, table_in, sent_refs, left_ref, lines_ref, table_ref, sems):
    [copy] = start_copies(((table_in, table_ref),), sems)
    low = low_half((SPOTS, LANES))
    for q in range(0, BRICK_ROWS // PARTS, 4):
        charge = dot(across_ref[...], brick_ref[:, q * LANES : (q + 4) * LANES])
        for one in range(4):
            there = slice(one * LANES, (one + 1) * LANES)
            here = slice((q + one) * SPOTS, (q + one + 1) * SPOTS)
            points = [charge[ty * SPOTS : (ty + 1) * SPOTS, there] for ty in range(8)]
            for pair, (cosines, sines) in enumerate(class_sums(points)):
                write_left(pair, here, even_odd(cosines, sines, low), left_ref)
    copy.wait()
    for pair in range(PAIRS):
        for one, values in enumerate(line_product(pair, slice(0, PART_ROWS), left_ref, table_ref[pair])):
            most = jnp.max(jnp.abs(values).reshape(PART_ROWS // 8, 8, LANES), axis=0)
            level = level_of(jnp.max(most, axis=0, keepdims=True))
            lines_ref[2 * pair + one, :PART_ROWS, :] = fixed_of(values * inverse_of(level))
            lines_ref[2 * pair + one, PART_ROWS:, :] = head_of(level)
    for offset, sent_ref in zip(SEND, sent_refs):
        sent_ref[...] = lines_ref[own_ref[0] ^ offset]


def forward_first_kernel(own_ref, brick_ref, table_in, *refs):
    sent_refs, (picks_ref, across_ref) = refs[: len(SEND)], refs[len(SEND) : len(SEND) + 2]
    write_picks(brick_ref, picks_ref, across_ref)
    forward_lines(own_ref, brick_ref, across_ref, table_in, sent_refs, *refs[len(SEND) + 2 :])


def forward_later_kernel(own_ref, brick_ref, across_ref, table_in, *refs):
    forward_lines(own_ref, brick_ref, across_ref, table_in, refs[: len(SEND)], *refs[len(SEND) :])


def grid_rows(slabs, plane, xq, tx):
    start = ((plane * 4 + xq) * SPOTS + tx * 4) * slabs
    return pl.ds(pl.multiple_of(start, 4 * slabs), 4 * slabs)


def plane_product(plane_ref, lines):
    high, rest = split(lines)
    rows = plane_ref.shape[0]
    if plane_ref.shape[1] == 3 * high.shape[0]:
        return dot(plane_ref[...], jnp.concatenate([high, rest, high], axis=0))
    both = dot(plane_ref[...], jnp.concatenate([high, rest], axis=0))
    return both[: rows // 2] + both[rows // 2 :]


def add_sines(got_refs, plane_ref, grid_ref, finish):
    slabs = len(got_refs)
    for at, got_ref in enumerate(got_refs):
        grid_ref[pl.ds(at, PART_ROWS, stride=slabs), :] = wide(got_ref)

    def planes(tx, xq):
        return jnp.concatenate(
            [grid_ref[grid_rows(slabs, plane, xq, tx), :] for plane in range(PART_PLANES)], axis=0
        )

    def sines(tx, _):
        modes = plane_product(plane_ref, jnp.concatenate([planes(tx, xq) for xq in range(4)], axis=1))
        for xq in range(4):
            finish(tx * 4 + xq, modes[:, xq * LANES : (xq + 1) * LANES])
        return 0

    lax.fori_loop(0, 16, sines, 0, unroll=8)


def down_first_kernel(own_ref, *refs):
    count = len(ARRIVAL)
    planes_ref, base_ref, lam_ref, modes_ref, root_ref, gain_ref, power_ref, grid_ref = refs[count:]
    excess = base_ref[...] + lam_ref[pl.ds(own_ref[0], 1), :]
    spread = jnp.sqrt(excess * (excess + 4.0))
    root_ref[...] = 2.0 / (2.0 + excess + spread)
    gain_ref[...] = 1.0 / spread
    for part in range(2):
        here = pl.ds(part * PLANES // 2, PLANES // 2)
        square = root_ref[here, :] * root_ref[here, :]

        def raised(step, power):
            power_ref[step, here, :] = power
            return power * square

        lax.fori_loop(0, STEPS, raised, jnp.ones(square.shape, jnp.float32), unroll=8)

    def finish(line, values):
        modes_ref[line] = values

    add_sines(refs[:count], planes_ref.at[own_ref[0]], grid_ref, finish)


def down_middle_kernel(own_ref, *refs):
    count = len(TAKE_FIRST)
    sums_ref, planes_ref, out_ref, grid_ref = refs[count:]

    def finish(line, values):
        out_ref[line] = sums_ref[line] + values

    add_sines(refs[:count], planes_ref.at[own_ref[0]], grid_ref, finish)


def down_later_kernel(own_ref, *refs):
    count = len(TAKE_LATER)
    sums_ref, root_ref, planes_ref, walk_ref, end_ref, grid_ref, modes_ref, last_ref = refs[count:]

    def finish(line, values):
        modes_ref[line] = sums_ref[line] + values

    add_sines(refs[:count], planes_ref.at[own_ref[0]], grid_ref, finish)
    part_rows = 64
    low = low_half((part_rows, LANES))
    for part in range(PLANES // part_rows):
        here = pl.ds(part * part_rows, part_rows)
        root = root_ref[here, :]
        square = root * root

        def walk(step, held):
            ahead, behind = modes_ref[step, here, :], modes_ref[STEPS - 1 - step, here, :]
            own = jnp.where(low, behind, ahead)
            other = pltpu.roll(jnp.where(low, ahead, behind), HALF, 1)
            held = square * held + (own + root * other)
            walk_ref[step, here, :] = held
            return held

        last_ref[here, :] = lax.fori_loop(0, STEPS, walk, jnp.zeros((part_rows, LANES), jnp.float32), unroll=8)
    last = last_ref[...]
    level = level_of(jnp.max(jnp.abs(last), axis=0, keepdims=True))
    end_ref[:PLANES, :] = fixed_of(last * inverse_of(level))
    end_ref[PLANES:, :] = head_of(level)


def local_kernel(walk_ref, root_ref, gain_ref, local_ref):
    part_rows = 64
    low = low_half((part_rows, LANES))
    for part in range(PLANES // part_rows):
        here = pl.ds(part * part_rows, part_rows)
        root, gain = root_ref[here, :], gain_ref[here, :]
        zero = jnp.zeros(root.shape, jnp.float32)

        def line(step, ahead_before, behind_after):
            near = jnp.where(low, walk_ref[STEPS - 1 - step, here, :], walk_ref[step, here, :])
            far = pltpu.roll(jnp.where(low, behind_after, ahead_before), HALF, 1)
            local_ref[step, here, :] = gain * (near + root * far)

        def inner(step, _):
            line(step, walk_ref[step - 1, here, :], walk_ref[STEPS - 2 - step, here, :])
            return 0

        line(0, zero, walk_ref[STEPS - 2, here, :])
        lax.fori_loop(1, STEPS - 1, inner, 0, unroll=6)
        line(STEPS - 1, walk_ref[STEPS - 2, here, :], zero)


def up_kernel(own_ref, local_ref, power_ref, root_ref, gain_ref, *refs):
    end_refs, plane_ref = refs[:GROUPS], refs[GROUPS].at[own_ref[0]]
    count = GROUPS + 1 + len(SEND)
    sent_refs = refs[GROUPS + 1 : count]
    rise_ref, fall_ref, grid_ref, level_ref = refs[count:]
    low = low_half((PLANES, LANES))
    root = root_ref[...]
    square = root * root
    across = square
    for _ in range(6):
        across = across * across
    around = across
    for _ in range(2):
        around = around * around
    ends = [wide(end_ref) for end_ref in end_refs]
    entering = jnp.zeros((PLANES, LANES), jnp.float32)
    for step in range(GROUPS - 1, -1, -1):
        entering = entering * across + jnp.where(low, ends[GROUPS - 1 - step], ends[(step + 1) % GROUPS])
    entering = gain_ref[...] * entering / (1.0 - around)
    straight, turned = square * entering, root * pltpu.roll(entering, HALF, 1)
    rise_ref[...] = jnp.where(low, turned, straight)
    fall_ref[...] = jnp.where(low, straight, turned)
    slabs = len(sent_refs)

    def solved(step):
        reach = rise_ref[...] * power_ref[step] + fall_ref[...] * power_ref[STEPS - 1 - step]
        return local_ref[step] + reach

    def sines(tx, most):
        lines = plane_product(plane_ref, jnp.concatenate([solved(tx * 4 + xq) for xq in range(4)], axis=1))
        for xq in range(4):
            part = lines[:, xq * LANES : (xq + 1) * LANES]
            most = jnp.maximum(most, jnp.max(jnp.abs(part).reshape(4 * BZ, slabs, LANES), axis=0))
            for plane in range(BZ):
                grid_ref[grid_rows(slabs, plane, xq, tx), :] = part[plane * 4 * slabs : (plane + 1) * 4 * slabs]
        return most

    most = lax.fori_loop(0, 16, sines, jnp.zeros((slabs, LANES), jnp.float32), unroll=8)
    level_ref[...] = level_of(most)
    for at, sent_ref in enumerate(sent_refs):
        level = level_ref[at : at + 1, :]
        sent_ref[:ROWS, :] = fixed_of(grid_ref[pl.ds(at, ROWS, stride=slabs), :] * inverse_of(level))
        sent_ref[ROWS:, :] = head_of(level)


def take_lines(own_ref, offsets, got_refs, left_ref, lines_ref):
    own = own_ref[0]
    pairs = list(dict.fromkeys(offset // 2 for offset in offsets))
    for offset, got_ref in zip(offsets, got_refs):
        lines_ref[2 * pairs.index(offset // 2) + ((own ^ offset) & 1)] = wide(got_ref)
    low = low_half((DOT_ROWS, LANES))
    for at in range(len(pairs)):
        for start in range(0, ROWS, DOT_ROWS):
            here = slice(start, start + DOT_ROWS)
            write_left(at, here, even_odd(lines_ref[2 * at, here, :], lines_ref[2 * at + 1, here, :], low), left_ref)
    return [(own >> 1) ^ pair for pair in pairs]


def point_parts(pair, cosines, sines, weight_ref):
    for ty in range(4):
        part = weight_ref[pair, ty] * cosines + weight_ref[pair, 4 + ty] * sines
        yield ty, part
        yield ty + 4, weight_ref[pair, 8] * part


def reply_first_kernel(own_ref, weight_ref, *refs):
    count = len(TAKE_FIRST)
    table_ref, sums_ref, lines_ref, left_ref = refs[count:]
    pairs = take_lines(own_ref, TAKE_FIRST, refs[:count], left_ref, lines_ref)
    for at, pair in enumerate(pairs):
        for part in range(ROWS // DOT_ROWS):
            here = slice(part * DOT_ROWS, (part + 1) * DOT_ROWS)
            cosines, sines = line_product(at, here, left_ref, table_ref[pair])
            for ty, values in point_parts(pair, cosines, sines, weight_ref):
                sums_ref[ty, here, :] = values if at == 0 else sums_ref[ty, here, :] + values


def reply_later_kernel(own_ref, weight_ref, *refs):
    count = len(TAKE_LATER)
    sums_ref, picks_ref, table_ref, out_ref, lines_ref, left_ref, pot_ref = refs[count:]
    [pair] = take_lines(own_ref, TAKE_LATER, refs[:count], left_ref, lines_ref)
    for part in range(ROWS // DOT_ROWS):
        here = slice(part * DOT_ROWS, (part + 1) * DOT_ROWS)
        cosines, sines = line_product(0, here, left_ref, table_ref[pair])
        for ty, values in point_parts(pair, cosines, sines, weight_ref):
            values = (sums_ref[ty, here, :] + values).astype(jnp.bfloat16)
            for one in range(DOT_ROWS // SPOTS):
                q = part * (DOT_ROWS // SPOTS) + one
                pot_ref[ty * SPOTS : (ty + 1) * SPOTS, q * LANES : (q + 1) * LANES] = values[
                    one * SPOTS : (one + 1) * SPOTS
                ]
    for q in range(0, BRICK_ROWS, 4):
        there = slice(q * LANES, (q + 4) * LANES)
        out_ref[:, there] = dot(picks_ref[...], pot_ref[:, there]).astype(jnp.bfloat16)


def unpack_kernel(back_ref, got_ref, out_ref):
    for q in range(0, BRICK_ROWS, 4):
        there = slice(q * LANES, (q + 4) * LANES)
        out_ref[:, there] = dot(back_ref[...], got_ref[:, there]).astype(jnp.bfloat16)


def call(kernel, name, operands, spaces, outs, places, scratch, vmem=VMEM_BYTES):
    return pl.pallas_call(
        kernel,
        out_shape=outs,
        in_specs=[pl.BlockSpec(memory_space=space) for space in spaces],
        out_specs=[pl.BlockSpec(memory_space=space) for space in places],
        scratch_shapes=scratch,
        compiler_params=pltpu.CompilerParams(vmem_limit_bytes=vmem),
        name=name,
    )(*operands)


def on_device_8x4(bricks, owners, tile_ids, counts):
    V, S, H = pltpu.VMEM, pltpu.SMEM, pltpu.HBM
    f32, bf16, i32, i16 = jnp.float32, jnp.bfloat16, jnp.int32, jnp.int16
    shape, dma = jax.ShapeDtypeStruct, pltpu.SemaphoreType.DMA
    brick_rows = bricks.shape[0]
    lines_in, lines_out = (jnp.asarray(each) for each in line_tables())
    weights = jnp.asarray(class_weights())
    lines_in = pltpu.with_memory_space_constraint(lines_in, H)
    planes_in = [
        jnp.asarray(plane_tables(offsets, planes, False))
        for offsets, planes in ((ARRIVAL, (0, 1)), (TAKE_FIRST, (2, 3)), (TAKE_LATER, (2, 3)))
    ]
    planes_out = jnp.asarray(plane_tables(SEND, range(BZ), True))
    base, lam = (jnp.asarray(each) for each in mode_tables())
    own = lax.axis_index("gz").astype(i32).reshape(1)
    sent_shape = shape((ROWS + HEAD_ROWS, LANES), i16)
    end_shape = shape((PLANES + HEAD_ROWS, LANES), i16)
    cube, flat, sums_shape = (STEPS, PLANES, LANES), (PLANES, LANES), (8, ROWS, LANES)
    line, packed = (ROWS, LANES), [(SLOTS, PART_CELLS + LANES), (SLOTS, PART_CELLS)]
    part_shape = shape((PART_ROWS + HEAD_ROWS, LANES), i16)

    def all_ways(values):
        return lax.all_to_all(values, ("gz", "ma"), split_axis=0, concat_axis=0, tiled=True)

    def over_slabs(offset, values):
        return lax.ppermute(values, "gz", [(g, g ^ offset) for g in range(SLABS)]) if offset else values

    def round_groups(values, step):
        return lax.ppermute(values, "ma", [(m, (m + step) % GROUPS) for m in range(GROUPS)]) if step else values

    def exchanged(sent):
        sent = dict(zip(SEND, sent))
        return [over_slabs(offset, sent[offset]) for offset in ARRIVAL]

    outgoing, one_hot = call(
        pack_kernel,
        "pack",
        (owners.reshape(1, brick_rows), tile_ids.reshape(1, brick_rows), counts, bricks),
        [H] * 4,
        [shape(packed[0], bf16), shape((SLOTS, brick_rows), bf16)],
        [H, V],
        [
            V((1, brick_rows), i32),
            V((1, brick_rows), i32),
            S((1,), i32),
            V((brick_rows, PART_CELLS), bf16),
            V(packed[0], bf16),
            dma((4,)),
            dma((4,)),
        ],
        ALL_VMEM_BYTES,
    )
    outgoing_later, back = call(
        pack_later_kernel,
        "pack_later",
        (bricks, one_hot),
        [H, V],
        [shape(packed[1], bf16), shape((brick_rows, SLOTS), bf16)],
        [V, V],
        [V((brick_rows, PART_CELLS), bf16), dma((1,))],
    )
    incoming = [all_ways(outgoing), all_ways(outgoing_later)]
    forward_scratch = [
        V((PAIRS, 2 * PART_ROWS, 2 * LANES), bf16),
        V((len(SEND), *part_shape.shape), i16),
        V(lines_in.shape, bf16),
        dma((1,)),
    ]
    *sent, picks, across = call(
        forward_first_kernel,
        "forward_first",
        (own, incoming[0], lines_in),
        [S, V, H],
        [part_shape] * len(SEND) + [shape((SLOTS, TILES), bf16), shape((TILES, SLOTS), bf16)],
        [V] * (len(SEND) + 2),
        forward_scratch,
    )
    first = exchanged(sent)
    second, first[1], first[2] = lax.optimization_barrier((incoming[1], first[1], first[2]))
    sent = call(
        forward_later_kernel,
        "forward_later",
        (own, second, across, lines_in),
        [S, V, V, H],
        [part_shape] * len(SEND),
        [V] * len(SEND),
        forward_scratch,
    )
    later = exchanged(sent)
    sums, root, gain, power = call(
        down_first_kernel,
        "down_first",
        (own, *first, planes_in[0], base, lam),
        [S] + [V] * (len(first) + 3),
        [shape(cube, f32), shape(flat, f32), shape(flat, f32), shape(cube, f32)],
        [V] * 4,
        [
            V((len(first) * PART_ROWS, LANES), f32),
        ],
    )
    middle, later = later[: len(TAKE_FIRST)], later[len(TAKE_FIRST) :]
    (sums,) = call(
        down_middle_kernel,
        "down_middle",
        (own, *middle, sums, planes_in[1]),
        [S] + [V] * (len(middle) + 2),
        [shape(cube, f32)],
        [V],
        [V((len(middle) * PART_ROWS, LANES), f32)],
    )
    walk, end = call(
        down_later_kernel,
        "down_later",
        (own, *later, sums, root, planes_in[2]),
        [S] + [V] * (len(later) + 3),
        [shape(cube, f32), end_shape],
        [V, V],
        [
            V((len(later) * PART_ROWS, LANES), f32),
            V(cube, f32),
            V(flat, f32),
        ],
    )
    ends = [round_groups(end, step) for step in range(GROUPS)]
    (local,) = call(local_kernel, "local", (walk, root, gain), [V] * 3, [shape(cube, f32)], [V], [])
    sent = call(
        up_kernel,
        "up",
        (own, local, power, root, gain, *ends, planes_out),
        [S] + [V] * (5 + GROUPS),
        [sent_shape] * len(SEND),
        [V] * len(SEND),
        [
            V(flat, f32),
            V(flat, f32),
            V((len(SEND) * ROWS, LANES), f32),
            V((len(SEND), LANES), f32),
        ],
    )
    got = exchanged(sent)
    first, later = got[: len(TAKE_FIRST)], got[len(TAKE_FIRST) :]
    (sums,) = call(
        reply_first_kernel,
        "reply_first",
        (own, weights, *first, lines_out),
        [S, S] + [V] * (len(first) + 1),
        [shape(sums_shape, f32)],
        [V],
        [V((len(first), *line), f32), V((len(first) // 2, 2 * ROWS, 2 * LANES), bf16)],
    )
    (replies,) = call(
        reply_later_kernel,
        "reply_later",
        (own, weights, *later, sums, picks, lines_out),
        [S, S] + [V] * (len(later) + 3),
        [shape((SLOTS, CELLS), bf16)],
        [V],
        [
            V((len(later), *line), f32),
            V((len(later) // 2, 2 * ROWS, 2 * LANES), bf16),
            V((TILES, CELLS), bf16),
        ],
    )
    (result,) = call(
        unpack_kernel,
        "unpack",
        (back, all_ways(replies)),
        [V, V],
        [shape((brick_rows, CELLS), bf16)],
        [V],
        [],
    )
    return result


def solution(mesh):
    in_specs = (P(("gz", "ma"), None), P(("gz", "ma"), None), P(("gz", "ma")), P(("gz", "ma")))
    out_specs = P(("gz", "ma"), None)
    body = on_device_8x4 if (mesh.shape["gz"], mesh.shape["ma"]) == (SLABS, GROUPS) else on_device
    return jax.shard_map(body, mesh=mesh, in_specs=in_specs, out_specs=out_specs, check_vma=False)
```

```python
import math

import jax
import jax.numpy as jnp
import ml_dtypes
import numpy as np
from jax import lax
from jax.experimental import pallas as pl
from jax.experimental.pallas import tpu as pltpu
from jax.sharding import PartitionSpec as P

NX = 512
NY = 512
SCREEN = 16
BZ = 4
BX = 8
BY = 64
CZ = 16


def hartley(length):
    indices = jnp.arange(length, dtype=jnp.int32)
    products = indices[:, None] * indices[None, :] % length
    angles = 2.0 * math.pi / length * products.astype(jnp.float32)
    return (jnp.cos(angles) + jnp.sin(angles)) / math.sqrt(length)


def second_difference(length, indices):
    return 2.0 - 2.0 * jnp.cos(2.0 * math.pi / length * indices.astype(jnp.float32))


def thomas(right_side, diagonal):
    start_zero = jnp.zeros(right_side.shape[1:], jnp.float32)

    def down(state_pair, plane):
        factor = 1.0 / (diagonal - state_pair[0])
        partial_value = (plane + state_pair[1]) * factor
        return ((factor, partial_value), (factor, partial_value))

    _, (factors, partials) = lax.scan(down, (start_zero, start_zero), right_side)

    def upward(beyond, factor_partial):
        solved = factor_partial[1] + factor_partial[0] * beyond
        return (solved, solved)

    _, solutions = lax.scan(upward, start_zero, (factors, partials), reverse=True)
    return solutions


def regroup(values):
    return lax.all_to_all(values, "ma", split_axis=2, concat_axis=1, tiled=True)


def on_device(bricks, owners, tile_ids, counts):
    domains = lax.axis_size(("gz", "ma"))
    group_count = lax.axis_size("ma")
    slab_count = lax.axis_size("gz")
    brick_rows, brick_cells = bricks.shape
    slot_count = max(2, 2 * brick_rows // domains)
    local_x = NX // group_count
    local_y = NY // group_count
    tiles_dev = CZ // BZ * (local_x // BX) * (NY // BY)
    highest = lax.Precision.HIGHEST
    target = owners[:, 0]
    row_order = jnp.arange(brick_rows, dtype=jnp.int32)
    earlier_same = (target[:, None] == target[None, :]) & (row_order[None, :] < row_order[:, None])
    within = jnp.sum(earlier_same.astype(jnp.int32), axis=1)
    slot_of = target * slot_count + within
    is_live = row_order < counts[0]
    loaded = jnp.where(is_live[:, None], bricks, jnp.zeros_like(bricks))
    outgoing = jnp.zeros((domains * slot_count, brick_cells), jnp.bfloat16).at[slot_of].set(loaded)
    out_ids = jnp.full((domains * slot_count,), tiles_dev, jnp.int32).at[slot_of].set(tile_ids)
    incoming, in_ids = (
        lax.all_to_all(outgoing, ("gz", "ma"), split_axis=0, concat_axis=0, tiled=True),
        lax.all_to_all(out_ids, ("gz", "ma"), split_axis=0, concat_axis=0, tiled=True),
    )
    picker = (jnp.arange(tiles_dev, dtype=jnp.int32)[:, None] == in_ids[None, :]).astype(
        jnp.bfloat16
    )
    deposit = jnp.dot(picker, incoming, preferred_element_type=jnp.float32)
    charge = deposit.reshape(CZ // BZ, local_x // BX, NY // BY, BZ, BX, BY)
    charge = charge.transpose(0, 3, 1, 4, 2, 5).reshape(CZ, local_x, NY)
    table_x = hartley(NX)
    table_y = hartley(NY)
    along_y = jnp.einsum("zxy,ky->zxk", charge, table_y, precision=highest)
    gathered_x = regroup(along_y)
    spectrum = jnp.einsum("zxk,jx->zjk", gathered_x, table_x, precision=highest)
    columns = lax.axis_index("ma") * local_y + jnp.arange(local_y, dtype=jnp.int32)
    lam_y = second_difference(NY, columns)
    screening = 1.0 / (SCREEN * SCREEN)
    slab_index = lax.axis_index("gz")
    lam_x = second_difference(NX, jnp.arange(NX, dtype=jnp.int32))
    diagonal = 2.0 + screening + lam_x[:, None] + lam_y[None, :]
    interior = spectrum[1:]
    particular = thomas(interior, diagonal)
    unit_rhs = jnp.zeros_like(interior).at[0].set(1.0)
    spike = thomas(unit_rhs, diagonal)
    near_weight = spike[0]
    far_weight = spike[-1]
    head_term = spectrum[0] + particular[0]
    tail_term = particular[-1]
    reduced_first = diagonal - near_weight
    reduced_rest = diagonal - 2.0 * near_weight
    start_zero = jnp.zeros_like(diagonal)
    heads, tails = (
        lax.all_gather(head_term[None], "gz", axis=0, tiled=True),
        lax.all_gather(tail_term[None], "gz", axis=0, tiled=True),
    )
    before = jnp.concatenate([start_zero[None], tails[:-1]], axis=0)
    sources = heads + before

    def chain_down(state_pair, packed):
        source, position = packed
        base_term = jnp.where(position == 0, reduced_first, reduced_rest)
        pivot_now = 1.0 / (base_term - far_weight * far_weight * state_pair[0])
        forward_part = pivot_now * (source + far_weight * state_pair[1])
        return ((pivot_now, forward_part), (pivot_now, forward_part))

    _, (pivots, forwards) = lax.scan(
        chain_down, (start_zero, start_zero), (sources, jnp.arange(slab_count, dtype=jnp.int32))
    )

    def chain_up(beyond, packed):
        plane_value = packed[1] + far_weight * packed[0] * beyond
        return (plane_value, plane_value)

    _, separators = lax.scan(chain_up, start_zero, (pivots, forwards), reverse=True)
    padded_sep = jnp.concatenate([separators, start_zero[None]], axis=0)
    own_plane = lax.dynamic_index_in_dim(padded_sep, slab_index, 0, keepdims=False)
    next_plane = lax.dynamic_index_in_dim(padded_sep, slab_index + 1, 0, keepdims=False)
    interior_sol = particular + own_plane[None] * spike + next_plane[None] * spike[::-1]
    modal = jnp.concatenate([own_plane[None], interior_sol], axis=0)
    back_x = jnp.einsum("zjk,jx->zkx", modal, table_x, precision=highest)
    gathered_y = regroup(back_x)
    potential = jnp.einsum("zkx,ky->zxy", gathered_y, table_y, precision=highest)
    pot_tiles = potential.reshape(CZ // BZ, BZ, local_x // BX, BX, NY // BY, BY)
    pot_tiles = (
        pot_tiles.transpose(0, 2, 4, 1, 3, 5).reshape(tiles_dev, brick_cells).astype(jnp.bfloat16)
    )
    padded_tiles = jnp.concatenate([pot_tiles, jnp.zeros((1, brick_cells), jnp.bfloat16)], axis=0)
    replies = padded_tiles[in_ids]
    returned = lax.all_to_all(replies, ("gz", "ma"), split_axis=0, concat_axis=0, tiled=True)
    result = returned[slot_of]
    return jnp.where(is_live[:, None], result, jnp.zeros_like(result))


DOMAINS = 32
GROUPS = 4
SLABS = 8
SEND = (4, 2, 5, 3, 0, 1, 6, 7)
ARRIVAL = (0, 4, 2, 5, 3, 1, 6, 7)
PARTS = 2
PART_PLANES = 2
TAKE_FIRST = (0, 4, 2, 5, 3, 1)
TAKE_LATER = (6, 7)
PAIR_SLOTS = 8
SLOTS = DOMAINS * PAIR_SLOTS
TILES = 512
BRICK_ROWS = 16
CELLS = 2048
LANES = 128
HALF = 64
SPOTS = 64
ROWS = BRICK_ROWS * SPOTS
PART_ROWS = ROWS // PARTS
PART_CELLS = CELLS // PARTS
DOT_ROWS = 512
PAIRS = 4
CLASSES = (0, 4, 1, 7, 2, 6, 3, 5)
HEAD_ROWS = 8
STEPS = 64
PLANES = 128
FULL = 32700.0
LOG_UNIT = 128.0
VMEM_BYTES = 24 * 1024 * 1024
ALL_VMEM_BYTES = 60 * 1024 * 1024


def split_table(table):
    high = table.astype(ml_dtypes.bfloat16)
    low = (table - high.astype(np.float64)).astype(ml_dtypes.bfloat16)
    return high, low


def line_tables():
    iy, k2 = np.arange(HALF)[:, None], np.arange(HALF)[None, :]
    tables = []
    for pair in range(PAIRS):
        table = np.zeros((LANES, LANES))
        for one in range(2):
            angle = 2.0 * np.pi / NY * (iy * (CLASSES[2 * pair + one] + 8 * k2) % NY)
            cosine, sine = np.cos(angle) / np.sqrt(NY), np.sin(angle) / np.sqrt(NY)
            there = slice(one * HALF, (one + 1) * HALF)
            if pair == 0:
                table[there, there] = cosine + sine
            else:
                table[:HALF, there] = cosine + sine
                table[HALF:, there] = (cosine - sine) * (1 - 2 * one)
        tables.append(table)

    def stacked(table):
        high, low = split_table(table)
        return np.concatenate(
            [np.concatenate([high, low], axis=1), np.concatenate([high, np.zeros_like(low)], axis=1)], axis=0
        )

    return np.stack([stacked(table) for table in tables]), np.stack([stacked(table.T) for table in tables])


def class_weights():
    pair, ty = np.arange(PAIRS)[:, None], np.arange(4)[None, :]
    cosine, sine = np.cos(np.pi / 4.0 * pair * ty), np.sin(np.pi / 4.0 * pair * ty)
    sine[0] = (-1.0) ** np.arange(4)
    sign = (-1.0) ** pair * np.ones((1, 4))
    return np.concatenate([cosine, sine, sign], axis=1).astype(np.float32)


def plane_tables(offsets, planes, turned):
    index = np.arange(PLANES)
    table = np.sqrt(2.0 / (PLANES + 1)) * np.sin(
        np.pi / (PLANES + 1) * ((index[:, None] + 1) * (index[None, :] + 1) % (2 * PLANES + 2))
    )
    each = []
    for own in range(SLABS):
        slabs = np.array([own ^ offset for offset in offsets])
        plane, tz = np.array(planes)[:, None, None], np.arange(BZ)[None, :, None]
        part = table[:, (slabs * CZ + tz * BZ + plane).reshape(-1)]
        high, low = split_table(part.T if turned else part)
        if turned or 3 * high.shape[1] <= 2 * LANES:
            each.append(np.concatenate([high, high, low], axis=1))
            continue
        top = np.concatenate([high, high], axis=1)
        bottom = np.concatenate([low, np.zeros_like(low)], axis=1)
        each.append(np.concatenate([top, bottom], axis=0))
    return np.stack(each)


def mode_tables():
    mu = 2.0 - 2.0 * np.cos(np.pi / (PLANES + 1) * (np.arange(PLANES) + 1))
    base = np.broadcast_to((mu + 1.0 / (SCREEN * SCREEN))[:, None], (PLANES, LANES))
    lam = 2.0 - 2.0 * np.cos(2.0 * np.pi / NY * np.arange(NY))
    lam = np.stack([lam[number::8] for number in CLASSES])
    return base.astype(np.float32), np.concatenate([lam, lam], axis=1).astype(np.float32)


def low_half(shape):
    return lax.broadcasted_iota(jnp.int32, shape, len(shape) - 1) < HALF


def split(values):
    high = values.astype(jnp.bfloat16)
    return high, (values - high.astype(jnp.float32)).astype(jnp.bfloat16)


def dot(left, right):
    return jnp.dot(left, right, preferred_element_type=jnp.float32)


def start_copies(pairs, sems):
    copies = [pltpu.make_async_copy(source, place, sems.at[at]) for at, (source, place) in enumerate(pairs)]
    for each in copies:
        each.start()
    return copies


def even_odd(first, second, low):
    crossed = pltpu.roll(jnp.where(low, second, first), HALF, 1)
    return jnp.where(low, first, crossed), jnp.where(low, crossed, second)


def write_left(at, here, lines, left_ref):
    rows = left_ref.shape[1] // 2
    for line, values in enumerate(lines):
        high, rest = split(values)
        there = slice(line * rows + here.start, line * rows + here.stop)
        left_ref[at, there, :LANES] = high
        left_ref[at, there, LANES:] = rest


def line_product(at, here, left_ref, table):
    products = []
    rows = left_ref.shape[1] // 2
    for line in range(2):
        there = slice(line * rows + here.start, line * rows + here.stop)
        both = dot(left_ref[at, there, :], table)
        products.append(both[:, :LANES] + both[:, LANES:])
    return even_odd(*products, low_half(products[0].shape))


def class_sums(points):
    half = [points[ty] + points[ty + 4] for ty in range(4)]
    rest = [points[ty] - points[ty + 4] for ty in range(4)]
    even, odd = half[0] + half[2], half[1] + half[3]
    turn = math.sqrt(0.5)
    across, along = turn * (rest[1] - rest[3]), turn * (rest[1] + rest[3])
    return (
        (even + odd, even - odd),
        (rest[0] + across, rest[2] + along),
        (half[0] - half[2], half[1] - half[3]),
        (rest[0] - across, along - rest[2]),
    )


def level_of(most):
    return jnp.floor(jnp.log2(jnp.maximum(most, 1e-30)) * LOG_UNIT) + 2.0


def inverse_of(level):
    return FULL * jnp.exp2(level * (-1.0 / LOG_UNIT))


def fixed_of(values):
    return jnp.floor(values + 0.5).astype(jnp.int32).astype(jnp.int16)


def head_of(level):
    return jnp.broadcast_to(level, (HEAD_ROWS, LANES)).astype(jnp.int32).astype(jnp.int16)


def unit_of(sent_ref):
    head = sent_ref[sent_ref.shape[0] - HEAD_ROWS :, :].astype(jnp.int32).astype(jnp.float32)
    return jnp.exp2(head[0:1] * (1.0 / LOG_UNIT)) * (1.0 / FULL)


def wide(sent_ref):
    block = sent_ref[: sent_ref.shape[0] - HEAD_ROWS, :]
    return block.astype(jnp.int32).astype(jnp.float32) * unit_of(sent_ref)


def turned_up(row):
    return jnp.broadcast_to(row, (row.shape[1], row.shape[1])).T


def pack_kernel(
    owner_in, tile_in, count_in, brick_in, out_ref, one_hot_ref,
    owner_ref, tile_ref, count_ref, brick_ref, ready_ref, sems, out_sems,
):
    cells = brick_in.at[:, pl.ds(0, PART_CELLS)]
    copies = start_copies(((owner_in, owner_ref), (tile_in, tile_ref), (count_in, count_ref), (cells, brick_ref)), sems)
    for each in copies[:3]:
        each.wait()
    owner, tile = owner_ref[...], tile_ref[...]
    brick_rows = owner.shape[1]
    square = (brick_rows, brick_rows)
    position = (tile & 7) * SPOTS + ((tile >> 3) & 15) * 4 + (tile >> 7)
    spot = (position + 1).astype(jnp.float32)
    high = jnp.floor(spot * (1.0 / 32.0))
    heads = jnp.where(low_half(square), turned_up(high), turned_up(spot - 32.0 * high)).astype(jnp.bfloat16)
    named = owner.astype(jnp.float32)
    earlier = lax.broadcasted_iota(jnp.int32, square, 0) < lax.broadcasted_iota(jnp.int32, square, 1)
    same = jnp.where((turned_up(named) == named) & earlier, 1.0, 0.0)
    within = jnp.sum(same, axis=0, keepdims=True).astype(jnp.int32)
    live = lax.broadcasted_iota(jnp.int32, owner.shape, 1) < count_ref[0]
    slot = jnp.where(live, owner * PAIR_SLOTS + within, SLOTS)
    copies[3].wait()
    copies = []
    rows = 64
    for part in range(SLOTS // rows):
        here = slice(part * rows, (part + 1) * rows)
        index = lax.broadcasted_iota(jnp.int32, (rows, brick_rows), 0) + part * rows
        picks = jnp.where(index == slot, 1.0, 0.0).astype(jnp.bfloat16)
        one_hot_ref[here, :] = picks
        ready_ref[here, :PART_CELLS] = dot(picks, brick_ref[...]).astype(jnp.bfloat16)
        ready_ref[here, PART_CELLS:] = dot(picks, heads).astype(jnp.bfloat16)
        some = pl.ds(part * rows, rows)
        copies.append(pltpu.make_async_copy(ready_ref.at[some], out_ref.at[some], out_sems.at[part]))
        copies[-1].start()
    for each in copies:
        each.wait()


def pack_later_kernel(brick_in, one_hot_ref, out_ref, back_ref, brick_ref, sems):
    [copy] = start_copies(((brick_in.at[:, pl.ds(PART_CELLS, PART_CELLS)], brick_ref),), sems)
    for part in range(SLOTS // LANES):
        here = slice(part * LANES, (part + 1) * LANES)
        back_ref[:, here] = one_hot_ref[here, :].astype(jnp.float32).T.astype(jnp.bfloat16)
    copy.wait()
    out_ref[...] = dot(one_hot_ref[...], brick_ref[...]).astype(jnp.bfloat16)


def write_across(brick_ref, across_ref):
    for part in range(SLOTS // LANES):
        here = slice(part * LANES, (part + 1) * LANES)
        head = brick_ref[here, PART_CELLS:].astype(jnp.float32)
        turned = pltpu.roll(head, HALF, 1)
        low = low_half(head.shape)
        places = jnp.where(low, head, turned) * 32.0 + jnp.where(low, turned, head)
        row = places.T[0:1, :].astype(jnp.int32) - 1
        for block in range(TILES // LANES):
            there = slice(block * LANES, (block + 1) * LANES)
            tile = lax.broadcasted_iota(jnp.int32, (LANES, LANES), 0) + block * LANES
            across_ref[there, here] = jnp.where(tile == row, 1.0, 0.0).astype(jnp.bfloat16)


def write_picks(across_ref, picks_ref):
    for part in range(SLOTS // LANES):
        here = slice(part * LANES, (part + 1) * LANES)
        for block in range(TILES // LANES):
            there = slice(block * LANES, (block + 1) * LANES)
            picks_ref[here, there] = across_ref[there, here].astype(jnp.float32).T.astype(jnp.bfloat16)


def forward_lines(own_ref, brick_ref, across_ref, table_in, sent_refs, left_ref, lines_ref, table_ref, sems):
    [copy] = start_copies(((table_in, table_ref),), sems)
    low = low_half((SPOTS, LANES))
    for q in range(0, BRICK_ROWS // PARTS, 4):
        charge = dot(across_ref[...], brick_ref[:, q * LANES : (q + 4) * LANES])
        for one in range(4):
            there = slice(one * LANES, (one + 1) * LANES)
            here = slice((q + one) * SPOTS, (q + one + 1) * SPOTS)
            points = [charge[ty * SPOTS : (ty + 1) * SPOTS, there] for ty in range(8)]
            for pair, (cosines, sines) in enumerate(class_sums(points)):
                write_left(pair, here, even_odd(cosines, sines, low), left_ref)
    copy.wait()
    for pair in range(PAIRS):
        for one, values in enumerate(line_product(pair, slice(0, PART_ROWS), left_ref, table_ref[pair])):
            most = jnp.max(jnp.abs(values).reshape(PART_ROWS // 8, 8, LANES), axis=0)
            level = level_of(jnp.max(most, axis=0, keepdims=True))
            lines_ref[2 * pair + one, :PART_ROWS, :] = fixed_of(values * inverse_of(level))
            lines_ref[2 * pair + one, PART_ROWS:, :] = head_of(level)
    for offset, sent_ref in zip(SEND, sent_refs):
        sent_ref[...] = lines_ref[own_ref[0] ^ offset]


def forward_first_kernel(own_ref, brick_ref, table_in, *refs):
    sent_refs, across_ref = refs[: len(SEND)], refs[len(SEND)]
    write_across(brick_ref, across_ref)
    forward_lines(own_ref, brick_ref, across_ref, table_in, sent_refs, *refs[len(SEND) + 1 :])


def forward_later_kernel(own_ref, brick_ref, across_ref, table_in, *refs):
    sent_refs, picks_ref = refs[: len(SEND)], refs[len(SEND)]
    write_picks(across_ref, picks_ref)
    forward_lines(own_ref, brick_ref, across_ref, table_in, sent_refs, *refs[len(SEND) + 1 :])


def grid_rows(slabs, plane, xq, tx):
    start = ((plane * 4 + xq) * SPOTS + tx * 4) * slabs
    return pl.ds(pl.multiple_of(start, 4 * slabs), 4 * slabs)


def plane_product(plane_ref, lines):
    high, rest = split(lines)
    rows = plane_ref.shape[0]
    if plane_ref.shape[1] == 3 * high.shape[0]:
        return dot(plane_ref[...], jnp.concatenate([high, rest, high], axis=0))
    both = dot(plane_ref[...], jnp.concatenate([high, rest], axis=0))
    return both[: rows // 2] + both[rows // 2 :]


def add_sines(got_refs, plane_ref, grid_ref, finish, swapped=False):
    slabs = len(got_refs)
    for at, got_ref in enumerate(got_refs):
        grid_ref[pl.ds(at, PART_ROWS, stride=slabs), :] = wide(got_ref)

    def planes(tx, xq):
        return jnp.concatenate(
            [grid_ref[grid_rows(slabs, plane, xq, tx), :] for plane in range(PART_PLANES)], axis=0
        )

    def sines(tx, _):
        lines = [planes(tx, xq) for xq in range(4)]
        if swapped:
            lines += [pltpu.roll(line, HALF, 1) for line in lines]
        modes = plane_product(plane_ref, jnp.concatenate(lines, axis=1))
        parts = [modes[:, at * LANES : (at + 1) * LANES] for at in range(len(lines))]
        for xq in range(4):
            finish(tx * 4 + xq, *parts[xq::4])
        return 0

    lax.fori_loop(0, 16, sines, 0, unroll=8)


def down_first_kernel(own_ref, *refs):
    count = len(ARRIVAL)
    planes_ref, base_ref, lam_ref, modes_ref, root_ref, gain_ref, power_ref, grid_ref = refs[count:]
    excess = base_ref[...] + lam_ref[pl.ds(own_ref[0], 1), :]
    spread = jnp.sqrt(excess * (excess + 4.0))
    root_ref[...] = 2.0 / (2.0 + excess + spread)
    gain_ref[...] = 1.0 / spread
    for part in range(2):
        here = pl.ds(part * PLANES // 2, PLANES // 2)
        square = root_ref[here, :] * root_ref[here, :]

        def raised(step, power):
            power_ref[step, here, :] = power
            return power * square

        lax.fori_loop(0, STEPS, raised, jnp.ones(square.shape, jnp.float32), unroll=8)

    def finish(line, values):
        modes_ref[line] = values

    add_sines(refs[:count], planes_ref.at[own_ref[0]], grid_ref, finish)


def down_middle_kernel(own_ref, *refs):
    count = len(TAKE_FIRST)
    sums_ref, root_ref, planes_ref, out_ref, grid_ref = refs[count:]

    def finish(line, values):
        values = sums_ref[line] + values
        out_ref[line] = values + root_ref[...] * pltpu.roll(values, HALF, 1)

    add_sines(refs[:count], planes_ref.at[own_ref[0]], grid_ref, finish)


def down_later_kernel(own_ref, *refs):
    count = len(TAKE_LATER)
    sums_ref, root_ref, planes_ref, walk_ref, end_ref, grid_ref, modes_ref, last_ref = refs[count:]

    def finish(line, values, swapped):
        modes_ref[line] = sums_ref[line] + (values + root_ref[...] * swapped)

    add_sines(refs[:count], planes_ref.at[own_ref[0]], grid_ref, finish, True)
    part_rows = 64
    low = low_half((part_rows, LANES))
    for part in range(PLANES // part_rows):
        here = pl.ds(part * part_rows, part_rows)
        square = root_ref[here, :] * root_ref[here, :]

        def walk(step, held):
            held = square * held + jnp.where(low, modes_ref[STEPS - 1 - step, here, :], modes_ref[step, here, :])
            walk_ref[step, here, :] = held
            return held

        last_ref[here, :] = lax.fori_loop(0, STEPS, walk, jnp.zeros((part_rows, LANES), jnp.float32), unroll=8)
    last = last_ref[...]
    level = level_of(jnp.max(jnp.abs(last), axis=0, keepdims=True))
    end_ref[:PLANES, :] = fixed_of(last * inverse_of(level))
    end_ref[PLANES:, :] = head_of(level)


def local_kernel(walk_ref, root_ref, gain_ref, local_ref):
    part_rows = 64
    low = low_half((part_rows, LANES))
    for part in range(PLANES // part_rows):
        here = pl.ds(part * part_rows, part_rows)
        root, gain = root_ref[here, :], gain_ref[here, :]
        zero = jnp.zeros(root.shape, jnp.float32)

        def line(step, ahead_before, behind_after):
            near = jnp.where(low, walk_ref[STEPS - 1 - step, here, :], walk_ref[step, here, :])
            far = pltpu.roll(jnp.where(low, behind_after, ahead_before), HALF, 1)
            local_ref[step, here, :] = gain * (near + root * far)

        def inner(step, _):
            line(step, walk_ref[step - 1, here, :], walk_ref[STEPS - 2 - step, here, :])
            return 0

        line(0, zero, walk_ref[STEPS - 2, here, :])
        lax.fori_loop(1, STEPS - 1, inner, 0, unroll=6)
        line(STEPS - 1, walk_ref[STEPS - 2, here, :], zero)


def up_kernel(own_ref, local_ref, power_ref, root_ref, gain_ref, *refs):
    end_refs, plane_ref = refs[:GROUPS], refs[GROUPS].at[own_ref[0]]
    count = GROUPS + 1 + len(SEND)
    sent_refs = refs[GROUPS + 1 : count]
    rise_ref, fall_ref, grid_ref, level_ref = refs[count:]
    low = low_half((PLANES, LANES))
    root = root_ref[...]
    square = root * root
    across = square
    for _ in range(6):
        across = across * across
    around = across
    for _ in range(2):
        around = around * around
    ends = [wide(end_ref) for end_ref in end_refs]
    entering = jnp.zeros((PLANES, LANES), jnp.float32)
    for step in range(GROUPS - 1, -1, -1):
        entering = entering * across + jnp.where(low, ends[GROUPS - 1 - step], ends[(step + 1) % GROUPS])
    entering = gain_ref[...] * entering / (1.0 - around)
    straight, turned = square * entering, root * pltpu.roll(entering, HALF, 1)
    rise_ref[...] = jnp.where(low, turned, straight)
    fall_ref[...] = jnp.where(low, straight, turned)
    slabs = len(sent_refs)

    def solved(step):
        reach = rise_ref[...] * power_ref[step] + fall_ref[...] * power_ref[STEPS - 1 - step]
        return local_ref[step] + reach

    def sines(tx, most):
        lines = plane_product(plane_ref, jnp.concatenate([solved(tx * 4 + xq) for xq in range(4)], axis=1))
        for xq in range(4):
            part = lines[:, xq * LANES : (xq + 1) * LANES]
            most = jnp.maximum(most, jnp.max(jnp.abs(part).reshape(4 * BZ, slabs, LANES), axis=0))
            for plane in range(BZ):
                grid_ref[grid_rows(slabs, plane, xq, tx), :] = part[plane * 4 * slabs : (plane + 1) * 4 * slabs]
        return most

    most = lax.fori_loop(0, 16, sines, jnp.zeros((slabs, LANES), jnp.float32), unroll=8)
    level_ref[...] = level_of(most)
    for at, sent_ref in enumerate(sent_refs):
        level = level_ref[at : at + 1, :]
        sent_ref[:ROWS, :] = fixed_of(grid_ref[pl.ds(at, ROWS, stride=slabs), :] * inverse_of(level))
        sent_ref[ROWS:, :] = head_of(level)


def take_lines(own_ref, offsets, got_refs, left_ref, lines_ref):
    own = own_ref[0]
    pairs = list(dict.fromkeys(offset // 2 for offset in offsets))
    for offset, got_ref in zip(offsets, got_refs):
        lines_ref[2 * pairs.index(offset // 2) + ((own ^ offset) & 1)] = wide(got_ref)
    low = low_half((DOT_ROWS, LANES))
    for at in range(len(pairs)):
        for start in range(0, ROWS, DOT_ROWS):
            here = slice(start, start + DOT_ROWS)
            write_left(at, here, even_odd(lines_ref[2 * at, here, :], lines_ref[2 * at + 1, here, :], low), left_ref)
    return [(own >> 1) ^ pair for pair in pairs]


def point_parts(pair, cosines, sines, weight_ref):
    for ty in range(4):
        part = weight_ref[pair, ty] * cosines + weight_ref[pair, 4 + ty] * sines
        yield ty, part
        yield ty + 4, weight_ref[pair, 8] * part


def reply_first_kernel(own_ref, weight_ref, *refs):
    count = len(TAKE_FIRST)
    table_ref, sums_ref, lines_ref, left_ref = refs[count:]
    pairs = take_lines(own_ref, TAKE_FIRST, refs[:count], left_ref, lines_ref)
    for at, pair in enumerate(pairs):
        for part in range(ROWS // DOT_ROWS):
            here = slice(part * DOT_ROWS, (part + 1) * DOT_ROWS)
            cosines, sines = line_product(at, here, left_ref, table_ref[pair])
            for ty, values in point_parts(pair, cosines, sines, weight_ref):
                sums_ref[ty, here, :] = values if at == 0 else sums_ref[ty, here, :] + values


def reply_later_kernel(own_ref, weight_ref, *refs):
    count = len(TAKE_LATER)
    sums_ref, picks_ref, table_ref, out_ref, lines_ref, left_ref, pot_ref = refs[count:]
    [pair] = take_lines(own_ref, TAKE_LATER, refs[:count], left_ref, lines_ref)
    for part in range(ROWS // DOT_ROWS):
        here = slice(part * DOT_ROWS, (part + 1) * DOT_ROWS)
        cosines, sines = line_product(0, here, left_ref, table_ref[pair])
        for ty, values in point_parts(pair, cosines, sines, weight_ref):
            values = (sums_ref[ty, here, :] + values).astype(jnp.bfloat16)
            for one in range(DOT_ROWS // SPOTS):
                q = part * (DOT_ROWS // SPOTS) + one
                pot_ref[ty * SPOTS : (ty + 1) * SPOTS, q * LANES : (q + 1) * LANES] = values[
                    one * SPOTS : (one + 1) * SPOTS
                ]
    for q in range(0, BRICK_ROWS, 4):
        there = slice(q * LANES, (q + 4) * LANES)
        out_ref[:, there] = dot(picks_ref[...], pot_ref[:, there]).astype(jnp.bfloat16)


def unpack_kernel(back_ref, got_ref, out_ref):
    for q in range(0, BRICK_ROWS, 4):
        there = slice(q * LANES, (q + 4) * LANES)
        out_ref[:, there] = dot(back_ref[...], got_ref[:, there]).astype(jnp.bfloat16)


def call(kernel, name, operands, spaces, outs, places, scratch, vmem=VMEM_BYTES):
    return pl.pallas_call(
        kernel,
        out_shape=outs,
        in_specs=[pl.BlockSpec(memory_space=space) for space in spaces],
        out_specs=[pl.BlockSpec(memory_space=space) for space in places],
        scratch_shapes=scratch,
        compiler_params=pltpu.CompilerParams(vmem_limit_bytes=vmem),
        name=name,
    )(*operands)


def on_device_8x4(bricks, owners, tile_ids, counts):
    V, S, H = pltpu.VMEM, pltpu.SMEM, pltpu.HBM
    f32, bf16, i32, i16 = jnp.float32, jnp.bfloat16, jnp.int32, jnp.int16
    shape, dma = jax.ShapeDtypeStruct, pltpu.SemaphoreType.DMA
    brick_rows = bricks.shape[0]
    lines_in, lines_out = (jnp.asarray(each) for each in line_tables())
    weights = jnp.asarray(class_weights())
    lines_in = pltpu.with_memory_space_constraint(lines_in, H)
    planes_in = [
        jnp.asarray(plane_tables(offsets, planes, False))
        for offsets, planes in ((ARRIVAL, (0, 1)), (TAKE_FIRST, (2, 3)), (TAKE_LATER, (2, 3)))
    ]
    planes_out = jnp.asarray(plane_tables(SEND, range(BZ), True))
    base, lam = (jnp.asarray(each) for each in mode_tables())
    own = lax.axis_index("gz").astype(i32).reshape(1)
    sent_shape = shape((ROWS + HEAD_ROWS, LANES), i16)
    end_shape = shape((PLANES + HEAD_ROWS, LANES), i16)
    cube, flat, sums_shape = (STEPS, PLANES, LANES), (PLANES, LANES), (8, ROWS, LANES)
    line, packed = (ROWS, LANES), [(SLOTS, PART_CELLS + LANES), (SLOTS, PART_CELLS)]
    part_shape = shape((PART_ROWS + HEAD_ROWS, LANES), i16)

    def all_ways(values):
        return lax.all_to_all(values, ("gz", "ma"), split_axis=0, concat_axis=0, tiled=True)

    def over_slabs(offset, values):
        return lax.ppermute(values, "gz", [(g, g ^ offset) for g in range(SLABS)]) if offset else values

    def round_groups(values, step):
        return lax.ppermute(values, "ma", [(m, (m + step) % GROUPS) for m in range(GROUPS)]) if step else values

    def exchanged(sent):
        sent = dict(zip(SEND, sent))
        return [over_slabs(offset, sent[offset]) for offset in ARRIVAL]

    outgoing, one_hot = call(
        pack_kernel,
        "pack",
        (owners.reshape(1, brick_rows), tile_ids.reshape(1, brick_rows), counts, bricks),
        [H] * 4,
        [shape(packed[0], bf16), shape((SLOTS, brick_rows), bf16)],
        [H, V],
        [
            V((1, brick_rows), i32),
            V((1, brick_rows), i32),
            S((1,), i32),
            V((brick_rows, PART_CELLS), bf16),
            V(packed[0], bf16),
            dma((4,)),
            dma((4,)),
        ],
        ALL_VMEM_BYTES,
    )
    outgoing_later, back = call(
        pack_later_kernel,
        "pack_later",
        (bricks, one_hot),
        [H, V],
        [shape(packed[1], bf16), shape((brick_rows, SLOTS), bf16)],
        [V, V],
        [V((brick_rows, PART_CELLS), bf16), dma((1,))],
    )
    incoming = [all_ways(outgoing), all_ways(outgoing_later)]
    forward_scratch = [
        V((PAIRS, 2 * PART_ROWS, 2 * LANES), bf16),
        V((len(SEND), *part_shape.shape), i16),
        V(lines_in.shape, bf16),
        dma((1,)),
    ]
    *sent, across = call(
        forward_first_kernel,
        "forward_first",
        (own, incoming[0], lines_in),
        [S, V, H],
        [part_shape] * len(SEND) + [shape((TILES, SLOTS), bf16)],
        [V] * (len(SEND) + 1),
        forward_scratch,
    )
    first = exchanged(sent)
    second, first[1], first[2] = lax.optimization_barrier((incoming[1], first[1], first[2]))
    *sent, picks = call(
        forward_later_kernel,
        "forward_later",
        (own, second, across, lines_in),
        [S, V, V, H],
        [part_shape] * len(SEND) + [shape((SLOTS, TILES), bf16)],
        [V] * (len(SEND) + 1),
        forward_scratch,
    )
    later = exchanged(sent)
    sums, root, gain, power = call(
        down_first_kernel,
        "down_first",
        (own, *first, planes_in[0], base, lam),
        [S] + [V] * (len(first) + 3),
        [shape(cube, f32), shape(flat, f32), shape(flat, f32), shape(cube, f32)],
        [V] * 4,
        [
            V((len(first) * PART_ROWS, LANES), f32),
        ],
    )
    middle, later = later[: len(TAKE_FIRST)], later[len(TAKE_FIRST) :]
    (sums,) = call(
        down_middle_kernel,
        "down_middle",
        (own, *middle, sums, root, planes_in[1]),
        [S] + [V] * (len(middle) + 3),
        [shape(cube, f32)],
        [V],
        [V((len(middle) * PART_ROWS, LANES), f32)],
    )
    walk, end = call(
        down_later_kernel,
        "down_later",
        (own, *later, sums, root, planes_in[2]),
        [S] + [V] * (len(later) + 3),
        [shape(cube, f32), end_shape],
        [V, V],
        [
            V((len(later) * PART_ROWS, LANES), f32),
            V(cube, f32),
            V(flat, f32),
        ],
    )
    ends = [round_groups(end, step) for step in range(GROUPS)]
    (local,) = call(local_kernel, "local", (walk, root, gain), [V] * 3, [shape(cube, f32)], [V], [])
    sent = call(
        up_kernel,
        "up",
        (own, local, power, root, gain, *ends, planes_out),
        [S] + [V] * (5 + GROUPS),
        [sent_shape] * len(SEND),
        [V] * len(SEND),
        [
            V(flat, f32),
            V(flat, f32),
            V((len(SEND) * ROWS, LANES), f32),
            V((len(SEND), LANES), f32),
        ],
    )
    got = exchanged(sent)
    first, later = got[: len(TAKE_FIRST)], got[len(TAKE_FIRST) :]
    (sums,) = call(
        reply_first_kernel,
        "reply_first",
        (own, weights, *first, lines_out),
        [S, S] + [V] * (len(first) + 1),
        [shape(sums_shape, f32)],
        [V],
        [V((len(first), *line), f32), V((len(first) // 2, 2 * ROWS, 2 * LANES), bf16)],
    )
    (replies,) = call(
        reply_later_kernel,
        "reply_later",
        (own, weights, *later, sums, picks, lines_out),
        [S, S] + [V] * (len(later) + 3),
        [shape((SLOTS, CELLS), bf16)],
        [V],
        [
            V((len(later), *line), f32),
            V((len(later) // 2, 2 * ROWS, 2 * LANES), bf16),
            V((TILES, CELLS), bf16),
        ],
    )
    (result,) = call(
        unpack_kernel,
        "unpack",
        (back, all_ways(replies)),
        [V, V],
        [shape((brick_rows, CELLS), bf16)],
        [V],
        [],
    )
    return result


def solution(mesh):
    in_specs = (P(("gz", "ma"), None), P(("gz", "ma"), None), P(("gz", "ma")), P(("gz", "ma")))
    out_specs = P(("gz", "ma"), None)
    body = on_device_8x4 if (mesh.shape["gz"], mesh.shape["ma"]) == (SLABS, GROUPS) else on_device
    return jax.shard_map(body, mesh=mesh, in_specs=in_specs, out_specs=out_specs, check_vma=False)
```

```python
import math

import jax
import jax.numpy as jnp
import ml_dtypes
import numpy as np
from jax import lax
from jax.experimental import pallas as pl
from jax.experimental.pallas import tpu as pltpu
from jax.sharding import PartitionSpec as P

NX = 512
NY = 512
SCREEN = 16
BZ = 4
BX = 8
BY = 64
CZ = 16


def hartley(length):
    indices = jnp.arange(length, dtype=jnp.int32)
    products = indices[:, None] * indices[None, :] % length
    angles = 2.0 * math.pi / length * products.astype(jnp.float32)
    return (jnp.cos(angles) + jnp.sin(angles)) / math.sqrt(length)


def second_difference(length, indices):
    return 2.0 - 2.0 * jnp.cos(2.0 * math.pi / length * indices.astype(jnp.float32))


def thomas(right_side, diagonal):
    start_zero = jnp.zeros(right_side.shape[1:], jnp.float32)

    def down(state_pair, plane):
        factor = 1.0 / (diagonal - state_pair[0])
        partial_value = (plane + state_pair[1]) * factor
        return ((factor, partial_value), (factor, partial_value))

    _, (factors, partials) = lax.scan(down, (start_zero, start_zero), right_side)

    def upward(beyond, factor_partial):
        solved = factor_partial[1] + factor_partial[0] * beyond
        return (solved, solved)

    _, solutions = lax.scan(upward, start_zero, (factors, partials), reverse=True)
    return solutions


def regroup(values):
    return lax.all_to_all(values, "ma", split_axis=2, concat_axis=1, tiled=True)


def on_device(bricks, owners, tile_ids, counts):
    domains = lax.axis_size(("gz", "ma"))
    group_count = lax.axis_size("ma")
    slab_count = lax.axis_size("gz")
    brick_rows, brick_cells = bricks.shape
    slot_count = max(2, 2 * brick_rows // domains)
    local_x = NX // group_count
    local_y = NY // group_count
    tiles_dev = CZ // BZ * (local_x // BX) * (NY // BY)
    highest = lax.Precision.HIGHEST
    target = owners[:, 0]
    row_order = jnp.arange(brick_rows, dtype=jnp.int32)
    earlier_same = (target[:, None] == target[None, :]) & (row_order[None, :] < row_order[:, None])
    within = jnp.sum(earlier_same.astype(jnp.int32), axis=1)
    slot_of = target * slot_count + within
    is_live = row_order < counts[0]
    loaded = jnp.where(is_live[:, None], bricks, jnp.zeros_like(bricks))
    outgoing = jnp.zeros((domains * slot_count, brick_cells), jnp.bfloat16).at[slot_of].set(loaded)
    out_ids = jnp.full((domains * slot_count,), tiles_dev, jnp.int32).at[slot_of].set(tile_ids)
    incoming, in_ids = (
        lax.all_to_all(outgoing, ("gz", "ma"), split_axis=0, concat_axis=0, tiled=True),
        lax.all_to_all(out_ids, ("gz", "ma"), split_axis=0, concat_axis=0, tiled=True),
    )
    picker = (jnp.arange(tiles_dev, dtype=jnp.int32)[:, None] == in_ids[None, :]).astype(
        jnp.bfloat16
    )
    deposit = jnp.dot(picker, incoming, preferred_element_type=jnp.float32)
    charge = deposit.reshape(CZ // BZ, local_x // BX, NY // BY, BZ, BX, BY)
    charge = charge.transpose(0, 3, 1, 4, 2, 5).reshape(CZ, local_x, NY)
    table_x = hartley(NX)
    table_y = hartley(NY)
    along_y = jnp.einsum("zxy,ky->zxk", charge, table_y, precision=highest)
    gathered_x = regroup(along_y)
    spectrum = jnp.einsum("zxk,jx->zjk", gathered_x, table_x, precision=highest)
    columns = lax.axis_index("ma") * local_y + jnp.arange(local_y, dtype=jnp.int32)
    lam_y = second_difference(NY, columns)
    screening = 1.0 / (SCREEN * SCREEN)
    slab_index = lax.axis_index("gz")
    lam_x = second_difference(NX, jnp.arange(NX, dtype=jnp.int32))
    diagonal = 2.0 + screening + lam_x[:, None] + lam_y[None, :]
    interior = spectrum[1:]
    particular = thomas(interior, diagonal)
    unit_rhs = jnp.zeros_like(interior).at[0].set(1.0)
    spike = thomas(unit_rhs, diagonal)
    near_weight = spike[0]
    far_weight = spike[-1]
    head_term = spectrum[0] + particular[0]
    tail_term = particular[-1]
    reduced_first = diagonal - near_weight
    reduced_rest = diagonal - 2.0 * near_weight
    start_zero = jnp.zeros_like(diagonal)
    heads, tails = (
        lax.all_gather(head_term[None], "gz", axis=0, tiled=True),
        lax.all_gather(tail_term[None], "gz", axis=0, tiled=True),
    )
    before = jnp.concatenate([start_zero[None], tails[:-1]], axis=0)
    sources = heads + before

    def chain_down(state_pair, packed):
        source, position = packed
        base_term = jnp.where(position == 0, reduced_first, reduced_rest)
        pivot_now = 1.0 / (base_term - far_weight * far_weight * state_pair[0])
        forward_part = pivot_now * (source + far_weight * state_pair[1])
        return ((pivot_now, forward_part), (pivot_now, forward_part))

    _, (pivots, forwards) = lax.scan(
        chain_down, (start_zero, start_zero), (sources, jnp.arange(slab_count, dtype=jnp.int32))
    )

    def chain_up(beyond, packed):
        plane_value = packed[1] + far_weight * packed[0] * beyond
        return (plane_value, plane_value)

    _, separators = lax.scan(chain_up, start_zero, (pivots, forwards), reverse=True)
    padded_sep = jnp.concatenate([separators, start_zero[None]], axis=0)
    own_plane = lax.dynamic_index_in_dim(padded_sep, slab_index, 0, keepdims=False)
    next_plane = lax.dynamic_index_in_dim(padded_sep, slab_index + 1, 0, keepdims=False)
    interior_sol = particular + own_plane[None] * spike + next_plane[None] * spike[::-1]
    modal = jnp.concatenate([own_plane[None], interior_sol], axis=0)
    back_x = jnp.einsum("zjk,jx->zkx", modal, table_x, precision=highest)
    gathered_y = regroup(back_x)
    potential = jnp.einsum("zkx,ky->zxy", gathered_y, table_y, precision=highest)
    pot_tiles = potential.reshape(CZ // BZ, BZ, local_x // BX, BX, NY // BY, BY)
    pot_tiles = (
        pot_tiles.transpose(0, 2, 4, 1, 3, 5).reshape(tiles_dev, brick_cells).astype(jnp.bfloat16)
    )
    padded_tiles = jnp.concatenate([pot_tiles, jnp.zeros((1, brick_cells), jnp.bfloat16)], axis=0)
    replies = padded_tiles[in_ids]
    returned = lax.all_to_all(replies, ("gz", "ma"), split_axis=0, concat_axis=0, tiled=True)
    result = returned[slot_of]
    return jnp.where(is_live[:, None], result, jnp.zeros_like(result))


DOMAINS = 32
GROUPS = 4
SLABS = 8
SEND = (4, 2, 5, 3, 0, 1, 6, 7)
ARRIVAL = (0, 4, 2, 5, 3, 1, 6, 7)
PARTS = 2
PART_PLANES = 2
TAKE_FIRST = (0, 4, 2, 5, 3, 1)
TAKE_LATER = (6, 7)
PAIR_SLOTS = 8
SLOTS = DOMAINS * PAIR_SLOTS
TILES = 512
BRICK_ROWS = 16
CELLS = 2048
LANES = 128
HALF = 64
SPOTS = 64
ROWS = BRICK_ROWS * SPOTS
PART_ROWS = ROWS // PARTS
PART_CELLS = CELLS // PARTS
DOT_ROWS = 512
PAIRS = 4
CLASSES = (0, 4, 1, 7, 2, 6, 3, 5)
HEAD_ROWS = 8
STEPS = 64
PLANES = 128
FULL = 32700.0
LOG_UNIT = 128.0
VMEM_BYTES = 24 * 1024 * 1024
ALL_VMEM_BYTES = 60 * 1024 * 1024


def split_table(table):
    high = table.astype(ml_dtypes.bfloat16)
    low = (table - high.astype(np.float64)).astype(ml_dtypes.bfloat16)
    return high, low


def line_tables():
    iy, k2 = np.arange(HALF)[:, None], np.arange(HALF)[None, :]
    tables = []
    for pair in range(PAIRS):
        table = np.zeros((LANES, LANES))
        for one in range(2):
            angle = 2.0 * np.pi / NY * (iy * (CLASSES[2 * pair + one] + 8 * k2) % NY)
            cosine, sine = np.cos(angle) / np.sqrt(NY), np.sin(angle) / np.sqrt(NY)
            there = slice(one * HALF, (one + 1) * HALF)
            if pair == 0:
                table[there, there] = cosine + sine
            else:
                table[:HALF, there] = cosine + sine
                table[HALF:, there] = (cosine - sine) * (1 - 2 * one)
        tables.append(table)

    def stacked(table):
        high, low = split_table(table)
        return np.concatenate(
            [np.concatenate([high, low], axis=1), np.concatenate([high, np.zeros_like(low)], axis=1)], axis=0
        )

    return np.stack([stacked(table) for table in tables]), np.stack([stacked(table.T) for table in tables])


def class_weights():
    pair, ty = np.arange(PAIRS)[:, None], np.arange(4)[None, :]
    cosine, sine = np.cos(np.pi / 4.0 * pair * ty), np.sin(np.pi / 4.0 * pair * ty)
    sine[0] = (-1.0) ** np.arange(4)
    sign = (-1.0) ** pair * np.ones((1, 4))
    return np.concatenate([cosine, sine, sign], axis=1).astype(np.float32)


def plane_tables(offsets, planes, turned):
    index = np.arange(PLANES)
    table = np.sqrt(2.0 / (PLANES + 1)) * np.sin(
        np.pi / (PLANES + 1) * ((index[:, None] + 1) * (index[None, :] + 1) % (2 * PLANES + 2))
    )
    each = []
    for own in range(SLABS):
        slabs = np.array([own ^ offset for offset in offsets])
        plane, tz = np.array(planes)[:, None, None], np.arange(BZ)[None, :, None]
        place = slabs * CZ + tz * BZ + plane
        part = table[:, (place.transpose(0, 2, 1) if turned else place).reshape(-1)]
        high, low = split_table(part.T if turned else part)
        if turned or 3 * high.shape[1] <= 2 * LANES:
            each.append(np.concatenate([high, high, low], axis=1))
            continue
        top = np.concatenate([high, high], axis=1)
        bottom = np.concatenate([low, np.zeros_like(low)], axis=1)
        each.append(np.concatenate([top, bottom], axis=0))
    return np.stack(each)


def mode_tables():
    mu = 2.0 - 2.0 * np.cos(np.pi / (PLANES + 1) * (np.arange(PLANES) + 1))
    base = np.broadcast_to((mu + 1.0 / (SCREEN * SCREEN))[:, None], (PLANES, LANES))
    lam = 2.0 - 2.0 * np.cos(2.0 * np.pi / NY * np.arange(NY))
    lam = np.stack([lam[number::8] for number in CLASSES])
    return base.astype(np.float32), np.concatenate([lam, lam], axis=1).astype(np.float32)


def low_half(shape):
    return lax.broadcasted_iota(jnp.int32, shape, len(shape) - 1) < HALF


def split(values):
    high = values.astype(jnp.bfloat16)
    return high, (values - high.astype(jnp.float32)).astype(jnp.bfloat16)


def dot(left, right):
    return jnp.dot(left, right, preferred_element_type=jnp.float32)


def start_copies(pairs, sems):
    copies = [pltpu.make_async_copy(source, place, sems.at[at]) for at, (source, place) in enumerate(pairs)]
    for each in copies:
        each.start()
    return copies


def even_odd(first, second, low):
    crossed = pltpu.roll(jnp.where(low, second, first), HALF, 1)
    return jnp.where(low, first, crossed), jnp.where(low, crossed, second)


def write_left(at, here, lines, left_ref):
    rows = left_ref.shape[1] // 2
    for line, values in enumerate(lines):
        high, rest = split(values)
        there = slice(line * rows + here.start, line * rows + here.stop)
        left_ref[at, there, :LANES] = high
        left_ref[at, there, LANES:] = rest


def line_product(at, here, left_ref, table):
    products = []
    rows = left_ref.shape[1] // 2
    for line in range(2):
        there = slice(line * rows + here.start, line * rows + here.stop)
        both = dot(left_ref[at, there, :], table)
        products.append(both[:, :LANES] + both[:, LANES:])
    return even_odd(*products, low_half(products[0].shape))


def class_sums(points):
    half = [points[ty] + points[ty + 4] for ty in range(4)]
    rest = [points[ty] - points[ty + 4] for ty in range(4)]
    even, odd = half[0] + half[2], half[1] + half[3]
    turn = math.sqrt(0.5)
    across, along = turn * (rest[1] - rest[3]), turn * (rest[1] + rest[3])
    return (
        (even + odd, even - odd),
        (rest[0] + across, rest[2] + along),
        (half[0] - half[2], half[1] - half[3]),
        (rest[0] - across, along - rest[2]),
    )


def level_of(most):
    return jnp.floor(jnp.log2(jnp.maximum(most, 1e-30)) * LOG_UNIT) + 2.0


def inverse_of(level):
    return FULL * jnp.exp2(level * (-1.0 / LOG_UNIT))


def fixed_of(values):
    return jnp.floor(values + 0.5).astype(jnp.int32).astype(jnp.int16)


def head_of(level):
    return jnp.broadcast_to(level, (HEAD_ROWS, LANES)).astype(jnp.int32).astype(jnp.int16)


def unit_of(sent_ref):
    head = sent_ref[sent_ref.shape[0] - HEAD_ROWS :, :].astype(jnp.int32).astype(jnp.float32)
    return jnp.exp2(head[0:1] * (1.0 / LOG_UNIT)) * (1.0 / FULL)


def wide(sent_ref):
    block = sent_ref[: sent_ref.shape[0] - HEAD_ROWS, :]
    return block.astype(jnp.int32).astype(jnp.float32) * unit_of(sent_ref)


def turned_up(row):
    return jnp.broadcast_to(row, (row.shape[1], row.shape[1])).T


def pack_kernel(
    owner_in, tile_in, count_in, brick_in, out_ref, one_hot_ref,
    owner_ref, tile_ref, count_ref, brick_ref, ready_ref, sems, out_sems,
):
    cells = brick_in.at[:, pl.ds(0, PART_CELLS)]
    copies = start_copies(((owner_in, owner_ref), (tile_in, tile_ref), (count_in, count_ref), (cells, brick_ref)), sems)
    for each in copies[:3]:
        each.wait()
    owner, tile = owner_ref[...], tile_ref[...]
    brick_rows = owner.shape[1]
    square = (brick_rows, brick_rows)
    position = (tile & 7) * SPOTS + ((tile >> 3) & 15) * 4 + (tile >> 7)
    spot = (position + 1).astype(jnp.float32)
    high = jnp.floor(spot * (1.0 / 32.0))
    heads = jnp.where(low_half(square), turned_up(high), turned_up(spot - 32.0 * high)).astype(jnp.bfloat16)
    named = owner.astype(jnp.float32)
    earlier = lax.broadcasted_iota(jnp.int32, square, 0) < lax.broadcasted_iota(jnp.int32, square, 1)
    same = jnp.where((turned_up(named) == named) & earlier, 1.0, 0.0)
    within = jnp.sum(same, axis=0, keepdims=True).astype(jnp.int32)
    live = lax.broadcasted_iota(jnp.int32, owner.shape, 1) < count_ref[0]
    slot = jnp.where(live, owner * PAIR_SLOTS + within, SLOTS)
    copies[3].wait()
    copies = []
    rows = 64
    for part in range(SLOTS // rows):
        here = slice(part * rows, (part + 1) * rows)
        index = lax.broadcasted_iota(jnp.int32, (rows, brick_rows), 0) + part * rows
        picks = jnp.where(index == slot, 1.0, 0.0).astype(jnp.bfloat16)
        one_hot_ref[here, :] = picks
        ready_ref[here, :PART_CELLS] = dot(picks, brick_ref[...]).astype(jnp.bfloat16)
        ready_ref[here, PART_CELLS:] = dot(picks, heads).astype(jnp.bfloat16)
        some = pl.ds(part * rows, rows)
        copies.append(pltpu.make_async_copy(ready_ref.at[some], out_ref.at[some], out_sems.at[part]))
        copies[-1].start()
    for each in copies:
        each.wait()


def pack_later_kernel(brick_in, one_hot_ref, out_ref, back_ref, brick_ref, sems):
    [copy] = start_copies(((brick_in.at[:, pl.ds(PART_CELLS, PART_CELLS)], brick_ref),), sems)
    for part in range(SLOTS // LANES):
        here = slice(part * LANES, (part + 1) * LANES)
        back_ref[:, here] = one_hot_ref[here, :].astype(jnp.float32).T.astype(jnp.bfloat16)
    copy.wait()
    out_ref[...] = dot(one_hot_ref[...], brick_ref[...]).astype(jnp.bfloat16)


def write_across(brick_ref, across_ref):
    for part in range(SLOTS // LANES):
        here = slice(part * LANES, (part + 1) * LANES)
        head = brick_ref[here, PART_CELLS:].astype(jnp.float32)
        turned = pltpu.roll(head, HALF, 1)
        low = low_half(head.shape)
        places = jnp.where(low, head, turned) * 32.0 + jnp.where(low, turned, head)
        row = places.T[0:1, :].astype(jnp.int32) - 1
        for block in range(TILES // LANES):
            there = slice(block * LANES, (block + 1) * LANES)
            tile = lax.broadcasted_iota(jnp.int32, (LANES, LANES), 0) + block * LANES
            across_ref[there, here] = jnp.where(tile == row, 1.0, 0.0).astype(jnp.bfloat16)


def write_picks(across_ref, picks_ref):
    for part in range(SLOTS // LANES):
        here = slice(part * LANES, (part + 1) * LANES)
        for block in range(TILES // LANES):
            there = slice(block * LANES, (block + 1) * LANES)
            picks_ref[here, there] = across_ref[there, here].astype(jnp.float32).T.astype(jnp.bfloat16)


def forward_lines(own_ref, brick_ref, across_ref, table_in, sent_refs, left_ref, lines_ref, table_ref, sems):
    [copy] = start_copies(((table_in, table_ref),), sems)
    low = low_half((SPOTS, LANES))
    for q in range(0, BRICK_ROWS // PARTS, 4):
        charge = dot(across_ref[...], brick_ref[:, q * LANES : (q + 4) * LANES])
        for one in range(4):
            there = slice(one * LANES, (one + 1) * LANES)
            here = slice((q + one) * SPOTS, (q + one + 1) * SPOTS)
            points = [charge[ty * SPOTS : (ty + 1) * SPOTS, there] for ty in range(8)]
            for pair, (cosines, sines) in enumerate(class_sums(points)):
                write_left(pair, here, even_odd(cosines, sines, low), left_ref)
    copy.wait()
    for pair in range(PAIRS):
        for one, values in enumerate(line_product(pair, slice(0, PART_ROWS), left_ref, table_ref[pair])):
            most = jnp.max(jnp.abs(values).reshape(PART_ROWS // 8, 8, LANES), axis=0)
            level = level_of(jnp.max(most, axis=0, keepdims=True))
            lines_ref[2 * pair + one, :PART_ROWS, :] = fixed_of(values * inverse_of(level))
            lines_ref[2 * pair + one, PART_ROWS:, :] = head_of(level)
    for offset, sent_ref in zip(SEND, sent_refs):
        sent_ref[...] = lines_ref[own_ref[0] ^ offset]


def forward_first_kernel(own_ref, brick_ref, table_in, *refs):
    sent_refs, across_ref = refs[: len(SEND)], refs[len(SEND)]
    write_across(brick_ref, across_ref)
    forward_lines(own_ref, brick_ref, across_ref, table_in, sent_refs, *refs[len(SEND) + 1 :])


def forward_later_kernel(own_ref, brick_ref, across_ref, table_in, *refs):
    sent_refs, picks_ref = refs[: len(SEND)], refs[len(SEND)]
    write_picks(across_ref, picks_ref)
    forward_lines(own_ref, brick_ref, across_ref, table_in, sent_refs, *refs[len(SEND) + 1 :])


def grid_rows(slabs, plane, xq, tx):
    start = ((plane * 4 + xq) * SPOTS + tx * 4) * slabs
    return pl.ds(pl.multiple_of(start, 4 * slabs), 4 * slabs)


def plane_product(plane_ref, lines):
    high, rest = split(lines)
    rows = plane_ref.shape[0]
    if plane_ref.shape[1] == 3 * high.shape[0]:
        return dot(plane_ref[...], jnp.concatenate([high, rest, high], axis=0))
    both = dot(plane_ref[...], jnp.concatenate([high, rest], axis=0))
    return both[: rows // 2] + both[rows // 2 :]


def add_sines(got_refs, plane_ref, grid_ref, finish, swapped=False):
    slabs = len(got_refs)
    for at, got_ref in enumerate(got_refs):
        grid_ref[pl.ds(at, PART_ROWS, stride=slabs), :] = wide(got_ref)

    def planes(tx, xq):
        return jnp.concatenate(
            [grid_ref[grid_rows(slabs, plane, xq, tx), :] for plane in range(PART_PLANES)], axis=0
        )

    def sines(tx, _):
        lines = [planes(tx, xq) for xq in range(4)]
        if swapped:
            lines += [pltpu.roll(line, HALF, 1) for line in lines]
        modes = plane_product(plane_ref, jnp.concatenate(lines, axis=1))
        parts = [modes[:, at * LANES : (at + 1) * LANES] for at in range(len(lines))]
        for xq in range(4):
            finish(tx * 4 + xq, *parts[xq::4])
        return 0

    lax.fori_loop(0, 16, sines, 0, unroll=8)


def down_first_kernel(own_ref, *refs):
    count = len(ARRIVAL)
    planes_ref, base_ref, lam_ref, modes_ref, root_ref, gain_ref, power_ref, grid_ref = refs[count:]
    excess = base_ref[...] + lam_ref[pl.ds(own_ref[0], 1), :]
    spread = jnp.sqrt(excess * (excess + 4.0))
    root_ref[...] = 2.0 / (2.0 + excess + spread)
    gain_ref[...] = 1.0 / spread
    for part in range(2):
        here = pl.ds(part * PLANES // 2, PLANES // 2)
        square = root_ref[here, :] * root_ref[here, :]

        def raised(step, power):
            power_ref[step, here, :] = power
            return power * square

        lax.fori_loop(0, STEPS, raised, jnp.ones(square.shape, jnp.float32), unroll=8)

    def finish(line, values):
        modes_ref[line] = values

    add_sines(refs[:count], planes_ref.at[own_ref[0]], grid_ref, finish)


def down_middle_kernel(own_ref, *refs):
    count = len(TAKE_FIRST)
    sums_ref, root_ref, planes_ref, out_ref, grid_ref = refs[count:]

    def finish(line, values):
        values = sums_ref[line] + values
        out_ref[line] = values + root_ref[...] * pltpu.roll(values, HALF, 1)

    add_sines(refs[:count], planes_ref.at[own_ref[0]], grid_ref, finish)


def down_later_kernel(own_ref, *refs):
    count = len(TAKE_LATER)
    sums_ref, root_ref, planes_ref, walk_ref, end_ref, grid_ref, modes_ref, last_ref = refs[count:]

    def finish(line, values, swapped):
        modes_ref[line] = sums_ref[line] + (values + root_ref[...] * swapped)

    add_sines(refs[:count], planes_ref.at[own_ref[0]], grid_ref, finish, True)
    part_rows = 64
    low = low_half((part_rows, LANES))
    for part in range(PLANES // part_rows):
        here = pl.ds(part * part_rows, part_rows)
        square = root_ref[here, :] * root_ref[here, :]

        def walk(step, held):
            held = square * held + jnp.where(low, modes_ref[STEPS - 1 - step, here, :], modes_ref[step, here, :])
            walk_ref[step, here, :] = held
            return held

        last_ref[here, :] = lax.fori_loop(0, STEPS, walk, jnp.zeros((part_rows, LANES), jnp.float32), unroll=8)
    last = last_ref[...]
    level = level_of(jnp.max(jnp.abs(last), axis=0, keepdims=True))
    end_ref[:PLANES, :] = fixed_of(last * inverse_of(level))
    end_ref[PLANES:, :] = head_of(level)


def local_kernel(walk_ref, root_ref, gain_ref, local_ref):
    part_rows = 64
    low = low_half((part_rows, LANES))
    for part in range(PLANES // part_rows):
        here = pl.ds(part * part_rows, part_rows)
        root, gain = root_ref[here, :], gain_ref[here, :]
        zero = jnp.zeros(root.shape, jnp.float32)

        def line(step, ahead_before, behind_after):
            near = jnp.where(low, walk_ref[STEPS - 1 - step, here, :], walk_ref[step, here, :])
            far = pltpu.roll(jnp.where(low, behind_after, ahead_before), HALF, 1)
            local_ref[step, here, :] = gain * (near + root * far)

        def inner(step, _):
            line(step, walk_ref[step - 1, here, :], walk_ref[STEPS - 2 - step, here, :])
            return 0

        line(0, zero, walk_ref[STEPS - 2, here, :])
        lax.fori_loop(1, STEPS - 1, inner, 0, unroll=6)
        line(STEPS - 1, walk_ref[STEPS - 2, here, :], zero)


def up_kernel(own_ref, local_ref, power_ref, root_ref, gain_ref, *refs):
    end_refs, plane_ref = refs[:GROUPS], refs[GROUPS].at[own_ref[0]]
    count = GROUPS + 1 + len(SEND)
    sent_refs = refs[GROUPS + 1 : count]
    rise_ref, fall_ref, lines_ref = refs[count:]
    low = low_half((PLANES, LANES))
    root = root_ref[...]
    square = root * root
    across = square
    for _ in range(6):
        across = across * across
    around = across
    for _ in range(2):
        around = around * around
    ends = [wide(end_ref) for end_ref in end_refs]
    entering = jnp.zeros((PLANES, LANES), jnp.float32)
    for step in range(GROUPS - 1, -1, -1):
        entering = entering * across + jnp.where(low, ends[GROUPS - 1 - step], ends[(step + 1) % GROUPS])
    entering = gain_ref[...] * entering / (1.0 - around)
    straight, turned = square * entering, root * pltpu.roll(entering, HALF, 1)
    rise_ref[...] = jnp.where(low, turned, straight)
    fall_ref[...] = jnp.where(low, straight, turned)
    slabs = len(sent_refs)
    upper = lax.broadcasted_iota(jnp.int32, (8, LANES), 0) < 4

    def solved(step):
        reach = rise_ref[...] * power_ref[step] + fall_ref[...] * power_ref[STEPS - 1 - step]
        return local_ref[step] + reach

    def lines_of(tx):
        return plane_product(plane_ref, jnp.concatenate([solved(tx * 4 + xq) for xq in range(4)], axis=1))

    def sines(step, most):
        most = list(most)
        both = lines_of(2 * step), lines_of(2 * step + 1)
        for xq in range(4):
            there = slice(xq * LANES, (xq + 1) * LANES)
            for plane in range(BZ):
                row = pl.multiple_of((plane * 4 + xq) * SPOTS + step * 8, 8)
                for slab in range(0, slabs, 2):
                    start = plane * 4 * slabs + slab * 4
                    first, second = (each[start : start + 8, there] for each in both)
                    crossed = pltpu.roll(jnp.where(upper, second, first), 4, 0)
                    for one, values in enumerate((jnp.where(upper, first, crossed), jnp.where(upper, crossed, second))):
                        lines_ref[slab + one, pl.ds(row, 8), :] = values
                        most[slab + one] = jnp.maximum(most[slab + one], jnp.abs(values))
        return tuple(most)

    most = lax.fori_loop(0, 8, sines, (jnp.zeros((8, LANES), jnp.float32),) * slabs, unroll=4)
    for at, sent_ref in enumerate(sent_refs):
        level = level_of(jnp.max(most[at], axis=0, keepdims=True))
        sent_ref[:ROWS, :] = fixed_of(lines_ref[at] * inverse_of(level))
        sent_ref[ROWS:, :] = head_of(level)


def take_lines(own_ref, offsets, got_refs, left_ref, lines_ref):
    own = own_ref[0]
    pairs = list(dict.fromkeys(offset // 2 for offset in offsets))
    for offset, got_ref in zip(offsets, got_refs):
        lines_ref[2 * pairs.index(offset // 2) + ((own ^ offset) & 1)] = wide(got_ref)
    low = low_half((DOT_ROWS, LANES))
    for at in range(len(pairs)):
        for start in range(0, ROWS, DOT_ROWS):
            here = slice(start, start + DOT_ROWS)
            write_left(at, here, even_odd(lines_ref[2 * at, here, :], lines_ref[2 * at + 1, here, :], low), left_ref)
    return [(own >> 1) ^ pair for pair in pairs]


def point_parts(pair, cosines, sines, weight_ref):
    for ty in range(4):
        part = weight_ref[pair, ty] * cosines + weight_ref[pair, 4 + ty] * sines
        yield ty, part
        yield ty + 4, weight_ref[pair, 8] * part


def reply_first_kernel(own_ref, weight_ref, *refs):
    count = len(TAKE_FIRST)
    table_ref, sums_ref, lines_ref, left_ref = refs[count:]
    pairs = take_lines(own_ref, TAKE_FIRST, refs[:count], left_ref, lines_ref)
    for at, pair in enumerate(pairs):
        for part in range(ROWS // DOT_ROWS):
            here = slice(part * DOT_ROWS, (part + 1) * DOT_ROWS)
            cosines, sines = line_product(at, here, left_ref, table_ref[pair])
            for ty, values in point_parts(pair, cosines, sines, weight_ref):
                sums_ref[ty, here, :] = values if at == 0 else sums_ref[ty, here, :] + values


def reply_later_kernel(own_ref, weight_ref, *refs):
    count = len(TAKE_LATER)
    sums_ref, picks_ref, table_ref, out_ref, lines_ref, left_ref, pot_ref = refs[count:]
    [pair] = take_lines(own_ref, TAKE_LATER, refs[:count], left_ref, lines_ref)
    for part in range(ROWS // DOT_ROWS):
        here = slice(part * DOT_ROWS, (part + 1) * DOT_ROWS)
        cosines, sines = line_product(0, here, left_ref, table_ref[pair])
        for ty, values in point_parts(pair, cosines, sines, weight_ref):
            values = (sums_ref[ty, here, :] + values).astype(jnp.bfloat16)
            for one in range(DOT_ROWS // SPOTS):
                q = part * (DOT_ROWS // SPOTS) + one
                pot_ref[ty * SPOTS : (ty + 1) * SPOTS, q * LANES : (q + 1) * LANES] = values[
                    one * SPOTS : (one + 1) * SPOTS
                ]
    for q in range(0, BRICK_ROWS, 4):
        there = slice(q * LANES, (q + 4) * LANES)
        out_ref[:, there] = dot(picks_ref[...], pot_ref[:, there]).astype(jnp.bfloat16)


def unpack_kernel(back_ref, got_ref, out_ref):
    for q in range(0, BRICK_ROWS, 4):
        there = slice(q * LANES, (q + 4) * LANES)
        out_ref[:, there] = dot(back_ref[...], got_ref[:, there]).astype(jnp.bfloat16)


def call(kernel, name, operands, spaces, outs, places, scratch, vmem=VMEM_BYTES):
    return pl.pallas_call(
        kernel,
        out_shape=outs,
        in_specs=[pl.BlockSpec(memory_space=space) for space in spaces],
        out_specs=[pl.BlockSpec(memory_space=space) for space in places],
        scratch_shapes=scratch,
        compiler_params=pltpu.CompilerParams(vmem_limit_bytes=vmem),
        name=name,
    )(*operands)


def on_device_8x4(bricks, owners, tile_ids, counts):
    V, S, H = pltpu.VMEM, pltpu.SMEM, pltpu.HBM
    f32, bf16, i32, i16 = jnp.float32, jnp.bfloat16, jnp.int32, jnp.int16
    shape, dma = jax.ShapeDtypeStruct, pltpu.SemaphoreType.DMA
    brick_rows = bricks.shape[0]
    lines_in, lines_out = (jnp.asarray(each) for each in line_tables())
    weights = jnp.asarray(class_weights())
    lines_in = pltpu.with_memory_space_constraint(lines_in, H)
    planes_in = [
        jnp.asarray(plane_tables(offsets, planes, False))
        for offsets, planes in ((ARRIVAL, (0, 1)), (TAKE_FIRST, (2, 3)), (TAKE_LATER, (2, 3)))
    ]
    planes_out = jnp.asarray(plane_tables(SEND, range(BZ), True))
    base, lam = (jnp.asarray(each) for each in mode_tables())
    own = lax.axis_index("gz").astype(i32).reshape(1)
    sent_shape = shape((ROWS + HEAD_ROWS, LANES), i16)
    end_shape = shape((PLANES + HEAD_ROWS, LANES), i16)
    cube, flat, sums_shape = (STEPS, PLANES, LANES), (PLANES, LANES), (8, ROWS, LANES)
    line, packed = (ROWS, LANES), [(SLOTS, PART_CELLS + LANES), (SLOTS, PART_CELLS)]
    part_shape = shape((PART_ROWS + HEAD_ROWS, LANES), i16)

    def all_ways(values):
        return lax.all_to_all(values, ("gz", "ma"), split_axis=0, concat_axis=0, tiled=True)

    def over_slabs(offset, values):
        return lax.ppermute(values, "gz", [(g, g ^ offset) for g in range(SLABS)]) if offset else values

    def round_groups(values, step):
        return lax.ppermute(values, "ma", [(m, (m + step) % GROUPS) for m in range(GROUPS)]) if step else values

    def exchanged(sent):
        sent = dict(zip(SEND, sent))
        return [over_slabs(offset, sent[offset]) for offset in ARRIVAL]

    outgoing, one_hot = call(
        pack_kernel,
        "pack",
        (owners.reshape(1, brick_rows), tile_ids.reshape(1, brick_rows), counts, bricks),
        [H] * 4,
        [shape(packed[0], bf16), shape((SLOTS, brick_rows), bf16)],
        [H, V],
        [
            V((1, brick_rows), i32),
            V((1, brick_rows), i32),
            S((1,), i32),
            V((brick_rows, PART_CELLS), bf16),
            V(packed[0], bf16),
            dma((4,)),
            dma((4,)),
        ],
        ALL_VMEM_BYTES,
    )
    outgoing_later, back = call(
        pack_later_kernel,
        "pack_later",
        (bricks, one_hot),
        [H, V],
        [shape(packed[1], bf16), shape((brick_rows, SLOTS), bf16)],
        [V, V],
        [V((brick_rows, PART_CELLS), bf16), dma((1,))],
    )
    incoming = [all_ways(outgoing), all_ways(outgoing_later)]
    forward_scratch = [
        V((PAIRS, 2 * PART_ROWS, 2 * LANES), bf16),
        V((len(SEND), *part_shape.shape), i16),
        V(lines_in.shape, bf16),
        dma((1,)),
    ]
    *sent, across = call(
        forward_first_kernel,
        "forward_first",
        (own, incoming[0], lines_in),
        [S, V, H],
        [part_shape] * len(SEND) + [shape((TILES, SLOTS), bf16)],
        [V] * (len(SEND) + 1),
        forward_scratch,
    )
    first = exchanged(sent)
    second, first[1], first[2] = lax.optimization_barrier((incoming[1], first[1], first[2]))
    *sent, picks = call(
        forward_later_kernel,
        "forward_later",
        (own, second, across, lines_in),
        [S, V, V, H],
        [part_shape] * len(SEND) + [shape((SLOTS, TILES), bf16)],
        [V] * (len(SEND) + 1),
        forward_scratch,
    )
    later = exchanged(sent)
    sums, root, gain, power = call(
        down_first_kernel,
        "down_first",
        (own, *first, planes_in[0], base, lam),
        [S] + [V] * (len(first) + 3),
        [shape(cube, f32), shape(flat, f32), shape(flat, f32), shape(cube, f32)],
        [V] * 4,
        [
            V((len(first) * PART_ROWS, LANES), f32),
        ],
    )
    middle, later = later[: len(TAKE_FIRST)], later[len(TAKE_FIRST) :]
    (sums,) = call(
        down_middle_kernel,
        "down_middle",
        (own, *middle, sums, root, planes_in[1]),
        [S] + [V] * (len(middle) + 3),
        [shape(cube, f32)],
        [V],
        [V((len(middle) * PART_ROWS, LANES), f32)],
    )
    walk, end = call(
        down_later_kernel,
        "down_later",
        (own, *later, sums, root, planes_in[2]),
        [S] + [V] * (len(later) + 3),
        [shape(cube, f32), end_shape],
        [V, V],
        [
            V((len(later) * PART_ROWS, LANES), f32),
            V(cube, f32),
            V(flat, f32),
        ],
    )
    ends = [round_groups(end, step) for step in range(GROUPS)]
    (local,) = call(local_kernel, "local", (walk, root, gain), [V] * 3, [shape(cube, f32)], [V], [])
    sent = call(
        up_kernel,
        "up",
        (own, local, power, root, gain, *ends, planes_out),
        [S] + [V] * (5 + GROUPS),
        [sent_shape] * len(SEND),
        [V] * len(SEND),
        [
            V(flat, f32),
            V(flat, f32),
            V((len(SEND), ROWS, LANES), f32),
        ],
    )
    got = exchanged(sent)
    first, later = got[: len(TAKE_FIRST)], got[len(TAKE_FIRST) :]
    (sums,) = call(
        reply_first_kernel,
        "reply_first",
        (own, weights, *first, lines_out),
        [S, S] + [V] * (len(first) + 1),
        [shape(sums_shape, f32)],
        [V],
        [V((len(first), *line), f32), V((len(first) // 2, 2 * ROWS, 2 * LANES), bf16)],
    )
    (replies,) = call(
        reply_later_kernel,
        "reply_later",
        (own, weights, *later, sums, picks, lines_out),
        [S, S] + [V] * (len(later) + 3),
        [shape((SLOTS, CELLS), bf16)],
        [V],
        [
            V((len(later), *line), f32),
            V((len(later) // 2, 2 * ROWS, 2 * LANES), bf16),
            V((TILES, CELLS), bf16),
        ],
    )
    (result,) = call(
        unpack_kernel,
        "unpack",
        (back, all_ways(replies)),
        [V, V],
        [shape((brick_rows, CELLS), bf16)],
        [V],
        [],
    )
    return result


def solution(mesh):
    in_specs = (P(("gz", "ma"), None), P(("gz", "ma"), None), P(("gz", "ma")), P(("gz", "ma")))
    out_specs = P(("gz", "ma"), None)
    body = on_device_8x4 if (mesh.shape["gz"], mesh.shape["ma"]) == (SLABS, GROUPS) else on_device
    return jax.shard_map(body, mesh=mesh, in_specs=in_specs, out_specs=out_specs, check_vma=False)
```

```python
import math

import jax
import jax.numpy as jnp
import ml_dtypes
import numpy as np
from jax import lax
from jax.experimental import pallas as pl
from jax.experimental.pallas import tpu as pltpu
from jax.sharding import PartitionSpec as P

NX = 512
NY = 512
SCREEN = 16
BZ = 4
BX = 8
BY = 64
CZ = 16


def hartley(length):
    indices = jnp.arange(length, dtype=jnp.int32)
    products = indices[:, None] * indices[None, :] % length
    angles = 2.0 * math.pi / length * products.astype(jnp.float32)
    return (jnp.cos(angles) + jnp.sin(angles)) / math.sqrt(length)


def second_difference(length, indices):
    return 2.0 - 2.0 * jnp.cos(2.0 * math.pi / length * indices.astype(jnp.float32))


def thomas(right_side, diagonal):
    start_zero = jnp.zeros(right_side.shape[1:], jnp.float32)

    def down(state_pair, plane):
        factor = 1.0 / (diagonal - state_pair[0])
        partial_value = (plane + state_pair[1]) * factor
        return ((factor, partial_value), (factor, partial_value))

    _, (factors, partials) = lax.scan(down, (start_zero, start_zero), right_side)

    def upward(beyond, factor_partial):
        solved = factor_partial[1] + factor_partial[0] * beyond
        return (solved, solved)

    _, solutions = lax.scan(upward, start_zero, (factors, partials), reverse=True)
    return solutions


def regroup(values):
    return lax.all_to_all(values, "ma", split_axis=2, concat_axis=1, tiled=True)


def on_device(bricks, owners, tile_ids, counts):
    domains = lax.axis_size(("gz", "ma"))
    group_count = lax.axis_size("ma")
    slab_count = lax.axis_size("gz")
    brick_rows, brick_cells = bricks.shape
    slot_count = max(2, 2 * brick_rows // domains)
    local_x = NX // group_count
    local_y = NY // group_count
    tiles_dev = CZ // BZ * (local_x // BX) * (NY // BY)
    highest = lax.Precision.HIGHEST
    target = owners[:, 0]
    row_order = jnp.arange(brick_rows, dtype=jnp.int32)
    earlier_same = (target[:, None] == target[None, :]) & (row_order[None, :] < row_order[:, None])
    within = jnp.sum(earlier_same.astype(jnp.int32), axis=1)
    slot_of = target * slot_count + within
    is_live = row_order < counts[0]
    loaded = jnp.where(is_live[:, None], bricks, jnp.zeros_like(bricks))
    outgoing = jnp.zeros((domains * slot_count, brick_cells), jnp.bfloat16).at[slot_of].set(loaded)
    out_ids = jnp.full((domains * slot_count,), tiles_dev, jnp.int32).at[slot_of].set(tile_ids)
    incoming, in_ids = (
        lax.all_to_all(outgoing, ("gz", "ma"), split_axis=0, concat_axis=0, tiled=True),
        lax.all_to_all(out_ids, ("gz", "ma"), split_axis=0, concat_axis=0, tiled=True),
    )
    picker = (jnp.arange(tiles_dev, dtype=jnp.int32)[:, None] == in_ids[None, :]).astype(
        jnp.bfloat16
    )
    deposit = jnp.dot(picker, incoming, preferred_element_type=jnp.float32)
    charge = deposit.reshape(CZ // BZ, local_x // BX, NY // BY, BZ, BX, BY)
    charge = charge.transpose(0, 3, 1, 4, 2, 5).reshape(CZ, local_x, NY)
    table_x = hartley(NX)
    table_y = hartley(NY)
    along_y = jnp.einsum("zxy,ky->zxk", charge, table_y, precision=highest)
    gathered_x = regroup(along_y)
    spectrum = jnp.einsum("zxk,jx->zjk", gathered_x, table_x, precision=highest)
    columns = lax.axis_index("ma") * local_y + jnp.arange(local_y, dtype=jnp.int32)
    lam_y = second_difference(NY, columns)
    screening = 1.0 / (SCREEN * SCREEN)
    slab_index = lax.axis_index("gz")
    lam_x = second_difference(NX, jnp.arange(NX, dtype=jnp.int32))
    diagonal = 2.0 + screening + lam_x[:, None] + lam_y[None, :]
    interior = spectrum[1:]
    particular = thomas(interior, diagonal)
    unit_rhs = jnp.zeros_like(interior).at[0].set(1.0)
    spike = thomas(unit_rhs, diagonal)
    near_weight = spike[0]
    far_weight = spike[-1]
    head_term = spectrum[0] + particular[0]
    tail_term = particular[-1]
    reduced_first = diagonal - near_weight
    reduced_rest = diagonal - 2.0 * near_weight
    start_zero = jnp.zeros_like(diagonal)
    heads, tails = (
        lax.all_gather(head_term[None], "gz", axis=0, tiled=True),
        lax.all_gather(tail_term[None], "gz", axis=0, tiled=True),
    )
    before = jnp.concatenate([start_zero[None], tails[:-1]], axis=0)
    sources = heads + before

    def chain_down(state_pair, packed):
        source, position = packed
        base_term = jnp.where(position == 0, reduced_first, reduced_rest)
        pivot_now = 1.0 / (base_term - far_weight * far_weight * state_pair[0])
        forward_part = pivot_now * (source + far_weight * state_pair[1])
        return ((pivot_now, forward_part), (pivot_now, forward_part))

    _, (pivots, forwards) = lax.scan(
        chain_down, (start_zero, start_zero), (sources, jnp.arange(slab_count, dtype=jnp.int32))
    )

    def chain_up(beyond, packed):
        plane_value = packed[1] + far_weight * packed[0] * beyond
        return (plane_value, plane_value)

    _, separators = lax.scan(chain_up, start_zero, (pivots, forwards), reverse=True)
    padded_sep = jnp.concatenate([separators, start_zero[None]], axis=0)
    own_plane = lax.dynamic_index_in_dim(padded_sep, slab_index, 0, keepdims=False)
    next_plane = lax.dynamic_index_in_dim(padded_sep, slab_index + 1, 0, keepdims=False)
    interior_sol = particular + own_plane[None] * spike + next_plane[None] * spike[::-1]
    modal = jnp.concatenate([own_plane[None], interior_sol], axis=0)
    back_x = jnp.einsum("zjk,jx->zkx", modal, table_x, precision=highest)
    gathered_y = regroup(back_x)
    potential = jnp.einsum("zkx,ky->zxy", gathered_y, table_y, precision=highest)
    pot_tiles = potential.reshape(CZ // BZ, BZ, local_x // BX, BX, NY // BY, BY)
    pot_tiles = (
        pot_tiles.transpose(0, 2, 4, 1, 3, 5).reshape(tiles_dev, brick_cells).astype(jnp.bfloat16)
    )
    padded_tiles = jnp.concatenate([pot_tiles, jnp.zeros((1, brick_cells), jnp.bfloat16)], axis=0)
    replies = padded_tiles[in_ids]
    returned = lax.all_to_all(replies, ("gz", "ma"), split_axis=0, concat_axis=0, tiled=True)
    result = returned[slot_of]
    return jnp.where(is_live[:, None], result, jnp.zeros_like(result))


DOMAINS = 32
GROUPS = 4
SLABS = 8
SEND = (4, 2, 5, 3, 0, 1, 6, 7)
ARRIVAL = (0, 4, 2, 5, 3, 1, 6, 7)
PARTS = 2
PART_PLANES = 2
TAKE_FIRST = (0, 4, 2, 5, 3, 1)
TAKE_LATER = (6, 7)
PAIR_SLOTS = 8
SLOTS = DOMAINS * PAIR_SLOTS
TILES = 512
BRICK_ROWS = 16
CELLS = 2048
LANES = 128
HALF = 64
SPOTS = 64
ROWS = BRICK_ROWS * SPOTS
PART_ROWS = ROWS // PARTS
PART_CELLS = CELLS // PARTS
DOT_ROWS = 512
PAIRS = 4
CLASSES = (0, 4, 1, 7, 2, 6, 3, 5)
HEAD_ROWS = 8
STEPS = 64
PLANES = 128
FULL = 32700.0
LOG_UNIT = 128.0
VMEM_BYTES = 24 * 1024 * 1024
ALL_VMEM_BYTES = 60 * 1024 * 1024


def split_table(table):
    high = table.astype(ml_dtypes.bfloat16)
    low = (table - high.astype(np.float64)).astype(ml_dtypes.bfloat16)
    return high, low


def line_tables():
    iy, k2 = np.arange(HALF)[:, None], np.arange(HALF)[None, :]
    tables = []
    for pair in range(PAIRS):
        table = np.zeros((LANES, LANES))
        for one in range(2):
            angle = 2.0 * np.pi / NY * (iy * (CLASSES[2 * pair + one] + 8 * k2) % NY)
            cosine, sine = np.cos(angle) / np.sqrt(NY), np.sin(angle) / np.sqrt(NY)
            there = slice(one * HALF, (one + 1) * HALF)
            if pair == 0:
                table[there, there] = cosine + sine
            else:
                table[:HALF, there] = cosine + sine
                table[HALF:, there] = (cosine - sine) * (1 - 2 * one)
        tables.append(table)

    def stacked(table):
        high, low = split_table(table)
        return np.concatenate(
            [np.concatenate([high, low], axis=1), np.concatenate([high, np.zeros_like(low)], axis=1)], axis=0
        )

    return np.stack([stacked(table) for table in tables]), np.stack([stacked(table.T) for table in tables])


def class_weights():
    pair, ty = np.arange(PAIRS)[:, None], np.arange(4)[None, :]
    cosine, sine = np.cos(np.pi / 4.0 * pair * ty), np.sin(np.pi / 4.0 * pair * ty)
    sine[0] = (-1.0) ** np.arange(4)
    sign = (-1.0) ** pair * np.ones((1, 4))
    return np.concatenate([cosine, sine, sign], axis=1).astype(np.float32)


def plane_tables(offsets, planes, turned):
    index = np.arange(PLANES)
    table = np.sqrt(2.0 / (PLANES + 1)) * np.sin(
        np.pi / (PLANES + 1) * ((index[:, None] + 1) * (index[None, :] + 1) % (2 * PLANES + 2))
    )
    each = []
    for own in range(SLABS):
        slabs = np.array([own ^ offset for offset in offsets])
        plane, tz = np.array(planes)[:, None, None], np.arange(BZ)[None, :, None]
        place = slabs * CZ + tz * BZ + plane
        part = table[:, (place.transpose(0, 2, 1) if turned else place).reshape(-1)]
        high, low = split_table(part.T if turned else part)
        if turned or 3 * high.shape[1] <= 2 * LANES:
            each.append(np.concatenate([high, high, low], axis=1))
            continue
        top = np.concatenate([high, high], axis=1)
        bottom = np.concatenate([low, np.zeros_like(low)], axis=1)
        each.append(np.concatenate([top, bottom], axis=0))
    return np.stack(each)


def mode_tables():
    mu = 2.0 - 2.0 * np.cos(np.pi / (PLANES + 1) * (np.arange(PLANES) + 1))
    base = np.broadcast_to((mu + 1.0 / (SCREEN * SCREEN))[:, None], (PLANES, LANES))
    lam = 2.0 - 2.0 * np.cos(2.0 * np.pi / NY * np.arange(NY))
    lam = np.stack([lam[number::8] for number in CLASSES])
    return base.astype(np.float32), np.concatenate([lam, lam], axis=1).astype(np.float32)


def low_half(shape):
    return lax.broadcasted_iota(jnp.int32, shape, len(shape) - 1) < HALF


def split(values):
    high = values.astype(jnp.bfloat16)
    return high, (values - high.astype(jnp.float32)).astype(jnp.bfloat16)


def dot(left, right):
    return jnp.dot(left, right, preferred_element_type=jnp.float32)


def start_copies(pairs, sems):
    copies = [pltpu.make_async_copy(source, place, sems.at[at]) for at, (source, place) in enumerate(pairs)]
    for each in copies:
        each.start()
    return copies


def even_odd(first, second, low):
    crossed = pltpu.roll(jnp.where(low, second, first), HALF, 1)
    return jnp.where(low, first, crossed), jnp.where(low, crossed, second)


def write_left(at, here, lines, left_ref):
    rows = left_ref.shape[1] // 2
    for line, values in enumerate(lines):
        high, rest = split(values)
        there = slice(line * rows + here.start, line * rows + here.stop)
        left_ref[at, there, :LANES] = high
        left_ref[at, there, LANES:] = rest


def line_product(at, here, left_ref, table):
    products = []
    rows = left_ref.shape[1] // 2
    for line in range(2):
        there = slice(line * rows + here.start, line * rows + here.stop)
        both = dot(left_ref[at, there, :], table)
        products.append(both[:, :LANES] + both[:, LANES:])
    return even_odd(*products, low_half(products[0].shape))


def class_sums(points):
    half = [points[ty] + points[ty + 4] for ty in range(4)]
    rest = [points[ty] - points[ty + 4] for ty in range(4)]
    even, odd = half[0] + half[2], half[1] + half[3]
    turn = math.sqrt(0.5)
    across, along = turn * (rest[1] - rest[3]), turn * (rest[1] + rest[3])
    return (
        (even + odd, even - odd),
        (rest[0] + across, rest[2] + along),
        (half[0] - half[2], half[1] - half[3]),
        (rest[0] - across, along - rest[2]),
    )


def level_of(most):
    return jnp.floor(jnp.log2(jnp.maximum(most, 1e-30)) * LOG_UNIT) + 2.0


def inverse_of(level):
    return FULL * jnp.exp2(level * (-1.0 / LOG_UNIT))


def fixed_of(values):
    return jnp.floor(values + 0.5).astype(jnp.int32).astype(jnp.int16)


def head_of(level):
    return jnp.broadcast_to(level, (HEAD_ROWS, LANES)).astype(jnp.int32).astype(jnp.int16)


def unit_of(sent_ref):
    head = sent_ref[sent_ref.shape[0] - HEAD_ROWS :, :].astype(jnp.int32).astype(jnp.float32)
    return jnp.exp2(head[0:1] * (1.0 / LOG_UNIT)) * (1.0 / FULL)


def wide(sent_ref):
    block = sent_ref[: sent_ref.shape[0] - HEAD_ROWS, :]
    return block.astype(jnp.int32).astype(jnp.float32) * unit_of(sent_ref)


def turned_up(row):
    return jnp.broadcast_to(row, (row.shape[1], row.shape[1])).T


def pack_kernel(
    owner_in, tile_in, count_in, brick_in, out_ref, one_hot_ref,
    owner_ref, tile_ref, count_ref, brick_ref, ready_ref, sems, out_sems,
):
    cells = brick_in.at[:, pl.ds(0, PART_CELLS)]
    copies = start_copies(((owner_in, owner_ref), (tile_in, tile_ref), (count_in, count_ref), (cells, brick_ref)), sems)
    for each in copies[:3]:
        each.wait()
    owner, tile = owner_ref[...], tile_ref[...]
    brick_rows = owner.shape[1]
    square = (brick_rows, brick_rows)
    position = (tile & 7) * SPOTS + ((tile >> 3) & 15) * 4 + (tile >> 7)
    spot = (position + 1).astype(jnp.float32)
    high = jnp.floor(spot * (1.0 / 32.0))
    heads = jnp.where(low_half(square), turned_up(high), turned_up(spot - 32.0 * high)).astype(jnp.bfloat16)
    named = owner.astype(jnp.float32)
    earlier = lax.broadcasted_iota(jnp.int32, square, 0) < lax.broadcasted_iota(jnp.int32, square, 1)
    same = jnp.where((turned_up(named) == named) & earlier, 1.0, 0.0)
    within = jnp.sum(same, axis=0, keepdims=True).astype(jnp.int32)
    live = lax.broadcasted_iota(jnp.int32, owner.shape, 1) < count_ref[0]
    slot = jnp.where(live, owner * PAIR_SLOTS + within, SLOTS)
    copies[3].wait()
    copies = []
    rows = 64
    for part in range(SLOTS // rows):
        here = slice(part * rows, (part + 1) * rows)
        index = lax.broadcasted_iota(jnp.int32, (rows, brick_rows), 0) + part * rows
        picks = jnp.where(index == slot, 1.0, 0.0).astype(jnp.bfloat16)
        one_hot_ref[here, :] = picks
        ready_ref[here, :PART_CELLS] = dot(picks, brick_ref[...]).astype(jnp.bfloat16)
        ready_ref[here, PART_CELLS:] = dot(picks, heads).astype(jnp.bfloat16)
        some = pl.ds(part * rows, rows)
        copies.append(pltpu.make_async_copy(ready_ref.at[some], out_ref.at[some], out_sems.at[part]))
        copies[-1].start()
    for each in copies:
        each.wait()


def pack_later_kernel(brick_in, one_hot_ref, out_ref, back_ref, brick_ref, sems):
    [copy] = start_copies(((brick_in.at[:, pl.ds(PART_CELLS, PART_CELLS)], brick_ref),), sems)
    for part in range(SLOTS // LANES):
        here = slice(part * LANES, (part + 1) * LANES)
        back_ref[:, here] = one_hot_ref[here, :].astype(jnp.float32).T.astype(jnp.bfloat16)
    copy.wait()
    out_ref[...] = dot(one_hot_ref[...], brick_ref[...]).astype(jnp.bfloat16)


def write_across(brick_ref, across_ref):
    for part in range(SLOTS // LANES):
        here = slice(part * LANES, (part + 1) * LANES)
        head = brick_ref[here, PART_CELLS:].astype(jnp.float32)
        turned = pltpu.roll(head, HALF, 1)
        low = low_half(head.shape)
        places = jnp.where(low, head, turned) * 32.0 + jnp.where(low, turned, head)
        row = places.T[0:1, :].astype(jnp.int32) - 1
        for block in range(TILES // LANES):
            there = slice(block * LANES, (block + 1) * LANES)
            tile = lax.broadcasted_iota(jnp.int32, (LANES, LANES), 0) + block * LANES
            across_ref[there, here] = jnp.where(tile == row, 1.0, 0.0).astype(jnp.bfloat16)


def write_picks(across_ref, picks_ref):
    for part in range(SLOTS // LANES):
        here = slice(part * LANES, (part + 1) * LANES)
        for block in range(TILES // LANES):
            there = slice(block * LANES, (block + 1) * LANES)
            picks_ref[here, there] = across_ref[there, here].astype(jnp.float32).T.astype(jnp.bfloat16)


def forward_lines(own_ref, brick_ref, across_ref, table_in, sent_refs, left_ref, lines_ref, table_ref, sems):
    [copy] = start_copies(((table_in, table_ref),), sems)
    low = low_half((SPOTS, LANES))
    for q in range(0, BRICK_ROWS // PARTS, 4):
        charge = dot(across_ref[...], brick_ref[:, q * LANES : (q + 4) * LANES])
        for one in range(4):
            there = slice(one * LANES, (one + 1) * LANES)
            here = slice((q + one) * SPOTS, (q + one + 1) * SPOTS)
            points = [charge[ty * SPOTS : (ty + 1) * SPOTS, there] for ty in range(8)]
            for pair, (cosines, sines) in enumerate(class_sums(points)):
                write_left(pair, here, even_odd(cosines, sines, low), left_ref)
    copy.wait()
    for pair in range(PAIRS):
        for one, values in enumerate(line_product(pair, slice(0, PART_ROWS), left_ref, table_ref[pair])):
            most = jnp.max(jnp.abs(values).reshape(PART_ROWS // 8, 8, LANES), axis=0)
            level = level_of(jnp.max(most, axis=0, keepdims=True))
            lines_ref[2 * pair + one, :PART_ROWS, :] = fixed_of(values * inverse_of(level))
            lines_ref[2 * pair + one, PART_ROWS:, :] = head_of(level)
    for offset, sent_ref in zip(SEND, sent_refs):
        sent_ref[...] = lines_ref[own_ref[0] ^ offset]


def forward_first_kernel(own_ref, brick_ref, table_in, *refs):
    sent_refs, across_ref = refs[: len(SEND)], refs[len(SEND)]
    write_across(brick_ref, across_ref)
    forward_lines(own_ref, brick_ref, across_ref, table_in, sent_refs, *refs[len(SEND) + 1 :])


def forward_later_kernel(own_ref, brick_ref, across_ref, table_in, *refs):
    sent_refs, picks_ref = refs[: len(SEND)], refs[len(SEND)]
    write_picks(across_ref, picks_ref)
    forward_lines(own_ref, brick_ref, across_ref, table_in, sent_refs, *refs[len(SEND) + 1 :])


def grid_rows(slabs, plane, xq, tx):
    start = ((plane * 4 + xq) * SPOTS + tx * 4) * slabs
    return pl.ds(pl.multiple_of(start, 4 * slabs), 4 * slabs)


def plane_product(plane_ref, lines):
    high, rest = split(lines)
    rows = plane_ref.shape[0]
    if plane_ref.shape[1] == 3 * high.shape[0]:
        return dot(plane_ref[...], jnp.concatenate([high, rest, high], axis=0))
    both = dot(plane_ref[...], jnp.concatenate([high, rest], axis=0))
    return both[: rows // 2] + both[rows // 2 :]


def add_sines(got_refs, plane_ref, grid_ref, finish, swapped=False):
    slabs = len(got_refs)
    for at, got_ref in enumerate(got_refs):
        grid_ref[pl.ds(at, PART_ROWS, stride=slabs), :] = wide(got_ref)

    def planes(tx, xq):
        return jnp.concatenate(
            [grid_ref[grid_rows(slabs, plane, xq, tx), :] for plane in range(PART_PLANES)], axis=0
        )

    def sines(tx, _):
        lines = [planes(tx, xq) for xq in range(4)]
        if swapped:
            lines += [pltpu.roll(line, HALF, 1) for line in lines]
        modes = plane_product(plane_ref, jnp.concatenate(lines, axis=1))
        parts = [modes[:, at * LANES : (at + 1) * LANES] for at in range(len(lines))]
        for xq in range(4):
            finish(tx * 4 + xq, *parts[xq::4])
        return 0

    lax.fori_loop(0, 16, sines, 0, unroll=8)


def down_first_kernel(own_ref, *refs):
    count = len(ARRIVAL)
    planes_ref, base_ref, lam_ref, modes_ref, root_ref, gain_ref, power_ref, grid_ref = refs[count:]
    excess = base_ref[...] + lam_ref[pl.ds(own_ref[0], 1), :]
    spread = jnp.sqrt(excess * (excess + 4.0))
    root_ref[...] = 2.0 / (2.0 + excess + spread)
    gain_ref[...] = 1.0 / spread
    for part in range(2):
        here = pl.ds(part * PLANES // 2, PLANES // 2)
        square = root_ref[here, :] * root_ref[here, :]

        def raised(step, power):
            power_ref[step, here, :] = power
            return power * square

        lax.fori_loop(0, STEPS, raised, jnp.ones(square.shape, jnp.float32), unroll=8)

    def finish(line, values):
        modes_ref[line] = values

    add_sines(refs[:count], planes_ref.at[own_ref[0]], grid_ref, finish)


def down_middle_kernel(own_ref, *refs):
    count = len(TAKE_FIRST)
    sums_ref, root_ref, planes_ref, out_ref, grid_ref = refs[count:]

    def finish(line, values):
        values = sums_ref[line] + values
        out_ref[line] = values + root_ref[...] * pltpu.roll(values, HALF, 1)

    add_sines(refs[:count], planes_ref.at[own_ref[0]], grid_ref, finish)


def down_later_kernel(own_ref, *refs):
    count = len(TAKE_LATER)
    sums_ref, root_ref, planes_ref, walk_ref, end_ref, grid_ref, modes_ref, last_ref = refs[count:]

    def finish(line, values, swapped):
        modes_ref[line] = sums_ref[line] + (values + root_ref[...] * swapped)

    add_sines(refs[:count], planes_ref.at[own_ref[0]], grid_ref, finish, True)
    part_rows = 64
    low = low_half((part_rows, LANES))
    for part in range(PLANES // part_rows):
        here = pl.ds(part * part_rows, part_rows)
        square = root_ref[here, :] * root_ref[here, :]

        def walk(step, held):
            held = square * held + jnp.where(low, modes_ref[STEPS - 1 - step, here, :], modes_ref[step, here, :])
            walk_ref[step, here, :] = held
            return held

        last_ref[here, :] = lax.fori_loop(0, STEPS, walk, jnp.zeros((part_rows, LANES), jnp.float32), unroll=8)
    last = last_ref[...]
    level = level_of(jnp.max(jnp.abs(last), axis=0, keepdims=True))
    end_ref[:PLANES, :] = fixed_of(last * inverse_of(level))
    end_ref[PLANES:, :] = head_of(level)


def local_kernel(walk_ref, root_ref, gain_ref, local_ref):
    part_rows = 64
    low = low_half((part_rows, LANES))
    for part in range(PLANES // part_rows):
        here = pl.ds(part * part_rows, part_rows)
        root, gain = root_ref[here, :], gain_ref[here, :]
        zero = jnp.zeros(root.shape, jnp.float32)

        def line(step, ahead_before, behind_after):
            near = jnp.where(low, walk_ref[STEPS - 1 - step, here, :], walk_ref[step, here, :])
            far = pltpu.roll(jnp.where(low, behind_after, ahead_before), HALF, 1)
            local_ref[step, here, :] = gain * (near + root * far)

        def inner(step, _):
            line(step, walk_ref[step - 1, here, :], walk_ref[STEPS - 2 - step, here, :])
            return 0

        line(0, zero, walk_ref[STEPS - 2, here, :])
        lax.fori_loop(1, STEPS - 1, inner, 0, unroll=6)
        line(STEPS - 1, walk_ref[STEPS - 2, here, :], zero)


def up_kernel(own_ref, local_ref, power_ref, root_ref, gain_ref, *refs):
    end_refs, plane_ref = refs[:GROUPS], refs[GROUPS].at[own_ref[0]]
    count = GROUPS + 1 + len(SEND)
    sent_refs = refs[GROUPS + 1 : count]
    rise_ref, fall_ref, lines_ref = refs[count:]
    low = low_half((PLANES, LANES))
    root = root_ref[...]
    square = root * root
    across = square
    for _ in range(6):
        across = across * across
    around = across
    for _ in range(2):
        around = around * around
    ends = [wide(end_ref) for end_ref in end_refs]
    entering = jnp.zeros((PLANES, LANES), jnp.float32)
    for step in range(GROUPS - 1, -1, -1):
        entering = entering * across + jnp.where(low, ends[GROUPS - 1 - step], ends[(step + 1) % GROUPS])
    entering = gain_ref[...] * entering / (1.0 - around)
    straight, turned = square * entering, root * pltpu.roll(entering, HALF, 1)
    rise_ref[...] = jnp.where(low, turned, straight)
    fall_ref[...] = jnp.where(low, straight, turned)
    slabs = len(sent_refs)
    upper = lax.broadcasted_iota(jnp.int32, (8, LANES), 0) < 4

    def solved(step):
        reach = rise_ref[...] * power_ref[step] + fall_ref[...] * power_ref[STEPS - 1 - step]
        return local_ref[step] + reach

    def lines_of(tx):
        return plane_product(plane_ref, jnp.concatenate([solved(tx * 4 + xq) for xq in range(4)], axis=1))

    def sines(step, most):
        most = list(most)
        both = lines_of(2 * step), lines_of(2 * step + 1)
        for xq in range(4):
            there = slice(xq * LANES, (xq + 1) * LANES)
            for plane in range(BZ):
                row = pl.multiple_of((plane * 4 + xq) * SPOTS + step * 8, 8)
                for slab in range(0, slabs, 2):
                    start = plane * 4 * slabs + slab * 4
                    first, second = (each[start : start + 8, there] for each in both)
                    crossed = pltpu.roll(jnp.where(upper, second, first), 4, 0)
                    for one, values in enumerate((jnp.where(upper, first, crossed), jnp.where(upper, crossed, second))):
                        lines_ref[slab + one, pl.ds(row, 8), :] = values
                        most[slab + one] = jnp.maximum(most[slab + one], jnp.abs(values))
        return tuple(most)

    most = lax.fori_loop(0, 8, sines, (jnp.zeros((8, LANES), jnp.float32),) * slabs, unroll=4)
    for at, sent_ref in enumerate(sent_refs):
        level = level_of(jnp.max(most[at], axis=0, keepdims=True))
        sent_ref[:ROWS, :] = fixed_of(lines_ref[at] * inverse_of(level))
        sent_ref[ROWS:, :] = head_of(level)


def take_lines(own_ref, offsets, got_refs, left_ref, lines_ref):
    own = own_ref[0]
    pairs = list(dict.fromkeys(offset // 2 for offset in offsets))
    for offset, got_ref in zip(offsets, got_refs):
        lines_ref[2 * pairs.index(offset // 2) + ((own ^ offset) & 1)] = wide(got_ref)
    low = low_half((DOT_ROWS, LANES))
    for at in range(len(pairs)):
        for start in range(0, ROWS, DOT_ROWS):
            here = slice(start, start + DOT_ROWS)
            write_left(at, here, even_odd(lines_ref[2 * at, here, :], lines_ref[2 * at + 1, here, :], low), left_ref)
    return [(own >> 1) ^ pair for pair in pairs]


def point_parts(pair, cosines, sines, weight_ref):
    for ty in range(4):
        part = weight_ref[pair, ty] * cosines + weight_ref[pair, 4 + ty] * sines
        yield ty, part
        yield ty + 4, weight_ref[pair, 8] * part


def slot_weights(pair, weight_ref, picks_ref):
    low = low_half((SLOTS, LANES))
    sums = [jnp.zeros((SLOTS, LANES), jnp.float32) for _ in range(2)]
    for block in range(TILES // LANES):
        picks = picks_ref[:, block * LANES : (block + 1) * LANES].astype(jnp.float32)
        for kind in range(2):
            pieces = []
            for ty in (2 * block, 2 * block + 1):
                weight = weight_ref[pair, 4 * kind + ty % 4]
                pieces.append(weight * weight_ref[pair, 8] if ty >= 4 else weight)
            sums[kind] = sums[kind] + picks * jnp.where(low, pieces[0], pieces[1])
    cosines, sines = (each + pltpu.roll(each, HALF, 1) for each in sums)
    high, rest = split(jnp.where(low, cosines, sines))
    return jnp.concatenate([high, high, rest], axis=1)


def reply_first_kernel(own_ref, weight_ref, *refs):
    count = len(TAKE_FIRST)
    picks_ref, table_ref, picked_ref, left_out_ref, lines_ref, left_ref, sums_ref = refs[count:]
    pairs = take_lines(own_ref, TAKE_FIRST, refs[:count], left_ref, lines_ref)
    for at, pair in enumerate(pairs):
        for part in range(ROWS // DOT_ROWS):
            here = slice(part * DOT_ROWS, (part + 1) * DOT_ROWS)
            cosines, sines = line_product(at, here, left_ref, table_ref[pair])
            for ty, values in point_parts(pair, cosines, sines, weight_ref):
                sums_ref[ty, here, :] = values if at == 0 else sums_ref[ty, here, :] + values
    for q in range(0, BRICK_ROWS, 2):
        points = jnp.concatenate(
            [
                jnp.concatenate([sums_ref[ty, one * SPOTS : (one + 1) * SPOTS, :] for one in (q, q + 1)], axis=1)
                for ty in range(8)
            ],
            axis=0,
        )
        high, rest = split(points)
        middle, last = split(points - high.astype(jnp.float32))
        picks = picks_ref[...]
        picked_ref[:, q * LANES : (q + 2) * LANES] = dot(picks, high) + (dot(picks, middle) + dot(picks, last))
    left_out_ref[...] = slot_weights((own_ref[0] >> 1) ^ (TAKE_LATER[0] // 2), weight_ref, picks_ref)


def reply_later_kernel(own_ref, *refs):
    count = len(TAKE_LATER)
    picked_ref, left_in_ref, table_ref, out_ref, lines_ref, left_ref, high_ref, rest_ref = refs[count:]
    [pair] = take_lines(own_ref, TAKE_LATER, refs[:count], left_ref, lines_ref)
    for part in range(ROWS // DOT_ROWS):
        here = slice(part * DOT_ROWS, (part + 1) * DOT_ROWS)
        both = line_product(0, here, left_ref, table_ref[pair])
        for one in range(DOT_ROWS // SPOTS):
            rows = slice(one * SPOTS, (one + 1) * SPOTS)
            q = part * (DOT_ROWS // SPOTS) + one
            there = slice(q * LANES, (q + 1) * LANES)
            high_ref[:, there], rest_ref[:, there] = split(jnp.concatenate([each[rows] for each in both], axis=0))
    for q in range(0, BRICK_ROWS, 4):
        there = slice(q * LANES, (q + 4) * LANES)
        high = high_ref[:, there]
        part = dot(left_in_ref[...], jnp.concatenate([high, rest_ref[:, there], high], axis=0))
        out_ref[:, there] = (picked_ref[:, there] + part).astype(jnp.bfloat16)


def unpack_kernel(back_ref, got_ref, out_ref):
    for q in range(0, BRICK_ROWS, 4):
        there = slice(q * LANES, (q + 4) * LANES)
        out_ref[:, there] = dot(back_ref[...], got_ref[:, there]).astype(jnp.bfloat16)


def call(kernel, name, operands, spaces, outs, places, scratch, vmem=VMEM_BYTES):
    return pl.pallas_call(
        kernel,
        out_shape=outs,
        in_specs=[pl.BlockSpec(memory_space=space) for space in spaces],
        out_specs=[pl.BlockSpec(memory_space=space) for space in places],
        scratch_shapes=scratch,
        compiler_params=pltpu.CompilerParams(vmem_limit_bytes=vmem),
        name=name,
    )(*operands)


def on_device_8x4(bricks, owners, tile_ids, counts):
    V, S, H = pltpu.VMEM, pltpu.SMEM, pltpu.HBM
    f32, bf16, i32, i16 = jnp.float32, jnp.bfloat16, jnp.int32, jnp.int16
    shape, dma = jax.ShapeDtypeStruct, pltpu.SemaphoreType.DMA
    brick_rows = bricks.shape[0]
    lines_in, lines_out = (jnp.asarray(each) for each in line_tables())
    weights = jnp.asarray(class_weights())
    lines_in = pltpu.with_memory_space_constraint(lines_in, H)
    planes_in = [
        jnp.asarray(plane_tables(offsets, planes, False))
        for offsets, planes in ((ARRIVAL, (0, 1)), (TAKE_FIRST, (2, 3)), (TAKE_LATER, (2, 3)))
    ]
    planes_out = jnp.asarray(plane_tables(SEND, range(BZ), True))
    base, lam = (jnp.asarray(each) for each in mode_tables())
    own = lax.axis_index("gz").astype(i32).reshape(1)
    sent_shape = shape((ROWS + HEAD_ROWS, LANES), i16)
    end_shape = shape((PLANES + HEAD_ROWS, LANES), i16)
    cube, flat, sums_shape = (STEPS, PLANES, LANES), (PLANES, LANES), (8, ROWS, LANES)
    line, packed = (ROWS, LANES), [(SLOTS, PART_CELLS + LANES), (SLOTS, PART_CELLS)]
    part_shape = shape((PART_ROWS + HEAD_ROWS, LANES), i16)

    def all_ways(values):
        return lax.all_to_all(values, ("gz", "ma"), split_axis=0, concat_axis=0, tiled=True)

    def over_slabs(offset, values):
        return lax.ppermute(values, "gz", [(g, g ^ offset) for g in range(SLABS)]) if offset else values

    def round_groups(values, step):
        return lax.ppermute(values, "ma", [(m, (m + step) % GROUPS) for m in range(GROUPS)]) if step else values

    def exchanged(sent):
        sent = dict(zip(SEND, sent))
        return [over_slabs(offset, sent[offset]) for offset in ARRIVAL]

    outgoing, one_hot = call(
        pack_kernel,
        "pack",
        (owners.reshape(1, brick_rows), tile_ids.reshape(1, brick_rows), counts, bricks),
        [H] * 4,
        [shape(packed[0], bf16), shape((SLOTS, brick_rows), bf16)],
        [H, V],
        [
            V((1, brick_rows), i32),
            V((1, brick_rows), i32),
            S((1,), i32),
            V((brick_rows, PART_CELLS), bf16),
            V(packed[0], bf16),
            dma((4,)),
            dma((4,)),
        ],
        ALL_VMEM_BYTES,
    )
    outgoing_later, back = call(
        pack_later_kernel,
        "pack_later",
        (bricks, one_hot),
        [H, V],
        [shape(packed[1], bf16), shape((brick_rows, SLOTS), bf16)],
        [V, V],
        [V((brick_rows, PART_CELLS), bf16), dma((1,))],
    )
    incoming = [all_ways(outgoing), all_ways(outgoing_later)]
    forward_scratch = [
        V((PAIRS, 2 * PART_ROWS, 2 * LANES), bf16),
        V((len(SEND), *part_shape.shape), i16),
        V(lines_in.shape, bf16),
        dma((1,)),
    ]
    *sent, across = call(
        forward_first_kernel,
        "forward_first",
        (own, incoming[0], lines_in),
        [S, V, H],
        [part_shape] * len(SEND) + [shape((TILES, SLOTS), bf16)],
        [V] * (len(SEND) + 1),
        forward_scratch,
    )
    first = exchanged(sent)
    second, first[1], first[2] = lax.optimization_barrier((incoming[1], first[1], first[2]))
    *sent, picks = call(
        forward_later_kernel,
        "forward_later",
        (own, second, across, lines_in),
        [S, V, V, H],
        [part_shape] * len(SEND) + [shape((SLOTS, TILES), bf16)],
        [V] * (len(SEND) + 1),
        forward_scratch,
    )
    later = exchanged(sent)
    sums, root, gain, power = call(
        down_first_kernel,
        "down_first",
        (own, *first, planes_in[0], base, lam),
        [S] + [V] * (len(first) + 3),
        [shape(cube, f32), shape(flat, f32), shape(flat, f32), shape(cube, f32)],
        [V] * 4,
        [
            V((len(first) * PART_ROWS, LANES), f32),
        ],
    )
    middle, later = later[: len(TAKE_FIRST)], later[len(TAKE_FIRST) :]
    (sums,) = call(
        down_middle_kernel,
        "down_middle",
        (own, *middle, sums, root, planes_in[1]),
        [S] + [V] * (len(middle) + 3),
        [shape(cube, f32)],
        [V],
        [V((len(middle) * PART_ROWS, LANES), f32)],
    )
    walk, end = call(
        down_later_kernel,
        "down_later",
        (own, *later, sums, root, planes_in[2]),
        [S] + [V] * (len(later) + 3),
        [shape(cube, f32), end_shape],
        [V, V],
        [
            V((len(later) * PART_ROWS, LANES), f32),
            V(cube, f32),
            V(flat, f32),
        ],
    )
    ends = [round_groups(end, step) for step in range(GROUPS)]
    (local,) = call(local_kernel, "local", (walk, root, gain), [V] * 3, [shape(cube, f32)], [V], [])
    sent = call(
        up_kernel,
        "up",
        (own, local, power, root, gain, *ends, planes_out),
        [S] + [V] * (5 + GROUPS),
        [sent_shape] * len(SEND),
        [V] * len(SEND),
        [
            V(flat, f32),
            V(flat, f32),
            V((len(SEND), ROWS, LANES), f32),
        ],
    )
    got = exchanged(sent)
    first, later = got[: len(TAKE_FIRST)], got[len(TAKE_FIRST) :]
    picked, slot_left = call(
        reply_first_kernel,
        "reply_first",
        (own, weights, *first, picks, lines_out),
        [S, S] + [V] * (len(first) + 2),
        [shape((SLOTS, CELLS), f32), shape((SLOTS, 3 * LANES), bf16)],
        [V, V],
        [V((len(first), *line), f32), V((len(first) // 2, 2 * ROWS, 2 * LANES), bf16), V(sums_shape, f32)],
    )
    (replies,) = call(
        reply_later_kernel,
        "reply_later",
        (own, *later, picked, slot_left, lines_out),
        [S] + [V] * (len(later) + 3),
        [shape((SLOTS, CELLS), bf16)],
        [V],
        [
            V((len(later), *line), f32),
            V((len(later) // 2, 2 * ROWS, 2 * LANES), bf16),
            V((LANES, CELLS), bf16),
            V((LANES, CELLS), bf16),
        ],
    )
    (result,) = call(
        unpack_kernel,
        "unpack",
        (back, all_ways(replies)),
        [V, V],
        [shape((brick_rows, CELLS), bf16)],
        [V],
        [],
    )
    return result


def solution(mesh):
    in_specs = (P(("gz", "ma"), None), P(("gz", "ma"), None), P(("gz", "ma")), P(("gz", "ma")))
    out_specs = P(("gz", "ma"), None)
    body = on_device_8x4 if (mesh.shape["gz"], mesh.shape["ma"]) == (SLABS, GROUPS) else on_device
    return jax.shard_map(body, mesh=mesh, in_specs=in_specs, out_specs=out_specs, check_vma=False)
```

```python
import math

import jax
import jax.numpy as jnp
import ml_dtypes
import numpy as np
from jax import lax
from jax.experimental import pallas as pl
from jax.experimental.pallas import tpu as pltpu
from jax.sharding import PartitionSpec as P

NX = 512
NY = 512
SCREEN = 16
BZ = 4
BX = 8
BY = 64
CZ = 16


def hartley(length):
    indices = jnp.arange(length, dtype=jnp.int32)
    products = indices[:, None] * indices[None, :] % length
    angles = 2.0 * math.pi / length * products.astype(jnp.float32)
    return (jnp.cos(angles) + jnp.sin(angles)) / math.sqrt(length)


def second_difference(length, indices):
    return 2.0 - 2.0 * jnp.cos(2.0 * math.pi / length * indices.astype(jnp.float32))


def thomas(right_side, diagonal):
    start_zero = jnp.zeros(right_side.shape[1:], jnp.float32)

    def down(state_pair, plane):
        factor = 1.0 / (diagonal - state_pair[0])
        partial_value = (plane + state_pair[1]) * factor
        return ((factor, partial_value), (factor, partial_value))

    _, (factors, partials) = lax.scan(down, (start_zero, start_zero), right_side)

    def upward(beyond, factor_partial):
        solved = factor_partial[1] + factor_partial[0] * beyond
        return (solved, solved)

    _, solutions = lax.scan(upward, start_zero, (factors, partials), reverse=True)
    return solutions


def regroup(values):
    return lax.all_to_all(values, "ma", split_axis=2, concat_axis=1, tiled=True)


def on_device(bricks, owners, tile_ids, counts):
    domains = lax.axis_size(("gz", "ma"))
    group_count = lax.axis_size("ma")
    slab_count = lax.axis_size("gz")
    brick_rows, brick_cells = bricks.shape
    slot_count = max(2, 2 * brick_rows // domains)
    local_x = NX // group_count
    local_y = NY // group_count
    tiles_dev = CZ // BZ * (local_x // BX) * (NY // BY)
    highest = lax.Precision.HIGHEST
    target = owners[:, 0]
    row_order = jnp.arange(brick_rows, dtype=jnp.int32)
    earlier_same = (target[:, None] == target[None, :]) & (row_order[None, :] < row_order[:, None])
    within = jnp.sum(earlier_same.astype(jnp.int32), axis=1)
    slot_of = target * slot_count + within
    is_live = row_order < counts[0]
    loaded = jnp.where(is_live[:, None], bricks, jnp.zeros_like(bricks))
    outgoing = jnp.zeros((domains * slot_count, brick_cells), jnp.bfloat16).at[slot_of].set(loaded)
    out_ids = jnp.full((domains * slot_count,), tiles_dev, jnp.int32).at[slot_of].set(tile_ids)
    incoming, in_ids = (
        lax.all_to_all(outgoing, ("gz", "ma"), split_axis=0, concat_axis=0, tiled=True),
        lax.all_to_all(out_ids, ("gz", "ma"), split_axis=0, concat_axis=0, tiled=True),
    )
    picker = (jnp.arange(tiles_dev, dtype=jnp.int32)[:, None] == in_ids[None, :]).astype(
        jnp.bfloat16
    )
    deposit = jnp.dot(picker, incoming, preferred_element_type=jnp.float32)
    charge = deposit.reshape(CZ // BZ, local_x // BX, NY // BY, BZ, BX, BY)
    charge = charge.transpose(0, 3, 1, 4, 2, 5).reshape(CZ, local_x, NY)
    table_x = hartley(NX)
    table_y = hartley(NY)
    along_y = jnp.einsum("zxy,ky->zxk", charge, table_y, precision=highest)
    gathered_x = regroup(along_y)
    spectrum = jnp.einsum("zxk,jx->zjk", gathered_x, table_x, precision=highest)
    columns = lax.axis_index("ma") * local_y + jnp.arange(local_y, dtype=jnp.int32)
    lam_y = second_difference(NY, columns)
    screening = 1.0 / (SCREEN * SCREEN)
    slab_index = lax.axis_index("gz")
    lam_x = second_difference(NX, jnp.arange(NX, dtype=jnp.int32))
    diagonal = 2.0 + screening + lam_x[:, None] + lam_y[None, :]
    interior = spectrum[1:]
    particular = thomas(interior, diagonal)
    unit_rhs = jnp.zeros_like(interior).at[0].set(1.0)
    spike = thomas(unit_rhs, diagonal)
    near_weight = spike[0]
    far_weight = spike[-1]
    head_term = spectrum[0] + particular[0]
    tail_term = particular[-1]
    reduced_first = diagonal - near_weight
    reduced_rest = diagonal - 2.0 * near_weight
    start_zero = jnp.zeros_like(diagonal)
    heads, tails = (
        lax.all_gather(head_term[None], "gz", axis=0, tiled=True),
        lax.all_gather(tail_term[None], "gz", axis=0, tiled=True),
    )
    before = jnp.concatenate([start_zero[None], tails[:-1]], axis=0)
    sources = heads + before

    def chain_down(state_pair, packed):
        source, position = packed
        base_term = jnp.where(position == 0, reduced_first, reduced_rest)
        pivot_now = 1.0 / (base_term - far_weight * far_weight * state_pair[0])
        forward_part = pivot_now * (source + far_weight * state_pair[1])
        return ((pivot_now, forward_part), (pivot_now, forward_part))

    _, (pivots, forwards) = lax.scan(
        chain_down, (start_zero, start_zero), (sources, jnp.arange(slab_count, dtype=jnp.int32))
    )

    def chain_up(beyond, packed):
        plane_value = packed[1] + far_weight * packed[0] * beyond
        return (plane_value, plane_value)

    _, separators = lax.scan(chain_up, start_zero, (pivots, forwards), reverse=True)
    padded_sep = jnp.concatenate([separators, start_zero[None]], axis=0)
    own_plane = lax.dynamic_index_in_dim(padded_sep, slab_index, 0, keepdims=False)
    next_plane = lax.dynamic_index_in_dim(padded_sep, slab_index + 1, 0, keepdims=False)
    interior_sol = particular + own_plane[None] * spike + next_plane[None] * spike[::-1]
    modal = jnp.concatenate([own_plane[None], interior_sol], axis=0)
    back_x = jnp.einsum("zjk,jx->zkx", modal, table_x, precision=highest)
    gathered_y = regroup(back_x)
    potential = jnp.einsum("zkx,ky->zxy", gathered_y, table_y, precision=highest)
    pot_tiles = potential.reshape(CZ // BZ, BZ, local_x // BX, BX, NY // BY, BY)
    pot_tiles = (
        pot_tiles.transpose(0, 2, 4, 1, 3, 5).reshape(tiles_dev, brick_cells).astype(jnp.bfloat16)
    )
    padded_tiles = jnp.concatenate([pot_tiles, jnp.zeros((1, brick_cells), jnp.bfloat16)], axis=0)
    replies = padded_tiles[in_ids]
    returned = lax.all_to_all(replies, ("gz", "ma"), split_axis=0, concat_axis=0, tiled=True)
    result = returned[slot_of]
    return jnp.where(is_live[:, None], result, jnp.zeros_like(result))


DOMAINS = 32
GROUPS = 4
SLABS = 8
SEND = (4, 2, 5, 3, 0, 1, 6, 7)
ARRIVAL = (0, 4, 2, 5, 3, 1, 6, 7)
PARTS = 2
PART_PLANES = 2
TAKE_FIRST = (0, 4, 2, 5, 3, 1)
TAKE_LATER = (6, 7)
PAIR_SLOTS = 8
SLOTS = DOMAINS * PAIR_SLOTS
TILES = 512
BRICK_ROWS = 16
CELLS = 2048
LANES = 128
HALF = 64
SPOTS = 64
ROWS = BRICK_ROWS * SPOTS
PART_ROWS = ROWS // PARTS
PART_CELLS = CELLS // PARTS
DOT_ROWS = 512
PAIRS = 4
CLASSES = (0, 4, 1, 7, 2, 6, 3, 5)
HEAD_ROWS = 8
STEPS = 64
PLANES = 128
FULL = 32700.0
LOG_UNIT = 128.0
VMEM_BYTES = 24 * 1024 * 1024
ALL_VMEM_BYTES = 60 * 1024 * 1024


def split_table(table):
    high = table.astype(ml_dtypes.bfloat16)
    low = (table - high.astype(np.float64)).astype(ml_dtypes.bfloat16)
    return high, low


def line_tables():
    iy, k2 = np.arange(HALF)[:, None], np.arange(HALF)[None, :]
    tables = []
    for pair in range(PAIRS):
        table = np.zeros((LANES, LANES))
        for one in range(2):
            angle = 2.0 * np.pi / NY * (iy * (CLASSES[2 * pair + one] + 8 * k2) % NY)
            cosine, sine = np.cos(angle) / np.sqrt(NY), np.sin(angle) / np.sqrt(NY)
            there = slice(one * HALF, (one + 1) * HALF)
            if pair == 0:
                table[there, there] = cosine + sine
            else:
                table[:HALF, there] = cosine + sine
                table[HALF:, there] = (cosine - sine) * (1 - 2 * one)
        tables.append(table)

    def stacked(table):
        high, low = split_table(table)
        return np.concatenate(
            [np.concatenate([high, low], axis=1), np.concatenate([high, np.zeros_like(low)], axis=1)], axis=0
        )

    return np.stack([stacked(table) for table in tables]), np.stack([stacked(table.T) for table in tables])


def class_weights():
    pair, ty = np.arange(PAIRS)[:, None], np.arange(4)[None, :]
    cosine, sine = np.cos(np.pi / 4.0 * pair * ty), np.sin(np.pi / 4.0 * pair * ty)
    sine[0] = (-1.0) ** np.arange(4)
    sign = (-1.0) ** pair * np.ones((1, 4))
    return np.concatenate([cosine, sine, sign], axis=1).astype(np.float32)


def plane_tables(offsets, planes, turned):
    index = np.arange(PLANES)
    table = np.sqrt(2.0 / (PLANES + 1)) * np.sin(
        np.pi / (PLANES + 1) * ((index[:, None] + 1) * (index[None, :] + 1) % (2 * PLANES + 2))
    )
    each = []
    for own in range(SLABS):
        slabs = np.array([own ^ offset for offset in offsets])
        plane, tz = np.array(planes)[:, None, None], np.arange(BZ)[None, :, None]
        place = slabs * CZ + tz * BZ + plane
        part = table[:, (place.transpose(0, 2, 1) if turned else place).reshape(-1)]
        high, low = split_table(part.T if turned else part)
        if turned or 3 * high.shape[1] <= 2 * LANES:
            each.append(np.concatenate([high, high, low], axis=1))
            continue
        top = np.concatenate([high, high], axis=1)
        bottom = np.concatenate([low, np.zeros_like(low)], axis=1)
        each.append(np.concatenate([top, bottom], axis=0))
    return np.stack(each)


def mode_tables():
    mu = 2.0 - 2.0 * np.cos(np.pi / (PLANES + 1) * (np.arange(PLANES) + 1))
    base = np.broadcast_to((mu + 1.0 / (SCREEN * SCREEN))[:, None], (PLANES, LANES))
    lam = 2.0 - 2.0 * np.cos(2.0 * np.pi / NY * np.arange(NY))
    lam = np.stack([lam[number::8] for number in CLASSES])
    return base.astype(np.float32), np.concatenate([lam, lam], axis=1).astype(np.float32)


def low_half(shape):
    return lax.broadcasted_iota(jnp.int32, shape, len(shape) - 1) < HALF


def split(values):
    high = values.astype(jnp.bfloat16)
    return high, (values - high.astype(jnp.float32)).astype(jnp.bfloat16)


def dot(left, right):
    return jnp.dot(left, right, preferred_element_type=jnp.float32)


def start_copies(pairs, sems):
    copies = [pltpu.make_async_copy(source, place, sems.at[at]) for at, (source, place) in enumerate(pairs)]
    for each in copies:
        each.start()
    return copies


def even_odd(first, second, low):
    crossed = pltpu.roll(jnp.where(low, second, first), HALF, 1)
    return jnp.where(low, first, crossed), jnp.where(low, crossed, second)


def write_left(at, here, lines, left_ref):
    rows = left_ref.shape[1] // 2
    for line, values in enumerate(lines):
        high, rest = split(values)
        there = slice(line * rows + here.start, line * rows + here.stop)
        left_ref[at, there, :LANES] = high
        left_ref[at, there, LANES:] = rest


def line_product(at, here, left_ref, table):
    rows, size = left_ref.shape[1] // 2, here.stop - here.start
    if size == rows:
        left = left_ref[at]
    else:
        left = jnp.concatenate([left_ref[at, here, :], left_ref[at, rows + here.start : rows + here.stop, :]], axis=0)
    both = dot(left, table)
    values = both[:, :LANES] + both[:, LANES:]
    return even_odd(values[:size], values[size:], low_half((size, LANES)))


def class_sums(points):
    half = [points[ty] + points[ty + 4] for ty in range(4)]
    rest = [points[ty] - points[ty + 4] for ty in range(4)]
    even, odd = half[0] + half[2], half[1] + half[3]
    turn = math.sqrt(0.5)
    across, along = turn * (rest[1] - rest[3]), turn * (rest[1] + rest[3])
    return (
        (even + odd, even - odd),
        (rest[0] + across, rest[2] + along),
        (half[0] - half[2], half[1] - half[3]),
        (rest[0] - across, along - rest[2]),
    )


def level_of(most):
    return jnp.floor(jnp.log2(jnp.maximum(most, 1e-30)) * LOG_UNIT) + 2.0


def inverse_of(level):
    return FULL * jnp.exp2(level * (-1.0 / LOG_UNIT))


def fixed_of(values):
    return jnp.floor(values + 0.5).astype(jnp.int32).astype(jnp.int16)


def head_of(level):
    return jnp.broadcast_to(level, (HEAD_ROWS, LANES)).astype(jnp.int32).astype(jnp.int16)


def unit_of(sent_ref):
    head = sent_ref[sent_ref.shape[0] - HEAD_ROWS :, :].astype(jnp.int32).astype(jnp.float32)
    return jnp.exp2(head[0:1] * (1.0 / LOG_UNIT)) * (1.0 / FULL)


def wide(sent_ref):
    block = sent_ref[: sent_ref.shape[0] - HEAD_ROWS, :]
    return block.astype(jnp.int32).astype(jnp.float32) * unit_of(sent_ref)


def turned_up(row):
    return jnp.broadcast_to(row, (row.shape[1], row.shape[1])).T


def pack_kernel(
    owner_in, tile_in, count_in, brick_in, out_ref, one_hot_ref,
    owner_ref, tile_ref, count_ref, brick_ref, ready_ref, sems, out_sems,
):
    cells = brick_in.at[:, pl.ds(0, PART_CELLS)]
    copies = start_copies(((owner_in, owner_ref), (tile_in, tile_ref), (count_in, count_ref), (cells, brick_ref)), sems)
    for each in copies[:3]:
        each.wait()
    owner, tile = owner_ref[...], tile_ref[...]
    brick_rows = owner.shape[1]
    square = (brick_rows, brick_rows)
    position = (tile & 7) * SPOTS + ((tile >> 3) & 15) * 4 + (tile >> 7)
    spot = (position + 1).astype(jnp.float32)
    high = jnp.floor(spot * (1.0 / 32.0))
    heads = jnp.where(low_half(square), turned_up(high), turned_up(spot - 32.0 * high)).astype(jnp.bfloat16)
    named = owner.astype(jnp.float32)
    earlier = lax.broadcasted_iota(jnp.int32, square, 0) < lax.broadcasted_iota(jnp.int32, square, 1)
    same = jnp.where((turned_up(named) == named) & earlier, 1.0, 0.0)
    within = jnp.sum(same, axis=0, keepdims=True).astype(jnp.int32)
    live = lax.broadcasted_iota(jnp.int32, owner.shape, 1) < count_ref[0]
    slot = jnp.where(live, owner * PAIR_SLOTS + within, SLOTS)
    copies[3].wait()
    copies = []
    rows = 64
    for part in range(SLOTS // rows):
        here = slice(part * rows, (part + 1) * rows)
        index = lax.broadcasted_iota(jnp.int32, (rows, brick_rows), 0) + part * rows
        picks = jnp.where(index == slot, 1.0, 0.0).astype(jnp.bfloat16)
        one_hot_ref[here, :] = picks
        ready_ref[here, :PART_CELLS] = dot(picks, brick_ref[...]).astype(jnp.bfloat16)
        ready_ref[here, PART_CELLS:] = dot(picks, heads).astype(jnp.bfloat16)
        some = pl.ds(part * rows, rows)
        copies.append(pltpu.make_async_copy(ready_ref.at[some], out_ref.at[some], out_sems.at[part]))
        copies[-1].start()
    for each in copies:
        each.wait()


def pack_later_kernel(brick_in, one_hot_ref, out_ref, back_ref, brick_ref, sems):
    [copy] = start_copies(((brick_in.at[:, pl.ds(PART_CELLS, PART_CELLS)], brick_ref),), sems)
    for part in range(SLOTS // LANES):
        here = slice(part * LANES, (part + 1) * LANES)
        back_ref[:, here] = one_hot_ref[here, :].astype(jnp.float32).T.astype(jnp.bfloat16)
    copy.wait()
    out_ref[...] = dot(one_hot_ref[...], brick_ref[...]).astype(jnp.bfloat16)


def write_across(brick_ref, across_ref):
    for part in range(SLOTS // LANES):
        here = slice(part * LANES, (part + 1) * LANES)
        head = brick_ref[here, PART_CELLS:].astype(jnp.float32)
        turned = pltpu.roll(head, HALF, 1)
        low = low_half(head.shape)
        places = jnp.where(low, head, turned) * 32.0 + jnp.where(low, turned, head)
        row = places.T[0:1, :].astype(jnp.int32) - 1
        for block in range(TILES // LANES):
            there = slice(block * LANES, (block + 1) * LANES)
            tile = lax.broadcasted_iota(jnp.int32, (LANES, LANES), 0) + block * LANES
            across_ref[there, here] = jnp.where(tile == row, 1.0, 0.0).astype(jnp.bfloat16)


def write_picks(across_ref, picks_ref):
    for part in range(SLOTS // LANES):
        here = slice(part * LANES, (part + 1) * LANES)
        for block in range(TILES // LANES):
            there = slice(block * LANES, (block + 1) * LANES)
            picks_ref[here, there] = across_ref[there, here].astype(jnp.float32).T.astype(jnp.bfloat16)


def forward_lines(own_ref, brick_ref, across_ref, table_in, sent_refs, left_ref, lines_ref, table_ref, sems):
    [copy] = start_copies(((table_in, table_ref),), sems)
    low = low_half((SPOTS, LANES))
    for q in range(0, BRICK_ROWS // PARTS, 4):
        charge = dot(across_ref[...], brick_ref[:, q * LANES : (q + 4) * LANES])
        for one in range(4):
            there = slice(one * LANES, (one + 1) * LANES)
            here = slice((q + one) * SPOTS, (q + one + 1) * SPOTS)
            points = [charge[ty * SPOTS : (ty + 1) * SPOTS, there] for ty in range(8)]
            for pair, (cosines, sines) in enumerate(class_sums(points)):
                write_left(pair, here, even_odd(cosines, sines, low), left_ref)
    copy.wait()
    for pair in range(PAIRS):
        for one, values in enumerate(line_product(pair, slice(0, PART_ROWS), left_ref, table_ref[pair])):
            most = jnp.max(jnp.abs(values).reshape(PART_ROWS // 8, 8, LANES), axis=0)
            level = level_of(jnp.max(most, axis=0, keepdims=True))
            lines_ref[2 * pair + one, :PART_ROWS, :] = fixed_of(values * inverse_of(level))
            lines_ref[2 * pair + one, PART_ROWS:, :] = head_of(level)
    for offset, sent_ref in zip(SEND, sent_refs):
        sent_ref[...] = lines_ref[own_ref[0] ^ offset]


def forward_first_kernel(own_ref, brick_ref, table_in, *refs):
    sent_refs, across_ref = refs[: len(SEND)], refs[len(SEND)]
    write_across(brick_ref, across_ref)
    forward_lines(own_ref, brick_ref, across_ref, table_in, sent_refs, *refs[len(SEND) + 1 :])


def forward_later_kernel(own_ref, brick_ref, across_ref, table_in, *refs):
    sent_refs, picks_ref = refs[: len(SEND)], refs[len(SEND)]
    write_picks(across_ref, picks_ref)
    forward_lines(own_ref, brick_ref, across_ref, table_in, sent_refs, *refs[len(SEND) + 1 :])


def grid_rows(slabs, plane, xq, tx):
    start = ((plane * 4 + xq) * SPOTS + tx * 4) * slabs
    return pl.ds(pl.multiple_of(start, 4 * slabs), 4 * slabs)


def plane_product(plane_ref, lines):
    high, rest = split(lines)
    rows = plane_ref.shape[0]
    if plane_ref.shape[1] == 3 * high.shape[0]:
        return dot(plane_ref[...], jnp.concatenate([high, rest, high], axis=0))
    both = dot(plane_ref[...], jnp.concatenate([high, rest], axis=0))
    return both[: rows // 2] + both[rows // 2 :]


def add_sines(got_refs, plane_ref, grid_ref, finish, swapped=False):
    slabs = len(got_refs)
    for at, got_ref in enumerate(got_refs):
        grid_ref[pl.ds(at, PART_ROWS, stride=slabs), :] = wide(got_ref)

    def planes(tx, xq):
        return jnp.concatenate(
            [grid_ref[grid_rows(slabs, plane, xq, tx), :] for plane in range(PART_PLANES)], axis=0
        )

    def sines(tx, _):
        lines = [planes(tx, xq) for xq in range(4)]
        if swapped:
            lines += [pltpu.roll(line, HALF, 1) for line in lines]
        modes = plane_product(plane_ref, jnp.concatenate(lines, axis=1))
        parts = [modes[:, at * LANES : (at + 1) * LANES] for at in range(len(lines))]
        for xq in range(4):
            finish(tx * 4 + xq, *parts[xq::4])
        return 0

    lax.fori_loop(0, 16, sines, 0, unroll=8)


def down_first_kernel(own_ref, *refs):
    count = len(ARRIVAL)
    planes_ref, base_ref, lam_ref, modes_ref, root_ref, gain_ref, power_ref, grid_ref = refs[count:]
    excess = base_ref[...] + lam_ref[pl.ds(own_ref[0], 1), :]
    spread = jnp.sqrt(excess * (excess + 4.0))
    root_ref[...] = 2.0 / (2.0 + excess + spread)
    gain_ref[...] = 1.0 / spread
    for part in range(2):
        here = pl.ds(part * PLANES // 2, PLANES // 2)
        square = root_ref[here, :] * root_ref[here, :]

        def raised(step, power):
            power_ref[step, here, :] = power
            return power * square

        lax.fori_loop(0, STEPS, raised, jnp.ones(square.shape, jnp.float32), unroll=8)

    def finish(line, values):
        modes_ref[line] = values

    add_sines(refs[:count], planes_ref.at[own_ref[0]], grid_ref, finish)


def down_middle_kernel(own_ref, *refs):
    count = len(TAKE_FIRST)
    sums_ref, root_ref, planes_ref, out_ref, grid_ref = refs[count:]

    def finish(line, values):
        values = sums_ref[line] + values
        out_ref[line] = values + root_ref[...] * pltpu.roll(values, HALF, 1)

    add_sines(refs[:count], planes_ref.at[own_ref[0]], grid_ref, finish)


def down_later_kernel(own_ref, *refs):
    count = len(TAKE_LATER)
    sums_ref, root_ref, planes_ref, walk_ref, end_ref, grid_ref, modes_ref, last_ref = refs[count:]

    def finish(line, values, swapped):
        modes_ref[line] = sums_ref[line] + (values + root_ref[...] * swapped)

    add_sines(refs[:count], planes_ref.at[own_ref[0]], grid_ref, finish, True)
    part_rows = 64
    low = low_half((part_rows, LANES))
    for part in range(PLANES // part_rows):
        here = pl.ds(part * part_rows, part_rows)
        square = root_ref[here, :] * root_ref[here, :]

        def walk(step, held):
            held = square * held + jnp.where(low, modes_ref[STEPS - 1 - step, here, :], modes_ref[step, here, :])
            walk_ref[step, here, :] = held
            return held

        last_ref[here, :] = lax.fori_loop(0, STEPS, walk, jnp.zeros((part_rows, LANES), jnp.float32), unroll=8)
    last = last_ref[...]
    level = level_of(jnp.max(jnp.abs(last), axis=0, keepdims=True))
    end_ref[:PLANES, :] = fixed_of(last * inverse_of(level))
    end_ref[PLANES:, :] = head_of(level)


def local_kernel(walk_ref, root_ref, gain_ref, local_ref):
    part_rows = 64
    low = low_half((part_rows, LANES))
    for part in range(PLANES // part_rows):
        here = pl.ds(part * part_rows, part_rows)
        root, gain = root_ref[here, :], gain_ref[here, :]
        zero = jnp.zeros(root.shape, jnp.float32)

        def line(step, ahead_before, behind_after):
            near = jnp.where(low, walk_ref[STEPS - 1 - step, here, :], walk_ref[step, here, :])
            far = pltpu.roll(jnp.where(low, behind_after, ahead_before), HALF, 1)
            local_ref[step, here, :] = gain * (near + root * far)

        def inner(step, _):
            line(step, walk_ref[step - 1, here, :], walk_ref[STEPS - 2 - step, here, :])
            return 0

        line(0, zero, walk_ref[STEPS - 2, here, :])
        lax.fori_loop(1, STEPS - 1, inner, 0, unroll=6)
        line(STEPS - 1, walk_ref[STEPS - 2, here, :], zero)


def up_kernel(own_ref, local_ref, power_ref, root_ref, gain_ref, *refs):
    end_refs, plane_ref = refs[:GROUPS], refs[GROUPS].at[own_ref[0]]
    count = GROUPS + 1 + len(SEND)
    sent_refs = refs[GROUPS + 1 : count]
    rise_ref, fall_ref, lines_ref = refs[count:]
    low = low_half((PLANES, LANES))
    root = root_ref[...]
    square = root * root
    across = square
    for _ in range(6):
        across = across * across
    around = across
    for _ in range(2):
        around = around * around
    ends = [wide(end_ref) for end_ref in end_refs]
    entering = jnp.zeros((PLANES, LANES), jnp.float32)
    for step in range(GROUPS - 1, -1, -1):
        entering = entering * across + jnp.where(low, ends[GROUPS - 1 - step], ends[(step + 1) % GROUPS])
    entering = gain_ref[...] * entering / (1.0 - around)
    straight, turned = square * entering, root * pltpu.roll(entering, HALF, 1)
    rise_ref[...] = jnp.where(low, turned, straight)
    fall_ref[...] = jnp.where(low, straight, turned)
    slabs = len(sent_refs)
    upper = lax.broadcasted_iota(jnp.int32, (8, LANES), 0) < 4

    def solved(step):
        reach = rise_ref[...] * power_ref[step] + fall_ref[...] * power_ref[STEPS - 1 - step]
        return local_ref[step] + reach

    def lines_of(tx):
        return plane_product(plane_ref, jnp.concatenate([solved(tx * 4 + xq) for xq in range(4)], axis=1))

    def sines(step, most):
        most = list(most)
        both = lines_of(2 * step), lines_of(2 * step + 1)
        for xq in range(4):
            there = slice(xq * LANES, (xq + 1) * LANES)
            for plane in range(BZ):
                row = pl.multiple_of((plane * 4 + xq) * SPOTS + step * 8, 8)
                for slab in range(0, slabs, 2):
                    start = plane * 4 * slabs + slab * 4
                    first, second = (each[start : start + 8, there] for each in both)
                    crossed = pltpu.roll(jnp.where(upper, second, first), 4, 0)
                    for one, values in enumerate((jnp.where(upper, first, crossed), jnp.where(upper, crossed, second))):
                        lines_ref[slab + one, pl.ds(row, 8), :] = values
                        most[slab + one] = jnp.maximum(most[slab + one], jnp.abs(values))
        return tuple(most)

    most = lax.fori_loop(0, 8, sines, (jnp.zeros((8, LANES), jnp.float32),) * slabs, unroll=4)
    for at, sent_ref in enumerate(sent_refs):
        level = level_of(jnp.max(most[at], axis=0, keepdims=True))
        sent_ref[:ROWS, :] = fixed_of(lines_ref[at] * inverse_of(level))
        sent_ref[ROWS:, :] = head_of(level)


def take_lines(own_ref, offsets, got_refs, left_ref, lines_ref):
    own = own_ref[0]
    pairs = list(dict.fromkeys(offset // 2 for offset in offsets))
    for offset, got_ref in zip(offsets, got_refs):
        lines_ref[2 * pairs.index(offset // 2) + ((own ^ offset) & 1)] = wide(got_ref)
    low = low_half((DOT_ROWS, LANES))
    for at in range(len(pairs)):
        for start in range(0, ROWS, DOT_ROWS):
            here = slice(start, start + DOT_ROWS)
            write_left(at, here, even_odd(lines_ref[2 * at, here, :], lines_ref[2 * at + 1, here, :], low), left_ref)
    return [(own >> 1) ^ pair for pair in pairs]


def point_parts(pair, cosines, sines, weight_ref):
    for ty in range(4):
        part = weight_ref[pair, ty] * cosines + weight_ref[pair, 4 + ty] * sines
        yield ty, part
        yield ty + 4, weight_ref[pair, 8] * part


def slot_weights(pair, weight_ref, picks_ref):
    low = low_half((SLOTS, LANES))
    sums = [jnp.zeros((SLOTS, LANES), jnp.float32) for _ in range(2)]
    for block in range(TILES // LANES):
        picks = picks_ref[:, block * LANES : (block + 1) * LANES].astype(jnp.float32)
        for kind in range(2):
            pieces = []
            for ty in (2 * block, 2 * block + 1):
                weight = weight_ref[pair, 4 * kind + ty % 4]
                pieces.append(weight * weight_ref[pair, 8] if ty >= 4 else weight)
            sums[kind] = sums[kind] + picks * jnp.where(low, pieces[0], pieces[1])
    cosines, sines = (each + pltpu.roll(each, HALF, 1) for each in sums)
    high, rest = split(jnp.where(low, cosines, sines))
    return jnp.concatenate([high, high, rest], axis=1)


def reply_first_kernel(own_ref, weight_ref, *refs):
    count = len(TAKE_FIRST)
    picks_ref, table_ref, picked_ref, left_out_ref, lines_ref, left_ref, sums_ref = refs[count:]
    pairs = take_lines(own_ref, TAKE_FIRST, refs[:count], left_ref, lines_ref)
    for at, pair in enumerate(pairs):
        for part in range(ROWS // DOT_ROWS):
            here = slice(part * DOT_ROWS, (part + 1) * DOT_ROWS)
            cosines, sines = line_product(at, here, left_ref, table_ref[pair])
            for ty, values in point_parts(pair, cosines, sines, weight_ref):
                sums_ref[ty, here, :] = values if at == 0 else sums_ref[ty, here, :] + values
    for q in range(0, BRICK_ROWS, 2):
        points = jnp.concatenate(
            [
                jnp.concatenate([sums_ref[ty, one * SPOTS : (one + 1) * SPOTS, :] for one in (q, q + 1)], axis=1)
                for ty in range(8)
            ],
            axis=0,
        )
        high = points.astype(jnp.bfloat16)
        middle, last = split(points - high.astype(jnp.float32))
        picks = picks_ref[...]
        picked_ref[:, q * LANES : (q + 2) * LANES] = dot(picks, high) + (dot(picks, middle) + dot(picks, last))
    left_out_ref[...] = slot_weights((own_ref[0] >> 1) ^ (TAKE_LATER[0] // 2), weight_ref, picks_ref)


def reply_later_kernel(own_ref, *refs):
    count = len(TAKE_LATER)
    picked_ref, left_in_ref, table_ref, out_ref, lines_ref, left_ref, high_ref, rest_ref = refs[count:]
    [pair] = take_lines(own_ref, TAKE_LATER, refs[:count], left_ref, lines_ref)
    for part in range(ROWS // DOT_ROWS):
        here = slice(part * DOT_ROWS, (part + 1) * DOT_ROWS)
        both = line_product(0, here, left_ref, table_ref[pair])
        for one in range(DOT_ROWS // SPOTS):
            rows = slice(one * SPOTS, (one + 1) * SPOTS)
            q = part * (DOT_ROWS // SPOTS) + one
            there = slice(q * LANES, (q + 1) * LANES)
            high_ref[:, there], rest_ref[:, there] = split(jnp.concatenate([each[rows] for each in both], axis=0))
    for q in range(0, BRICK_ROWS, 4):
        there = slice(q * LANES, (q + 4) * LANES)
        high = high_ref[:, there]
        part = dot(left_in_ref[...], jnp.concatenate([high, rest_ref[:, there], high], axis=0))
        out_ref[:, there] = (picked_ref[:, there] + part).astype(jnp.bfloat16)


def unpack_kernel(back_ref, got_ref, out_ref):
    for q in range(0, BRICK_ROWS, 4):
        there = slice(q * LANES, (q + 4) * LANES)
        out_ref[:, there] = dot(back_ref[...], got_ref[:, there]).astype(jnp.bfloat16)


def call(kernel, name, operands, spaces, outs, places, scratch, vmem=VMEM_BYTES):
    return pl.pallas_call(
        kernel,
        out_shape=outs,
        in_specs=[pl.BlockSpec(memory_space=space) for space in spaces],
        out_specs=[pl.BlockSpec(memory_space=space) for space in places],
        scratch_shapes=scratch,
        compiler_params=pltpu.CompilerParams(vmem_limit_bytes=vmem),
        name=name,
    )(*operands)


def on_device_8x4(bricks, owners, tile_ids, counts):
    V, S, H = pltpu.VMEM, pltpu.SMEM, pltpu.HBM
    f32, bf16, i32, i16 = jnp.float32, jnp.bfloat16, jnp.int32, jnp.int16
    shape, dma = jax.ShapeDtypeStruct, pltpu.SemaphoreType.DMA
    brick_rows = bricks.shape[0]
    lines_in, lines_out = (jnp.asarray(each) for each in line_tables())
    weights = jnp.asarray(class_weights())
    lines_in = pltpu.with_memory_space_constraint(lines_in, H)
    planes_in = [
        jnp.asarray(plane_tables(offsets, planes, False))
        for offsets, planes in ((ARRIVAL, (0, 1)), (TAKE_FIRST, (2, 3)), (TAKE_LATER, (2, 3)))
    ]
    planes_out = jnp.asarray(plane_tables(SEND, range(BZ), True))
    base, lam = (jnp.asarray(each) for each in mode_tables())
    own = lax.axis_index("gz").astype(i32).reshape(1)
    sent_shape = shape((ROWS + HEAD_ROWS, LANES), i16)
    end_shape = shape((PLANES + HEAD_ROWS, LANES), i16)
    cube, flat, sums_shape = (STEPS, PLANES, LANES), (PLANES, LANES), (8, ROWS, LANES)
    line, packed = (ROWS, LANES), [(SLOTS, PART_CELLS + LANES), (SLOTS, PART_CELLS)]
    part_shape = shape((PART_ROWS + HEAD_ROWS, LANES), i16)

    def all_ways(values):
        return lax.all_to_all(values, ("gz", "ma"), split_axis=0, concat_axis=0, tiled=True)

    def over_slabs(offset, values):
        return lax.ppermute(values, "gz", [(g, g ^ offset) for g in range(SLABS)]) if offset else values

    def round_groups(values, step):
        return lax.ppermute(values, "ma", [(m, (m + step) % GROUPS) for m in range(GROUPS)]) if step else values

    def exchanged(sent):
        sent = dict(zip(SEND, sent))
        return [over_slabs(offset, sent[offset]) for offset in ARRIVAL]

    outgoing, one_hot = call(
        pack_kernel,
        "pack",
        (owners.reshape(1, brick_rows), tile_ids.reshape(1, brick_rows), counts, bricks),
        [H] * 4,
        [shape(packed[0], bf16), shape((SLOTS, brick_rows), bf16)],
        [H, V],
        [
            V((1, brick_rows), i32),
            V((1, brick_rows), i32),
            S((1,), i32),
            V((brick_rows, PART_CELLS), bf16),
            V(packed[0], bf16),
            dma((4,)),
            dma((4,)),
        ],
        ALL_VMEM_BYTES,
    )
    outgoing_later, back = call(
        pack_later_kernel,
        "pack_later",
        (bricks, one_hot),
        [H, V],
        [shape(packed[1], bf16), shape((brick_rows, SLOTS), bf16)],
        [V, V],
        [V((brick_rows, PART_CELLS), bf16), dma((1,))],
    )
    incoming = [all_ways(outgoing), all_ways(outgoing_later)]
    forward_scratch = [
        V((PAIRS, 2 * PART_ROWS, 2 * LANES), bf16),
        V((len(SEND), *part_shape.shape), i16),
        V(lines_in.shape, bf16),
        dma((1,)),
    ]
    *sent, across = call(
        forward_first_kernel,
        "forward_first",
        (own, incoming[0], lines_in),
        [S, V, H],
        [part_shape] * len(SEND) + [shape((TILES, SLOTS), bf16)],
        [V] * (len(SEND) + 1),
        forward_scratch,
    )
    first = exchanged(sent)
    second, first[1], first[2] = lax.optimization_barrier((incoming[1], first[1], first[2]))
    *sent, picks = call(
        forward_later_kernel,
        "forward_later",
        (own, second, across, lines_in),
        [S, V, V, H],
        [part_shape] * len(SEND) + [shape((SLOTS, TILES), bf16)],
        [V] * (len(SEND) + 1),
        forward_scratch,
    )
    later = exchanged(sent)
    sums, root, gain, power = call(
        down_first_kernel,
        "down_first",
        (own, *first, planes_in[0], base, lam),
        [S] + [V] * (len(first) + 3),
        [shape(cube, f32), shape(flat, f32), shape(flat, f32), shape(cube, f32)],
        [V] * 4,
        [
            V((len(first) * PART_ROWS, LANES), f32),
        ],
    )
    middle, later = later[: len(TAKE_FIRST)], later[len(TAKE_FIRST) :]
    (sums,) = call(
        down_middle_kernel,
        "down_middle",
        (own, *middle, sums, root, planes_in[1]),
        [S] + [V] * (len(middle) + 3),
        [shape(cube, f32)],
        [V],
        [V((len(middle) * PART_ROWS, LANES), f32)],
    )
    walk, end = call(
        down_later_kernel,
        "down_later",
        (own, *later, sums, root, planes_in[2]),
        [S] + [V] * (len(later) + 3),
        [shape(cube, f32), end_shape],
        [V, V],
        [
            V((len(later) * PART_ROWS, LANES), f32),
            V(cube, f32),
            V(flat, f32),
        ],
    )
    ends = [round_groups(end, step) for step in range(GROUPS)]
    (local,) = call(local_kernel, "local", (walk, root, gain), [V] * 3, [shape(cube, f32)], [V], [])
    sent = call(
        up_kernel,
        "up",
        (own, local, power, root, gain, *ends, planes_out),
        [S] + [V] * (5 + GROUPS),
        [sent_shape] * len(SEND),
        [V] * len(SEND),
        [
            V(flat, f32),
            V(flat, f32),
            V((len(SEND), ROWS, LANES), f32),
        ],
    )
    got = exchanged(sent)
    first, later = got[: len(TAKE_FIRST)], got[len(TAKE_FIRST) :]
    picked, slot_left = call(
        reply_first_kernel,
        "reply_first",
        (own, weights, *first, picks, lines_out),
        [S, S] + [V] * (len(first) + 2),
        [shape((SLOTS, CELLS), f32), shape((SLOTS, 3 * LANES), bf16)],
        [V, V],
        [V((len(first), *line), f32), V((len(first) // 2, 2 * ROWS, 2 * LANES), bf16), V(sums_shape, f32)],
    )
    (replies,) = call(
        reply_later_kernel,
        "reply_later",
        (own, *later, picked, slot_left, lines_out),
        [S] + [V] * (len(later) + 3),
        [shape((SLOTS, CELLS), bf16)],
        [V],
        [
            V((len(later), *line), f32),
            V((len(later) // 2, 2 * ROWS, 2 * LANES), bf16),
            V((LANES, CELLS), bf16),
            V((LANES, CELLS), bf16),
        ],
    )
    (result,) = call(
        unpack_kernel,
        "unpack",
        (back, all_ways(replies)),
        [V, V],
        [shape((brick_rows, CELLS), bf16)],
        [V],
        [],
    )
    return result


def solution(mesh):
    in_specs = (P(("gz", "ma"), None), P(("gz", "ma"), None), P(("gz", "ma")), P(("gz", "ma")))
    out_specs = P(("gz", "ma"), None)
    body = on_device_8x4 if (mesh.shape["gz"], mesh.shape["ma"]) == (SLABS, GROUPS) else on_device
    return jax.shard_map(body, mesh=mesh, in_specs=in_specs, out_specs=out_specs, check_vma=False)
```

```python
import math

import jax
import jax.numpy as jnp
import ml_dtypes
import numpy as np
from jax import lax
from jax.experimental import pallas as pl
from jax.experimental.pallas import tpu as pltpu
from jax.sharding import PartitionSpec as P

NX = 512
NY = 512
SCREEN = 16
BZ = 4
BX = 8
BY = 64
CZ = 16


def hartley(length):
    indices = jnp.arange(length, dtype=jnp.int32)
    products = indices[:, None] * indices[None, :] % length
    angles = 2.0 * math.pi / length * products.astype(jnp.float32)
    return (jnp.cos(angles) + jnp.sin(angles)) / math.sqrt(length)


def second_difference(length, indices):
    return 2.0 - 2.0 * jnp.cos(2.0 * math.pi / length * indices.astype(jnp.float32))


def thomas(right_side, diagonal):
    start_zero = jnp.zeros(right_side.shape[1:], jnp.float32)

    def down(state_pair, plane):
        factor = 1.0 / (diagonal - state_pair[0])
        partial_value = (plane + state_pair[1]) * factor
        return ((factor, partial_value), (factor, partial_value))

    _, (factors, partials) = lax.scan(down, (start_zero, start_zero), right_side)

    def upward(beyond, factor_partial):
        solved = factor_partial[1] + factor_partial[0] * beyond
        return (solved, solved)

    _, solutions = lax.scan(upward, start_zero, (factors, partials), reverse=True)
    return solutions


def regroup(values):
    return lax.all_to_all(values, "ma", split_axis=2, concat_axis=1, tiled=True)


def on_device(bricks, owners, tile_ids, counts):
    domains = lax.axis_size(("gz", "ma"))
    group_count = lax.axis_size("ma")
    slab_count = lax.axis_size("gz")
    brick_rows, brick_cells = bricks.shape
    slot_count = max(2, 2 * brick_rows // domains)
    local_x = NX // group_count
    local_y = NY // group_count
    tiles_dev = CZ // BZ * (local_x // BX) * (NY // BY)
    highest = lax.Precision.HIGHEST
    target = owners[:, 0]
    row_order = jnp.arange(brick_rows, dtype=jnp.int32)
    earlier_same = (target[:, None] == target[None, :]) & (row_order[None, :] < row_order[:, None])
    within = jnp.sum(earlier_same.astype(jnp.int32), axis=1)
    slot_of = target * slot_count + within
    is_live = row_order < counts[0]
    loaded = jnp.where(is_live[:, None], bricks, jnp.zeros_like(bricks))
    outgoing = jnp.zeros((domains * slot_count, brick_cells), jnp.bfloat16).at[slot_of].set(loaded)
    out_ids = jnp.full((domains * slot_count,), tiles_dev, jnp.int32).at[slot_of].set(tile_ids)
    incoming, in_ids = (
        lax.all_to_all(outgoing, ("gz", "ma"), split_axis=0, concat_axis=0, tiled=True),
        lax.all_to_all(out_ids, ("gz", "ma"), split_axis=0, concat_axis=0, tiled=True),
    )
    picker = (jnp.arange(tiles_dev, dtype=jnp.int32)[:, None] == in_ids[None, :]).astype(
        jnp.bfloat16
    )
    deposit = jnp.dot(picker, incoming, preferred_element_type=jnp.float32)
    charge = deposit.reshape(CZ // BZ, local_x // BX, NY // BY, BZ, BX, BY)
    charge = charge.transpose(0, 3, 1, 4, 2, 5).reshape(CZ, local_x, NY)
    table_x = hartley(NX)
    table_y = hartley(NY)
    along_y = jnp.einsum("zxy,ky->zxk", charge, table_y, precision=highest)
    gathered_x = regroup(along_y)
    spectrum = jnp.einsum("zxk,jx->zjk", gathered_x, table_x, precision=highest)
    columns = lax.axis_index("ma") * local_y + jnp.arange(local_y, dtype=jnp.int32)
    lam_y = second_difference(NY, columns)
    screening = 1.0 / (SCREEN * SCREEN)
    slab_index = lax.axis_index("gz")
    lam_x = second_difference(NX, jnp.arange(NX, dtype=jnp.int32))
    diagonal = 2.0 + screening + lam_x[:, None] + lam_y[None, :]
    interior = spectrum[1:]
    particular = thomas(interior, diagonal)
    unit_rhs = jnp.zeros_like(interior).at[0].set(1.0)
    spike = thomas(unit_rhs, diagonal)
    near_weight = spike[0]
    far_weight = spike[-1]
    head_term = spectrum[0] + particular[0]
    tail_term = particular[-1]
    reduced_first = diagonal - near_weight
    reduced_rest = diagonal - 2.0 * near_weight
    start_zero = jnp.zeros_like(diagonal)
    heads, tails = (
        lax.all_gather(head_term[None], "gz", axis=0, tiled=True),
        lax.all_gather(tail_term[None], "gz", axis=0, tiled=True),
    )
    before = jnp.concatenate([start_zero[None], tails[:-1]], axis=0)
    sources = heads + before

    def chain_down(state_pair, packed):
        source, position = packed
        base_term = jnp.where(position == 0, reduced_first, reduced_rest)
        pivot_now = 1.0 / (base_term - far_weight * far_weight * state_pair[0])
        forward_part = pivot_now * (source + far_weight * state_pair[1])
        return ((pivot_now, forward_part), (pivot_now, forward_part))

    _, (pivots, forwards) = lax.scan(
        chain_down, (start_zero, start_zero), (sources, jnp.arange(slab_count, dtype=jnp.int32))
    )

    def chain_up(beyond, packed):
        plane_value = packed[1] + far_weight * packed[0] * beyond
        return (plane_value, plane_value)

    _, separators = lax.scan(chain_up, start_zero, (pivots, forwards), reverse=True)
    padded_sep = jnp.concatenate([separators, start_zero[None]], axis=0)
    own_plane = lax.dynamic_index_in_dim(padded_sep, slab_index, 0, keepdims=False)
    next_plane = lax.dynamic_index_in_dim(padded_sep, slab_index + 1, 0, keepdims=False)
    interior_sol = particular + own_plane[None] * spike + next_plane[None] * spike[::-1]
    modal = jnp.concatenate([own_plane[None], interior_sol], axis=0)
    back_x = jnp.einsum("zjk,jx->zkx", modal, table_x, precision=highest)
    gathered_y = regroup(back_x)
    potential = jnp.einsum("zkx,ky->zxy", gathered_y, table_y, precision=highest)
    pot_tiles = potential.reshape(CZ // BZ, BZ, local_x // BX, BX, NY // BY, BY)
    pot_tiles = (
        pot_tiles.transpose(0, 2, 4, 1, 3, 5).reshape(tiles_dev, brick_cells).astype(jnp.bfloat16)
    )
    padded_tiles = jnp.concatenate([pot_tiles, jnp.zeros((1, brick_cells), jnp.bfloat16)], axis=0)
    replies = padded_tiles[in_ids]
    returned = lax.all_to_all(replies, ("gz", "ma"), split_axis=0, concat_axis=0, tiled=True)
    result = returned[slot_of]
    return jnp.where(is_live[:, None], result, jnp.zeros_like(result))


DOMAINS = 32
GROUPS = 4
SLABS = 8
SEND = (4, 2, 5, 3, 0, 1, 6, 7)
ARRIVAL = (0, 4, 2, 5, 3, 1, 6, 7)
PARTS = 2
PART_PLANES = 2
TAKE_FIRST = (0, 4, 2, 5, 3, 1)
TAKE_LATER = (6, 7)
PAIR_SLOTS = 8
SLOTS = DOMAINS * PAIR_SLOTS
TILES = 512
BRICK_ROWS = 16
CELLS = 2048
LANES = 128
HALF = 64
SPOTS = 64
ROWS = BRICK_ROWS * SPOTS
PART_ROWS = ROWS // PARTS
PART_CELLS = CELLS // PARTS
DOT_ROWS = 512
PAIRS = 4
CLASSES = (0, 4, 1, 7, 2, 6, 3, 5)
HEAD_ROWS = 8
STEPS = 64
PLANES = 128
FULL = 32700.0
LOG_UNIT = 128.0
VMEM_BYTES = 24 * 1024 * 1024
ALL_VMEM_BYTES = 60 * 1024 * 1024


def split_table(table):
    high = table.astype(ml_dtypes.bfloat16)
    low = (table - high.astype(np.float64)).astype(ml_dtypes.bfloat16)
    return high, low


def line_tables():
    iy, k2 = np.arange(HALF)[:, None], np.arange(HALF)[None, :]
    tables = []
    for pair in range(PAIRS):
        table = np.zeros((LANES, LANES))
        for one in range(2):
            angle = 2.0 * np.pi / NY * (iy * (CLASSES[2 * pair + one] + 8 * k2) % NY)
            cosine, sine = np.cos(angle) / np.sqrt(NY), np.sin(angle) / np.sqrt(NY)
            there = slice(one * HALF, (one + 1) * HALF)
            if pair == 0:
                table[there, there] = cosine + sine
            else:
                table[:HALF, there] = cosine + sine
                table[HALF:, there] = (cosine - sine) * (1 - 2 * one)
        tables.append(table)

    def stacked(table):
        high, low = split_table(table)
        return np.concatenate(
            [np.concatenate([high, low], axis=1), np.concatenate([high, np.zeros_like(low)], axis=1)], axis=0
        )

    return np.stack([stacked(table) for table in tables]), np.stack([stacked(table.T) for table in tables])


def class_weights():
    pair, ty = np.arange(PAIRS)[:, None], np.arange(4)[None, :]
    cosine, sine = np.cos(np.pi / 4.0 * pair * ty), np.sin(np.pi / 4.0 * pair * ty)
    sine[0] = (-1.0) ** np.arange(4)
    sign = (-1.0) ** pair * np.ones((1, 4))
    return np.concatenate([cosine, sine, sign], axis=1).astype(np.float32)


def plane_tables(offsets, planes, turned):
    index = np.arange(PLANES)
    table = np.sqrt(2.0 / (PLANES + 1)) * np.sin(
        np.pi / (PLANES + 1) * ((index[:, None] + 1) * (index[None, :] + 1) % (2 * PLANES + 2))
    )
    each = []
    for own in range(SLABS):
        slabs = np.array([own ^ offset for offset in offsets])
        plane, tz = np.array(planes)[:, None, None], np.arange(BZ)[None, :, None]
        place = slabs * CZ + tz * BZ + plane
        part = table[:, (place.transpose(0, 2, 1) if turned else place).reshape(-1)]
        high, low = split_table(part.T if turned else part)
        if 3 * high.shape[1] <= 2 * LANES:
            each.append(np.concatenate([high, high, low], axis=1))
            continue
        top = np.concatenate([high, high], axis=1)
        bottom = np.concatenate([low, np.zeros_like(low)], axis=1)
        each.append(np.concatenate([top, bottom], axis=0))
    return np.stack(each)


def mode_tables():
    mu = 2.0 - 2.0 * np.cos(np.pi / (PLANES + 1) * (np.arange(PLANES) + 1))
    base = np.broadcast_to((mu + 1.0 / (SCREEN * SCREEN))[:, None], (PLANES, LANES))
    lam = 2.0 - 2.0 * np.cos(2.0 * np.pi / NY * np.arange(NY))
    lam = np.stack([lam[number::8] for number in CLASSES])
    return base.astype(np.float32), np.concatenate([lam, lam], axis=1).astype(np.float32)


def low_half(shape):
    return lax.broadcasted_iota(jnp.int32, shape, len(shape) - 1) < HALF


def split(values):
    high = values.astype(jnp.bfloat16)
    return high, (values - high.astype(jnp.float32)).astype(jnp.bfloat16)


def dot(left, right):
    return jnp.dot(left, right, preferred_element_type=jnp.float32)


def start_copies(pairs, sems):
    copies = [pltpu.make_async_copy(source, place, sems.at[at]) for at, (source, place) in enumerate(pairs)]
    for each in copies:
        each.start()
    return copies


def even_odd(first, second, low):
    crossed = pltpu.roll(jnp.where(low, second, first), HALF, 1)
    return jnp.where(low, first, crossed), jnp.where(low, crossed, second)


def write_left(at, here, lines, left_ref):
    rows = left_ref.shape[1] // 2
    for line, values in enumerate(lines):
        high, rest = split(values)
        there = slice(line * rows + here.start, line * rows + here.stop)
        left_ref[at, there, :LANES] = high
        left_ref[at, there, LANES:] = rest


def line_product(at, here, left_ref, table):
    products = []
    rows = left_ref.shape[1] // 2
    for line in range(2):
        there = slice(line * rows + here.start, line * rows + here.stop)
        both = dot(left_ref[at, there, :], table)
        products.append(both[:, :LANES] + both[:, LANES:])
    return even_odd(*products, low_half(products[0].shape))


def class_sums(points):
    half = [points[ty] + points[ty + 4] for ty in range(4)]
    rest = [points[ty] - points[ty + 4] for ty in range(4)]
    even, odd = half[0] + half[2], half[1] + half[3]
    turn = math.sqrt(0.5)
    across, along = turn * (rest[1] - rest[3]), turn * (rest[1] + rest[3])
    return (
        (even + odd, even - odd),
        (rest[0] + across, rest[2] + along),
        (half[0] - half[2], half[1] - half[3]),
        (rest[0] - across, along - rest[2]),
    )


def level_of(most):
    return jnp.floor(jnp.log2(jnp.maximum(most, 1e-30)) * LOG_UNIT) + 2.0


def inverse_of(level):
    return FULL * jnp.exp2(level * (-1.0 / LOG_UNIT))


def fixed_of(values):
    return jnp.floor(values + 0.5).astype(jnp.int32).astype(jnp.int16)


def head_of(level):
    return jnp.broadcast_to(level, (HEAD_ROWS, LANES)).astype(jnp.int32).astype(jnp.int16)


def unit_of(sent_ref):
    head = sent_ref[sent_ref.shape[0] - HEAD_ROWS :, :].astype(jnp.int32).astype(jnp.float32)
    return jnp.exp2(head[0:1] * (1.0 / LOG_UNIT)) * (1.0 / FULL)


def wide(sent_ref):
    block = sent_ref[: sent_ref.shape[0] - HEAD_ROWS, :]
    return block.astype(jnp.int32).astype(jnp.float32) * unit_of(sent_ref)


def turned_up(row):
    return jnp.broadcast_to(row, (row.shape[1], row.shape[1])).T


def pack_kernel(
    owner_in, tile_in, count_in, brick_in, out_ref, one_hot_ref,
    owner_ref, tile_ref, count_ref, brick_ref, ready_ref, sems, out_sems,
):
    cells = brick_in.at[:, pl.ds(0, PART_CELLS)]
    copies = start_copies(((owner_in, owner_ref), (tile_in, tile_ref), (count_in, count_ref), (cells, brick_ref)), sems)
    for each in copies[:3]:
        each.wait()
    owner, tile = owner_ref[...], tile_ref[...]
    brick_rows = owner.shape[1]
    square = (brick_rows, brick_rows)
    position = (tile & 7) * SPOTS + ((tile >> 3) & 15) * 4 + (tile >> 7)
    spot = (position + 1).astype(jnp.float32)
    high = jnp.floor(spot * (1.0 / 32.0))
    heads = jnp.where(low_half(square), turned_up(high), turned_up(spot - 32.0 * high)).astype(jnp.bfloat16)
    named = owner.astype(jnp.float32)
    earlier = lax.broadcasted_iota(jnp.int32, square, 0) < lax.broadcasted_iota(jnp.int32, square, 1)
    same = jnp.where((turned_up(named) == named) & earlier, 1.0, 0.0)
    within = jnp.sum(same, axis=0, keepdims=True).astype(jnp.int32)
    live = lax.broadcasted_iota(jnp.int32, owner.shape, 1) < count_ref[0]
    slot = jnp.where(live, owner * PAIR_SLOTS + within, SLOTS)
    copies[3].wait()
    copies = []
    rows = 64
    for part in range(SLOTS // rows):
        here = slice(part * rows, (part + 1) * rows)
        index = lax.broadcasted_iota(jnp.int32, (rows, brick_rows), 0) + part * rows
        picks = jnp.where(index == slot, 1.0, 0.0).astype(jnp.bfloat16)
        one_hot_ref[here, :] = picks
        ready_ref[here, :PART_CELLS] = dot(picks, brick_ref[...]).astype(jnp.bfloat16)
        ready_ref[here, PART_CELLS:] = dot(picks, heads).astype(jnp.bfloat16)
        some = pl.ds(part * rows, rows)
        copies.append(pltpu.make_async_copy(ready_ref.at[some], out_ref.at[some], out_sems.at[part]))
        copies[-1].start()
    for each in copies:
        each.wait()


def pack_later_kernel(brick_in, one_hot_ref, out_ref, back_ref, brick_ref, sems):
    [copy] = start_copies(((brick_in.at[:, pl.ds(PART_CELLS, PART_CELLS)], brick_ref),), sems)
    for part in range(SLOTS // LANES):
        here = slice(part * LANES, (part + 1) * LANES)
        back_ref[:, here] = one_hot_ref[here, :].astype(jnp.float32).T.astype(jnp.bfloat16)
    copy.wait()
    out_ref[...] = dot(one_hot_ref[...], brick_ref[...]).astype(jnp.bfloat16)


def write_across(brick_ref, across_ref):
    for part in range(SLOTS // LANES):
        here = slice(part * LANES, (part + 1) * LANES)
        head = brick_ref[here, PART_CELLS:].astype(jnp.float32)
        turned = pltpu.roll(head, HALF, 1)
        low = low_half(head.shape)
        places = jnp.where(low, head, turned) * 32.0 + jnp.where(low, turned, head)
        row = places.T[0:1, :].astype(jnp.int32) - 1
        for block in range(TILES // LANES):
            there = slice(block * LANES, (block + 1) * LANES)
            tile = lax.broadcasted_iota(jnp.int32, (LANES, LANES), 0) + block * LANES
            across_ref[there, here] = jnp.where(tile == row, 1.0, 0.0).astype(jnp.bfloat16)


def write_picks(across_ref, picks_ref):
    for part in range(SLOTS // LANES):
        here = slice(part * LANES, (part + 1) * LANES)
        for block in range(TILES // LANES):
            there = slice(block * LANES, (block + 1) * LANES)
            picks_ref[here, there] = across_ref[there, here].astype(jnp.float32).T.astype(jnp.bfloat16)


def forward_lines(own_ref, brick_ref, across_ref, table_in, sent_refs, left_ref, lines_ref, table_ref, sems):
    [copy] = start_copies(((table_in, table_ref),), sems)
    low = low_half((SPOTS, LANES))
    for q in range(0, BRICK_ROWS // PARTS, 4):
        charge = dot(across_ref[...], brick_ref[:, q * LANES : (q + 4) * LANES])
        for one in range(4):
            there = slice(one * LANES, (one + 1) * LANES)
            here = slice((q + one) * SPOTS, (q + one + 1) * SPOTS)
            points = [charge[ty * SPOTS : (ty + 1) * SPOTS, there] for ty in range(8)]
            for pair, (cosines, sines) in enumerate(class_sums(points)):
                write_left(pair, here, even_odd(cosines, sines, low), left_ref)
    copy.wait()
    for pair in range(PAIRS):
        for one, values in enumerate(line_product(pair, slice(0, PART_ROWS), left_ref, table_ref[pair])):
            most = jnp.max(jnp.abs(values).reshape(PART_ROWS // 8, 8, LANES), axis=0)
            level = level_of(jnp.max(most, axis=0, keepdims=True))
            lines_ref[2 * pair + one, :PART_ROWS, :] = fixed_of(values * inverse_of(level))
            lines_ref[2 * pair + one, PART_ROWS:, :] = head_of(level)
    for offset, sent_ref in zip(SEND, sent_refs):
        sent_ref[...] = lines_ref[own_ref[0] ^ offset]


def forward_first_kernel(own_ref, brick_ref, table_in, *refs):
    sent_refs, across_ref = refs[: len(SEND)], refs[len(SEND)]
    write_across(brick_ref, across_ref)
    forward_lines(own_ref, brick_ref, across_ref, table_in, sent_refs, *refs[len(SEND) + 1 :])


def forward_later_kernel(own_ref, brick_ref, across_ref, table_in, *refs):
    sent_refs, picks_ref = refs[: len(SEND)], refs[len(SEND)]
    write_picks(across_ref, picks_ref)
    forward_lines(own_ref, brick_ref, across_ref, table_in, sent_refs, *refs[len(SEND) + 1 :])


def grid_rows(slabs, plane, xq, tx):
    start = ((plane * 4 + xq) * SPOTS + tx * 4) * slabs
    return pl.ds(pl.multiple_of(start, 4 * slabs), 4 * slabs)


def plane_product(plane_ref, lines):
    high, rest = split(lines)
    rows = plane_ref.shape[0]
    if plane_ref.shape[1] == 3 * high.shape[0]:
        return dot(plane_ref[...], jnp.concatenate([high, rest, high], axis=0))
    both = dot(plane_ref[...], jnp.concatenate([high, rest], axis=0))
    return both[: rows // 2] + both[rows // 2 :]


def add_sines(got_refs, plane_ref, grid_ref, finish, swapped=False):
    slabs = len(got_refs)
    for at, got_ref in enumerate(got_refs):
        grid_ref[pl.ds(at, PART_ROWS, stride=slabs), :] = wide(got_ref)

    def planes(tx, xq):
        return jnp.concatenate(
            [grid_ref[grid_rows(slabs, plane, xq, tx), :] for plane in range(PART_PLANES)], axis=0
        )

    def sines(tx, _):
        lines = [planes(tx, xq) for xq in range(4)]
        if swapped:
            lines += [pltpu.roll(line, HALF, 1) for line in lines]
        modes = plane_product(plane_ref, jnp.concatenate(lines, axis=1))
        parts = [modes[:, at * LANES : (at + 1) * LANES] for at in range(len(lines))]
        for xq in range(4):
            finish(tx * 4 + xq, *parts[xq::4])
        return 0

    lax.fori_loop(0, 16, sines, 0, unroll=8)


def down_first_kernel(own_ref, *refs):
    count = len(ARRIVAL)
    planes_ref, base_ref, lam_ref, modes_ref, root_ref, gain_ref, power_ref, grid_ref = refs[count:]
    excess = base_ref[...] + lam_ref[pl.ds(own_ref[0], 1), :]
    spread = jnp.sqrt(excess * (excess + 4.0))
    root_ref[...] = 2.0 / (2.0 + excess + spread)
    gain_ref[...] = 1.0 / spread
    for part in range(2):
        here = pl.ds(part * PLANES // 2, PLANES // 2)
        square = root_ref[here, :] * root_ref[here, :]

        def raised(step, power):
            power_ref[step, here, :] = power
            return power * square

        lax.fori_loop(0, STEPS, raised, jnp.ones(square.shape, jnp.float32), unroll=8)

    def finish(line, values):
        modes_ref[line] = values

    add_sines(refs[:count], planes_ref.at[own_ref[0]], grid_ref, finish)


def down_middle_kernel(own_ref, *refs):
    count = len(TAKE_FIRST)
    sums_ref, root_ref, planes_ref, out_ref, grid_ref = refs[count:]

    def finish(line, values):
        values = sums_ref[line] + values
        out_ref[line] = values + root_ref[...] * pltpu.roll(values, HALF, 1)

    add_sines(refs[:count], planes_ref.at[own_ref[0]], grid_ref, finish)


def down_later_kernel(own_ref, *refs):
    count = len(TAKE_LATER)
    sums_ref, root_ref, planes_ref, walk_ref, end_ref, grid_ref, modes_ref, last_ref = refs[count:]

    def finish(line, values, swapped):
        modes_ref[line] = sums_ref[line] + (values + root_ref[...] * swapped)

    add_sines(refs[:count], planes_ref.at[own_ref[0]], grid_ref, finish, True)
    part_rows = 64
    low = low_half((part_rows, LANES))
    for part in range(PLANES // part_rows):
        here = pl.ds(part * part_rows, part_rows)
        square = root_ref[here, :] * root_ref[here, :]

        def walk(step, held):
            held = square * held + jnp.where(low, modes_ref[STEPS - 1 - step, here, :], modes_ref[step, here, :])
            walk_ref[step, here, :] = held
            return held

        last_ref[here, :] = lax.fori_loop(0, STEPS, walk, jnp.zeros((part_rows, LANES), jnp.float32), unroll=16)
    last = last_ref[...]
    level = level_of(jnp.max(jnp.abs(last), axis=0, keepdims=True))
    end_ref[:PLANES, :] = fixed_of(last * inverse_of(level))
    end_ref[PLANES:, :] = head_of(level)


def local_kernel(walk_ref, root_ref, gain_ref, local_ref):
    part_rows = 64
    low = low_half((part_rows, LANES))
    for part in range(PLANES // part_rows):
        here = pl.ds(part * part_rows, part_rows)
        root, gain = root_ref[here, :], gain_ref[here, :]
        zero = jnp.zeros(root.shape, jnp.float32)

        def line(step, ahead_before, behind_after):
            near = jnp.where(low, walk_ref[STEPS - 1 - step, here, :], walk_ref[step, here, :])
            far = pltpu.roll(jnp.where(low, behind_after, ahead_before), HALF, 1)
            local_ref[step, here, :] = gain * (near + root * far)

        def inner(step, _):
            line(step, walk_ref[step - 1, here, :], walk_ref[STEPS - 2 - step, here, :])
            return 0

        line(0, zero, walk_ref[STEPS - 2, here, :])
        lax.fori_loop(1, STEPS - 1, inner, 0, unroll=6)
        line(STEPS - 1, walk_ref[STEPS - 2, here, :], zero)


def up_kernel(own_ref, local_ref, power_ref, root_ref, gain_ref, *refs):
    end_refs, plane_ref = refs[:GROUPS], refs[GROUPS].at[own_ref[0]]
    count = GROUPS + 1 + len(SEND)
    sent_refs = refs[GROUPS + 1 : count]
    rise_ref, fall_ref, lines_ref = refs[count:]
    low = low_half((PLANES, LANES))
    root = root_ref[...]
    square = root * root
    across = square
    for _ in range(6):
        across = across * across
    around = across
    for _ in range(2):
        around = around * around
    ends = [wide(end_ref) for end_ref in end_refs]
    entering = jnp.zeros((PLANES, LANES), jnp.float32)
    for step in range(GROUPS - 1, -1, -1):
        entering = entering * across + jnp.where(low, ends[GROUPS - 1 - step], ends[(step + 1) % GROUPS])
    entering = gain_ref[...] * entering / (1.0 - around)
    straight, turned = square * entering, root * pltpu.roll(entering, HALF, 1)
    rise_ref[...] = jnp.where(low, turned, straight)
    fall_ref[...] = jnp.where(low, straight, turned)
    slabs = len(sent_refs)
    upper = lax.broadcasted_iota(jnp.int32, (8, LANES), 0) < 4

    def solved(step):
        reach = rise_ref[...] * power_ref[step] + fall_ref[...] * power_ref[STEPS - 1 - step]
        return local_ref[step] + reach

    def lines_of(tx):
        return plane_product(plane_ref, jnp.concatenate([solved(tx * 4 + xq) for xq in range(4)], axis=1))

    def sines(step, most):
        most = list(most)
        both = lines_of(2 * step), lines_of(2 * step + 1)
        for xq in range(4):
            there = slice(xq * LANES, (xq + 1) * LANES)
            for plane in range(BZ):
                row = pl.multiple_of((plane * 4 + xq) * SPOTS + step * 8, 8)
                for slab in range(0, slabs, 2):
                    start = plane * 4 * slabs + slab * 4
                    first, second = (each[start : start + 8, there] for each in both)
                    crossed = pltpu.roll(jnp.where(upper, second, first), 4, 0)
                    for one, values in enumerate((jnp.where(upper, first, crossed), jnp.where(upper, crossed, second))):
                        lines_ref[slab + one, pl.ds(row, 8), :] = values
                        most[slab + one] = jnp.maximum(most[slab + one], jnp.abs(values))
        return tuple(most)

    most = lax.fori_loop(0, 8, sines, (jnp.zeros((8, LANES), jnp.float32),) * slabs, unroll=4)
    for at, sent_ref in enumerate(sent_refs):
        level = level_of(jnp.max(most[at], axis=0, keepdims=True))
        sent_ref[:ROWS, :] = fixed_of(lines_ref[at] * inverse_of(level))
        sent_ref[ROWS:, :] = head_of(level)


def take_lines(own_ref, offsets, got_refs, left_ref, lines_ref):
    own = own_ref[0]
    pairs = list(dict.fromkeys(offset // 2 for offset in offsets))
    for offset, got_ref in zip(offsets, got_refs):
        lines_ref[2 * pairs.index(offset // 2) + ((own ^ offset) & 1)] = wide(got_ref)
    low = low_half((DOT_ROWS, LANES))
    for at in range(len(pairs)):
        for start in range(0, ROWS, DOT_ROWS):
            here = slice(start, start + DOT_ROWS)
            write_left(at, here, even_odd(lines_ref[2 * at, here, :], lines_ref[2 * at + 1, here, :], low), left_ref)
    return [(own >> 1) ^ pair for pair in pairs]


def point_parts(pair, cosines, sines, weight_ref):
    for ty in range(4):
        part = weight_ref[pair, ty] * cosines + weight_ref[pair, 4 + ty] * sines
        yield ty, part
        yield ty + 4, weight_ref[pair, 8] * part


def slot_weights(pair, weight_ref, picks_ref):
    low = low_half((SLOTS, LANES))
    sums = [jnp.zeros((SLOTS, LANES), jnp.float32) for _ in range(2)]
    for block in range(TILES // LANES):
        picks = picks_ref[:, block * LANES : (block + 1) * LANES].astype(jnp.float32)
        for kind in range(2):
            pieces = []
            for ty in (2 * block, 2 * block + 1):
                weight = weight_ref[pair, 4 * kind + ty % 4]
                pieces.append(weight * weight_ref[pair, 8] if ty >= 4 else weight)
            sums[kind] = sums[kind] + picks * jnp.where(low, pieces[0], pieces[1])
    cosines, sines = (each + pltpu.roll(each, HALF, 1) for each in sums)
    high, rest = split(jnp.where(low, cosines, sines))
    return jnp.concatenate([high, high, rest], axis=1)


def reply_first_kernel(own_ref, weight_ref, *refs):
    count = len(TAKE_FIRST)
    picks_ref, table_ref, picked_ref, left_out_ref, lines_ref, left_ref, sums_ref = refs[count:]
    pairs = take_lines(own_ref, TAKE_FIRST, refs[:count], left_ref, lines_ref)
    for at, pair in enumerate(pairs):
        for part in range(ROWS // DOT_ROWS):
            here = slice(part * DOT_ROWS, (part + 1) * DOT_ROWS)
            cosines, sines = line_product(at, here, left_ref, table_ref[pair])
            for ty, values in point_parts(pair, cosines, sines, weight_ref):
                sums_ref[ty, here, :] = values if at == 0 else sums_ref[ty, here, :] + values
    for q in range(0, BRICK_ROWS, 2):
        points = jnp.concatenate(
            [
                jnp.concatenate([sums_ref[ty, one * SPOTS : (one + 1) * SPOTS, :] for one in (q, q + 1)], axis=1)
                for ty in range(8)
            ],
            axis=0,
        )
        high, rest = split(points)
        middle, last = split(points - high.astype(jnp.float32))
        picks = picks_ref[...]
        picked_ref[:, q * LANES : (q + 2) * LANES] = dot(picks, high) + (dot(picks, middle) + dot(picks, last))
    left_out_ref[...] = slot_weights((own_ref[0] >> 1) ^ (TAKE_LATER[0] // 2), weight_ref, picks_ref)


def reply_later_kernel(own_ref, *refs):
    count = len(TAKE_LATER)
    picked_ref, left_in_ref, table_ref, out_ref, lines_ref, left_ref, high_ref, rest_ref = refs[count:]
    [pair] = take_lines(own_ref, TAKE_LATER, refs[:count], left_ref, lines_ref)
    for part in range(ROWS // DOT_ROWS):
        here = slice(part * DOT_ROWS, (part + 1) * DOT_ROWS)
        both = line_product(0, here, left_ref, table_ref[pair])
        for one in range(DOT_ROWS // SPOTS):
            rows = slice(one * SPOTS, (one + 1) * SPOTS)
            q = part * (DOT_ROWS // SPOTS) + one
            there = slice(q * LANES, (q + 1) * LANES)
            high_ref[:, there], rest_ref[:, there] = split(jnp.concatenate([each[rows] for each in both], axis=0))
    for q in range(0, BRICK_ROWS, 4):
        there = slice(q * LANES, (q + 4) * LANES)
        high = high_ref[:, there]
        part = dot(left_in_ref[...], jnp.concatenate([high, rest_ref[:, there], high], axis=0))
        out_ref[:, there] = (picked_ref[:, there] + part).astype(jnp.bfloat16)


def unpack_kernel(back_ref, got_ref, out_ref):
    for q in range(0, BRICK_ROWS, 4):
        there = slice(q * LANES, (q + 4) * LANES)
        out_ref[:, there] = dot(back_ref[...], got_ref[:, there]).astype(jnp.bfloat16)


def call(kernel, name, operands, spaces, outs, places, scratch, vmem=VMEM_BYTES):
    return pl.pallas_call(
        kernel,
        out_shape=outs,
        in_specs=[pl.BlockSpec(memory_space=space) for space in spaces],
        out_specs=[pl.BlockSpec(memory_space=space) for space in places],
        scratch_shapes=scratch,
        compiler_params=pltpu.CompilerParams(vmem_limit_bytes=vmem),
        name=name,
    )(*operands)


def on_device_8x4(bricks, owners, tile_ids, counts):
    V, S, H = pltpu.VMEM, pltpu.SMEM, pltpu.HBM
    f32, bf16, i32, i16 = jnp.float32, jnp.bfloat16, jnp.int32, jnp.int16
    shape, dma = jax.ShapeDtypeStruct, pltpu.SemaphoreType.DMA
    brick_rows = bricks.shape[0]
    lines_in, lines_out = (jnp.asarray(each) for each in line_tables())
    weights = jnp.asarray(class_weights())
    lines_in = pltpu.with_memory_space_constraint(lines_in, H)
    planes_in = [
        jnp.asarray(plane_tables(offsets, planes, False))
        for offsets, planes in ((ARRIVAL, (0, 1)), (TAKE_FIRST, (2, 3)), (TAKE_LATER, (2, 3)))
    ]
    planes_out = jnp.asarray(plane_tables(SEND, range(BZ), True))
    base, lam = (jnp.asarray(each) for each in mode_tables())
    own = lax.axis_index("gz").astype(i32).reshape(1)
    sent_shape = shape((ROWS + HEAD_ROWS, LANES), i16)
    end_shape = shape((PLANES + HEAD_ROWS, LANES), i16)
    cube, flat, sums_shape = (STEPS, PLANES, LANES), (PLANES, LANES), (8, ROWS, LANES)
    line, packed = (ROWS, LANES), [(SLOTS, PART_CELLS + LANES), (SLOTS, PART_CELLS)]
    part_shape = shape((PART_ROWS + HEAD_ROWS, LANES), i16)

    def all_ways(values):
        return lax.all_to_all(values, ("gz", "ma"), split_axis=0, concat_axis=0, tiled=True)

    def over_slabs(offset, values):
        return lax.ppermute(values, "gz", [(g, g ^ offset) for g in range(SLABS)]) if offset else values

    def round_groups(values, step):
        return lax.ppermute(values, "ma", [(m, (m + step) % GROUPS) for m in range(GROUPS)]) if step else values

    def exchanged(sent):
        sent = dict(zip(SEND, sent))
        return [over_slabs(offset, sent[offset]) for offset in ARRIVAL]

    outgoing, one_hot = call(
        pack_kernel,
        "pack",
        (owners.reshape(1, brick_rows), tile_ids.reshape(1, brick_rows), counts, bricks),
        [H] * 4,
        [shape(packed[0], bf16), shape((SLOTS, brick_rows), bf16)],
        [H, V],
        [
            V((1, brick_rows), i32),
            V((1, brick_rows), i32),
            S((1,), i32),
            V((brick_rows, PART_CELLS), bf16),
            V(packed[0], bf16),
            dma((4,)),
            dma((4,)),
        ],
        ALL_VMEM_BYTES,
    )
    outgoing_later, back = call(
        pack_later_kernel,
        "pack_later",
        (bricks, one_hot),
        [H, V],
        [shape(packed[1], bf16), shape((brick_rows, SLOTS), bf16)],
        [V, V],
        [V((brick_rows, PART_CELLS), bf16), dma((1,))],
    )
    incoming = [all_ways(outgoing), all_ways(outgoing_later)]
    forward_scratch = [
        V((PAIRS, 2 * PART_ROWS, 2 * LANES), bf16),
        V((len(SEND), *part_shape.shape), i16),
        V(lines_in.shape, bf16),
        dma((1,)),
    ]
    *sent, across = call(
        forward_first_kernel,
        "forward_first",
        (own, incoming[0], lines_in),
        [S, V, H],
        [part_shape] * len(SEND) + [shape((TILES, SLOTS), bf16)],
        [V] * (len(SEND) + 1),
        forward_scratch,
    )
    first = exchanged(sent)
    second, first[1], first[2] = lax.optimization_barrier((incoming[1], first[1], first[2]))
    *sent, picks = call(
        forward_later_kernel,
        "forward_later",
        (own, second, across, lines_in),
        [S, V, V, H],
        [part_shape] * len(SEND) + [shape((SLOTS, TILES), bf16)],
        [V] * (len(SEND) + 1),
        forward_scratch,
    )
    later = exchanged(sent)
    sums, root, gain, power = call(
        down_first_kernel,
        "down_first",
        (own, *first, planes_in[0], base, lam),
        [S] + [V] * (len(first) + 3),
        [shape(cube, f32), shape(flat, f32), shape(flat, f32), shape(cube, f32)],
        [V] * 4,
        [
            V((len(first) * PART_ROWS, LANES), f32),
        ],
    )
    middle, later = later[: len(TAKE_FIRST)], later[len(TAKE_FIRST) :]
    (sums,) = call(
        down_middle_kernel,
        "down_middle",
        (own, *middle, sums, root, planes_in[1]),
        [S] + [V] * (len(middle) + 3),
        [shape(cube, f32)],
        [V],
        [V((len(middle) * PART_ROWS, LANES), f32)],
    )
    walk, end = call(
        down_later_kernel,
        "down_later",
        (own, *later, sums, root, planes_in[2]),
        [S] + [V] * (len(later) + 3),
        [shape(cube, f32), end_shape],
        [V, V],
        [
            V((len(later) * PART_ROWS, LANES), f32),
            V(cube, f32),
            V(flat, f32),
        ],
    )
    ends = [round_groups(end, step) for step in range(GROUPS)]
    (local,) = call(local_kernel, "local", (walk, root, gain), [V] * 3, [shape(cube, f32)], [V], [])
    sent = call(
        up_kernel,
        "up",
        (own, local, power, root, gain, *ends, planes_out),
        [S] + [V] * (5 + GROUPS),
        [sent_shape] * len(SEND),
        [V] * len(SEND),
        [
            V(flat, f32),
            V(flat, f32),
            V((len(SEND), ROWS, LANES), f32),
        ],
    )
    got = exchanged(sent)
    first, later = got[: len(TAKE_FIRST)], got[len(TAKE_FIRST) :]
    picked, slot_left = call(
        reply_first_kernel,
        "reply_first",
        (own, weights, *first, picks, lines_out),
        [S, S] + [V] * (len(first) + 2),
        [shape((SLOTS, CELLS), f32), shape((SLOTS, 3 * LANES), bf16)],
        [V, V],
        [V((len(first), *line), f32), V((len(first) // 2, 2 * ROWS, 2 * LANES), bf16), V(sums_shape, f32)],
    )
    (replies,) = call(
        reply_later_kernel,
        "reply_later",
        (own, *later, picked, slot_left, lines_out),
        [S] + [V] * (len(later) + 3),
        [shape((SLOTS, CELLS), bf16)],
        [V],
        [
            V((len(later), *line), f32),
            V((len(later) // 2, 2 * ROWS, 2 * LANES), bf16),
            V((LANES, CELLS), bf16),
            V((LANES, CELLS), bf16),
        ],
    )
    (result,) = call(
        unpack_kernel,
        "unpack",
        (back, all_ways(replies)),
        [V, V],
        [shape((brick_rows, CELLS), bf16)],
        [V],
        [],
    )
    return result


def solution(mesh):
    in_specs = (P(("gz", "ma"), None), P(("gz", "ma"), None), P(("gz", "ma")), P(("gz", "ma")))
    out_specs = P(("gz", "ma"), None)
    body = on_device_8x4 if (mesh.shape["gz"], mesh.shape["ma"]) == (SLABS, GROUPS) else on_device
    return jax.shard_map(body, mesh=mesh, in_specs=in_specs, out_specs=out_specs, check_vma=False)
```
